32 devices in a mesh: span: 16 (over z, y, x), width: 2 (over core).
Axes of the slice: x: 2, y: 2, z: 4, core: 2. Of those that a mesh axis runs over, the one named last changes fastest.
Arguments:
- right_side: float32 [32, 128, 1024], P(None, 'span', 'width'), may hold values from -6 to 6
- diffusivity: float32 [32, 128, 1024], P(None, 'span', 'width'), may hold values from 0.2 to 5
- reaction: float32 [32, 128, 1024], P(None, 'span', 'width'), may hold values from 0.01 to 0.2
Outputs:
- correction: float32 [32, 128, 1024], P(None, 'span', 'width')
The draws below stay inside these ranges and needn't reach their ends.
All inputs are finite; a program needn't handle non-finite values.
Results may differ from the reference program's by a relative error of at most 0.0003.
Values sent between devices are 32-bit elements; how exact they have to be, the bound alone decides.
No kernel may reach another device: no remote copies, remote signals or barrier semaphores. Data moves between devices by JAX's collectives and lax.ppermute only.
A program may use at most 128 MiB of HBM per device.

```python
import math
import jax
import jax.numpy as jnp

NZ = 32
LEVELS = 6
COARSE_SWEEPS = 3
NX = 128
NY = 1024


def steps_of(rng, extent, cuts, least, largest):
    def one(dim, parts):
        steps = jax.random.uniform(jax.random.fold_in(jax.random.fold_in(rng, 6), dim), (parts,), jnp.float32, least / len(cuts), largest / len(cuts))
        return jnp.repeat(jnp.exp(steps), extent[dim] // parts).reshape((-1,) + (1,) * (len(extent) - dim - 1))

    factor_of = one(*cuts[0])
    for cut in cuts[1:]:
        factor_of = factor_of * one(*cut)
    return factor_of


def normal_values(own_key, extent, spread, reach, shards=(), kind=jnp.bfloat16):
    array = spread * jax.random.normal(own_key, extent, jnp.float32)
    if shards:
        array = array * steps_of(own_key, extent, shards, -0.22, 0.18)
    return jnp.clip(array, -reach, reach).astype(kind)


def setup_inputs(seed: int = 0) -> dict:
    arg_keys = jax.random.split(jax.random.key(seed), 4)
    right_side = normal_values(arg_keys[0], (NZ, NX, NY), 1.0, 6.0, ((1, 16), (2, 2)), jnp.float32)
    diffusivity = jnp.clip(jnp.exp(math.log(5.0) - 3.218876 * jax.random.uniform(arg_keys[1], (NZ, NX, NY), jnp.float32) ** steps_of(arg_keys[1], (NZ, NX, NY), ((1, 16), (2, 2)), -0.2, 0.2)), 0.2, 5.0)
    reaction = jnp.clip(jnp.exp(math.log(0.2) - 2.9957323 * jax.random.uniform(arg_keys[2], (NZ, NX, NY), jnp.float32) ** steps_of(arg_keys[2], (NZ, NX, NY), ((1, 16), (2, 2)), -0.2, 0.2)), 0.01, 0.2)
    return {"right_side": right_side, "diffusivity": diffusivity, "reaction": reaction}


relax_weight = 0.8


def harmonic(first, second):
    return 2.0 * first * second / (first + second)


def face_terms(diffusivity, reaction, grid_level):
    padded = jnp.pad(diffusivity, ((1, 1), (1, 1), (1, 1)))
    face_scale = 0.25 ** grid_level
    west = face_scale * harmonic(diffusivity, padded[1:-1, :-2, 1:-1])
    east = face_scale * harmonic(diffusivity, padded[1:-1, 2:, 1:-1])
    south = face_scale * harmonic(diffusivity, padded[1:-1, 1:-1, :-2])
    north = face_scale * harmonic(diffusivity, padded[1:-1, 1:-1, 2:])
    upward = face_scale * harmonic(diffusivity, padded[:-2, 1:-1, 1:-1])
    downward = face_scale * harmonic(diffusivity, padded[2:, 1:-1, 1:-1])
    diagonal = west + east + south + north + upward + downward + face_scale * reaction
    return (west, east, south, north, upward, downward, diagonal)


def operate(field, coeffs):
    padded = jnp.pad(field, ((1, 1), (1, 1), (1, 1)))
    beside = coeffs[0] * padded[1:-1, :-2, 1:-1] + coeffs[1] * padded[1:-1, 2:, 1:-1]
    beside = beside + coeffs[2] * padded[1:-1, 1:-1, :-2] + coeffs[3] * padded[1:-1, 1:-1, 2:]
    beside = beside + coeffs[4] * padded[:-2, 1:-1, 1:-1] + coeffs[5] * padded[2:, 1:-1, 1:-1]
    return coeffs[6] * field - beside


def restrict(field):
    depth, first, second = field.shape
    return jnp.mean(field.reshape(depth, first // 2, 2, second // 2, 2), axis=(2, 4))


def prolong(field):
    return jnp.repeat(jnp.repeat(field, 2, axis=1), 2, axis=2)


def reference(right_side, diffusivity, reaction):
    source = right_side
    conduct = diffusivity
    binding = reaction
    saved = []
    for grid_level in range(LEVELS - 1):
        coeffs = face_terms(conduct, binding, grid_level)
        smooth_one = relax_weight * source / coeffs[6]
        defect = source - operate(smooth_one, coeffs)
        saved.append((source, smooth_one, conduct, binding))
        source = restrict(defect)
        conduct = restrict(conduct)
        binding = restrict(binding)
    coeffs = face_terms(conduct, binding, LEVELS - 1)
    iterate = relax_weight * source / coeffs[6]
    for sweep_index in range(COARSE_SWEEPS - 1):
        iterate = iterate + relax_weight * (source - operate(iterate, coeffs)) / coeffs[6]
    for grid_level in range(LEVELS - 2, -1, -1):
        source, smooth_one, conduct, binding = saved[grid_level]
        coeffs = face_terms(conduct, binding, grid_level)
        lifted = smooth_one + prolong(iterate)
        iterate = lifted + relax_weight * (source - operate(lifted, coeffs)) / coeffs[6]
    return iterate
```

```python
import functools

import jax
import jax.numpy as jnp
from jax import lax
from jax.experimental import pallas as pl
from jax.experimental.pallas import tpu as pltpu
from jax.sharding import PartitionSpec as P

LEVELS = 6
COARSE_SWEEPS = 3
LANES = 128
BORDER = 128
relax_weight = 0.8
f32 = jnp.float32
VMEM_LIMIT = 40 * 1024 * 1024


class Sizes:
    def __init__(self, depth, extent_x, extent_y, span_count, width_count):
        self.depth, self.extent_x, self.extent_y = depth, extent_x, extent_y
        self.span_count, self.width_count = span_count, width_count
        self.sides = min(width_count - 1, 2)
        self.used = [(extent_y + self.sides * BORDER) >> level for level in range(LEVELS)]
        self.held = [-(-used // LANES) * LANES for used in self.used]
        self.tiles = [held // LANES for held in self.held]
        self.slots = []
        start = 0
        for level in (0, 1, 1, 1, 2, 2, 2):
            self.slots.append((start, self.tiles[level]))
            start += self.tiles[level]
        self.message = (start, depth, LANES)


def put(message, slot, row):
    start, tiles = slot
    for tile in range(tiles):
        message[start + tile] = row[:, tile * LANES : (tile + 1) * LANES]


def get(message, slot):
    start, tiles = slot
    return jnp.concatenate([message[start + tile] for tile in range(tiles)], axis=1)


def roll(value, steps, axis):
    return pltpu.roll(value, steps % value.shape[axis], axis=axis)


def reciprocal(value):
    return pltpu.reciprocal(value, approx=True)


def harmonic(first, second, guard):
    total = first + second
    if guard:
        total = jnp.maximum(total, 1e-3)
    return (2.0 * first) * second * reciprocal(total)


def split(value):
    high = value.astype(jnp.bfloat16)
    return high, (value - high.astype(f32)).astype(jnp.bfloat16)


def pairs(fine, coarse, weight):
    fine_at = lax.broadcasted_iota(jnp.int32, (fine, coarse), 0)
    coarse_at = lax.broadcasted_iota(jnp.int32, (fine, coarse), 1)
    return jnp.where(fine_at // 2 == coarse_at, weight, 0.0).astype(jnp.bfloat16)


def pairs_up(coarse, fine, weight):
    coarse_at = lax.broadcasted_iota(jnp.int32, (coarse, fine), 0)
    fine_at = lax.broadcasted_iota(jnp.int32, (coarse, fine), 1)
    return jnp.where(fine_at // 2 == coarse_at, weight, 0.0).astype(jnp.bfloat16)


def dot(first, second):
    return jnp.dot(first, second, preferred_element_type=f32)


def narrow(sums, target, rows):
    depth, held = sums.shape[1], sums.shape[2]
    high, low = split(sums[0:rows].reshape(rows * depth, held))
    table = pairs(min(held, 2 * LANES), LANES, 0.25)
    for tile in range(target.shape[2] // LANES):
        start, stop = 2 * LANES * tile, min(2 * LANES * (tile + 1), held)
        part = table[: stop - start]
        result = dot(high[:, start:stop], part) + dot(low[:, start:stop], part)
        target[0:rows, :, tile * LANES : (tile + 1) * LANES] = result.reshape(rows, depth, LANES)


def widen(coarse, target, rows):
    depth, held = coarse.shape[1], target.shape[2]
    high, low = split(coarse.reshape(rows * depth, coarse.shape[2]))
    table = pairs_up(LANES, min(held, 2 * LANES), 4.0)
    for tile in range(coarse.shape[2] // LANES):
        start, stop = 2 * LANES * tile, min(2 * LANES * (tile + 1), held)
        if start >= stop:
            break
        part = table[:, : stop - start]
        mine = slice(tile * LANES, (tile + 1) * LANES)
        result = dot(high[:, mine], part) + dot(low[:, mine], part)
        target[0:rows, :, start:stop] = result.reshape(rows, depth, stop - start)


def coefficients(count, conduct, binding, fx, fy, fz, weight, used, guard):
    for row in range(1, count):
        fx[row - 1] = harmonic(conduct(row - 1), conduct(row), guard)
    for row in range(1, count - 1):
        mine = conduct(row)
        shape = mine.shape
        south = harmonic(mine, roll(mine, 1, 1), guard)
        if used == shape[1]:
            south = jnp.where(lax.broadcasted_iota(jnp.int32, shape, 1) == 0, 0.0, south)
        below = harmonic(mine, roll(mine, 1, 0), guard)
        below = jnp.where(lax.broadcasted_iota(jnp.int32, shape, 0) == 0, 0.0, below)
        diagonal = fx[row - 1] + fx[row] + binding(row)
        diagonal = diagonal + (south + roll(south, -1, 1)) + (below + roll(below, -1, 0))
        if guard:
            diagonal = jnp.maximum(diagonal, 1e-6)
        fy[row - 1] = south
        fz[row - 1] = below
        weight[row - 1] = relax_weight * reciprocal(diagonal)


def sweep(count, field, binding, fx, fy, fz, emit):
    lower = fx[0] * (field(1) - field(0))
    for row in range(1, count - 1):
        mine = field(row)
        upper = fx[row] * (field(row + 1) - mine)
        south = fy[row - 1] * (mine - roll(mine, 1, 1))
        below = fz[row - 1] * (mine - roll(mine, 1, 0))
        across = (south - roll(south, -1, 1)) + (below - roll(below, -1, 0))
        emit(row, binding(row) * mine + (lower - upper) + across)
        lower = upper


def own_defect(count, smooth, source, binding, fx, fy, fz, sums, first):
    zero = jnp.zeros(smooth.shape[1:], f32)

    def field(row):
        return smooth[row - 1] if 0 < row < count - 1 else zero

    def add(row, value):
        slot = (row + first) // 2
        if (row + first) % 2 == 0 or row == 0:
            sums[slot] = value
        else:
            sums[slot] = sums[slot] + value

    add(0, fx[0] * field(1))
    sweep(count, field, binding, fx, fy, fz, lambda row, result: add(row, source(row) - result))
    add(count - 1, fx[count - 2] * field(count - 2))


def start_kernel(sizes, place, right_side, conduct, binding, *out):
    rows, sends = out[:3], out[3:]
    last = sizes.extent_y - BORDER
    for index, array in enumerate((conduct, binding, right_side)):
        turned = jnp.swapaxes(array[...], 0, 1)
        rows[index][...] = turned
        if sizes.width_count == 2:

            @pl.when(place[1] == 0)
            def _():
                sends[0][index] = turned[:, :, last:]

            @pl.when(place[1] == 1)
            def _():
                sends[0][index] = turned[:, :, :BORDER]

        elif sizes.width_count > 2:
            sends[0][index] = turned[:, :, last:]
            sends[1][index] = turned[:, :, :BORDER]


def border_kernel(sizes, place, conduct, binding, right_side, *refs):
    borders, refs = refs[: sizes.sides], refs[sizes.sides :]
    wide, refs = refs[:3], refs[3:]
    conducts, bindings, to_next, to_prev, sums = refs[0:3], refs[3:6], refs[6], refs[7], refs[8]
    for index, (array, target) in enumerate(zip((conduct, binding, right_side), wide)):
        if sizes.sides == 0:
            target[...] = array[...]
        elif sizes.sides == 1:

            @pl.when(place[1] == 0)
            def _():
                target[:, :, : sizes.extent_y] = array[...]
                target[:, :, sizes.extent_y :] = borders[0][index]

            @pl.when(place[1] == 1)
            def _():
                target[:, :, :BORDER] = borders[0][index]
                target[:, :, BORDER:] = array[...]

        else:
            target[:, :, :BORDER] = borders[0][index]
            target[:, :, BORDER : BORDER + sizes.extent_y] = array[...]
            target[:, :, BORDER + sizes.extent_y :] = borders[1][index]
    for fine, coarse in ((wide[0], conducts), (wide[1], bindings)):
        for level in range(3):
            count = coarse[level].shape[0]
            held = fine.shape[2]
            for row in range(count):
                sums[row, :, :held] = fine[2 * row] + fine[2 * row + 1]
            narrow(sums.at[:, :, :held], coarse[level], count)
            fine = coarse[level]
    c1, c2 = conducts[0], conducts[1]
    b1, b2 = bindings[0], bindings[1]
    high = sizes.extent_x - 1
    half = sizes.extent_x // 2 - 1
    for message, rows in (
        (to_next, (wide[0][high], c1[half - 1], c1[half], b1[half], c2[0], c2[1], b2[1])),
        (to_prev, (wide[0][0], c1[0], c1[1], b1[0], c2[0], c2[1], b2[0])),
    ):
        for slot, row in zip(sizes.slots, rows):
            put(message, slot, row)


def down_kernel(sizes, *refs):
    (source0, c0, b0, c1, b1, c2, b2, c3, b3, from_prev, from_next), refs = refs[:11], refs[11:]
    gathered, to_next, to_prev, to_next_2, to_prev_2 = refs[:5]
    v0, level0, level1, level2 = refs[5], refs[6:10], refs[10:17], refs[17:24]
    sums = refs[24]
    slots = sizes.slots
    guard = sizes.sides > 1
    n0, n1, n2 = (sizes.extent_x >> level for level in range(3))

    def conduct0(row):
        if row == 0:
            return get(from_prev, slots[0])
        if row == n0 + 1:
            return get(from_next, slots[0])
        return c0[row - 1]

    def bordered(array, count, first, second):
        def at(row):
            if row < 2:
                return get(from_prev, slots[first + row])
            if row >= count + 2:
                return get(from_next, slots[first + row - count - 2])
            return array[row - 2]

        return at

    def single(array, count, slot):
        def at(row):
            if row == 1:
                return get(from_prev, slots[slot])
            if row == count + 2:
                return get(from_next, slots[slot])
            return array[row - 2]

        return at

    fx, fy, fz, weight = level0
    coefficients(n0 + 2, conduct0, lambda row: b0[row - 1], fx, fy, fz, weight, sizes.used[0], guard)
    for row in range(n0):
        v0[row] = weight[row] * source0[row]
    own_defect(n0 + 2, v0, lambda row: source0[row - 1], lambda row: b0[row - 1], fx, fy, fz, sums, 1)
    fine_held = sizes.held[0]
    count = n1 + 2
    for level, n, array, bind, refs_of, slot in (
        (1, n1, c1, b1, level1, 1),
        (2, n2, c2, b2, level2, 4),
    ):
        fx, fy, fz, weight, binding, source, smooth = refs_of
        held = sizes.held[level]
        narrow(sums.at[:, :, :fine_held], source, n + 2)
        lookup = single(bind, n, slot + 2)
        for row in range(1, n + 3):
            binding[row - 1] = lookup(row)
        bound = lambda row, binding=binding: binding[row - 1]
        coefficients(n + 4, bordered(array, n, slot, slot + 1), bound, fx, fy, fz, weight, sizes.used[level], True)
        for row in range(n + 2):
            smooth[row] = weight[row] * source[row]
        own_defect(
            n + 4, smooth, lambda row, source=source: source[row - 1], bound, fx, fy, fz, sums.at[:, :, :held], 0
        )
        fine_held = held
    narrow(sums.at[:, :, :fine_held], gathered, 3)
    gathered[3] = c3[0]
    gathered[4] = b3[0]
    s1, v1 = level1[5], level1[6]
    s2, v2 = level2[5], level2[6]
    for message, rows in (
        (to_next, (v0[n0 - 1], s1[n1], s1[n1 + 1], v1[n1 - 1], s2[n2], s2[n2 + 1], v2[n2 - 1])),
        (to_prev, (v0[0], s1[1], s1[0], v1[2], s2[1], s2[0], v2[2])),
    ):
        for slot, row in zip(slots, rows):
            put(message, slot, row)
    put(to_next_2, (0, sizes.tiles[2]), v2[n2 + 1])
    put(to_prev_2, (0, sizes.tiles[2]), v2[0])


def up_kernel(sizes, place, gathered, from_prev, from_next, from_prev_2, from_next_2, source0, b0, v0, *refs):
    level0, level1, level2, out, scratch = refs[0:4], refs[4:11], refs[11:18], refs[18], refs[19:]
    slots = sizes.slots
    n0, n1, n2 = (sizes.extent_x >> level for level in range(3))
    total = sizes.span_count
    sums = scratch[0]
    coarse = [scratch[1 + 9 * index : 10 + 9 * index] for index in range(3)]
    wide2, wide1, wide0, lift2, lift1, lift0, it2, it1, it0 = scratch[28:37]
    zero = jnp.zeros(gathered.shape[2:], f32)

    for index in range(3):
        level = 3 + index
        fx, fy, fz, weight, conduct, binding, source, smooth, iterate = coarse[index]
        count = total >> index
        for array in (conduct, smooth, iterate):
            array[0] = zero
            array[count + 1] = zero
        if index == 0:
            for row in range(count):
                conduct[row + 1] = gathered[row, 3]
                binding[row] = gathered[row, 4]
                value = gathered[row, 1]
                if row > 0:
                    value = value + gathered[row - 1, 2]
                if row < count - 1:
                    value = value + gathered[row + 1, 0]
                source[row] = value
        bound = lambda row, binding=binding: binding[row - 1]
        coefficients(
            count + 2, lambda row, conduct=conduct: conduct[row], bound, fx, fy, fz, weight, sizes.used[level], True
        )
        for row in range(count):
            smooth[row + 1] = weight[row] * source[row]
        if index < 2:
            _, _, _, _, conduct_next, binding_next, source_next = coarse[index + 1][:7]
            for row in range(count // 2):
                sums[row, :, :LANES] = conduct[2 * row + 1] + conduct[2 * row + 2]
            narrow(sums.at[:, :, :LANES], conduct_next.at[1 : count // 2 + 1], count // 2)
            for row in range(count // 2):
                sums[row, :, :LANES] = binding[2 * row] + binding[2 * row + 1]
            narrow(sums.at[:, :, :LANES], binding_next, count // 2)

            def add(row, result, source=source):
                value = source[row - 1] - result
                slot = (row - 1) // 2
                if row % 2 == 1:
                    sums[slot, :, :LANES] = value
                else:
                    sums[slot, :, :LANES] = sums[slot, :, :LANES] + value

            sweep(count + 2, lambda row, smooth=smooth: smooth[row], bound, fx, fy, fz, add)
            narrow(sums.at[:, :, :LANES], source_next, count // 2)

    fx, fy, fz, weight, conduct, binding, source, smooth, iterate = coarse[2]
    held, other = smooth, iterate
    for _ in range(COARSE_SWEEPS - 1):

        def relax(row, result, held=held, other=other):
            other[row] = held[row] + weight[row - 1] * (source[row - 1] - result)

        sweep((total >> 2) + 2, lambda row, held=held: held[row], lambda row: binding[row - 1], fx, fy, fz, relax)
        held, other = other, held
    for index in (1, 0):
        fx, fy, fz, weight, conduct, binding, source, smooth, iterate = coarse[index]
        count = total >> index
        widen(held[1 : count // 2 + 1], sums.at[:, :, :LANES], count // 2)
        for row in range(count):
            smooth[row + 1] = smooth[row + 1] + sums[row // 2, :, :LANES]

        def relax(row, result, smooth=smooth, iterate=iterate, weight=weight, source=source):
            iterate[row] = smooth[row] + weight[row - 1] * (source[row - 1] - result)

        sweep(
            count + 2,
            lambda row, smooth=smooth: smooth[row],
            lambda row, binding=binding: binding[row - 1],
            fx,
            fy,
            fz,
            relax,
        )
        held = iterate

    widen(held[pl.ds(place[0], 3)], wide2, 3)
    for level, n, refs_of, slot, wide, lift, result_rows, upper in (
        (2, n2, level2, 4, wide2, lift2, it2, wide1),
        (1, n1, level1, 1, wide1, lift1, it1, wide0),
    ):
        fx, fy, fz, weight, binding, own, smooth = refs_of

        def source(row, own=own, slot=slot, n=n):
            value = own[row - 1]
            if row in (1, 2):
                value = value + get(from_prev, slots[slot + row - 1])
            if row in (n + 1, n + 2):
                value = value + get(from_next, slots[slot + n + 2 - row])
            return value

        for row in range(n + 4):
            if row == 0:
                value = get(from_prev, slots[slot + 2])
                if level == 2:
                    value = value + get(from_prev_2, (0, sizes.tiles[2]))
            elif row == n + 3:
                value = get(from_next, slots[slot + 2])
                if level == 2:
                    value = value + get(from_next_2, (0, sizes.tiles[2]))
            elif row in (1, 2, n + 1, n + 2):
                value = weight[row - 1] * source(row)
            else:
                value = smooth[row - 1]
            lift[row] = value + wide[row // 2]

        def relax(row, result, lift=lift, weight=weight, source=source, result_rows=result_rows):
            result_rows[row - 1] = lift[row] + weight[row - 1] * (source(row) - result)

        sweep(
            n + 4,
            lambda row, lift=lift: lift[row],
            lambda row, binding=binding: binding[row - 1],
            fx,
            fy,
            fz,
            relax,
        )
        widen(result_rows[...], upper, n + 2)

    fx, fy, fz, weight = level0
    lift0[0] = get(from_prev, slots[0]) + wide0[0]
    lift0[n0 + 1] = get(from_next, slots[0]) + wide0[n1 + 1]
    for row in range(1, n0 + 1):
        lift0[row] = v0[row - 1] + wide0[(row + 1) // 2]

    def relax0(row, result):
        it0[row - 1] = lift0[row] + weight[row - 1] * (source0[row - 1] - result)

    sweep(n0 + 2, lambda row: lift0[row], lambda row: b0[row - 1], fx, fy, fz, relax0)
    if sizes.sides == 1:

        @pl.when(place[1] == 0)
        def _():
            out[...] = jnp.swapaxes(it0[:, :, : sizes.extent_y], 0, 1)

        @pl.when(place[1] == 1)
        def _():
            out[...] = jnp.swapaxes(it0[:, :, BORDER:], 0, 1)

    else:
        start = BORDER if sizes.sides else 0
        out[...] = jnp.swapaxes(it0[:, :, start : start + sizes.extent_y], 0, 1)


def call(body, sizes, name, outputs, scratch, inputs, scalars=0):
    in_specs = [pl.BlockSpec(memory_space=pltpu.SMEM)] * scalars
    in_specs += [pl.BlockSpec(memory_space=pltpu.VMEM)] * (len(inputs) - scalars)
    return pl.pallas_call(
        functools.partial(body, sizes),
        name=name,
        out_shape=[jax.ShapeDtypeStruct(shape, f32) for shape in outputs],
        in_specs=in_specs,
        out_specs=[pl.BlockSpec(memory_space=pltpu.VMEM)] * len(outputs),
        scratch_shapes=[pltpu.VMEM(shape, f32) for shape in scratch],
        compiler_params=pltpu.CompilerParams(vmem_limit_bytes=VMEM_LIMIT),
    )(*inputs)


def along(value, axis, steps):
    count = lax.axis_size(axis)
    initial, last = max(0, -steps), min(count, count - steps)
    return lax.ppermute(value, axis, [(source, source + steps) for source in range(initial, last)])


def on_device(right_side, diffusivity, reaction):
    depth, extent_x, extent_y = diffusivity.shape
    sizes = Sizes(depth, extent_x, extent_y, lax.axis_size("span"), lax.axis_size("width"))
    place = jnp.stack([lax.axis_index("span"), lax.axis_index("width")]).astype(jnp.int32)
    own = (extent_x, depth, extent_y)
    edge = (3, extent_x, depth, BORDER)
    started = call(
        start_kernel,
        sizes,
        "start",
        [own] * 3 + [edge] * sizes.sides,
        [],
        [place, right_side, diffusivity, reaction],
        1,
    )
    if sizes.sides == 0:
        borders = []
    elif sizes.sides == 1:
        borders = [lax.ppermute(started[3], "width", [(0, 1), (1, 0)])]
    else:
        borders = [along(started[3], "width", 1), along(started[4], "width", -1)]

    def shape(level, rows):
        return (rows, depth, sizes.held[level])

    n0, n1, n2, n3 = (extent_x >> level for level in range(4))
    coarse = [shape(1, n1), shape(2, n2), shape(3, n3)]
    bordered = call(
        border_kernel,
        sizes,
        "border",
        [shape(0, n0)] * 3 + coarse * 2 + [sizes.message] * 2,
        [shape(0, n1)],
        [place, *started[:3], *borders],
        1,
    )
    (c0, b0, r0), (c1, c2, c3), (b1, b2, b3) = bordered[0:3], bordered[3:6], bordered[6:9]
    from_prev = along(bordered[9], "span", 1)
    from_next = along(bordered[10], "span", -1)

    def level_shapes(level, n):
        return [shape(level, n + 3)] + [shape(level, n + 2)] * 6

    far = (sizes.tiles[2], depth, LANES)
    part = (5, depth, LANES)
    coefficient_shapes = [shape(0, n0 + 1)] + [shape(0, n0)] * 3
    coefficient_shapes += level_shapes(1, n1) + level_shapes(2, n2)
    downs = call(
        down_kernel,
        sizes,
        "down",
        [part, sizes.message, sizes.message, far, far, shape(0, n0)] + coefficient_shapes,
        [shape(0, n1 + 2)],
        [r0, c0, b0, c1, b1, c2, b2, c3, b3, from_prev, from_next],
    )
    gathered = lax.all_gather(downs[0], "span", axis=0, tiled=False)
    from_prev = along(downs[1], "span", 1)
    from_next = along(downs[2], "span", -1)
    from_prev_2 = along(downs[3], "span", 2)
    from_next_2 = along(downs[4], "span", -2)
    scratch = [(max(sizes.span_count, n1 + 2), depth, sizes.held[0])]
    for index in range(3):
        count = sizes.span_count >> index
        scratch += [(count + 1, depth, LANES)] + [(count, depth, LANES)] * 3
        scratch += [(count + 2, depth, LANES), (count, depth, LANES), (count, depth, LANES)]
        scratch += [(count + 2, depth, LANES)] * 2
    scratch += [shape(2, n3 + 2), shape(1, n2 + 2), shape(0, n1 + 2)]
    scratch += [shape(2, n2 + 4), shape(1, n1 + 4), shape(0, n0 + 2)]
    scratch += [shape(2, n2 + 2), shape(1, n1 + 2), shape(0, n0)]
    (correction,) = call(
        up_kernel,
        sizes,
        "up",
        [diffusivity.shape],
        scratch,
        [place, gathered, from_prev, from_next, from_prev_2, from_next_2, r0, b0, *downs[5:]],
        1,
    )
    return correction


def solution(mesh):
    in_specs = (P(None, "span", "width"),) * 3
    return jax.shard_map(
        on_device, mesh=mesh, in_specs=in_specs, out_specs=P(None, "span", "width"), check_vma=False
    )
```

```python
import functools

import jax
import jax.numpy as jnp
from jax import lax
from jax.experimental import pallas as pl
from jax.experimental.pallas import tpu as pltpu
from jax.sharding import PartitionSpec as P

LEVELS = 6
COARSE_SWEEPS = 3
LANES = 128
BORDER = 128
FRINGE = 4
SPREAD = 16
relax_weight = 0.8
f32 = jnp.float32
VMEM_LIMIT = 40 * 1024 * 1024


class Sizes:
    def __init__(self, depth, extent_x, extent_y, span_count, width_count):
        self.depth, self.extent_x, self.extent_y = depth, extent_x, extent_y
        self.span_count, self.width_count = span_count, width_count
        self.sides = min(width_count - 1, 2)
        self.own = [(extent_y >> level) // LANES for level in range(3)]
        self.border = [self.sides, min(self.sides, 1), min(self.sides, 1)]
        self.held = [(self.own[level] + self.border[level]) * LANES for level in range(3)] + [LANES] * 3
        self.rows = [extent_x >> level for level in range(4)]
        self.slots = []
        start = 0
        for level in (0, 1, 1, 1, 2, 2, 2):
            self.slots.append((start, self.own[level]))
            start += self.own[level]
        self.tiles = start


class Copies:
    def __init__(self, semaphores):
        self.semaphores, self.used = semaphores, 0

    def start(self, source, target):
        copy = pltpu.make_async_copy(source, target, self.semaphores.at[self.used])
        self.used += 1
        copy.start()
        return copy


def wait(copies):
    for copy in copies:
        copy.wait()


def put(message, slot, row):
    start, tiles = slot
    for tile in range(tiles):
        message[start + tile] = row[:, tile * LANES : (tile + 1) * LANES]


def get(message, slot):
    start, tiles = slot
    return [message[start + tile] for tile in range(tiles)]


def lane_at(shape):
    return lax.broadcasted_iota(jnp.int32, shape, len(shape) - 1)


def roll(value, steps, axis):
    return pltpu.roll(value, steps % value.shape[axis], axis=axis)


def reciprocal(value):
    return pltpu.reciprocal(value, approx=True)


def harmonic(first, second, guard):
    total = first + second
    if guard:
        total = jnp.maximum(total, 1e-3)
    return (2.0 * first) * second * reciprocal(total)


def split(value):
    high = value.astype(jnp.bfloat16)
    return high, (value - high.astype(f32)).astype(jnp.bfloat16)


def dot(halves, table):
    high, low = halves
    return jnp.dot(high, table, preferred_element_type=f32) + jnp.dot(low, table, preferred_element_type=f32)


def pair_table(fine, fine_dim, turn, weight):
    shape = (fine, LANES) if fine_dim == 0 else (LANES, fine)
    fine_at = lax.broadcasted_iota(jnp.int32, shape, fine_dim)
    coarse_at = lax.broadcasted_iota(jnp.int32, shape, 1 - fine_dim)
    if turn is not None:
        coarse_at = coarse_at - jnp.where(fine_at >= turn, LANES // 2, 0)
    return jnp.where(fine_at // 2 == coarse_at, weight, 0.0).astype(jnp.bfloat16)


def turns(sizes, place, level):
    if sizes.sides == 0:
        return []
    if level == 0:
        return [jnp.where(place[1] == 0, LANES, 0)] if sizes.sides == 1 else [LANES, 0]
    return [LANES // 2]


def transfer_plan(sizes, place, level, part):
    plan = []
    if level >= 3:
        return [((0, LANES), 0, 3 * LANES // 4)]
    if level == 2:
        return [((0, sizes.held[2]), 0, None)]
    own = sizes.own[level]
    if part != "border":
        plan += [((2 * LANES * tile, 2 * LANES * (tile + 1)), tile, None) for tile in range(own // 2)]
    if part != "own":
        for index, turn in enumerate(turns(sizes, place, level)):
            start = (own + index) * LANES
            plan.append(((start, start + LANES), own // 2, turn))
    return plan


def narrow(sizes, place, level, sums, target, rows, part="all", shift=0):
    depth = sums.shape[1]
    done = {}
    for (start, stop), tile, turn in transfer_plan(sizes, place, level, part):
        start, stop, tile = start - shift, stop - shift, tile - shift // (2 * LANES)
        columns = split(sums[0:rows, :, start:stop].reshape(rows * depth, stop - start))
        result = dot(columns, pair_table(stop - start, 0, turn, 0.25)).reshape(rows, depth, LANES)
        done[tile] = done[tile] + result if tile in done else result
    for tile, result in done.items():
        target[0:rows, :, tile * LANES : (tile + 1) * LANES] = result


def widen(sizes, place, level, coarse, target, rows):
    depth = coarse.shape[1]
    for (start, stop), tile, turn in transfer_plan(sizes, place, level, "all"):
        columns = split(coarse[0:rows, :, tile * LANES : (tile + 1) * LANES].reshape(rows * depth, LANES))
        result = dot(columns, pair_table(stop - start, 1, turn, 4.0))
        target[0:rows, :, start:stop] = result.reshape(rows, depth, stop - start)


def coefficients(sizes, place, level, count, conduct, binding, fx, fy, fz, weight):
    guard = level > 0 or sizes.sides > 1
    for row in range(1, count):
        fx[row - 1] = harmonic(conduct(row - 1), conduct(row), guard)
    for row in range(1, count - 1):
        mine = conduct(row)
        south = harmonic(mine, roll(mine, 1, 1), guard)
        if level == 0 and sizes.sides < 2:
            cut = 0 if sizes.sides == 0 else jnp.where(place[1] == 0, 0, sizes.extent_y)
            south = jnp.where(lane_at(mine.shape) == cut, 0.0, south)
        below = harmonic(mine, roll(mine, 1, 0), guard)
        below = jnp.where(lax.broadcasted_iota(jnp.int32, mine.shape, 0) == 0, 0.0, below)
        diagonal = fx[row - 1] + fx[row] + binding(row)
        diagonal = diagonal + (south + roll(south, -1, 1)) + (below + roll(below, -1, 0))
        if guard:
            diagonal = jnp.maximum(diagonal, 1e-6)
        fy[row - 1] = south
        fz[row - 1] = below
        weight[row - 1] = relax_weight * reciprocal(diagonal)


def sweep(count, field, binding, fx, fy, fz, emit):
    lower = fx[0] * (field(1) - field(0))
    for row in range(1, count - 1):
        mine = field(row)
        upper = fx[row] * (field(row + 1) - mine)
        south = fy[row - 1] * (mine - roll(mine, 1, 1))
        below = fz[row - 1] * (mine - roll(mine, 1, 0))
        across = (south - roll(south, -1, 1)) + (below - roll(below, -1, 0))
        emit(row, binding(row) * mine + (lower - upper) + across)
        lower = upper


def own_defect(count, smooth, source, binding, fx, fy, fz, sums, first):
    zero = jnp.zeros(smooth.shape[1:], f32)

    def field(row):
        return smooth[row - 1] if 0 < row < count - 1 else zero

    def add(row, value):
        slot = (row + first) // 2
        if (row + first) % 2 == 0 or row == 0:
            sums[slot] = value
        else:
            sums[slot] = sums[slot] + value

    add(0, fx[0] * field(1))
    sweep(count, field, binding, fx, fy, fz, lambda row, result: add(row, source(row) - result))
    add(count - 1, fx[count - 2] * field(count - 2))


def parts(array, counts):
    views, start = [], 0
    for count in counts:
        views.append(array.at[start : start + count])
        start += count
    return views


def coefficient_rows(sizes, level):
    n = sizes.rows[level]
    if level == 0:
        return [n + 1, n, n, n, n]
    return [n + 3] + [n + 2] * 6


def start_kernel(sizes, place, right_side, conduct, binding, own0, own1, own2, to_next, to_prev, *refs):
    sends, refs = refs[: sizes.sides], refs[sizes.sides :]
    inputs, turned, level1, level2, next_out, prev_out = refs[:6]
    edges, sums, semaphores = refs[6 : 6 + sizes.sides], refs[-2], refs[-1]
    copies = Copies(semaphores)
    loads = [copies.start(array, inputs.at[at]) for at, array in enumerate((conduct, binding, right_side))]
    n0, n1, n2 = sizes.rows[:3]
    last = sizes.extent_y - BORDER

    def turn(at):
        loads[at].wait()
        turned[at] = jnp.swapaxes(inputs[at], 0, 1)

    for at in (0, 1):
        turn(at)
        for row in range(n1):
            sums[row] = turned[at, 2 * row] + turned[at, 2 * row + 1]
        narrow(sizes, place, 0, sums, level1.at[at], n1, "own")
        for row in range(n2):
            sums[row, :, : sizes.own[1] * LANES] = level1[at, 2 * row] + level1[at, 2 * row + 1]
        narrow(sizes, place, 1, sums, level2.at[at], n2, "own")
    for message, low, at1, at0 in ((next_out, n1 - 2, n1 - 1, n0 - 1), (prev_out, 0, 0, 0)):
        edge = n2 - 1 if at0 else 0
        rows = (turned[0, at0], level1[0, low], level1[0, low + 1], level1[1, at1])
        rows += (level2[0, n2 - 2], level2[0, n2 - 1], level2[1, edge])
        for slot, row in zip(sizes.slots, rows):
            put(message, slot, row)
    out = [copies.start(next_out, to_next), copies.start(prev_out, to_prev)]
    turn(2)
    out += [copies.start(turned, own0), copies.start(level1, own1), copies.start(level2, own2)]
    if sizes.sides == 1:
        at = pl.multiple_of(jnp.where(place[1] == 0, last, 0), LANES)
        edges[0][...] = turned[:, :, :, pl.ds(at, BORDER)]
    elif sizes.sides == 2:
        edges[0][...] = turned[:, :, :, last:]
        edges[1][...] = turned[:, :, :, :BORDER]
    for edge, send in zip(edges, sends):
        out.append(copies.start(edge, send))
    wait(out)


def border_kernel(sizes, place, own2, *refs):
    borders, refs = refs[: sizes.sides], refs[sizes.sides :]
    border1, border2, top = refs[:3]
    fine, level1, whole2, level3, sums, semaphores = refs[3:]
    copies = Copies(semaphores)
    n1, n2 = sizes.rows[1:3]
    own = sizes.own[2] * LANES
    loads = [copies.start(array.at[0:2], fine.at[side]) for side, array in enumerate(borders)]
    loads.append(copies.start(own2, whole2.at[:, :, :, :own]))
    wait(loads)
    out = []
    for at in (0, 1):
        if sizes.sides:
            for row in range(n1):
                for side in range(sizes.sides):
                    columns = slice(side * LANES, (side + 1) * LANES)
                    sums[row, :, columns] = fine[side, at, 2 * row] + fine[side, at, 2 * row + 1]
            narrow(sizes, place, 0, sums, level1.at[at], n1, "border", sizes.own[0] * LANES)
            for row in range(n2):
                sums[row, :, :LANES] = level1[at, 2 * row] + level1[at, 2 * row + 1]
            narrow(sizes, place, 1, sums, whole2.at[at, :, :, own:], n2, "border", sizes.own[1] * LANES)
        sums[0, :, : sizes.held[2]] = whole2[at, 0] + whole2[at, 1]
        narrow(sizes, place, 2, sums, level3.at[at : at + 1], 1)
    out.append(copies.start(level3, top))
    if sizes.sides:
        out.append(copies.start(level1, border1))
        out.append(copies.start(whole2.at[:, :, :, own:], border2))
    wait(out)


def message_row(sizes, place, level, slot, message, beside):
    start, tiles = slot
    row = get(message, slot)
    if sizes.sides == 1:
        left = place[1] != 0
        tile = beside[0][start + jnp.where(left, tiles - 1, 0)]
        if level > 0:
            reach = BORDER >> level
            lane = lane_at(tile.shape)
            first = jnp.where(left, LANES - reach, 0)
            tile = jnp.where((lane >= first) & (lane < first + reach), tile, 0.0)
        row.append(tile)
    elif sizes.sides == 2:
        right, left = beside[0][start], beside[1][start + tiles - 1]
        if level == 0:
            row += [right, left]
        else:
            reach = BORDER >> level
            lane = lane_at(right.shape)
            row.append(jnp.where(lane < reach, right, jnp.where(lane >= LANES - reach, left, 0.0)))
    return jnp.concatenate(row, axis=1)


def fringe_lanes(shape):
    lane = lane_at(shape)
    return (lane < FRINGE) | (lane >= LANES - FRINGE)


def put_fringes(sizes, message, rows):
    total = None
    for index, (level, row) in enumerate(rows):
        tile = row[:, sizes.own[level] * LANES :]
        tile = jnp.where(fringe_lanes(tile.shape), tile, 0.0)
        tile = roll(tile, SPREAD * index + SPREAD // 2, 1)
        total = tile if total is None else total + tile
    message[sizes.tiles] = total


def fringed_row(sizes, level, index, message):
    row = get(message, sizes.slots[index])
    if sizes.border[level]:
        if level == 0:
            row += [jnp.zeros(row[0].shape, f32)] * sizes.border[0]
        else:
            tile = roll(message[sizes.tiles], -(SPREAD * (index - 1) + SPREAD // 2), 1)
            row.append(jnp.where(fringe_lanes(tile.shape), tile, 0.0))
    return jnp.concatenate(row, axis=1)


def down_kernel(sizes, place, *refs):
    s = sizes.sides
    own0, own1, own2 = refs[:3]
    borders0, refs = refs[3 : 3 + s], refs[3 + s :]
    if s:
        (border1, border2), refs = refs[:2], refs[2:]
    halo_refs, refs = refs[: 2 * (1 + s)], refs[2 * (1 + s) :]
    coefs, contribution, ups, fars, refs = refs[:3], refs[3], refs[4:6], refs[6:8], refs[8:]
    wides, halos, refs = refs[:3], refs[3], refs[4:]
    rows_of, level3, up_rows, far_rows, sums, semaphores = refs[:3], refs[3], refs[4], refs[5], refs[6], refs[7]
    copies = Copies(semaphores)
    slots = sizes.slots
    n0, n1, n2 = sizes.rows[:3]

    def load(level, own, borders):
        width = sizes.own[level] * LANES
        started = [copies.start(own, wides[level].at[:, :, :, :width])]
        for index, border in enumerate(borders):
            start = width + index * LANES
            started.append(copies.start(border, wides[level].at[:, :, :, start : start + LANES]))
        return started

    loads = [copies.start(array, halos.at[at]) for at, array in enumerate(halo_refs)]
    loads += load(0, own0, borders0)
    later = load(1, own1, (border1,) if s else ()) + load(2, own2, (border2,) if s else ())
    wait(loads)
    from_prev, beside_prev = halos.at[0], [halos.at[2 + 2 * side] for side in range(s)]
    from_next, beside_next = halos.at[1], [halos.at[3 + 2 * side] for side in range(s)]
    c0, b0, r0 = (wides[0].at[at] for at in range(3))

    def prev_row(level, index):
        return message_row(sizes, place, level, slots[index], from_prev, beside_prev)

    def next_row(level, index):
        return message_row(sizes, place, level, slots[index], from_next, beside_next)

    def conduct0(row):
        if row == 0:
            return prev_row(0, 0)
        if row == n0 + 1:
            return next_row(0, 0)
        return c0[row - 1]

    fx, fy, fz, weight, v0 = parts(rows_of[0], coefficient_rows(sizes, 0))
    coefficients(sizes, place, 0, n0 + 2, conduct0, lambda row: b0[row - 1], fx, fy, fz, weight)
    for row in range(n0):
        v0[row] = weight[row] * r0[row]
    out = [copies.start(rows_of[0], coefs[0])]
    own_defect(n0 + 2, v0, lambda row: r0[row - 1], lambda row: b0[row - 1], fx, fy, fz, sums, 1)
    wait(later)
    smooths, sources = [], []
    for level, first in ((1, 1), (2, 4)):
        n = sizes.rows[level]
        conducts, bindings = wides[level].at[0], wides[level].at[1]
        fx, fy, fz, weight, binding, source, smooth = parts(rows_of[level], coefficient_rows(sizes, level))
        held = sizes.held[level]
        narrow(sizes, place, level - 1, sums.at[:, :, : sizes.held[level - 1]], source, n + 2)
        binding[0] = prev_row(level, first + 2)
        binding[n + 1] = next_row(level, first + 2)
        for row in range(n):
            binding[row + 1] = bindings[row]

        def conduct(row, n=n, level=level, first=first, conducts=conducts):
            if row < 2:
                return prev_row(level, first + row)
            if row >= n + 2:
                return next_row(level, first + row - n - 2)
            return conducts[row - 2]

        bound = lambda row, binding=binding: binding[row - 1]
        coefficients(sizes, place, level, n + 4, conduct, bound, fx, fy, fz, weight)
        for row in range(n + 2):
            smooth[row] = weight[row] * source[row]
        out.append(copies.start(rows_of[level], coefs[level]))
        mine = lambda row, source=source: source[row - 1]
        own_defect(n + 4, smooth, mine, bound, fx, fy, fz, sums.at[:, :, :held], 0)
        smooths.append(smooth)
        sources.append(source)
    narrow(sizes, place, 2, sums.at[:, :, : sizes.held[2]], level3, 3)
    out.append(copies.start(level3, contribution))
    (s1, s2), (v1, v2) = sources, smooths
    for at, rows in enumerate(
        (
            (v0[n0 - 1], s1[n1], s1[n1 + 1], v1[n1 - 1], s2[n2], s2[n2 + 1], v2[n2 - 1]),
            (v0[0], s1[1], s1[0], v1[2], s2[1], s2[0], v2[2]),
        )
    ):
        message = up_rows.at[at]
        for slot, row in zip(slots, rows):
            put(message, slot, row)
        if s:
            put_fringes(sizes, message, list(zip((1, 1, 1, 2, 2, 2), rows[1:])))
        out.append(copies.start(message, ups[at]))
        put(far_rows.at[at], (0, sizes.held[2] // LANES), v2[n2 + 1 if at == 0 else 0])
        out.append(copies.start(far_rows.at[at], fars[at]))
    wait(out)


def merge_into(place, stride, radix, arrays, target):
    position = (place[0] // stride) % radix
    target[...] = jnp.zeros(target.shape, f32)
    for step, array in enumerate(arrays):
        at = (position ^ step) * stride
        rows = pl.ds(at, stride + 2)
        target[rows] = target[rows] + array[...]


def merge_kernel(sizes, stride, radix, place, *refs):
    inputs, out, refs = refs[:radix], refs[radix], refs[radix + 1 :]
    arrays, total, semaphores = refs[:radix], refs[radix], refs[radix + 1]
    copies = Copies(semaphores)
    wait([copies.start(source, target) for source, target in zip(inputs, arrays)])
    merge_into(place, stride, radix, arrays, total)
    wait([copies.start(total, out)])


def up_kernel(sizes, stride, radix, place, *refs):
    s = sizes.sides
    sources, refs = refs[:radix], refs[radix:]
    tops, refs = refs[:radix], refs[radix:]
    halos, coefs, own0, borders0, out = refs[:4], refs[4:7], refs[7], refs[8 : 8 + s], refs[8 + s]
    scratch = refs[9 + s :]
    source_rows, top_rows, messages, fars, rows0, wide0, rows1, rows2, merged, sums, result = scratch[:11]
    coarse = [scratch[11 + 9 * index : 20 + 9 * index] for index in range(3)]
    over2, over1, over0, lift2, lift1, lift0, it2, it1, it0 = scratch[38:47]
    semaphores = scratch[47]
    copies = Copies(semaphores)
    slots = sizes.slots
    n0, n1, n2 = sizes.rows[:3]
    total = sizes.span_count
    loads = [copies.start(array, source_rows.at[step]) for step, array in enumerate(sources)]
    loads += [copies.start(array, top_rows.at[step]) for step, array in enumerate(tops)]
    later = [copies.start(array, messages.at[at]) for at, array in enumerate(halos[:2])]
    later += [copies.start(array, fars.at[at]) for at, array in enumerate(halos[2:])]
    for level in (2, 1, 0):
        later.append(copies.start(coefs[level], (rows0, rows1, rows2)[level]))
    width = sizes.own[0] * LANES
    later.append(copies.start(own0.at[1:3], wide0.at[:, :, :, :width]))
    for index, border in enumerate(borders0):
        start = width + index * LANES
        later.append(copies.start(border.at[1:3], wide0.at[:, :, :, start : start + LANES]))
    wait(loads)
    merge_into(place, stride, radix, [source_rows.at[step] for step in range(radix)], merged)

    zero = jnp.zeros((sizes.depth, LANES), f32)
    for index in range(3):
        level = 3 + index
        fx, fy, fz, weight, conduct, binding, source, smooth, iterate = coarse[index]
        count = total >> index
        for array in (conduct, smooth, iterate):
            array[0] = zero
            array[count + 1] = zero
        if index == 0:
            source = merged.at[1 : count + 1]
            for row in range(count):
                at = row ^ place[0]
                conduct[row + 1] = top_rows[at // stride, at % stride, 0]
                binding[row] = top_rows[at // stride, at % stride, 1]
        bound = lambda row, binding=binding: binding[row - 1]
        at_row = lambda row, conduct=conduct: conduct[row]
        coefficients(sizes, place, level, count + 2, at_row, bound, fx, fy, fz, weight)
        for row in range(count):
            smooth[row + 1] = weight[row] * source[row]
        if index < 2:
            conduct_next, binding_next, source_next = coarse[index + 1][4:7]
            half = count // 2
            for row in range(half):
                sums[row, :, :LANES] = conduct[2 * row + 1] + conduct[2 * row + 2]
            narrow(sizes, place, level, sums, conduct_next.at[1 : half + 1], half)
            for row in range(half):
                sums[row, :, :LANES] = binding[2 * row] + binding[2 * row + 1]
            narrow(sizes, place, level, sums, binding_next, half)

            def add(row, value, source=source):
                value = source[row - 1] - value
                slot = (row - 1) // 2
                if row % 2 == 1:
                    sums[slot, :, :LANES] = value
                else:
                    sums[slot, :, :LANES] = sums[slot, :, :LANES] + value

            sweep(count + 2, lambda row, smooth=smooth: smooth[row], bound, fx, fy, fz, add)
            narrow(sizes, place, level, sums, source_next, half)

    def relax(count, field, refs_of, source, target):
        fx, fy, fz, weight, binding = refs_of

        def update(row, value):
            target(row, field(row) + weight[row - 1] * (source(row) - value))

        sweep(count, field, lambda row: binding[row - 1], fx, fy, fz, update)

    def store(array, first):
        def put_row(row, value):
            array[row - first] = value

        return put_row

    fx, fy, fz, weight, conduct, binding, source, smooth, iterate = coarse[2]
    held, other = smooth, iterate
    for _ in range(COARSE_SWEEPS - 1):
        field = lambda row, held=held: held[row]
        mine = lambda row: source[row - 1]
        relax((total >> 2) + 2, field, (fx, fy, fz, weight, binding), mine, store(other, 0))
        held, other = other, held
    for index in (1, 0):
        fx, fy, fz, weight, conduct, binding, source, smooth, iterate = coarse[index]
        if index == 0:
            source = merged.at[1 : total + 1]
        count = total >> index
        widen(sizes, place, 3 + index, held.at[1 : count // 2 + 1], sums, count // 2)
        for row in range(count):
            smooth[row + 1] = smooth[row + 1] + sums[row // 2, :, :LANES]
        field = lambda row, smooth=smooth: smooth[row]
        mine = lambda row, source=source: source[row - 1]
        relax(count + 2, field, (fx, fy, fz, weight, binding), mine, store(iterate, 0))
        held = iterate

    wait(later)
    from_prev, from_next = messages.at[0], messages.at[1]
    widen(sizes, place, 2, held.at[pl.ds(place[0], 3)], over2, 3)
    for level, array, first, over, lift, target, upper in (
        (2, rows2, 4, over2, lift2, it2, over1),
        (1, rows1, 1, over1, lift1, it1, over0),
    ):
        n = sizes.rows[level]
        fx, fy, fz, weight, binding, own, smooth = parts(array, coefficient_rows(sizes, level))
        edge = {}
        for row, message, index in (
            (1, from_prev, first),
            (2, from_prev, first + 1),
            (n + 2, from_next, first),
            (n + 1, from_next, first + 1),
        ):
            value = edge.get(row, own[row - 1])
            edge[row] = value + fringed_row(sizes, level, index, message)
        for row, value in edge.items():
            own[row - 1] = value
        for row in range(n + 4):
            if row in (0, n + 3):
                value = fringed_row(sizes, level, first + 2, from_next if row else from_prev)
                if level == 2:
                    far = fars.at[1 if row else 0]
                    value = value + jnp.concatenate(get(far, (0, sizes.held[2] // LANES)), axis=1)
            elif row in edge:
                value = weight[row - 1] * own[row - 1]
            else:
                value = smooth[row - 1]
            lift[row] = value + over[row // 2]
        field = lambda row, lift=lift: lift[row]
        mine = lambda row, own=own: own[row - 1]
        relax(n + 4, field, (fx, fy, fz, weight, binding), mine, store(target, 1))
        widen(sizes, place, level - 1, target, upper, n + 2)

    b0, r0 = wide0.at[0], wide0.at[1]
    fx, fy, fz, weight, v0 = parts(rows0, coefficient_rows(sizes, 0))
    lift0[0] = fringed_row(sizes, 0, 0, from_prev) + over0[0]
    lift0[n0 + 1] = fringed_row(sizes, 0, 0, from_next) + over0[n1 + 1]
    for row in range(1, n0 + 1):
        lift0[row] = v0[row - 1] + over0[(row + 1) // 2]
    field = lambda row: lift0[row]
    mine = lambda row: r0[row - 1]
    relax(n0 + 2, field, (fx, fy, fz, weight, b0), mine, store(it0, 1))
    result[...] = jnp.swapaxes(it0[:, :, :width], 0, 1)
    wait([copies.start(result, out)])


def call(body, name, outputs, scratch, copies, place, inputs):
    return pl.pallas_call(
        body,
        name=name,
        out_shape=[jax.ShapeDtypeStruct(shape, f32) for shape in outputs],
        in_specs=[pl.BlockSpec(memory_space=pltpu.SMEM)] + [pl.BlockSpec(memory_space=pl.ANY)] * len(inputs),
        out_specs=[pl.BlockSpec(memory_space=pl.ANY)] * len(outputs),
        scratch_shapes=[pltpu.VMEM(shape, f32) for shape in scratch] + [pltpu.SemaphoreType.DMA((copies,))],
        compiler_params=pltpu.CompilerParams(vmem_limit_bytes=VMEM_LIMIT),
    )(place, *inputs)


def along(value, axis, steps):
    count = lax.axis_size(axis)
    initial, last = max(0, -steps), min(count, count - steps)
    return lax.ppermute(value, axis, [(source, source + steps) for source in range(initial, last)])


def beside(values, sizes):
    if sizes.sides == 1:
        return [[lax.ppermute(value, "width", [(0, 1), (1, 0)]) for value in values]]
    if sizes.sides == 2:
        return [[along(value, "width", steps) for value in values] for steps in (-1, 1)]
    return []


def stages(count):
    stride = 1
    while stride < count:
        radix = 4 if count // stride % 4 == 0 else 2
        yield stride, radix
        stride *= radix


def swap(value, stride, radix):
    count = lax.axis_size("span")
    others = range(1, radix)
    return [value] + [
        lax.ppermute(value, "span", [(device, device ^ step * stride) for device in range(count)]) for step in others
    ]


def on_device(right_side, diffusivity, reaction):
    depth, extent_x, extent_y = diffusivity.shape
    sizes = Sizes(depth, extent_x, extent_y, lax.axis_size("span"), lax.axis_size("width"))
    place = jnp.stack([lax.axis_index("span"), lax.axis_index("width")]).astype(jnp.int32)
    n0, n1, n2, n3 = sizes.rows
    s = sizes.sides

    def columns(count):
        return (depth, count * LANES)

    own = [columns(count) for count in sizes.own]
    held = [(depth, count) for count in sizes.held]
    down_message = (sizes.tiles, depth, LANES)
    up_message = (sizes.tiles + 1, depth, LANES)
    edge = (3, n0, depth, BORDER)

    outputs = [(3, n0, *own[0]), (2, n1, *own[1]), (2, n2, *own[2]), down_message, down_message] + [edge] * s
    own0, own1, own2, to_next, to_prev, *edges = call(
        functools.partial(start_kernel, sizes),
        "start",
        outputs,
        [(3, *diffusivity.shape), *outputs, (n1, *own[0])],
        8 + s,
        place,
        [right_side, diffusivity, reaction],
    )
    halos = [along(to_next, "span", 1), along(to_prev, "span", -1)]
    if s == 1:
        borders = [lax.ppermute(edges[0], "width", [(0, 1), (1, 0)])]
    elif s == 2:
        borders = [along(edges[1], "width", -1), along(edges[0], "width", 1)]
    else:
        borders = []

    outputs = [(2, n1, depth, LANES), (2, n2, depth, LANES), (2, depth, LANES)]
    border1, border2, top = call(
        functools.partial(border_kernel, sizes),
        "border",
        outputs,
        [(max(s, 1), 2, n0, depth, BORDER), outputs[0], (2, n2, *held[2]), outputs[2], (n1, depth, 2 * LANES)],
        4 + s,
        place,
        [own2, *borders],
    )
    plan = list(stages(sizes.span_count))
    for stride, radix in plan[:-1]:
        top = jnp.concatenate(swap(top.reshape(stride, 2, depth, LANES), stride, radix))
    stride, radix = plan[-1]
    tops = swap(top.reshape(stride, 2, depth, LANES), stride, radix)

    sides = beside(halos, sizes)
    lengths = [sum(coefficient_rows(sizes, level)) for level in range(3)]
    far = (sizes.held[2] // LANES, depth, LANES)
    coefs = [(lengths[level], *held[level]) for level in range(3)]
    downs = call(
        functools.partial(down_kernel, sizes),
        "down",
        [*coefs, (3, depth, LANES), up_message, up_message, far, far],
        [
            *((3 if level == 0 else 2, sizes.rows[level], *held[level]) for level in range(3)),
            (2 * (1 + s), *down_message),
            *coefs,
            (3, depth, LANES),
            (2, *up_message),
            (2, *far),
            (n1 + 2, *held[0]),
        ],
        20 + 4 * s,
        place,
        [own0, own1, own2, *borders, *([border1, border2] if s else []), *halos, *sum(sides, [])],
    )
    coefs_out, source, ups, fars = downs[:3], downs[3], downs[4:6], downs[6:8]
    for stride, radix in plan[:-1]:
        merged = (stride * radix + 2, depth, LANES)
        parts_of = swap(source, stride, radix)
        (source,) = call(
            functools.partial(merge_kernel, sizes, stride, radix),
            "merge",
            [merged],
            [(stride + 2, depth, LANES)] * radix + [merged],
            radix + 1,
            place,
            parts_of,
        )
    stride, radix = plan[-1]
    sources = swap(source, stride, radix)
    received = [along(ups[0], "span", 1), along(ups[1], "span", -1)]
    received += [along(fars[0], "span", 2), along(fars[1], "span", -2)]
    scratch = [
        (radix, stride + 2, depth, LANES),
        (radix, stride, 2, depth, LANES),
        (2, *up_message),
        (2, *far),
        coefs[0],
        (2, n0, *held[0]),
        coefs[1],
        coefs[2],
        (sizes.span_count + 2, depth, LANES),
        (max(sizes.span_count // 2, 2), depth, LANES),
        diffusivity.shape,
    ]
    for index in range(3):
        count = sizes.span_count >> index
        scratch += [(count + 1, depth, LANES)] + [(count, depth, LANES)] * 3
        scratch += [(count + 2, depth, LANES), (count, depth, LANES), (count, depth, LANES)]
        scratch += [(count + 2, depth, LANES)] * 2
    scratch += [(n3 + 2, *held[2]), (n2 + 2, *held[1]), (n1 + 2, *held[0])]
    scratch += [(n2 + 4, *held[2]), (n1 + 4, *held[1]), (n0 + 2, *held[0])]
    scratch += [(n2 + 2, *held[2]), (n1 + 2, *held[1]), (n0, *held[0])]
    (correction,) = call(
        functools.partial(up_kernel, sizes, stride, radix),
        "up",
        [diffusivity.shape],
        scratch,
        2 * radix + 9 + s,
        place,
        [*sources, *tops, *received, *coefs_out, own0, *borders],
    )
    return correction


def solution(mesh):
    in_specs = (P(None, "span", "width"),) * 3
    return jax.shard_map(
        on_device, mesh=mesh, in_specs=in_specs, out_specs=P(None, "span", "width"), check_vma=False
    )
```

```python
import functools

import jax
import jax.numpy as jnp
from jax import lax
from jax.experimental import pallas as pl
from jax.experimental.pallas import tpu as pltpu
from jax.sharding import PartitionSpec as P

LEVELS = 6
COARSE_SWEEPS = 3
LANES = 128
BORDER = 128
FRINGE = 4
SPREAD = 16
relax_weight = 0.8
f32 = jnp.float32
VMEM_LIMIT = 40 * 1024 * 1024
START_LIMIT = 58 * 1024 * 1024
CHUNKS = 4


class Sizes:
    def __init__(self, depth, extent_x, extent_y, span_count, width_count):
        self.depth, self.extent_x, self.extent_y = depth, extent_x, extent_y
        self.span_count, self.width_count = span_count, width_count
        self.sides = min(width_count - 1, 2)
        self.own = [(extent_y >> level) // LANES for level in range(3)]
        self.border = [self.sides, min(self.sides, 1), min(self.sides, 1)]
        self.held = [(self.own[level] + self.border[level]) * LANES for level in range(3)] + [LANES] * 3
        self.rows = [extent_x >> level for level in range(4)]
        self.slots = []
        start = 0
        for level in (0, 1, 1, 1, 2, 2, 2):
            self.slots.append((start, self.own[level]))
            start += self.own[level]
        self.tiles = start


def put(message, slot, row):
    start, tiles = slot
    for tile in range(tiles):
        message[start + tile] = row[:, tile * LANES : (tile + 1) * LANES]


def get(message, slot):
    start, tiles = slot
    return [message[start + tile] for tile in range(tiles)]


def lane_at(shape):
    return lax.broadcasted_iota(jnp.int32, shape, len(shape) - 1)


def roll(value, steps, axis):
    return pltpu.roll(value, steps % value.shape[axis], axis=axis)


def reciprocal(value):
    return pltpu.reciprocal(value, approx=True)


def harmonic(first, second, guard):
    total = first + second
    if guard:
        total = jnp.maximum(total, 1e-3)
    return (2.0 * first) * second * reciprocal(total)


def split(value):
    high = value.astype(jnp.bfloat16)
    return high, (value - high.astype(f32)).astype(jnp.bfloat16)


def dot(halves, table):
    high, low = halves
    return jnp.dot(high, table, preferred_element_type=f32) + jnp.dot(low, table, preferred_element_type=f32)


def pair_table(fine, fine_dim, turn, weight):
    shape = (fine, LANES) if fine_dim == 0 else (LANES, fine)
    fine_at = lax.broadcasted_iota(jnp.int32, shape, fine_dim)
    coarse_at = lax.broadcasted_iota(jnp.int32, shape, 1 - fine_dim)
    if turn is not None:
        coarse_at = coarse_at - jnp.where(fine_at >= turn, LANES // 2, 0)
    return jnp.where(fine_at // 2 == coarse_at, weight, 0.0).astype(jnp.bfloat16)


def turns(sizes, place, level):
    if sizes.sides == 0:
        return []
    if level == 0:
        return [jnp.where(place[1] == 0, LANES, 0)] if sizes.sides == 1 else [LANES, 0]
    return [LANES // 2]


def transfer_plan(sizes, place, level, part):
    plan = []
    if level >= 3:
        return [((0, LANES), 0, 3 * LANES // 4)]
    if level == 2:
        return [((0, sizes.held[2]), 0, None)]
    own = sizes.own[level]
    if part != "border":
        plan += [((2 * LANES * tile, 2 * LANES * (tile + 1)), tile, None) for tile in range(own // 2)]
    if part != "own":
        for index, turn in enumerate(turns(sizes, place, level)):
            start = (own + index) * LANES
            plan.append(((start, start + LANES), own // 2, turn))
    return plan


def narrow(sizes, place, level, sums, target, rows, part="all", shift=0):
    depth = sums.shape[1]
    done = {}
    for (start, stop), tile, turn in transfer_plan(sizes, place, level, part):
        start, stop, tile = start - shift, stop - shift, tile - shift // (2 * LANES)
        columns = split(sums[0:rows, :, start:stop].reshape(rows * depth, stop - start))
        result = dot(columns, pair_table(stop - start, 0, turn, 0.25)).reshape(rows, depth, LANES)
        done[tile] = done[tile] + result if tile in done else result
    for tile, result in done.items():
        target[0:rows, :, tile * LANES : (tile + 1) * LANES] = result


def widen(sizes, place, level, coarse, target, rows):
    depth = coarse.shape[1]
    for (start, stop), tile, turn in transfer_plan(sizes, place, level, "all"):
        columns = split(coarse[0:rows, :, tile * LANES : (tile + 1) * LANES].reshape(rows * depth, LANES))
        result = dot(columns, pair_table(stop - start, 1, turn, 4.0))
        target[0:rows, :, start:stop] = result.reshape(rows, depth, stop - start)


def coefficients(sizes, place, level, count, conduct, binding, fx, fy, fz, weight):
    guard = level > 0 or sizes.sides > 1
    for row in range(1, count):
        fx[row - 1] = harmonic(conduct(row - 1), conduct(row), guard)
    for row in range(1, count - 1):
        mine = conduct(row)
        south = harmonic(mine, roll(mine, 1, 1), guard)
        if level == 0 and sizes.sides < 2:
            cut = 0 if sizes.sides == 0 else jnp.where(place[1] == 0, 0, sizes.extent_y)
            south = jnp.where(lane_at(mine.shape) == cut, 0.0, south)
        below = harmonic(mine, roll(mine, 1, 0), guard)
        below = jnp.where(lax.broadcasted_iota(jnp.int32, mine.shape, 0) == 0, 0.0, below)
        diagonal = fx[row - 1] + fx[row] + binding(row)
        diagonal = diagonal + (south + roll(south, -1, 1)) + (below + roll(below, -1, 0))
        if guard:
            diagonal = jnp.maximum(diagonal, 1e-6)
        fy[row - 1] = south
        fz[row - 1] = below
        weight[row - 1] = relax_weight * reciprocal(diagonal)


def sweep(count, field, binding, fx, fy, fz, emit):
    lower = fx[0] * (field(1) - field(0))
    for row in range(1, count - 1):
        mine = field(row)
        upper = fx[row] * (field(row + 1) - mine)
        south = fy[row - 1] * (mine - roll(mine, 1, 1))
        below = fz[row - 1] * (mine - roll(mine, 1, 0))
        across = (south - roll(south, -1, 1)) + (below - roll(below, -1, 0))
        emit(row, binding(row) * mine + (lower - upper) + across)
        lower = upper


def own_defect(count, smooth, source, binding, fx, fy, fz, sums, first):
    zero = jnp.zeros(smooth.shape[1:], f32)

    def field(row):
        return smooth[row - 1] if 0 < row < count - 1 else zero

    def add(row, value):
        slot = (row + first) // 2
        if (row + first) % 2 == 0 or row == 0:
            sums[slot] = value
        else:
            sums[slot] = sums[slot] + value

    add(0, fx[0] * field(1))
    sweep(count, field, binding, fx, fy, fz, lambda row, result: add(row, source(row) - result))
    add(count - 1, fx[count - 2] * field(count - 2))


def parts(array, counts):
    views, start = [], 0
    for count in counts:
        views.append(array.at[start : start + count])
        start += count
    return views


def coefficient_rows(sizes, level):
    n = sizes.rows[level]
    if level == 0:
        return [n + 1, n, n, n, n]
    return [n + 3] + [n + 2] * 6


def start_kernel(sizes, place, right_side, conduct, binding, own0, own1, own2, to_next, to_prev, top, *refs):
    edges, (inputs, sums, semaphores) = refs[: sizes.sides], refs[sizes.sides :]
    n0, n1, n2 = sizes.rows[:3]
    step = sizes.depth // CHUNKS
    loads = [[], [], []]
    for at, array in enumerate((conduct, binding, right_side)):
        for chunk in range(CHUNKS):
            part = pl.ds(chunk * step, step)
            copy = pltpu.make_async_copy(array.at[part], inputs.at[at, part], semaphores.at[at * CHUNKS + chunk])
            copy.start()
            loads[at].append(copy)

    def turn(at):
        for copy in loads[at]:
            copy.wait()
        own0[at] = jnp.swapaxes(inputs[at], 0, 1)

    tops = []
    for at in (0, 1):
        turn(at)
        for row in range(n1):
            sums[row] = own0[at, 2 * row] + own0[at, 2 * row + 1]
        narrow(sizes, place, 0, sums, own1.at[at], n1, "own")
        for row in range(n2):
            sums[row, :, : sizes.own[1] * LANES] = own1[at, 2 * row] + own1[at, 2 * row + 1]
        narrow(sizes, place, 1, sums, own2.at[at], n2, "own")
        tops.append(dot(split(own2[at, 0] + own2[at, 1]), pair_table(LANES, 0, None, 0.25)))
    for message, low, at1, at0 in ((to_next, n1 - 2, n1 - 1, n0 - 1), (to_prev, 0, 0, 0)):
        edge = n2 - 1 if at0 else 0
        rows = (own0[0, at0], own1[0, low], own1[0, low + 1], own1[1, at1])
        rows += (own2[0, n2 - 2], own2[0, n2 - 1], own2[1, edge])
        for slot, row in zip(sizes.slots, rows):
            put(message, slot, row)
    block = tops[0] + roll(tops[1], LANES // 2, 1)
    for device in range(sizes.span_count):
        top[device] = block
    turn(2)
    last = sizes.extent_y - BORDER
    if sizes.sides == 1:
        at = pl.multiple_of(jnp.where(place[1] == 0, last, 0), LANES)
        edges[0][...] = own0[:, :, :, pl.ds(at, BORDER)]
    elif sizes.sides == 2:
        edges[0][...] = own0[:, :, :, last:]
        edges[1][...] = own0[:, :, :, :BORDER]


def message_row(sizes, place, level, slot, message, beside):
    start, tiles = slot
    row = get(message, slot)
    if sizes.sides == 1:
        left = place[1] != 0
        tile = beside[0][start + jnp.where(left, tiles - 1, 0)]
        if level > 0:
            reach = BORDER >> level
            lane = lane_at(tile.shape)
            first = jnp.where(left, LANES - reach, 0)
            tile = jnp.where((lane >= first) & (lane < first + reach), tile, 0.0)
        row.append(tile)
    elif sizes.sides == 2:
        right, left = beside[0][start], beside[1][start + tiles - 1]
        if level == 0:
            row += [right, left]
        else:
            reach = BORDER >> level
            lane = lane_at(right.shape)
            row.append(jnp.where(lane < reach, right, jnp.where(lane >= LANES - reach, left, 0.0)))
    return jnp.concatenate(row, axis=1)


def fringe_lanes(shape):
    lane = lane_at(shape)
    return (lane < FRINGE) | (lane >= LANES - FRINGE)


def put_fringes(sizes, message, rows):
    total = None
    for index, (level, row) in enumerate(rows):
        tile = row[:, sizes.own[level] * LANES :]
        tile = jnp.where(fringe_lanes(tile.shape), tile, 0.0)
        tile = roll(tile, SPREAD * index + SPREAD // 2, 1)
        total = tile if total is None else total + tile
    message[sizes.tiles] = total


def fringed_row(sizes, level, index, message):
    row = get(message, sizes.slots[index])
    if sizes.border[level]:
        if level == 0:
            row += [jnp.zeros(row[0].shape, f32)] * sizes.border[0]
        else:
            tile = roll(message[sizes.tiles], -(SPREAD * (index - 1) + SPREAD // 2), 1)
            row.append(jnp.where(fringe_lanes(tile.shape), tile, 0.0))
    return jnp.concatenate(row, axis=1)


def pack_edges(sizes, place, rows, target):
    if sizes.sides != 1:
        for index, row in enumerate(rows):
            target(index, row)
        return
    half, reach = LANES // 2, BORDER >> 3
    lane = lane_at(rows[0].shape)
    target(0, jnp.where(lane < half, rows[0], pltpu.roll(rows[1], half, axis=1)))
    mixed = jnp.where(lane < half, rows[2], 0.0)
    for index, row in enumerate(rows):
        first = half + index * reach
        moved = pltpu.roll(row, border_turn(place, index), axis=1)
        mixed = jnp.where((lane >= first) & (lane < first + reach), moved, mixed)
    target(1, mixed)


def border_turn(place, index):
    reach = BORDER >> 3
    return jnp.where(place[1] == 0, index * reach, LANES // 2 + (index + 1) * reach)


def unpack_edges(sizes, place, blocks, row, count):
    total = None
    if sizes.sides != 1:
        for index, device in ((2, row - 1), (1, row), (0, row + 1)):
            if 0 <= device < count:
                value = blocks[device, index]
                total = value if total is None else total + value
        return total
    half, reach = LANES // 2, BORDER >> 3
    own = pltpu.roll(blocks[row, 0], half, axis=1)
    border = turned = None
    for index, device in ((2, row - 1), (1, row), (0, row + 1)):
        if 0 <= device < count:
            if index != 1:
                own = own + blocks[device, 0 if index == 0 else 1]
            back = lax.rem(LANES - border_turn(place, index), LANES)
            value = pltpu.roll(blocks[device, 1], back, axis=1)
            border = value if border is None else border + value
    lane = lane_at(own.shape)
    first = jnp.where(place[1] == 0, half, LANES - reach)
    return jnp.where(lane < half, own, jnp.where((lane >= first) & (lane < first + reach), border, 0.0))


def top_row(sizes, place, top, beside, row):
    half, reach = LANES // 2, BORDER >> 3
    block = top[row]
    lane = lane_at(block.shape)
    values = [jnp.where(lane < half, block, 0.0), jnp.where(lane < half, pltpu.roll(block, half, axis=1), 0.0)]
    right = (lane >= half) & (lane < half + reach)
    left = lane >= LANES - reach
    for side in range(sizes.sides):
        other = beside[side][row]
        if sizes.sides == 2:
            here = left if side else right
        else:
            first = jnp.where(place[1] == 0, half, LANES - reach)
            here = (lane >= first) & (lane < first + reach)
        values[0] = jnp.where(here, pltpu.roll(other, half, axis=1), values[0])
        values[1] = jnp.where(here, other, values[1])
    return values


def down_kernel(sizes, place, *refs):
    s = sizes.sides
    owns, refs = refs[:3], refs[3:]
    borders0, refs = refs[:s], refs[s:]
    from_prev, from_next, refs = refs[0], refs[1], refs[2:]
    beside_prev, beside_next, refs = refs[: 2 * s : 2], refs[1 : 2 * s : 2], refs[2 * s :]
    coefs, contribution, ups, fars, refs = refs[:3], refs[3], refs[4:6], refs[6:8], refs[8:]
    border1, border2, level3, sums = refs
    slots = sizes.slots
    n0, n1, n2 = sizes.rows[:3]

    if s:
        for at in (0, 1):
            for row in range(n1):
                for side in range(s):
                    columns = slice(side * LANES, (side + 1) * LANES)
                    sums[row, :, columns] = borders0[side][at, 2 * row] + borders0[side][at, 2 * row + 1]
            narrow(sizes, place, 0, sums, border1.at[at], n1, "border", sizes.own[0] * LANES)
            for row in range(n2):
                sums[row, :, :LANES] = border1[at, 2 * row] + border1[at, 2 * row + 1]
            narrow(sizes, place, 1, sums, border2.at[at], n2, "border", sizes.own[1] * LANES)
    borders = [borders0, [border1][:s], [border2][:s]]

    def held_row(level, at, row):
        return jnp.concatenate([owns[level][at, row], *(array[at, row] for array in borders[level])], axis=1)

    def prev_row(level, index):
        return message_row(sizes, place, level, slots[index], from_prev, beside_prev)

    def next_row(level, index):
        return message_row(sizes, place, level, slots[index], from_next, beside_next)

    def conduct0(row):
        if row == 0:
            return prev_row(0, 0)
        if row == n0 + 1:
            return next_row(0, 0)
        return held_row(0, 0, row - 1)

    bound0 = lambda row: held_row(0, 1, row - 1)
    fx, fy, fz, weight, v0 = parts(coefs[0], coefficient_rows(sizes, 0))
    coefficients(sizes, place, 0, n0 + 2, conduct0, bound0, fx, fy, fz, weight)
    for row in range(n0):
        v0[row] = weight[row] * held_row(0, 2, row)
    own_defect(n0 + 2, v0, lambda row: held_row(0, 2, row - 1), bound0, fx, fy, fz, sums, 1)
    smooths, sources = [], []
    for level, first in ((1, 1), (2, 4)):
        n = sizes.rows[level]
        fx, fy, fz, weight, binding, source, smooth = parts(coefs[level], coefficient_rows(sizes, level))
        held = sizes.held[level]
        narrow(sizes, place, level - 1, sums.at[:, :, : sizes.held[level - 1]], source, n + 2)
        binding[0] = prev_row(level, first + 2)
        binding[n + 1] = next_row(level, first + 2)
        for row in range(n):
            binding[row + 1] = held_row(level, 1, row)

        def conduct(row, n=n, level=level, first=first):
            if row < 2:
                return prev_row(level, first + row)
            if row >= n + 2:
                return next_row(level, first + row - n - 2)
            return held_row(level, 0, row - 2)

        bound = lambda row, binding=binding: binding[row - 1]
        coefficients(sizes, place, level, n + 4, conduct, bound, fx, fy, fz, weight)
        for row in range(n + 2):
            smooth[row] = weight[row] * source[row]
        mine = lambda row, source=source: source[row - 1]
        own_defect(n + 4, smooth, mine, bound, fx, fy, fz, sums.at[:, :, :held], 0)
        smooths.append(smooth)
        sources.append(source)
    narrow(sizes, place, 2, sums.at[:, :, : sizes.held[2]], level3, 3)

    def send(index, value):
        for device in range(sizes.span_count):
            contribution[device, index] = value

    pack_edges(sizes, place, [level3[row] for row in range(3)], send)
    (s1, s2), (v1, v2) = sources, smooths
    for at, rows in enumerate(
        (
            (v0[n0 - 1], s1[n1], s1[n1 + 1], v1[n1 - 1], s2[n2], s2[n2 + 1], v2[n2 - 1]),
            (v0[0], s1[1], s1[0], v1[2], s2[1], s2[0], v2[2]),
        )
    ):
        for slot, row in zip(slots, rows):
            put(ups[at], slot, row)
        if s:
            put_fringes(sizes, ups[at], list(zip((1, 1, 1, 2, 2, 2), rows[1:])))
        put(fars[at], (0, sizes.held[2] // LANES), v2[n2 + 1 if at == 0 else 0])


def up_kernel(sizes, place, blocks, top, *refs):
    s = sizes.sides
    tops, refs = refs[:s], refs[s:]
    (from_prev, from_next), fars, coefs, own0 = refs[:2], refs[2:4], refs[4:7], refs[7]
    borders0, out, refs = refs[8 : 8 + s], refs[8 + s], refs[9 + s :]
    total1, total2, sums, result = refs[:4]
    coarse = [refs[4 + 9 * index : 13 + 9 * index] for index in range(3)]
    over2, over1, over0, lift2, lift1, lift0, it2, it1, it0, semaphores = refs[31:]
    slots = sizes.slots
    n0, n1, n2 = sizes.rows[:3]
    total = sizes.span_count
    width = sizes.own[0] * LANES

    zero = jnp.zeros((sizes.depth, LANES), f32)
    for index in range(3):
        level = 3 + index
        fx, fy, fz, weight, conduct, binding, source, smooth, iterate = coarse[index]
        count = total >> index
        for array in (conduct, smooth, iterate):
            array[0] = zero
            array[count + 1] = zero
        if index == 0:
            for row in range(count):
                conduct[row + 1], binding[row] = top_row(sizes, place, top, tops, row)
                source[row] = unpack_edges(sizes, place, blocks, row, count)
        bound = lambda row, binding=binding: binding[row - 1]
        at_row = lambda row, conduct=conduct: conduct[row]
        coefficients(sizes, place, level, count + 2, at_row, bound, fx, fy, fz, weight)
        for row in range(count):
            smooth[row + 1] = weight[row] * source[row]
        if index < 2:
            conduct_next, binding_next, source_next = coarse[index + 1][4:7]
            half = count // 2
            for row in range(half):
                sums[row, :, :LANES] = conduct[2 * row + 1] + conduct[2 * row + 2]
            narrow(sizes, place, level, sums, conduct_next.at[1 : half + 1], half)
            for row in range(half):
                sums[row, :, :LANES] = binding[2 * row] + binding[2 * row + 1]
            narrow(sizes, place, level, sums, binding_next, half)

            def add(row, value, source=source):
                value = source[row - 1] - value
                slot = (row - 1) // 2
                if row % 2 == 1:
                    sums[slot, :, :LANES] = value
                else:
                    sums[slot, :, :LANES] = sums[slot, :, :LANES] + value

            sweep(count + 2, lambda row, smooth=smooth: smooth[row], bound, fx, fy, fz, add)
            narrow(sizes, place, level, sums, source_next, half)

    def relax(count, field, refs_of, source, target):
        fx, fy, fz, weight, binding = refs_of

        def update(row, value):
            target(row, field(row) + weight[row - 1] * (source(row) - value))

        sweep(count, field, binding, fx, fy, fz, update)

    def store(array, first):
        def put_row(row, value):
            array[row - first] = value

        return put_row

    fx, fy, fz, weight, conduct, binding, source, smooth, iterate = coarse[2]
    held, other = smooth, iterate
    for _ in range(COARSE_SWEEPS - 1):
        field = lambda row, held=held: held[row]
        mine = lambda row: source[row - 1]
        bound = lambda row: binding[row - 1]
        relax((total >> 2) + 2, field, (fx, fy, fz, weight, bound), mine, store(other, 0))
        held, other = other, held
    for index in (1, 0):
        fx, fy, fz, weight, conduct, binding, source, smooth, iterate = coarse[index]
        count = total >> index
        widen(sizes, place, 3 + index, held.at[1 : count // 2 + 1], sums, count // 2)
        for row in range(count):
            smooth[row + 1] = smooth[row + 1] + sums[row // 2, :, :LANES]
        field = lambda row, smooth=smooth: smooth[row]
        mine = lambda row, source=source: source[row - 1]
        bound = lambda row, binding=binding: binding[row - 1]
        relax(count + 2, field, (fx, fy, fz, weight, bound), mine, store(iterate, 0))
        held = iterate

    widen(sizes, place, 2, held.at[pl.ds(place[0], 3)], over2, 3)
    for level, array, first, totals, over, lift, target, upper in (
        (2, coefs[2], 4, total2, over2, lift2, it2, over1),
        (1, coefs[1], 1, total1, over1, lift1, it1, over0),
    ):
        n = sizes.rows[level]
        fx, fy, fz, weight, binding, own, smooth = parts(array, coefficient_rows(sizes, level))
        edge = {}
        for row, message, index in (
            (1, from_prev, first),
            (2, from_prev, first + 1),
            (n + 2, from_next, first),
            (n + 1, from_next, first + 1),
        ):
            value = edge.get(row, own[row - 1])
            edge[row] = value + fringed_row(sizes, level, index, message)
        for row, value in edge.items():
            totals[row - 1] = value
        for row in range(n + 4):
            if row in (0, n + 3):
                value = fringed_row(sizes, level, first + 2, from_next if row else from_prev)
                if level == 2:
                    far = fars[1 if row else 0]
                    value = value + jnp.concatenate(get(far, (0, sizes.held[2] // LANES)), axis=1)
            elif row in edge:
                value = weight[row - 1] * totals[row - 1]
            else:
                value = smooth[row - 1]
            lift[row] = value + over[row // 2]
        field = lambda row, lift=lift: lift[row]
        mine = lambda row, own=own, totals=totals, edge=edge: (totals if row in edge else own)[row - 1]
        bound = lambda row, binding=binding: binding[row - 1]
        relax(n + 4, field, (fx, fy, fz, weight, bound), mine, store(target, 1))
        widen(sizes, place, level - 1, target, upper, n + 2)

    def held_row(at, row):
        return jnp.concatenate([own0[at, row - 1], *(array[at, row - 1] for array in borders0)], axis=1)

    fx, fy, fz, weight, v0 = parts(coefs[0], coefficient_rows(sizes, 0))
    lift0[0] = fringed_row(sizes, 0, 0, from_prev) + over0[0]
    lift0[n0 + 1] = fringed_row(sizes, 0, 0, from_next) + over0[n1 + 1]
    for row in range(1, n0 + 1):
        lift0[row] = v0[row - 1] + over0[(row + 1) // 2]
    field = lambda row: lift0[row]
    bound = lambda row: held_row(1, row)
    relax(n0 + 2, field, (fx, fy, fz, weight, bound), lambda row: held_row(2, row), store(it0, 1))
    step = sizes.depth // CHUNKS
    copies = []
    for chunk in range(CHUNKS):
        part = slice(chunk * step, (chunk + 1) * step)
        result[part] = jnp.swapaxes(it0[:, part, :width], 0, 1)
        copies.append(pltpu.make_async_copy(result.at[part], out.at[part], semaphores.at[chunk]))
        copies[-1].start()
    for copy in copies:
        copy.wait()


def call(body, name, outputs, scratch, place, inputs, limit=VMEM_LIMIT, copies=0, far_in=False, far_out=False):
    near, far = pl.BlockSpec(memory_space=pltpu.VMEM), pl.BlockSpec(memory_space=pl.ANY)
    scratch = [pltpu.VMEM(shape, f32) for shape in scratch]
    if copies:
        scratch.append(pltpu.SemaphoreType.DMA((copies,)))
    return pl.pallas_call(
        body,
        name=name,
        out_shape=[jax.ShapeDtypeStruct(shape, f32) for shape in outputs],
        in_specs=[pl.BlockSpec(memory_space=pltpu.SMEM)] + [far if far_in else near] * len(inputs),
        out_specs=[far if far_out else near] * len(outputs),
        scratch_shapes=scratch,
        compiler_params=pltpu.CompilerParams(vmem_limit_bytes=limit),
    )(place, *inputs)


def along(value, axis, steps):
    count = lax.axis_size(axis)
    initial, last = max(0, -steps), min(count, count - steps)
    return lax.ppermute(value, axis, [(source, source + steps) for source in range(initial, last)])


def beside(values, sizes):
    if sizes.sides == 1:
        return [[lax.ppermute(value, "width", [(0, 1), (1, 0)]) for value in values]]
    if sizes.sides == 2:
        return [[along(value, "width", steps) for value in values] for steps in (-1, 1)]
    return []


def to_all(value):
    return lax.all_to_all(value, "span", split_axis=0, concat_axis=0, tiled=True)


def on_device(right_side, diffusivity, reaction):
    depth, extent_x, extent_y = diffusivity.shape
    sizes = Sizes(depth, extent_x, extent_y, lax.axis_size("span"), lax.axis_size("width"))
    place = jnp.stack([lax.axis_index("span"), lax.axis_index("width")]).astype(jnp.int32)
    n0, n1, n2, n3 = sizes.rows
    s = sizes.sides
    tile = (depth, LANES)
    own = [(depth, count * LANES) for count in sizes.own]
    held = [(depth, count) for count in sizes.held]
    down_message = (sizes.tiles, *tile)
    up_message = (sizes.tiles + 1, *tile)
    own0, own1, own2, to_next, to_prev, top, *edges = call(
        functools.partial(start_kernel, sizes),
        "start",
        [(3, n0, *own[0]), (2, n1, *own[1]), (2, n2, *own[2]), down_message, down_message]
        + [(sizes.span_count, *tile)]
        + [(3, n0, depth, BORDER)] * s,
        [(3, *diffusivity.shape), (n1, *own[0])],
        place,
        [right_side, diffusivity, reaction],
        limit=START_LIMIT,
        copies=3 * CHUNKS,
        far_in=True,
    )
    halos = [along(to_next, "span", 1), along(to_prev, "span", -1)]
    if s == 1:
        borders = [lax.ppermute(edges[0], "width", [(0, 1), (1, 0)])]
    elif s == 2:
        borders = [along(edges[1], "width", -1), along(edges[0], "width", 1)]
    else:
        borders = []
    top, *halos = lax.optimization_barrier((top, *halos))
    sides = beside(halos, sizes)
    top = to_all(top)

    lengths = [sum(coefficient_rows(sizes, level)) for level in range(3)]
    far = (sizes.held[2] // LANES, *tile)
    coefs = [(lengths[level], *held[level]) for level in range(3)]
    downs = call(
        functools.partial(down_kernel, sizes),
        "down",
        [*coefs, (sizes.span_count, 2 if s == 1 else 3, *tile), up_message, up_message, far, far],
        [(2, n1, *tile), (2, n2, *tile), (3, *tile), (n1 + 2, *held[0])],
        place,
        [own0, own1, own2, *borders, *halos, *sum(sides, [])],
    )
    coefs_out, blocks, ups, fars = downs[:3], downs[3], downs[4:6], downs[6:8]
    blocks = to_all(blocks)
    tops = [side[0] for side in beside([top], sizes)]
    received = [along(ups[0], "span", 1), along(ups[1], "span", -1)]
    received += [along(fars[0], "span", 2), along(fars[1], "span", -2)]
    scratch = [(n1 + 2, *held[1]), (n2 + 2, *held[2]), (max(sizes.span_count // 2, 2), *tile), diffusivity.shape]
    for index in range(3):
        count = sizes.span_count >> index
        scratch += [(count + 1, *tile)] + [(count, *tile)] * 3 + [(count + 2, *tile)] + [(count, *tile)] * 2
        scratch += [(count + 2, *tile)] * 2
    scratch += [(n3 + 2, *held[2]), (n2 + 2, *held[1]), (n1 + 2, *held[0])]
    scratch += [(n2 + 4, *held[2]), (n1 + 4, *held[1]), (n0 + 2, *held[0])]
    scratch += [(n2 + 2, *held[2]), (n1 + 2, *held[1]), (n0, *held[0])]
    (correction,) = call(
        functools.partial(up_kernel, sizes),
        "up",
        [diffusivity.shape],
        scratch,
        place,
        [blocks, top, *tops, *received, *coefs_out, own0, *borders],
        copies=CHUNKS,
        far_out=True,
    )
    return correction


def solution(mesh):
    in_specs = (P(None, "span", "width"),) * 3
    return jax.shard_map(
        on_device, mesh=mesh, in_specs=in_specs, out_specs=P(None, "span", "width"), check_vma=False
    )
```

```python
import functools

import jax
import jax.numpy as jnp
from jax import lax
from jax.experimental import pallas as pl
from jax.experimental.pallas import tpu as pltpu
from jax.sharding import PartitionSpec as P

LEVELS = 6
COARSE_SWEEPS = 3
LANES = 128
BORDER = 128
FRINGE = 4
SPREAD = 16
relax_weight = 0.8
f32 = jnp.float32
VMEM_LIMIT = 32 * 1024 * 1024
CHUNKS = 4


class Sizes:
    def __init__(self, depth, extent_x, extent_y, span_count, width_count):
        self.depth, self.extent_x, self.extent_y = depth, extent_x, extent_y
        self.span_count, self.width_count = span_count, width_count
        self.sides = min(width_count - 1, 2)
        self.own = [(extent_y >> level) // LANES for level in range(3)]
        self.border = [self.sides, min(self.sides, 1), min(self.sides, 1)]
        self.held = [(self.own[level] + self.border[level]) * LANES for level in range(3)] + [LANES] * 3
        self.rows = [extent_x >> level for level in range(4)]
        self.slots = []
        start = 0
        for level in (0, 1, 1, 1, 2, 2, 2):
            self.slots.append((start, self.own[level]))
            start += self.own[level]
        self.tiles = start


def put(message, slot, row):
    start, tiles = slot
    for tile in range(tiles):
        message[start + tile] = row[:, tile * LANES : (tile + 1) * LANES]


def get(message, slot):
    start, tiles = slot
    return [message[start + tile] for tile in range(tiles)]


def lane_at(shape):
    return lax.broadcasted_iota(jnp.int32, shape, len(shape) - 1)


def roll(value, steps, axis):
    return pltpu.roll(value, steps % value.shape[axis], axis=axis)


def reciprocal(value):
    return pltpu.reciprocal(value, approx=True)


def harmonic(first, second, guard):
    total = first + second
    if guard:
        total = jnp.maximum(total, 1e-3)
    return (2.0 * first) * second * reciprocal(total)


def split(value):
    high = value.astype(jnp.bfloat16)
    return high, (value - high.astype(f32)).astype(jnp.bfloat16)


def dot(halves, table):
    high, low = halves
    return jnp.dot(high, table, preferred_element_type=f32) + jnp.dot(low, table, preferred_element_type=f32)


def pair_table(fine, fine_dim, turn, weight):
    shape = (fine, LANES) if fine_dim == 0 else (LANES, fine)
    fine_at = lax.broadcasted_iota(jnp.int32, shape, fine_dim)
    coarse_at = lax.broadcasted_iota(jnp.int32, shape, 1 - fine_dim)
    if turn is not None:
        coarse_at = coarse_at - jnp.where(fine_at >= turn, LANES // 2, 0)
    return jnp.where(fine_at // 2 == coarse_at, weight, 0.0).astype(jnp.bfloat16)


def turns(sizes, place, level):
    if sizes.sides == 0:
        return []
    if level == 0:
        return [jnp.where(place[1] == 0, LANES, 0)] if sizes.sides == 1 else [LANES, 0]
    return [LANES // 2]


def transfer_plan(sizes, place, level, part):
    plan = []
    if level >= 3:
        return [((0, LANES), 0, 3 * LANES // 4)]
    if level == 2:
        return [((0, sizes.held[2]), 0, None)]
    own = sizes.own[level]
    if part != "border":
        plan += [((2 * LANES * tile, 2 * LANES * (tile + 1)), tile, None) for tile in range(own // 2)]
    if part != "own":
        for index, turn in enumerate(turns(sizes, place, level)):
            start = (own + index) * LANES
            plan.append(((start, start + LANES), own // 2, turn))
    return plan


def narrow(sizes, place, level, sums, target, rows, part="all", shift=0):
    depth = sums.shape[1]
    done = {}
    for (start, stop), tile, turn in transfer_plan(sizes, place, level, part):
        start, stop, tile = start - shift, stop - shift, tile - shift // (2 * LANES)
        columns = split(sums[0:rows, :, start:stop].reshape(rows * depth, stop - start))
        result = dot(columns, pair_table(stop - start, 0, turn, 0.25)).reshape(rows, depth, LANES)
        done[tile] = done[tile] + result if tile in done else result
    for tile, result in done.items():
        target[0:rows, :, tile * LANES : (tile + 1) * LANES] = result


def widen(sizes, place, level, coarse, target, rows):
    depth = coarse.shape[1]
    for (start, stop), tile, turn in transfer_plan(sizes, place, level, "all"):
        columns = split(coarse[0:rows, :, tile * LANES : (tile + 1) * LANES].reshape(rows * depth, LANES))
        result = dot(columns, pair_table(stop - start, 1, turn, 4.0))
        target[0:rows, :, start:stop] = result.reshape(rows, depth, stop - start)


def coefficients(sizes, place, level, count, conduct, binding, fx, fy, fz, weight):
    guard = level > 0 or sizes.sides > 1
    for row in range(1, count):
        fx[row - 1] = harmonic(conduct(row - 1), conduct(row), guard)
    for row in range(1, count - 1):
        mine = conduct(row)
        south = harmonic(mine, roll(mine, 1, 1), guard)
        if level == 0 and sizes.sides < 2:
            cut = 0 if sizes.sides == 0 else jnp.where(place[1] == 0, 0, sizes.extent_y)
            south = jnp.where(lane_at(mine.shape) == cut, 0.0, south)
        below = harmonic(mine, roll(mine, 1, 0), guard)
        below = jnp.where(lax.broadcasted_iota(jnp.int32, mine.shape, 0) == 0, 0.0, below)
        diagonal = fx[row - 1] + fx[row] + binding(row)
        diagonal = diagonal + (south + roll(south, -1, 1)) + (below + roll(below, -1, 0))
        if guard:
            diagonal = jnp.maximum(diagonal, 1e-6)
        fy[row - 1] = south
        fz[row - 1] = below
        weight[row - 1] = relax_weight * reciprocal(diagonal)


def sweep(count, field, binding, fx, fy, fz, emit):
    lower = fx[0] * (field(1) - field(0))
    for row in range(1, count - 1):
        mine = field(row)
        upper = fx[row] * (field(row + 1) - mine)
        south = fy[row - 1] * (mine - roll(mine, 1, 1))
        below = fz[row - 1] * (mine - roll(mine, 1, 0))
        across = (south - roll(south, -1, 1)) + (below - roll(below, -1, 0))
        emit(row, binding(row) * mine + (lower - upper) + across)
        lower = upper


def own_defect(count, smooth, source, binding, fx, fy, fz, sums, first):
    zero = jnp.zeros(smooth.shape[1:], f32)

    def field(row):
        return smooth[row - 1] if 0 < row < count - 1 else zero

    def add(row, value):
        slot = (row + first) // 2
        if (row + first) % 2 == 0 or row == 0:
            sums[slot] = value
        else:
            sums[slot] = sums[slot] + value

    add(0, fx[0] * field(1))
    sweep(count, field, binding, fx, fy, fz, lambda row, result: add(row, source(row) - result))
    add(count - 1, fx[count - 2] * field(count - 2))


def parts(array, counts):
    views, start = [], 0
    for count in counts:
        views.append(array.at[start : start + count])
        start += count
    return views


def coefficient_rows(sizes, level):
    n = sizes.rows[level]
    if level == 0:
        return [n + 1, n, n, n, n]
    return [n + 3] + [n + 2] * 6


def start_kernel(sizes, place, right_side, conduct, binding, own0, own1, own2, to_next, to_prev, top, *refs):
    edges, sums = refs[: sizes.sides], refs[-1]
    n0, n1, n2 = sizes.rows[:3]
    for at, array in enumerate((conduct, binding, right_side)):
        own0[at] = jnp.swapaxes(array[...], 0, 1)
    for at in (0, 1):
        for row in range(n1):
            sums[at * n1 + row] = own0[at, 2 * row] + own0[at, 2 * row + 1]
    narrow(sizes, place, 0, sums, own1, 2 * n1, "own")
    for row in range(2 * n2):
        sums[row, :, : sizes.own[1] * LANES] = own1[2 * row] + own1[2 * row + 1]
    narrow(sizes, place, 1, sums, own2, 2 * n2, "own")
    last = jnp.concatenate([own2[0] + own2[1], own2[n2] + own2[n2 + 1]], axis=0)
    last = dot(split(last), pair_table(LANES, 0, None, 0.25))
    top[0] = last[: sizes.depth] + roll(last[sizes.depth :], LANES // 2, 1)
    for message, low, at1, at0 in ((to_next, n1 - 2, n1 - 1, n0 - 1), (to_prev, 0, 0, 0)):
        edge = n2 - 1 if at0 else 0
        rows = (own0[0, at0], own1[low], own1[low + 1], own1[n1 + at1])
        rows += (own2[n2 - 2], own2[n2 - 1], own2[n2 + edge])
        for slot, row in zip(sizes.slots, rows):
            put(message, slot, row)
    last = sizes.extent_y - BORDER
    if sizes.sides == 1:
        at = pl.multiple_of(jnp.where(place[1] == 0, last, 0), LANES)
        edges[0][...] = own0[:, :, :, pl.ds(at, BORDER)]
    elif sizes.sides == 2:
        edges[0][...] = own0[:, :, :, last:]
        edges[1][...] = own0[:, :, :, :BORDER]


def message_row(sizes, place, level, slot, message, beside):
    start, tiles = slot
    row = get(message, slot)
    if sizes.sides == 1:
        left = place[1] != 0
        tile = beside[0][start + jnp.where(left, tiles - 1, 0)]
        if level > 0:
            reach = BORDER >> level
            lane = lane_at(tile.shape)
            first = jnp.where(left, LANES - reach, 0)
            tile = jnp.where((lane >= first) & (lane < first + reach), tile, 0.0)
        row.append(tile)
    elif sizes.sides == 2:
        right, left = beside[0][start], beside[1][start + tiles - 1]
        if level == 0:
            row += [right, left]
        else:
            reach = BORDER >> level
            lane = lane_at(right.shape)
            row.append(jnp.where(lane < reach, right, jnp.where(lane >= LANES - reach, left, 0.0)))
    return jnp.concatenate(row, axis=1)


def fringe_lanes(shape):
    lane = lane_at(shape)
    return (lane < FRINGE) | (lane >= LANES - FRINGE)


def put_fringes(sizes, message, rows):
    total = None
    for index, (level, row) in enumerate(rows):
        tile = row[:, sizes.own[level] * LANES :]
        tile = jnp.where(fringe_lanes(tile.shape), tile, 0.0)
        tile = roll(tile, SPREAD * index + SPREAD // 2, 1)
        total = tile if total is None else total + tile
    message[sizes.tiles] = total


def fringed_row(sizes, level, index, message):
    row = get(message, sizes.slots[index])
    if sizes.border[level]:
        if level == 0:
            row += [jnp.zeros(row[0].shape, f32)] * sizes.border[0]
        else:
            tile = roll(message[sizes.tiles], -(SPREAD * (index - 1) + SPREAD // 2), 1)
            row.append(jnp.where(fringe_lanes(tile.shape), tile, 0.0))
    return jnp.concatenate(row, axis=1)


def packing(sizes, count):
    half, reach = LANES // 2, BORDER >> 3
    pairs = -(-count // 2)
    if sizes.sides != 1 or count * reach > LANES:
        return False, count, None, None
    if count % 2 and count * reach <= half:
        return True, pairs, pairs - 1, half
    return True, pairs + 1, pairs, 0


def border_turn(place, first, index):
    reach = BORDER >> 3
    goal = first + index * reach
    return jnp.where(place[1] == 0, (goal - LANES // 2) % LANES, (goal + reach) % LANES)


def pack_rows(sizes, place, rows, target):
    packed, tiles, border, first = packing(sizes, len(rows))
    if not packed:
        for index, row in enumerate(rows):
            target[index] = row
        return
    half, reach = LANES // 2, BORDER >> 3
    lane = lane_at(rows[0].shape)
    held = [jnp.zeros(rows[0].shape, f32)] * tiles
    for index, row in enumerate(rows):
        if index % 2 == 0:
            held[index // 2] = jnp.where(lane < half, row, 0.0)
        else:
            held[index // 2] = jnp.where(lane < half, held[index // 2], pltpu.roll(row, half, axis=1))
    for index, row in enumerate(rows):
        start = first + index * reach
        moved = pltpu.roll(row, border_turn(place, first, index), axis=1)
        held[border] = jnp.where((lane >= start) & (lane < start + reach), moved, held[border])
    for index, tile in enumerate(held):
        target[index] = tile


def unpack_rows(sizes, place, blocks, count):
    packed, _, border, first = packing(sizes, count)
    if not packed:
        return [blocks[index] for index in range(count)]
    half, reach = LANES // 2, BORDER >> 3
    rows = []
    for index in range(count):
        own = blocks[index // 2]
        lane = lane_at(own.shape)
        if index % 2:
            own = pltpu.roll(own, half, axis=1)
        back = lax.rem(LANES - border_turn(place, first, index), LANES)
        beside = pltpu.roll(blocks[border], back, axis=1)
        start = jnp.where(place[1] == 0, half, LANES - reach)
        here = (lane >= start) & (lane < start + reach)
        rows.append(jnp.where(lane < half, own, jnp.where(here, beside, 0.0)))
    return rows


def merge_into(sizes, place, stride, radix, arrays, target):
    position = (place[0] // stride) % radix
    target[...] = jnp.zeros(target.shape, f32)
    for step, array in enumerate(arrays):
        at = (position ^ step) * stride
        for index, row in enumerate(unpack_rows(sizes, place, array, stride + 2)):
            target[at + index] = target[at + index] + row


def merge_kernel(sizes, stride, radix, place, *refs):
    arrays, out, total = refs[:radix], refs[radix], refs[radix + 1]
    merge_into(sizes, place, stride, radix, arrays, total)
    pack_rows(sizes, place, [total[row] for row in range(stride * radix + 2)], out)


def top_row(sizes, place, block, beside):
    half, reach = LANES // 2, BORDER >> 3
    lane = lane_at(block.shape)
    values = [jnp.where(lane < half, block, 0.0), jnp.where(lane < half, pltpu.roll(block, half, axis=1), 0.0)]
    right = (lane >= half) & (lane < half + reach)
    left = lane >= LANES - reach
    for side in range(sizes.sides):
        other = beside[side]
        if sizes.sides == 2:
            here = left if side else right
        else:
            first = jnp.where(place[1] == 0, half, LANES - reach)
            here = (lane >= first) & (lane < first + reach)
        values[0] = jnp.where(here, pltpu.roll(other, half, axis=1), values[0])
        values[1] = jnp.where(here, other, values[1])
    return values


def down_kernel(sizes, place, *refs):
    s = sizes.sides
    owns, refs = refs[:3], refs[3:]
    borders0, refs = refs[:s], refs[s:]
    from_prev, from_next, refs = refs[0], refs[1], refs[2:]
    beside_prev, beside_next, refs = refs[: 2 * s : 2], refs[1 : 2 * s : 2], refs[2 * s :]
    coefs, contribution, ups, fars, refs = refs[:3], refs[3], refs[4:6], refs[6:8], refs[8:]
    border1, border2, level3, sums = refs
    slots = sizes.slots
    n0, n1, n2 = sizes.rows[:3]

    if s:
        for row in range(2 * n1):
            for side in range(s):
                columns = slice(side * LANES, (side + 1) * LANES)
                at, low = row // n1, 2 * (row % n1)
                sums[row, :, columns] = borders0[side][at, low] + borders0[side][at, low + 1]
        narrow(sizes, place, 0, sums, border1, 2 * n1, "border", sizes.own[0] * LANES)
        for row in range(2 * n2):
            sums[row, :, :LANES] = border1[2 * row] + border1[2 * row + 1]
        narrow(sizes, place, 1, sums, border2, 2 * n2, "border", sizes.own[1] * LANES)

    def held_row(level, at, row):
        if level == 0:
            tiles = [owns[0][at, row], *(array[at, row] for array in borders0)]
        else:
            row = at * sizes.rows[level] + row
            tiles = [owns[level][row], *([(border1, border2)[level - 1][row]] if s else [])]
        return jnp.concatenate(tiles, axis=1)

    def prev_row(level, index):
        return message_row(sizes, place, level, slots[index], from_prev, beside_prev)

    def next_row(level, index):
        return message_row(sizes, place, level, slots[index], from_next, beside_next)

    def conduct0(row):
        if row == 0:
            return prev_row(0, 0)
        if row == n0 + 1:
            return next_row(0, 0)
        return held_row(0, 0, row - 1)

    bound0 = lambda row: held_row(0, 1, row - 1)
    fx, fy, fz, weight, v0 = parts(coefs[0], coefficient_rows(sizes, 0))
    coefficients(sizes, place, 0, n0 + 2, conduct0, bound0, fx, fy, fz, weight)
    for row in range(n0):
        v0[row] = weight[row] * held_row(0, 2, row)
    own_defect(n0 + 2, v0, lambda row: held_row(0, 2, row - 1), bound0, fx, fy, fz, sums, 1)
    smooths, sources = [], []
    for level, first in ((1, 1), (2, 4)):
        n = sizes.rows[level]
        fx, fy, fz, weight, binding, source, smooth = parts(coefs[level], coefficient_rows(sizes, level))
        held = sizes.held[level]
        narrow(sizes, place, level - 1, sums.at[:, :, : sizes.held[level - 1]], source, n + 2)
        binding[0] = prev_row(level, first + 2)
        binding[n + 1] = next_row(level, first + 2)
        for row in range(n):
            binding[row + 1] = held_row(level, 1, row)

        def conduct(row, n=n, level=level, first=first):
            if row < 2:
                return prev_row(level, first + row)
            if row >= n + 2:
                return next_row(level, first + row - n - 2)
            return held_row(level, 0, row - 2)

        bound = lambda row, binding=binding: binding[row - 1]
        coefficients(sizes, place, level, n + 4, conduct, bound, fx, fy, fz, weight)
        for row in range(n + 2):
            smooth[row] = weight[row] * source[row]
        mine = lambda row, source=source: source[row - 1]
        own_defect(n + 4, smooth, mine, bound, fx, fy, fz, sums.at[:, :, :held], 0)
        smooths.append(smooth)
        sources.append(source)
    narrow(sizes, place, 2, sums.at[:, :, : sizes.held[2]], level3, 3)

    pack_rows(sizes, place, [level3[row] for row in range(3)], contribution)
    (s1, s2), (v1, v2) = sources, smooths
    for at, rows in enumerate(
        (
            (v0[n0 - 1], s1[n1], s1[n1 + 1], v1[n1 - 1], s2[n2], s2[n2 + 1], v2[n2 - 1]),
            (v0[0], s1[1], s1[0], v1[2], s2[1], s2[0], v2[2]),
        )
    ):
        for slot, row in zip(slots, rows):
            put(ups[at], slot, row)
        if s:
            put_fringes(sizes, ups[at], list(zip((1, 1, 1, 2, 2, 2), rows[1:])))
        put(fars[at], (0, sizes.held[2] // LANES), v2[n2 + 1 if at == 0 else 0])


def relax(count, field, refs_of, source, target):
    fx, fy, fz, weight, binding = refs_of

    def update(row, value):
        target(row, field(row) + weight[row - 1] * (source(row) - value))

    sweep(count, field, binding, fx, fy, fz, update)


def store(array, first):
    def put_row(row, value):
        array[row - first] = value

    return put_row


def coarse_kernel(sizes, stride, radix, place, *refs):
    s = sizes.sides
    blocks, tops, refs = refs[:radix], refs[radix : 2 * radix], refs[2 * radix :]
    beside, refs = [refs[side * radix : (side + 1) * radix] for side in range(s)], refs[s * radix :]
    out, merged, sums = refs[:3]
    coarse = [refs[3 + 9 * index : 12 + 9 * index] for index in range(3)]
    total = sizes.span_count
    merge_into(sizes, place, stride, radix, blocks, merged)
    zero = jnp.zeros((sizes.depth, LANES), f32)
    for index in range(3):
        level = 3 + index
        fx, fy, fz, weight, conduct, binding, source, smooth, iterate = coarse[index]
        count = total >> index
        for array in (conduct, smooth, iterate):
            array[0] = zero
            array[count + 1] = zero
        if index == 0:
            source = merged.at[1 : count + 1]
            base = place[0] // stride % radix
            for step in range(radix):
                for low in range(stride):
                    row = ((base ^ step) * stride) + ((place[0] % stride) ^ low)
                    others = [arrays[step][low] for arrays in beside]
                    conduct[row + 1], binding[row] = top_row(sizes, place, tops[step][low], others)
        bound = lambda row, binding=binding: binding[row - 1]
        at_row = lambda row, conduct=conduct: conduct[row]
        coefficients(sizes, place, level, count + 2, at_row, bound, fx, fy, fz, weight)
        for row in range(count):
            smooth[row + 1] = weight[row] * source[row]
        if index < 2:
            conduct_next, binding_next, source_next = coarse[index + 1][4:7]
            half = count // 2
            for row in range(half):
                sums[row, :, :LANES] = conduct[2 * row + 1] + conduct[2 * row + 2]
            narrow(sizes, place, level, sums, conduct_next.at[1 : half + 1], half)
            for row in range(half):
                sums[row, :, :LANES] = binding[2 * row] + binding[2 * row + 1]
            narrow(sizes, place, level, sums, binding_next, half)

            def add(row, value, source=source):
                value = source[row - 1] - value
                slot = (row - 1) // 2
                if row % 2 == 1:
                    sums[slot, :, :LANES] = value
                else:
                    sums[slot, :, :LANES] = sums[slot, :, :LANES] + value

            sweep(count + 2, lambda row, smooth=smooth: smooth[row], bound, fx, fy, fz, add)
            narrow(sizes, place, level, sums, source_next, half)

    fx, fy, fz, weight, conduct, binding, source, smooth, iterate = coarse[2]
    held, other = smooth, iterate
    for _ in range(COARSE_SWEEPS - 1):
        field = lambda row, held=held: held[row]
        mine = lambda row: source[row - 1]
        bound = lambda row: binding[row - 1]
        relax((total >> 2) + 2, field, (fx, fy, fz, weight, bound), mine, store(other, 0))
        held, other = other, held
    for index in (1, 0):
        fx, fy, fz, weight, conduct, binding, source, smooth, iterate = coarse[index]
        if index == 0:
            source = merged.at[1 : total + 1]
        count = total >> index
        widen(sizes, place, 3 + index, held.at[1 : count // 2 + 1], sums, count // 2)
        for row in range(count):
            smooth[row + 1] = smooth[row + 1] + sums[row // 2, :, :LANES]
        field = lambda row, smooth=smooth: smooth[row]
        mine = lambda row, source=source: source[row - 1]
        bound = lambda row, binding=binding: binding[row - 1]
        relax(count + 2, field, (fx, fy, fz, weight, bound), mine, store(iterate, 0))
        held = iterate

    out[...] = held[pl.ds(place[0], 3)]


def up_kernel(sizes, place, coarse, *refs):
    s = sizes.sides
    (from_prev, from_next), fars, coefs, own0 = refs[:2], refs[2:4], refs[4:7], refs[7]
    borders0, out, refs = refs[8 : 8 + s], refs[8 + s], refs[9 + s :]
    total1, total2, result = refs[:3]
    over2, over1, over0, lift2, lift1, lift0, it2, it1, it0, semaphores = refs[3:]
    slots = sizes.slots
    n0, n1, n2 = sizes.rows[:3]
    width = sizes.own[0] * LANES

    widen(sizes, place, 2, coarse, over2, 3)
    for level, array, first, totals, over, lift, target, upper in (
        (2, coefs[2], 4, total2, over2, lift2, it2, over1),
        (1, coefs[1], 1, total1, over1, lift1, it1, over0),
    ):
        n = sizes.rows[level]
        fx, fy, fz, weight, binding, own, smooth = parts(array, coefficient_rows(sizes, level))
        edge = {}
        for row, message, index in (
            (1, from_prev, first),
            (2, from_prev, first + 1),
            (n + 2, from_next, first),
            (n + 1, from_next, first + 1),
        ):
            value = edge.get(row, own[row - 1])
            edge[row] = value + fringed_row(sizes, level, index, message)
        for row, value in edge.items():
            totals[row - 1] = value
        for row in range(n + 4):
            if row in (0, n + 3):
                value = fringed_row(sizes, level, first + 2, from_next if row else from_prev)
                if level == 2:
                    far = fars[1 if row else 0]
                    value = value + jnp.concatenate(get(far, (0, sizes.held[2] // LANES)), axis=1)
            elif row in edge:
                value = weight[row - 1] * totals[row - 1]
            else:
                value = smooth[row - 1]
            lift[row] = value + over[row // 2]
        field = lambda row, lift=lift: lift[row]
        mine = lambda row, own=own, totals=totals, edge=edge: (totals if row in edge else own)[row - 1]
        bound = lambda row, binding=binding: binding[row - 1]
        relax(n + 4, field, (fx, fy, fz, weight, bound), mine, store(target, 1))
        widen(sizes, place, level - 1, target, upper, n + 2)

    def held_row(at, row):
        return jnp.concatenate([own0[at, row - 1], *(array[at, row - 1] for array in borders0)], axis=1)

    fx, fy, fz, weight, v0 = parts(coefs[0], coefficient_rows(sizes, 0))
    lift0[0] = fringed_row(sizes, 0, 0, from_prev) + over0[0]
    lift0[n0 + 1] = fringed_row(sizes, 0, 0, from_next) + over0[n1 + 1]
    for row in range(1, n0 + 1):
        lift0[row] = v0[row - 1] + over0[(row + 1) // 2]
    field = lambda row: lift0[row]
    bound = lambda row: held_row(1, row)
    relax(n0 + 2, field, (fx, fy, fz, weight, bound), lambda row: held_row(2, row), store(it0, 1))
    step = sizes.depth // CHUNKS
    copies = []
    for chunk in range(CHUNKS):
        part = slice(chunk * step, (chunk + 1) * step)
        result[part] = jnp.swapaxes(it0[:, part, :width], 0, 1)
        copies.append(pltpu.make_async_copy(result.at[part], out.at[part], semaphores.at[chunk]))
        copies[-1].start()
    for copy in copies:
        copy.wait()


def call(body, name, outputs, scratch, place, inputs, copies=0, far_out=False):
    near, far = pl.BlockSpec(memory_space=pltpu.VMEM), pl.BlockSpec(memory_space=pl.ANY)
    scratch = [pltpu.VMEM(shape, f32) for shape in scratch]
    if copies:
        scratch.append(pltpu.SemaphoreType.DMA((copies,)))
    return pl.pallas_call(
        body,
        name=name,
        out_shape=[jax.ShapeDtypeStruct(shape, f32) for shape in outputs],
        in_specs=[pl.BlockSpec(memory_space=pltpu.SMEM)] + [near] * len(inputs),
        out_specs=[far if far_out else near] * len(outputs),
        scratch_shapes=scratch,
        compiler_params=pltpu.CompilerParams(vmem_limit_bytes=VMEM_LIMIT),
    )(place, *inputs)


def along(value, axis, steps):
    count = lax.axis_size(axis)
    initial, last = max(0, -steps), min(count, count - steps)
    return lax.ppermute(value, axis, [(source, source + steps) for source in range(initial, last)])


def beside(values, sizes):
    if sizes.sides == 1:
        return [[lax.ppermute(value, "width", [(0, 1), (1, 0)]) for value in values]]
    if sizes.sides == 2:
        return [[along(value, "width", steps) for value in values] for steps in (-1, 1)]
    return []


def stages(count):
    stride = 1
    while stride < count:
        radix = 4 if count // stride % 4 == 0 else 2
        yield stride, radix
        stride *= radix


def swap(value, stride, radix):
    count = lax.axis_size("span")
    return [value] + [
        lax.ppermute(value, "span", [(device, device ^ step * stride) for device in range(count)])
        for step in range(1, radix)
    ]


def on_device(right_side, diffusivity, reaction):
    depth, extent_x, extent_y = diffusivity.shape
    sizes = Sizes(depth, extent_x, extent_y, lax.axis_size("span"), lax.axis_size("width"))
    place = jnp.stack([lax.axis_index("span"), lax.axis_index("width")]).astype(jnp.int32)
    n0, n1, n2, n3 = sizes.rows
    s = sizes.sides
    tile = (depth, LANES)
    own = [(depth, count * LANES) for count in sizes.own]
    held = [(depth, count) for count in sizes.held]
    down_message = (sizes.tiles, *tile)
    up_message = (sizes.tiles + 1, *tile)
    own0, own1, own2, to_next, to_prev, top, *edges = call(
        functools.partial(start_kernel, sizes),
        "start",
        [(3, n0, *own[0]), (2 * n1, *own[1]), (2 * n2, *own[2]), down_message, down_message]
        + [(1, *tile)]
        + [(3, n0, depth, BORDER)] * s,
        [(2 * n1, *own[0])],
        place,
        [right_side, diffusivity, reaction],
    )
    halos = [along(to_next, "span", 1), along(to_prev, "span", -1)]
    if s == 1:
        borders = [lax.ppermute(edges[0], "width", [(0, 1), (1, 0)])]
    elif s == 2:
        borders = [along(edges[1], "width", -1), along(edges[0], "width", 1)]
    else:
        borders = []
    plan = list(stages(sizes.span_count))
    for stride, radix in plan[:-1]:
        top = jnp.concatenate(swap(top, stride, radix))
    sides = beside(halos, sizes)
    tops = swap(top, *plan[-1])
    beside_tops = beside(tops, sizes)
    halos, sides, tops, beside_tops = lax.optimization_barrier((halos, sides, tops, beside_tops))

    lengths = [sum(coefficient_rows(sizes, level)) for level in range(3)]
    far = (sizes.held[2] // LANES, *tile)
    coefs = [(lengths[level], *held[level]) for level in range(3)]
    downs = call(
        functools.partial(down_kernel, sizes),
        "down",
        [*coefs, (packing(sizes, 3)[1], *tile), up_message, up_message, far, far],
        [(2 * n1, *tile), (2 * n2, *tile), (3, *tile), (max(2 * n1, n1 + 2), *held[0])],
        place,
        [own0, own1, own2, *borders, *halos, *sum(sides, [])],
    )
    coefs_out, blocks, ups, fars = downs[:3], downs[3], downs[4:6], downs[6:8]
    for stride, radix in plan[:-1]:
        rows = stride * radix + 2
        (blocks,) = call(
            functools.partial(merge_kernel, sizes, stride, radix),
            "merge",
            [(packing(sizes, rows)[1], *tile)],
            [(rows, *tile)],
            place,
            swap(blocks, stride, radix),
        )
    blocks, *sent = lax.optimization_barrier((blocks, *ups, *fars))
    stride, radix = plan[-1]
    blocks = swap(blocks, stride, radix)
    received = [along(sent[0], "span", 1), along(sent[1], "span", -1)]
    received += [along(sent[2], "span", 2), along(sent[3], "span", -2)]
    scratch = [(sizes.span_count + 2, *tile), (max(sizes.span_count // 2, 2), *tile)]
    for index in range(3):
        count = sizes.span_count >> index
        scratch += [(count + 1, *tile)] + [(count, *tile)] * 3 + [(count + 2, *tile)] + [(count, *tile)] * 2
        scratch += [(count + 2, *tile)] * 2
    (coarse,) = call(
        functools.partial(coarse_kernel, sizes, stride, radix),
        "coarse",
        [(n3 + 2, *tile)],
        scratch,
        place,
        [*blocks, *tops, *sum(beside_tops, [])],
    )
    scratch = [(n1 + 2, *held[1]), (n2 + 2, *held[2]), diffusivity.shape]
    scratch += [(n3 + 2, *held[2]), (n2 + 2, *held[1]), (n1 + 2, *held[0])]
    scratch += [(n2 + 4, *held[2]), (n1 + 4, *held[1]), (n0 + 2, *held[0])]
    scratch += [(n2 + 2, *held[2]), (n1 + 2, *held[1]), (n0, *held[0])]
    (correction,) = call(
        functools.partial(up_kernel, sizes),
        "up",
        [diffusivity.shape],
        scratch,
        place,
        [coarse, *received, *coefs_out, own0, *borders],
        copies=CHUNKS,
        far_out=True,
    )
    return correction


def solution(mesh):
    in_specs = (P(None, "span", "width"),) * 3
    return jax.shard_map(
        on_device, mesh=mesh, in_specs=in_specs, out_specs=P(None, "span", "width"), check_vma=False
    )
```

```python
import functools

import jax
import jax.numpy as jnp
from jax import lax
from jax.experimental import pallas as pl
from jax.experimental.pallas import tpu as pltpu
from jax.sharding import PartitionSpec as P

LEVELS = 6
COARSE_SWEEPS = 3
LANES = 128
BORDER = 128
FRINGE = 4
SPREAD = 16
relax_weight = 0.8
f32 = jnp.float32
VMEM_LIMIT = 32 * 1024 * 1024
CHUNKS = 4


class Sizes:
    def __init__(self, depth, extent_x, extent_y, span_count, width_count):
        self.depth, self.extent_x, self.extent_y = depth, extent_x, extent_y
        self.span_count, self.width_count = span_count, width_count
        self.sides = min(width_count - 1, 2)
        self.own = [(extent_y >> level) // LANES for level in range(3)]
        self.border = [self.sides, min(self.sides, 1), min(self.sides, 1)]
        self.held = [(self.own[level] + self.border[level]) * LANES for level in range(3)] + [LANES] * 3
        self.rows = [extent_x >> level for level in range(4)]
        self.slots = []
        start = 0
        for level in (0, 1, 1, 1, 2, 2, 2):
            self.slots.append((start, self.own[level]))
            start += self.own[level]
        self.tiles = start


def put(message, slot, row):
    start, tiles = slot
    for tile in range(tiles):
        message[start + tile] = row[:, tile * LANES : (tile + 1) * LANES]


def get(message, slot):
    start, tiles = slot
    return [message[start + tile] for tile in range(tiles)]


def lane_at(shape):
    return lax.broadcasted_iota(jnp.int32, shape, len(shape) - 1)


def roll(value, steps, axis):
    return pltpu.roll(value, steps % value.shape[axis], axis=axis)


def reciprocal(value):
    return pltpu.reciprocal(value, approx=True)


def harmonic(first, second, guard):
    total = first + second
    if guard:
        total = jnp.maximum(total, 1e-3)
    return (2.0 * first) * second * reciprocal(total)


def split(value):
    high = value.astype(jnp.bfloat16)
    return high, (value - high.astype(f32)).astype(jnp.bfloat16)


def dot(halves, table):
    high, low = halves
    return jnp.dot(high, table, preferred_element_type=f32) + jnp.dot(low, table, preferred_element_type=f32)


def pair_table(fine, fine_dim, turn, weight):
    shape = (fine, LANES) if fine_dim == 0 else (LANES, fine)
    fine_at = lax.broadcasted_iota(jnp.int32, shape, fine_dim)
    coarse_at = lax.broadcasted_iota(jnp.int32, shape, 1 - fine_dim)
    if turn is not None:
        coarse_at = coarse_at - jnp.where(fine_at >= turn, LANES // 2, 0)
    return jnp.where(fine_at // 2 == coarse_at, weight, 0.0).astype(jnp.bfloat16)


def turns(sizes, place, level):
    if sizes.sides == 0:
        return []
    if level == 0:
        return [jnp.where(place[1] == 0, LANES, 0)] if sizes.sides == 1 else [LANES, 0]
    return [LANES // 2]


def transfer_plan(sizes, place, level, part):
    plan = []
    if level >= 3:
        return [((0, LANES), 0, 3 * LANES // 4)]
    if level == 2:
        return [((0, sizes.held[2]), 0, None)]
    own = sizes.own[level]
    if part != "border":
        plan += [((2 * LANES * tile, 2 * LANES * (tile + 1)), tile, None) for tile in range(own // 2)]
    if part != "own":
        for index, turn in enumerate(turns(sizes, place, level)):
            start = (own + index) * LANES
            plan.append(((start, start + LANES), own // 2, turn))
    return plan


def narrow(sizes, place, level, sums, target, rows, part="all", shift=0):
    depth = sums.shape[1]
    done = {}
    for (start, stop), tile, turn in transfer_plan(sizes, place, level, part):
        start, stop, tile = start - shift, stop - shift, tile - shift // (2 * LANES)
        columns = split(sums[0:rows, :, start:stop].reshape(rows * depth, stop - start))
        result = dot(columns, pair_table(stop - start, 0, turn, 0.25)).reshape(rows, depth, LANES)
        done[tile] = done[tile] + result if tile in done else result
    for tile, result in done.items():
        target[0:rows, :, tile * LANES : (tile + 1) * LANES] = result


def widen(sizes, place, level, coarse, target, rows):
    depth = coarse.shape[1]
    for (start, stop), tile, turn in transfer_plan(sizes, place, level, "all"):
        columns = split(coarse[0:rows, :, tile * LANES : (tile + 1) * LANES].reshape(rows * depth, LANES))
        result = dot(columns, pair_table(stop - start, 1, turn, 4.0))
        target[0:rows, :, start:stop] = result.reshape(rows, depth, stop - start)


def coefficients(sizes, place, level, count, conduct, binding, fx, fy, fz, weight):
    guard = level > 0 or sizes.sides > 1
    for row in range(1, count):
        fx[row - 1] = harmonic(conduct(row - 1), conduct(row), guard)
    for row in range(1, count - 1):
        mine = conduct(row)
        south = harmonic(mine, roll(mine, 1, 1), guard)
        if level == 0 and sizes.sides < 2:
            cut = 0 if sizes.sides == 0 else jnp.where(place[1] == 0, 0, sizes.extent_y)
            south = jnp.where(lane_at(mine.shape) == cut, 0.0, south)
        below = harmonic(mine, roll(mine, 1, 0), guard)
        below = jnp.where(lax.broadcasted_iota(jnp.int32, mine.shape, 0) == 0, 0.0, below)
        diagonal = fx[row - 1] + fx[row] + binding(row)
        diagonal = diagonal + (south + roll(south, -1, 1)) + (below + roll(below, -1, 0))
        if guard:
            diagonal = jnp.maximum(diagonal, 1e-6)
        fy[row - 1] = south
        fz[row - 1] = below
        weight[row - 1] = relax_weight * reciprocal(diagonal)


def sweep(count, field, binding, fx, fy, fz, emit):
    lower = fx[0] * (field(1) - field(0))
    for row in range(1, count - 1):
        mine = field(row)
        upper = fx[row] * (field(row + 1) - mine)
        south = fy[row - 1] * (mine - roll(mine, 1, 1))
        below = fz[row - 1] * (mine - roll(mine, 1, 0))
        across = (south - roll(south, -1, 1)) + (below - roll(below, -1, 0))
        emit(row, binding(row) * mine + (lower - upper) + across)
        lower = upper


def own_defect(count, smooth, source, binding, fx, fy, fz, sums, first):
    zero = jnp.zeros(smooth.shape[1:], f32)

    def field(row):
        return smooth[row - 1] if 0 < row < count - 1 else zero

    def add(row, value):
        slot = (row + first) // 2
        if (row + first) % 2 == 0 or row == 0:
            sums[slot] = value
        else:
            sums[slot] = sums[slot] + value

    add(0, fx[0] * field(1))
    sweep(count, field, binding, fx, fy, fz, lambda row, result: add(row, source(row) - result))
    add(count - 1, fx[count - 2] * field(count - 2))


def parts(array, counts):
    views, start = [], 0
    for count in counts:
        views.append(array.at[start : start + count])
        start += count
    return views


def coefficient_rows(sizes, level):
    n = sizes.rows[level]
    if level == 0:
        return [n + 1, n, n, n, n]
    return [n + 3] + [n + 2] * 6


def start_kernel(sizes, place, conduct, binding, own0, own1, own2, to_next, to_prev, sums):
    n0, n1, n2 = sizes.rows[:3]
    for at, array in enumerate((conduct, binding)):
        own0[at] = jnp.swapaxes(array[...], 0, 1)
    for at in (0, 1):
        for row in range(n1):
            sums[at * n1 + row] = own0[at, 2 * row] + own0[at, 2 * row + 1]
    narrow(sizes, place, 0, sums, own1, 2 * n1, "own")
    for row in range(2 * n2):
        sums[row, :, : sizes.own[1] * LANES] = own1[2 * row] + own1[2 * row + 1]
    narrow(sizes, place, 1, sums, own2, 2 * n2, "own")
    for message, low, at1, at0 in ((to_next, n1 - 2, n1 - 1, n0 - 1), (to_prev, 0, 0, 0)):
        edge = n2 - 1 if at0 else 0
        rows = (own0[0, at0], own1[low], own1[low + 1], own1[n1 + at1])
        rows += (own2[n2 - 2], own2[n2 - 1], own2[n2 + edge])
        for slot, row in zip(sizes.slots, rows):
            put(message, slot, row)


def turn_kernel(sizes, place, right_side, own0, turned, *edges):
    turned[...] = jnp.swapaxes(right_side[...], 0, 1)
    last = sizes.extent_y - BORDER
    for index, array in enumerate((own0.at[0], own0.at[1], turned)):
        if sizes.sides == 1:
            at = pl.multiple_of(jnp.where(place[1] == 0, last, 0), LANES)
            edges[0][index] = array[:, :, pl.ds(at, BORDER)]
        elif sizes.sides == 2:
            edges[0][index] = array[:, :, last:]
            edges[1][index] = array[:, :, :BORDER]


def message_row(sizes, place, level, slot, message, beside):
    start, tiles = slot
    row = get(message, slot)
    if sizes.sides == 1:
        left = place[1] != 0
        tile = beside[0][start + jnp.where(left, tiles - 1, 0)]
        if level > 0:
            reach = BORDER >> level
            lane = lane_at(tile.shape)
            first = jnp.where(left, LANES - reach, 0)
            tile = jnp.where((lane >= first) & (lane < first + reach), tile, 0.0)
        row.append(tile)
    elif sizes.sides == 2:
        right, left = beside[0][start], beside[1][start + tiles - 1]
        if level == 0:
            row += [right, left]
        else:
            reach = BORDER >> level
            lane = lane_at(right.shape)
            row.append(jnp.where(lane < reach, right, jnp.where(lane >= LANES - reach, left, 0.0)))
    return jnp.concatenate(row, axis=1)


def fringe_lanes(shape):
    lane = lane_at(shape)
    return (lane < FRINGE) | (lane >= LANES - FRINGE)


def put_fringes(sizes, message, rows):
    total = None
    for index, (level, row) in enumerate(rows):
        tile = row[:, sizes.own[level] * LANES :]
        tile = jnp.where(fringe_lanes(tile.shape), tile, 0.0)
        tile = roll(tile, SPREAD * index + SPREAD // 2, 1)
        total = tile if total is None else total + tile
    message[sizes.tiles] = total


def fringed_row(sizes, level, index, message):
    row = get(message, sizes.slots[index])
    if sizes.border[level]:
        if level == 0:
            row += [jnp.zeros(row[0].shape, f32)] * sizes.border[0]
        else:
            tile = roll(message[sizes.tiles], -(SPREAD * (index - 1) + SPREAD // 2), 1)
            row.append(jnp.where(fringe_lanes(tile.shape), tile, 0.0))
    return jnp.concatenate(row, axis=1)


def packing(sizes, count):
    if sizes.sides != 1:
        return False, count, count
    own = -(-count // 2)
    return True, own, own - (-count * (BORDER >> 3) // LANES)


def border_turn(place, goal):
    return jnp.where(place[1] == 0, (goal - LANES // 2) % LANES, (goal + (BORDER >> 3)) % LANES)


def pack_rows(sizes, place, rows, target):
    packed, own, tiles = packing(sizes, len(rows))
    if not packed:
        for index, row in enumerate(rows):
            target[index] = row
        return
    half, reach = LANES // 2, BORDER >> 3
    lane = lane_at(rows[0].shape)
    for index in range(own):
        held = rows[2 * index]
        other = rows[2 * index + 1] if 2 * index + 1 < len(rows) else jnp.zeros(held.shape, f32)
        target[index] = jnp.where(lane < half, held, pltpu.roll(other, half, axis=1))
    for index in range(own, tiles):
        held = jnp.zeros(rows[0].shape, f32)
        some = rows[(index - own) * (LANES // reach) :][: LANES // reach]
        for place_at, row in enumerate(some):
            goal = place_at * reach
            moved = pltpu.roll(row, border_turn(place, goal), axis=1)
            held = jnp.where((lane >= goal) & (lane < goal + reach), moved, held)
        target[index] = held


def unpack_rows(sizes, place, blocks, count):
    packed, own, _ = packing(sizes, count)
    if not packed:
        return [blocks[index] for index in range(count)]
    half, reach = LANES // 2, BORDER >> 3
    rows = []
    for index in range(count):
        held = blocks[index // 2]
        lane = lane_at(held.shape)
        if index % 2:
            held = pltpu.roll(held, half, axis=1)
        at, goal = index // (LANES // reach), index % (LANES // reach) * reach
        back = lax.rem(LANES - border_turn(place, goal), LANES)
        beside = pltpu.roll(blocks[own + at], back, axis=1)
        start = jnp.where(place[1] == 0, half, LANES - reach)
        here = (lane >= start) & (lane < start + reach)
        rows.append(jnp.where(lane < half, held, jnp.where(here, beside, 0.0)))
    return rows


def merge_into(sizes, place, stride, radix, arrays, source, conduct, binding, first):
    position = (place[0] // stride) % radix
    source[...] = jnp.zeros(source.shape, f32)
    for step, array in enumerate(arrays):
        at = (position ^ step) * stride
        rows = unpack_rows(sizes, place, array, 3 * stride + 2)
        for index, row in enumerate(rows[: stride + 2]):
            source[at + index] = source[at + index] + row
        for index in range(stride):
            conduct[at + index + first] = rows[stride + 2 + index]
            binding[at + index] = rows[2 * stride + 2 + index]


def merge_kernel(sizes, stride, radix, place, *refs):
    arrays, out, (source, conduct, binding) = refs[:radix], refs[radix], refs[radix + 1 :]
    merge_into(sizes, place, stride, radix, arrays, source, conduct, binding, 0)
    count = stride * radix
    rows = [source[row] for row in range(count + 2)]
    rows += [conduct[row] for row in range(count)] + [binding[row] for row in range(count)]
    pack_rows(sizes, place, rows, out)


def down_kernel(sizes, place, *refs):
    s = sizes.sides
    owns, turned, refs = refs[:3], refs[3], refs[4:]
    borders0, refs = refs[:s], refs[s:]
    from_prev, from_next, refs = refs[0], refs[1], refs[2:]
    beside_prev, beside_next, refs = refs[: 2 * s : 2], refs[1 : 2 * s : 2], refs[2 * s :]
    coefs, contribution, ups, fars, refs = refs[:3], refs[3], refs[4:6], refs[6:8], refs[8:]
    border1, border2, level3, sums = refs
    slots = sizes.slots
    n0, n1, n2 = sizes.rows[:3]

    if s:
        for row in range(2 * n1):
            for side in range(s):
                columns = slice(side * LANES, (side + 1) * LANES)
                at, low = row // n1, 2 * (row % n1)
                sums[row, :, columns] = borders0[side][at, low] + borders0[side][at, low + 1]
        narrow(sizes, place, 0, sums, border1, 2 * n1, "border", sizes.own[0] * LANES)
        for row in range(2 * n2):
            sums[row, :, :LANES] = border1[2 * row] + border1[2 * row + 1]
        narrow(sizes, place, 1, sums, border2, 2 * n2, "border", sizes.own[1] * LANES)

    def held_row(level, at, row):
        if level == 0:
            tiles = [turned[row] if at == 2 else owns[0][at, row], *(array[at, row] for array in borders0)]
        else:
            row = at * sizes.rows[level] + row
            tiles = [owns[level][row], *([(border1, border2)[level - 1][row]] if s else [])]
        return jnp.concatenate(tiles, axis=1)

    def prev_row(level, index):
        return message_row(sizes, place, level, slots[index], from_prev, beside_prev)

    def next_row(level, index):
        return message_row(sizes, place, level, slots[index], from_next, beside_next)

    def conduct0(row):
        if row == 0:
            return prev_row(0, 0)
        if row == n0 + 1:
            return next_row(0, 0)
        return held_row(0, 0, row - 1)

    bound0 = lambda row: held_row(0, 1, row - 1)
    fx, fy, fz, weight, v0 = parts(coefs[0], coefficient_rows(sizes, 0))
    coefficients(sizes, place, 0, n0 + 2, conduct0, bound0, fx, fy, fz, weight)
    for row in range(n0):
        v0[row] = weight[row] * held_row(0, 2, row)
    own_defect(n0 + 2, v0, lambda row: held_row(0, 2, row - 1), bound0, fx, fy, fz, sums, 1)
    smooths, sources = [], []
    for level, first in ((1, 1), (2, 4)):
        n = sizes.rows[level]
        fx, fy, fz, weight, binding, source, smooth = parts(coefs[level], coefficient_rows(sizes, level))
        held = sizes.held[level]
        narrow(sizes, place, level - 1, sums.at[:, :, : sizes.held[level - 1]], source, n + 2)
        binding[0] = prev_row(level, first + 2)
        binding[n + 1] = next_row(level, first + 2)
        for row in range(n):
            binding[row + 1] = held_row(level, 1, row)

        def conduct(row, n=n, level=level, first=first):
            if row < 2:
                return prev_row(level, first + row)
            if row >= n + 2:
                return next_row(level, first + row - n - 2)
            return held_row(level, 0, row - 2)

        bound = lambda row, binding=binding: binding[row - 1]
        coefficients(sizes, place, level, n + 4, conduct, bound, fx, fy, fz, weight)
        for row in range(n + 2):
            smooth[row] = weight[row] * source[row]
        mine = lambda row, source=source: source[row - 1]
        own_defect(n + 4, smooth, mine, bound, fx, fy, fz, sums.at[:, :, :held], 0)
        smooths.append(smooth)
        sources.append(source)
    narrow(sizes, place, 2, sums.at[:, :, : sizes.held[2]], level3, 3)

    for at in (0, 1):
        sums[at, :, : sizes.held[2]] = held_row(2, at, 0) + held_row(2, at, 1)
    narrow(sizes, place, 2, sums.at[:, :, : sizes.held[2]], level3.at[3:5], 2)
    pack_rows(sizes, place, [level3[row] for row in range(5)], contribution)
    (s1, s2), (v1, v2) = sources, smooths
    for at, rows in enumerate(
        (
            (v0[n0 - 1], s1[n1], s1[n1 + 1], v1[n1 - 1], s2[n2], s2[n2 + 1], v2[n2 - 1]),
            (v0[0], s1[1], s1[0], v1[2], s2[1], s2[0], v2[2]),
        )
    ):
        for slot, row in zip(slots, rows):
            put(ups[at], slot, row)
        if s:
            put_fringes(sizes, ups[at], list(zip((1, 1, 1, 2, 2, 2), rows[1:])))
        put(fars[at], (0, sizes.held[2] // LANES), v2[n2 + 1 if at == 0 else 0])


def relax(count, field, refs_of, source, target):
    fx, fy, fz, weight, binding = refs_of

    def update(row, value):
        target(row, field(row) + weight[row - 1] * (source(row) - value))

    sweep(count, field, binding, fx, fy, fz, update)


def store(array, first):
    def put_row(row, value):
        array[row - first] = value

    return put_row


def coarse_kernel(sizes, stride, radix, place, *refs):
    blocks, refs = refs[:radix], refs[radix:]
    out, merged, sums = refs[:3]
    coarse = [refs[3 + 9 * index : 12 + 9 * index] for index in range(3)]
    total = sizes.span_count
    merge_into(sizes, place, stride, radix, blocks, merged, coarse[0][4], coarse[0][5], 1)
    zero = jnp.zeros((sizes.depth, LANES), f32)
    for index in range(3):
        level = 3 + index
        fx, fy, fz, weight, conduct, binding, source, smooth, iterate = coarse[index]
        count = total >> index
        for array in (conduct, smooth, iterate):
            array[0] = zero
            array[count + 1] = zero
        if index == 0:
            source = merged.at[1 : count + 1]
        bound = lambda row, binding=binding: binding[row - 1]
        at_row = lambda row, conduct=conduct: conduct[row]
        coefficients(sizes, place, level, count + 2, at_row, bound, fx, fy, fz, weight)
        for row in range(count):
            smooth[row + 1] = weight[row] * source[row]
        if index < 2:
            conduct_next, binding_next, source_next = coarse[index + 1][4:7]
            half = count // 2
            for row in range(half):
                sums[row, :, :LANES] = conduct[2 * row + 1] + conduct[2 * row + 2]
            narrow(sizes, place, level, sums, conduct_next.at[1 : half + 1], half)
            for row in range(half):
                sums[row, :, :LANES] = binding[2 * row] + binding[2 * row + 1]
            narrow(sizes, place, level, sums, binding_next, half)

            def add(row, value, source=source):
                value = source[row - 1] - value
                slot = (row - 1) // 2
                if row % 2 == 1:
                    sums[slot, :, :LANES] = value
                else:
                    sums[slot, :, :LANES] = sums[slot, :, :LANES] + value

            sweep(count + 2, lambda row, smooth=smooth: smooth[row], bound, fx, fy, fz, add)
            narrow(sizes, place, level, sums, source_next, half)

    fx, fy, fz, weight, conduct, binding, source, smooth, iterate = coarse[2]
    held, other = smooth, iterate
    for _ in range(COARSE_SWEEPS - 1):
        field = lambda row, held=held: held[row]
        mine = lambda row: source[row - 1]
        bound = lambda row: binding[row - 1]
        relax((total >> 2) + 2, field, (fx, fy, fz, weight, bound), mine, store(other, 0))
        held, other = other, held
    for index in (1, 0):
        fx, fy, fz, weight, conduct, binding, source, smooth, iterate = coarse[index]
        if index == 0:
            source = merged.at[1 : total + 1]
        count = total >> index
        widen(sizes, place, 3 + index, held.at[1 : count // 2 + 1], sums, count // 2)
        for row in range(count):
            smooth[row + 1] = smooth[row + 1] + sums[row // 2, :, :LANES]
        field = lambda row, smooth=smooth: smooth[row]
        mine = lambda row, source=source: source[row - 1]
        bound = lambda row, binding=binding: binding[row - 1]
        relax(count + 2, field, (fx, fy, fz, weight, bound), mine, store(iterate, 0))
        held = iterate

    out[...] = held[pl.ds(place[0], 3)]


def up_kernel(sizes, place, coarse, *refs):
    s = sizes.sides
    (from_prev, from_next), fars, coefs, (own0, turned) = refs[:2], refs[2:4], refs[4:7], refs[7:9]
    borders0, out, refs = refs[9 : 9 + s], refs[9 + s], refs[10 + s :]
    total1, total2, result = refs[:3]
    over2, over1, over0, lift2, lift1, lift0, it2, it1, it0, semaphores = refs[3:]
    slots = sizes.slots
    n0, n1, n2 = sizes.rows[:3]
    width = sizes.own[0] * LANES

    widen(sizes, place, 2, coarse, over2, 3)
    for level, array, first, totals, over, lift, target, upper in (
        (2, coefs[2], 4, total2, over2, lift2, it2, over1),
        (1, coefs[1], 1, total1, over1, lift1, it1, over0),
    ):
        n = sizes.rows[level]
        fx, fy, fz, weight, binding, own, smooth = parts(array, coefficient_rows(sizes, level))
        edge = {}
        for row, message, index in (
            (1, from_prev, first),
            (2, from_prev, first + 1),
            (n + 2, from_next, first),
            (n + 1, from_next, first + 1),
        ):
            value = edge.get(row, own[row - 1])
            edge[row] = value + fringed_row(sizes, level, index, message)
        for row, value in edge.items():
            totals[row - 1] = value
        for row in range(n + 4):
            if row in (0, n + 3):
                value = fringed_row(sizes, level, first + 2, from_next if row else from_prev)
                if level == 2:
                    far = fars[1 if row else 0]
                    value = value + jnp.concatenate(get(far, (0, sizes.held[2] // LANES)), axis=1)
            elif row in edge:
                value = weight[row - 1] * totals[row - 1]
            else:
                value = smooth[row - 1]
            lift[row] = value + over[row // 2]
        field = lambda row, lift=lift: lift[row]
        mine = lambda row, own=own, totals=totals, edge=edge: (totals if row in edge else own)[row - 1]
        bound = lambda row, binding=binding: binding[row - 1]
        relax(n + 4, field, (fx, fy, fz, weight, bound), mine, store(target, 1))
        widen(sizes, place, level - 1, target, upper, n + 2)

    def held_row(at, row):
        own = turned[row - 1] if at == 2 else own0[at, row - 1]
        return jnp.concatenate([own, *(array[at, row - 1] for array in borders0)], axis=1)

    fx, fy, fz, weight, v0 = parts(coefs[0], coefficient_rows(sizes, 0))
    lift0[0] = fringed_row(sizes, 0, 0, from_prev) + over0[0]
    lift0[n0 + 1] = fringed_row(sizes, 0, 0, from_next) + over0[n1 + 1]
    for row in range(1, n0 + 1):
        lift0[row] = v0[row - 1] + over0[(row + 1) // 2]
    field = lambda row: lift0[row]
    bound = lambda row: held_row(1, row)
    relax(n0 + 2, field, (fx, fy, fz, weight, bound), lambda row: held_row(2, row), store(it0, 1))
    step = sizes.depth // CHUNKS
    copies = []
    for chunk in range(CHUNKS):
        part = slice(chunk * step, (chunk + 1) * step)
        result[part] = jnp.swapaxes(it0[:, part, :width], 0, 1)
        copies.append(pltpu.make_async_copy(result.at[part], out.at[part], semaphores.at[chunk]))
        copies[-1].start()
    for copy in copies:
        copy.wait()


def call(body, name, outputs, scratch, place, inputs, copies=0, far_out=False):
    near, far = pl.BlockSpec(memory_space=pltpu.VMEM), pl.BlockSpec(memory_space=pl.ANY)
    scratch = [pltpu.VMEM(shape, f32) for shape in scratch]
    if copies:
        scratch.append(pltpu.SemaphoreType.DMA((copies,)))
    return pl.pallas_call(
        body,
        name=name,
        out_shape=[jax.ShapeDtypeStruct(shape, f32) for shape in outputs],
        in_specs=[pl.BlockSpec(memory_space=pltpu.SMEM)] + [near] * len(inputs),
        out_specs=[far if far_out else near] * len(outputs),
        scratch_shapes=scratch,
        compiler_params=pltpu.CompilerParams(vmem_limit_bytes=VMEM_LIMIT),
    )(place, *inputs)


def along(value, axis, steps):
    count = lax.axis_size(axis)
    initial, last = max(0, -steps), min(count, count - steps)
    return lax.ppermute(value, axis, [(source, source + steps) for source in range(initial, last)])


def beside(values, sizes):
    if sizes.sides == 1:
        return [[lax.ppermute(value, "width", [(0, 1), (1, 0)]) for value in values]]
    if sizes.sides == 2:
        return [[along(value, "width", steps) for value in values] for steps in (-1, 1)]
    return []


def stages(count):
    stride = 1
    while stride < count:
        radix = 4 if count // stride % 4 == 0 else 2
        yield stride, radix
        stride *= radix


def swap(value, stride, radix):
    count = lax.axis_size("span")
    return [value] + [
        lax.ppermute(value, "span", [(device, device ^ step * stride) for device in range(count)])
        for step in range(1, radix)
    ]


def on_device(right_side, diffusivity, reaction):
    depth, extent_x, extent_y = diffusivity.shape
    sizes = Sizes(depth, extent_x, extent_y, lax.axis_size("span"), lax.axis_size("width"))
    place = jnp.stack([lax.axis_index("span"), lax.axis_index("width")]).astype(jnp.int32)
    n0, n1, n2, n3 = sizes.rows
    s = sizes.sides
    tile = (depth, LANES)
    own = [(depth, count * LANES) for count in sizes.own]
    held = [(depth, count) for count in sizes.held]
    down_message = (sizes.tiles, *tile)
    up_message = (sizes.tiles + 1, *tile)
    own0, own1, own2, to_next, to_prev = call(
        functools.partial(start_kernel, sizes),
        "start",
        [(2, n0, *own[0]), (2 * n1, *own[1]), (2 * n2, *own[2]), down_message, down_message],
        [(2 * n1, *own[0])],
        place,
        [diffusivity, reaction],
    )
    halos = [along(to_next, "span", 1), along(to_prev, "span", -1)]
    turned, *edges = call(
        functools.partial(turn_kernel, sizes),
        "turn",
        [(n0, *own[0])] + [(3, n0, depth, BORDER)] * s,
        [],
        place,
        [right_side, own0],
    )
    if s == 1:
        borders = [lax.ppermute(edges[0], "width", [(0, 1), (1, 0)])]
    elif s == 2:
        borders = [along(edges[1], "width", -1), along(edges[0], "width", 1)]
    else:
        borders = []
    plan = list(stages(sizes.span_count))
    sides = beside(halos, sizes)

    lengths = [sum(coefficient_rows(sizes, level)) for level in range(3)]
    far = (sizes.held[2] // LANES, *tile)
    coefs = [(lengths[level], *held[level]) for level in range(3)]
    downs = call(
        functools.partial(down_kernel, sizes),
        "down",
        [*coefs, (packing(sizes, 5)[2], *tile), up_message, up_message, far, far],
        [(2 * n1, *tile), (2 * n2, *tile), (5, *tile), (max(2 * n1, n1 + 2), *held[0])],
        place,
        [own0, own1, own2, turned, *borders, *halos, *sum(sides, [])],
    )
    coefs_out, blocks, ups, fars = downs[:3], downs[3], downs[4:6], downs[6:8]
    for stride, radix in plan[:-1]:
        count = stride * radix
        (blocks,) = call(
            functools.partial(merge_kernel, sizes, stride, radix),
            "merge",
            [(packing(sizes, 3 * count + 2)[2], *tile)],
            [(count + 2, *tile), (count, *tile), (count, *tile)],
            place,
            swap(blocks, stride, radix),
        )
    blocks, *sent = lax.optimization_barrier((blocks, *ups, *fars))
    stride, radix = plan[-1]
    blocks = swap(blocks, stride, radix)
    received = [along(sent[0], "span", 1), along(sent[1], "span", -1)]
    received += [along(sent[2], "span", 2), along(sent[3], "span", -2)]
    scratch = [(sizes.span_count + 2, *tile), (max(sizes.span_count // 2, 2), *tile)]
    for index in range(3):
        count = sizes.span_count >> index
        scratch += [(count + 1, *tile)] + [(count, *tile)] * 3 + [(count + 2, *tile)] + [(count, *tile)] * 2
        scratch += [(count + 2, *tile)] * 2
    (coarse,) = call(
        functools.partial(coarse_kernel, sizes, stride, radix),
        "coarse",
        [(n3 + 2, *tile)],
        scratch,
        place,
        blocks,
    )
    scratch = [(n1 + 2, *held[1]), (n2 + 2, *held[2]), diffusivity.shape]
    scratch += [(n3 + 2, *held[2]), (n2 + 2, *held[1]), (n1 + 2, *held[0])]
    scratch += [(n2 + 4, *held[2]), (n1 + 4, *held[1]), (n0 + 2, *held[0])]
    scratch += [(n2 + 2, *held[2]), (n1 + 2, *held[1]), (n0, *held[0])]
    (correction,) = call(
        functools.partial(up_kernel, sizes),
        "up",
        [diffusivity.shape],
        scratch,
        place,
        [coarse, *received, *coefs_out, own0, turned, *borders],
        copies=CHUNKS,
        far_out=True,
    )
    return correction


def solution(mesh):
    in_specs = (P(None, "span", "width"),) * 3
    return jax.shard_map(
        on_device, mesh=mesh, in_specs=in_specs, out_specs=P(None, "span", "width"), check_vma=False
    )
```

```python
import functools

import jax
import jax.numpy as jnp
from jax import lax
from jax.experimental import pallas as pl
from jax.experimental.pallas import tpu as pltpu
from jax.sharding import PartitionSpec as P

LEVELS = 6
COARSE_SWEEPS = 3
LANES = 128
BORDER = 128
FRINGE = 4
SPREAD = 16
relax_weight = 0.8
f32 = jnp.float32
VMEM_LIMIT = 32 * 1024 * 1024
CHUNKS = 4


class Sizes:
    def __init__(self, depth, extent_x, extent_y, span_count, width_count):
        self.depth, self.extent_x, self.extent_y = depth, extent_x, extent_y
        self.span_count, self.width_count = span_count, width_count
        self.sides = min(width_count - 1, 2)
        self.own = [(extent_y >> level) // LANES for level in range(3)]
        self.border = [self.sides, min(self.sides, 1), min(self.sides, 1)]
        self.held = [(self.own[level] + self.border[level]) * LANES for level in range(3)] + [LANES] * 3
        self.rows = [extent_x >> level for level in range(4)]
        self.slots = []
        start = 0
        for level in (0, 1, 1, 1, 2, 2, 2):
            self.slots.append((start, self.own[level]))
            start += self.own[level]
        self.tiles = start


def put(message, slot, row):
    start, tiles = slot
    for tile in range(tiles):
        message[start + tile] = row[:, tile * LANES : (tile + 1) * LANES]


def get(message, slot):
    start, tiles = slot
    return [message[start + tile] for tile in range(tiles)]


def lane_at(shape):
    return lax.broadcasted_iota(jnp.int32, shape, len(shape) - 1)


def roll(value, steps, axis):
    return pltpu.roll(value, steps % value.shape[axis], axis=axis)


def reciprocal(value):
    return pltpu.reciprocal(value, approx=True)


def harmonic(first, second, guard):
    total = first + second
    if guard:
        total = jnp.maximum(total, 1e-3)
    return (2.0 * first) * second * reciprocal(total)


def split(value):
    high = value.astype(jnp.bfloat16)
    return high, (value - high.astype(f32)).astype(jnp.bfloat16)


def dot(halves, table):
    high, low = halves
    return jnp.dot(high, table, preferred_element_type=f32) + jnp.dot(low, table, preferred_element_type=f32)


def pair_table(fine, fine_dim, turn, weight):
    shape = (fine, LANES) if fine_dim == 0 else (LANES, fine)
    fine_at = lax.broadcasted_iota(jnp.int32, shape, fine_dim)
    coarse_at = lax.broadcasted_iota(jnp.int32, shape, 1 - fine_dim)
    if turn is not None:
        coarse_at = coarse_at - jnp.where(fine_at >= turn, LANES // 2, 0)
    return jnp.where(fine_at // 2 == coarse_at, weight, 0.0).astype(jnp.bfloat16)


def turns(sizes, place, level):
    if sizes.sides == 0:
        return []
    if level == 0:
        return [jnp.where(place[1] == 0, LANES, 0)] if sizes.sides == 1 else [LANES, 0]
    return [LANES // 2]


def transfer_plan(sizes, place, level, part):
    plan = []
    if level >= 3:
        return [((0, LANES), 0, 3 * LANES // 4)]
    if level == 2:
        return [((0, sizes.held[2]), 0, None)]
    own = sizes.own[level]
    if part != "border":
        plan += [((2 * LANES * tile, 2 * LANES * (tile + 1)), tile, None) for tile in range(own // 2)]
    if part != "own":
        for index, turn in enumerate(turns(sizes, place, level)):
            start = (own + index) * LANES
            plan.append(((start, start + LANES), own // 2, turn))
    return plan


def narrow(sizes, place, level, sums, target, rows, part="all", shift=0):
    depth = sums.shape[1]
    done = {}
    for (start, stop), tile, turn in transfer_plan(sizes, place, level, part):
        start, stop, tile = start - shift, stop - shift, tile - shift // (2 * LANES)
        columns = split(sums[0:rows, :, start:stop].reshape(rows * depth, stop - start))
        result = dot(columns, pair_table(stop - start, 0, turn, 0.25)).reshape(rows, depth, LANES)
        done[tile] = done[tile] + result if tile in done else result
    for tile, result in done.items():
        target[0:rows, :, tile * LANES : (tile + 1) * LANES] = result


def widen(sizes, place, level, coarse, target, rows):
    depth = coarse.shape[1]
    for (start, stop), tile, turn in transfer_plan(sizes, place, level, "all"):
        columns = split(coarse[0:rows, :, tile * LANES : (tile + 1) * LANES].reshape(rows * depth, LANES))
        result = dot(columns, pair_table(stop - start, 1, turn, 4.0))
        target[0:rows, :, start:stop] = result.reshape(rows, depth, stop - start)


def coefficients(sizes, place, level, count, conduct, binding, fx, fy, fz, weight):
    guard = level > 0 or sizes.sides > 1
    for row in range(1, count):
        fx[row - 1] = harmonic(conduct(row - 1), conduct(row), guard)
    for row in range(1, count - 1):
        mine = conduct(row)
        south = harmonic(mine, roll(mine, 1, 1), guard)
        if level == 0 and sizes.sides < 2:
            cut = 0 if sizes.sides == 0 else jnp.where(place[1] == 0, 0, sizes.extent_y)
            south = jnp.where(lane_at(mine.shape) == cut, 0.0, south)
        below = harmonic(mine, roll(mine, 1, 0), guard)
        below = jnp.where(lax.broadcasted_iota(jnp.int32, mine.shape, 0) == 0, 0.0, below)
        diagonal = fx[row - 1] + fx[row] + binding(row)
        diagonal = diagonal + (south + roll(south, -1, 1)) + (below + roll(below, -1, 0))
        if guard:
            diagonal = jnp.maximum(diagonal, 1e-6)
        fy[row - 1] = south
        fz[row - 1] = below
        weight[row - 1] = relax_weight * reciprocal(diagonal)


def sweep(count, field, binding, fx, fy, fz, emit):
    lower = fx[0] * (field(1) - field(0))
    for row in range(1, count - 1):
        mine = field(row)
        upper = fx[row] * (field(row + 1) - mine)
        south = fy[row - 1] * (mine - roll(mine, 1, 1))
        below = fz[row - 1] * (mine - roll(mine, 1, 0))
        across = (south - roll(south, -1, 1)) + (below - roll(below, -1, 0))
        emit(row, binding(row) * mine + (lower - upper) + across)
        lower = upper


def own_defect(count, smooth, source, binding, fx, fy, fz, sums, first):
    zero = jnp.zeros(smooth.shape[1:], f32)

    def field(row):
        return smooth[row - 1] if 0 < row < count - 1 else zero

    def add(row, value):
        slot = (row + first) // 2
        if (row + first) % 2 == 0 or row == 0:
            sums[slot] = value
        else:
            sums[slot] = sums[slot] + value

    add(0, fx[0] * field(1))
    sweep(count, field, binding, fx, fy, fz, lambda row, result: add(row, source(row) - result))
    add(count - 1, fx[count - 2] * field(count - 2))


def parts(array, counts):
    views, start = [], 0
    for count in counts:
        views.append(array.at[start : start + count])
        start += count
    return views


def coefficient_rows(sizes, level):
    n = sizes.rows[level]
    if level == 0:
        return [n + 1, n, n, n, n]
    return [n + 3] + [n + 2] * 6


def start_kernel(sizes, place, conduct, binding, own0, own1, own2, to_next, to_prev, sums):
    n0, n1, n2 = sizes.rows[:3]
    for at, array in enumerate((conduct, binding)):
        own0[at] = jnp.swapaxes(array[...], 0, 1)
    for at in (0, 1):
        for row in range(n1):
            sums[at * n1 + row] = own0[at, 2 * row] + own0[at, 2 * row + 1]
    narrow(sizes, place, 0, sums, own1, 2 * n1, "own")
    for row in range(2 * n2):
        sums[row, :, : sizes.own[1] * LANES] = own1[2 * row] + own1[2 * row + 1]
    narrow(sizes, place, 1, sums, own2, 2 * n2, "own")
    for message, low, at1, at0 in ((to_next, n1 - 2, n1 - 1, n0 - 1), (to_prev, 0, 0, 0)):
        edge = n2 - 1 if at0 else 0
        rows = (own0[0, at0], own1[low], own1[low + 1], own1[n1 + at1])
        rows += (own2[n2 - 2], own2[n2 - 1], own2[n2 + edge])
        for slot, row in zip(sizes.slots, rows):
            put(message, slot, row)


def turn_kernel(sizes, place, right_side, own0, turned, *edges):
    turned[...] = jnp.swapaxes(right_side[...], 0, 1)
    last = sizes.extent_y - BORDER
    for index, array in enumerate((own0.at[0], own0.at[1], turned)):
        if sizes.sides == 1:
            at = pl.multiple_of(jnp.where(place[1] == 0, last, 0), LANES)
            edges[0][index] = array[:, :, pl.ds(at, BORDER)]
        elif sizes.sides == 2:
            edges[0][index] = array[:, :, last:]
            edges[1][index] = array[:, :, :BORDER]


def message_row(sizes, place, level, slot, message, beside):
    start, tiles = slot
    row = get(message, slot)
    if sizes.sides == 1:
        left = place[1] != 0
        tile = beside[0][start + jnp.where(left, tiles - 1, 0)]
        if level > 0:
            reach = BORDER >> level
            lane = lane_at(tile.shape)
            first = jnp.where(left, LANES - reach, 0)
            tile = jnp.where((lane >= first) & (lane < first + reach), tile, 0.0)
        row.append(tile)
    elif sizes.sides == 2:
        right, left = beside[0][start], beside[1][start + tiles - 1]
        if level == 0:
            row += [right, left]
        else:
            reach = BORDER >> level
            lane = lane_at(right.shape)
            row.append(jnp.where(lane < reach, right, jnp.where(lane >= LANES - reach, left, 0.0)))
    return jnp.concatenate(row, axis=1)


def fringe_lanes(shape):
    lane = lane_at(shape)
    return (lane < FRINGE) | (lane >= LANES - FRINGE)


def put_fringes(sizes, message, rows):
    total = None
    for index, (level, row) in enumerate(rows):
        tile = row[:, sizes.own[level] * LANES :]
        tile = jnp.where(fringe_lanes(tile.shape), tile, 0.0)
        tile = roll(tile, SPREAD * index + SPREAD // 2, 1)
        total = tile if total is None else total + tile
    message[sizes.tiles] = total


def fringed_row(sizes, level, index, message):
    row = get(message, sizes.slots[index])
    if sizes.border[level]:
        if level == 0:
            row += [jnp.zeros(row[0].shape, f32)] * sizes.border[0]
        else:
            tile = roll(message[sizes.tiles], -(SPREAD * (index - 1) + SPREAD // 2), 1)
            row.append(jnp.where(fringe_lanes(tile.shape), tile, 0.0))
    return jnp.concatenate(row, axis=1)


def packing(sizes, count):
    if sizes.sides != 1:
        return False, count, count
    own = -(-count // 2)
    return True, own, own - (-count * (BORDER >> 3) // LANES)


def border_turn(place, goal):
    return jnp.where(place[1] == 0, (goal - LANES // 2) % LANES, (goal + (BORDER >> 3)) % LANES)


def pack_rows(sizes, place, rows, target):
    packed, own, tiles = packing(sizes, len(rows))
    if not packed:
        for index, row in enumerate(rows):
            target[index] = row
        return
    half, reach = LANES // 2, BORDER >> 3
    lane = lane_at(rows[0].shape)
    for index in range(own):
        held = rows[2 * index]
        other = rows[2 * index + 1] if 2 * index + 1 < len(rows) else jnp.zeros(held.shape, f32)
        target[index] = jnp.where(lane < half, held, pltpu.roll(other, half, axis=1))
    for index in range(own, tiles):
        held = jnp.zeros(rows[0].shape, f32)
        some = rows[(index - own) * (LANES // reach) :][: LANES // reach]
        for place_at, row in enumerate(some):
            goal = place_at * reach
            moved = pltpu.roll(row, border_turn(place, goal), axis=1)
            held = jnp.where((lane >= goal) & (lane < goal + reach), moved, held)
        target[index] = held


def unpack_rows(sizes, place, blocks, count):
    packed, own, _ = packing(sizes, count)
    if not packed:
        return [blocks[index] for index in range(count)]
    half, reach = LANES // 2, BORDER >> 3
    rows = []
    for index in range(count):
        held = blocks[index // 2]
        lane = lane_at(held.shape)
        if index % 2:
            held = pltpu.roll(held, half, axis=1)
        at, goal = index // (LANES // reach), index % (LANES // reach) * reach
        back = lax.rem(LANES - border_turn(place, goal), LANES)
        beside = pltpu.roll(blocks[own + at], back, axis=1)
        start = jnp.where(place[1] == 0, half, LANES - reach)
        here = (lane >= start) & (lane < start + reach)
        rows.append(jnp.where(lane < half, held, jnp.where(here, beside, 0.0)))
    return rows


def merge_into(sizes, place, stride, radix, arrays, source, conduct, binding, first):
    position = (place[0] // stride) % radix
    source[...] = jnp.zeros(source.shape, f32)
    for step, array in enumerate(arrays):
        at = (position ^ step) * stride
        rows = unpack_rows(sizes, place, array, 3 * stride + 2)
        for index, row in enumerate(rows[: stride + 2]):
            source[at + index] = source[at + index] + row
        for index in range(stride):
            conduct[at + index + first] = rows[stride + 2 + index]
            binding[at + index] = rows[2 * stride + 2 + index]


def merge_kernel(sizes, stride, radix, place, *refs):
    arrays, out, (source, conduct, binding) = refs[:radix], refs[radix], refs[radix + 1 :]
    merge_into(sizes, place, stride, radix, arrays, source, conduct, binding, 0)
    count = stride * radix
    rows = [source[row] for row in range(count + 2)]
    rows += [conduct[row] for row in range(count)] + [binding[row] for row in range(count)]
    pack_rows(sizes, place, rows, out)


def down_kernel(sizes, place, *refs):
    s = sizes.sides
    owns, turned, refs = refs[:3], refs[3], refs[4:]
    borders0, refs = refs[:s], refs[s:]
    from_prev, from_next, refs = refs[0], refs[1], refs[2:]
    beside_prev, beside_next, refs = refs[: 2 * s : 2], refs[1 : 2 * s : 2], refs[2 * s :]
    coefs, contribution, ups, fars, refs = refs[:3], refs[3], refs[4:6], refs[6:8], refs[8:]
    border1, border2, level3, sums = refs
    slots = sizes.slots
    n0, n1, n2 = sizes.rows[:3]

    if s:
        for row in range(2 * n1):
            for side in range(s):
                columns = slice(side * LANES, (side + 1) * LANES)
                at, low = row // n1, 2 * (row % n1)
                sums[row, :, columns] = borders0[side][at, low] + borders0[side][at, low + 1]
        narrow(sizes, place, 0, sums, border1, 2 * n1, "border", sizes.own[0] * LANES)
        for row in range(2 * n2):
            sums[row, :, :LANES] = border1[2 * row] + border1[2 * row + 1]
        narrow(sizes, place, 1, sums, border2, 2 * n2, "border", sizes.own[1] * LANES)

    def held_row(level, at, row):
        if level == 0:
            tiles = [turned[row] if at == 2 else owns[0][at, row], *(array[at, row] for array in borders0)]
        else:
            row = at * sizes.rows[level] + row
            tiles = [owns[level][row], *([(border1, border2)[level - 1][row]] if s else [])]
        return jnp.concatenate(tiles, axis=1)

    def prev_row(level, index):
        return message_row(sizes, place, level, slots[index], from_prev, beside_prev)

    def next_row(level, index):
        return message_row(sizes, place, level, slots[index], from_next, beside_next)

    def conduct0(row):
        if row == 0:
            return prev_row(0, 0)
        if row == n0 + 1:
            return next_row(0, 0)
        return held_row(0, 0, row - 1)

    bound0 = lambda row: held_row(0, 1, row - 1)
    fx, fy, fz, weight, v0 = parts(coefs[0], coefficient_rows(sizes, 0))
    coefficients(sizes, place, 0, n0 + 2, conduct0, bound0, fx, fy, fz, weight)
    for row in range(n0):
        v0[row] = weight[row] * held_row(0, 2, row)
    own_defect(n0 + 2, v0, lambda row: held_row(0, 2, row - 1), bound0, fx, fy, fz, sums, 1)
    smooths, sources = [], []
    for level, first in ((1, 1), (2, 4)):
        n = sizes.rows[level]
        fx, fy, fz, weight, binding, source, smooth = parts(coefs[level], coefficient_rows(sizes, level))
        held = sizes.held[level]
        narrow(sizes, place, level - 1, sums.at[:, :, : sizes.held[level - 1]], source, n + 2)
        binding[0] = prev_row(level, first + 2)
        binding[n + 1] = next_row(level, first + 2)
        for row in range(n):
            binding[row + 1] = held_row(level, 1, row)

        def conduct(row, n=n, level=level, first=first):
            if row < 2:
                return prev_row(level, first + row)
            if row >= n + 2:
                return next_row(level, first + row - n - 2)
            return held_row(level, 0, row - 2)

        bound = lambda row, binding=binding: binding[row - 1]
        coefficients(sizes, place, level, n + 4, conduct, bound, fx, fy, fz, weight)
        for row in range(n + 2):
            smooth[row] = weight[row] * source[row]
        mine = lambda row, source=source: source[row - 1]
        own_defect(n + 4, smooth, mine, bound, fx, fy, fz, sums.at[:, :, :held], 0)
        smooths.append(smooth)
        sources.append(source)
    narrow(sizes, place, 2, sums.at[:, :, : sizes.held[2]], level3, 3)

    for at in (0, 1):
        sums[at, :, : sizes.held[2]] = held_row(2, at, 0) + held_row(2, at, 1)
    narrow(sizes, place, 2, sums.at[:, :, : sizes.held[2]], level3.at[3:5], 2)
    pack_rows(sizes, place, [level3[row] for row in range(5)], contribution)
    (s1, s2), (v1, v2) = sources, smooths
    for at, rows in enumerate(
        (
            (v0[n0 - 1], s1[n1], s1[n1 + 1], v1[n1 - 1], s2[n2], s2[n2 + 1], v2[n2 - 1]),
            (v0[0], s1[1], s1[0], v1[2], s2[1], s2[0], v2[2]),
        )
    ):
        for slot, row in zip(slots, rows):
            put(ups[at], slot, row)
        if s:
            put_fringes(sizes, ups[at], list(zip((1, 1, 1, 2, 2, 2), rows[1:])))
        put(fars[at], (0, sizes.held[2] // LANES), v2[n2 + 1 if at == 0 else 0])


def relax(count, field, refs_of, source, target):
    fx, fy, fz, weight, binding = refs_of

    def update(row, value):
        target(row, field(row) + weight[row - 1] * (source(row) - value))

    sweep(count, field, binding, fx, fy, fz, update)


def store(array, first):
    def put_row(row, value):
        array[row - first] = value

    return put_row


def coarse_kernel(sizes, stride, radix, place, *refs):
    blocks, refs = refs[:radix], refs[radix:]
    out, merged, sums = refs[:3]
    coarse = [refs[3 + 9 * index : 12 + 9 * index] for index in range(3)]
    total = sizes.span_count
    merge_into(sizes, place, stride, radix, blocks, merged, coarse[0][4], coarse[0][5], 1)
    zero = jnp.zeros((sizes.depth, LANES), f32)
    for index in range(3):
        level = 3 + index
        fx, fy, fz, weight, conduct, binding, source, smooth, iterate = coarse[index]
        count = total >> index
        for array in (conduct, smooth, iterate):
            array[0] = zero
            array[count + 1] = zero
        if index == 0:
            source = merged.at[1 : count + 1]
        bound = lambda row, binding=binding: binding[row - 1]
        at_row = lambda row, conduct=conduct: conduct[row]
        coefficients(sizes, place, level, count + 2, at_row, bound, fx, fy, fz, weight)
        for row in range(count):
            smooth[row + 1] = weight[row] * source[row]
        if index < 2:
            conduct_next, binding_next, source_next = coarse[index + 1][4:7]
            half = count // 2
            for row in range(half):
                sums[row, :, :LANES] = conduct[2 * row + 1] + conduct[2 * row + 2]
            narrow(sizes, place, level, sums, conduct_next.at[1 : half + 1], half)
            for row in range(half):
                sums[row, :, :LANES] = binding[2 * row] + binding[2 * row + 1]
            narrow(sizes, place, level, sums, binding_next, half)

            def add(row, value, source=source):
                value = source[row - 1] - value
                slot = (row - 1) // 2
                if row % 2 == 1:
                    sums[slot, :, :LANES] = value
                else:
                    sums[slot, :, :LANES] = sums[slot, :, :LANES] + value

            sweep(count + 2, lambda row, smooth=smooth: smooth[row], bound, fx, fy, fz, add)
            narrow(sizes, place, level, sums, source_next, half)

    fx, fy, fz, weight, conduct, binding, source, smooth, iterate = coarse[2]
    held, other = smooth, iterate
    for _ in range(COARSE_SWEEPS - 1):
        field = lambda row, held=held: held[row]
        mine = lambda row: source[row - 1]
        bound = lambda row: binding[row - 1]
        relax((total >> 2) + 2, field, (fx, fy, fz, weight, bound), mine, store(other, 0))
        held, other = other, held
    for index in (1, 0):
        fx, fy, fz, weight, conduct, binding, source, smooth, iterate = coarse[index]
        if index == 0:
            source = merged.at[1 : total + 1]
        count = total >> index
        widen(sizes, place, 3 + index, held.at[1 : count // 2 + 1], sums, count // 2)
        for row in range(count):
            smooth[row + 1] = smooth[row + 1] + sums[row // 2, :, :LANES]
        field = lambda row, smooth=smooth: smooth[row]
        mine = lambda row, source=source: source[row - 1]
        bound = lambda row, binding=binding: binding[row - 1]
        relax(count + 2, field, (fx, fy, fz, weight, bound), mine, store(iterate, 0))
        held = iterate

    out[...] = held[pl.ds(place[0], 3)]


def up_kernel(sizes, place, coarse, *refs):
    s = sizes.sides
    (from_prev, from_next), fars, coefs, (own0, turned) = refs[:2], refs[2:4], refs[4:7], refs[7:9]
    borders0, out, refs = refs[9 : 9 + s], refs[9 + s], refs[10 + s :]
    total1, total2, result = refs[:3]
    over2, over1, over0, lift2, lift1, lift0, it2, it1, it0, semaphores = refs[3:]
    slots = sizes.slots
    n0, n1, n2 = sizes.rows[:3]
    width = sizes.own[0] * LANES

    widen(sizes, place, 2, coarse, over2, 3)
    for level, array, first, totals, over, lift, target, upper in (
        (2, coefs[2], 4, total2, over2, lift2, it2, over1),
        (1, coefs[1], 1, total1, over1, lift1, it1, over0),
    ):
        n = sizes.rows[level]
        fx, fy, fz, weight, binding, own, smooth = parts(array, coefficient_rows(sizes, level))
        edge = {}
        for row, message, index in (
            (1, from_prev, first),
            (2, from_prev, first + 1),
            (n + 2, from_next, first),
            (n + 1, from_next, first + 1),
        ):
            value = edge.get(row, own[row - 1])
            edge[row] = value + fringed_row(sizes, level, index, message)
        for row, value in edge.items():
            totals[row - 1] = value
        for row in range(n + 4):
            if row in (0, n + 3):
                value = fringed_row(sizes, level, first + 2, from_next if row else from_prev)
                if level == 2:
                    far = fars[1 if row else 0]
                    value = value + jnp.concatenate(get(far, (0, sizes.held[2] // LANES)), axis=1)
            elif row in edge:
                value = weight[row - 1] * totals[row - 1]
            else:
                value = smooth[row - 1]
            lift[row] = value + over[row // 2]
        field = lambda row, lift=lift: lift[row]
        mine = lambda row, own=own, totals=totals, edge=edge: (totals if row in edge else own)[row - 1]
        bound = lambda row, binding=binding: binding[row - 1]
        relax(n + 4, field, (fx, fy, fz, weight, bound), mine, store(target, 1))
        widen(sizes, place, level - 1, target, upper, n + 2)

    def held_row(at, row):
        own = turned[row - 1] if at == 2 else own0[at, row - 1]
        return jnp.concatenate([own, *(array[at, row - 1] for array in borders0)], axis=1)

    fx, fy, fz, weight, v0 = parts(coefs[0], coefficient_rows(sizes, 0))
    lift0[0] = fringed_row(sizes, 0, 0, from_prev) + over0[0]
    lift0[n0 + 1] = fringed_row(sizes, 0, 0, from_next) + over0[n1 + 1]
    for row in range(1, n0 + 1):
        lift0[row] = v0[row - 1] + over0[(row + 1) // 2]
    field = lambda row: lift0[row]
    bound = lambda row: held_row(1, row)
    relax(n0 + 2, field, (fx, fy, fz, weight, bound), lambda row: held_row(2, row), store(it0, 1))
    step = sizes.depth // CHUNKS
    copies = []
    for chunk in range(CHUNKS):
        part = slice(chunk * step, (chunk + 1) * step)
        result[part] = jnp.swapaxes(it0[:, part, :width], 0, 1)
        copies.append(pltpu.make_async_copy(result.at[part], out.at[part], semaphores.at[chunk]))
        copies[-1].start()
    for copy in copies:
        copy.wait()


def call(body, name, outputs, scratch, place, inputs, copies=0, far_out=False):
    near, far = pl.BlockSpec(memory_space=pltpu.VMEM), pl.BlockSpec(memory_space=pl.ANY)
    scratch = [pltpu.VMEM(shape, f32) for shape in scratch]
    if copies:
        scratch.append(pltpu.SemaphoreType.DMA((copies,)))
    return pl.pallas_call(
        body,
        name=name,
        out_shape=[jax.ShapeDtypeStruct(shape, f32) for shape in outputs],
        in_specs=[pl.BlockSpec(memory_space=pltpu.SMEM)] + [near] * len(inputs),
        out_specs=[far if far_out else near] * len(outputs),
        scratch_shapes=scratch,
        compiler_params=pltpu.CompilerParams(vmem_limit_bytes=VMEM_LIMIT),
    )(place, *inputs)


def along(value, axis, steps):
    count = lax.axis_size(axis)
    initial, last = max(0, -steps), min(count, count - steps)
    return lax.ppermute(value, axis, [(source, source + steps) for source in range(initial, last)])


def beside(values, sizes):
    if sizes.sides == 1:
        return [[lax.ppermute(value, "width", [(0, 1), (1, 0)]) for value in values]]
    if sizes.sides == 2:
        return [[along(value, "width", steps) for value in values] for steps in (-1, 1)]
    return []


def stages(count):
    stride = 1
    while stride < count:
        radix = 4 if count // stride % 4 == 0 else 2
        yield stride, radix
        stride *= radix


def swap(value, stride, radix):
    count = lax.axis_size("span")
    return [value] + [
        lax.ppermute(value, "span", [(device, device ^ step * stride) for device in range(count)])
        for step in range(1, radix)
    ]


def on_device(right_side, diffusivity, reaction):
    depth, extent_x, extent_y = diffusivity.shape
    sizes = Sizes(depth, extent_x, extent_y, lax.axis_size("span"), lax.axis_size("width"))
    place = jnp.stack([lax.axis_index("span"), lax.axis_index("width")]).astype(jnp.int32)
    n0, n1, n2, n3 = sizes.rows
    s = sizes.sides
    tile = (depth, LANES)
    own = [(depth, count * LANES) for count in sizes.own]
    held = [(depth, count) for count in sizes.held]
    down_message = (sizes.tiles, *tile)
    up_message = (sizes.tiles + 1, *tile)
    own0, own1, own2, to_next, to_prev = call(
        functools.partial(start_kernel, sizes),
        "start",
        [(2, n0, *own[0]), (2 * n1, *own[1]), (2 * n2, *own[2]), down_message, down_message],
        [(2 * n1, *own[0])],
        place,
        [diffusivity, reaction],
    )
    halos = [along(to_next, "span", 1), along(to_prev, "span", -1)]
    turned, *edges = call(
        functools.partial(turn_kernel, sizes),
        "turn",
        [(n0, *own[0])] + [(3, n0, depth, BORDER)] * s,
        [],
        place,
        [right_side, own0],
    )
    if s == 1:
        borders = [lax.ppermute(edges[0], "width", [(0, 1), (1, 0)])]
    elif s == 2:
        borders = [along(edges[1], "width", -1), along(edges[0], "width", 1)]
    else:
        borders = []
    plan = list(stages(sizes.span_count))
    sides = beside(halos, sizes)

    lengths = [sum(coefficient_rows(sizes, level)) for level in range(3)]
    far = (sizes.held[2] // LANES, *tile)
    coefs = [(lengths[level], *held[level]) for level in range(3)]
    downs = call(
        functools.partial(down_kernel, sizes),
        "down",
        [*coefs, (packing(sizes, 5)[2], *tile), up_message, up_message, far, far],
        [(2 * n1, *tile), (2 * n2, *tile), (5, *tile), (max(2 * n1, n1 + 2), *held[0])],
        place,
        [own0, own1, own2, turned, *borders, *halos, *sum(sides, [])],
    )
    coefs_out, blocks, ups, fars = downs[:3], downs[3], downs[4:6], downs[6:8]
    for stride, radix in plan[:-1]:
        count = stride * radix
        (blocks,) = call(
            functools.partial(merge_kernel, sizes, stride, radix),
            "merge",
            [(packing(sizes, 3 * count + 2)[2], *tile)],
            [(count + 2, *tile), (count, *tile), (count, *tile)],
            place,
            swap(blocks, stride, radix),
        )
    stride, radix = plan[-1]
    blocks = swap(blocks, stride, radix)
    received = [along(ups[0], "span", 1), along(ups[1], "span", -1)]
    received += [along(fars[0], "span", 2), along(fars[1], "span", -2)]
    scratch = [(sizes.span_count + 2, *tile), (max(sizes.span_count // 2, 2), *tile)]
    for index in range(3):
        count = sizes.span_count >> index
        scratch += [(count + 1, *tile)] + [(count, *tile)] * 3 + [(count + 2, *tile)] + [(count, *tile)] * 2
        scratch += [(count + 2, *tile)] * 2
    (coarse,) = call(
        functools.partial(coarse_kernel, sizes, stride, radix),
        "coarse",
        [(n3 + 2, *tile)],
        scratch,
        place,
        blocks,
    )
    scratch = [(n1 + 2, *held[1]), (n2 + 2, *held[2]), diffusivity.shape]
    scratch += [(n3 + 2, *held[2]), (n2 + 2, *held[1]), (n1 + 2, *held[0])]
    scratch += [(n2 + 4, *held[2]), (n1 + 4, *held[1]), (n0 + 2, *held[0])]
    scratch += [(n2 + 2, *held[2]), (n1 + 2, *held[1]), (n0, *held[0])]
    (correction,) = call(
        functools.partial(up_kernel, sizes),
        "up",
        [diffusivity.shape],
        scratch,
        place,
        [coarse, *received, *coefs_out, own0, turned, *borders],
        copies=CHUNKS,
        far_out=True,
    )
    return correction


def solution(mesh):
    in_specs = (P(None, "span", "width"),) * 3
    return jax.shard_map(
        on_device, mesh=mesh, in_specs=in_specs, out_specs=P(None, "span", "width"), check_vma=False
    )
```

```python
import functools

import jax
import jax.numpy as jnp
from jax import lax
from jax.experimental import pallas as pl
from jax.experimental.pallas import tpu as pltpu
from jax.sharding import PartitionSpec as P

LEVELS = 6
COARSE_SWEEPS = 3
LANES = 128
BORDER = 128
FRINGE = 4
SPREAD = 16
relax_weight = 0.8
f32 = jnp.float32
VMEM_LIMIT = 32 * 1024 * 1024
BYTES_A_MICRO = 3.69e6
CHUNKS = 4


class Sizes:
    def __init__(self, depth, extent_x, extent_y, span_count, width_count):
        self.depth, self.extent_x, self.extent_y = depth, extent_x, extent_y
        self.span_count, self.width_count = span_count, width_count
        self.sides = min(width_count - 1, 2)
        self.own = [(extent_y >> level) // LANES for level in range(3)]
        self.border = [self.sides, min(self.sides, 1), min(self.sides, 1)]
        self.held = [(self.own[level] + self.border[level]) * LANES for level in range(3)] + [LANES] * 3
        self.rows = [extent_x >> level for level in range(4)]
        self.slots = []
        start = 0
        for level in (0, 1, 1, 1, 2, 2, 2):
            self.slots.append((start, self.own[level]))
            start += self.own[level]
        self.tiles = start


def put(message, slot, row):
    start, tiles = slot
    for tile in range(tiles):
        message[start + tile] = row[:, tile * LANES : (tile + 1) * LANES]


def get(message, slot):
    start, tiles = slot
    return [message[start + tile] for tile in range(tiles)]


def lane_at(shape):
    return lax.broadcasted_iota(jnp.int32, shape, len(shape) - 1)


def roll(value, steps, axis):
    return pltpu.roll(value, steps % value.shape[axis], axis=axis)


def reciprocal(value):
    return pltpu.reciprocal(value, approx=True)


def harmonic(first, second, guard):
    total = first + second
    if guard:
        total = jnp.maximum(total, 1e-3)
    return (2.0 * first) * second * reciprocal(total)


def split(value):
    high = value.astype(jnp.bfloat16)
    return high, (value - high.astype(f32)).astype(jnp.bfloat16)


def dot(halves, table):
    high, low = halves
    return jnp.dot(high, table, preferred_element_type=f32) + jnp.dot(low, table, preferred_element_type=f32)


def pair_table(fine, fine_dim, turn, weight):
    shape = (fine, LANES) if fine_dim == 0 else (LANES, fine)
    fine_at = lax.broadcasted_iota(jnp.int32, shape, fine_dim)
    coarse_at = lax.broadcasted_iota(jnp.int32, shape, 1 - fine_dim)
    if turn is not None:
        coarse_at = coarse_at - jnp.where(fine_at >= turn, LANES // 2, 0)
    return jnp.where(fine_at // 2 == coarse_at, weight, 0.0).astype(jnp.bfloat16)


def turns(sizes, place, level):
    if sizes.sides == 0:
        return []
    if level == 0:
        return [jnp.where(place[1] == 0, LANES, 0)] if sizes.sides == 1 else [LANES, 0]
    return [LANES // 2]


def transfer_plan(sizes, place, level, part):
    plan = []
    if level >= 3:
        return [((0, LANES), 0, 3 * LANES // 4)]
    if level == 2:
        return [((0, sizes.held[2]), 0, None)]
    own = sizes.own[level]
    if part != "border":
        plan += [((2 * LANES * tile, 2 * LANES * (tile + 1)), tile, None) for tile in range(own // 2)]
    if part != "own":
        for index, turn in enumerate(turns(sizes, place, level)):
            start = (own + index) * LANES
            plan.append(((start, start + LANES), own // 2, turn))
    return plan


def narrow(sizes, place, level, sums, target, rows, part="all", shift=0):
    depth = sums.shape[1]
    done = {}
    for (start, stop), tile, turn in transfer_plan(sizes, place, level, part):
        start, stop, tile = start - shift, stop - shift, tile - shift // (2 * LANES)
        columns = split(sums[0:rows, :, start:stop].reshape(rows * depth, stop - start))
        result = dot(columns, pair_table(stop - start, 0, turn, 0.25)).reshape(rows, depth, LANES)
        done[tile] = done[tile] + result if tile in done else result
    for tile, result in done.items():
        target[0:rows, :, tile * LANES : (tile + 1) * LANES] = result


def widen(sizes, place, level, coarse, target, rows):
    depth = coarse.shape[1]
    for (start, stop), tile, turn in transfer_plan(sizes, place, level, "all"):
        columns = split(coarse[0:rows, :, tile * LANES : (tile + 1) * LANES].reshape(rows * depth, LANES))
        result = dot(columns, pair_table(stop - start, 1, turn, 4.0))
        target[0:rows, :, start:stop] = result.reshape(rows, depth, stop - start)


def coefficients(sizes, place, level, count, conduct, binding, fx, fy, fz, weight):
    guard = level > 0 or sizes.sides > 1
    for row in range(1, count):
        fx[row - 1] = harmonic(conduct(row - 1), conduct(row), guard)
    for row in range(1, count - 1):
        mine = conduct(row)
        south = harmonic(mine, roll(mine, 1, 1), guard)
        if level == 0 and sizes.sides < 2:
            cut = 0 if sizes.sides == 0 else jnp.where(place[1] == 0, 0, sizes.extent_y)
            south = jnp.where(lane_at(mine.shape) == cut, 0.0, south)
        below = harmonic(mine, roll(mine, 1, 0), guard)
        below = jnp.where(lax.broadcasted_iota(jnp.int32, mine.shape, 0) == 0, 0.0, below)
        diagonal = fx[row - 1] + fx[row] + binding(row)
        diagonal = diagonal + (south + roll(south, -1, 1)) + (below + roll(below, -1, 0))
        if guard:
            diagonal = jnp.maximum(diagonal, 1e-6)
        fy[row - 1] = south
        fz[row - 1] = below
        weight[row - 1] = relax_weight * reciprocal(diagonal)


def sweep(count, field, binding, fx, fy, fz, emit):
    lower = fx[0] * (field(1) - field(0))
    for row in range(1, count - 1):
        mine = field(row)
        upper = fx[row] * (field(row + 1) - mine)
        south = fy[row - 1] * (mine - roll(mine, 1, 1))
        below = fz[row - 1] * (mine - roll(mine, 1, 0))
        across = (south - roll(south, -1, 1)) + (below - roll(below, -1, 0))
        emit(row, binding(row) * mine + (lower - upper) + across)
        lower = upper


def own_defect(count, smooth, source, binding, fx, fy, fz, sums, first):
    zero = jnp.zeros(smooth.shape[1:], f32)

    def field(row):
        return smooth[row - 1] if 0 < row < count - 1 else zero

    def add(row, value):
        slot = (row + first) // 2
        if (row + first) % 2 == 0 or row == 0:
            sums[slot] = value
        else:
            sums[slot] = sums[slot] + value

    add(0, fx[0] * field(1))
    sweep(count, field, binding, fx, fy, fz, lambda row, result: add(row, source(row) - result))
    add(count - 1, fx[count - 2] * field(count - 2))


def parts(array, counts):
    views, start = [], 0
    for count in counts:
        views.append(array.at[start : start + count])
        start += count
    return views


def coefficient_rows(sizes, level):
    n = sizes.rows[level]
    if level == 0:
        return [n + 1, n, n, n, n]
    return [n + 3] + [n + 2] * 6


def start_kernel(sizes, place, conduct, binding, own0, own1, own2, to_next, to_prev, sums):
    n0, n1, n2 = sizes.rows[:3]
    for at, array in enumerate((conduct, binding)):
        own0[at] = jnp.swapaxes(array[...], 0, 1)
    for at in (0, 1):
        for row in range(n1):
            sums[at * n1 + row] = own0[at, 2 * row] + own0[at, 2 * row + 1]
    narrow(sizes, place, 0, sums, own1, 2 * n1, "own")
    for row in range(2 * n2):
        sums[row, :, : sizes.own[1] * LANES] = own1[2 * row] + own1[2 * row + 1]
    narrow(sizes, place, 1, sums, own2, 2 * n2, "own")
    for message, low, at1, at0 in ((to_next, n1 - 2, n1 - 1, n0 - 1), (to_prev, 0, 0, 0)):
        edge = n2 - 1 if at0 else 0
        rows = (own0[0, at0], own1[low], own1[low + 1], own1[n1 + at1])
        rows += (own2[n2 - 2], own2[n2 - 1], own2[n2 + edge])
        for slot, row in zip(sizes.slots, rows):
            put(message, slot, row)


def turn_kernel(sizes, place, right_side, own0, turned, *edges):
    turned[...] = jnp.swapaxes(right_side[...], 0, 1)
    last = sizes.extent_y - BORDER
    for index, array in enumerate((own0.at[0], own0.at[1], turned)):
        if sizes.sides == 1:
            at = pl.multiple_of(jnp.where(place[1] == 0, last, 0), LANES)
            edges[0][index] = array[:, :, pl.ds(at, BORDER)]
        elif sizes.sides == 2:
            edges[0][index] = array[:, :, last:]
            edges[1][index] = array[:, :, :BORDER]


def message_row(sizes, place, level, slot, message, beside):
    start, tiles = slot
    row = get(message, slot)
    if sizes.sides == 1:
        left = place[1] != 0
        tile = beside[0][start + jnp.where(left, tiles - 1, 0)]
        if level > 0:
            reach = BORDER >> level
            lane = lane_at(tile.shape)
            first = jnp.where(left, LANES - reach, 0)
            tile = jnp.where((lane >= first) & (lane < first + reach), tile, 0.0)
        row.append(tile)
    elif sizes.sides == 2:
        right, left = beside[0][start], beside[1][start + tiles - 1]
        if level == 0:
            row += [right, left]
        else:
            reach = BORDER >> level
            lane = lane_at(right.shape)
            row.append(jnp.where(lane < reach, right, jnp.where(lane >= LANES - reach, left, 0.0)))
    return jnp.concatenate(row, axis=1)


def fringe_lanes(shape):
    lane = lane_at(shape)
    return (lane < FRINGE) | (lane >= LANES - FRINGE)


def put_fringes(sizes, message, rows):
    total = None
    for index, (level, row) in enumerate(rows):
        tile = row[:, sizes.own[level] * LANES :]
        tile = jnp.where(fringe_lanes(tile.shape), tile, 0.0)
        tile = roll(tile, SPREAD * index + SPREAD // 2, 1)
        total = tile if total is None else total + tile
    message[sizes.tiles] = total


def fringed_row(sizes, level, index, message):
    row = get(message, sizes.slots[index])
    if sizes.border[level]:
        if level == 0:
            row += [jnp.zeros(row[0].shape, f32)] * sizes.border[0]
        else:
            tile = roll(message[sizes.tiles], -(SPREAD * (index - 1) + SPREAD // 2), 1)
            row.append(jnp.where(fringe_lanes(tile.shape), tile, 0.0))
    return jnp.concatenate(row, axis=1)


def packing(sizes, count):
    if sizes.sides != 1:
        return False, count, count
    own = -(-count // 2)
    return True, own, own - (-count * (BORDER >> 3) // LANES)


def border_turn(place, goal):
    return jnp.where(place[1] == 0, (goal - LANES // 2) % LANES, (goal + (BORDER >> 3)) % LANES)


def pack_rows(sizes, place, rows, target):
    packed, own, tiles = packing(sizes, len(rows))
    if not packed:
        for index, row in enumerate(rows):
            target[index] = row
        return
    half, reach = LANES // 2, BORDER >> 3
    lane = lane_at(rows[0].shape)
    for index in range(own):
        held = rows[2 * index]
        other = rows[2 * index + 1] if 2 * index + 1 < len(rows) else jnp.zeros(held.shape, f32)
        target[index] = jnp.where(lane < half, held, pltpu.roll(other, half, axis=1))
    for index in range(own, tiles):
        held = jnp.zeros(rows[0].shape, f32)
        some = rows[(index - own) * (LANES // reach) :][: LANES // reach]
        for place_at, row in enumerate(some):
            goal = place_at * reach
            moved = pltpu.roll(row, border_turn(place, goal), axis=1)
            held = jnp.where((lane >= goal) & (lane < goal + reach), moved, held)
        target[index] = held


def unpack_rows(sizes, place, blocks, count):
    packed, own, _ = packing(sizes, count)
    if not packed:
        return [blocks[index] for index in range(count)]
    half, reach = LANES // 2, BORDER >> 3
    rows = []
    for index in range(count):
        held = blocks[index // 2]
        lane = lane_at(held.shape)
        if index % 2:
            held = pltpu.roll(held, half, axis=1)
        at, goal = index // (LANES // reach), index % (LANES // reach) * reach
        back = lax.rem(LANES - border_turn(place, goal), LANES)
        beside = pltpu.roll(blocks[own + at], back, axis=1)
        start = jnp.where(place[1] == 0, half, LANES - reach)
        here = (lane >= start) & (lane < start + reach)
        rows.append(jnp.where(lane < half, held, jnp.where(here, beside, 0.0)))
    return rows


def merge_into(sizes, place, stride, radix, arrays, source, conduct, binding, first):
    position = (place[0] // stride) % radix
    source[...] = jnp.zeros(source.shape, f32)
    for step, array in enumerate(arrays):
        at = (position ^ step) * stride
        rows = unpack_rows(sizes, place, array, 3 * stride + 2)
        for index, row in enumerate(rows[: stride + 2]):
            source[at + index] = source[at + index] + row
        for index in range(stride):
            conduct[at + index + first] = rows[stride + 2 + index]
            binding[at + index] = rows[2 * stride + 2 + index]


def merge_kernel(sizes, stride, radix, place, *refs):
    arrays, out, (source, conduct, binding) = refs[:radix], refs[radix], refs[radix + 1 :]
    merge_into(sizes, place, stride, radix, arrays, source, conduct, binding, 0)
    count = stride * radix
    rows = [source[row] for row in range(count + 2)]
    rows += [conduct[row] for row in range(count)] + [binding[row] for row in range(count)]
    pack_rows(sizes, place, rows, out)


def down_kernel(sizes, place, *refs):
    s = sizes.sides
    owns, turned, refs = refs[:3], refs[3], refs[4:]
    borders0, refs = refs[:s], refs[s:]
    from_prev, from_next, refs = refs[0], refs[1], refs[2:]
    beside_prev, beside_next, refs = refs[: 2 * s : 2], refs[1 : 2 * s : 2], refs[2 * s :]
    coefs, contribution, ups, fars, refs = refs[:3], refs[3], refs[4:6], refs[6:8], refs[8:]
    border1, border2, level3, sums = refs
    slots = sizes.slots
    n0, n1, n2 = sizes.rows[:3]

    if s:
        for row in range(2 * n1):
            for side in range(s):
                columns = slice(side * LANES, (side + 1) * LANES)
                at, low = row // n1, 2 * (row % n1)
                sums[row, :, columns] = borders0[side][at, low] + borders0[side][at, low + 1]
        narrow(sizes, place, 0, sums, border1, 2 * n1, "border", sizes.own[0] * LANES)
        for row in range(2 * n2):
            sums[row, :, :LANES] = border1[2 * row] + border1[2 * row + 1]
        narrow(sizes, place, 1, sums, border2, 2 * n2, "border", sizes.own[1] * LANES)

    def held_row(level, at, row):
        if level == 0:
            tiles = [turned[row] if at == 2 else owns[0][at, row], *(array[at, row] for array in borders0)]
        else:
            row = at * sizes.rows[level] + row
            tiles = [owns[level][row], *([(border1, border2)[level - 1][row]] if s else [])]
        return jnp.concatenate(tiles, axis=1)

    def prev_row(level, index):
        return message_row(sizes, place, level, slots[index], from_prev, beside_prev)

    def next_row(level, index):
        return message_row(sizes, place, level, slots[index], from_next, beside_next)

    def conduct0(row):
        if row == 0:
            return prev_row(0, 0)
        if row == n0 + 1:
            return next_row(0, 0)
        return held_row(0, 0, row - 1)

    bound0 = lambda row: held_row(0, 1, row - 1)
    fx, fy, fz, weight, v0 = parts(coefs[0], coefficient_rows(sizes, 0))
    coefficients(sizes, place, 0, n0 + 2, conduct0, bound0, fx, fy, fz, weight)
    for row in range(n0):
        v0[row] = weight[row] * held_row(0, 2, row)
    own_defect(n0 + 2, v0, lambda row: held_row(0, 2, row - 1), bound0, fx, fy, fz, sums, 1)
    smooths, sources = [], []
    for level, first in ((1, 1), (2, 4)):
        n = sizes.rows[level]
        fx, fy, fz, weight, binding, source, smooth = parts(coefs[level], coefficient_rows(sizes, level))
        held = sizes.held[level]
        narrow(sizes, place, level - 1, sums.at[:, :, : sizes.held[level - 1]], source, n + 2)
        binding[0] = prev_row(level, first + 2)
        binding[n + 1] = next_row(level, first + 2)
        for row in range(n):
            binding[row + 1] = held_row(level, 1, row)

        def conduct(row, n=n, level=level, first=first):
            if row < 2:
                return prev_row(level, first + row)
            if row >= n + 2:
                return next_row(level, first + row - n - 2)
            return held_row(level, 0, row - 2)

        bound = lambda row, binding=binding: binding[row - 1]
        coefficients(sizes, place, level, n + 4, conduct, bound, fx, fy, fz, weight)
        for row in range(n + 2):
            smooth[row] = weight[row] * source[row]
        mine = lambda row, source=source: source[row - 1]
        own_defect(n + 4, smooth, mine, bound, fx, fy, fz, sums.at[:, :, :held], 0)
        smooths.append(smooth)
        sources.append(source)
    narrow(sizes, place, 2, sums.at[:, :, : sizes.held[2]], level3, 3)

    for at in (0, 1):
        sums[at, :, : sizes.held[2]] = held_row(2, at, 0) + held_row(2, at, 1)
    narrow(sizes, place, 2, sums.at[:, :, : sizes.held[2]], level3.at[3:5], 2)
    pack_rows(sizes, place, [level3[row] for row in range(5)], contribution)
    (s1, s2), (v1, v2) = sources, smooths
    for at, rows in enumerate(
        (
            (v0[n0 - 1], s1[n1], s1[n1 + 1], v1[n1 - 1], s2[n2], s2[n2 + 1], v2[n2 - 1]),
            (v0[0], s1[1], s1[0], v1[2], s2[1], s2[0], v2[2]),
        )
    ):
        for slot, row in zip(slots, rows):
            put(ups[at], slot, row)
        if s:
            put_fringes(sizes, ups[at], list(zip((1, 1, 1, 2, 2, 2), rows[1:])))
        put(fars[at], (0, sizes.held[2] // LANES), v2[n2 + 1 if at == 0 else 0])


def relax(count, field, refs_of, source, target):
    fx, fy, fz, weight, binding = refs_of

    def update(row, value):
        target(row, field(row) + weight[row - 1] * (source(row) - value))

    sweep(count, field, binding, fx, fy, fz, update)


def store(array, first):
    def put_row(row, value):
        array[row - first] = value

    return put_row


def coarse_kernel(sizes, stride, radix, place, *refs):
    blocks, refs = refs[:radix], refs[radix:]
    out, merged, sums = refs[:3]
    coarse = [refs[3 + 9 * index : 12 + 9 * index] for index in range(3)]
    total = sizes.span_count
    merge_into(sizes, place, stride, radix, blocks, merged, coarse[0][4], coarse[0][5], 1)
    zero = jnp.zeros((sizes.depth, LANES), f32)
    for index in range(3):
        level = 3 + index
        fx, fy, fz, weight, conduct, binding, source, smooth, iterate = coarse[index]
        count = total >> index
        for array in (conduct, smooth, iterate):
            array[0] = zero
            array[count + 1] = zero
        if index == 0:
            source = merged.at[1 : count + 1]
        bound = lambda row, binding=binding: binding[row - 1]
        at_row = lambda row, conduct=conduct: conduct[row]
        coefficients(sizes, place, level, count + 2, at_row, bound, fx, fy, fz, weight)
        for row in range(count):
            smooth[row + 1] = weight[row] * source[row]
        if index < 2:
            conduct_next, binding_next, source_next = coarse[index + 1][4:7]
            half = count // 2
            for row in range(half):
                sums[row, :, :LANES] = conduct[2 * row + 1] + conduct[2 * row + 2]
            narrow(sizes, place, level, sums, conduct_next.at[1 : half + 1], half)
            for row in range(half):
                sums[row, :, :LANES] = binding[2 * row] + binding[2 * row + 1]
            narrow(sizes, place, level, sums, binding_next, half)

            def add(row, value, source=source):
                value = source[row - 1] - value
                slot = (row - 1) // 2
                if row % 2 == 1:
                    sums[slot, :, :LANES] = value
                else:
                    sums[slot, :, :LANES] = sums[slot, :, :LANES] + value

            sweep(count + 2, lambda row, smooth=smooth: smooth[row], bound, fx, fy, fz, add)
            narrow(sizes, place, level, sums, source_next, half)

    fx, fy, fz, weight, conduct, binding, source, smooth, iterate = coarse[2]
    held, other = smooth, iterate
    for _ in range(COARSE_SWEEPS - 1):
        field = lambda row, held=held: held[row]
        mine = lambda row: source[row - 1]
        bound = lambda row: binding[row - 1]
        relax((total >> 2) + 2, field, (fx, fy, fz, weight, bound), mine, store(other, 0))
        held, other = other, held
    for index in (1, 0):
        fx, fy, fz, weight, conduct, binding, source, smooth, iterate = coarse[index]
        if index == 0:
            source = merged.at[1 : total + 1]
        count = total >> index
        widen(sizes, place, 3 + index, held.at[1 : count // 2 + 1], sums, count // 2)
        for row in range(count):
            smooth[row + 1] = smooth[row + 1] + sums[row // 2, :, :LANES]
        field = lambda row, smooth=smooth: smooth[row]
        mine = lambda row, source=source: source[row - 1]
        bound = lambda row, binding=binding: binding[row - 1]
        relax(count + 2, field, (fx, fy, fz, weight, bound), mine, store(iterate, 0))
        held = iterate

    out[...] = held[pl.ds(place[0], 3)]


def up_kernel(sizes, place, coarse, *refs):
    s = sizes.sides
    (from_prev, from_next), fars, coefs, (own0, turned) = refs[:2], refs[2:4], refs[4:7], refs[7:9]
    borders0, out, refs = refs[9 : 9 + s], refs[9 + s], refs[10 + s :]
    total1, total2, result = refs[:3]
    over2, over1, over0, lift2, lift1, lift0, it2, it1, it0, semaphores = refs[3:]
    slots = sizes.slots
    n0, n1, n2 = sizes.rows[:3]
    width = sizes.own[0] * LANES

    widen(sizes, place, 2, coarse, over2, 3)
    for level, array, first, totals, over, lift, target, upper in (
        (2, coefs[2], 4, total2, over2, lift2, it2, over1),
        (1, coefs[1], 1, total1, over1, lift1, it1, over0),
    ):
        n = sizes.rows[level]
        fx, fy, fz, weight, binding, own, smooth = parts(array, coefficient_rows(sizes, level))
        edge = {}
        for row, message, index in (
            (1, from_prev, first),
            (2, from_prev, first + 1),
            (n + 2, from_next, first),
            (n + 1, from_next, first + 1),
        ):
            value = edge.get(row, own[row - 1])
            edge[row] = value + fringed_row(sizes, level, index, message)
        for row, value in edge.items():
            totals[row - 1] = value
        for row in range(n + 4):
            if row in (0, n + 3):
                value = fringed_row(sizes, level, first + 2, from_next if row else from_prev)
                if level == 2:
                    far = fars[1 if row else 0]
                    value = value + jnp.concatenate(get(far, (0, sizes.held[2] // LANES)), axis=1)
            elif row in edge:
                value = weight[row - 1] * totals[row - 1]
            else:
                value = smooth[row - 1]
            lift[row] = value + over[row // 2]
        field = lambda row, lift=lift: lift[row]
        mine = lambda row, own=own, totals=totals, edge=edge: (totals if row in edge else own)[row - 1]
        bound = lambda row, binding=binding: binding[row - 1]
        relax(n + 4, field, (fx, fy, fz, weight, bound), mine, store(target, 1))
        widen(sizes, place, level - 1, target, upper, n + 2)

    def held_row(at, row):
        own = turned[row - 1] if at == 2 else own0[at, row - 1]
        return jnp.concatenate([own, *(array[at, row - 1] for array in borders0)], axis=1)

    fx, fy, fz, weight, v0 = parts(coefs[0], coefficient_rows(sizes, 0))
    lift0[0] = fringed_row(sizes, 0, 0, from_prev) + over0[0]
    lift0[n0 + 1] = fringed_row(sizes, 0, 0, from_next) + over0[n1 + 1]
    for row in range(1, n0 + 1):
        lift0[row] = v0[row - 1] + over0[(row + 1) // 2]
    field = lambda row: lift0[row]
    bound = lambda row: held_row(1, row)
    relax(n0 + 2, field, (fx, fy, fz, weight, bound), lambda row: held_row(2, row), store(it0, 1))
    step = sizes.depth // CHUNKS
    copies = []
    for chunk in range(CHUNKS):
        part = slice(chunk * step, (chunk + 1) * step)
        result[part] = jnp.swapaxes(it0[:, part, :width], 0, 1)
        copies.append(pltpu.make_async_copy(result.at[part], out.at[part], semaphores.at[chunk]))
        copies[-1].start()
    for copy in copies:
        copy.wait()


def call(body, name, micros, outputs, scratch, place, inputs, copies=0, far_out=False):
    near, far = pl.BlockSpec(memory_space=pltpu.VMEM), pl.BlockSpec(memory_space=pl.ANY)
    scratch = [pltpu.VMEM(shape, f32) for shape in scratch]
    if copies:
        scratch.append(pltpu.SemaphoreType.DMA((copies,)))
    return pl.pallas_call(
        body,
        name=name,
        out_shape=[jax.ShapeDtypeStruct(shape, f32) for shape in outputs],
        in_specs=[pl.BlockSpec(memory_space=pltpu.SMEM)] + [near] * len(inputs),
        out_specs=[far if far_out else near] * len(outputs),
        scratch_shapes=scratch,
        cost_estimate=pl.CostEstimate(flops=int(micros * 1.15e9), bytes_accessed=int(micros * BYTES_A_MICRO), transcendentals=0),
        compiler_params=pltpu.CompilerParams(vmem_limit_bytes=VMEM_LIMIT),
    )(place, *inputs)


def along(value, axis, steps):
    count = lax.axis_size(axis)
    initial, last = max(0, -steps), min(count, count - steps)
    return lax.ppermute(value, axis, [(source, source + steps) for source in range(initial, last)])


def beside(values, sizes):
    if sizes.sides == 1:
        return [[lax.ppermute(value, "width", [(0, 1), (1, 0)]) for value in values]]
    if sizes.sides == 2:
        return [[along(value, "width", steps) for value in values] for steps in (-1, 1)]
    return []


def stages(count):
    stride = 1
    while stride < count:
        radix = 4 if count // stride % 4 == 0 else 2
        yield stride, radix
        stride *= radix


def swap(value, stride, radix):
    count = lax.axis_size("span")
    return [value] + [
        lax.ppermute(value, "span", [(device, device ^ step * stride) for device in range(count)])
        for step in range(1, radix)
    ]


def on_device(right_side, diffusivity, reaction):
    depth, extent_x, extent_y = diffusivity.shape
    sizes = Sizes(depth, extent_x, extent_y, lax.axis_size("span"), lax.axis_size("width"))
    place = jnp.stack([lax.axis_index("span"), lax.axis_index("width")]).astype(jnp.int32)
    n0, n1, n2, n3 = sizes.rows
    s = sizes.sides
    tile = (depth, LANES)
    own = [(depth, count * LANES) for count in sizes.own]
    held = [(depth, count) for count in sizes.held]
    down_message = (sizes.tiles, *tile)
    up_message = (sizes.tiles + 1, *tile)
    own0, own1, own2, to_next, to_prev = call(
        functools.partial(start_kernel, sizes),
        "start",
        1.1,
        [(2, n0, *own[0]), (2 * n1, *own[1]), (2 * n2, *own[2]), down_message, down_message],
        [(2 * n1, *own[0])],
        place,
        [diffusivity, reaction],
    )
    halos = [along(to_next, "span", 1), along(to_prev, "span", -1)]
    turned, *edges = call(
        functools.partial(turn_kernel, sizes),
        "turn",
        0.7,
        [(n0, *own[0])] + [(3, n0, depth, BORDER)] * s,
        [],
        place,
        [right_side, own0],
    )
    if s == 1:
        borders = [lax.ppermute(edges[0], "width", [(0, 1), (1, 0)])]
    elif s == 2:
        borders = [along(edges[1], "width", -1), along(edges[0], "width", 1)]
    else:
        borders = []
    plan = list(stages(sizes.span_count))
    sides = beside(halos, sizes)

    lengths = [sum(coefficient_rows(sizes, level)) for level in range(3)]
    far = (sizes.held[2] // LANES, *tile)
    coefs = [(lengths[level], *held[level]) for level in range(3)]
    downs = call(
        functools.partial(down_kernel, sizes),
        "down",
        3.6,
        [*coefs, (packing(sizes, 5)[2], *tile), up_message, up_message, far, far],
        [(2 * n1, *tile), (2 * n2, *tile), (5, *tile), (max(2 * n1, n1 + 2), *held[0])],
        place,
        [own0, own1, own2, turned, *borders, *halos, *sum(sides, [])],
    )
    coefs_out, blocks, ups, fars = downs[:3], downs[3], downs[4:6], downs[6:8]
    far_rows = [along(fars[0], "span", 2), along(fars[1], "span", -2)]
    for stride, radix in plan[:-1]:
        count = stride * radix
        blocks = swap(blocks, stride, radix)
        blocks, far_rows = lax.optimization_barrier((blocks, far_rows))
        (blocks,) = call(
            functools.partial(merge_kernel, sizes, stride, radix),
            "merge",
            0.9,
            [(packing(sizes, 3 * count + 2)[2], *tile)],
            [(count + 2, *tile), (count, *tile), (count, *tile)],
            place,
            blocks,
        )
    stride, radix = plan[-1]
    blocks = swap(blocks, stride, radix)
    received = [along(ups[0], "span", 1), along(ups[1], "span", -1)]
    received += far_rows
    scratch = [(sizes.span_count + 2, *tile), (max(sizes.span_count // 2, 2), *tile)]
    for index in range(3):
        count = sizes.span_count >> index
        scratch += [(count + 1, *tile)] + [(count, *tile)] * 3 + [(count + 2, *tile)] + [(count, *tile)] * 2
        scratch += [(count + 2, *tile)] * 2
    (coarse,) = call(
        functools.partial(coarse_kernel, sizes, stride, radix),
        "coarse",
        2.9,
        [(n3 + 2, *tile)],
        scratch,
        place,
        blocks,
    )
    scratch = [(n1 + 2, *held[1]), (n2 + 2, *held[2]), diffusivity.shape]
    scratch += [(n3 + 2, *held[2]), (n2 + 2, *held[1]), (n1 + 2, *held[0])]
    scratch += [(n2 + 4, *held[2]), (n1 + 4, *held[1]), (n0 + 2, *held[0])]
    scratch += [(n2 + 2, *held[2]), (n1 + 2, *held[1]), (n0, *held[0])]
    (correction,) = call(
        functools.partial(up_kernel, sizes),
        "up",
        3.0,
        [diffusivity.shape],
        scratch,
        place,
        [coarse, *received, *coefs_out, own0, turned, *borders],
        copies=CHUNKS,
        far_out=True,
    )
    return correction


def solution(mesh):
    in_specs = (P(None, "span", "width"),) * 3
    return jax.shard_map(
        on_device, mesh=mesh, in_specs=in_specs, out_specs=P(None, "span", "width"), check_vma=False
    )
```

```python
import functools

import jax
import jax.numpy as jnp
from jax import lax
from jax.experimental import pallas as pl
from jax.experimental.pallas import tpu as pltpu
from jax.sharding import PartitionSpec as P

LEVELS = 6
COARSE_SWEEPS = 3
LANES = 128
BORDER = 128
FRINGE = 4
SPREAD = 16
relax_weight = 0.8
f32 = jnp.float32
VMEM_LIMIT = 32 * 1024 * 1024
BYTES_A_MICRO = 3.69e6
CHUNKS = 4


class Sizes:
    def __init__(self, depth, extent_x, extent_y, span_count, width_count):
        self.depth, self.extent_x, self.extent_y = depth, extent_x, extent_y
        self.span_count, self.width_count = span_count, width_count
        self.sides = min(width_count - 1, 2)
        self.own = [(extent_y >> level) // LANES for level in range(3)]
        self.border = [self.sides, min(self.sides, 1), min(self.sides, 1)]
        self.held = [(self.own[level] + self.border[level]) * LANES for level in range(3)] + [LANES] * 3
        self.rows = [extent_x >> level for level in range(4)]
        self.slots = []
        start = 0
        for level in (0, 1, 1, 1, 2, 2, 2):
            self.slots.append((start, self.own[level]))
            start += self.own[level]
        self.tiles = start


def put(message, slot, row):
    start, tiles = slot
    for tile in range(tiles):
        message[start + tile] = row[:, tile * LANES : (tile + 1) * LANES]


class Arrived:
    def __init__(self, place, pair, forward, stride=1):
        self.even = place[0] // stride % 2 == 0
        self.first, self.second = (pair[0], pair[1]) if forward else (pair[1], pair[0])

    def __getitem__(self, index):
        return jnp.where(self.even, self.first[index], self.second[index])


def put_pair(place, pair, slot, next_row, prev_row, stride=1):
    even = place[0] // stride % 2 == 0
    put(pair[0], slot, jnp.where(even, next_row, prev_row))
    put(pair[1], slot, jnp.where(even, prev_row, next_row))


def get(message, slot):
    start, tiles = slot
    return [message[start + tile] for tile in range(tiles)]


def lane_at(shape):
    return lax.broadcasted_iota(jnp.int32, shape, len(shape) - 1)


def roll(value, steps, axis):
    return pltpu.roll(value, steps % value.shape[axis], axis=axis)


def reciprocal(value):
    return pltpu.reciprocal(value, approx=True)


def harmonic(first, second, guard):
    total = first + second
    if guard:
        total = jnp.maximum(total, 1e-3)
    return (2.0 * first) * second * reciprocal(total)


def split(value):
    high = value.astype(jnp.bfloat16)
    return high, (value - high.astype(f32)).astype(jnp.bfloat16)


def dot(halves, table):
    high, low = halves
    return jnp.dot(high, table, preferred_element_type=f32) + jnp.dot(low, table, preferred_element_type=f32)


def pair_table(fine, fine_dim, turn, weight):
    shape = (fine, LANES) if fine_dim == 0 else (LANES, fine)
    fine_at = lax.broadcasted_iota(jnp.int32, shape, fine_dim)
    coarse_at = lax.broadcasted_iota(jnp.int32, shape, 1 - fine_dim)
    if turn is not None:
        coarse_at = coarse_at - jnp.where(fine_at >= turn, LANES // 2, 0)
    return jnp.where(fine_at // 2 == coarse_at, weight, 0.0).astype(jnp.bfloat16)


def turns(sizes, place, level):
    if sizes.sides == 0:
        return []
    if level == 0:
        return [jnp.where(place[1] == 0, LANES, 0)] if sizes.sides == 1 else [LANES, 0]
    return [LANES // 2]


def transfer_plan(sizes, place, level, part):
    plan = []
    if level >= 3:
        return [((0, LANES), 0, 3 * LANES // 4)]
    if level == 2:
        return [((0, sizes.held[2]), 0, None)]
    own = sizes.own[level]
    if part != "border":
        plan += [((2 * LANES * tile, 2 * LANES * (tile + 1)), tile, None) for tile in range(own // 2)]
    if part != "own":
        for index, turn in enumerate(turns(sizes, place, level)):
            start = (own + index) * LANES
            plan.append(((start, start + LANES), own // 2, turn))
    return plan


def narrow(sizes, place, level, sums, target, rows, part="all", shift=0):
    depth = sums.shape[1]
    done = {}
    for (start, stop), tile, turn in transfer_plan(sizes, place, level, part):
        start, stop, tile = start - shift, stop - shift, tile - shift // (2 * LANES)
        columns = split(sums[0:rows, :, start:stop].reshape(rows * depth, stop - start))
        result = dot(columns, pair_table(stop - start, 0, turn, 0.25)).reshape(rows, depth, LANES)
        done[tile] = done[tile] + result if tile in done else result
    for tile, result in done.items():
        target[0:rows, :, tile * LANES : (tile + 1) * LANES] = result


def widen(sizes, place, level, coarse, target, rows):
    depth = coarse.shape[1]
    for (start, stop), tile, turn in transfer_plan(sizes, place, level, "all"):
        columns = split(coarse[0:rows, :, tile * LANES : (tile + 1) * LANES].reshape(rows * depth, LANES))
        result = dot(columns, pair_table(stop - start, 1, turn, 4.0))
        target[0:rows, :, start:stop] = result.reshape(rows, depth, stop - start)


def coefficients(sizes, place, level, count, conduct, binding, fx, fy, fz, weight):
    guard = level > 0 or sizes.sides > 1
    for row in range(1, count):
        fx[row - 1] = harmonic(conduct(row - 1), conduct(row), guard)
    for row in range(1, count - 1):
        mine = conduct(row)
        south = harmonic(mine, roll(mine, 1, 1), guard)
        if level == 0 and sizes.sides < 2:
            cut = 0 if sizes.sides == 0 else jnp.where(place[1] == 0, 0, sizes.extent_y)
            south = jnp.where(lane_at(mine.shape) == cut, 0.0, south)
        below = harmonic(mine, roll(mine, 1, 0), guard)
        below = jnp.where(lax.broadcasted_iota(jnp.int32, mine.shape, 0) == 0, 0.0, below)
        diagonal = fx[row - 1] + fx[row] + binding(row)
        diagonal = diagonal + (south + roll(south, -1, 1)) + (below + roll(below, -1, 0))
        if guard:
            diagonal = jnp.maximum(diagonal, 1e-6)
        fy[row - 1] = south
        fz[row - 1] = below
        weight[row - 1] = relax_weight * reciprocal(diagonal)


def sweep(count, field, binding, fx, fy, fz, emit):
    lower = fx[0] * (field(1) - field(0))
    for row in range(1, count - 1):
        mine = field(row)
        upper = fx[row] * (field(row + 1) - mine)
        south = fy[row - 1] * (mine - roll(mine, 1, 1))
        below = fz[row - 1] * (mine - roll(mine, 1, 0))
        across = (south - roll(south, -1, 1)) + (below - roll(below, -1, 0))
        emit(row, binding(row) * mine + (lower - upper) + across)
        lower = upper


def own_defect(count, smooth, source, binding, fx, fy, fz, sums, first):
    zero = jnp.zeros(smooth.shape[1:], f32)

    def field(row):
        return smooth[row - 1] if 0 < row < count - 1 else zero

    def add(row, value):
        slot = (row + first) // 2
        if (row + first) % 2 == 0 or row == 0:
            sums[slot] = value
        else:
            sums[slot] = sums[slot] + value

    add(0, fx[0] * field(1))
    sweep(count, field, binding, fx, fy, fz, lambda row, result: add(row, source(row) - result))
    add(count - 1, fx[count - 2] * field(count - 2))


def parts(array, counts):
    views, start = [], 0
    for count in counts:
        views.append(array.at[start : start + count])
        start += count
    return views


def coefficient_rows(sizes, level):
    n = sizes.rows[level]
    if level == 0:
        return [n + 1, n, n, n, n]
    return [n + 3] + [n + 2] * 6


def start_kernel(sizes, place, conduct, binding, own0, own1, own2, first, second, sums):
    n0, n1, n2 = sizes.rows[:3]
    for at, array in enumerate((conduct, binding)):
        own0[at] = jnp.swapaxes(array[...], 0, 1)
    for at in (0, 1):
        for row in range(n1):
            sums[at * n1 + row] = own0[at, 2 * row] + own0[at, 2 * row + 1]
    narrow(sizes, place, 0, sums, own1, 2 * n1, "own")
    for row in range(2 * n2):
        sums[row, :, : sizes.own[1] * LANES] = own1[2 * row] + own1[2 * row + 1]
    narrow(sizes, place, 1, sums, own2, 2 * n2, "own")
    ends = []
    for low, at1, at0 in ((n1 - 2, n1 - 1, n0 - 1), (0, 0, 0)):
        edge = n2 - 1 if at0 else 0
        rows = (own0[0, at0], own1[low], own1[low + 1], own1[n1 + at1])
        ends.append(rows + (own2[n2 - 2], own2[n2 - 1], own2[n2 + edge]))
    for slot, next_row, prev_row in zip(sizes.slots, *ends):
        put_pair(place, (first, second), slot, next_row, prev_row)


def turn_kernel(sizes, place, right_side, own0, turned, *edges):
    turned[...] = jnp.swapaxes(right_side[...], 0, 1)
    last = sizes.extent_y - BORDER
    for index, array in enumerate((own0.at[0], own0.at[1], turned)):
        if sizes.sides == 1:
            at = pl.multiple_of(jnp.where(place[1] == 0, last, 0), LANES)
            edges[0][index] = array[:, :, pl.ds(at, BORDER)]
        elif sizes.sides == 2:
            edges[0][index] = array[:, :, last:]
            edges[1][index] = array[:, :, :BORDER]


def message_row(sizes, place, level, slot, message, beside):
    start, tiles = slot
    row = get(message, slot)
    if sizes.sides == 1:
        left = place[1] != 0
        tile = beside[0][start + jnp.where(left, tiles - 1, 0)]
        if level > 0:
            reach = BORDER >> level
            lane = lane_at(tile.shape)
            first = jnp.where(left, LANES - reach, 0)
            tile = jnp.where((lane >= first) & (lane < first + reach), tile, 0.0)
        row.append(tile)
    elif sizes.sides == 2:
        right, left = beside[0][start], beside[1][start + tiles - 1]
        if level == 0:
            row += [right, left]
        else:
            reach = BORDER >> level
            lane = lane_at(right.shape)
            row.append(jnp.where(lane < reach, right, jnp.where(lane >= LANES - reach, left, 0.0)))
    return jnp.concatenate(row, axis=1)


def fringe_lanes(shape):
    lane = lane_at(shape)
    return (lane < FRINGE) | (lane >= LANES - FRINGE)


def fringes(sizes, rows):
    total = None
    for index, (level, row) in enumerate(rows):
        tile = row[:, sizes.own[level] * LANES :]
        tile = jnp.where(fringe_lanes(tile.shape), tile, 0.0)
        tile = roll(tile, SPREAD * index + SPREAD // 2, 1)
        total = tile if total is None else total + tile
    return total


def fringed_row(sizes, level, index, message):
    row = get(message, sizes.slots[index])
    if sizes.border[level]:
        if level == 0:
            row += [jnp.zeros(row[0].shape, f32)] * sizes.border[0]
        else:
            tile = roll(message[sizes.tiles], -(SPREAD * (index - 1) + SPREAD // 2), 1)
            row.append(jnp.where(fringe_lanes(tile.shape), tile, 0.0))
    return jnp.concatenate(row, axis=1)


def packing(sizes, count):
    if sizes.sides != 1:
        return False, count, count
    own = -(-count // 2)
    return True, own, own - (-count * (BORDER >> 3) // LANES)


def border_turn(place, goal):
    return jnp.where(place[1] == 0, (goal - LANES // 2) % LANES, (goal + (BORDER >> 3)) % LANES)


def pack_rows(sizes, place, rows, target):
    packed, own, tiles = packing(sizes, len(rows))
    if not packed:
        for index, row in enumerate(rows):
            target[index] = row
        return
    half, reach = LANES // 2, BORDER >> 3
    lane = lane_at(rows[0].shape)
    for index in range(own):
        held = rows[2 * index]
        other = rows[2 * index + 1] if 2 * index + 1 < len(rows) else jnp.zeros(held.shape, f32)
        target[index] = jnp.where(lane < half, held, pltpu.roll(other, half, axis=1))
    for index in range(own, tiles):
        held = jnp.zeros(rows[0].shape, f32)
        some = rows[(index - own) * (LANES // reach) :][: LANES // reach]
        for place_at, row in enumerate(some):
            goal = place_at * reach
            moved = pltpu.roll(row, border_turn(place, goal), axis=1)
            held = jnp.where((lane >= goal) & (lane < goal + reach), moved, held)
        target[index] = held


def unpack_rows(sizes, place, blocks, count):
    packed, own, _ = packing(sizes, count)
    if not packed:
        return [blocks[index] for index in range(count)]
    half, reach = LANES // 2, BORDER >> 3
    rows = []
    for index in range(count):
        held = blocks[index // 2]
        lane = lane_at(held.shape)
        if index % 2:
            held = pltpu.roll(held, half, axis=1)
        at, goal = index // (LANES // reach), index % (LANES // reach) * reach
        back = lax.rem(LANES - border_turn(place, goal), LANES)
        beside = pltpu.roll(blocks[own + at], back, axis=1)
        start = jnp.where(place[1] == 0, half, LANES - reach)
        here = (lane >= start) & (lane < start + reach)
        rows.append(jnp.where(lane < half, held, jnp.where(here, beside, 0.0)))
    return rows


def merge_into(sizes, place, stride, radix, arrays, source, conduct, binding, first):
    position = (place[0] // stride) % radix
    source[...] = jnp.zeros(source.shape, f32)
    for step, array in enumerate(arrays):
        at = (position ^ step) * stride
        rows = unpack_rows(sizes, place, array, 3 * stride + 2)
        for index, row in enumerate(rows[: stride + 2]):
            source[at + index] = source[at + index] + row
        for index in range(stride):
            conduct[at + index + first] = rows[stride + 2 + index]
            binding[at + index] = rows[2 * stride + 2 + index]


def merge_kernel(sizes, stride, radix, place, *refs):
    arrays, out, (source, conduct, binding) = refs[:radix], refs[radix], refs[radix + 1 :]
    merge_into(sizes, place, stride, radix, arrays, source, conduct, binding, 0)
    count = stride * radix
    rows = [source[row] for row in range(count + 2)]
    rows += [conduct[row] for row in range(count)] + [binding[row] for row in range(count)]
    pack_rows(sizes, place, rows, out)


def down_kernel(sizes, place, *refs):
    s = sizes.sides
    owns, turned, refs = refs[:3], refs[3], refs[4:]
    borders0, refs = refs[:s], refs[s:]
    pairs_of = [refs[2 * index : 2 * index + 2] for index in range(1 + s)]
    refs = refs[2 * (1 + s) :]
    from_prev, *beside_prev = (Arrived(place, pair, 0) for pair in pairs_of)
    from_next, *beside_next = (Arrived(place, pair, 1) for pair in pairs_of)
    coefs, contribution, with_far, ups, far, refs = refs[:3], refs[3], refs[4], refs[5:7], refs[7], refs[8:]
    border1, border2, level3, sums = refs
    slots = sizes.slots
    n0, n1, n2 = sizes.rows[:3]

    if s:
        for row in range(2 * n1):
            for side in range(s):
                columns = slice(side * LANES, (side + 1) * LANES)
                at, low = row // n1, 2 * (row % n1)
                sums[row, :, columns] = borders0[side][at, low] + borders0[side][at, low + 1]
        narrow(sizes, place, 0, sums, border1, 2 * n1, "border", sizes.own[0] * LANES)
        for row in range(2 * n2):
            sums[row, :, :LANES] = border1[2 * row] + border1[2 * row + 1]
        narrow(sizes, place, 1, sums, border2, 2 * n2, "border", sizes.own[1] * LANES)

    def held_row(level, at, row):
        if level == 0:
            tiles = [turned[row] if at == 2 else owns[0][at, row], *(array[at, row] for array in borders0)]
        else:
            row = at * sizes.rows[level] + row
            tiles = [owns[level][row], *([(border1, border2)[level - 1][row]] if s else [])]
        return jnp.concatenate(tiles, axis=1)

    def prev_row(level, index):
        return message_row(sizes, place, level, slots[index], from_prev, beside_prev)

    def next_row(level, index):
        return message_row(sizes, place, level, slots[index], from_next, beside_next)

    def conduct0(row):
        if row == 0:
            return prev_row(0, 0)
        if row == n0 + 1:
            return next_row(0, 0)
        return held_row(0, 0, row - 1)

    bound0 = lambda row: held_row(0, 1, row - 1)
    fx, fy, fz, weight, v0 = parts(coefs[0], coefficient_rows(sizes, 0))
    coefficients(sizes, place, 0, n0 + 2, conduct0, bound0, fx, fy, fz, weight)
    for row in range(n0):
        v0[row] = weight[row] * held_row(0, 2, row)
    own_defect(n0 + 2, v0, lambda row: held_row(0, 2, row - 1), bound0, fx, fy, fz, sums, 1)
    smooths, sources = [], []
    for level, first in ((1, 1), (2, 4)):
        n = sizes.rows[level]
        fx, fy, fz, weight, binding, source, smooth = parts(coefs[level], coefficient_rows(sizes, level))
        held = sizes.held[level]
        narrow(sizes, place, level - 1, sums.at[:, :, : sizes.held[level - 1]], source, n + 2)
        binding[0] = prev_row(level, first + 2)
        binding[n + 1] = next_row(level, first + 2)
        for row in range(n):
            binding[row + 1] = held_row(level, 1, row)

        def conduct(row, n=n, level=level, first=first):
            if row < 2:
                return prev_row(level, first + row)
            if row >= n + 2:
                return next_row(level, first + row - n - 2)
            return held_row(level, 0, row - 2)

        bound = lambda row, binding=binding: binding[row - 1]
        coefficients(sizes, place, level, n + 4, conduct, bound, fx, fy, fz, weight)
        for row in range(n + 2):
            smooth[row] = weight[row] * source[row]
        mine = lambda row, source=source: source[row - 1]
        own_defect(n + 4, smooth, mine, bound, fx, fy, fz, sums.at[:, :, :held], 0)
        smooths.append(smooth)
        sources.append(source)
    narrow(sizes, place, 2, sums.at[:, :, : sizes.held[2]], level3, 3)

    for at in (0, 1):
        sums[at, :, : sizes.held[2]] = held_row(2, at, 0) + held_row(2, at, 1)
    narrow(sizes, place, 2, sums.at[:, :, : sizes.held[2]], level3.at[3:5], 2)
    tiles = packing(sizes, 5)[2]
    pack_rows(sizes, place, [level3[row] for row in range(5)], contribution)
    with_far[0:tiles] = contribution[...]
    (s1, s2), (v1, v2) = sources, smooths
    next_rows = (v0[n0 - 1], s1[n1], s1[n1 + 1], v1[n1 - 1], s2[n2], s2[n2 + 1], v2[n2 - 1])
    prev_rows = (v0[0], s1[1], s1[0], v1[2], s2[1], s2[0], v2[2])
    for slot, next_row, prev_row in zip(slots, next_rows, prev_rows):
        put_pair(place, ups, slot, next_row, prev_row)
    if s:
        ends = [fringes(sizes, list(zip((1, 1, 1, 2, 2, 2), rows[1:]))) for rows in (next_rows, prev_rows)]
        put_pair(place, ups, (sizes.tiles, 1), *ends)
    far_tiles = sizes.held[2] // LANES
    put_pair(place, (with_far.at[tiles : tiles + far_tiles], far), (0, far_tiles), v2[n2 + 1], v2[0], 2)


def relax(count, field, refs_of, source, target):
    fx, fy, fz, weight, binding = refs_of

    def update(row, value):
        target(row, field(row) + weight[row - 1] * (source(row) - value))

    sweep(count, field, binding, fx, fy, fz, update)


def store(array, first):
    def put_row(row, value):
        array[row - first] = value

    return put_row


def coarse_kernel(sizes, stride, radix, place, *refs):
    blocks, refs = refs[:radix], refs[radix:]
    out, merged, sums = refs[:3]
    coarse = [refs[3 + 9 * index : 12 + 9 * index] for index in range(3)]
    total = sizes.span_count
    merge_into(sizes, place, stride, radix, blocks, merged, coarse[0][4], coarse[0][5], 1)
    zero = jnp.zeros((sizes.depth, LANES), f32)
    for index in range(3):
        level = 3 + index
        fx, fy, fz, weight, conduct, binding, source, smooth, iterate = coarse[index]
        count = total >> index
        for array in (conduct, smooth, iterate):
            array[0] = zero
            array[count + 1] = zero
        if index == 0:
            source = merged.at[1 : count + 1]
        bound = lambda row, binding=binding: binding[row - 1]
        at_row = lambda row, conduct=conduct: conduct[row]
        coefficients(sizes, place, level, count + 2, at_row, bound, fx, fy, fz, weight)
        for row in range(count):
            smooth[row + 1] = weight[row] * source[row]
        if index < 2:
            conduct_next, binding_next, source_next = coarse[index + 1][4:7]
            half = count // 2
            for row in range(half):
                sums[row, :, :LANES] = conduct[2 * row + 1] + conduct[2 * row + 2]
            narrow(sizes, place, level, sums, conduct_next.at[1 : half + 1], half)
            for row in range(half):
                sums[row, :, :LANES] = binding[2 * row] + binding[2 * row + 1]
            narrow(sizes, place, level, sums, binding_next, half)

            def add(row, value, source=source):
                value = source[row - 1] - value
                slot = (row - 1) // 2
                if row % 2 == 1:
                    sums[slot, :, :LANES] = value
                else:
                    sums[slot, :, :LANES] = sums[slot, :, :LANES] + value

            sweep(count + 2, lambda row, smooth=smooth: smooth[row], bound, fx, fy, fz, add)
            narrow(sizes, place, level, sums, source_next, half)

    fx, fy, fz, weight, conduct, binding, source, smooth, iterate = coarse[2]
    held, other = smooth, iterate
    for _ in range(COARSE_SWEEPS - 1):
        field = lambda row, held=held: held[row]
        mine = lambda row: source[row - 1]
        bound = lambda row: binding[row - 1]
        relax((total >> 2) + 2, field, (fx, fy, fz, weight, bound), mine, store(other, 0))
        held, other = other, held
    for index in (1, 0):
        fx, fy, fz, weight, conduct, binding, source, smooth, iterate = coarse[index]
        if index == 0:
            source = merged.at[1 : total + 1]
        count = total >> index
        widen(sizes, place, 3 + index, held.at[1 : count // 2 + 1], sums, count // 2)
        for row in range(count):
            smooth[row + 1] = smooth[row + 1] + sums[row // 2, :, :LANES]
        field = lambda row, smooth=smooth: smooth[row]
        mine = lambda row, source=source: source[row - 1]
        bound = lambda row, binding=binding: binding[row - 1]
        relax(count + 2, field, (fx, fy, fz, weight, bound), mine, store(iterate, 0))
        held = iterate

    out[...] = held[pl.ds(place[0], 3)]


def up_kernel(sizes, place, coarse, *refs):
    s = sizes.sides
    pair, far_pair, coefs, (own0, turned) = refs[:2], refs[2:4], refs[4:7], refs[7:9]
    from_prev, from_next = (Arrived(place, pair, forward) for forward in (0, 1))
    tiles = packing(sizes, 5)[2]
    far_pair = (far_pair[0].at[tiles : tiles + sizes.held[2] // LANES], far_pair[1])
    fars = [Arrived(place, far_pair, forward, 2) for forward in (0, 1)]
    borders0, out, refs = refs[9 : 9 + s], refs[9 + s], refs[10 + s :]
    total1, total2, result = refs[:3]
    over2, over1, over0, lift2, lift1, lift0, it2, it1, it0, semaphores = refs[3:]
    slots = sizes.slots
    n0, n1, n2 = sizes.rows[:3]
    width = sizes.own[0] * LANES

    widen(sizes, place, 2, coarse, over2, 3)
    for level, array, first, totals, over, lift, target, upper in (
        (2, coefs[2], 4, total2, over2, lift2, it2, over1),
        (1, coefs[1], 1, total1, over1, lift1, it1, over0),
    ):
        n = sizes.rows[level]
        fx, fy, fz, weight, binding, own, smooth = parts(array, coefficient_rows(sizes, level))
        edge = {}
        for row, message, index in (
            (1, from_prev, first),
            (2, from_prev, first + 1),
            (n + 2, from_next, first),
            (n + 1, from_next, first + 1),
        ):
            value = edge.get(row, own[row - 1])
            edge[row] = value + fringed_row(sizes, level, index, message)
        for row, value in edge.items():
            totals[row - 1] = value
        for row in range(n + 4):
            if row in (0, n + 3):
                value = fringed_row(sizes, level, first + 2, from_next if row else from_prev)
                if level == 2:
                    far = fars[1 if row else 0]
                    value = value + jnp.concatenate(get(far, (0, sizes.held[2] // LANES)), axis=1)
            elif row in edge:
                value = weight[row - 1] * totals[row - 1]
            else:
                value = smooth[row - 1]
            lift[row] = value + over[row // 2]
        field = lambda row, lift=lift: lift[row]
        mine = lambda row, own=own, totals=totals, edge=edge: (totals if row in edge else own)[row - 1]
        bound = lambda row, binding=binding: binding[row - 1]
        relax(n + 4, field, (fx, fy, fz, weight, bound), mine, store(target, 1))
        widen(sizes, place, level - 1, target, upper, n + 2)

    def held_row(at, row):
        own = turned[row - 1] if at == 2 else own0[at, row - 1]
        return jnp.concatenate([own, *(array[at, row - 1] for array in borders0)], axis=1)

    fx, fy, fz, weight, v0 = parts(coefs[0], coefficient_rows(sizes, 0))
    lift0[0] = fringed_row(sizes, 0, 0, from_prev) + over0[0]
    lift0[n0 + 1] = fringed_row(sizes, 0, 0, from_next) + over0[n1 + 1]
    for row in range(1, n0 + 1):
        lift0[row] = v0[row - 1] + over0[(row + 1) // 2]
    field = lambda row: lift0[row]
    bound = lambda row: held_row(1, row)
    relax(n0 + 2, field, (fx, fy, fz, weight, bound), lambda row: held_row(2, row), store(it0, 1))
    step = sizes.depth // CHUNKS
    copies = []
    for chunk in range(CHUNKS):
        part = slice(chunk * step, (chunk + 1) * step)
        result[part] = jnp.swapaxes(it0[:, part, :width], 0, 1)
        copies.append(pltpu.make_async_copy(result.at[part], out.at[part], semaphores.at[chunk]))
        copies[-1].start()
    for copy in copies:
        copy.wait()


def call(body, name, micros, outputs, scratch, place, inputs, copies=0, far_out=False):
    near, far = pl.BlockSpec(memory_space=pltpu.VMEM), pl.BlockSpec(memory_space=pl.ANY)
    scratch = [pltpu.VMEM(shape, f32) for shape in scratch]
    if copies:
        scratch.append(pltpu.SemaphoreType.DMA((copies,)))
    return pl.pallas_call(
        body,
        name=name,
        out_shape=[jax.ShapeDtypeStruct(shape, f32) for shape in outputs],
        in_specs=[pl.BlockSpec(memory_space=pltpu.SMEM)] + [near] * len(inputs),
        out_specs=[far if far_out else near] * len(outputs),
        scratch_shapes=scratch,
        cost_estimate=pl.CostEstimate(flops=int(micros * 1.15e9), bytes_accessed=int(micros * BYTES_A_MICRO), transcendentals=0),
        compiler_params=pltpu.CompilerParams(vmem_limit_bytes=VMEM_LIMIT),
    )(place, *inputs)


def along(value, axis, steps):
    count = lax.axis_size(axis)
    initial, last = max(0, -steps), min(count, count - steps)
    return lax.ppermute(value, axis, [(source, source + steps) for source in range(initial, last)])


def beside(values, sizes):
    if sizes.sides == 1:
        return [[lax.ppermute(value, "width", [(0, 1), (1, 0)]) for value in values]]
    if sizes.sides == 2:
        return [[along(value, "width", steps) for value in values] for steps in (-1, 1)]
    return []


def stages(count):
    stride = 1
    while stride < count:
        radix = 4 if count // stride % 4 == 0 else 2
        yield stride, radix
        stride *= radix


def swap(value, stride, radix, others=None):
    count = lax.axis_size("span")
    others = others or {}
    return [value] + [
        lax.ppermute(others.get(step, value), "span", [(device, device ^ step * stride) for device in range(count)])
        for step in range(1, radix)
    ]


def exchange(pair, stride):
    count = lax.axis_size("span")
    routes = [[], []]
    for low in range(count - stride):
        routes[low // stride % 2] += [(low, low + stride), (low + stride, low)]
    return [None if value is None else lax.ppermute(value, "span", route) for value, route in zip(pair, routes)]


def on_device(right_side, diffusivity, reaction):
    depth, extent_x, extent_y = diffusivity.shape
    sizes = Sizes(depth, extent_x, extent_y, lax.axis_size("span"), lax.axis_size("width"))
    place = jnp.stack([lax.axis_index("span"), lax.axis_index("width")]).astype(jnp.int32)
    n0, n1, n2, n3 = sizes.rows
    s = sizes.sides
    tile = (depth, LANES)
    own = [(depth, count * LANES) for count in sizes.own]
    held = [(depth, count) for count in sizes.held]
    down_message = (sizes.tiles, *tile)
    up_message = (sizes.tiles + 1, *tile)
    own0, own1, own2, *to_pairs = call(
        functools.partial(start_kernel, sizes),
        "start",
        1.1,
        [(2, n0, *own[0]), (2 * n1, *own[1]), (2 * n2, *own[2]), down_message, down_message],
        [(2 * n1, *own[0])],
        place,
        [diffusivity, reaction],
    )
    halos = exchange(to_pairs, 1)
    turned, *edges = call(
        functools.partial(turn_kernel, sizes),
        "turn",
        0.7,
        [(n0, *own[0])] + [(3, n0, depth, BORDER)] * s,
        [],
        place,
        [right_side, own0],
    )
    if s == 1:
        borders = [lax.ppermute(edges[0], "width", [(0, 1), (1, 0)])]
    elif s == 2:
        borders = [along(edges[1], "width", -1), along(edges[0], "width", 1)]
    else:
        borders = []
    plan = list(stages(sizes.span_count))
    sides = beside(halos, sizes)

    part = packing(sizes, 5)[2]
    lengths = [sum(coefficient_rows(sizes, level)) for level in range(3)]
    far = (sizes.held[2] // LANES, *tile)
    coefs = [(lengths[level], *held[level]) for level in range(3)]
    downs = call(
        functools.partial(down_kernel, sizes),
        "down",
        3.6,
        [*coefs, (part, *tile), (part + far[0], *tile), up_message, up_message, far],
        [(2 * n1, *tile), (2 * n2, *tile), (5, *tile), (max(2 * n1, n1 + 2), *held[0])],
        place,
        [own0, own1, own2, turned, *borders, *halos, *sum(sides, [])],
    )
    coefs_out, blocks, with_far, ups, far_second = downs[:3], downs[3], downs[4], downs[5:7], downs[7]
    far_rows = None
    for stride, radix in plan[:-1]:
        count = stride * radix
        if far_rows is None:
            blocks = swap(blocks, stride, radix, {2: with_far})
            far_rows = [blocks[2], exchange([None, far_second], 2)[1]]
            blocks, far_rows = lax.optimization_barrier((blocks, far_rows))
        else:
            blocks = swap(blocks, stride, radix)
        (blocks,) = call(
            functools.partial(merge_kernel, sizes, stride, radix),
            "merge",
            0.9,
            [(packing(sizes, 3 * count + 2)[2], *tile)],
            [(count + 2, *tile), (count, *tile), (count, *tile)],
            place,
            blocks,
        )
    stride, radix = plan[-1]
    blocks = swap(blocks, stride, radix)
    received = exchange(ups, 1) + far_rows
    scratch = [(sizes.span_count + 2, *tile), (max(sizes.span_count // 2, 2), *tile)]
    for index in range(3):
        count = sizes.span_count >> index
        scratch += [(count + 1, *tile)] + [(count, *tile)] * 3 + [(count + 2, *tile)] + [(count, *tile)] * 2
        scratch += [(count + 2, *tile)] * 2
    (coarse,) = call(
        functools.partial(coarse_kernel, sizes, stride, radix),
        "coarse",
        2.9,
        [(n3 + 2, *tile)],
        scratch,
        place,
        blocks,
    )
    scratch = [(n1 + 2, *held[1]), (n2 + 2, *held[2]), diffusivity.shape]
    scratch += [(n3 + 2, *held[2]), (n2 + 2, *held[1]), (n1 + 2, *held[0])]
    scratch += [(n2 + 4, *held[2]), (n1 + 4, *held[1]), (n0 + 2, *held[0])]
    scratch += [(n2 + 2, *held[2]), (n1 + 2, *held[1]), (n0, *held[0])]
    (correction,) = call(
        functools.partial(up_kernel, sizes),
        "up",
        3.0,
        [diffusivity.shape],
        scratch,
        place,
        [coarse, *received, *coefs_out, own0, turned, *borders],
        copies=CHUNKS,
        far_out=True,
    )
    return correction


def solution(mesh):
    in_specs = (P(None, "span", "width"),) * 3
    return jax.shard_map(
        on_device, mesh=mesh, in_specs=in_specs, out_specs=P(None, "span", "width"), check_vma=False
    )
```

```python
import functools

import jax
import jax.numpy as jnp
from jax import lax
from jax.experimental import pallas as pl
from jax.experimental.pallas import tpu as pltpu
from jax.sharding import PartitionSpec as P

LEVELS = 6
COARSE_SWEEPS = 3
LANES = 128
BORDER = 128
FRINGE = 4
SPREAD = 16
relax_weight = 0.8
f32 = jnp.float32
VMEM_LIMIT = 32 * 1024 * 1024
BYTES_A_MICRO = 3.69e6
CHUNKS = 4


class Sizes:
    def __init__(self, depth, extent_x, extent_y, span_count, width_count):
        self.depth, self.extent_x, self.extent_y = depth, extent_x, extent_y
        self.span_count, self.width_count = span_count, width_count
        self.sides = min(width_count - 1, 2)
        self.own = [(extent_y >> level) // LANES for level in range(3)]
        self.border = [self.sides, min(self.sides, 1), min(self.sides, 1)]
        self.held = [(self.own[level] + self.border[level]) * LANES for level in range(3)] + [LANES] * 3
        self.rows = [extent_x >> level for level in range(4)]
        self.slots = []
        start = 0
        for level in (0, 1, 1, 1, 2, 2, 2):
            self.slots.append((start, self.own[level]))
            start += self.own[level]
        self.tiles = start
        self.last = list(stages(span_count))[-1][1]


def put(message, slot, row):
    start, tiles = slot
    for tile in range(tiles):
        message[start + tile] = row[:, tile * LANES : (tile + 1) * LANES]


class Arrived:
    def __init__(self, place, pair, forward, stride=1):
        self.even = place[0] // stride % 2 == 0
        self.first, self.second = (pair[0], pair[1]) if forward else (pair[1], pair[0])

    def __getitem__(self, index):
        return jnp.where(self.even, self.first[index], self.second[index])


def put_pair(place, pair, slot, next_row, prev_row, stride=1):
    even = place[0] // stride % 2 == 0
    put(pair[0], slot, jnp.where(even, next_row, prev_row))
    put(pair[1], slot, jnp.where(even, prev_row, next_row))


def get(message, slot):
    start, tiles = slot
    return [message[start + tile] for tile in range(tiles)]


def lane_at(shape):
    return lax.broadcasted_iota(jnp.int32, shape, len(shape) - 1)


def roll(value, steps, axis):
    return pltpu.roll(value, steps % value.shape[axis], axis=axis)


def reciprocal(value):
    return pltpu.reciprocal(value, approx=True)


def harmonic(first, second, guard):
    total = first + second
    if guard:
        total = jnp.maximum(total, 1e-3)
    return (2.0 * first) * second * reciprocal(total)


def split(value):
    high = value.astype(jnp.bfloat16)
    return high, (value - high.astype(f32)).astype(jnp.bfloat16)


def dot(halves, table):
    high, low = halves
    return jnp.dot(high, table, preferred_element_type=f32) + jnp.dot(low, table, preferred_element_type=f32)


def pair_table(fine, fine_dim, turn, weight):
    shape = (fine, LANES) if fine_dim == 0 else (LANES, fine)
    fine_at = lax.broadcasted_iota(jnp.int32, shape, fine_dim)
    coarse_at = lax.broadcasted_iota(jnp.int32, shape, 1 - fine_dim)
    if turn is not None:
        coarse_at = coarse_at - jnp.where(fine_at >= turn, LANES // 2, 0)
    return jnp.where(fine_at // 2 == coarse_at, weight, 0.0).astype(jnp.bfloat16)


def turns(sizes, place, level):
    if sizes.sides == 0:
        return []
    if level == 0:
        return [jnp.where(place[1] == 0, LANES, 0)] if sizes.sides == 1 else [LANES, 0]
    return [LANES // 2]


def transfer_plan(sizes, place, level, part):
    plan = []
    if level >= 3:
        return [((0, LANES), 0, 3 * LANES // 4)]
    if level == 2:
        return [((0, sizes.held[2]), 0, None)]
    own = sizes.own[level]
    if part != "border":
        plan += [((2 * LANES * tile, 2 * LANES * (tile + 1)), tile, None) for tile in range(own // 2)]
    if part != "own":
        for index, turn in enumerate(turns(sizes, place, level)):
            start = (own + index) * LANES
            plan.append(((start, start + LANES), own // 2, turn))
    return plan


def narrow(sizes, place, level, sums, target, rows, part="all", shift=0):
    depth = sums.shape[1]
    done = {}
    for (start, stop), tile, turn in transfer_plan(sizes, place, level, part):
        start, stop, tile = start - shift, stop - shift, tile - shift // (2 * LANES)
        columns = split(sums[0:rows, :, start:stop].reshape(rows * depth, stop - start))
        result = dot(columns, pair_table(stop - start, 0, turn, 0.25)).reshape(rows, depth, LANES)
        done[tile] = done[tile] + result if tile in done else result
    for tile, result in done.items():
        target[0:rows, :, tile * LANES : (tile + 1) * LANES] = result


def widen(sizes, place, level, coarse, target, rows):
    depth = coarse.shape[1]
    for (start, stop), tile, turn in transfer_plan(sizes, place, level, "all"):
        columns = split(coarse[0:rows, :, tile * LANES : (tile + 1) * LANES].reshape(rows * depth, LANES))
        result = dot(columns, pair_table(stop - start, 1, turn, 4.0))
        target[0:rows, :, start:stop] = result.reshape(rows, depth, stop - start)


def coefficients(sizes, place, level, count, conduct, binding, fx, fy, fz, weight):
    guard = level > 0 or sizes.sides > 1
    for row in range(1, count):
        fx[row - 1] = harmonic(conduct(row - 1), conduct(row), guard)
    for row in range(1, count - 1):
        mine = conduct(row)
        south = harmonic(mine, roll(mine, 1, 1), guard)
        if level == 0 and sizes.sides < 2:
            cut = 0 if sizes.sides == 0 else jnp.where(place[1] == 0, 0, sizes.extent_y)
            south = jnp.where(lane_at(mine.shape) == cut, 0.0, south)
        below = harmonic(mine, roll(mine, 1, 0), guard)
        below = jnp.where(lax.broadcasted_iota(jnp.int32, mine.shape, 0) == 0, 0.0, below)
        diagonal = fx[row - 1] + fx[row] + binding(row)
        diagonal = diagonal + (south + roll(south, -1, 1)) + (below + roll(below, -1, 0))
        if guard:
            diagonal = jnp.maximum(diagonal, 1e-6)
        fy[row - 1] = south
        fz[row - 1] = below
        weight[row - 1] = relax_weight * reciprocal(diagonal)


def sweep(count, field, binding, fx, fy, fz, emit):
    lower = fx[0] * (field(1) - field(0))
    for row in range(1, count - 1):
        mine = field(row)
        upper = fx[row] * (field(row + 1) - mine)
        south = fy[row - 1] * (mine - roll(mine, 1, 1))
        below = fz[row - 1] * (mine - roll(mine, 1, 0))
        across = (south - roll(south, -1, 1)) + (below - roll(below, -1, 0))
        emit(row, binding(row) * mine + (lower - upper) + across)
        lower = upper


def own_defect(count, smooth, source, binding, fx, fy, fz, sums, first):
    zero = jnp.zeros(smooth.shape[1:], f32)

    def field(row):
        return smooth[row - 1] if 0 < row < count - 1 else zero

    def add(row, value):
        slot = (row + first) // 2
        if (row + first) % 2 == 0 or row == 0:
            sums[slot] = value
        else:
            sums[slot] = sums[slot] + value

    add(0, fx[0] * field(1))
    sweep(count, field, binding, fx, fy, fz, lambda row, result: add(row, source(row) - result))
    add(count - 1, fx[count - 2] * field(count - 2))


def parts(array, counts):
    views, start = [], 0
    for count in counts:
        views.append(array.at[start : start + count])
        start += count
    return views


def coefficient_rows(sizes, level):
    n = sizes.rows[level]
    if level == 0:
        return [n + 1, n, n, n, n]
    return [n + 3] + [n + 2] * 6


def start_kernel(sizes, place, conduct, binding, own0, own1, own2, first, second, *refs):
    edges, sums = refs[: sizes.sides], refs[-1]
    n0, n1, n2 = sizes.rows[:3]
    for at, array in enumerate((conduct, binding)):
        own0[at] = jnp.swapaxes(array[...], 0, 1)
    for at in (0, 1):
        for row in range(n1):
            sums[at * n1 + row] = own0[at, 2 * row] + own0[at, 2 * row + 1]
    narrow(sizes, place, 0, sums, own1, 2 * n1, "own")
    for row in range(2 * n2):
        sums[row, :, : sizes.own[1] * LANES] = own1[2 * row] + own1[2 * row + 1]
    narrow(sizes, place, 1, sums, own2, 2 * n2, "own")
    ends = []
    for low, at1, at0 in ((n1 - 2, n1 - 1, n0 - 1), (0, 0, 0)):
        edge = n2 - 1 if at0 else 0
        rows = (own0[0, at0], own1[low], own1[low + 1], own1[n1 + at1])
        ends.append(rows + (own2[n2 - 2], own2[n2 - 1], own2[n2 + edge]))
    for slot, next_row, prev_row in zip(sizes.slots, *ends):
        put_pair(place, (first, second), slot, next_row, prev_row)
    for at in (0, 1):
        cut_edges(sizes, place, own0.at[at], [edge.at[at] for edge in edges])


def cut_edges(sizes, place, array, edges):
    last = sizes.extent_y - BORDER
    if sizes.sides == 1:
        at = pl.multiple_of(jnp.where(place[1] == 0, last, 0), LANES)
        edges[0][...] = array[:, :, pl.ds(at, BORDER)]
    elif sizes.sides == 2:
        edges[0][...] = array[:, :, last:]
        edges[1][...] = array[:, :, :BORDER]


def turn_kernel(sizes, place, right_side, turned, *edges):
    turned[...] = jnp.swapaxes(right_side[...], 0, 1)
    cut_edges(sizes, place, turned, edges)


def message_row(sizes, place, level, slot, message, beside):
    start, tiles = slot
    row = get(message, slot)
    if sizes.sides == 1:
        left = place[1] != 0
        tile = beside[0][start + jnp.where(left, tiles - 1, 0)]
        if level > 0:
            reach = BORDER >> level
            lane = lane_at(tile.shape)
            first = jnp.where(left, LANES - reach, 0)
            tile = jnp.where((lane >= first) & (lane < first + reach), tile, 0.0)
        row.append(tile)
    elif sizes.sides == 2:
        right, left = beside[0][start], beside[1][start + tiles - 1]
        if level == 0:
            row += [right, left]
        else:
            reach = BORDER >> level
            lane = lane_at(right.shape)
            row.append(jnp.where(lane < reach, right, jnp.where(lane >= LANES - reach, left, 0.0)))
    return jnp.concatenate(row, axis=1)


def fringe_lanes(shape):
    lane = lane_at(shape)
    return (lane < FRINGE) | (lane >= LANES - FRINGE)


def fringes(sizes, rows):
    total = None
    for index, (level, row) in enumerate(rows):
        tile = row[:, sizes.own[level] * LANES :]
        tile = jnp.where(fringe_lanes(tile.shape), tile, 0.0)
        tile = roll(tile, SPREAD * index + SPREAD // 2, 1)
        total = tile if total is None else total + tile
    return total


def fringed_row(sizes, level, index, message):
    row = get(message, sizes.slots[index])
    if sizes.border[level]:
        if level == 0:
            row += [jnp.zeros(row[0].shape, f32)] * sizes.border[0]
        else:
            tile = roll(message[sizes.tiles], -(SPREAD * (index - 1) + SPREAD // 2), 1)
            row.append(jnp.where(fringe_lanes(tile.shape), tile, 0.0))
    return jnp.concatenate(row, axis=1)


def packing(sizes, count):
    if sizes.sides != 1:
        return False, count, None
    half, reach = LANES // 2, BORDER >> 3
    own = -(-count // 2)
    free = [(own - 1, column) for column in range(half, LANES, reach)] if count % 2 else []
    while len(free) < count:
        free += [(own, column) for column in range(0, LANES, reach)]
        own += 1
    return True, own, free[:count]


def border_turn(place, goal):
    return jnp.where(place[1] == 0, (goal - LANES // 2) % LANES, (goal + (BORDER >> 3)) % LANES)


def pack_rows(sizes, place, rows, target):
    packed, tiles, borders = packing(sizes, len(rows))
    if not packed:
        for index, row in enumerate(rows):
            target[index] = row
        return
    half, reach = LANES // 2, BORDER >> 3
    lane = lane_at(rows[0].shape)
    for index in range(tiles):
        held = jnp.zeros(rows[0].shape, f32)
        if 2 * index < len(rows):
            held = jnp.where(lane < half, rows[2 * index], 0.0)
        if 2 * index + 1 < len(rows):
            held = jnp.where(lane < half, held, pltpu.roll(rows[2 * index + 1], half, axis=1))
        for row, (tile, goal) in zip(rows, borders):
            if tile == index:
                moved = pltpu.roll(row, border_turn(place, goal), axis=1)
                held = jnp.where((lane >= goal) & (lane < goal + reach), moved, held)
        target[index] = held


def unpack_rows(sizes, place, blocks, count):
    packed, _, borders = packing(sizes, count)
    if not packed:
        return [blocks[index] for index in range(count)]
    half, reach = LANES // 2, BORDER >> 3
    rows = []
    for index, (tile, goal) in enumerate(borders):
        held = blocks[index // 2]
        lane = lane_at(held.shape)
        if index % 2:
            held = pltpu.roll(held, half, axis=1)
        back = lax.rem(LANES - border_turn(place, goal), LANES)
        beside = pltpu.roll(blocks[tile], back, axis=1)
        start = jnp.where(place[1] == 0, half, LANES - reach)
        here = (lane >= start) & (lane < start + reach)
        rows.append(jnp.where(lane < half, held, jnp.where(here, beside, 0.0)))
    return rows


def merge_into(sizes, place, stride, radix, arrays, source, tops=None):
    position = (place[0] // stride) % radix
    source[...] = jnp.zeros(source.shape, f32)
    kinds = 0 if tops is None else tops.shape[0]
    for step, array in enumerate(arrays):
        at = (position ^ step) * stride
        rows = unpack_rows(sizes, place, array, stride + 2 + kinds * stride)
        for index, row in enumerate(rows[: stride + 2]):
            source[at + index] = source[at + index] + row
        for kind in range(kinds):
            for index in range(stride):
                tops[kind, at + index] = rows[stride + 2 + kind * stride + index]


def merge_kernel(sizes, stride, radix, final, place, *refs):
    arrays, out, tops, source = refs[:radix], refs[radix], refs[radix + 1], refs[radix + 2]
    merge_into(sizes, place, stride, radix, arrays, source, tops)
    count = stride * radix
    rows = [source[row] for row in range(count + 2)]
    if not final:
        rows += [tops[kind, row] for kind in range(tops.shape[0]) for row in range(count)]
    pack_rows(sizes, place, rows, out)


def top_kernel(sizes, place, own2, *refs):
    s = sizes.sides
    borders0, (border1, border2, top, sums) = refs[:s], refs[s:]
    n1, n2 = sizes.rows[1:3]
    if s:
        for row in range(2 * n1):
            for side in range(s):
                columns = slice(side * LANES, (side + 1) * LANES)
                at, low = row // n1, 2 * (row % n1)
                sums[row, :, columns] = borders0[side][at, low] + borders0[side][at, low + 1]
        narrow(sizes, place, 0, sums, border1, 2 * n1, "border", sizes.own[0] * LANES)
        for row in range(2 * n2):
            sums[row, :, :LANES] = border1[2 * row] + border1[2 * row + 1]
        narrow(sizes, place, 1, sums, border2, 2 * n2, "border", sizes.own[1] * LANES)
    for at in (0, 1):
        row = at * n2
        sums[at, :, :LANES] = own2[row] + own2[row + 1]
        if s:
            sums[at, :, LANES : 2 * LANES] = border2[row] + border2[row + 1]
    narrow(sizes, place, 2, sums, top, 2)


def down_kernel(sizes, place, *refs):
    s = sizes.sides
    owns, turned, refs = refs[:3], refs[3], refs[4:]
    borders0, borders_r, refs = refs[:s], refs[s : 2 * s], refs[2 * s :]
    pairs_of = [refs[2 * index : 2 * index + 2] for index in range(1 + s)]
    refs = refs[2 * (1 + s) :]
    from_prev, *beside_prev = (Arrived(place, pair, 0) for pair in pairs_of)
    from_next, *beside_next = (Arrived(place, pair, 1) for pair in pairs_of)
    (border1, border2), refs = refs[:2], refs[2:]
    tops, refs = refs[: sizes.last], refs[sizes.last :]
    coefs, contribution, with_far, ups, far, refs = refs[:3], refs[3], refs[4], refs[5:7], refs[7], refs[8:]
    level3, sums = refs
    slots = sizes.slots
    n0, n1, n2 = sizes.rows[:3]

    def held_row(level, at, row):
        if level == 0:
            if at == 2:
                tiles = [turned[row], *(array[row] for array in borders_r)]
            else:
                tiles = [owns[0][at, row], *(array[at, row] for array in borders0)]
        else:
            row = at * sizes.rows[level] + row
            tiles = [owns[level][row], *([(border1, border2)[level - 1][row]] if s else [])]
        return jnp.concatenate(tiles, axis=1)

    def prev_row(level, index):
        return message_row(sizes, place, level, slots[index], from_prev, beside_prev)

    def next_row(level, index):
        return message_row(sizes, place, level, slots[index], from_next, beside_next)

    def conduct0(row):
        if row == 0:
            return prev_row(0, 0)
        if row == n0 + 1:
            return next_row(0, 0)
        return held_row(0, 0, row - 1)

    bound0 = lambda row: held_row(0, 1, row - 1)
    fx, fy, fz, weight, v0 = parts(coefs[0], coefficient_rows(sizes, 0))
    coefficients(sizes, place, 0, n0 + 2, conduct0, bound0, fx, fy, fz, weight)
    for row in range(n0):
        v0[row] = weight[row] * held_row(0, 2, row)
    own_defect(n0 + 2, v0, lambda row: held_row(0, 2, row - 1), bound0, fx, fy, fz, sums, 1)
    smooths, sources = [], []
    for level, first in ((1, 1), (2, 4)):
        n = sizes.rows[level]
        fx, fy, fz, weight, binding, source, smooth = parts(coefs[level], coefficient_rows(sizes, level))
        held = sizes.held[level]
        narrow(sizes, place, level - 1, sums.at[:, :, : sizes.held[level - 1]], source, n + 2)
        binding[0] = prev_row(level, first + 2)
        binding[n + 1] = next_row(level, first + 2)
        for row in range(n):
            binding[row + 1] = held_row(level, 1, row)

        def conduct(row, n=n, level=level, first=first):
            if row < 2:
                return prev_row(level, first + row)
            if row >= n + 2:
                return next_row(level, first + row - n - 2)
            return held_row(level, 0, row - 2)

        bound = lambda row, binding=binding: binding[row - 1]
        coefficients(sizes, place, level, n + 4, conduct, bound, fx, fy, fz, weight)
        for row in range(n + 2):
            smooth[row] = weight[row] * source[row]
        mine = lambda row, source=source: source[row - 1]
        own_defect(n + 4, smooth, mine, bound, fx, fy, fz, sums.at[:, :, :held], 0)
        smooths.append(smooth)
        sources.append(source)
    narrow(sizes, place, 2, sums.at[:, :, : sizes.held[2]], level3, 3)

    rows = [level3[row] for row in range(3)] + [top[at] for top in tops for at in (0, 1)]
    tiles = packing(sizes, len(rows))[1]
    pack_rows(sizes, place, rows, contribution)
    with_far[0:tiles] = contribution[...]
    (s1, s2), (v1, v2) = sources, smooths
    next_rows = (v0[n0 - 1], s1[n1], s1[n1 + 1], v1[n1 - 1], s2[n2], s2[n2 + 1], v2[n2 - 1])
    prev_rows = (v0[0], s1[1], s1[0], v1[2], s2[1], s2[0], v2[2])
    for slot, next_row, prev_row in zip(slots, next_rows, prev_rows):
        put_pair(place, ups, slot, next_row, prev_row)
    if s:
        ends = [fringes(sizes, list(zip((1, 1, 1, 2, 2, 2), rows[1:]))) for rows in (next_rows, prev_rows)]
        put_pair(place, ups, (sizes.tiles, 1), *ends)
    far_tiles = sizes.held[2] // LANES
    put_pair(place, (with_far.at[tiles : tiles + far_tiles], far), (0, far_tiles), v2[n2 + 1], v2[0], 2)


def relax(count, field, refs_of, source, target):
    fx, fy, fz, weight, binding = refs_of

    def update(row, value):
        target(row, field(row) + weight[row - 1] * (source(row) - value))

    sweep(count, field, binding, fx, fy, fz, update)


def store(array, first):
    def put_row(row, value):
        array[row - first] = value

    return put_row


def coarse_kernel(sizes, stride, radix, place, *refs):
    blocks, tops, refs = refs[:radix], refs[radix], refs[radix + 1 :]
    out, merged, sums = refs[:3]
    coarse = [refs[3 + 9 * index : 12 + 9 * index] for index in range(3)]
    total = sizes.span_count
    merge_into(sizes, place, stride, radix, blocks, merged)
    position = (place[0] // stride) % radix
    for step in range(radix):
        at = (position ^ step) * stride
        coarse[0][4][pl.ds(at + 1, stride)] = tops[2 * step]
        coarse[0][5][pl.ds(at, stride)] = tops[2 * step + 1]
    zero = jnp.zeros((sizes.depth, LANES), f32)
    for index in range(3):
        level = 3 + index
        fx, fy, fz, weight, conduct, binding, source, smooth, iterate = coarse[index]
        count = total >> index
        for array in (conduct, smooth, iterate):
            array[0] = zero
            array[count + 1] = zero
        if index == 0:
            source = merged.at[1 : count + 1]
        bound = lambda row, binding=binding: binding[row - 1]
        at_row = lambda row, conduct=conduct: conduct[row]
        coefficients(sizes, place, level, count + 2, at_row, bound, fx, fy, fz, weight)
        for row in range(count):
            smooth[row + 1] = weight[row] * source[row]
        if index < 2:
            conduct_next, binding_next, source_next = coarse[index + 1][4:7]
            half = count // 2
            for row in range(half):
                sums[row, :, :LANES] = conduct[2 * row + 1] + conduct[2 * row + 2]
            narrow(sizes, place, level, sums, conduct_next.at[1 : half + 1], half)
            for row in range(half):
                sums[row, :, :LANES] = binding[2 * row] + binding[2 * row + 1]
            narrow(sizes, place, level, sums, binding_next, half)

            def add(row, value, source=source):
                value = source[row - 1] - value
                slot = (row - 1) // 2
                if row % 2 == 1:
                    sums[slot, :, :LANES] = value
                else:
                    sums[slot, :, :LANES] = sums[slot, :, :LANES] + value

            sweep(count + 2, lambda row, smooth=smooth: smooth[row], bound, fx, fy, fz, add)
            narrow(sizes, place, level, sums, source_next, half)

    fx, fy, fz, weight, conduct, binding, source, smooth, iterate = coarse[2]
    held, other = smooth, iterate
    for _ in range(COARSE_SWEEPS - 1):
        field = lambda row, held=held: held[row]
        mine = lambda row: source[row - 1]
        bound = lambda row: binding[row - 1]
        relax((total >> 2) + 2, field, (fx, fy, fz, weight, bound), mine, store(other, 0))
        held, other = other, held
    for index in (1, 0):
        fx, fy, fz, weight, conduct, binding, source, smooth, iterate = coarse[index]
        if index == 0:
            source = merged.at[1 : total + 1]
        count = total >> index
        widen(sizes, place, 3 + index, held.at[1 : count // 2 + 1], sums, count // 2)
        for row in range(count):
            smooth[row + 1] = smooth[row + 1] + sums[row // 2, :, :LANES]
        field = lambda row, smooth=smooth: smooth[row]
        mine = lambda row, source=source: source[row - 1]
        bound = lambda row, binding=binding: binding[row - 1]
        relax(count + 2, field, (fx, fy, fz, weight, bound), mine, store(iterate, 0))
        held = iterate

    out[...] = held[pl.ds(place[0], 3)]


def up_kernel(sizes, place, coarse, *refs):
    s = sizes.sides
    pair, far_pair, coefs, (own0, turned) = refs[:2], refs[2:4], refs[4:7], refs[7:9]
    from_prev, from_next = (Arrived(place, pair, forward) for forward in (0, 1))
    tiles = far_pair[0].shape[0] - sizes.held[2] // LANES
    far_pair = (far_pair[0].at[tiles : tiles + sizes.held[2] // LANES], far_pair[1])
    fars = [Arrived(place, far_pair, forward, 2) for forward in (0, 1)]
    borders0, borders_r, out, refs = refs[9 : 9 + s], refs[9 + s : 9 + 2 * s], refs[9 + 2 * s], refs[10 + 2 * s :]
    total1, total2, result = refs[:3]
    over2, over1, over0, lift2, lift1, lift0, it2, it1, it0, semaphores = refs[3:]
    slots = sizes.slots
    n0, n1, n2 = sizes.rows[:3]
    width = sizes.own[0] * LANES

    widen(sizes, place, 2, coarse, over2, 3)
    for level, array, first, totals, over, lift, target, upper in (
        (2, coefs[2], 4, total2, over2, lift2, it2, over1),
        (1, coefs[1], 1, total1, over1, lift1, it1, over0),
    ):
        n = sizes.rows[level]
        fx, fy, fz, weight, binding, own, smooth = parts(array, coefficient_rows(sizes, level))
        edge = {}
        for row, message, index in (
            (1, from_prev, first),
            (2, from_prev, first + 1),
            (n + 2, from_next, first),
            (n + 1, from_next, first + 1),
        ):
            value = edge.get(row, own[row - 1])
            edge[row] = value + fringed_row(sizes, level, index, message)
        for row, value in edge.items():
            totals[row - 1] = value
        for row in range(n + 4):
            if row in (0, n + 3):
                value = fringed_row(sizes, level, first + 2, from_next if row else from_prev)
                if level == 2:
                    far = fars[1 if row else 0]
                    value = value + jnp.concatenate(get(far, (0, sizes.held[2] // LANES)), axis=1)
            elif row in edge:
                value = weight[row - 1] * totals[row - 1]
            else:
                value = smooth[row - 1]
            lift[row] = value + over[row // 2]
        field = lambda row, lift=lift: lift[row]
        mine = lambda row, own=own, totals=totals, edge=edge: (totals if row in edge else own)[row - 1]
        bound = lambda row, binding=binding: binding[row - 1]
        relax(n + 4, field, (fx, fy, fz, weight, bound), mine, store(target, 1))
        widen(sizes, place, level - 1, target, upper, n + 2)

    def held_row(at, row):
        if at == 2:
            tiles = [turned[row - 1], *(array[row - 1] for array in borders_r)]
        else:
            tiles = [own0[at, row - 1], *(array[at, row - 1] for array in borders0)]
        return jnp.concatenate(tiles, axis=1)

    fx, fy, fz, weight, v0 = parts(coefs[0], coefficient_rows(sizes, 0))
    lift0[0] = fringed_row(sizes, 0, 0, from_prev) + over0[0]
    lift0[n0 + 1] = fringed_row(sizes, 0, 0, from_next) + over0[n1 + 1]
    for row in range(1, n0 + 1):
        lift0[row] = v0[row - 1] + over0[(row + 1) // 2]
    field = lambda row: lift0[row]
    bound = lambda row: held_row(1, row)
    relax(n0 + 2, field, (fx, fy, fz, weight, bound), lambda row: held_row(2, row), store(it0, 1))
    step = sizes.depth // CHUNKS
    copies = []
    for chunk in range(CHUNKS):
        part = slice(chunk * step, (chunk + 1) * step)
        result[part] = jnp.swapaxes(it0[:, part, :width], 0, 1)
        copies.append(pltpu.make_async_copy(result.at[part], out.at[part], semaphores.at[chunk]))
        copies[-1].start()
    for copy in copies:
        copy.wait()


def call(body, name, micros, outputs, scratch, place, inputs, copies=0, far_out=False):
    near, far = pl.BlockSpec(memory_space=pltpu.VMEM), pl.BlockSpec(memory_space=pl.ANY)
    scratch = [pltpu.VMEM(shape, f32) for shape in scratch]
    if copies:
        scratch.append(pltpu.SemaphoreType.DMA((copies,)))
    return pl.pallas_call(
        body,
        name=name,
        out_shape=[jax.ShapeDtypeStruct(shape, f32) for shape in outputs],
        in_specs=[pl.BlockSpec(memory_space=pltpu.SMEM)] + [near] * len(inputs),
        out_specs=[far if far_out else near] * len(outputs),
        scratch_shapes=scratch,
        cost_estimate=pl.CostEstimate(flops=int(micros * 1.15e9), bytes_accessed=int(micros * BYTES_A_MICRO), transcendentals=0),
        compiler_params=pltpu.CompilerParams(vmem_limit_bytes=VMEM_LIMIT),
    )(place, *inputs)


def along(value, axis, steps):
    count = lax.axis_size(axis)
    initial, last = max(0, -steps), min(count, count - steps)
    return lax.ppermute(value, axis, [(source, source + steps) for source in range(initial, last)])


def beside(values, sizes):
    if sizes.sides == 1:
        return [[lax.ppermute(value, "width", [(0, 1), (1, 0)]) for value in values]]
    if sizes.sides == 2:
        return [[along(value, "width", steps) for value in values] for steps in (-1, 1)]
    return []


def edge_columns(edges, sizes):
    if sizes.sides == 1:
        return [lax.ppermute(edges[0], "width", [(0, 1), (1, 0)])]
    if sizes.sides == 2:
        return [along(edges[1], "width", -1), along(edges[0], "width", 1)]
    return []


def stages(count):
    stride = 1
    while stride < count:
        radix = 4 if count // stride % 4 == 0 else 2
        yield stride, radix
        stride *= radix


def swap(value, stride, radix, others=None):
    count = lax.axis_size("span")
    others = others or {}
    return [value] + [
        lax.ppermute(others.get(step, value), "span", [(device, device ^ step * stride) for device in range(count)])
        for step in range(1, radix)
    ]


def exchange(pair, stride):
    count = lax.axis_size("span")
    routes = [[], []]
    for low in range(count - stride):
        routes[low // stride % 2] += [(low, low + stride), (low + stride, low)]
    return [None if value is None else lax.ppermute(value, "span", route) for value, route in zip(pair, routes)]


def on_device(right_side, diffusivity, reaction):
    depth, extent_x, extent_y = diffusivity.shape
    sizes = Sizes(depth, extent_x, extent_y, lax.axis_size("span"), lax.axis_size("width"))
    place = jnp.stack([lax.axis_index("span"), lax.axis_index("width")]).astype(jnp.int32)
    n0, n1, n2, n3 = sizes.rows
    s = sizes.sides
    tile = (depth, LANES)
    own = [(depth, count * LANES) for count in sizes.own]
    held = [(depth, count) for count in sizes.held]
    down_message = (sizes.tiles, *tile)
    up_message = (sizes.tiles + 1, *tile)
    own0, own1, own2, first, second, *edges = call(
        functools.partial(start_kernel, sizes),
        "start",
        1.1,
        [(2, n0, *own[0]), (2 * n1, *own[1]), (2 * n2, *own[2]), down_message, down_message]
        + [(2, n0, depth, BORDER)] * s,
        [(2 * n1, *own[0])],
        place,
        [diffusivity, reaction],
    )
    borders = edge_columns(edges, sizes)
    halos = exchange([first, second], 1)
    turned, *edges = call(
        functools.partial(turn_kernel, sizes),
        "turn",
        0.7,
        [(n0, *own[0])] + [(n0, depth, BORDER)] * s,
        [],
        place,
        [right_side],
    )
    borders_r = edge_columns(edges, sizes)
    plan = list(stages(sizes.span_count))
    border1, border2, top = call(
        functools.partial(top_kernel, sizes),
        "top",
        0.9,
        [(2 * n1, *tile), (2 * n2, *tile), (2, *tile)],
        [(2 * n1, depth, 2 * LANES)],
        place,
        [own2, *borders],
    )
    tops = swap(top, *plan[-1])
    halos, tops, borders_r = lax.optimization_barrier((halos, tops, borders_r))
    sides = beside(halos, sizes)
    part = packing(sizes, 3 + 2 * sizes.last)[1]
    lengths = [sum(coefficient_rows(sizes, level)) for level in range(3)]
    far = (sizes.held[2] // LANES, *tile)
    coefs = [(lengths[level], *held[level]) for level in range(3)]
    downs = call(
        functools.partial(down_kernel, sizes),
        "down",
        3.6,
        [*coefs, (part, *tile), (part + far[0], *tile), up_message, up_message, far],
        [(3, *tile), (n1 + 2, *held[0])],
        place,
        [own0, own1, own2, turned, *borders, *borders_r, *halos, *sum(sides, []), border1, border2, *tops],
    )
    coefs_out, blocks, with_far, ups, far_second = downs[:3], downs[3], downs[4], downs[5:7], downs[7]
    far_first = None
    for stride, radix in plan[:-1]:
        count = stride * radix
        blocks = swap(blocks, stride, radix, None if far_first is not None else {2: with_far})
        far_first = blocks[2] if far_first is None else far_first
        final = (stride, radix) == plan[-2]
        rows = count + 2 + (0 if final else 2 * sizes.last * count)
        blocks, top_rows = call(
            functools.partial(merge_kernel, sizes, stride, radix, final),
            "merge",
            0.9,
            [(packing(sizes, rows)[1], *tile), (2 * sizes.last, count, *tile)],
            [(count + 2, *tile)],
            place,
            blocks,
        )
    stride, radix = plan[-1]
    blocks = swap(blocks, stride, radix)
    received = exchange(ups, 1) + [far_first, exchange([None, far_second], 2)[1]]
    scratch = [(sizes.span_count + 2, *tile), (max(sizes.span_count // 2, 2), *tile)]
    for index in range(3):
        count = sizes.span_count >> index
        scratch += [(count + 1, *tile)] + [(count, *tile)] * 3 + [(count + 2, *tile)] + [(count, *tile)] * 2
        scratch += [(count + 2, *tile)] * 2
    (coarse,) = call(
        functools.partial(coarse_kernel, sizes, stride, radix),
        "coarse",
        2.9,
        [(n3 + 2, *tile)],
        scratch,
        place,
        [*blocks, top_rows],
    )
    scratch = [(n1 + 2, *held[1]), (n2 + 2, *held[2]), diffusivity.shape]
    scratch += [(n3 + 2, *held[2]), (n2 + 2, *held[1]), (n1 + 2, *held[0])]
    scratch += [(n2 + 4, *held[2]), (n1 + 4, *held[1]), (n0 + 2, *held[0])]
    scratch += [(n2 + 2, *held[2]), (n1 + 2, *held[1]), (n0, *held[0])]
    (correction,) = call(
        functools.partial(up_kernel, sizes),
        "up",
        3.0,
        [diffusivity.shape],
        scratch,
        place,
        [coarse, *received, *coefs_out, own0, turned, *borders, *borders_r],
        copies=CHUNKS,
        far_out=True,
    )
    return correction


def solution(mesh):
    in_specs = (P(None, "span", "width"),) * 3
    return jax.shard_map(
        on_device, mesh=mesh, in_specs=in_specs, out_specs=P(None, "span", "width"), check_vma=False
    )
```

```python
import functools

import jax
import jax.numpy as jnp
from jax import lax
from jax.experimental import pallas as pl
from jax.experimental.pallas import tpu as pltpu
from jax.sharding import PartitionSpec as P

LEVELS = 6
COARSE_SWEEPS = 3
LANES = 128
BORDER = 128
FRINGE = 4
SPREAD = 16
relax_weight = 0.8
f32 = jnp.float32
VMEM_LIMIT = 32 * 1024 * 1024
BYTES_A_MICRO = 3.69e6
CHUNKS = 4


class Sizes:
    def __init__(self, depth, extent_x, extent_y, span_count, width_count):
        self.depth, self.extent_x, self.extent_y = depth, extent_x, extent_y
        self.span_count, self.width_count = span_count, width_count
        self.sides = min(width_count - 1, 2)
        self.own = [(extent_y >> level) // LANES for level in range(3)]
        self.border = [self.sides, min(self.sides, 1), min(self.sides, 1)]
        self.held = [(self.own[level] + self.border[level]) * LANES for level in range(3)] + [LANES] * 3
        self.rows = [extent_x >> level for level in range(4)]
        self.slots = []
        start = 0
        for level in (0, 1, 1, 1, 2, 2, 2):
            self.slots.append((start, self.own[level]))
            start += self.own[level]
        self.tiles = start


def put(message, slot, row):
    start, tiles = slot
    for tile in range(tiles):
        message[start + tile] = row[:, tile * LANES : (tile + 1) * LANES]


class Arrived:
    def __init__(self, place, pair, forward, stride=1):
        self.even = place[0] // stride % 2 == 0
        self.first, self.second = (pair[0], pair[1]) if forward else (pair[1], pair[0])

    def __getitem__(self, index):
        return jnp.where(self.even, self.first[index], self.second[index])


def put_pair(place, pair, slot, next_row, prev_row, stride=1):
    even = place[0] // stride % 2 == 0
    put(pair[0], slot, jnp.where(even, next_row, prev_row))
    put(pair[1], slot, jnp.where(even, prev_row, next_row))


def get(message, slot):
    start, tiles = slot
    return [message[start + tile] for tile in range(tiles)]


def lane_at(shape):
    return lax.broadcasted_iota(jnp.int32, shape, len(shape) - 1)


def roll(value, steps, axis):
    return pltpu.roll(value, steps % value.shape[axis], axis=axis)


def reciprocal(value):
    return pltpu.reciprocal(value, approx=True)


def harmonic(first, second, guard):
    total = first + second
    if guard:
        total = jnp.maximum(total, 1e-3)
    return (2.0 * first) * second * reciprocal(total)


def split(value):
    high = value.astype(jnp.bfloat16)
    return high, (value - high.astype(f32)).astype(jnp.bfloat16)


def dot(halves, table):
    high, low = halves
    return jnp.dot(high, table, preferred_element_type=f32) + jnp.dot(low, table, preferred_element_type=f32)


def pair_table(fine, fine_dim, turn, weight):
    shape = (fine, LANES) if fine_dim == 0 else (LANES, fine)
    fine_at = lax.broadcasted_iota(jnp.int32, shape, fine_dim)
    coarse_at = lax.broadcasted_iota(jnp.int32, shape, 1 - fine_dim)
    if turn is not None:
        coarse_at = coarse_at - jnp.where(fine_at >= turn, LANES // 2, 0)
    return jnp.where(fine_at // 2 == coarse_at, weight, 0.0).astype(jnp.bfloat16)


def turns(sizes, place, level):
    if sizes.sides == 0:
        return []
    if level == 0:
        return [jnp.where(place[1] == 0, LANES, 0)] if sizes.sides == 1 else [LANES, 0]
    return [LANES // 2]


def transfer_plan(sizes, place, level, part):
    plan = []
    if level >= 3:
        return [((0, LANES), 0, 3 * LANES // 4)]
    if level == 2:
        return [((0, sizes.held[2]), 0, None)]
    own = sizes.own[level]
    if part != "border":
        plan += [((2 * LANES * tile, 2 * LANES * (tile + 1)), tile, None) for tile in range(own // 2)]
    if part != "own":
        for index, turn in enumerate(turns(sizes, place, level)):
            start = (own + index) * LANES
            plan.append(((start, start + LANES), own // 2, turn))
    return plan


def narrow(sizes, place, level, sums, target, rows, part="all", shift=0):
    depth = sums.shape[1]
    done = {}
    for (start, stop), tile, turn in transfer_plan(sizes, place, level, part):
        start, stop, tile = start - shift, stop - shift, tile - shift // (2 * LANES)
        columns = split(sums[0:rows, :, start:stop].reshape(rows * depth, stop - start))
        result = dot(columns, pair_table(stop - start, 0, turn, 0.25)).reshape(rows, depth, LANES)
        done[tile] = done[tile] + result if tile in done else result
    for tile, result in done.items():
        target[0:rows, :, tile * LANES : (tile + 1) * LANES] = result


def widen(sizes, place, level, coarse, target, rows):
    depth = coarse.shape[1]
    for (start, stop), tile, turn in transfer_plan(sizes, place, level, "all"):
        columns = split(coarse[0:rows, :, tile * LANES : (tile + 1) * LANES].reshape(rows * depth, LANES))
        result = dot(columns, pair_table(stop - start, 1, turn, 4.0))
        target[0:rows, :, start:stop] = result.reshape(rows, depth, stop - start)


def coefficients(sizes, place, level, count, conduct, binding, fx, fy, fz, weight):
    guard = level > 0 or sizes.sides > 1
    for row in range(1, count):
        fx[row - 1] = harmonic(conduct(row - 1), conduct(row), guard)
    for row in range(1, count - 1):
        mine = conduct(row)
        south = harmonic(mine, roll(mine, 1, 1), guard)
        if level == 0 and sizes.sides < 2:
            cut = 0 if sizes.sides == 0 else jnp.where(place[1] == 0, 0, sizes.extent_y)
            south = jnp.where(lane_at(mine.shape) == cut, 0.0, south)
        below = harmonic(mine, roll(mine, 1, 0), guard)
        below = jnp.where(lax.broadcasted_iota(jnp.int32, mine.shape, 0) == 0, 0.0, below)
        diagonal = fx[row - 1] + fx[row] + binding(row)
        diagonal = diagonal + (south + roll(south, -1, 1)) + (below + roll(below, -1, 0))
        if guard:
            diagonal = jnp.maximum(diagonal, 1e-6)
        fy[row - 1] = south
        fz[row - 1] = below
        weight[row - 1] = relax_weight * reciprocal(diagonal)


def sweep(count, field, binding, fx, fy, fz, emit):
    lower = fx[0] * (field(1) - field(0))
    for row in range(1, count - 1):
        mine = field(row)
        upper = fx[row] * (field(row + 1) - mine)
        south = fy[row - 1] * (mine - roll(mine, 1, 1))
        below = fz[row - 1] * (mine - roll(mine, 1, 0))
        across = (south - roll(south, -1, 1)) + (below - roll(below, -1, 0))
        emit(row, binding(row) * mine + (lower - upper) + across)
        lower = upper


def own_defect(count, smooth, source, binding, fx, fy, fz, sums, first):
    zero = jnp.zeros(smooth.shape[1:], f32)

    def field(row):
        return smooth[row - 1] if 0 < row < count - 1 else zero

    def add(row, value):
        slot = (row + first) // 2
        if (row + first) % 2 == 0 or row == 0:
            sums[slot] = value
        else:
            sums[slot] = sums[slot] + value

    add(0, fx[0] * field(1))
    sweep(count, field, binding, fx, fy, fz, lambda row, result: add(row, source(row) - result))
    add(count - 1, fx[count - 2] * field(count - 2))


def parts(array, counts):
    views, start = [], 0
    for count in counts:
        views.append(array.at[start : start + count])
        start += count
    return views


def coefficient_rows(sizes, level):
    n = sizes.rows[level]
    if level == 0:
        return [n + 1, n, n, n, n]
    return [n + 3] + [n + 2] * 6


def start_kernel(sizes, place, conduct, binding, own0, own1, own2, first, second, *refs):
    edges, sums = refs[: sizes.sides], refs[-1]
    n0, n1, n2 = sizes.rows[:3]
    for at, array in enumerate((conduct, binding)):
        own0[at] = jnp.swapaxes(array[...], 0, 1)
    for at in (0, 1):
        for row in range(n1):
            sums[at * n1 + row] = own0[at, 2 * row] + own0[at, 2 * row + 1]
    narrow(sizes, place, 0, sums, own1, 2 * n1, "own")
    for row in range(2 * n2):
        sums[row, :, : sizes.own[1] * LANES] = own1[2 * row] + own1[2 * row + 1]
    narrow(sizes, place, 1, sums, own2, 2 * n2, "own")
    ends = []
    for low, at1, at0 in ((n1 - 2, n1 - 1, n0 - 1), (0, 0, 0)):
        edge = n2 - 1 if at0 else 0
        rows = (own0[0, at0], own1[low], own1[low + 1], own1[n1 + at1])
        ends.append(rows + (own2[n2 - 2], own2[n2 - 1], own2[n2 + edge]))
    for slot, next_row, prev_row in zip(sizes.slots, *ends):
        put_pair(place, (first, second), slot, next_row, prev_row)
    for at in (0, 1):
        cut_edges(sizes, place, own0.at[at], [edge.at[at] for edge in edges])


def cut_edges(sizes, place, array, edges):
    last = sizes.extent_y - BORDER
    if sizes.sides == 1:
        at = pl.multiple_of(jnp.where(place[1] == 0, last, 0), LANES)
        edges[0][...] = array[:, :, pl.ds(at, BORDER)]
    elif sizes.sides == 2:
        edges[0][...] = array[:, :, last:]
        edges[1][...] = array[:, :, :BORDER]


def turn_kernel(sizes, place, right_side, turned, *edges):
    turned[...] = jnp.swapaxes(right_side[...], 0, 1)
    cut_edges(sizes, place, turned, edges)


def message_row(sizes, place, level, slot, message, beside):
    start, tiles = slot
    row = get(message, slot)
    if sizes.sides == 1:
        left = place[1] != 0
        tile = beside[0][start + jnp.where(left, tiles - 1, 0)]
        if level > 0:
            reach = BORDER >> level
            lane = lane_at(tile.shape)
            first = jnp.where(left, LANES - reach, 0)
            tile = jnp.where((lane >= first) & (lane < first + reach), tile, 0.0)
        row.append(tile)
    elif sizes.sides == 2:
        right, left = beside[0][start], beside[1][start + tiles - 1]
        if level == 0:
            row += [right, left]
        else:
            reach = BORDER >> level
            lane = lane_at(right.shape)
            row.append(jnp.where(lane < reach, right, jnp.where(lane >= LANES - reach, left, 0.0)))
    return jnp.concatenate(row, axis=1)


def fringe_lanes(shape):
    lane = lane_at(shape)
    return (lane < FRINGE) | (lane >= LANES - FRINGE)


def fringes(sizes, rows):
    total = None
    for index, (level, row) in enumerate(rows):
        tile = row[:, sizes.own[level] * LANES :]
        tile = jnp.where(fringe_lanes(tile.shape), tile, 0.0)
        tile = roll(tile, SPREAD * index + SPREAD // 2, 1)
        total = tile if total is None else total + tile
    return total


def fringed_row(sizes, level, index, message):
    row = get(message, sizes.slots[index])
    if sizes.border[level]:
        if level == 0:
            row += [jnp.zeros(row[0].shape, f32)] * sizes.border[0]
        else:
            tile = roll(message[sizes.tiles], -(SPREAD * (index - 1) + SPREAD // 2), 1)
            row.append(jnp.where(fringe_lanes(tile.shape), tile, 0.0))
    return jnp.concatenate(row, axis=1)


def packing(sizes, count):
    if sizes.sides != 1:
        return False, count, None
    half, reach = LANES // 2, BORDER >> 3
    own = -(-count // 2)
    free = [(own - 1, column) for column in range(half, LANES, reach)] if count % 2 else []
    while len(free) < count:
        free += [(own, column) for column in range(0, LANES, reach)]
        own += 1
    return True, own, free[:count]


def border_turn(place, goal):
    return jnp.where(place[1] == 0, (goal - LANES // 2) % LANES, (goal + (BORDER >> 3)) % LANES)


def pack_rows(sizes, place, rows, target):
    packed, tiles, borders = packing(sizes, len(rows))
    if not packed:
        for index, row in enumerate(rows):
            target[index] = row
        return
    half, reach = LANES // 2, BORDER >> 3
    lane = lane_at(rows[0].shape)
    for index in range(tiles):
        held = jnp.zeros(rows[0].shape, f32)
        if 2 * index < len(rows):
            held = jnp.where(lane < half, rows[2 * index], 0.0)
        if 2 * index + 1 < len(rows):
            held = jnp.where(lane < half, held, pltpu.roll(rows[2 * index + 1], half, axis=1))
        for row, (tile, goal) in zip(rows, borders):
            if tile == index:
                moved = pltpu.roll(row, border_turn(place, goal), axis=1)
                held = jnp.where((lane >= goal) & (lane < goal + reach), moved, held)
        target[index] = held


def unpack_rows(sizes, place, blocks, count):
    packed, _, borders = packing(sizes, count)
    if not packed:
        return [blocks[index] for index in range(count)]
    half, reach = LANES // 2, BORDER >> 3
    rows = []
    for index, (tile, goal) in enumerate(borders):
        held = blocks[index // 2]
        lane = lane_at(held.shape)
        if index % 2:
            held = pltpu.roll(held, half, axis=1)
        back = lax.rem(LANES - border_turn(place, goal), LANES)
        beside = pltpu.roll(blocks[tile], back, axis=1)
        start = jnp.where(place[1] == 0, half, LANES - reach)
        here = (lane >= start) & (lane < start + reach)
        rows.append(jnp.where(lane < half, held, jnp.where(here, beside, 0.0)))
    return rows


def merge_into(sizes, place, stride, radix, arrays, source, tops):
    position = (place[0] // stride) % radix
    source[...] = jnp.zeros(source.shape, f32)
    for step, array in enumerate(arrays):
        at = (position ^ step) * stride
        rows = unpack_rows(sizes, place, array, 3 * stride + 2)
        for index, row in enumerate(rows[: stride + 2]):
            source[at + index] = source[at + index] + row
        for kind, top in enumerate(tops):
            for index in range(stride):
                top[at + index] = rows[stride + 2 + kind * stride + index]


def merge_kernel(sizes, stride, radix, place, *refs):
    arrays, out, (source, *tops) = refs[:radix], refs[radix], refs[radix + 1 :]
    merge_into(sizes, place, stride, radix, arrays, source, tops)
    pack_rows(sizes, place, [array[row] for array in (source, *tops) for row in range(array.shape[0])], out)


def top_kernel(sizes, place, own2, *refs):
    s = sizes.sides
    borders0, (border1, border2, top, sums) = refs[:s], refs[s:]
    n1, n2 = sizes.rows[1:3]
    if s:
        for row in range(2 * n1):
            for side in range(s):
                columns = slice(side * LANES, (side + 1) * LANES)
                at, low = row // n1, 2 * (row % n1)
                sums[row, :, columns] = borders0[side][at, low] + borders0[side][at, low + 1]
        narrow(sizes, place, 0, sums, border1, 2 * n1, "border", sizes.own[0] * LANES)
        for row in range(2 * n2):
            sums[row, :, :LANES] = border1[2 * row] + border1[2 * row + 1]
        narrow(sizes, place, 1, sums, border2, 2 * n2, "border", sizes.own[1] * LANES)
    for at in (0, 1):
        row = at * n2
        sums[at, :, :LANES] = own2[row] + own2[row + 1]
        if s:
            sums[at, :, LANES : 2 * LANES] = border2[row] + border2[row + 1]
    narrow(sizes, place, 2, sums, top, 2)


def down_kernel(sizes, place, *refs):
    s = sizes.sides
    owns, turned, refs = refs[:3], refs[3], refs[4:]
    borders0, borders_r, refs = refs[:s], refs[s : 2 * s], refs[2 * s :]
    pairs_of = [refs[2 * index : 2 * index + 2] for index in range(1 + s)]
    refs = refs[2 * (1 + s) :]
    from_prev, *beside_prev = (Arrived(place, pair, 0) for pair in pairs_of)
    from_next, *beside_next = (Arrived(place, pair, 1) for pair in pairs_of)
    (border1, border2), refs = refs[:2], refs[2:]
    top, refs = refs[0], refs[1:]
    coefs, contribution, with_far, ups, far, refs = refs[:3], refs[3], refs[4], refs[5:7], refs[7], refs[8:]
    level3, sums = refs
    slots = sizes.slots
    n0, n1, n2 = sizes.rows[:3]

    def held_row(level, at, row):
        if level == 0:
            if at == 2:
                tiles = [turned[row], *(array[row] for array in borders_r)]
            else:
                tiles = [owns[0][at, row], *(array[at, row] for array in borders0)]
        else:
            row = at * sizes.rows[level] + row
            tiles = [owns[level][row], *([(border1, border2)[level - 1][row]] if s else [])]
        return jnp.concatenate(tiles, axis=1)

    def prev_row(level, index):
        return message_row(sizes, place, level, slots[index], from_prev, beside_prev)

    def next_row(level, index):
        return message_row(sizes, place, level, slots[index], from_next, beside_next)

    def conduct0(row):
        if row == 0:
            return prev_row(0, 0)
        if row == n0 + 1:
            return next_row(0, 0)
        return held_row(0, 0, row - 1)

    bound0 = lambda row: held_row(0, 1, row - 1)
    fx, fy, fz, weight, v0 = parts(coefs[0], coefficient_rows(sizes, 0))
    coefficients(sizes, place, 0, n0 + 2, conduct0, bound0, fx, fy, fz, weight)
    for row in range(n0):
        v0[row] = weight[row] * held_row(0, 2, row)
    own_defect(n0 + 2, v0, lambda row: held_row(0, 2, row - 1), bound0, fx, fy, fz, sums, 1)
    smooths, sources = [], []
    for level, first in ((1, 1), (2, 4)):
        n = sizes.rows[level]
        fx, fy, fz, weight, binding, source, smooth = parts(coefs[level], coefficient_rows(sizes, level))
        held = sizes.held[level]
        narrow(sizes, place, level - 1, sums.at[:, :, : sizes.held[level - 1]], source, n + 2)
        binding[0] = prev_row(level, first + 2)
        binding[n + 1] = next_row(level, first + 2)
        for row in range(n):
            binding[row + 1] = held_row(level, 1, row)

        def conduct(row, n=n, level=level, first=first):
            if row < 2:
                return prev_row(level, first + row)
            if row >= n + 2:
                return next_row(level, first + row - n - 2)
            return held_row(level, 0, row - 2)

        bound = lambda row, binding=binding: binding[row - 1]
        coefficients(sizes, place, level, n + 4, conduct, bound, fx, fy, fz, weight)
        for row in range(n + 2):
            smooth[row] = weight[row] * source[row]
        mine = lambda row, source=source: source[row - 1]
        own_defect(n + 4, smooth, mine, bound, fx, fy, fz, sums.at[:, :, :held], 0)
        smooths.append(smooth)
        sources.append(source)
    narrow(sizes, place, 2, sums.at[:, :, : sizes.held[2]], level3, 3)

    rows = [level3[row] for row in range(3)] + [top[0], top[1]]
    tiles = packing(sizes, len(rows))[1]
    pack_rows(sizes, place, rows, contribution)
    with_far[0:tiles] = contribution[...]
    (s1, s2), (v1, v2) = sources, smooths
    next_rows = (v0[n0 - 1], s1[n1], s1[n1 + 1], v1[n1 - 1], s2[n2], s2[n2 + 1], v2[n2 - 1])
    prev_rows = (v0[0], s1[1], s1[0], v1[2], s2[1], s2[0], v2[2])
    for slot, next_row, prev_row in zip(slots, next_rows, prev_rows):
        put_pair(place, ups, slot, next_row, prev_row)
    if s:
        ends = [fringes(sizes, list(zip((1, 1, 1, 2, 2, 2), rows[1:]))) for rows in (next_rows, prev_rows)]
        put_pair(place, ups, (sizes.tiles, 1), *ends)
    far_tiles = sizes.held[2] // LANES
    put_pair(place, (with_far.at[tiles : tiles + far_tiles], far), (0, far_tiles), v2[n2 + 1], v2[0], 2)


def relax(count, field, refs_of, source, target):
    fx, fy, fz, weight, binding = refs_of

    def update(row, value):
        target(row, field(row) + weight[row - 1] * (source(row) - value))

    sweep(count, field, binding, fx, fy, fz, update)


def store(array, first):
    def put_row(row, value):
        array[row - first] = value

    return put_row


def coarse_kernel(sizes, stride, radix, place, *refs):
    blocks, refs = refs[:radix], refs[radix:]
    out, merged, sums = refs[:3]
    coarse = [refs[3 + 9 * index : 12 + 9 * index] for index in range(3)]
    total = sizes.span_count
    merge_into(sizes, place, stride, radix, blocks, merged, (coarse[0][4].at[1 : total + 1], coarse[0][5]))
    zero = jnp.zeros((sizes.depth, LANES), f32)
    for index in range(3):
        level = 3 + index
        fx, fy, fz, weight, conduct, binding, source, smooth, iterate = coarse[index]
        count = total >> index
        for array in (conduct, smooth, iterate):
            array[0] = zero
            array[count + 1] = zero
        if index == 0:
            source = merged.at[1 : count + 1]
        bound = lambda row, binding=binding: binding[row - 1]
        at_row = lambda row, conduct=conduct: conduct[row]
        coefficients(sizes, place, level, count + 2, at_row, bound, fx, fy, fz, weight)
        for row in range(count):
            smooth[row + 1] = weight[row] * source[row]
        if index < 2:
            conduct_next, binding_next, source_next = coarse[index + 1][4:7]
            half = count // 2
            for row in range(half):
                sums[row, :, :LANES] = conduct[2 * row + 1] + conduct[2 * row + 2]
            narrow(sizes, place, level, sums, conduct_next.at[1 : half + 1], half)
            for row in range(half):
                sums[row, :, :LANES] = binding[2 * row] + binding[2 * row + 1]
            narrow(sizes, place, level, sums, binding_next, half)

            def add(row, value, source=source):
                value = source[row - 1] - value
                slot = (row - 1) // 2
                if row % 2 == 1:
                    sums[slot, :, :LANES] = value
                else:
                    sums[slot, :, :LANES] = sums[slot, :, :LANES] + value

            sweep(count + 2, lambda row, smooth=smooth: smooth[row], bound, fx, fy, fz, add)
            narrow(sizes, place, level, sums, source_next, half)

    fx, fy, fz, weight, conduct, binding, source, smooth, iterate = coarse[2]
    held, other = smooth, iterate
    for _ in range(COARSE_SWEEPS - 1):
        field = lambda row, held=held: held[row]
        mine = lambda row: source[row - 1]
        bound = lambda row: binding[row - 1]
        relax((total >> 2) + 2, field, (fx, fy, fz, weight, bound), mine, store(other, 0))
        held, other = other, held
    for index in (1, 0):
        fx, fy, fz, weight, conduct, binding, source, smooth, iterate = coarse[index]
        if index == 0:
            source = merged.at[1 : total + 1]
        count = total >> index
        widen(sizes, place, 3 + index, held.at[1 : count // 2 + 1], sums, count // 2)
        for row in range(count):
            smooth[row + 1] = smooth[row + 1] + sums[row // 2, :, :LANES]
        field = lambda row, smooth=smooth: smooth[row]
        mine = lambda row, source=source: source[row - 1]
        bound = lambda row, binding=binding: binding[row - 1]
        relax(count + 2, field, (fx, fy, fz, weight, bound), mine, store(iterate, 0))
        held = iterate

    out[...] = held[pl.ds(place[0], 3)]


def up_kernel(sizes, place, coarse, *refs):
    s = sizes.sides
    pair, far_pair, coefs, (own0, turned) = refs[:2], refs[2:4], refs[4:7], refs[7:9]
    from_prev, from_next = (Arrived(place, pair, forward) for forward in (0, 1))
    tiles = far_pair[0].shape[0] - sizes.held[2] // LANES
    far_pair = (far_pair[0].at[tiles : tiles + sizes.held[2] // LANES], far_pair[1])
    fars = [Arrived(place, far_pair, forward, 2) for forward in (0, 1)]
    borders0, borders_r, out, refs = refs[9 : 9 + s], refs[9 + s : 9 + 2 * s], refs[9 + 2 * s], refs[10 + 2 * s :]
    total1, total2, result = refs[:3]
    over2, over1, over0, lift2, lift1, lift0, it2, it1, it0, semaphores = refs[3:]
    slots = sizes.slots
    n0, n1, n2 = sizes.rows[:3]
    width = sizes.own[0] * LANES

    widen(sizes, place, 2, coarse, over2, 3)
    for level, array, first, totals, over, lift, target, upper in (
        (2, coefs[2], 4, total2, over2, lift2, it2, over1),
        (1, coefs[1], 1, total1, over1, lift1, it1, over0),
    ):
        n = sizes.rows[level]
        fx, fy, fz, weight, binding, own, smooth = parts(array, coefficient_rows(sizes, level))
        edge = {}
        for row, message, index in (
            (1, from_prev, first),
            (2, from_prev, first + 1),
            (n + 2, from_next, first),
            (n + 1, from_next, first + 1),
        ):
            value = edge.get(row, own[row - 1])
            edge[row] = value + fringed_row(sizes, level, index, message)
        for row, value in edge.items():
            totals[row - 1] = value
        for row in range(n + 4):
            if row in (0, n + 3):
                value = fringed_row(sizes, level, first + 2, from_next if row else from_prev)
                if level == 2:
                    far = fars[1 if row else 0]
                    value = value + jnp.concatenate(get(far, (0, sizes.held[2] // LANES)), axis=1)
            elif row in edge:
                value = weight[row - 1] * totals[row - 1]
            else:
                value = smooth[row - 1]
            lift[row] = value + over[row // 2]
        field = lambda row, lift=lift: lift[row]
        mine = lambda row, own=own, totals=totals, edge=edge: (totals if row in edge else own)[row - 1]
        bound = lambda row, binding=binding: binding[row - 1]
        relax(n + 4, field, (fx, fy, fz, weight, bound), mine, store(target, 1))
        widen(sizes, place, level - 1, target, upper, n + 2)

    def held_row(at, row):
        if at == 2:
            tiles = [turned[row - 1], *(array[row - 1] for array in borders_r)]
        else:
            tiles = [own0[at, row - 1], *(array[at, row - 1] for array in borders0)]
        return jnp.concatenate(tiles, axis=1)

    fx, fy, fz, weight, v0 = parts(coefs[0], coefficient_rows(sizes, 0))
    lift0[0] = fringed_row(sizes, 0, 0, from_prev) + over0[0]
    lift0[n0 + 1] = fringed_row(sizes, 0, 0, from_next) + over0[n1 + 1]
    for row in range(1, n0 + 1):
        lift0[row] = v0[row - 1] + over0[(row + 1) // 2]
    field = lambda row: lift0[row]
    bound = lambda row: held_row(1, row)
    relax(n0 + 2, field, (fx, fy, fz, weight, bound), lambda row: held_row(2, row), store(it0, 1))
    step = sizes.depth // CHUNKS
    copies = []
    for chunk in range(CHUNKS):
        part = slice(chunk * step, (chunk + 1) * step)
        result[part] = jnp.swapaxes(it0[:, part, :width], 0, 1)
        copies.append(pltpu.make_async_copy(result.at[part], out.at[part], semaphores.at[chunk]))
        copies[-1].start()
    for copy in copies:
        copy.wait()


def call(body, name, micros, outputs, scratch, place, inputs, copies=0, far_out=False):
    near, far = pl.BlockSpec(memory_space=pltpu.VMEM), pl.BlockSpec(memory_space=pl.ANY)
    scratch = [pltpu.VMEM(shape, f32) for shape in scratch]
    if copies:
        scratch.append(pltpu.SemaphoreType.DMA((copies,)))
    return pl.pallas_call(
        body,
        name=name,
        out_shape=[jax.ShapeDtypeStruct(shape, f32) for shape in outputs],
        in_specs=[pl.BlockSpec(memory_space=pltpu.SMEM)] + [near] * len(inputs),
        out_specs=[far if far_out else near] * len(outputs),
        scratch_shapes=scratch,
        cost_estimate=pl.CostEstimate(flops=int(micros * 1.15e9), bytes_accessed=int(micros * BYTES_A_MICRO), transcendentals=0),
        compiler_params=pltpu.CompilerParams(vmem_limit_bytes=VMEM_LIMIT),
    )(place, *inputs)


def along(value, axis, steps):
    count = lax.axis_size(axis)
    initial, last = max(0, -steps), min(count, count - steps)
    return lax.ppermute(value, axis, [(source, source + steps) for source in range(initial, last)])


def beside(values, sizes):
    if sizes.sides == 1:
        return [[lax.ppermute(value, "width", [(0, 1), (1, 0)]) for value in values]]
    if sizes.sides == 2:
        return [[along(value, "width", steps) for value in values] for steps in (-1, 1)]
    return []


def edge_columns(edges, sizes):
    if sizes.sides == 1:
        return [lax.ppermute(edges[0], "width", [(0, 1), (1, 0)])]
    if sizes.sides == 2:
        return [along(edges[1], "width", -1), along(edges[0], "width", 1)]
    return []


def stages(count):
    stride = 1
    while stride < count:
        radix = 4 if count // stride % 4 == 0 else 2
        yield stride, radix
        stride *= radix


def swap(value, stride, radix, others=None):
    count = lax.axis_size("span")
    others = others or {}
    return [value] + [
        lax.ppermute(others.get(step, value), "span", [(device, device ^ step * stride) for device in range(count)])
        for step in range(1, radix)
    ]


def exchange(pair, stride):
    count = lax.axis_size("span")
    routes = [[], []]
    for low in range(count - stride):
        routes[low // stride % 2] += [(low, low + stride), (low + stride, low)]
    return [None if value is None else lax.ppermute(value, "span", route) for value, route in zip(pair, routes)]


def on_device(right_side, diffusivity, reaction):
    depth, extent_x, extent_y = diffusivity.shape
    sizes = Sizes(depth, extent_x, extent_y, lax.axis_size("span"), lax.axis_size("width"))
    place = jnp.stack([lax.axis_index("span"), lax.axis_index("width")]).astype(jnp.int32)
    n0, n1, n2, n3 = sizes.rows
    s = sizes.sides
    tile = (depth, LANES)
    own = [(depth, count * LANES) for count in sizes.own]
    held = [(depth, count) for count in sizes.held]
    down_message = (sizes.tiles, *tile)
    up_message = (sizes.tiles + 1, *tile)
    own0, own1, own2, first, second, *edges = call(
        functools.partial(start_kernel, sizes),
        "start",
        1.1,
        [(2, n0, *own[0]), (2 * n1, *own[1]), (2 * n2, *own[2]), down_message, down_message]
        + [(2, n0, depth, BORDER)] * s,
        [(2 * n1, *own[0])],
        place,
        [diffusivity, reaction],
    )
    borders = edge_columns(edges, sizes)
    halos = exchange([first, second], 1)
    turned, *edges = call(
        functools.partial(turn_kernel, sizes),
        "turn",
        0.7,
        [(n0, *own[0])] + [(n0, depth, BORDER)] * s,
        [],
        place,
        [right_side],
    )
    borders_r = edge_columns(edges, sizes)
    plan = list(stages(sizes.span_count))
    border1, border2, top = call(
        functools.partial(top_kernel, sizes),
        "top",
        0.9,
        [(2 * n1, *tile), (2 * n2, *tile), (2, *tile)],
        [(2 * n1, depth, 2 * LANES)],
        place,
        [own2, *borders],
    )
    halos, top, borders_r = lax.optimization_barrier((halos, top, borders_r))
    sides = beside(halos, sizes)
    part = packing(sizes, 5)[1]
    lengths = [sum(coefficient_rows(sizes, level)) for level in range(3)]
    far = (sizes.held[2] // LANES, *tile)
    coefs = [(lengths[level], *held[level]) for level in range(3)]
    downs = call(
        functools.partial(down_kernel, sizes),
        "down",
        3.6,
        [*coefs, (part, *tile), (part + far[0], *tile), up_message, up_message, far],
        [(3, *tile), (n1 + 2, *held[0])],
        place,
        [own0, own1, own2, turned, *borders, *borders_r, *halos, *sum(sides, []), border1, border2, top],
    )
    coefs_out, blocks, with_far, ups, far_second = downs[:3], downs[3], downs[4], downs[5:7], downs[7]
    far_first = None
    for stride, radix in plan[:-1]:
        count = stride * radix
        blocks = swap(blocks, stride, radix, None if far_first is not None else {2: with_far})
        far_first = blocks[2] if far_first is None else far_first
        (blocks,) = call(
            functools.partial(merge_kernel, sizes, stride, radix),
            "merge",
            0.9,
            [(packing(sizes, 3 * count + 2)[1], *tile)],
            [(count + 2, *tile), (count, *tile), (count, *tile)],
            place,
            blocks,
        )
    stride, radix = plan[-1]
    blocks = swap(blocks, stride, radix)
    received = exchange(ups, 1) + [far_first, exchange([None, far_second], 2)[1]]
    scratch = [(sizes.span_count + 2, *tile), (max(sizes.span_count // 2, 2), *tile)]
    for index in range(3):
        count = sizes.span_count >> index
        scratch += [(count + 1, *tile)] + [(count, *tile)] * 3 + [(count + 2, *tile)] + [(count, *tile)] * 2
        scratch += [(count + 2, *tile)] * 2
    (coarse,) = call(
        functools.partial(coarse_kernel, sizes, stride, radix),
        "coarse",
        2.9,
        [(n3 + 2, *tile)],
        scratch,
        place,
        blocks,
    )
    scratch = [(n1 + 2, *held[1]), (n2 + 2, *held[2]), diffusivity.shape]
    scratch += [(n3 + 2, *held[2]), (n2 + 2, *held[1]), (n1 + 2, *held[0])]
    scratch += [(n2 + 4, *held[2]), (n1 + 4, *held[1]), (n0 + 2, *held[0])]
    scratch += [(n2 + 2, *held[2]), (n1 + 2, *held[1]), (n0, *held[0])]
    (correction,) = call(
        functools.partial(up_kernel, sizes),
        "up",
        3.0,
        [diffusivity.shape],
        scratch,
        place,
        [coarse, *received, *coefs_out, own0, turned, *borders, *borders_r],
        copies=CHUNKS,
        far_out=True,
    )
    return correction


def solution(mesh):
    in_specs = (P(None, "span", "width"),) * 3
    return jax.shard_map(
        on_device, mesh=mesh, in_specs=in_specs, out_specs=P(None, "span", "width"), check_vma=False
    )
```

```python
import functools

import jax
import jax.numpy as jnp
from jax import lax
from jax.experimental import pallas as pl
from jax.experimental.pallas import tpu as pltpu
from jax.sharding import PartitionSpec as P

LEVELS = 6
COARSE_SWEEPS = 3
LANES = 128
BORDER = 128
FRINGE = 4
SPREAD = 16
relax_weight = 0.8
f32 = jnp.float32
VMEM_LIMIT = 32 * 1024 * 1024
BYTES_A_MICRO = 3.69e6
CHUNKS = 4


class Sizes:
    def __init__(self, depth, extent_x, extent_y, span_count, width_count):
        self.depth, self.extent_x, self.extent_y = depth, extent_x, extent_y
        self.span_count, self.width_count = span_count, width_count
        self.sides = min(width_count - 1, 2)
        self.own = [(extent_y >> level) // LANES for level in range(3)]
        self.border = [self.sides, min(self.sides, 1), min(self.sides, 1)]
        self.held = [(self.own[level] + self.border[level]) * LANES for level in range(3)] + [LANES] * 3
        self.rows = [extent_x >> level for level in range(4)]
        self.slots = []
        start = 0
        for level in (0, 1, 1, 1, 2, 2, 2):
            self.slots.append((start, self.own[level]))
            start += self.own[level]
        self.tiles = start


def put(message, slot, row):
    start, tiles = slot
    for tile in range(tiles):
        message[start + tile] = row[:, tile * LANES : (tile + 1) * LANES]


class Arrived:
    def __init__(self, place, pair, forward, stride=1):
        self.even = place[0] // stride % 2 == 0
        self.first, self.second = (pair[0], pair[1]) if forward else (pair[1], pair[0])

    def __getitem__(self, index):
        return jnp.where(self.even, self.first[index], self.second[index])


def put_pair(place, pair, slot, next_row, prev_row, stride=1):
    even = place[0] // stride % 2 == 0
    put(pair[0], slot, jnp.where(even, next_row, prev_row))
    put(pair[1], slot, jnp.where(even, prev_row, next_row))


def get(message, slot):
    start, tiles = slot
    return [message[start + tile] for tile in range(tiles)]


def lane_at(shape):
    return lax.broadcasted_iota(jnp.int32, shape, len(shape) - 1)


def roll(value, steps, axis):
    return pltpu.roll(value, steps % value.shape[axis], axis=axis)


def reciprocal(value):
    return pltpu.reciprocal(value, approx=True)


def harmonic(first, second, guard):
    total = first + second
    if guard:
        total = jnp.maximum(total, 1e-3)
    return (2.0 * first) * second * reciprocal(total)


def split(value):
    high = value.astype(jnp.bfloat16)
    return high, (value - high.astype(f32)).astype(jnp.bfloat16)


def dot(halves, table):
    high, low = halves
    return jnp.dot(high, table, preferred_element_type=f32) + jnp.dot(low, table, preferred_element_type=f32)


def pair_table(fine, fine_dim, turn, weight):
    shape = (fine, LANES) if fine_dim == 0 else (LANES, fine)
    fine_at = lax.broadcasted_iota(jnp.int32, shape, fine_dim)
    coarse_at = lax.broadcasted_iota(jnp.int32, shape, 1 - fine_dim)
    if turn is not None:
        coarse_at = coarse_at - jnp.where(fine_at >= turn, LANES // 2, 0)
    return jnp.where(fine_at // 2 == coarse_at, weight, 0.0).astype(jnp.bfloat16)


def turns(sizes, place, level):
    if sizes.sides == 0:
        return []
    if level == 0:
        return [jnp.where(place[1] == 0, LANES, 0)] if sizes.sides == 1 else [LANES, 0]
    return [LANES // 2]


def transfer_plan(sizes, place, level, part):
    plan = []
    if level >= 3:
        return [((0, LANES), 0, 3 * LANES // 4)]
    if level == 2:
        return [((0, sizes.held[2]), 0, None)]
    own = sizes.own[level]
    if part != "border":
        plan += [((2 * LANES * tile, 2 * LANES * (tile + 1)), tile, None) for tile in range(own // 2)]
    if part != "own":
        for index, turn in enumerate(turns(sizes, place, level)):
            start = (own + index) * LANES
            plan.append(((start, start + LANES), own // 2, turn))
    return plan


def narrow(sizes, place, level, sums, target, rows, part="all", shift=0):
    depth = sums.shape[1]
    done = {}
    for (start, stop), tile, turn in transfer_plan(sizes, place, level, part):
        start, stop, tile = start - shift, stop - shift, tile - shift // (2 * LANES)
        columns = split(sums[0:rows, :, start:stop].reshape(rows * depth, stop - start))
        result = dot(columns, pair_table(stop - start, 0, turn, 0.25)).reshape(rows, depth, LANES)
        done[tile] = done[tile] + result if tile in done else result
    for tile, result in done.items():
        target[0:rows, :, tile * LANES : (tile + 1) * LANES] = result


def widen(sizes, place, level, coarse, target, rows):
    depth = coarse.shape[1]
    for (start, stop), tile, turn in transfer_plan(sizes, place, level, "all"):
        columns = split(coarse[0:rows, :, tile * LANES : (tile + 1) * LANES].reshape(rows * depth, LANES))
        result = dot(columns, pair_table(stop - start, 1, turn, 4.0))
        target[0:rows, :, start:stop] = result.reshape(rows, depth, stop - start)


def coefficients(sizes, place, level, count, conduct, binding, fx, fy, fz, weight):
    guard = level > 0 or sizes.sides > 1
    for row in range(1, count):
        fx[row - 1] = harmonic(conduct(row - 1), conduct(row), guard)
    for row in range(1, count - 1):
        mine = conduct(row)
        south = harmonic(mine, roll(mine, 1, 1), guard)
        if level == 0 and sizes.sides < 2:
            cut = 0 if sizes.sides == 0 else jnp.where(place[1] == 0, 0, sizes.extent_y)
            south = jnp.where(lane_at(mine.shape) == cut, 0.0, south)
        below = harmonic(mine, roll(mine, 1, 0), guard)
        below = jnp.where(lax.broadcasted_iota(jnp.int32, mine.shape, 0) == 0, 0.0, below)
        diagonal = fx[row - 1] + fx[row] + binding(row)
        diagonal = diagonal + (south + roll(south, -1, 1)) + (below + roll(below, -1, 0))
        if guard:
            diagonal = jnp.maximum(diagonal, 1e-6)
        fy[row - 1] = south
        fz[row - 1] = below
        weight[row - 1] = relax_weight * reciprocal(diagonal)


def sweep(count, field, binding, fx, fy, fz, emit):
    lower = fx[0] * (field(1) - field(0))
    for row in range(1, count - 1):
        mine = field(row)
        upper = fx[row] * (field(row + 1) - mine)
        south = fy[row - 1] * (mine - roll(mine, 1, 1))
        below = fz[row - 1] * (mine - roll(mine, 1, 0))
        across = (south - roll(south, -1, 1)) + (below - roll(below, -1, 0))
        emit(row, binding(row) * mine + (lower - upper) + across)
        lower = upper


def own_defect(count, smooth, source, binding, fx, fy, fz, sums, first):
    zero = jnp.zeros(smooth.shape[1:], f32)

    def field(row):
        return smooth[row - 1] if 0 < row < count - 1 else zero

    def add(row, value):
        slot = (row + first) // 2
        if (row + first) % 2 == 0 or row == 0:
            sums[slot] = value
        else:
            sums[slot] = sums[slot] + value

    add(0, fx[0] * field(1))
    sweep(count, field, binding, fx, fy, fz, lambda row, result: add(row, source(row) - result))
    add(count - 1, fx[count - 2] * field(count - 2))


def parts(array, counts):
    views, start = [], 0
    for count in counts:
        views.append(array.at[start : start + count])
        start += count
    return views


def coefficient_rows(sizes, level):
    n = sizes.rows[level]
    if level == 0:
        return [n + 1, n, n, n, n]
    return [n + 3] + [n + 2] * 6


def start_kernel(sizes, place, conduct, binding, own0, own1, own2, first, second, top, *refs):
    edges, sums = refs[: sizes.sides], refs[-1]
    n0, n1, n2 = sizes.rows[:3]
    for at, array in enumerate((conduct, binding)):
        own0[at] = jnp.swapaxes(array[...], 0, 1)
    for at in (0, 1):
        for row in range(n1):
            sums[at * n1 + row] = own0[at, 2 * row] + own0[at, 2 * row + 1]
    narrow(sizes, place, 0, sums, own1, 2 * n1, "own")
    for row in range(2 * n2):
        sums[row, :, : sizes.own[1] * LANES] = own1[2 * row] + own1[2 * row + 1]
    narrow(sizes, place, 1, sums, own2, 2 * n2, "own")
    last = jnp.concatenate([own2[0] + own2[1], own2[n2] + own2[n2 + 1]], axis=0)
    last = dot(split(last), pair_table(LANES, 0, None, 0.25))
    top[0] = last[: sizes.depth] + roll(last[sizes.depth :], LANES // 2, 1)
    ends = []
    for low, at1, at0 in ((n1 - 2, n1 - 1, n0 - 1), (0, 0, 0)):
        edge = n2 - 1 if at0 else 0
        rows = (own0[0, at0], own1[low], own1[low + 1], own1[n1 + at1])
        ends.append(rows + (own2[n2 - 2], own2[n2 - 1], own2[n2 + edge]))
    for slot, next_row, prev_row in zip(sizes.slots, *ends):
        put_pair(place, (first, second), slot, next_row, prev_row)
    for at in (0, 1):
        cut_edges(sizes, place, own0.at[at], [edge.at[at] for edge in edges])


def cut_edges(sizes, place, array, edges):
    last = sizes.extent_y - BORDER
    if sizes.sides == 1:
        at = pl.multiple_of(jnp.where(place[1] == 0, last, 0), LANES)
        edges[0][...] = array[:, :, pl.ds(at, BORDER)]
    elif sizes.sides == 2:
        edges[0][...] = array[:, :, last:]
        edges[1][...] = array[:, :, :BORDER]


def turn_kernel(sizes, place, right_side, turned, *edges):
    turned[...] = jnp.swapaxes(right_side[...], 0, 1)
    cut_edges(sizes, place, turned, edges)


def message_row(sizes, place, level, slot, message, beside):
    start, tiles = slot
    row = get(message, slot)
    if sizes.sides == 1:
        left = place[1] != 0
        tile = beside[0][start + jnp.where(left, tiles - 1, 0)]
        if level > 0:
            reach = BORDER >> level
            lane = lane_at(tile.shape)
            first = jnp.where(left, LANES - reach, 0)
            tile = jnp.where((lane >= first) & (lane < first + reach), tile, 0.0)
        row.append(tile)
    elif sizes.sides == 2:
        right, left = beside[0][start], beside[1][start + tiles - 1]
        if level == 0:
            row += [right, left]
        else:
            reach = BORDER >> level
            lane = lane_at(right.shape)
            row.append(jnp.where(lane < reach, right, jnp.where(lane >= LANES - reach, left, 0.0)))
    return jnp.concatenate(row, axis=1)


def fringe_lanes(shape):
    lane = lane_at(shape)
    return (lane < FRINGE) | (lane >= LANES - FRINGE)


def fringes(sizes, rows):
    total = None
    for index, (level, row) in enumerate(rows):
        tile = row[:, sizes.own[level] * LANES :]
        tile = jnp.where(fringe_lanes(tile.shape), tile, 0.0)
        tile = roll(tile, SPREAD * index + SPREAD // 2, 1)
        total = tile if total is None else total + tile
    return total


def fringed_row(sizes, level, index, message):
    row = get(message, sizes.slots[index])
    if sizes.border[level]:
        if level == 0:
            row += [jnp.zeros(row[0].shape, f32)] * sizes.border[0]
        else:
            tile = roll(message[sizes.tiles], -(SPREAD * (index - 1) + SPREAD // 2), 1)
            row.append(jnp.where(fringe_lanes(tile.shape), tile, 0.0))
    return jnp.concatenate(row, axis=1)


def packing(sizes, count):
    if sizes.sides != 1:
        return False, count, None
    half, reach = LANES // 2, BORDER >> 3
    own = -(-count // 2)
    free = [(own - 1, column) for column in range(half, LANES, reach)] if count % 2 else []
    while len(free) < count:
        free += [(own, column) for column in range(0, LANES, reach)]
        own += 1
    return True, own, free[:count]


def border_turn(place, goal):
    return jnp.where(place[1] == 0, (goal - LANES // 2) % LANES, (goal + (BORDER >> 3)) % LANES)


def pack_rows(sizes, place, rows, target):
    packed, tiles, borders = packing(sizes, len(rows))
    if not packed:
        for index, row in enumerate(rows):
            target[index] = row
        return
    half, reach = LANES // 2, BORDER >> 3
    lane = lane_at(rows[0].shape)
    for index in range(tiles):
        held = jnp.zeros(rows[0].shape, f32)
        if 2 * index < len(rows):
            held = jnp.where(lane < half, rows[2 * index], 0.0)
        if 2 * index + 1 < len(rows):
            held = jnp.where(lane < half, held, pltpu.roll(rows[2 * index + 1], half, axis=1))
        for row, (tile, goal) in zip(rows, borders):
            if tile == index:
                moved = pltpu.roll(row, border_turn(place, goal), axis=1)
                held = jnp.where((lane >= goal) & (lane < goal + reach), moved, held)
        target[index] = held


def unpack_rows(sizes, place, blocks, count):
    packed, _, borders = packing(sizes, count)
    if not packed:
        return [blocks[index] for index in range(count)]
    half, reach = LANES // 2, BORDER >> 3
    rows = []
    for index, (tile, goal) in enumerate(borders):
        held = blocks[index // 2]
        lane = lane_at(held.shape)
        if index % 2:
            held = pltpu.roll(held, half, axis=1)
        back = lax.rem(LANES - border_turn(place, goal), LANES)
        beside = pltpu.roll(blocks[tile], back, axis=1)
        start = jnp.where(place[1] == 0, half, LANES - reach)
        here = (lane >= start) & (lane < start + reach)
        rows.append(jnp.where(lane < half, held, jnp.where(here, beside, 0.0)))
    return rows


def merge_into(sizes, place, stride, radix, arrays, source):
    position = (place[0] // stride) % radix
    source[...] = jnp.zeros(source.shape, f32)
    for step, array in enumerate(arrays):
        at = (position ^ step) * stride
        for index, row in enumerate(unpack_rows(sizes, place, array, stride + 2)):
            source[at + index] = source[at + index] + row


def merge_kernel(sizes, stride, radix, place, *refs):
    arrays, out, source = refs[:radix], refs[radix], refs[radix + 1]
    merge_into(sizes, place, stride, radix, arrays, source)
    pack_rows(sizes, place, [source[row] for row in range(source.shape[0])], out)


def top_row(sizes, place, block, beside):
    half, reach = LANES // 2, BORDER >> 3
    lane = lane_at(block.shape)
    values = [jnp.where(lane < half, block, 0.0), jnp.where(lane < half, pltpu.roll(block, half, axis=1), 0.0)]
    for side, other in enumerate(beside):
        first = LANES - reach if side else half
        if sizes.sides == 1:
            first = jnp.where(place[1] == 0, half, LANES - reach)
        here = (lane >= first) & (lane < first + reach)
        values[0] = jnp.where(here, pltpu.roll(other, half, axis=1), values[0])
        values[1] = jnp.where(here, other, values[1])
    return values


def column_kernel(sizes, place, column, *refs):
    beside, out = refs[: sizes.sides], refs[sizes.sides]
    rows = []
    for index in range(column.shape[0]):
        rows += top_row(sizes, place, column[index], [other[index] for other in beside])
    pack_rows(sizes, place, rows, out)


def border_kernel(sizes, place, *refs):
    s = sizes.sides
    borders0, (border1, border2, sums) = refs[:s], refs[s:]
    n1, n2 = sizes.rows[1:3]
    if s:
        for row in range(2 * n1):
            for side in range(s):
                columns = slice(side * LANES, (side + 1) * LANES)
                at, low = row // n1, 2 * (row % n1)
                sums[row, :, columns] = borders0[side][at, low] + borders0[side][at, low + 1]
        narrow(sizes, place, 0, sums, border1, 2 * n1, "border", sizes.own[0] * LANES)
        for row in range(2 * n2):
            sums[row, :, :LANES] = border1[2 * row] + border1[2 * row + 1]
        narrow(sizes, place, 1, sums, border2, 2 * n2, "border", sizes.own[1] * LANES)


def down_kernel(sizes, place, *refs):
    s = sizes.sides
    owns, turned, refs = refs[:3], refs[3], refs[4:]
    borders0, borders_r, refs = refs[:s], refs[s : 2 * s], refs[2 * s :]
    pairs_of = [refs[2 * index : 2 * index + 2] for index in range(1 + s)]
    refs = refs[2 * (1 + s) :]
    from_prev, *beside_prev = (Arrived(place, pair, 0) for pair in pairs_of)
    from_next, *beside_next = (Arrived(place, pair, 1) for pair in pairs_of)
    (border1, border2), refs = refs[:2], refs[2:]
    coefs, contribution, with_far, ups, far, refs = refs[:3], refs[3], refs[4], refs[5:7], refs[7], refs[8:]
    level3, sums = refs
    slots = sizes.slots
    n0, n1, n2 = sizes.rows[:3]

    def held_row(level, at, row):
        if level == 0:
            if at == 2:
                tiles = [turned[row], *(array[row] for array in borders_r)]
            else:
                tiles = [owns[0][at, row], *(array[at, row] for array in borders0)]
        else:
            row = at * sizes.rows[level] + row
            tiles = [owns[level][row], *([(border1, border2)[level - 1][row]] if s else [])]
        return jnp.concatenate(tiles, axis=1)

    def prev_row(level, index):
        return message_row(sizes, place, level, slots[index], from_prev, beside_prev)

    def next_row(level, index):
        return message_row(sizes, place, level, slots[index], from_next, beside_next)

    def conduct0(row):
        if row == 0:
            return prev_row(0, 0)
        if row == n0 + 1:
            return next_row(0, 0)
        return held_row(0, 0, row - 1)

    bound0 = lambda row: held_row(0, 1, row - 1)
    fx, fy, fz, weight, v0 = parts(coefs[0], coefficient_rows(sizes, 0))
    coefficients(sizes, place, 0, n0 + 2, conduct0, bound0, fx, fy, fz, weight)
    for row in range(n0):
        v0[row] = weight[row] * held_row(0, 2, row)
    own_defect(n0 + 2, v0, lambda row: held_row(0, 2, row - 1), bound0, fx, fy, fz, sums, 1)
    smooths, sources = [], []
    for level, first in ((1, 1), (2, 4)):
        n = sizes.rows[level]
        fx, fy, fz, weight, binding, source, smooth = parts(coefs[level], coefficient_rows(sizes, level))
        held = sizes.held[level]
        narrow(sizes, place, level - 1, sums.at[:, :, : sizes.held[level - 1]], source, n + 2)
        binding[0] = prev_row(level, first + 2)
        binding[n + 1] = next_row(level, first + 2)
        for row in range(n):
            binding[row + 1] = held_row(level, 1, row)

        def conduct(row, n=n, level=level, first=first):
            if row < 2:
                return prev_row(level, first + row)
            if row >= n + 2:
                return next_row(level, first + row - n - 2)
            return held_row(level, 0, row - 2)

        bound = lambda row, binding=binding: binding[row - 1]
        coefficients(sizes, place, level, n + 4, conduct, bound, fx, fy, fz, weight)
        for row in range(n + 2):
            smooth[row] = weight[row] * source[row]
        mine = lambda row, source=source: source[row - 1]
        own_defect(n + 4, smooth, mine, bound, fx, fy, fz, sums.at[:, :, :held], 0)
        smooths.append(smooth)
        sources.append(source)
    narrow(sizes, place, 2, sums.at[:, :, : sizes.held[2]], level3, 3)

    tiles = packing(sizes, 3)[1]
    pack_rows(sizes, place, [level3[row] for row in range(3)], contribution)
    with_far[0:tiles] = contribution[...]
    (s1, s2), (v1, v2) = sources, smooths
    next_rows = (v0[n0 - 1], s1[n1], s1[n1 + 1], v1[n1 - 1], s2[n2], s2[n2 + 1], v2[n2 - 1])
    prev_rows = (v0[0], s1[1], s1[0], v1[2], s2[1], s2[0], v2[2])
    for slot, next_row, prev_row in zip(slots, next_rows, prev_rows):
        put_pair(place, ups, slot, next_row, prev_row)
    if s:
        ends = [fringes(sizes, list(zip((1, 1, 1, 2, 2, 2), rows[1:]))) for rows in (next_rows, prev_rows)]
        put_pair(place, ups, (sizes.tiles, 1), *ends)
    far_tiles = sizes.held[2] // LANES
    put_pair(place, (with_far.at[tiles : tiles + far_tiles], far), (0, far_tiles), v2[n2 + 1], v2[0], 2)


def relax(count, field, refs_of, source, target):
    fx, fy, fz, weight, binding = refs_of

    def update(row, value):
        target(row, field(row) + weight[row - 1] * (source(row) - value))

    sweep(count, field, binding, fx, fy, fz, update)


def store(array, first):
    def put_row(row, value):
        array[row - first] = value

    return put_row


def coarse_kernel(sizes, stride, radix, low_stride, place, *refs):
    blocks, refs = refs[:radix], refs[radix:]
    groups, refs = refs[: stride // low_stride], refs[stride // low_stride :]
    out, merged, sums = refs[:3]
    coarse = [refs[3 + 9 * index : 12 + 9 * index] for index in range(3)]
    total = sizes.span_count
    merge_into(sizes, place, stride, radix, blocks, merged)
    tiles = packing(sizes, 2 * radix)[1]
    for step, group in enumerate(groups):
        for low in range(low_stride):
            rows = unpack_rows(sizes, place, group.at[low * tiles : (low + 1) * tiles], 2 * radix)
            for high in range(radix):
                row = place[0] ^ (step * low_stride + low + high * stride)
                coarse[0][4][row + 1] = rows[2 * high]
                coarse[0][5][row] = rows[2 * high + 1]
    zero = jnp.zeros((sizes.depth, LANES), f32)
    for index in range(3):
        level = 3 + index
        fx, fy, fz, weight, conduct, binding, source, smooth, iterate = coarse[index]
        count = total >> index
        for array in (conduct, smooth, iterate):
            array[0] = zero
            array[count + 1] = zero
        if index == 0:
            source = merged.at[1 : count + 1]
        bound = lambda row, binding=binding: binding[row - 1]
        at_row = lambda row, conduct=conduct: conduct[row]
        coefficients(sizes, place, level, count + 2, at_row, bound, fx, fy, fz, weight)
        for row in range(count):
            smooth[row + 1] = weight[row] * source[row]
        if index < 2:
            conduct_next, binding_next, source_next = coarse[index + 1][4:7]
            half = count // 2
            for row in range(half):
                sums[row, :, :LANES] = conduct[2 * row + 1] + conduct[2 * row + 2]
            narrow(sizes, place, level, sums, conduct_next.at[1 : half + 1], half)
            for row in range(half):
                sums[row, :, :LANES] = binding[2 * row] + binding[2 * row + 1]
            narrow(sizes, place, level, sums, binding_next, half)

            def add(row, value, source=source):
                value = source[row - 1] - value
                slot = (row - 1) // 2
                if row % 2 == 1:
                    sums[slot, :, :LANES] = value
                else:
                    sums[slot, :, :LANES] = sums[slot, :, :LANES] + value

            sweep(count + 2, lambda row, smooth=smooth: smooth[row], bound, fx, fy, fz, add)
            narrow(sizes, place, level, sums, source_next, half)

    fx, fy, fz, weight, conduct, binding, source, smooth, iterate = coarse[2]
    held, other = smooth, iterate
    for _ in range(COARSE_SWEEPS - 1):
        field = lambda row, held=held: held[row]
        mine = lambda row: source[row - 1]
        bound = lambda row: binding[row - 1]
        relax((total >> 2) + 2, field, (fx, fy, fz, weight, bound), mine, store(other, 0))
        held, other = other, held
    for index in (1, 0):
        fx, fy, fz, weight, conduct, binding, source, smooth, iterate = coarse[index]
        if index == 0:
            source = merged.at[1 : total + 1]
        count = total >> index
        widen(sizes, place, 3 + index, held.at[1 : count // 2 + 1], sums, count // 2)
        for row in range(count):
            smooth[row + 1] = smooth[row + 1] + sums[row // 2, :, :LANES]
        field = lambda row, smooth=smooth: smooth[row]
        mine = lambda row, source=source: source[row - 1]
        bound = lambda row, binding=binding: binding[row - 1]
        relax(count + 2, field, (fx, fy, fz, weight, bound), mine, store(iterate, 0))
        held = iterate

    out[...] = held[pl.ds(place[0], 3)]


def up_kernel(sizes, place, coarse, *refs):
    s = sizes.sides
    pair, far_pair, coefs, (own0, turned) = refs[:2], refs[2:4], refs[4:7], refs[7:9]
    from_prev, from_next = (Arrived(place, pair, forward) for forward in (0, 1))
    tiles = far_pair[0].shape[0] - sizes.held[2] // LANES
    far_pair = (far_pair[0].at[tiles : tiles + sizes.held[2] // LANES], far_pair[1])
    fars = [Arrived(place, far_pair, forward, 2) for forward in (0, 1)]
    borders0, borders_r, out, refs = refs[9 : 9 + s], refs[9 + s : 9 + 2 * s], refs[9 + 2 * s], refs[10 + 2 * s :]
    total1, total2, result = refs[:3]
    over2, over1, over0, lift2, lift1, lift0, it2, it1, it0, semaphores = refs[3:]
    slots = sizes.slots
    n0, n1, n2 = sizes.rows[:3]
    width = sizes.own[0] * LANES

    widen(sizes, place, 2, coarse, over2, 3)
    for level, array, first, totals, over, lift, target, upper in (
        (2, coefs[2], 4, total2, over2, lift2, it2, over1),
        (1, coefs[1], 1, total1, over1, lift1, it1, over0),
    ):
        n = sizes.rows[level]
        fx, fy, fz, weight, binding, own, smooth = parts(array, coefficient_rows(sizes, level))
        edge = {}
        for row, message, index in (
            (1, from_prev, first),
            (2, from_prev, first + 1),
            (n + 2, from_next, first),
            (n + 1, from_next, first + 1),
        ):
            value = edge.get(row, own[row - 1])
            edge[row] = value + fringed_row(sizes, level, index, message)
        for row, value in edge.items():
            totals[row - 1] = value
        for row in range(n + 4):
            if row in (0, n + 3):
                value = fringed_row(sizes, level, first + 2, from_next if row else from_prev)
                if level == 2:
                    far = fars[1 if row else 0]
                    value = value + jnp.concatenate(get(far, (0, sizes.held[2] // LANES)), axis=1)
            elif row in edge:
                value = weight[row - 1] * totals[row - 1]
            else:
                value = smooth[row - 1]
            lift[row] = value + over[row // 2]
        field = lambda row, lift=lift: lift[row]
        mine = lambda row, own=own, totals=totals, edge=edge: (totals if row in edge else own)[row - 1]
        bound = lambda row, binding=binding: binding[row - 1]
        relax(n + 4, field, (fx, fy, fz, weight, bound), mine, store(target, 1))
        widen(sizes, place, level - 1, target, upper, n + 2)

    def held_row(at, row):
        if at == 2:
            tiles = [turned[row - 1], *(array[row - 1] for array in borders_r)]
        else:
            tiles = [own0[at, row - 1], *(array[at, row - 1] for array in borders0)]
        return jnp.concatenate(tiles, axis=1)

    fx, fy, fz, weight, v0 = parts(coefs[0], coefficient_rows(sizes, 0))
    lift0[0] = fringed_row(sizes, 0, 0, from_prev) + over0[0]
    lift0[n0 + 1] = fringed_row(sizes, 0, 0, from_next) + over0[n1 + 1]
    for row in range(1, n0 + 1):
        lift0[row] = v0[row - 1] + over0[(row + 1) // 2]
    field = lambda row: lift0[row]
    bound = lambda row: held_row(1, row)
    relax(n0 + 2, field, (fx, fy, fz, weight, bound), lambda row: held_row(2, row), store(it0, 1))
    step = sizes.depth // CHUNKS
    copies = []
    for chunk in range(CHUNKS):
        part = slice(chunk * step, (chunk + 1) * step)
        result[part] = jnp.swapaxes(it0[:, part, :width], 0, 1)
        copies.append(pltpu.make_async_copy(result.at[part], out.at[part], semaphores.at[chunk]))
        copies[-1].start()
    for copy in copies:
        copy.wait()


def call(body, name, micros, outputs, scratch, place, inputs, copies=0, far_out=False):
    near, far = pl.BlockSpec(memory_space=pltpu.VMEM), pl.BlockSpec(memory_space=pl.ANY)
    scratch = [pltpu.VMEM(shape, f32) for shape in scratch]
    if copies:
        scratch.append(pltpu.SemaphoreType.DMA((copies,)))
    return pl.pallas_call(
        body,
        name=name,
        out_shape=[jax.ShapeDtypeStruct(shape, f32) for shape in outputs],
        in_specs=[pl.BlockSpec(memory_space=pltpu.SMEM)] + [near] * len(inputs),
        out_specs=[far if far_out else near] * len(outputs),
        scratch_shapes=scratch,
        cost_estimate=pl.CostEstimate(flops=int(micros * 1.15e9), bytes_accessed=int(micros * BYTES_A_MICRO), transcendentals=0),
        compiler_params=pltpu.CompilerParams(vmem_limit_bytes=VMEM_LIMIT),
    )(place, *inputs)


def along(value, axis, steps):
    count = lax.axis_size(axis)
    initial, last = max(0, -steps), min(count, count - steps)
    return lax.ppermute(value, axis, [(source, source + steps) for source in range(initial, last)])


def beside(values, sizes):
    if sizes.sides == 1:
        return [[lax.ppermute(value, "width", [(0, 1), (1, 0)]) for value in values]]
    if sizes.sides == 2:
        return [[along(value, "width", steps) for value in values] for steps in (-1, 1)]
    return []


def edge_columns(edges, sizes):
    if sizes.sides == 1:
        return [lax.ppermute(edges[0], "width", [(0, 1), (1, 0)])]
    if sizes.sides == 2:
        return [along(edges[1], "width", -1), along(edges[0], "width", 1)]
    return []


def stages(count):
    stride = 1
    while stride < count:
        radix = 4 if count // stride % 4 == 0 else 2
        yield stride, radix
        stride *= radix


def swap(value, stride, radix, others=None):
    count = lax.axis_size("span")
    others = others or {}
    return [value] + [
        lax.ppermute(others.get(step, value), "span", [(device, device ^ step * stride) for device in range(count)])
        for step in range(1, radix)
    ]


def exchange(pair, stride):
    count = lax.axis_size("span")
    routes = [[], []]
    for low in range(count - stride):
        routes[low // stride % 2] += [(low, low + stride), (low + stride, low)]
    return [None if value is None else lax.ppermute(value, "span", route) for value, route in zip(pair, routes)]


def on_device(right_side, diffusivity, reaction):
    depth, extent_x, extent_y = diffusivity.shape
    sizes = Sizes(depth, extent_x, extent_y, lax.axis_size("span"), lax.axis_size("width"))
    place = jnp.stack([lax.axis_index("span"), lax.axis_index("width")]).astype(jnp.int32)
    n0, n1, n2, n3 = sizes.rows
    s = sizes.sides
    tile = (depth, LANES)
    own = [(depth, count * LANES) for count in sizes.own]
    held = [(depth, count) for count in sizes.held]
    down_message = (sizes.tiles, *tile)
    up_message = (sizes.tiles + 1, *tile)
    own0, own1, own2, first, second, top, *edges = call(
        functools.partial(start_kernel, sizes),
        "start",
        1.1,
        [(2, n0, *own[0]), (2 * n1, *own[1]), (2 * n2, *own[2]), down_message, down_message, (1, *tile)]
        + [(2, n0, depth, BORDER)] * s,
        [(2 * n1, *own[0])],
        place,
        [diffusivity, reaction],
    )
    borders = edge_columns(edges, sizes)
    plan = list(stages(sizes.span_count))
    column = jnp.concatenate(swap(top, *plan[-1]))
    halos = exchange([first, second], 1)
    turned, *edges = call(
        functools.partial(turn_kernel, sizes),
        "turn",
        0.7,
        [(n0, *own[0])] + [(n0, depth, BORDER)] * s,
        [],
        place,
        [right_side],
    )
    borders_r = edge_columns(edges, sizes)
    border1, border2 = call(
        functools.partial(border_kernel, sizes),
        "border",
        0.8,
        [(2 * n1, *tile), (2 * n2, *tile)],
        [(2 * n1, depth, 2 * LANES)],
        place,
        borders,
    )
    tiles = packing(sizes, 2 * plan[-1][1])[1]
    (packed,) = call(
        functools.partial(column_kernel, sizes),
        "column",
        0.6,
        [(tiles, *tile)],
        [],
        place,
        [column, *(side[0] for side in beside([column], sizes))],
    )
    halos, packed, border1, borders_r = lax.optimization_barrier((halos, packed, border1, borders_r))
    sides = beside(halos, sizes)
    for stride, radix in plan[:-1]:
        groups = swap(packed, stride, radix)
        packed = jnp.concatenate(groups) if (stride, radix) != plan[-2] else packed
    sides, groups = lax.optimization_barrier((sides, groups))
    part = packing(sizes, 3)[1]
    lengths = [sum(coefficient_rows(sizes, level)) for level in range(3)]
    far = (sizes.held[2] // LANES, *tile)
    coefs = [(lengths[level], *held[level]) for level in range(3)]
    downs = call(
        functools.partial(down_kernel, sizes),
        "down",
        3.6,
        [*coefs, (part, *tile), (part + far[0], *tile), up_message, up_message, far],
        [(3, *tile), (n1 + 2, *held[0])],
        place,
        [own0, own1, own2, turned, *borders, *borders_r, *halos, *sum(sides, []), border1, border2],
    )
    coefs_out, blocks, with_far, ups, far_second = downs[:3], downs[3], downs[4], list(downs[5:7]), downs[7]
    far_first = None
    for stride, radix in plan[:-1]:
        count = stride * radix
        blocks = swap(blocks, stride, radix, None if far_first is not None else {2: with_far})
        if far_first is None:
            far_first = blocks[2]
            blocks, ups[0] = lax.optimization_barrier((blocks, ups[0]))
        (blocks,) = call(
            functools.partial(merge_kernel, sizes, stride, radix),
            "merge",
            0.9,
            [(packing(sizes, count + 2)[1], *tile)],
            [(count + 2, *tile)],
            place,
            blocks,
        )
    stride, radix = plan[-1]
    blocks = swap(blocks, stride, radix)
    received = exchange(ups, 1) + [far_first, exchange([None, far_second], 2)[1]]
    blocks, received[0] = lax.optimization_barrier((blocks, received[0]))
    scratch = [(sizes.span_count + 2, *tile), (max(sizes.span_count // 2, 2), *tile)]
    for index in range(3):
        count = sizes.span_count >> index
        scratch += [(count + 1, *tile)] + [(count, *tile)] * 3 + [(count + 2, *tile)] + [(count, *tile)] * 2
        scratch += [(count + 2, *tile)] * 2
    (coarse,) = call(
        functools.partial(coarse_kernel, sizes, stride, radix, plan[-2][0]),
        "coarse",
        2.9,
        [(n3 + 2, *tile)],
        scratch,
        place,
        [*blocks, *groups],
    )
    scratch = [(n1 + 2, *held[1]), (n2 + 2, *held[2]), diffusivity.shape]
    scratch += [(n3 + 2, *held[2]), (n2 + 2, *held[1]), (n1 + 2, *held[0])]
    scratch += [(n2 + 4, *held[2]), (n1 + 4, *held[1]), (n0 + 2, *held[0])]
    scratch += [(n2 + 2, *held[2]), (n1 + 2, *held[1]), (n0, *held[0])]
    (correction,) = call(
        functools.partial(up_kernel, sizes),
        "up",
        3.0,
        [diffusivity.shape],
        scratch,
        place,
        [coarse, *received, *coefs_out, own0, turned, *borders, *borders_r],
        copies=CHUNKS,
        far_out=True,
    )
    return correction


def solution(mesh):
    in_specs = (P(None, "span", "width"),) * 3
    return jax.shard_map(
        on_device, mesh=mesh, in_specs=in_specs, out_specs=P(None, "span", "width"), check_vma=False
    )
```

```python
import functools

import jax
import jax.numpy as jnp
from jax import lax
from jax.experimental import pallas as pl
from jax.experimental.pallas import tpu as pltpu
from jax.sharding import PartitionSpec as P

LEVELS = 6
COARSE_SWEEPS = 3
LANES = 128
BORDER = 128
FRINGE = 4
SPREAD = 16
relax_weight = 0.8
f32 = jnp.float32
VMEM_LIMIT = 32 * 1024 * 1024
BYTES_A_MICRO = 3.69e6
CHUNKS = 4


class Sizes:
    def __init__(self, depth, extent_x, extent_y, span_count, width_count):
        self.depth, self.extent_x, self.extent_y = depth, extent_x, extent_y
        self.span_count, self.width_count = span_count, width_count
        self.sides = min(width_count - 1, 2)
        self.own = [(extent_y >> level) // LANES for level in range(3)]
        self.border = [self.sides, min(self.sides, 1), min(self.sides, 1)]
        self.held = [(self.own[level] + self.border[level]) * LANES for level in range(3)] + [LANES] * 3
        self.rows = [extent_x >> level for level in range(4)]
        self.slots = []
        start = 0
        for level in (0, 1, 1, 1, 2, 2, 2):
            self.slots.append((start, self.own[level]))
            start += self.own[level]
        self.tiles = start


def put(message, slot, row):
    start, tiles = slot
    for tile in range(tiles):
        message[start + tile] = row[:, tile * LANES : (tile + 1) * LANES]


class Arrived:
    def __init__(self, place, pair, forward, stride=1):
        self.even = place[0] // stride % 2 == 0
        self.first, self.second = (pair[0], pair[1]) if forward else (pair[1], pair[0])

    def __getitem__(self, index):
        return jnp.where(self.even, self.first[index], self.second[index])


def put_pair(place, pair, slot, next_row, prev_row, stride=1):
    even = place[0] // stride % 2 == 0
    put(pair[0], slot, jnp.where(even, next_row, prev_row))
    put(pair[1], slot, jnp.where(even, prev_row, next_row))


def get(message, slot):
    start, tiles = slot
    return [message[start + tile] for tile in range(tiles)]


def lane_at(shape):
    return lax.broadcasted_iota(jnp.int32, shape, len(shape) - 1)


def roll(value, steps, axis):
    return pltpu.roll(value, steps % value.shape[axis], axis=axis)


def reciprocal(value):
    return pltpu.reciprocal(value, approx=True)


def harmonic(first, second, guard):
    total = first + second
    if guard:
        total = jnp.maximum(total, 1e-3)
    return (2.0 * first) * second * reciprocal(total)


def split(value):
    high = value.astype(jnp.bfloat16)
    return high, (value - high.astype(f32)).astype(jnp.bfloat16)


def dot(halves, table):
    high, low = halves
    return jnp.dot(high, table, preferred_element_type=f32) + jnp.dot(low, table, preferred_element_type=f32)


def pair_table(fine, fine_dim, turn, weight):
    shape = (fine, LANES) if fine_dim == 0 else (LANES, fine)
    fine_at = lax.broadcasted_iota(jnp.int32, shape, fine_dim)
    coarse_at = lax.broadcasted_iota(jnp.int32, shape, 1 - fine_dim)
    if turn is not None:
        coarse_at = coarse_at - jnp.where(fine_at >= turn, LANES // 2, 0)
    return jnp.where(fine_at // 2 == coarse_at, weight, 0.0).astype(jnp.bfloat16)


def turns(sizes, place, level):
    if sizes.sides == 0:
        return []
    if level == 0:
        return [jnp.where(place[1] == 0, LANES, 0)] if sizes.sides == 1 else [LANES, 0]
    return [LANES // 2]


def transfer_plan(sizes, place, level, part):
    plan = []
    if level >= 3:
        return [((0, LANES), 0, 3 * LANES // 4)]
    if level == 2:
        return [((0, sizes.held[2]), 0, None)]
    own = sizes.own[level]
    if part != "border":
        plan += [((2 * LANES * tile, 2 * LANES * (tile + 1)), tile, None) for tile in range(own // 2)]
    if part != "own":
        for index, turn in enumerate(turns(sizes, place, level)):
            start = (own + index) * LANES
            plan.append(((start, start + LANES), own // 2, turn))
    return plan


def narrow(sizes, place, level, sums, target, rows, part="all", shift=0):
    depth = sums.shape[1]
    done = {}
    for (start, stop), tile, turn in transfer_plan(sizes, place, level, part):
        start, stop, tile = start - shift, stop - shift, tile - shift // (2 * LANES)
        columns = split(sums[0:rows, :, start:stop].reshape(rows * depth, stop - start))
        result = dot(columns, pair_table(stop - start, 0, turn, 0.25)).reshape(rows, depth, LANES)
        done[tile] = done[tile] + result if tile in done else result
    for tile, result in done.items():
        target[0:rows, :, tile * LANES : (tile + 1) * LANES] = result


def widen(sizes, place, level, coarse, target, rows):
    depth = coarse.shape[1]
    for (start, stop), tile, turn in transfer_plan(sizes, place, level, "all"):
        columns = split(coarse[0:rows, :, tile * LANES : (tile + 1) * LANES].reshape(rows * depth, LANES))
        result = dot(columns, pair_table(stop - start, 1, turn, 4.0))
        target[0:rows, :, start:stop] = result.reshape(rows, depth, stop - start)


def coefficients(sizes, place, level, count, conduct, binding, fx, fy, fz, weight):
    guard = level > 0 or sizes.sides > 1
    for row in range(1, count):
        fx[row - 1] = harmonic(conduct(row - 1), conduct(row), guard)
    for row in range(1, count - 1):
        mine = conduct(row)
        south = harmonic(mine, roll(mine, 1, 1), guard)
        if level == 0 and sizes.sides < 2:
            cut = 0 if sizes.sides == 0 else jnp.where(place[1] == 0, 0, sizes.extent_y)
            south = jnp.where(lane_at(mine.shape) == cut, 0.0, south)
        below = harmonic(mine, roll(mine, 1, 0), guard)
        below = jnp.where(lax.broadcasted_iota(jnp.int32, mine.shape, 0) == 0, 0.0, below)
        diagonal = fx[row - 1] + fx[row] + binding(row)
        diagonal = diagonal + (south + roll(south, -1, 1)) + (below + roll(below, -1, 0))
        if guard:
            diagonal = jnp.maximum(diagonal, 1e-6)
        fy[row - 1] = south
        fz[row - 1] = below
        weight[row - 1] = relax_weight * reciprocal(diagonal)


def sweep(count, field, binding, fx, fy, fz, emit):
    lower = fx[0] * (field(1) - field(0))
    for row in range(1, count - 1):
        mine = field(row)
        upper = fx[row] * (field(row + 1) - mine)
        south = fy[row - 1] * (mine - roll(mine, 1, 1))
        below = fz[row - 1] * (mine - roll(mine, 1, 0))
        across = (south - roll(south, -1, 1)) + (below - roll(below, -1, 0))
        emit(row, binding(row) * mine + (lower - upper) + across)
        lower = upper


def own_defect(count, smooth, source, binding, fx, fy, fz, sums, first):
    zero = jnp.zeros(smooth.shape[1:], f32)

    def field(row):
        return smooth[row - 1] if 0 < row < count - 1 else zero

    def add(row, value):
        slot = (row + first) // 2
        if (row + first) % 2 == 0 or row == 0:
            sums[slot] = value
        else:
            sums[slot] = sums[slot] + value

    add(0, fx[0] * field(1))
    sweep(count, field, binding, fx, fy, fz, lambda row, result: add(row, source(row) - result))
    add(count - 1, fx[count - 2] * field(count - 2))


def parts(array, counts):
    views, start = [], 0
    for count in counts:
        views.append(array.at[start : start + count])
        start += count
    return views


def coefficient_rows(sizes, level):
    n = sizes.rows[level]
    if level == 0:
        return [n + 1, n, n, n, n]
    return [n + 3] + [n + 2] * 6


def start_kernel(sizes, place, conduct, binding, own0, own1, own2, first, second, sums):
    n0, n1, n2 = sizes.rows[:3]
    for at, array in enumerate((conduct, binding)):
        own0[at] = jnp.swapaxes(array[...], 0, 1)
    for at in (0, 1):
        for row in range(n1):
            sums[at * n1 + row] = own0[at, 2 * row] + own0[at, 2 * row + 1]
    narrow(sizes, place, 0, sums, own1, 2 * n1, "own")
    for row in range(2 * n2):
        sums[row, :, : sizes.own[1] * LANES] = own1[2 * row] + own1[2 * row + 1]
    narrow(sizes, place, 1, sums, own2, 2 * n2, "own")
    ends = []
    for low, at1, at0 in ((n1 - 2, n1 - 1, n0 - 1), (0, 0, 0)):
        edge = n2 - 1 if at0 else 0
        rows = (own0[0, at0], own1[low], own1[low + 1], own1[n1 + at1])
        ends.append(rows + (own2[n2 - 2], own2[n2 - 1], own2[n2 + edge]))
    for slot, next_row, prev_row in zip(sizes.slots, *ends):
        put_pair(place, (first, second), slot, next_row, prev_row)


def turn_kernel(sizes, place, right_side, own0, turned, *edges):
    turned[...] = jnp.swapaxes(right_side[...], 0, 1)
    last = sizes.extent_y - BORDER
    for index, array in enumerate((own0.at[0], own0.at[1], turned)):
        if sizes.sides == 1:
            at = pl.multiple_of(jnp.where(place[1] == 0, last, 0), LANES)
            edges[0][index] = array[:, :, pl.ds(at, BORDER)]
        elif sizes.sides == 2:
            edges[0][index] = array[:, :, last:]
            edges[1][index] = array[:, :, :BORDER]


def message_row(sizes, place, level, slot, message, beside):
    start, tiles = slot
    row = get(message, slot)
    if sizes.sides == 1:
        left = place[1] != 0
        tile = beside[0][start + jnp.where(left, tiles - 1, 0)]
        if level > 0:
            reach = BORDER >> level
            lane = lane_at(tile.shape)
            first = jnp.where(left, LANES - reach, 0)
            tile = jnp.where((lane >= first) & (lane < first + reach), tile, 0.0)
        row.append(tile)
    elif sizes.sides == 2:
        right, left = beside[0][start], beside[1][start + tiles - 1]
        if level == 0:
            row += [right, left]
        else:
            reach = BORDER >> level
            lane = lane_at(right.shape)
            row.append(jnp.where(lane < reach, right, jnp.where(lane >= LANES - reach, left, 0.0)))
    return jnp.concatenate(row, axis=1)


def fringe_lanes(shape):
    lane = lane_at(shape)
    return (lane < FRINGE) | (lane >= LANES - FRINGE)


def fringes(sizes, rows):
    total = None
    for index, (level, row) in enumerate(rows):
        tile = row[:, sizes.own[level] * LANES :]
        tile = jnp.where(fringe_lanes(tile.shape), tile, 0.0)
        tile = roll(tile, SPREAD * index + SPREAD // 2, 1)
        total = tile if total is None else total + tile
    return total


def fringed_row(sizes, level, index, message):
    row = get(message, sizes.slots[index])
    if sizes.border[level]:
        if level == 0:
            row += [jnp.zeros(row[0].shape, f32)] * sizes.border[0]
        else:
            tile = roll(message[sizes.tiles], -(SPREAD * (index - 1) + SPREAD // 2), 1)
            row.append(jnp.where(fringe_lanes(tile.shape), tile, 0.0))
    return jnp.concatenate(row, axis=1)


def packing(sizes, count):
    if sizes.sides != 1:
        return False, count, count
    own = -(-count // 2)
    return True, own, own - (-count * (BORDER >> 3) // LANES)


def border_turn(place, goal):
    return jnp.where(place[1] == 0, (goal - LANES // 2) % LANES, (goal + (BORDER >> 3)) % LANES)


def pack_rows(sizes, place, rows, target):
    packed, own, tiles = packing(sizes, len(rows))
    if not packed:
        for index, row in enumerate(rows):
            target[index] = row
        return
    half, reach = LANES // 2, BORDER >> 3
    lane = lane_at(rows[0].shape)
    for index in range(own):
        held = rows[2 * index]
        other = rows[2 * index + 1] if 2 * index + 1 < len(rows) else jnp.zeros(held.shape, f32)
        target[index] = jnp.where(lane < half, held, pltpu.roll(other, half, axis=1))
    for index in range(own, tiles):
        held = jnp.zeros(rows[0].shape, f32)
        some = rows[(index - own) * (LANES // reach) :][: LANES // reach]
        for place_at, row in enumerate(some):
            goal = place_at * reach
            moved = pltpu.roll(row, border_turn(place, goal), axis=1)
            held = jnp.where((lane >= goal) & (lane < goal + reach), moved, held)
        target[index] = held


def unpack_rows(sizes, place, blocks, count):
    packed, own, _ = packing(sizes, count)
    if not packed:
        return [blocks[index] for index in range(count)]
    half, reach = LANES // 2, BORDER >> 3
    rows = []
    for index in range(count):
        held = blocks[index // 2]
        lane = lane_at(held.shape)
        if index % 2:
            held = pltpu.roll(held, half, axis=1)
        at, goal = index // (LANES // reach), index % (LANES // reach) * reach
        back = lax.rem(LANES - border_turn(place, goal), LANES)
        beside = pltpu.roll(blocks[own + at], back, axis=1)
        start = jnp.where(place[1] == 0, half, LANES - reach)
        here = (lane >= start) & (lane < start + reach)
        rows.append(jnp.where(lane < half, held, jnp.where(here, beside, 0.0)))
    return rows


def merge_into(sizes, place, stride, radix, arrays, source, conduct, binding, first):
    position = (place[0] // stride) % radix
    source[...] = jnp.zeros(source.shape, f32)
    for step, array in enumerate(arrays):
        at = (position ^ step) * stride
        rows = unpack_rows(sizes, place, array, 3 * stride + 2)
        for index, row in enumerate(rows[: stride + 2]):
            source[at + index] = source[at + index] + row
        for index in range(stride):
            conduct[at + index + first] = rows[stride + 2 + index]
            binding[at + index] = rows[2 * stride + 2 + index]


def merge_kernel(sizes, stride, radix, place, *refs):
    arrays, out, (source, conduct, binding) = refs[:radix], refs[radix], refs[radix + 1 :]
    merge_into(sizes, place, stride, radix, arrays, source, conduct, binding, 0)
    count = stride * radix
    rows = [source[row] for row in range(count + 2)]
    rows += [conduct[row] for row in range(count)] + [binding[row] for row in range(count)]
    pack_rows(sizes, place, rows, out)


def down_kernel(sizes, place, *refs):
    s = sizes.sides
    owns, turned, refs = refs[:3], refs[3], refs[4:]
    borders0, refs = refs[:s], refs[s:]
    pairs_of = [refs[2 * index : 2 * index + 2] for index in range(1 + s)]
    refs = refs[2 * (1 + s) :]
    from_prev, *beside_prev = (Arrived(place, pair, 0) for pair in pairs_of)
    from_next, *beside_next = (Arrived(place, pair, 1) for pair in pairs_of)
    coefs, contribution, with_far, ups, far, refs = refs[:3], refs[3], refs[4], refs[5:7], refs[7], refs[8:]
    border1, border2, level3, sums = refs
    slots = sizes.slots
    n0, n1, n2 = sizes.rows[:3]

    if s:
        for row in range(2 * n1):
            for side in range(s):
                columns = slice(side * LANES, (side + 1) * LANES)
                at, low = row // n1, 2 * (row % n1)
                sums[row, :, columns] = borders0[side][at, low] + borders0[side][at, low + 1]
        narrow(sizes, place, 0, sums, border1, 2 * n1, "border", sizes.own[0] * LANES)
        for row in range(2 * n2):
            sums[row, :, :LANES] = border1[2 * row] + border1[2 * row + 1]
        narrow(sizes, place, 1, sums, border2, 2 * n2, "border", sizes.own[1] * LANES)

    def held_row(level, at, row):
        if level == 0:
            tiles = [turned[row] if at == 2 else owns[0][at, row], *(array[at, row] for array in borders0)]
        else:
            row = at * sizes.rows[level] + row
            tiles = [owns[level][row], *([(border1, border2)[level - 1][row]] if s else [])]
        return jnp.concatenate(tiles, axis=1)

    def prev_row(level, index):
        return message_row(sizes, place, level, slots[index], from_prev, beside_prev)

    def next_row(level, index):
        return message_row(sizes, place, level, slots[index], from_next, beside_next)

    def conduct0(row):
        if row == 0:
            return prev_row(0, 0)
        if row == n0 + 1:
            return next_row(0, 0)
        return held_row(0, 0, row - 1)

    bound0 = lambda row: held_row(0, 1, row - 1)
    fx, fy, fz, weight, v0 = parts(coefs[0], coefficient_rows(sizes, 0))
    coefficients(sizes, place, 0, n0 + 2, conduct0, bound0, fx, fy, fz, weight)
    for row in range(n0):
        v0[row] = weight[row] * held_row(0, 2, row)
    own_defect(n0 + 2, v0, lambda row: held_row(0, 2, row - 1), bound0, fx, fy, fz, sums, 1)
    smooths, sources = [], []
    for level, first in ((1, 1), (2, 4)):
        n = sizes.rows[level]
        fx, fy, fz, weight, binding, source, smooth = parts(coefs[level], coefficient_rows(sizes, level))
        held = sizes.held[level]
        narrow(sizes, place, level - 1, sums.at[:, :, : sizes.held[level - 1]], source, n + 2)
        binding[0] = prev_row(level, first + 2)
        binding[n + 1] = next_row(level, first + 2)
        for row in range(n):
            binding[row + 1] = held_row(level, 1, row)

        def conduct(row, n=n, level=level, first=first):
            if row < 2:
                return prev_row(level, first + row)
            if row >= n + 2:
                return next_row(level, first + row - n - 2)
            return held_row(level, 0, row - 2)

        bound = lambda row, binding=binding: binding[row - 1]
        coefficients(sizes, place, level, n + 4, conduct, bound, fx, fy, fz, weight)
        for row in range(n + 2):
            smooth[row] = weight[row] * source[row]
        mine = lambda row, source=source: source[row - 1]
        own_defect(n + 4, smooth, mine, bound, fx, fy, fz, sums.at[:, :, :held], 0)
        smooths.append(smooth)
        sources.append(source)
    narrow(sizes, place, 2, sums.at[:, :, : sizes.held[2]], level3, 3)

    for at in (0, 1):
        sums[at, :, : sizes.held[2]] = held_row(2, at, 0) + held_row(2, at, 1)
    narrow(sizes, place, 2, sums.at[:, :, : sizes.held[2]], level3.at[3:5], 2)
    tiles = packing(sizes, 5)[2]
    pack_rows(sizes, place, [level3[row] for row in range(5)], contribution)
    with_far[0:tiles] = contribution[...]
    (s1, s2), (v1, v2) = sources, smooths
    next_rows = (v0[n0 - 1], s1[n1], s1[n1 + 1], v1[n1 - 1], s2[n2], s2[n2 + 1], v2[n2 - 1])
    prev_rows = (v0[0], s1[1], s1[0], v1[2], s2[1], s2[0], v2[2])
    for slot, next_row, prev_row in zip(slots, next_rows, prev_rows):
        put_pair(place, ups, slot, next_row, prev_row)
    if s:
        ends = [fringes(sizes, list(zip((1, 1, 1, 2, 2, 2), rows[1:]))) for rows in (next_rows, prev_rows)]
        put_pair(place, ups, (sizes.tiles, 1), *ends)
    far_tiles = sizes.held[2] // LANES
    put_pair(place, (with_far.at[tiles : tiles + far_tiles], far), (0, far_tiles), v2[n2 + 1], v2[0], 2)


def relax(count, field, refs_of, source, target):
    fx, fy, fz, weight, binding = refs_of

    def update(row, value):
        target(row, field(row) + weight[row - 1] * (source(row) - value))

    sweep(count, field, binding, fx, fy, fz, update)


def store(array, first):
    def put_row(row, value):
        array[row - first] = value

    return put_row


def coarse_kernel(sizes, stride, radix, place, *refs):
    blocks, refs = refs[:radix], refs[radix:]
    out, merged, sums = refs[:3]
    coarse = [refs[3 + 9 * index : 12 + 9 * index] for index in range(3)]
    total = sizes.span_count
    merge_into(sizes, place, stride, radix, blocks, merged, coarse[0][4], coarse[0][5], 1)
    zero = jnp.zeros((sizes.depth, LANES), f32)
    for index in range(3):
        level = 3 + index
        fx, fy, fz, weight, conduct, binding, source, smooth, iterate = coarse[index]
        count = total >> index
        for array in (conduct, smooth, iterate):
            array[0] = zero
            array[count + 1] = zero
        if index == 0:
            source = merged.at[1 : count + 1]
        bound = lambda row, binding=binding: binding[row - 1]
        at_row = lambda row, conduct=conduct: conduct[row]
        coefficients(sizes, place, level, count + 2, at_row, bound, fx, fy, fz, weight)
        for row in range(count):
            smooth[row + 1] = weight[row] * source[row]
        if index < 2:
            conduct_next, binding_next, source_next = coarse[index + 1][4:7]
            half = count // 2
            for row in range(half):
                sums[row, :, :LANES] = conduct[2 * row + 1] + conduct[2 * row + 2]
            narrow(sizes, place, level, sums, conduct_next.at[1 : half + 1], half)
            for row in range(half):
                sums[row, :, :LANES] = binding[2 * row] + binding[2 * row + 1]
            narrow(sizes, place, level, sums, binding_next, half)

            def add(row, value, source=source):
                value = source[row - 1] - value
                slot = (row - 1) // 2
                if row % 2 == 1:
                    sums[slot, :, :LANES] = value
                else:
                    sums[slot, :, :LANES] = sums[slot, :, :LANES] + value

            sweep(count + 2, lambda row, smooth=smooth: smooth[row], bound, fx, fy, fz, add)
            narrow(sizes, place, level, sums, source_next, half)

    fx, fy, fz, weight, conduct, binding, source, smooth, iterate = coarse[2]
    held, other = smooth, iterate
    for _ in range(COARSE_SWEEPS - 1):
        field = lambda row, held=held: held[row]
        mine = lambda row: source[row - 1]
        bound = lambda row: binding[row - 1]
        relax((total >> 2) + 2, field, (fx, fy, fz, weight, bound), mine, store(other, 0))
        held, other = other, held
    for index in (1, 0):
        fx, fy, fz, weight, conduct, binding, source, smooth, iterate = coarse[index]
        if index == 0:
            source = merged.at[1 : total + 1]
        count = total >> index
        widen(sizes, place, 3 + index, held.at[1 : count // 2 + 1], sums, count // 2)
        for row in range(count):
            smooth[row + 1] = smooth[row + 1] + sums[row // 2, :, :LANES]
        field = lambda row, smooth=smooth: smooth[row]
        mine = lambda row, source=source: source[row - 1]
        bound = lambda row, binding=binding: binding[row - 1]
        relax(count + 2, field, (fx, fy, fz, weight, bound), mine, store(iterate, 0))
        held = iterate

    out[...] = held[pl.ds(place[0], 3)]


def up_kernel(sizes, place, coarse, *refs):
    s = sizes.sides
    pair, far_pair, coefs, (own0, turned) = refs[:2], refs[2:4], refs[4:7], refs[7:9]
    from_prev, from_next = (Arrived(place, pair, forward) for forward in (0, 1))
    tiles = packing(sizes, 5)[2]
    far_pair = (far_pair[0].at[tiles : tiles + sizes.held[2] // LANES], far_pair[1])
    fars = [Arrived(place, far_pair, forward, 2) for forward in (0, 1)]
    borders0, out, refs = refs[9 : 9 + s], refs[9 + s], refs[10 + s :]
    total1, total2, result = refs[:3]
    over2, over1, over0, lift2, lift1, lift0, it2, it1, it0, semaphores = refs[3:]
    slots = sizes.slots
    n0, n1, n2 = sizes.rows[:3]
    width = sizes.own[0] * LANES

    widen(sizes, place, 2, coarse, over2, 3)
    for level, array, first, totals, over, lift, target, upper in (
        (2, coefs[2], 4, total2, over2, lift2, it2, over1),
        (1, coefs[1], 1, total1, over1, lift1, it1, over0),
    ):
        n = sizes.rows[level]
        fx, fy, fz, weight, binding, own, smooth = parts(array, coefficient_rows(sizes, level))
        edge = {}
        for row, message, index in (
            (1, from_prev, first),
            (2, from_prev, first + 1),
            (n + 2, from_next, first),
            (n + 1, from_next, first + 1),
        ):
            value = edge.get(row, own[row - 1])
            edge[row] = value + fringed_row(sizes, level, index, message)
        for row, value in edge.items():
            totals[row - 1] = value
        for row in range(n + 4):
            if row in (0, n + 3):
                value = fringed_row(sizes, level, first + 2, from_next if row else from_prev)
                if level == 2:
                    far = fars[1 if row else 0]
                    value = value + jnp.concatenate(get(far, (0, sizes.held[2] // LANES)), axis=1)
            elif row in edge:
                value = weight[row - 1] * totals[row - 1]
            else:
                value = smooth[row - 1]
            lift[row] = value + over[row // 2]
        field = lambda row, lift=lift: lift[row]
        mine = lambda row, own=own, totals=totals, edge=edge: (totals if row in edge else own)[row - 1]
        bound = lambda row, binding=binding: binding[row - 1]
        relax(n + 4, field, (fx, fy, fz, weight, bound), mine, store(target, 1))
        widen(sizes, place, level - 1, target, upper, n + 2)

    def held_row(at, row):
        own = turned[row - 1] if at == 2 else own0[at, row - 1]
        return jnp.concatenate([own, *(array[at, row - 1] for array in borders0)], axis=1)

    fx, fy, fz, weight, v0 = parts(coefs[0], coefficient_rows(sizes, 0))
    lift0[0] = fringed_row(sizes, 0, 0, from_prev) + over0[0]
    lift0[n0 + 1] = fringed_row(sizes, 0, 0, from_next) + over0[n1 + 1]
    for row in range(1, n0 + 1):
        lift0[row] = v0[row - 1] + over0[(row + 1) // 2]
    field = lambda row: lift0[row]
    bound = lambda row: held_row(1, row)
    relax(n0 + 2, field, (fx, fy, fz, weight, bound), lambda row: held_row(2, row), store(it0, 1))
    step = sizes.depth // CHUNKS
    copies = []
    for chunk in range(CHUNKS):
        part = slice(chunk * step, (chunk + 1) * step)
        result[part] = jnp.swapaxes(it0[:, part, :width], 0, 1)
        copies.append(pltpu.make_async_copy(result.at[part], out.at[part], semaphores.at[chunk]))
        copies[-1].start()
    for copy in copies:
        copy.wait()


def call(body, name, micros, outputs, scratch, place, inputs, copies=0, far_out=False):
    near, far = pl.BlockSpec(memory_space=pltpu.VMEM), pl.BlockSpec(memory_space=pl.ANY)
    scratch = [pltpu.VMEM(shape, f32) for shape in scratch]
    if copies:
        scratch.append(pltpu.SemaphoreType.DMA((copies,)))
    return pl.pallas_call(
        body,
        name=name,
        out_shape=[jax.ShapeDtypeStruct(shape, f32) for shape in outputs],
        in_specs=[pl.BlockSpec(memory_space=pltpu.SMEM)] + [near] * len(inputs),
        out_specs=[far if far_out else near] * len(outputs),
        scratch_shapes=scratch,
        cost_estimate=pl.CostEstimate(flops=int(micros * 1.15e9), bytes_accessed=int(micros * BYTES_A_MICRO), transcendentals=0),
        compiler_params=pltpu.CompilerParams(vmem_limit_bytes=VMEM_LIMIT),
    )(place, *inputs)


def along(value, axis, steps):
    count = lax.axis_size(axis)
    initial, last = max(0, -steps), min(count, count - steps)
    return lax.ppermute(value, axis, [(source, source + steps) for source in range(initial, last)])


def beside(values, sizes):
    if sizes.sides == 1:
        return [[lax.ppermute(value, "width", [(0, 1), (1, 0)]) for value in values]]
    if sizes.sides == 2:
        return [[along(value, "width", steps) for value in values] for steps in (-1, 1)]
    return []


def stages(count):
    stride = 1
    while stride < count:
        radix = 4 if count // stride % 4 == 0 else 2
        yield stride, radix
        stride *= radix


def swap(value, stride, radix, others=None):
    count = lax.axis_size("span")
    others = others or {}
    return [value] + [
        lax.ppermute(others.get(step, value), "span", [(device, device ^ step * stride) for device in range(count)])
        for step in range(1, radix)
    ]


def exchange(pair, stride):
    count = lax.axis_size("span")
    routes = [[], []]
    for low in range(count - stride):
        routes[low // stride % 2] += [(low, low + stride), (low + stride, low)]
    return [None if value is None else lax.ppermute(value, "span", route) for value, route in zip(pair, routes)]


def on_device(right_side, diffusivity, reaction):
    depth, extent_x, extent_y = diffusivity.shape
    sizes = Sizes(depth, extent_x, extent_y, lax.axis_size("span"), lax.axis_size("width"))
    place = jnp.stack([lax.axis_index("span"), lax.axis_index("width")]).astype(jnp.int32)
    n0, n1, n2, n3 = sizes.rows
    s = sizes.sides
    tile = (depth, LANES)
    own = [(depth, count * LANES) for count in sizes.own]
    held = [(depth, count) for count in sizes.held]
    down_message = (sizes.tiles, *tile)
    up_message = (sizes.tiles + 1, *tile)
    own0, own1, own2, *to_pairs = call(
        functools.partial(start_kernel, sizes),
        "start",
        1.1,
        [(2, n0, *own[0]), (2 * n1, *own[1]), (2 * n2, *own[2]), down_message, down_message],
        [(2 * n1, *own[0])],
        place,
        [diffusivity, reaction],
    )
    halos = exchange(to_pairs, 1)
    turned, *edges = call(
        functools.partial(turn_kernel, sizes),
        "turn",
        0.7,
        [(n0, *own[0])] + [(3, n0, depth, BORDER)] * s,
        [],
        place,
        [right_side, own0],
    )
    if s == 1:
        borders = [lax.ppermute(edges[0], "width", [(0, 1), (1, 0)])]
    elif s == 2:
        borders = [along(edges[1], "width", -1), along(edges[0], "width", 1)]
    else:
        borders = []
    plan = list(stages(sizes.span_count))
    sides = beside(halos, sizes)

    part = packing(sizes, 5)[2]
    lengths = [sum(coefficient_rows(sizes, level)) for level in range(3)]
    far = (sizes.held[2] // LANES, *tile)
    coefs = [(lengths[level], *held[level]) for level in range(3)]
    downs = call(
        functools.partial(down_kernel, sizes),
        "down",
        3.6,
        [*coefs, (part, *tile), (part + far[0], *tile), up_message, up_message, far],
        [(2 * n1, *tile), (2 * n2, *tile), (5, *tile), (max(2 * n1, n1 + 2), *held[0])],
        place,
        [own0, own1, own2, turned, *borders, *halos, *sum(sides, [])],
    )
    coefs_out, blocks, with_far, ups, far_second = downs[:3], downs[3], downs[4], list(downs[5:7]), downs[7]
    far_rows = None
    for stride, radix in plan[:-1]:
        count = stride * radix
        if far_rows is None:
            blocks = swap(blocks, stride, radix, {2: with_far})
            far_rows = [blocks[2], exchange([None, far_second], 2)[1]]
            blocks, ups[0] = lax.optimization_barrier((blocks, ups[0]))
        else:
            blocks = swap(blocks, stride, radix)
        (blocks,) = call(
            functools.partial(merge_kernel, sizes, stride, radix),
            "merge",
            0.9,
            [(packing(sizes, 3 * count + 2)[2], *tile)],
            [(count + 2, *tile), (count, *tile), (count, *tile)],
            place,
            blocks,
        )
    stride, radix = plan[-1]
    blocks = swap(blocks, stride, radix)
    received = lax.optimization_barrier([exchange([ups[0], None], 1)[0], ups[1]])
    received = [received[0], exchange([None, received[1]], 1)[1]] + far_rows
    scratch = [(sizes.span_count + 2, *tile), (max(sizes.span_count // 2, 2), *tile)]
    for index in range(3):
        count = sizes.span_count >> index
        scratch += [(count + 1, *tile)] + [(count, *tile)] * 3 + [(count + 2, *tile)] + [(count, *tile)] * 2
        scratch += [(count + 2, *tile)] * 2
    (coarse,) = call(
        functools.partial(coarse_kernel, sizes, stride, radix),
        "coarse",
        2.9,
        [(n3 + 2, *tile)],
        scratch,
        place,
        blocks,
    )
    scratch = [(n1 + 2, *held[1]), (n2 + 2, *held[2]), diffusivity.shape]
    scratch += [(n3 + 2, *held[2]), (n2 + 2, *held[1]), (n1 + 2, *held[0])]
    scratch += [(n2 + 4, *held[2]), (n1 + 4, *held[1]), (n0 + 2, *held[0])]
    scratch += [(n2 + 2, *held[2]), (n1 + 2, *held[1]), (n0, *held[0])]
    (correction,) = call(
        functools.partial(up_kernel, sizes),
        "up",
        3.0,
        [diffusivity.shape],
        scratch,
        place,
        [coarse, *received, *coefs_out, own0, turned, *borders],
        copies=CHUNKS,
        far_out=True,
    )
    return correction


def solution(mesh):
    in_specs = (P(None, "span", "width"),) * 3
    return jax.shard_map(
        on_device, mesh=mesh, in_specs=in_specs, out_specs=P(None, "span", "width"), check_vma=False
    )
```

```python
import functools

import jax
import jax.numpy as jnp
from jax import lax
from jax.experimental import pallas as pl
from jax.experimental.pallas import tpu as pltpu
from jax.sharding import PartitionSpec as P

LEVELS = 6
COARSE_SWEEPS = 3
LANES = 128
BORDER = 128
FRINGE = 4
SPREAD = 16
relax_weight = 0.8
f32 = jnp.float32
VMEM_LIMIT = 32 * 1024 * 1024
BYTES_A_MICRO = 3.69e6
CHUNKS = 4


class Sizes:
    def __init__(self, depth, extent_x, extent_y, span_count, width_count):
        self.depth, self.extent_x, self.extent_y = depth, extent_x, extent_y
        self.span_count, self.width_count = span_count, width_count
        self.sides = min(width_count - 1, 2)
        self.own = [(extent_y >> level) // LANES for level in range(3)]
        self.border = [self.sides, min(self.sides, 1), min(self.sides, 1)]
        self.held = [(self.own[level] + self.border[level]) * LANES for level in range(3)] + [LANES] * 3
        self.rows = [extent_x >> level for level in range(4)]
        self.slots = []
        start = 0
        for level in (0, 1, 1, 1, 2, 2, 2):
            self.slots.append((start, self.own[level]))
            start += self.own[level]
        self.tiles = start


def put(message, slot, row):
    start, tiles = slot
    for tile in range(tiles):
        message[start + tile] = row[:, tile * LANES : (tile + 1) * LANES]


class Arrived:
    def __init__(self, place, pair, forward, stride=1):
        self.even = place[0] // stride % 2 == 0
        self.first, self.second = (pair[0], pair[1]) if forward else (pair[1], pair[0])

    def __getitem__(self, index):
        return jnp.where(self.even, self.first[index], self.second[index])


def put_pair(place, pair, slot, next_row, prev_row, stride=1):
    even = place[0] // stride % 2 == 0
    put(pair[0], slot, jnp.where(even, next_row, prev_row))
    put(pair[1], slot, jnp.where(even, prev_row, next_row))


def get(message, slot):
    start, tiles = slot
    return [message[start + tile] for tile in range(tiles)]


def lane_at(shape):
    return lax.broadcasted_iota(jnp.int32, shape, len(shape) - 1)


def roll(value, steps, axis):
    return pltpu.roll(value, steps % value.shape[axis], axis=axis)


def reciprocal(value):
    return pltpu.reciprocal(value, approx=True)


def harmonic(first, second, guard):
    total = first + second
    if guard:
        total = jnp.maximum(total, 1e-3)
    return (2.0 * first) * second * reciprocal(total)


def split(value):
    high = value.astype(jnp.bfloat16)
    return high, (value - high.astype(f32)).astype(jnp.bfloat16)


def dot(halves, table):
    high, low = halves
    return jnp.dot(high, table, preferred_element_type=f32) + jnp.dot(low, table, preferred_element_type=f32)


def pair_table(fine, fine_dim, turn, weight):
    shape = (fine, LANES) if fine_dim == 0 else (LANES, fine)
    fine_at = lax.broadcasted_iota(jnp.int32, shape, fine_dim)
    coarse_at = lax.broadcasted_iota(jnp.int32, shape, 1 - fine_dim)
    if turn is not None:
        coarse_at = coarse_at - jnp.where(fine_at >= turn, LANES // 2, 0)
    return jnp.where(fine_at // 2 == coarse_at, weight, 0.0).astype(jnp.bfloat16)


def turns(sizes, place, level):
    if sizes.sides == 0:
        return []
    if level == 0:
        return [jnp.where(place[1] == 0, LANES, 0)] if sizes.sides == 1 else [LANES, 0]
    return [LANES // 2]


def transfer_plan(sizes, place, level, part):
    plan = []
    if level >= 3:
        return [((0, LANES), 0, 3 * LANES // 4)]
    if level == 2:
        return [((0, sizes.held[2]), 0, None)]
    own = sizes.own[level]
    if part != "border":
        plan += [((2 * LANES * tile, 2 * LANES * (tile + 1)), tile, None) for tile in range(own // 2)]
    if part != "own":
        for index, turn in enumerate(turns(sizes, place, level)):
            start = (own + index) * LANES
            plan.append(((start, start + LANES), own // 2, turn))
    return plan


def narrow(sizes, place, level, sums, target, rows, part="all", shift=0):
    depth = sums.shape[1]
    done = {}
    for (start, stop), tile, turn in transfer_plan(sizes, place, level, part):
        start, stop, tile = start - shift, stop - shift, tile - shift // (2 * LANES)
        columns = split(sums[0:rows, :, start:stop].reshape(rows * depth, stop - start))
        result = dot(columns, pair_table(stop - start, 0, turn, 0.25)).reshape(rows, depth, LANES)
        done[tile] = done[tile] + result if tile in done else result
    for tile, result in done.items():
        target[0:rows, :, tile * LANES : (tile + 1) * LANES] = result


def widen(sizes, place, level, coarse, target, rows):
    depth = coarse.shape[1]
    for (start, stop), tile, turn in transfer_plan(sizes, place, level, "all"):
        columns = split(coarse[0:rows, :, tile * LANES : (tile + 1) * LANES].reshape(rows * depth, LANES))
        result = dot(columns, pair_table(stop - start, 1, turn, 4.0))
        target[0:rows, :, start:stop] = result.reshape(rows, depth, stop - start)


class Joined:
    def __init__(self, inner, outer, first):
        self.inner, self.outer, self.first = inner, outer, first

    def find(self, row):
        place, count = row - self.first, 0 if self.inner is None else self.inner.shape[0]
        if 0 <= place < count:
            return self.inner, place
        return self.outer, row if place < 0 else row - count

    def __getitem__(self, row):
        array, place = self.find(row)
        return array[place]

    def __setitem__(self, row, value):
        array, place = self.find(row)
        array[place] = value


class Level:
    def __init__(self, sizes, level, inner, outer):
        self.n, self.halo = sizes.rows[level], 1 if level == 0 else 2
        counts = inner_rows(sizes, level)
        fx, fy, fz, *rest = parts(inner, counts)
        weight, source, smooth = (None, None, None) if level == 2 else (rest[0], None, rest[1])
        if level == 1:
            weight, source, smooth = rest
        others = [None] * 7 if outer is None else parts(outer, outer_rows(sizes, level))
        if level == 0 and outer is not None:
            others = [others[0], None, None, others[1], None, others[2], None]
        h = self.halo
        self.fx = Joined(fx, others[0], h)
        self.fy, self.fz = Joined(fy, others[1], h - 1), Joined(fz, others[2], h - 1)
        self.weight, self.source, self.smooth = (
            Joined(array, other, h) for array, other in zip((weight, source, smooth), others[3:6])
        )
        self.binding = others[6]

    def inner(self):
        first, last = self.halo, self.halo + self.n - 1
        return range(first + 1, last + 1), range(first, last + 1), range(first + 1, last)

    def outer(self):
        count = self.n + 2 * self.halo
        every = (range(1, count), range(1, count - 1), range(1, count - 1))
        return tuple([row for row in rows if row not in mine] for rows, mine in zip(every, self.inner()))


def inner_rows(sizes, level):
    n = sizes.rows[level]
    return [n - 1, n, n] + [[n - 2] * 2, [n - 2] * 3, []][level]


def outer_rows(sizes, level):
    n = sizes.rows[level]
    return [[2, 2, 2], [4, 2, 2, 4, 4, 4, n + 2], [4, 2, 2] + [n + 2] * 4][level]


def coefficients(sizes, place, level, conduct, binding, fx, fy, fz, weight, rows):
    guard = level > 0 or sizes.sides > 1
    for row in rows[0]:
        fx[row - 1] = harmonic(conduct(row - 1), conduct(row), guard)
    for row in rows[1]:
        mine = conduct(row)
        south = harmonic(mine, roll(mine, 1, 1), guard)
        if level == 0 and sizes.sides < 2:
            cut = 0 if sizes.sides == 0 else jnp.where(place[1] == 0, 0, sizes.extent_y)
            south = jnp.where(lane_at(mine.shape) == cut, 0.0, south)
        below = harmonic(mine, roll(mine, 1, 0), guard)
        fy[row - 1] = south
        fz[row - 1] = jnp.where(lax.broadcasted_iota(jnp.int32, mine.shape, 0) == 0, 0.0, below)
    for row in rows[2]:
        south, below = fy[row - 1], fz[row - 1]
        diagonal = fx[row - 1] + fx[row] + binding(row)
        diagonal = diagonal + (south + roll(south, -1, 1)) + (below + roll(below, -1, 0))
        if guard:
            diagonal = jnp.maximum(diagonal, 1e-6)
        weight[row - 1] = relax_weight * reciprocal(diagonal)


def sweep(first, last, field, binding, fx, fy, fz, emit):
    lower = fx[first - 1] * (field(first) - field(first - 1))
    for row in range(first, last + 1):
        mine = field(row)
        upper = fx[row] * (field(row + 1) - mine)
        south = fy[row - 1] * (mine - roll(mine, 1, 1))
        below = fz[row - 1] * (mine - roll(mine, 1, 0))
        across = (south - roll(south, -1, 1)) + (below - roll(below, -1, 0))
        emit(row, binding(row) * mine + (lower - upper) + across)
        lower = upper


def in_pairs(sums, slot_of):
    def add(row, value):
        slot, first = slot_of(row)
        if first:
            sums[slot] = value
        else:
            sums[slot] = sums[slot] + value

    return add


def parts(array, counts):
    views, start = [], 0
    for count in counts:
        views.append(array.at[start : start + count])
        start += count
    return views


def start_kernel(sizes, place, conduct, binding, own0, own1, own2, first, second, *refs):
    edges, sums = refs[: sizes.sides], refs[-1]
    n0, n1, n2 = sizes.rows[:3]
    for at, array in enumerate((conduct, binding)):
        own0[at] = jnp.swapaxes(array[...], 0, 1)
    for at in (0, 1):
        for row in range(n1):
            sums[at * n1 + row] = own0[at, 2 * row] + own0[at, 2 * row + 1]
    narrow(sizes, place, 0, sums, own1, 2 * n1, "own")
    for row in range(2 * n2):
        sums[row, :, : sizes.own[1] * LANES] = own1[2 * row] + own1[2 * row + 1]
    narrow(sizes, place, 1, sums, own2, 2 * n2, "own")
    ends = []
    for low, at1, at0 in ((n1 - 2, n1 - 1, n0 - 1), (0, 0, 0)):
        edge = n2 - 1 if at0 else 0
        rows = (own0[0, at0], own1[low], own1[low + 1], own1[n1 + at1])
        ends.append(rows + (own2[n2 - 2], own2[n2 - 1], own2[n2 + edge]))
    for slot, next_row, prev_row in zip(sizes.slots, *ends):
        put_pair(place, (first, second), slot, next_row, prev_row)
    for at in (0, 1):
        cut_edges(sizes, place, own0.at[at], [edge.at[at] for edge in edges])


def cut_edges(sizes, place, array, edges):
    last = sizes.extent_y - BORDER
    if sizes.sides == 1:
        at = pl.multiple_of(jnp.where(place[1] == 0, last, 0), LANES)
        edges[0][...] = array[:, :, pl.ds(at, BORDER)]
    elif sizes.sides == 2:
        edges[0][...] = array[:, :, last:]
        edges[1][...] = array[:, :, :BORDER]


def turn_kernel(sizes, place, right_side, turned, *edges):
    turned[...] = jnp.swapaxes(right_side[...], 0, 1)
    cut_edges(sizes, place, turned, edges)


def message_row(sizes, place, level, slot, message, beside):
    start, tiles = slot
    row = get(message, slot)
    if sizes.sides == 1:
        left = place[1] != 0
        tile = beside[0][start + jnp.where(left, tiles - 1, 0)]
        if level > 0:
            reach = BORDER >> level
            lane = lane_at(tile.shape)
            first = jnp.where(left, LANES - reach, 0)
            tile = jnp.where((lane >= first) & (lane < first + reach), tile, 0.0)
        row.append(tile)
    elif sizes.sides == 2:
        right, left = beside[0][start], beside[1][start + tiles - 1]
        if level == 0:
            row += [right, left]
        else:
            reach = BORDER >> level
            lane = lane_at(right.shape)
            row.append(jnp.where(lane < reach, right, jnp.where(lane >= LANES - reach, left, 0.0)))
    return jnp.concatenate(row, axis=1)


def fringe_lanes(shape):
    lane = lane_at(shape)
    return (lane < FRINGE) | (lane >= LANES - FRINGE)


def fringes(sizes, rows):
    total = None
    for index, (level, row) in enumerate(rows):
        tile = row[:, sizes.own[level] * LANES :]
        tile = jnp.where(fringe_lanes(tile.shape), tile, 0.0)
        tile = roll(tile, SPREAD * index + SPREAD // 2, 1)
        total = tile if total is None else total + tile
    return total


def fringed_row(sizes, level, index, message):
    row = get(message, sizes.slots[index])
    if sizes.border[level]:
        if level == 0:
            row += [jnp.zeros(row[0].shape, f32)] * sizes.border[0]
        else:
            tile = roll(message[sizes.tiles], -(SPREAD * (index - 1) + SPREAD // 2), 1)
            row.append(jnp.where(fringe_lanes(tile.shape), tile, 0.0))
    return jnp.concatenate(row, axis=1)


def packing(sizes, count):
    if sizes.sides != 1:
        return False, count, count
    own = -(-count // 2)
    return True, own, own - (-count * (BORDER >> 3) // LANES)


def border_turn(place, goal):
    return jnp.where(place[1] == 0, (goal - LANES // 2) % LANES, (goal + (BORDER >> 3)) % LANES)


def pack_rows(sizes, place, rows, target):
    packed, own, tiles = packing(sizes, len(rows))
    if not packed:
        for index, row in enumerate(rows):
            target[index] = row
        return
    half, reach = LANES // 2, BORDER >> 3
    lane = lane_at(rows[0].shape)
    for index in range(own):
        held = rows[2 * index]
        other = rows[2 * index + 1] if 2 * index + 1 < len(rows) else jnp.zeros(held.shape, f32)
        target[index] = jnp.where(lane < half, held, pltpu.roll(other, half, axis=1))
    for index in range(own, tiles):
        held = jnp.zeros(rows[0].shape, f32)
        some = rows[(index - own) * (LANES // reach) :][: LANES // reach]
        for place_at, row in enumerate(some):
            goal = place_at * reach
            moved = pltpu.roll(row, border_turn(place, goal), axis=1)
            held = jnp.where((lane >= goal) & (lane < goal + reach), moved, held)
        target[index] = held


def unpack_rows(sizes, place, blocks, count):
    packed, own, _ = packing(sizes, count)
    if not packed:
        return [blocks[index] for index in range(count)]
    half, reach = LANES // 2, BORDER >> 3
    rows = []
    for index in range(count):
        held = blocks[index // 2]
        lane = lane_at(held.shape)
        if index % 2:
            held = pltpu.roll(held, half, axis=1)
        at, goal = index // (LANES // reach), index % (LANES // reach) * reach
        back = lax.rem(LANES - border_turn(place, goal), LANES)
        beside = pltpu.roll(blocks[own + at], back, axis=1)
        start = jnp.where(place[1] == 0, half, LANES - reach)
        here = (lane >= start) & (lane < start + reach)
        rows.append(jnp.where(lane < half, held, jnp.where(here, beside, 0.0)))
    return rows


def merge_into(sizes, place, stride, radix, arrays, source, conduct, binding, first):
    position = (place[0] // stride) % radix
    source[...] = jnp.zeros(source.shape, f32)
    for step, array in enumerate(arrays):
        at = (position ^ step) * stride
        rows = unpack_rows(sizes, place, array, 3 * stride + 2)
        for index, row in enumerate(rows[: stride + 2]):
            source[at + index] = source[at + index] + row
        for index in range(stride):
            conduct[at + index + first] = rows[stride + 2 + index]
            binding[at + index] = rows[2 * stride + 2 + index]


def merge_kernel(sizes, stride, radix, place, *refs):
    arrays, out, (source, conduct, binding) = refs[:radix], refs[radix], refs[radix + 1 :]
    merge_into(sizes, place, stride, radix, arrays, source, conduct, binding, 0)
    count = stride * radix
    rows = [source[row] for row in range(count + 2)]
    rows += [conduct[row] for row in range(count)] + [binding[row] for row in range(count)]
    pack_rows(sizes, place, rows, out)


def held_rows(sizes, owns, borders):
    def held_row(level, at, row):
        if level > 0:
            row = at * sizes.rows[level] + row
            return jnp.concatenate([owns[level][row], *(array[row] for array in borders[level])], axis=1)
        sides = len(borders[0]) // 2
        if at == 2:
            return jnp.concatenate([owns[3][row], *(array[row] for array in borders[0][sides:])], axis=1)
        return jnp.concatenate([owns[0][at, row], *(array[at, row] for array in borders[0][:sides])], axis=1)

    return held_row


def inner_kernel(sizes, place, *refs):
    s = sizes.sides
    owns, borders0, refs = refs[:4], refs[4 : 4 + 2 * s], refs[4 + 2 * s :]
    border1, border2, inner0, inner1, inner2, sums = refs
    n0, n1, n2 = sizes.rows[:3]
    if s:
        for row in range(2 * n1):
            for side in range(s):
                columns = slice(side * LANES, (side + 1) * LANES)
                at, low = row // n1, 2 * (row % n1)
                sums[row, :, columns] = borders0[side][at, low] + borders0[side][at, low + 1]
        narrow(sizes, place, 0, sums, border1, 2 * n1, "border", sizes.own[0] * LANES)
        for row in range(2 * n2):
            sums[row, :, :LANES] = border1[2 * row] + border1[2 * row + 1]
        narrow(sizes, place, 1, sums, border2, 2 * n2, "border", sizes.own[1] * LANES)
    held_row = held_rows(sizes, owns, [borders0, [border1][:s], [border2][:s]])
    levels = [Level(sizes, level, inner, None) for level, inner in enumerate((inner0, inner1, inner2))]
    for index, level in enumerate(levels):
        conduct = lambda row, index=index, level=level: held_row(index, 0, row - level.halo)
        bound = lambda row, index=index, level=level: held_row(index, 1, row - level.halo)
        coefficients(
            sizes, place, index, conduct, bound, level.fx, level.fy, level.fz, level.weight, level.inner()
        )
        if index == 0:
            right = lambda row: held_row(0, 2, row - 1)
            for row in range(2, n0):
                level.smooth[row - 1] = level.weight[row - 1] * right(row)
            add = in_pairs(sums, lambda row: ((row - 3) // 2, row % 2 == 1))
            field = lambda row, level=level: level.smooth[row - 1]
            emit = lambda row, value: add(row, right(row) - value)
            sweep(3, n0 - 2, field, bound, level.fx, level.fy, level.fz, emit)
        if index == 1:
            narrow(sizes, place, 0, sums, level.source.inner, n1 - 2)
            for row in range(2, n1):
                level.smooth[row] = level.weight[row] * level.source[row]


def down_kernel(sizes, place, *refs):
    s = sizes.sides
    owns, borders0, refs = refs[:4], refs[4 : 4 + 2 * s], refs[4 + 2 * s :]
    pairs_of = [refs[2 * index : 2 * index + 2] for index in range(1 + s)]
    refs = refs[2 * (1 + s) :]
    from_prev, *beside_prev = (Arrived(place, pair, 0) for pair in pairs_of)
    from_next, *beside_next = (Arrived(place, pair, 1) for pair in pairs_of)
    (border1, border2), inners, refs = refs[:2], refs[2:5], refs[5:]
    outers, contribution, with_far, ups, far, refs = refs[:3], refs[3], refs[4], refs[5:7], refs[7], refs[8:]
    level3, sums = refs
    slots = sizes.slots
    n0, n1, n2 = sizes.rows[:3]
    levels = [Level(sizes, index, inner, outer) for index, (inner, outer) in enumerate(zip(inners, outers))]
    held_row = held_rows(sizes, owns, [borders0, [border1][:s], [border2][:s]])

    def prev_row(level, index):
        return message_row(sizes, place, level, slots[index], from_prev, beside_prev)

    def next_row(level, index):
        return message_row(sizes, place, level, slots[index], from_next, beside_next)

    def conduct0(row):
        if row == 0:
            return prev_row(0, 0)
        if row == n0 + 1:
            return next_row(0, 0)
        return held_row(0, 0, row - 1)

    zero = jnp.zeros((sizes.depth, sizes.held[0]), f32)
    level = levels[0]
    bound0 = lambda row: held_row(0, 1, row - 1)
    right = lambda row: held_row(0, 2, row - 1)
    coefficients(
        sizes, place, 0, conduct0, bound0, level.fx, level.fy, level.fz, level.weight, level.outer()
    )
    for row in (1, n0):
        level.smooth[row - 1] = level.weight[row - 1] * right(row)
    first_slot = lambda row: (row + 1) // 2
    add = in_pairs(
        sums,
        lambda row: (first_slot(row) - (n1 - 2 if row > n0 // 2 else 0), row % 2 == 1 or row == 0),
    )
    field = lambda row, level=level: level.smooth[row - 1] if 0 < row < n0 + 1 else zero
    emit = lambda row, value: add(row, right(row) - value)
    add(0, level.fx[0] * field(1))
    sweep(1, 2, field, bound0, level.fx, level.fy, level.fz, emit)
    sweep(n0 - 1, n0, field, bound0, level.fx, level.fy, level.fz, emit)
    add(n0 + 1, level.fx[n0] * field(n0))
    fine_held = sizes.held[0]
    for index, first in ((1, 1), (2, 4)):
        level, n = levels[index], sizes.rows[index]
        held = sizes.held[index]
        narrow(
            sizes, place, index - 1, sums.at[:, :, :fine_held], level.source.outer, level.source.outer.shape[0]
        )
        binding = level.binding
        binding[0] = prev_row(index, first + 2)
        binding[n + 1] = next_row(index, first + 2)
        for row in range(n):
            binding[row + 1] = held_row(index, 1, row)

        def conduct(row, n=n, index=index, first=first):
            if row < 2:
                return prev_row(index, first + row)
            if row >= n + 2:
                return next_row(index, first + row - n - 2)
            return held_row(index, 0, row - 2)

        bound = lambda row, binding=binding: binding[row - 1]
        coefficients(
            sizes, place, index, conduct, bound, level.fx, level.fy, level.fz, level.weight, level.outer()
        )
        for row in level.outer()[2] if index == 1 else range(1, n + 3):
            level.smooth[row - 1] = level.weight[row - 1] * level.source[row - 1]
        zero = jnp.zeros((sizes.depth, held), f32)
        field = lambda row, level=level, n=n, zero=zero: level.smooth[row - 1] if 0 < row < n + 3 else zero
        add = in_pairs(sums.at[:, :, :held], lambda row: (row // 2, row % 2 == 0))
        emit = lambda row, value, level=level, add=add: add(row, level.source[row - 1] - value)
        add(0, level.fx[0] * field(1))
        sweep(1, n + 2, field, bound, level.fx, level.fy, level.fz, emit)
        add(n + 3, level.fx[n + 2] * field(n + 2))
        fine_held = held
    narrow(sizes, place, 2, sums.at[:, :, : sizes.held[2]], level3, 3)
    for at in (0, 1):
        sums[at, :, : sizes.held[2]] = held_row(2, at, 0) + held_row(2, at, 1)
    narrow(sizes, place, 2, sums.at[:, :, : sizes.held[2]], level3.at[3:5], 2)
    tiles = packing(sizes, 5)[2]
    pack_rows(sizes, place, [level3[row] for row in range(5)], contribution)
    with_far[0:tiles] = contribution[...]
    v0, s1, v1 = levels[0].smooth, levels[1].source, levels[1].smooth
    s2, v2 = levels[2].source, levels[2].smooth
    next_rows = (v0[n0 - 1], s1[n1], s1[n1 + 1], v1[n1 - 1], s2[n2], s2[n2 + 1], v2[n2 - 1])
    prev_rows = (v0[0], s1[1], s1[0], v1[2], s2[1], s2[0], v2[2])
    for slot, next_row, prev_row in zip(slots, next_rows, prev_rows):
        put_pair(place, ups, slot, next_row, prev_row)
    if s:
        ends = [fringes(sizes, list(zip((1, 1, 1, 2, 2, 2), rows[1:]))) for rows in (next_rows, prev_rows)]
        put_pair(place, ups, (sizes.tiles, 1), *ends)
    far_tiles = sizes.held[2] // LANES
    put_pair(place, (with_far.at[tiles : tiles + far_tiles], far), (0, far_tiles), v2[n2 + 1], v2[0], 2)


def relax(count, field, refs_of, source, target):
    fx, fy, fz, weight, binding = refs_of

    def update(row, value):
        target(row, field(row) + weight[row - 1] * (source(row) - value))

    sweep(1, count - 2, field, binding, fx, fy, fz, update)


def store(array, first):
    def put_row(row, value):
        array[row - first] = value

    return put_row


def coarse_kernel(sizes, stride, radix, place, *refs):
    blocks, refs = refs[:radix], refs[radix:]
    out, merged, sums = refs[:3]
    coarse = [refs[3 + 9 * index : 12 + 9 * index] for index in range(3)]
    total = sizes.span_count
    merge_into(sizes, place, stride, radix, blocks, merged, coarse[0][4], coarse[0][5], 1)
    zero = jnp.zeros((sizes.depth, LANES), f32)
    for index in range(3):
        level = 3 + index
        fx, fy, fz, weight, conduct, binding, source, smooth, iterate = coarse[index]
        count = total >> index
        for array in (conduct, smooth, iterate):
            array[0] = zero
            array[count + 1] = zero
        if index == 0:
            source = merged.at[1 : count + 1]
        bound = lambda row, binding=binding: binding[row - 1]
        at_row = lambda row, conduct=conduct: conduct[row]
        every = (range(1, count + 2), range(1, count + 1), range(1, count + 1))
        coefficients(sizes, place, level, at_row, bound, fx, fy, fz, weight, every)
        for row in range(count):
            smooth[row + 1] = weight[row] * source[row]
        if index < 2:
            conduct_next, binding_next, source_next = coarse[index + 1][4:7]
            half = count // 2
            for row in range(half):
                sums[row, :, :LANES] = conduct[2 * row + 1] + conduct[2 * row + 2]
            narrow(sizes, place, level, sums, conduct_next.at[1 : half + 1], half)
            for row in range(half):
                sums[row, :, :LANES] = binding[2 * row] + binding[2 * row + 1]
            narrow(sizes, place, level, sums, binding_next, half)

            def add(row, value, source=source):
                value = source[row - 1] - value
                slot = (row - 1) // 2
                if row % 2 == 1:
                    sums[slot, :, :LANES] = value
                else:
                    sums[slot, :, :LANES] = sums[slot, :, :LANES] + value

            sweep(1, count, lambda row, smooth=smooth: smooth[row], bound, fx, fy, fz, add)
            narrow(sizes, place, level, sums, source_next, half)

    fx, fy, fz, weight, conduct, binding, source, smooth, iterate = coarse[2]
    held, other = smooth, iterate
    for _ in range(COARSE_SWEEPS - 1):
        field = lambda row, held=held: held[row]
        mine = lambda row: source[row - 1]
        bound = lambda row: binding[row - 1]
        relax((total >> 2) + 2, field, (fx, fy, fz, weight, bound), mine, store(other, 0))
        held, other = other, held
    for index in (1, 0):
        fx, fy, fz, weight, conduct, binding, source, smooth, iterate = coarse[index]
        if index == 0:
            source = merged.at[1 : total + 1]
        count = total >> index
        widen(sizes, place, 3 + index, held.at[1 : count // 2 + 1], sums, count // 2)
        for row in range(count):
            smooth[row + 1] = smooth[row + 1] + sums[row // 2, :, :LANES]
        field = lambda row, smooth=smooth: smooth[row]
        mine = lambda row, source=source: source[row - 1]
        bound = lambda row, binding=binding: binding[row - 1]
        relax(count + 2, field, (fx, fy, fz, weight, bound), mine, store(iterate, 0))
        held = iterate

    out[...] = held[pl.ds(place[0], 3)]


def up_kernel(sizes, place, coarse, *refs):
    s = sizes.sides
    pair, far_pair, inners, outers, owns = refs[:2], refs[2:4], refs[4:7], refs[7:10], refs[10:12]
    levels = [Level(sizes, index, inner, outer) for index, (inner, outer) in enumerate(zip(inners, outers))]
    from_prev, from_next = (Arrived(place, pair, forward) for forward in (0, 1))
    tiles = packing(sizes, 5)[2]
    far_pair = (far_pair[0].at[tiles : tiles + sizes.held[2] // LANES], far_pair[1])
    fars = [Arrived(place, far_pair, forward, 2) for forward in (0, 1)]
    borders0, out, refs = refs[12 : 12 + 2 * s], refs[12 + 2 * s], refs[13 + 2 * s :]
    total1, total2, result = refs[:3]
    over2, over1, over0, lift2, lift1, lift0, it2, it1, it0, semaphores = refs[3:]
    slots = sizes.slots
    n0, n1, n2 = sizes.rows[:3]
    width = sizes.own[0] * LANES

    widen(sizes, place, 2, coarse, over2, 3)
    for level, first, totals, over, lift, target, upper in (
        (2, 4, total2, over2, lift2, it2, over1),
        (1, 1, total1, over1, lift1, it1, over0),
    ):
        n, kept = sizes.rows[level], levels[level]
        fx, fy, fz, weight, binding = kept.fx, kept.fy, kept.fz, kept.weight, kept.binding
        own, smooth = kept.source, kept.smooth
        edge = {}
        for row, message, index in (
            (1, from_prev, first),
            (2, from_prev, first + 1),
            (n + 2, from_next, first),
            (n + 1, from_next, first + 1),
        ):
            value = edge.get(row, own[row - 1])
            edge[row] = value + fringed_row(sizes, level, index, message)
        for row, value in edge.items():
            totals[row - 1] = value
        for row in range(n + 4):
            if row in (0, n + 3):
                value = fringed_row(sizes, level, first + 2, from_next if row else from_prev)
                if level == 2:
                    far = fars[1 if row else 0]
                    value = value + jnp.concatenate(get(far, (0, sizes.held[2] // LANES)), axis=1)
            elif row in edge:
                value = weight[row - 1] * totals[row - 1]
            else:
                value = smooth[row - 1]
            lift[row] = value + over[row // 2]
        field = lambda row, lift=lift: lift[row]
        mine = lambda row, own=own, totals=totals, edge=edge: (totals if row in edge else own)[row - 1]
        bound = lambda row, binding=binding: binding[row - 1]
        relax(n + 4, field, (fx, fy, fz, weight, bound), mine, store(target, 1))
        widen(sizes, place, level - 1, target, upper, n + 2)

    held_row = held_rows(sizes, [owns[0], None, None, owns[1]], [borders0])
    fx, fy, fz, weight, v0 = levels[0].fx, levels[0].fy, levels[0].fz, levels[0].weight, levels[0].smooth
    lift0[0] = fringed_row(sizes, 0, 0, from_prev) + over0[0]
    lift0[n0 + 1] = fringed_row(sizes, 0, 0, from_next) + over0[n1 + 1]
    for row in range(1, n0 + 1):
        lift0[row] = v0[row - 1] + over0[(row + 1) // 2]
    field = lambda row: lift0[row]
    bound = lambda row: held_row(0, 1, row - 1)
    relax(n0 + 2, field, (fx, fy, fz, weight, bound), lambda row: held_row(0, 2, row - 1), store(it0, 1))
    step = sizes.depth // CHUNKS
    copies = []
    for chunk in range(CHUNKS):
        part = slice(chunk * step, (chunk + 1) * step)
        result[part] = jnp.swapaxes(it0[:, part, :width], 0, 1)
        copies.append(pltpu.make_async_copy(result.at[part], out.at[part], semaphores.at[chunk]))
        copies[-1].start()
    for copy in copies:
        copy.wait()


def call(body, name, micros, outputs, scratch, place, inputs, copies=0, far_out=False):
    near, far = pl.BlockSpec(memory_space=pltpu.VMEM), pl.BlockSpec(memory_space=pl.ANY)
    scratch = [pltpu.VMEM(shape, f32) for shape in scratch]
    if copies:
        scratch.append(pltpu.SemaphoreType.DMA((copies,)))
    return pl.pallas_call(
        body,
        name=name,
        out_shape=[jax.ShapeDtypeStruct(shape, f32) for shape in outputs],
        in_specs=[pl.BlockSpec(memory_space=pltpu.SMEM)] + [near] * len(inputs),
        out_specs=[far if far_out else near] * len(outputs),
        scratch_shapes=scratch,
        cost_estimate=pl.CostEstimate(flops=int(micros * 1.15e9), bytes_accessed=int(micros * BYTES_A_MICRO), transcendentals=0),
        compiler_params=pltpu.CompilerParams(vmem_limit_bytes=VMEM_LIMIT),
    )(place, *inputs)


def along(value, axis, steps):
    count = lax.axis_size(axis)
    initial, last = max(0, -steps), min(count, count - steps)
    return lax.ppermute(value, axis, [(source, source + steps) for source in range(initial, last)])


def beside(values, sizes):
    if sizes.sides == 1:
        return [[lax.ppermute(value, "width", [(0, 1), (1, 0)]) for value in values]]
    if sizes.sides == 2:
        return [[along(value, "width", steps) for value in values] for steps in (-1, 1)]
    return []


def edge_columns(edges, sizes):
    if sizes.sides == 1:
        return [lax.ppermute(edges[0], "width", [(0, 1), (1, 0)])]
    if sizes.sides == 2:
        return [along(edges[1], "width", -1), along(edges[0], "width", 1)]
    return []


def stages(count):
    stride = 1
    while stride < count:
        radix = 4 if count // stride % 4 == 0 else 2
        yield stride, radix
        stride *= radix


def swap(value, stride, radix, others=None):
    count = lax.axis_size("span")
    others = others or {}
    return [value] + [
        lax.ppermute(others.get(step, value), "span", [(device, device ^ step * stride) for device in range(count)])
        for step in range(1, radix)
    ]


def exchange(pair, stride):
    count = lax.axis_size("span")
    routes = [[], []]
    for low in range(count - stride):
        routes[low // stride % 2] += [(low, low + stride), (low + stride, low)]
    return [None if value is None else lax.ppermute(value, "span", route) for value, route in zip(pair, routes)]


def on_device(right_side, diffusivity, reaction):
    depth, extent_x, extent_y = diffusivity.shape
    sizes = Sizes(depth, extent_x, extent_y, lax.axis_size("span"), lax.axis_size("width"))
    place = jnp.stack([lax.axis_index("span"), lax.axis_index("width")]).astype(jnp.int32)
    n0, n1, n2, n3 = sizes.rows
    s = sizes.sides
    tile = (depth, LANES)
    own = [(depth, count * LANES) for count in sizes.own]
    held = [(depth, count) for count in sizes.held]
    down_message = (sizes.tiles, *tile)
    up_message = (sizes.tiles + 1, *tile)
    own0, own1, own2, first, second, *edges = call(
        functools.partial(start_kernel, sizes),
        "start",
        1.1,
        [(2, n0, *own[0]), (2 * n1, *own[1]), (2 * n2, *own[2]), down_message, down_message]
        + [(2, n0, depth, BORDER)] * s,
        [(2 * n1, *own[0])],
        place,
        [diffusivity, reaction],
    )
    borders = edge_columns(edges, sizes)
    halos = exchange([first, second], 1)
    turned, *edges = call(
        functools.partial(turn_kernel, sizes),
        "turn",
        0.7,
        [(n0, *own[0])] + [(n0, depth, BORDER)] * s,
        [],
        place,
        [right_side],
    )
    borders += edge_columns(edges, sizes)
    plan = list(stages(sizes.span_count))

    part = packing(sizes, 5)[2]
    far = (sizes.held[2] // LANES, *tile)
    inners = [(sum(inner_rows(sizes, level)), *held[level]) for level in range(3)]
    outers = [(sum(outer_rows(sizes, level)), *held[level]) for level in range(3)]
    inner = call(
        functools.partial(inner_kernel, sizes),
        "inner",
        0.5,
        [(2 * n1, *tile), (2 * n2, *tile), *inners],
        [(2 * n1, *held[0])],
        place,
        [own0, own1, own2, turned, *borders],
    )
    halos, inner = lax.optimization_barrier((halos, inner))
    sides = beside(halos, sizes)
    downs = call(
        functools.partial(down_kernel, sizes),
        "down",
        2.5,
        [*outers, (part, *tile), (part + far[0], *tile), up_message, up_message, far],
        [(5, *tile), (n1 + 2, *held[0])],
        place,
        [own0, own1, own2, turned, *borders, *halos, *sum(sides, []), *inner],
    )
    outer, blocks, with_far, ups, far_second = downs[:3], downs[3], downs[4], list(downs[5:7]), downs[7]
    far_rows = None
    for stride, radix in plan[:-1]:
        count = stride * radix
        if far_rows is None:
            blocks = swap(blocks, stride, radix, {2: with_far})
            far_rows = [blocks[2], exchange([None, far_second], 2)[1]]
            blocks, ups[0] = lax.optimization_barrier((blocks, ups[0]))
        else:
            blocks = swap(blocks, stride, radix)
        (blocks,) = call(
            functools.partial(merge_kernel, sizes, stride, radix),
            "merge",
            0.9,
            [(packing(sizes, 3 * count + 2)[2], *tile)],
            [(count + 2, *tile), (count, *tile), (count, *tile)],
            place,
            blocks,
        )
    stride, radix = plan[-1]
    blocks = swap(blocks, stride, radix)
    received = lax.optimization_barrier([exchange([ups[0], None], 1)[0], ups[1]])
    received = [received[0], exchange([None, received[1]], 1)[1]] + far_rows
    scratch = [(sizes.span_count + 2, *tile), (max(sizes.span_count // 2, 2), *tile)]
    for index in range(3):
        count = sizes.span_count >> index
        scratch += [(count + 1, *tile)] + [(count, *tile)] * 3 + [(count + 2, *tile)] + [(count, *tile)] * 2
        scratch += [(count + 2, *tile)] * 2
    (coarse,) = call(
        functools.partial(coarse_kernel, sizes, stride, radix),
        "coarse",
        2.9,
        [(n3 + 2, *tile)],
        scratch,
        place,
        blocks,
    )
    scratch = [(n1 + 2, *held[1]), (n2 + 2, *held[2]), diffusivity.shape]
    scratch += [(n3 + 2, *held[2]), (n2 + 2, *held[1]), (n1 + 2, *held[0])]
    scratch += [(n2 + 4, *held[2]), (n1 + 4, *held[1]), (n0 + 2, *held[0])]
    scratch += [(n2 + 2, *held[2]), (n1 + 2, *held[1]), (n0, *held[0])]
    (correction,) = call(
        functools.partial(up_kernel, sizes),
        "up",
        3.0,
        [diffusivity.shape],
        scratch,
        place,
        [coarse, *received, *inner[2:], *outer, own0, turned, *borders],
        copies=CHUNKS,
        far_out=True,
    )
    return correction


def solution(mesh):
    in_specs = (P(None, "span", "width"),) * 3
    return jax.shard_map(
        on_device, mesh=mesh, in_specs=in_specs, out_specs=P(None, "span", "width"), check_vma=False
    )
```

```python
import functools

import jax
import jax.numpy as jnp
from jax import lax
from jax.experimental import pallas as pl
from jax.experimental.pallas import tpu as pltpu
from jax.sharding import PartitionSpec as P

LEVELS = 6
COARSE_SWEEPS = 3
LANES = 128
BORDER = 128
FRINGE = 4
SPREAD = 16
relax_weight = 0.8
f32 = jnp.float32
VMEM_LIMIT = 32 * 1024 * 1024
BYTES_A_MICRO = 3.69e6
CHUNKS = 4


class Sizes:
    def __init__(self, depth, extent_x, extent_y, span_count, width_count):
        self.depth, self.extent_x, self.extent_y = depth, extent_x, extent_y
        self.span_count, self.width_count = span_count, width_count
        self.sides = min(width_count - 1, 2)
        self.own = [(extent_y >> level) // LANES for level in range(3)]
        self.border = [self.sides, min(self.sides, 1), min(self.sides, 1)]
        self.held = [(self.own[level] + self.border[level]) * LANES for level in range(3)] + [LANES] * 3
        self.rows = [extent_x >> level for level in range(4)]
        self.slots = []
        start = 0
        for level in (0, 1, 1, 1, 2, 2, 2):
            self.slots.append((start, self.own[level]))
            start += self.own[level]
        self.tiles = start


def put(message, slot, row):
    start, tiles = slot
    for tile in range(tiles):
        message[start + tile] = row[:, tile * LANES : (tile + 1) * LANES]


class Arrived:
    def __init__(self, place, pair, forward, stride=1):
        self.even = place[0] // stride % 2 == 0
        self.first, self.second = (pair[0], pair[1]) if forward else (pair[1], pair[0])

    def __getitem__(self, index):
        return jnp.where(self.even, self.first[index], self.second[index])


def put_pair(place, pair, slot, next_row, prev_row, stride=1):
    even = place[0] // stride % 2 == 0
    put(pair[0], slot, jnp.where(even, next_row, prev_row))
    put(pair[1], slot, jnp.where(even, prev_row, next_row))


def get(message, slot):
    start, tiles = slot
    return [message[start + tile] for tile in range(tiles)]


def lane_at(shape):
    return lax.broadcasted_iota(jnp.int32, shape, len(shape) - 1)


def roll(value, steps, axis):
    return pltpu.roll(value, steps % value.shape[axis], axis=axis)


def reciprocal(value):
    return pltpu.reciprocal(value, approx=True)


def harmonic(first, second, guard):
    total = first + second
    if guard:
        total = jnp.maximum(total, 1e-3)
    return (2.0 * first) * second * reciprocal(total)


def split(value):
    high = value.astype(jnp.bfloat16)
    return high, (value - high.astype(f32)).astype(jnp.bfloat16)


def dot(halves, table):
    high, low = halves
    return jnp.dot(high, table, preferred_element_type=f32) + jnp.dot(low, table, preferred_element_type=f32)


def pair_table(fine, fine_dim, turn, weight):
    shape = (fine, LANES) if fine_dim == 0 else (LANES, fine)
    fine_at = lax.broadcasted_iota(jnp.int32, shape, fine_dim)
    coarse_at = lax.broadcasted_iota(jnp.int32, shape, 1 - fine_dim)
    if turn is not None:
        coarse_at = coarse_at - jnp.where(fine_at >= turn, LANES // 2, 0)
    return jnp.where(fine_at // 2 == coarse_at, weight, 0.0).astype(jnp.bfloat16)


def turns(sizes, place, level):
    if sizes.sides == 0:
        return []
    if level == 0:
        return [jnp.where(place[1] == 0, LANES, 0)] if sizes.sides == 1 else [LANES, 0]
    return [LANES // 2]


def transfer_plan(sizes, place, level, part):
    plan = []
    if level >= 3:
        return [((0, LANES), 0, 3 * LANES // 4)]
    if level == 2:
        return [((0, sizes.held[2]), 0, None)]
    own = sizes.own[level]
    if part != "border":
        plan += [((2 * LANES * tile, 2 * LANES * (tile + 1)), tile, None) for tile in range(own // 2)]
    if part != "own":
        for index, turn in enumerate(turns(sizes, place, level)):
            start = (own + index) * LANES
            plan.append(((start, start + LANES), own // 2, turn))
    return plan


def narrow(sizes, place, level, sums, target, rows, part="all", shift=0):
    depth = sums.shape[1]
    done = {}
    for (start, stop), tile, turn in transfer_plan(sizes, place, level, part):
        start, stop, tile = start - shift, stop - shift, tile - shift // (2 * LANES)
        columns = split(sums[0:rows, :, start:stop].reshape(rows * depth, stop - start))
        result = dot(columns, pair_table(stop - start, 0, turn, 0.25)).reshape(rows, depth, LANES)
        done[tile] = done[tile] + result if tile in done else result
    for tile, result in done.items():
        target[0:rows, :, tile * LANES : (tile + 1) * LANES] = result


def widen(sizes, place, level, coarse, target, rows):
    depth = coarse.shape[1]
    for (start, stop), tile, turn in transfer_plan(sizes, place, level, "all"):
        columns = split(coarse[0:rows, :, tile * LANES : (tile + 1) * LANES].reshape(rows * depth, LANES))
        result = dot(columns, pair_table(stop - start, 1, turn, 4.0))
        target[0:rows, :, start:stop] = result.reshape(rows, depth, stop - start)


class Joined:
    def __init__(self, inner, outer, first):
        self.inner, self.outer, self.first = inner, outer, first

    def find(self, row):
        place, count = row - self.first, 0 if self.inner is None else self.inner.shape[0]
        if 0 <= place < count:
            return self.inner, place
        return self.outer, row if place < 0 else row - count

    def __getitem__(self, row):
        array, place = self.find(row)
        return array[place]

    def __setitem__(self, row, value):
        array, place = self.find(row)
        array[place] = value


class Level:
    def __init__(self, sizes, level, inner, outer):
        self.n, self.halo = sizes.rows[level], 1 if level == 0 else 2
        counts = inner_rows(sizes, level)
        fx, fy, fz, *rest = parts(inner, counts)
        weight, source, smooth = (None, None, None) if level == 2 else (rest[0], None, rest[1])
        if level == 1:
            weight, source, smooth = rest
        others = [None] * 7 if outer is None else parts(outer, outer_rows(sizes, level))
        if level == 0 and outer is not None:
            others = [others[0], None, None, others[1], None, others[2], None]
        h = self.halo
        self.fx = Joined(fx, others[0], h)
        self.fy, self.fz = Joined(fy, others[1], h - 1), Joined(fz, others[2], h - 1)
        self.weight, self.source, self.smooth = (
            Joined(array, other, h) for array, other in zip((weight, source, smooth), others[3:6])
        )
        self.binding = others[6]

    def inner(self):
        first, last = self.halo, self.halo + self.n - 1
        return range(first + 1, last + 1), range(first, last + 1), range(first + 1, last)

    def outer(self):
        count = self.n + 2 * self.halo
        every = (range(1, count), range(1, count - 1), range(1, count - 1))
        return tuple([row for row in rows if row not in mine] for rows, mine in zip(every, self.inner()))


def inner_rows(sizes, level):
    n = sizes.rows[level]
    return [n - 1, n, n] + [[n - 2] * 2, [n - 2] * 3, []][level]


def outer_rows(sizes, level):
    n = sizes.rows[level]
    return [[2, 2, 2], [4, 2, 2, 4, 4, 4, n + 2], [4, 2, 2] + [n + 2] * 4][level]


def coefficients(sizes, place, level, conduct, binding, fx, fy, fz, weight, rows):
    guard = level > 0 or sizes.sides > 1
    for row in rows[0]:
        fx[row - 1] = harmonic(conduct(row - 1), conduct(row), guard)
    for row in rows[1]:
        mine = conduct(row)
        south = harmonic(mine, roll(mine, 1, 1), guard)
        if level == 0 and sizes.sides < 2:
            cut = 0 if sizes.sides == 0 else jnp.where(place[1] == 0, 0, sizes.extent_y)
            south = jnp.where(lane_at(mine.shape) == cut, 0.0, south)
        below = harmonic(mine, roll(mine, 1, 0), guard)
        fy[row - 1] = south
        fz[row - 1] = jnp.where(lax.broadcasted_iota(jnp.int32, mine.shape, 0) == 0, 0.0, below)
    for row in rows[2]:
        south, below = fy[row - 1], fz[row - 1]
        diagonal = fx[row - 1] + fx[row] + binding(row)
        diagonal = diagonal + (south + roll(south, -1, 1)) + (below + roll(below, -1, 0))
        if guard:
            diagonal = jnp.maximum(diagonal, 1e-6)
        weight[row - 1] = relax_weight * reciprocal(diagonal)


def sweep(first, last, field, binding, fx, fy, fz, emit):
    lower = fx[first - 1] * (field(first) - field(first - 1))
    for row in range(first, last + 1):
        mine = field(row)
        upper = fx[row] * (field(row + 1) - mine)
        south = fy[row - 1] * (mine - roll(mine, 1, 1))
        below = fz[row - 1] * (mine - roll(mine, 1, 0))
        across = (south - roll(south, -1, 1)) + (below - roll(below, -1, 0))
        emit(row, binding(row) * mine + (lower - upper) + across)
        lower = upper


def in_pairs(sums, slot_of):
    def add(row, value):
        slot, first = slot_of(row)
        if first:
            sums[slot] = value
        else:
            sums[slot] = sums[slot] + value

    return add


def parts(array, counts):
    views, start = [], 0
    for count in counts:
        views.append(array.at[start : start + count])
        start += count
    return views


def start_kernel(sizes, place, conduct, binding, own0, own1, own2, first, second, *refs):
    edges, sums = refs[: 2 * sizes.sides], refs[-1]
    n0, n1, n2 = sizes.rows[:3]
    for at, array in enumerate((conduct, binding)):
        own0[at] = jnp.swapaxes(array[...], 0, 1)
    for at in (0, 1):
        for row in range(n1):
            sums[at * n1 + row] = own0[at, 2 * row] + own0[at, 2 * row + 1]
    narrow(sizes, place, 0, sums, own1, 2 * n1, "own")
    for row in range(2 * n2):
        sums[row, :, : sizes.own[1] * LANES] = own1[2 * row] + own1[2 * row + 1]
    narrow(sizes, place, 1, sums, own2, 2 * n2, "own")
    ends = []
    for low, at1, at0 in ((n1 - 2, n1 - 1, n0 - 1), (0, 0, 0)):
        edge = n2 - 1 if at0 else 0
        rows = (own0[0, at0], own1[low], own1[low + 1], own1[n1 + at1])
        ends.append(rows + (own2[n2 - 2], own2[n2 - 1], own2[n2 + edge]))
    for slot, next_row, prev_row in zip(sizes.slots, *ends):
        put_pair(place, (first, second), slot, next_row, prev_row)
    for at in (0, 1):
        cut_edges(sizes, place, own0.at[at], edges[at * sizes.sides : (at + 1) * sizes.sides])


def cut_edges(sizes, place, array, edges):
    last = sizes.extent_y - BORDER
    if sizes.sides == 1:
        at = pl.multiple_of(jnp.where(place[1] == 0, last, 0), LANES)
        edges[0][...] = array[:, :, pl.ds(at, BORDER)]
    elif sizes.sides == 2:
        edges[0][...] = array[:, :, last:]
        edges[1][...] = array[:, :, :BORDER]


def turn_kernel(sizes, place, right_side, turned, *edges):
    turned[...] = jnp.swapaxes(right_side[...], 0, 1)
    cut_edges(sizes, place, turned, edges)


def message_row(sizes, place, level, slot, message, beside):
    start, tiles = slot
    row = get(message, slot)
    if sizes.sides == 1:
        left = place[1] != 0
        tile = beside[0][start + jnp.where(left, tiles - 1, 0)]
        if level > 0:
            reach = BORDER >> level
            lane = lane_at(tile.shape)
            first = jnp.where(left, LANES - reach, 0)
            tile = jnp.where((lane >= first) & (lane < first + reach), tile, 0.0)
        row.append(tile)
    elif sizes.sides == 2:
        right, left = beside[0][start], beside[1][start + tiles - 1]
        if level == 0:
            row += [right, left]
        else:
            reach = BORDER >> level
            lane = lane_at(right.shape)
            row.append(jnp.where(lane < reach, right, jnp.where(lane >= LANES - reach, left, 0.0)))
    return jnp.concatenate(row, axis=1)


def fringe_lanes(shape):
    lane = lane_at(shape)
    return (lane < FRINGE) | (lane >= LANES - FRINGE)


def fringes(sizes, rows):
    total = None
    for index, (level, row) in enumerate(rows):
        tile = row[:, sizes.own[level] * LANES :]
        tile = jnp.where(fringe_lanes(tile.shape), tile, 0.0)
        tile = roll(tile, SPREAD * index + SPREAD // 2, 1)
        total = tile if total is None else total + tile
    return total


def fringed_row(sizes, level, index, message):
    row = get(message, sizes.slots[index])
    if sizes.border[level]:
        if level == 0:
            row += [jnp.zeros(row[0].shape, f32)] * sizes.border[0]
        else:
            tile = roll(message[sizes.tiles], -(SPREAD * (index - 1) + SPREAD // 2), 1)
            row.append(jnp.where(fringe_lanes(tile.shape), tile, 0.0))
    return jnp.concatenate(row, axis=1)


def packing(count):
    return -(-count // 2)


def pack_rows(rows, target):
    half = LANES // 2
    lane = lane_at(rows[0].shape)
    for index in range(packing(len(rows))):
        held = jnp.where(lane < half, rows[2 * index], 0.0)
        if 2 * index + 1 < len(rows):
            held = jnp.where(lane < half, held, pltpu.roll(rows[2 * index + 1], half, axis=1))
        target[index] = held


def unpack_rows(sizes, place, tiles, count, others=()):
    half, reach = LANES // 2, BORDER >> 3
    lane = lane_at(tiles.shape[1:])
    rows = []
    for index in range(count):
        held = tiles[index // 2]
        row = jnp.where(lane < half, pltpu.roll(held, half, axis=1) if index % 2 else held, 0.0)
        for side, other in enumerate(others):
            first = LANES - reach if side else half
            if sizes.sides == 1:
                first = jnp.where(place[1] == 0, half, LANES - reach)
            beside = other[index // 2]
            beside = beside if index % 2 else pltpu.roll(beside, half, axis=1)
            row = jnp.where((lane >= first) & (lane < first + reach), beside, row)
        rows.append(row)
    return rows


def merge_into(sizes, place, stride, radix, arrays, source, conduct, binding, first, others=()):
    position = (place[0] // stride) % radix
    source[...] = jnp.zeros(source.shape, f32)
    for step, array in enumerate(arrays):
        at = (position ^ step) * stride
        rows = unpack_rows(sizes, place, array, 3 * stride + 2, [other[step] for other in others])
        for index, row in enumerate(rows[: stride + 2]):
            source[at + index] = source[at + index] + row
        for index in range(stride):
            conduct[at + index + first] = rows[stride + 2 + index]
            binding[at + index] = rows[2 * stride + 2 + index]


def merge_kernel(sizes, stride, radix, place, *refs):
    arrays, out, (source, conduct, binding) = refs[:radix], refs[radix], refs[radix + 1 :]
    merge_into(sizes, place, stride, radix, arrays, source, conduct, binding, 0)
    count = stride * radix
    rows = [source[row] for row in range(count + 2)]
    rows += [conduct[row] for row in range(count)] + [binding[row] for row in range(count)]
    pack_rows(rows, out)


def held_rows(sizes, owns, borders):
    def held_row(level, at, row):
        if level > 0:
            row = at * sizes.rows[level] + row
            return jnp.concatenate([owns[level][row], *(array[row] for array in borders[level])], axis=1)
        own = owns[3][row] if at == 2 else owns[0][at, row]
        sides = len(borders[0]) // 3
        return jnp.concatenate([own, *(array[row] for array in borders[0][at * sides : (at + 1) * sides])], axis=1)

    return held_row


def inner_kernel(sizes, place, *refs):
    s = sizes.sides
    owns, borders0, refs = refs[:4], refs[4 : 4 + 3 * s], refs[4 + 3 * s :]
    border1, border2, inner0, inner1, inner2, sums = refs
    n0, n1, n2 = sizes.rows[:3]
    if s:
        for row in range(2 * n1):
            for side in range(s):
                columns = slice(side * LANES, (side + 1) * LANES)
                at, low = row // n1, 2 * (row % n1)
                sums[row, :, columns] = borders0[at * s + side][low] + borders0[at * s + side][low + 1]
        narrow(sizes, place, 0, sums, border1, 2 * n1, "border", sizes.own[0] * LANES)
        for row in range(2 * n2):
            sums[row, :, :LANES] = border1[2 * row] + border1[2 * row + 1]
        narrow(sizes, place, 1, sums, border2, 2 * n2, "border", sizes.own[1] * LANES)
    held_row = held_rows(sizes, owns, [borders0, [border1][:s], [border2][:s]])
    levels = [Level(sizes, level, inner, None) for level, inner in enumerate((inner0, inner1, inner2))]
    for index, level in enumerate(levels):
        conduct = lambda row, index=index, level=level: held_row(index, 0, row - level.halo)
        bound = lambda row, index=index, level=level: held_row(index, 1, row - level.halo)
        coefficients(
            sizes, place, index, conduct, bound, level.fx, level.fy, level.fz, level.weight, level.inner()
        )
        if index == 0:
            right = lambda row: held_row(0, 2, row - 1)
            for row in range(2, n0):
                level.smooth[row - 1] = level.weight[row - 1] * right(row)
            add = in_pairs(sums, lambda row: ((row - 3) // 2, row % 2 == 1))
            field = lambda row, level=level: level.smooth[row - 1]
            emit = lambda row, value: add(row, right(row) - value)
            sweep(3, n0 - 2, field, bound, level.fx, level.fy, level.fz, emit)
        if index == 1:
            narrow(sizes, place, 0, sums, level.source.inner, n1 - 2)
            for row in range(2, n1):
                level.smooth[row] = level.weight[row] * level.source[row]


def down_kernel(sizes, place, *refs):
    s = sizes.sides
    owns, borders0, refs = refs[:4], refs[4 : 4 + 3 * s], refs[4 + 3 * s :]
    pairs_of = [refs[2 * index : 2 * index + 2] for index in range(1 + s)]
    refs = refs[2 * (1 + s) :]
    from_prev, *beside_prev = (Arrived(place, pair, 0) for pair in pairs_of)
    from_next, *beside_next = (Arrived(place, pair, 1) for pair in pairs_of)
    (border1, border2), inners, refs = refs[:2], refs[2:5], refs[5:]
    outers, contribution, with_far, ups, far, refs = refs[:3], refs[3], refs[4], refs[5:7], refs[7], refs[8:]
    level3, sums = refs
    slots = sizes.slots
    n0, n1, n2 = sizes.rows[:3]
    levels = [Level(sizes, index, inner, outer) for index, (inner, outer) in enumerate(zip(inners, outers))]
    held_row = held_rows(sizes, owns, [borders0, [border1][:s], [border2][:s]])

    def prev_row(level, index):
        return message_row(sizes, place, level, slots[index], from_prev, beside_prev)

    def next_row(level, index):
        return message_row(sizes, place, level, slots[index], from_next, beside_next)

    def conduct0(row):
        if row == 0:
            return prev_row(0, 0)
        if row == n0 + 1:
            return next_row(0, 0)
        return held_row(0, 0, row - 1)

    zero = jnp.zeros((sizes.depth, sizes.held[0]), f32)
    level = levels[0]
    bound0 = lambda row: held_row(0, 1, row - 1)
    right = lambda row: held_row(0, 2, row - 1)
    coefficients(
        sizes, place, 0, conduct0, bound0, level.fx, level.fy, level.fz, level.weight, level.outer()
    )
    for row in (1, n0):
        level.smooth[row - 1] = level.weight[row - 1] * right(row)
    first_slot = lambda row: (row + 1) // 2
    add = in_pairs(
        sums,
        lambda row: (first_slot(row) - (n1 - 2 if row > n0 // 2 else 0), row % 2 == 1 or row == 0),
    )
    field = lambda row, level=level: level.smooth[row - 1] if 0 < row < n0 + 1 else zero
    emit = lambda row, value: add(row, right(row) - value)
    add(0, level.fx[0] * field(1))
    sweep(1, 2, field, bound0, level.fx, level.fy, level.fz, emit)
    sweep(n0 - 1, n0, field, bound0, level.fx, level.fy, level.fz, emit)
    add(n0 + 1, level.fx[n0] * field(n0))
    fine_held = sizes.held[0]
    for index, first in ((1, 1), (2, 4)):
        level, n = levels[index], sizes.rows[index]
        held = sizes.held[index]
        narrow(
            sizes, place, index - 1, sums.at[:, :, :fine_held], level.source.outer, level.source.outer.shape[0]
        )
        binding = level.binding
        binding[0] = prev_row(index, first + 2)
        binding[n + 1] = next_row(index, first + 2)
        for row in range(n):
            binding[row + 1] = held_row(index, 1, row)

        def conduct(row, n=n, index=index, first=first):
            if row < 2:
                return prev_row(index, first + row)
            if row >= n + 2:
                return next_row(index, first + row - n - 2)
            return held_row(index, 0, row - 2)

        bound = lambda row, binding=binding: binding[row - 1]
        coefficients(
            sizes, place, index, conduct, bound, level.fx, level.fy, level.fz, level.weight, level.outer()
        )
        for row in level.outer()[2] if index == 1 else range(1, n + 3):
            level.smooth[row - 1] = level.weight[row - 1] * level.source[row - 1]
        zero = jnp.zeros((sizes.depth, held), f32)
        field = lambda row, level=level, n=n, zero=zero: level.smooth[row - 1] if 0 < row < n + 3 else zero
        add = in_pairs(sums.at[:, :, :held], lambda row: (row // 2, row % 2 == 0))
        emit = lambda row, value, level=level, add=add: add(row, level.source[row - 1] - value)
        add(0, level.fx[0] * field(1))
        sweep(1, n + 2, field, bound, level.fx, level.fy, level.fz, emit)
        add(n + 3, level.fx[n + 2] * field(n + 2))
        fine_held = held
    narrow(sizes, place, 2, sums.at[:, :, : sizes.held[2]], level3, 3)
    for at in (0, 1):
        sums[at, :, : sizes.held[2]] = held_row(2, at, 0) + held_row(2, at, 1)
    narrow(sizes, place, 2, sums.at[:, :, : sizes.held[2]], level3.at[3:5], 2)
    tiles = packing(5)
    pack_rows([level3[row] for row in range(5)], contribution)
    with_far[0:tiles] = contribution[...]
    v0, s1, v1 = levels[0].smooth, levels[1].source, levels[1].smooth
    s2, v2 = levels[2].source, levels[2].smooth
    next_rows = (v0[n0 - 1], s1[n1], s1[n1 + 1], v1[n1 - 1], s2[n2], s2[n2 + 1], v2[n2 - 1])
    prev_rows = (v0[0], s1[1], s1[0], v1[2], s2[1], s2[0], v2[2])
    for slot, next_row, prev_row in zip(slots, next_rows, prev_rows):
        put_pair(place, ups, slot, next_row, prev_row)
    if s:
        ends = [fringes(sizes, list(zip((1, 1, 1, 2, 2, 2), rows[1:]))) for rows in (next_rows, prev_rows)]
        put_pair(place, ups, (sizes.tiles, 1), *ends)
    far_tiles = sizes.held[2] // LANES
    put_pair(place, (with_far.at[tiles : tiles + far_tiles], far), (0, far_tiles), v2[n2 + 1], v2[0], 2)


def relax(count, field, refs_of, source, target):
    fx, fy, fz, weight, binding = refs_of

    def update(row, value):
        target(row, field(row) + weight[row - 1] * (source(row) - value))

    sweep(1, count - 2, field, binding, fx, fy, fz, update)


def store(array, first):
    def put_row(row, value):
        array[row - first] = value

    return put_row


def coarse_kernel(sizes, stride, radix, place, *refs):
    blocks, refs = refs[:radix], refs[radix:]
    others, refs = [refs[side * radix : (side + 1) * radix] for side in range(sizes.sides)], refs[sizes.sides * radix :]
    out, merged, sums = refs[:3]
    coarse = [refs[3 + 9 * index : 12 + 9 * index] for index in range(3)]
    total = sizes.span_count
    merge_into(sizes, place, stride, radix, blocks, merged, coarse[0][4], coarse[0][5], 1, others)
    zero = jnp.zeros((sizes.depth, LANES), f32)
    for index in range(3):
        level = 3 + index
        fx, fy, fz, weight, conduct, binding, source, smooth, iterate = coarse[index]
        count = total >> index
        for array in (conduct, smooth, iterate):
            array[0] = zero
            array[count + 1] = zero
        if index == 0:
            source = merged.at[1 : count + 1]
        bound = lambda row, binding=binding: binding[row - 1]
        at_row = lambda row, conduct=conduct: conduct[row]
        every = (range(1, count + 2), range(1, count + 1), range(1, count + 1))
        coefficients(sizes, place, level, at_row, bound, fx, fy, fz, weight, every)
        for row in range(count):
            smooth[row + 1] = weight[row] * source[row]
        if index < 2:
            conduct_next, binding_next, source_next = coarse[index + 1][4:7]
            half = count // 2
            for row in range(half):
                sums[row, :, :LANES] = conduct[2 * row + 1] + conduct[2 * row + 2]
            narrow(sizes, place, level, sums, conduct_next.at[1 : half + 1], half)
            for row in range(half):
                sums[row, :, :LANES] = binding[2 * row] + binding[2 * row + 1]
            narrow(sizes, place, level, sums, binding_next, half)

            def add(row, value, source=source):
                value = source[row - 1] - value
                slot = (row - 1) // 2
                if row % 2 == 1:
                    sums[slot, :, :LANES] = value
                else:
                    sums[slot, :, :LANES] = sums[slot, :, :LANES] + value

            sweep(1, count, lambda row, smooth=smooth: smooth[row], bound, fx, fy, fz, add)
            narrow(sizes, place, level, sums, source_next, half)

    fx, fy, fz, weight, conduct, binding, source, smooth, iterate = coarse[2]
    held, other = smooth, iterate
    for _ in range(COARSE_SWEEPS - 1):
        field = lambda row, held=held: held[row]
        mine = lambda row: source[row - 1]
        bound = lambda row: binding[row - 1]
        relax((total >> 2) + 2, field, (fx, fy, fz, weight, bound), mine, store(other, 0))
        held, other = other, held
    for index in (1, 0):
        fx, fy, fz, weight, conduct, binding, source, smooth, iterate = coarse[index]
        if index == 0:
            source = merged.at[1 : total + 1]
        count = total >> index
        widen(sizes, place, 3 + index, held.at[1 : count // 2 + 1], sums, count // 2)
        for row in range(count):
            smooth[row + 1] = smooth[row + 1] + sums[row // 2, :, :LANES]
        field = lambda row, smooth=smooth: smooth[row]
        mine = lambda row, source=source: source[row - 1]
        bound = lambda row, binding=binding: binding[row - 1]
        relax(count + 2, field, (fx, fy, fz, weight, bound), mine, store(iterate, 0))
        held = iterate

    out[...] = held[pl.ds(place[0], 3)]


def up_kernel(sizes, place, coarse, *refs):
    s = sizes.sides
    pair, far_pair, inners, outers, owns = refs[:2], refs[2:4], refs[4:7], refs[7:10], refs[10:12]
    levels = [Level(sizes, index, inner, outer) for index, (inner, outer) in enumerate(zip(inners, outers))]
    from_prev, from_next = (Arrived(place, pair, forward) for forward in (0, 1))
    tiles = packing(5)
    far_pair = (far_pair[0].at[tiles : tiles + sizes.held[2] // LANES], far_pair[1])
    fars = [Arrived(place, far_pair, forward, 2) for forward in (0, 1)]
    borders0, out, refs = refs[12 : 12 + 3 * s], refs[12 + 3 * s], refs[13 + 3 * s :]
    total1, total2, result = refs[:3]
    over2, over1, over0, lift2, lift1, lift0, it2, it1, it0, semaphores = refs[3:]
    slots = sizes.slots
    n0, n1, n2 = sizes.rows[:3]
    width = sizes.own[0] * LANES

    widen(sizes, place, 2, coarse, over2, 3)
    for level, first, totals, over, lift, target, upper in (
        (2, 4, total2, over2, lift2, it2, over1),
        (1, 1, total1, over1, lift1, it1, over0),
    ):
        n, kept = sizes.rows[level], levels[level]
        fx, fy, fz, weight, binding = kept.fx, kept.fy, kept.fz, kept.weight, kept.binding
        own, smooth = kept.source, kept.smooth
        edge = {}
        for row, message, index in (
            (1, from_prev, first),
            (2, from_prev, first + 1),
            (n + 2, from_next, first),
            (n + 1, from_next, first + 1),
        ):
            value = edge.get(row, own[row - 1])
            edge[row] = value + fringed_row(sizes, level, index, message)
        for row, value in edge.items():
            totals[row - 1] = value
        for row in range(n + 4):
            if row in (0, n + 3):
                value = fringed_row(sizes, level, first + 2, from_next if row else from_prev)
                if level == 2:
                    far = fars[1 if row else 0]
                    value = value + jnp.concatenate(get(far, (0, sizes.held[2] // LANES)), axis=1)
            elif row in edge:
                value = weight[row - 1] * totals[row - 1]
            else:
                value = smooth[row - 1]
            lift[row] = value + over[row // 2]
        field = lambda row, lift=lift: lift[row]
        mine = lambda row, own=own, totals=totals, edge=edge: (totals if row in edge else own)[row - 1]
        bound = lambda row, binding=binding: binding[row - 1]
        relax(n + 4, field, (fx, fy, fz, weight, bound), mine, store(target, 1))
        widen(sizes, place, level - 1, target, upper, n + 2)

    held_row = held_rows(sizes, [owns[0], None, None, owns[1]], [borders0])
    fx, fy, fz, weight, v0 = levels[0].fx, levels[0].fy, levels[0].fz, levels[0].weight, levels[0].smooth
    lift0[0] = fringed_row(sizes, 0, 0, from_prev) + over0[0]
    lift0[n0 + 1] = fringed_row(sizes, 0, 0, from_next) + over0[n1 + 1]
    for row in range(1, n0 + 1):
        lift0[row] = v0[row - 1] + over0[(row + 1) // 2]
    field = lambda row: lift0[row]
    bound = lambda row: held_row(0, 1, row - 1)
    relax(n0 + 2, field, (fx, fy, fz, weight, bound), lambda row: held_row(0, 2, row - 1), store(it0, 1))
    step = sizes.depth // CHUNKS
    copies = []
    for chunk in range(CHUNKS):
        part = slice(chunk * step, (chunk + 1) * step)
        result[part] = jnp.swapaxes(it0[:, part, :width], 0, 1)
        copies.append(pltpu.make_async_copy(result.at[part], out.at[part], semaphores.at[chunk]))
        copies[-1].start()
    for copy in copies:
        copy.wait()


def call(body, name, micros, outputs, scratch, place, inputs, copies=0, far_out=False):
    near, far = pl.BlockSpec(memory_space=pltpu.VMEM), pl.BlockSpec(memory_space=pl.ANY)
    scratch = [pltpu.VMEM(shape, f32) for shape in scratch]
    if copies:
        scratch.append(pltpu.SemaphoreType.DMA((copies,)))
    return pl.pallas_call(
        body,
        name=name,
        out_shape=[jax.ShapeDtypeStruct(shape, f32) for shape in outputs],
        in_specs=[pl.BlockSpec(memory_space=pltpu.SMEM)] + [near] * len(inputs),
        out_specs=[far if far_out else near] * len(outputs),
        scratch_shapes=scratch,
        cost_estimate=pl.CostEstimate(flops=int(micros * 1.15e9), bytes_accessed=int(micros * BYTES_A_MICRO), transcendentals=0),
        compiler_params=pltpu.CompilerParams(vmem_limit_bytes=VMEM_LIMIT),
    )(place, *inputs)


def along(value, axis, steps):
    count = lax.axis_size(axis)
    initial, last = max(0, -steps), min(count, count - steps)
    return lax.ppermute(value, axis, [(source, source + steps) for source in range(initial, last)])


def beside(values, sizes):
    if sizes.sides == 1:
        return [[lax.ppermute(value, "width", [(0, 1), (1, 0)]) for value in values]]
    if sizes.sides == 2:
        return [[along(value, "width", steps) for value in values] for steps in (-1, 1)]
    return []


def edge_columns(edges, sizes):
    if sizes.sides == 1:
        return [lax.ppermute(edges[0], "width", [(0, 1), (1, 0)])]
    if sizes.sides == 2:
        return [along(edges[1], "width", -1), along(edges[0], "width", 1)]
    return []


def stages(count):
    stride = 1
    while stride < count:
        radix = 4 if count // stride % 4 == 0 else 2
        yield stride, radix
        stride *= radix


def swap(value, stride, radix, others=None):
    count = lax.axis_size("span")
    others = others or {}
    return [value] + [
        lax.ppermute(others.get(step, value), "span", [(device, device ^ step * stride) for device in range(count)])
        for step in range(1, radix)
    ]


def exchange(pair, stride):
    count = lax.axis_size("span")
    routes = [[], []]
    for low in range(count - stride):
        routes[low // stride % 2] += [(low, low + stride), (low + stride, low)]
    return [None if value is None else lax.ppermute(value, "span", route) for value, route in zip(pair, routes)]


def on_device(right_side, diffusivity, reaction):
    depth, extent_x, extent_y = diffusivity.shape
    sizes = Sizes(depth, extent_x, extent_y, lax.axis_size("span"), lax.axis_size("width"))
    place = jnp.stack([lax.axis_index("span"), lax.axis_index("width")]).astype(jnp.int32)
    n0, n1, n2, n3 = sizes.rows
    s = sizes.sides
    tile = (depth, LANES)
    own = [(depth, count * LANES) for count in sizes.own]
    held = [(depth, count) for count in sizes.held]
    down_message = (sizes.tiles, *tile)
    up_message = (sizes.tiles + 1, *tile)
    own0, own1, own2, first, second, *edges = call(
        functools.partial(start_kernel, sizes),
        "start",
        1.1,
        [(2, n0, *own[0]), (2 * n1, *own[1]), (2 * n2, *own[2]), down_message, down_message]
        + [(n0, depth, BORDER)] * 2 * s,
        [(2 * n1, *own[0])],
        place,
        [diffusivity, reaction],
    )
    borders = edge_columns(edges[:s], sizes) + edge_columns(edges[s:], sizes)
    halos = exchange([first, second], 1)
    turned, *edges = call(
        functools.partial(turn_kernel, sizes),
        "turn",
        0.7,
        [(n0, *own[0])] + [(n0, depth, BORDER)] * s,
        [],
        place,
        [right_side],
    )
    borders += edge_columns(edges, sizes)
    plan = list(stages(sizes.span_count))

    part = packing(5)
    far = (sizes.held[2] // LANES, *tile)
    inners = [(sum(inner_rows(sizes, level)), *held[level]) for level in range(3)]
    outers = [(sum(outer_rows(sizes, level)), *held[level]) for level in range(3)]
    inner = call(
        functools.partial(inner_kernel, sizes),
        "inner",
        0.5,
        [(2 * n1, *tile), (2 * n2, *tile), *inners],
        [(2 * n1, *held[0])],
        place,
        [own0, own1, own2, turned, *borders],
    )
    halos, inner = lax.optimization_barrier((halos, inner))
    sides = beside(halos, sizes)
    downs = call(
        functools.partial(down_kernel, sizes),
        "down",
        2.5,
        [*outers, (part, *tile), (part + far[0], *tile), up_message, up_message, far],
        [(5, *tile), (n1 + 2, *held[0])],
        place,
        [own0, own1, own2, turned, *borders, *halos, *sum(sides, []), *inner],
    )
    outer, blocks, with_far, ups, far_second = downs[:3], downs[3], downs[4], list(downs[5:7]), downs[7]
    far_rows = None
    for stride, radix in plan[:-1]:
        count = stride * radix
        if far_rows is None:
            blocks = swap(blocks, stride, radix, {2: with_far})
            far_rows = [blocks[2], exchange([None, far_second], 2)[1]]
            blocks, ups[0] = lax.optimization_barrier((blocks, ups[0]))
        else:
            blocks = swap(blocks, stride, radix)
        (blocks,) = call(
            functools.partial(merge_kernel, sizes, stride, radix),
            "merge",
            0.9,
            [(packing(3 * count + 2), *tile)],
            [(count + 2, *tile), (count, *tile), (count, *tile)],
            place,
            blocks,
        )
    stride, radix = plan[-1]
    blocks = swap(blocks, stride, radix)
    received = lax.optimization_barrier([exchange([ups[0], None], 1)[0], ups[1]])
    received = [received[0], exchange([None, received[1]], 1)[1]] + far_rows
    scratch = [(sizes.span_count + 2, *tile), (max(sizes.span_count // 2, 2), *tile)]
    for index in range(3):
        count = sizes.span_count >> index
        scratch += [(count + 1, *tile)] + [(count, *tile)] * 3 + [(count + 2, *tile)] + [(count, *tile)] * 2
        scratch += [(count + 2, *tile)] * 2
    blocks, received[3] = lax.optimization_barrier((blocks, received[3]))
    (coarse,) = call(
        functools.partial(coarse_kernel, sizes, stride, radix),
        "coarse",
        0.7,
        [(n3 + 2, *tile)],
        scratch,
        place,
        [*blocks, *sum(beside(blocks, sizes), [])],
    )
    scratch = [(n1 + 2, *held[1]), (n2 + 2, *held[2]), diffusivity.shape]
    scratch += [(n3 + 2, *held[2]), (n2 + 2, *held[1]), (n1 + 2, *held[0])]
    scratch += [(n2 + 4, *held[2]), (n1 + 4, *held[1]), (n0 + 2, *held[0])]
    scratch += [(n2 + 2, *held[2]), (n1 + 2, *held[1]), (n0, *held[0])]
    (correction,) = call(
        functools.partial(up_kernel, sizes),
        "up",
        3.0,
        [diffusivity.shape],
        scratch,
        place,
        [coarse, *received, *inner[2:], *outer, own0, turned, *borders],
        copies=CHUNKS,
        far_out=True,
    )
    return correction


def solution(mesh):
    in_specs = (P(None, "span", "width"),) * 3
    return jax.shard_map(
        on_device, mesh=mesh, in_specs=in_specs, out_specs=P(None, "span", "width"), check_vma=False
    )
```

```python
import functools

import jax
import jax.numpy as jnp
from jax import lax
from jax.experimental import pallas as pl
from jax.experimental.pallas import tpu as pltpu
from jax.sharding import PartitionSpec as P

LEVELS = 6
COARSE_SWEEPS = 3
LANES = 128
BORDER = 128
FRINGE = 4
SPREAD = 16
relax_weight = 0.8
f32 = jnp.float32
VMEM_LIMIT = 32 * 1024 * 1024
BYTES_A_MICRO = 3.69e6
CHUNKS = 4


class Sizes:
    def __init__(self, depth, extent_x, extent_y, span_count, width_count):
        self.depth, self.extent_x, self.extent_y = depth, extent_x, extent_y
        self.span_count, self.width_count = span_count, width_count
        self.sides = min(width_count - 1, 2)
        self.own = [(extent_y >> level) // LANES for level in range(3)]
        self.border = [self.sides, min(self.sides, 1), min(self.sides, 1)]
        self.held = [(self.own[level] + self.border[level]) * LANES for level in range(3)] + [LANES] * 3
        self.rows = [extent_x >> level for level in range(4)]
        self.slots = []
        start = 0
        for level in (0, 1, 1, 1, 2, 2, 2):
            self.slots.append((start, self.own[level]))
            start += self.own[level]
        self.tiles = start
        self.up_slots = []
        start = 0
        for level in (0, 1, 1, 2, 2, 2):
            self.up_slots.append((start, self.own[level]))
            start += self.own[level]
        self.up_tiles = start


def put(message, slot, row):
    start, tiles = slot
    for tile in range(tiles):
        message[start + tile] = row[:, tile * LANES : (tile + 1) * LANES]


class Arrived:
    def __init__(self, place, pair, forward, stride=1):
        self.even = place[0] // stride % 2 == 0
        self.first, self.second = (pair[0], pair[1]) if forward else (pair[1], pair[0])

    def __getitem__(self, index):
        return jnp.where(self.even, self.first[index], self.second[index])


def put_pair(place, pair, slot, next_row, prev_row, stride=1):
    even = place[0] // stride % 2 == 0
    put(pair[0], slot, jnp.where(even, next_row, prev_row))
    put(pair[1], slot, jnp.where(even, prev_row, next_row))


def get(message, slot):
    start, tiles = slot
    return [message[start + tile] for tile in range(tiles)]


def lane_at(shape):
    return lax.broadcasted_iota(jnp.int32, shape, len(shape) - 1)


def roll(value, steps, axis):
    return pltpu.roll(value, steps % value.shape[axis], axis=axis)


def reciprocal(value):
    return pltpu.reciprocal(value, approx=True)


def harmonic(first, second, guard):
    total = first + second
    if guard:
        total = jnp.maximum(total, 1e-3)
    return (2.0 * first) * second * reciprocal(total)


def split(value):
    high = value.astype(jnp.bfloat16)
    return high, (value - high.astype(f32)).astype(jnp.bfloat16)


def dot(halves, table):
    high, low = halves
    return jnp.dot(high, table, preferred_element_type=f32) + jnp.dot(low, table, preferred_element_type=f32)


def pair_table(fine, fine_dim, turn, weight):
    shape = (fine, LANES) if fine_dim == 0 else (LANES, fine)
    fine_at = lax.broadcasted_iota(jnp.int32, shape, fine_dim)
    coarse_at = lax.broadcasted_iota(jnp.int32, shape, 1 - fine_dim)
    if turn is not None:
        coarse_at = coarse_at - jnp.where(fine_at >= turn, LANES // 2, 0)
    return jnp.where(fine_at // 2 == coarse_at, weight, 0.0).astype(jnp.bfloat16)


def turns(sizes, place, level):
    if sizes.sides == 0:
        return []
    if level == 0:
        return [jnp.where(place[1] == 0, LANES, 0)] if sizes.sides == 1 else [LANES, 0]
    return [LANES // 2]


def transfer_plan(sizes, place, level, part):
    plan = []
    if level >= 3:
        return [((0, LANES), 0, 3 * LANES // 4)]
    if level == 2:
        return [((0, sizes.held[2]), 0, None)]
    own = sizes.own[level]
    if part != "border":
        plan += [((2 * LANES * tile, 2 * LANES * (tile + 1)), tile, None) for tile in range(own // 2)]
    if part != "own":
        for index, turn in enumerate(turns(sizes, place, level)):
            start = (own + index) * LANES
            plan.append(((start, start + LANES), own // 2, turn))
    return plan


def narrow(sizes, place, level, sums, target, rows, part="all", shift=0):
    depth = sums.shape[1]
    done = {}
    for (start, stop), tile, turn in transfer_plan(sizes, place, level, part):
        start, stop, tile = start - shift, stop - shift, tile - shift // (2 * LANES)
        columns = split(sums[0:rows, :, start:stop].reshape(rows * depth, stop - start))
        result = dot(columns, pair_table(stop - start, 0, turn, 0.25)).reshape(rows, depth, LANES)
        done[tile] = done[tile] + result if tile in done else result
    for tile, result in done.items():
        target[0:rows, :, tile * LANES : (tile + 1) * LANES] = result


def widen(sizes, place, level, coarse, target, rows):
    depth = coarse.shape[1]
    for (start, stop), tile, turn in transfer_plan(sizes, place, level, "all"):
        columns = split(coarse[0:rows, :, tile * LANES : (tile + 1) * LANES].reshape(rows * depth, LANES))
        result = dot(columns, pair_table(stop - start, 1, turn, 4.0))
        target[0:rows, :, start:stop] = result.reshape(rows, depth, stop - start)


class Joined:
    def __init__(self, inner, outer, first):
        self.inner, self.outer, self.first = inner, outer, first

    def find(self, row):
        place, count = row - self.first, 0 if self.inner is None else self.inner.shape[0]
        if 0 <= place < count:
            return self.inner, place
        return self.outer, row if place < 0 else row - count

    def __getitem__(self, row):
        array, place = self.find(row)
        return array[place]

    def __setitem__(self, row, value):
        array, place = self.find(row)
        array[place] = value


class Level:
    def __init__(self, sizes, level, inner, outer):
        self.n, self.halo = sizes.rows[level], 1 if level == 0 else 2
        counts = inner_rows(sizes, level)
        fx, fy, fz, *rest = parts(inner, counts)
        weight, source, smooth = (None, None, None) if level == 2 else (rest[0], None, rest[1])
        if level == 1:
            weight, source, smooth = rest
        others = [None] * 7 if outer is None else parts(outer, outer_rows(sizes, level))
        if level == 0 and outer is not None:
            others = [others[0], None, None, others[1], None, others[2], None]
        h = self.halo
        self.fx = Joined(fx, others[0], h)
        self.fy, self.fz = Joined(fy, others[1], h - 1), Joined(fz, others[2], h - 1)
        self.weight, self.source, self.smooth = (
            Joined(array, other, h) for array, other in zip((weight, source, smooth), others[3:6])
        )
        self.binding = others[6]

    def inner(self):
        first, last = self.halo, self.halo + self.n - 1
        return range(first + 1, last + 1), range(first, last + 1), range(first + 1, last)

    def outer(self):
        count = self.n + 2 * self.halo
        every = (range(1, count), range(1, count - 1), range(1, count - 1))
        return tuple([row for row in rows if row not in mine] for rows, mine in zip(every, self.inner()))


def inner_rows(sizes, level):
    n = sizes.rows[level]
    return [n - 1, n, n] + [[n - 2] * 2, [n - 2] * 3, []][level]


def outer_rows(sizes, level):
    n = sizes.rows[level]
    return [[2, 2, 2], [4, 2, 2, 4, 4, 4, n + 2], [4, 2, 2] + [n + 2] * 4][level]


def coefficients(sizes, place, level, conduct, binding, fx, fy, fz, weight, rows):
    guard = level > 0 or sizes.sides > 1
    for row in rows[0]:
        fx[row - 1] = harmonic(conduct(row - 1), conduct(row), guard)
    for row in rows[1]:
        mine = conduct(row)
        south = harmonic(mine, roll(mine, 1, 1), guard)
        if level == 0 and sizes.sides < 2:
            cut = 0 if sizes.sides == 0 else jnp.where(place[1] == 0, 0, sizes.extent_y)
            south = jnp.where(lane_at(mine.shape) == cut, 0.0, south)
        below = harmonic(mine, roll(mine, 1, 0), guard)
        fy[row - 1] = south
        fz[row - 1] = jnp.where(lax.broadcasted_iota(jnp.int32, mine.shape, 0) == 0, 0.0, below)
    for row in rows[2]:
        south, below = fy[row - 1], fz[row - 1]
        diagonal = fx[row - 1] + fx[row] + binding(row)
        diagonal = diagonal + (south + roll(south, -1, 1)) + (below + roll(below, -1, 0))
        if guard:
            diagonal = jnp.maximum(diagonal, 1e-6)
        weight[row - 1] = relax_weight * reciprocal(diagonal)


def sweep(first, last, field, binding, fx, fy, fz, emit):
    lower = fx[first - 1] * (field(first) - field(first - 1))
    for row in range(first, last + 1):
        mine = field(row)
        upper = fx[row] * (field(row + 1) - mine)
        south = fy[row - 1] * (mine - roll(mine, 1, 1))
        below = fz[row - 1] * (mine - roll(mine, 1, 0))
        across = (south - roll(south, -1, 1)) + (below - roll(below, -1, 0))
        emit(row, binding(row) * mine + (lower - upper) + across)
        lower = upper


def in_pairs(sums, slot_of):
    def add(row, value):
        slot, first = slot_of(row)
        if first:
            sums[slot] = value
        else:
            sums[slot] = sums[slot] + value

    return add


def parts(array, counts):
    views, start = [], 0
    for count in counts:
        views.append(array.at[start : start + count])
        start += count
    return views


def start_kernel(sizes, place, conduct, binding, own0, own1, own2, first, second, *refs):
    edges, sums = refs[: 2 * sizes.sides], refs[-1]
    n0, n1, n2 = sizes.rows[:3]
    for at, array in enumerate((conduct, binding)):
        own0[at] = jnp.swapaxes(array[...], 0, 1)
    for at in (0, 1):
        for row in range(n1):
            sums[at * n1 + row] = own0[at, 2 * row] + own0[at, 2 * row + 1]
    narrow(sizes, place, 0, sums, own1, 2 * n1, "own")
    for row in range(2 * n2):
        sums[row, :, : sizes.own[1] * LANES] = own1[2 * row] + own1[2 * row + 1]
    narrow(sizes, place, 1, sums, own2, 2 * n2, "own")
    ends = []
    for low, at1, at0 in ((n1 - 2, n1 - 1, n0 - 1), (0, 0, 0)):
        edge = n2 - 1 if at0 else 0
        rows = (own0[0, at0], own1[low], own1[low + 1], own1[n1 + at1])
        ends.append(rows + (own2[n2 - 2], own2[n2 - 1], own2[n2 + edge]))
    for slot, next_row, prev_row in zip(sizes.slots, *ends):
        put_pair(place, (first, second), slot, next_row, prev_row)
    for at in (0, 1):
        cut_edges(sizes, place, own0.at[at], edges[at * sizes.sides : (at + 1) * sizes.sides])


def cut_edges(sizes, place, array, edges):
    last = sizes.extent_y - BORDER
    if sizes.sides == 1:
        at = pl.multiple_of(jnp.where(place[1] == 0, last, 0), LANES)
        edges[0][...] = array[:, :, pl.ds(at, BORDER)]
    elif sizes.sides == 2:
        edges[0][...] = array[:, :, last:]
        edges[1][...] = array[:, :, :BORDER]


def turn_kernel(sizes, place, right_side, turned, *edges):
    turned[...] = jnp.swapaxes(right_side[...], 0, 1)
    cut_edges(sizes, place, turned, edges)


def message_row(sizes, place, level, slot, message, beside):
    start, tiles = slot
    row = get(message, slot)
    if sizes.sides == 1:
        left = place[1] != 0
        tile = beside[0][start + jnp.where(left, tiles - 1, 0)]
        if level > 0:
            reach = BORDER >> level
            lane = lane_at(tile.shape)
            first = jnp.where(left, LANES - reach, 0)
            tile = jnp.where((lane >= first) & (lane < first + reach), tile, 0.0)
        row.append(tile)
    elif sizes.sides == 2:
        right, left = beside[0][start], beside[1][start + tiles - 1]
        if level == 0:
            row += [right, left]
        else:
            reach = BORDER >> level
            lane = lane_at(right.shape)
            row.append(jnp.where(lane < reach, right, jnp.where(lane >= LANES - reach, left, 0.0)))
    return jnp.concatenate(row, axis=1)


def fringe_lanes(shape):
    lane = lane_at(shape)
    return (lane < FRINGE) | (lane >= LANES - FRINGE)


def fringes(sizes, rows):
    total = None
    for index, (level, row) in enumerate(rows):
        border = row[:, sizes.own[level] * LANES :]
        tile = border[:, :LANES]
        lane = lane_at(tile.shape)
        if border.shape[1] > LANES:
            tile = jnp.where(lane < FRINGE, tile, border[:, LANES:])
        tile = jnp.where((lane < FRINGE) | (lane >= LANES - FRINGE), tile, 0.0)
        tile = roll(tile, SPREAD * index + SPREAD // 2, 1)
        total = tile if total is None else total + tile
    return total


def fringed_row(sizes, level, index, message):
    row = get(message, sizes.up_slots[index])
    if sizes.border[level]:
        tile = roll(message[sizes.up_tiles], -(SPREAD * index + SPREAD // 2), 1)
        lane = lane_at(tile.shape)
        right, left = jnp.where(lane < FRINGE, tile, 0.0), jnp.where(lane >= LANES - FRINGE, tile, 0.0)
        row += [right, left] if sizes.border[level] == 2 else [right + left]
    return jnp.concatenate(row, axis=1)


def packing(count):
    return -(-count // 2)


def pack_rows(rows, target):
    half = LANES // 2
    lane = lane_at(rows[0].shape)
    for index in range(packing(len(rows))):
        held = jnp.where(lane < half, rows[2 * index], 0.0)
        if 2 * index + 1 < len(rows):
            held = jnp.where(lane < half, held, pltpu.roll(rows[2 * index + 1], half, axis=1))
        target[index] = held


def unpack_rows(sizes, place, tiles, count, others=()):
    half, reach = LANES // 2, BORDER >> 3
    lane = lane_at(tiles.shape[1:])
    rows = []
    for index in range(count):
        held = tiles[index // 2]
        row = jnp.where(lane < half, pltpu.roll(held, half, axis=1) if index % 2 else held, 0.0)
        for side, other in enumerate(others):
            first = LANES - reach if side else half
            if sizes.sides == 1:
                first = jnp.where(place[1] == 0, half, LANES - reach)
            beside = other[index // 2]
            beside = beside if index % 2 else pltpu.roll(beside, half, axis=1)
            row = jnp.where((lane >= first) & (lane < first + reach), beside, row)
        rows.append(row)
    return rows


def merge_into(sizes, place, stride, radix, arrays, source, conduct, binding, first, others=()):
    position = (place[0] // stride) % radix
    source[...] = jnp.zeros(source.shape, f32)
    for step, array in enumerate(arrays):
        at = (position ^ step) * stride
        rows = unpack_rows(sizes, place, array, 3 * stride + 2, [other[step] for other in others])
        for index, row in enumerate(rows[: stride + 2]):
            source[at + index] = source[at + index] + row
        for index in range(stride):
            conduct[at + index + first] = rows[stride + 2 + index]
            binding[at + index] = rows[2 * stride + 2 + index]


def merge_kernel(sizes, stride, radix, place, *refs):
    arrays, out, (source, conduct, binding) = refs[:radix], refs[radix], refs[radix + 1 :]
    merge_into(sizes, place, stride, radix, arrays, source, conduct, binding, 0)
    count = stride * radix
    rows = [source[row] for row in range(count + 2)]
    rows += [conduct[row] for row in range(count)] + [binding[row] for row in range(count)]
    pack_rows(rows, out)


def held_rows(sizes, owns, borders):
    def held_row(level, at, row):
        if level > 0:
            row = at * sizes.rows[level] + row
            return jnp.concatenate([owns[level][row], *(array[row] for array in borders[level])], axis=1)
        own = owns[3][row] if at == 2 else owns[0][at, row]
        sides = len(borders[0]) // 3
        return jnp.concatenate([own, *(array[row] for array in borders[0][at * sides : (at + 1) * sides])], axis=1)

    return held_row


def inner_kernel(sizes, place, *refs):
    s = sizes.sides
    owns, borders0, refs = refs[:4], refs[4 : 4 + 3 * s], refs[4 + 3 * s :]
    border1, border2, inner0, inner1, inner2, sums = refs
    n0, n1, n2 = sizes.rows[:3]
    if s:
        for row in range(2 * n1):
            for side in range(s):
                columns = slice(side * LANES, (side + 1) * LANES)
                at, low = row // n1, 2 * (row % n1)
                sums[row, :, columns] = borders0[at * s + side][low] + borders0[at * s + side][low + 1]
        narrow(sizes, place, 0, sums, border1, 2 * n1, "border", sizes.own[0] * LANES)
        for row in range(2 * n2):
            sums[row, :, :LANES] = border1[2 * row] + border1[2 * row + 1]
        narrow(sizes, place, 1, sums, border2, 2 * n2, "border", sizes.own[1] * LANES)
    held_row = held_rows(sizes, owns, [borders0, [border1][:s], [border2][:s]])
    levels = [Level(sizes, level, inner, None) for level, inner in enumerate((inner0, inner1, inner2))]
    for index, level in enumerate(levels):
        conduct = lambda row, index=index, level=level: held_row(index, 0, row - level.halo)
        bound = lambda row, index=index, level=level: held_row(index, 1, row - level.halo)
        coefficients(
            sizes, place, index, conduct, bound, level.fx, level.fy, level.fz, level.weight, level.inner()
        )
        if index == 0:
            right = lambda row: held_row(0, 2, row - 1)
            for row in range(2, n0):
                level.smooth[row - 1] = level.weight[row - 1] * right(row)
            add = in_pairs(sums, lambda row: ((row - 3) // 2, row % 2 == 1))
            field = lambda row, level=level: level.smooth[row - 1]
            emit = lambda row, value: add(row, right(row) - value)
            sweep(3, n0 - 2, field, bound, level.fx, level.fy, level.fz, emit)
        if index == 1:
            narrow(sizes, place, 0, sums, level.source.inner, n1 - 2)
            for row in range(2, n1):
                level.smooth[row] = level.weight[row] * level.source[row]


def down_kernel(sizes, place, *refs):
    s = sizes.sides
    owns, borders0, refs = refs[:4], refs[4 : 4 + 3 * s], refs[4 + 3 * s :]
    pairs_of = [refs[2 * index : 2 * index + 2] for index in range(1 + s)]
    refs = refs[2 * (1 + s) :]
    from_prev, *beside_prev = (Arrived(place, pair, 0) for pair in pairs_of)
    from_next, *beside_next = (Arrived(place, pair, 1) for pair in pairs_of)
    (border1, border2), inners, refs = refs[:2], refs[2:5], refs[5:]
    outers, contribution, with_far, ups, far, refs = refs[:3], refs[3], refs[4], refs[5:7], refs[7], refs[8:]
    level3, sums = refs
    slots = sizes.slots
    n0, n1, n2 = sizes.rows[:3]
    levels = [Level(sizes, index, inner, outer) for index, (inner, outer) in enumerate(zip(inners, outers))]
    held_row = held_rows(sizes, owns, [borders0, [border1][:s], [border2][:s]])

    def prev_row(level, index):
        return message_row(sizes, place, level, slots[index], from_prev, beside_prev)

    def next_row(level, index):
        return message_row(sizes, place, level, slots[index], from_next, beside_next)

    def conduct0(row):
        if row == 0:
            return prev_row(0, 0)
        if row == n0 + 1:
            return next_row(0, 0)
        return held_row(0, 0, row - 1)

    zero = jnp.zeros((sizes.depth, sizes.held[0]), f32)
    level = levels[0]
    bound0 = lambda row: held_row(0, 1, row - 1)
    right = lambda row: held_row(0, 2, row - 1)
    coefficients(
        sizes, place, 0, conduct0, bound0, level.fx, level.fy, level.fz, level.weight, level.outer()
    )
    for row in (1, n0):
        level.smooth[row - 1] = level.weight[row - 1] * right(row)
    first_slot = lambda row: (row + 1) // 2
    add = in_pairs(
        sums,
        lambda row: (first_slot(row) - (n1 - 2 if row > n0 // 2 else 0), row % 2 == 1 or row == 0),
    )
    field = lambda row, level=level: level.smooth[row - 1] if 0 < row < n0 + 1 else zero
    emit = lambda row, value: add(row, right(row) - value)
    add(0, level.fx[0] * field(1))
    sweep(1, 2, field, bound0, level.fx, level.fy, level.fz, emit)
    sweep(n0 - 1, n0, field, bound0, level.fx, level.fy, level.fz, emit)
    add(n0 + 1, level.fx[n0] * field(n0))
    fine_held = sizes.held[0]
    for index, first in ((1, 1), (2, 4)):
        level, n = levels[index], sizes.rows[index]
        held = sizes.held[index]
        narrow(
            sizes, place, index - 1, sums.at[:, :, :fine_held], level.source.outer, level.source.outer.shape[0]
        )
        binding = level.binding
        binding[0] = prev_row(index, first + 2)
        binding[n + 1] = next_row(index, first + 2)
        for row in range(n):
            binding[row + 1] = held_row(index, 1, row)

        def conduct(row, n=n, index=index, first=first):
            if row < 2:
                return prev_row(index, first + row)
            if row >= n + 2:
                return next_row(index, first + row - n - 2)
            return held_row(index, 0, row - 2)

        bound = lambda row, binding=binding: binding[row - 1]
        coefficients(
            sizes, place, index, conduct, bound, level.fx, level.fy, level.fz, level.weight, level.outer()
        )
        for row in level.outer()[2] if index == 1 else range(1, n + 3):
            level.smooth[row - 1] = level.weight[row - 1] * level.source[row - 1]
        zero = jnp.zeros((sizes.depth, held), f32)
        field = lambda row, level=level, n=n, zero=zero: level.smooth[row - 1] if 0 < row < n + 3 else zero
        add = in_pairs(sums.at[:, :, :held], lambda row: (row // 2, row % 2 == 0))
        emit = lambda row, value, level=level, add=add: add(row, level.source[row - 1] - value)
        add(0, level.fx[0] * field(1))
        sweep(1, n + 2, field, bound, level.fx, level.fy, level.fz, emit)
        add(n + 3, level.fx[n + 2] * field(n + 2))
        fine_held = held
    narrow(sizes, place, 2, sums.at[:, :, : sizes.held[2]], level3, 3)
    for at in (0, 1):
        sums[at, :, : sizes.held[2]] = held_row(2, at, 0) + held_row(2, at, 1)
    narrow(sizes, place, 2, sums.at[:, :, : sizes.held[2]], level3.at[3:5], 2)
    tiles = packing(5)
    pack_rows([level3[row] for row in range(5)], contribution)
    with_far[0:tiles] = contribution[...]
    v0, s1, v1 = levels[0].smooth, levels[1].source, levels[1].smooth
    s2, v2 = levels[2].source, levels[2].smooth
    next_rows = (v0[n0 - 1], s1[n1], v1[n1 - 1], s2[n2], s2[n2 + 1], v2[n2 - 1])
    prev_rows = (v0[0], s1[1], v1[2], s2[1], s2[0], v2[2])
    for slot, next_row, prev_row in zip(sizes.up_slots, next_rows, prev_rows):
        put_pair(place, ups, slot, next_row, prev_row)
    if s:
        ends = [fringes(sizes, list(zip((0, 1, 1, 2, 2, 2), rows))) for rows in (next_rows, prev_rows)]
        put_pair(place, ups, (sizes.up_tiles, 1), *ends)
    far_tiles = sizes.held[2] // LANES
    put_pair(place, (with_far.at[tiles : tiles + far_tiles], far), (0, far_tiles), v2[n2 + 1], v2[0], 2)


def relax(count, field, refs_of, source, target):
    fx, fy, fz, weight, binding = refs_of

    def update(row, value):
        target(row, field(row) + weight[row - 1] * (source(row) - value))

    sweep(1, count - 2, field, binding, fx, fy, fz, update)


def store(array, first):
    def put_row(row, value):
        array[row - first] = value

    return put_row


def coarse_kernel(sizes, stride, radix, place, *refs):
    blocks, refs = refs[:radix], refs[radix:]
    others, refs = [refs[side * radix : (side + 1) * radix] for side in range(sizes.sides)], refs[sizes.sides * radix :]
    out, merged, sums = refs[:3]
    coarse = [refs[3 + 9 * index : 12 + 9 * index] for index in range(3)]
    total = sizes.span_count
    merge_into(sizes, place, stride, radix, blocks, merged, coarse[0][4], coarse[0][5], 1, others)
    zero = jnp.zeros((sizes.depth, LANES), f32)
    for index in range(3):
        level = 3 + index
        fx, fy, fz, weight, conduct, binding, source, smooth, iterate = coarse[index]
        count = total >> index
        for array in (conduct, smooth, iterate):
            array[0] = zero
            array[count + 1] = zero
        if index == 0:
            source = merged.at[1 : count + 1]
        bound = lambda row, binding=binding: binding[row - 1]
        at_row = lambda row, conduct=conduct: conduct[row]
        every = (range(1, count + 2), range(1, count + 1), range(1, count + 1))
        coefficients(sizes, place, level, at_row, bound, fx, fy, fz, weight, every)
        for row in range(count):
            smooth[row + 1] = weight[row] * source[row]
        if index < 2:
            conduct_next, binding_next, source_next = coarse[index + 1][4:7]
            half = count // 2
            for row in range(half):
                sums[row, :, :LANES] = conduct[2 * row + 1] + conduct[2 * row + 2]
            narrow(sizes, place, level, sums, conduct_next.at[1 : half + 1], half)
            for row in range(half):
                sums[row, :, :LANES] = binding[2 * row] + binding[2 * row + 1]
            narrow(sizes, place, level, sums, binding_next, half)

            def add(row, value, source=source):
                value = source[row - 1] - value
                slot = (row - 1) // 2
                if row % 2 == 1:
                    sums[slot, :, :LANES] = value
                else:
                    sums[slot, :, :LANES] = sums[slot, :, :LANES] + value

            sweep(1, count, lambda row, smooth=smooth: smooth[row], bound, fx, fy, fz, add)
            narrow(sizes, place, level, sums, source_next, half)

    fx, fy, fz, weight, conduct, binding, source, smooth, iterate = coarse[2]
    held, other = smooth, iterate
    for _ in range(COARSE_SWEEPS - 1):
        field = lambda row, held=held: held[row]
        mine = lambda row: source[row - 1]
        bound = lambda row: binding[row - 1]
        relax((total >> 2) + 2, field, (fx, fy, fz, weight, bound), mine, store(other, 0))
        held, other = other, held
    for index in (1, 0):
        fx, fy, fz, weight, conduct, binding, source, smooth, iterate = coarse[index]
        if index == 0:
            source = merged.at[1 : total + 1]
        count = total >> index
        widen(sizes, place, 3 + index, held.at[1 : count // 2 + 1], sums, count // 2)
        for row in range(count):
            smooth[row + 1] = smooth[row + 1] + sums[row // 2, :, :LANES]
        field = lambda row, smooth=smooth: smooth[row]
        mine = lambda row, source=source: source[row - 1]
        bound = lambda row, binding=binding: binding[row - 1]
        relax(count + 2, field, (fx, fy, fz, weight, bound), mine, store(iterate, 0))
        held = iterate

    out[...] = held[pl.ds(place[0], 3)]


def up_kernel(sizes, place, coarse, *refs):
    s = sizes.sides
    pair, far_pair, inners, outers, owns = refs[:2], refs[2:4], refs[4:7], refs[7:10], refs[10:12]
    levels = [Level(sizes, index, inner, outer) for index, (inner, outer) in enumerate(zip(inners, outers))]
    from_prev, from_next = (Arrived(place, pair, forward) for forward in (0, 1))
    tiles = packing(5)
    far_pair = (far_pair[0].at[tiles : tiles + sizes.held[2] // LANES], far_pair[1])
    fars = [Arrived(place, far_pair, forward, 2) for forward in (0, 1)]
    borders0, out, refs = refs[12 : 12 + 3 * s], refs[12 + 3 * s], refs[13 + 3 * s :]
    total1, total2, result, edges0, edges1 = refs[:5]
    over2, over1, over0, lift2, lift1, lift0, it2, it1, it0, semaphores = refs[5:]
    slots = sizes.slots
    n0, n1, n2 = sizes.rows[:3]
    width = sizes.own[0] * LANES

    before, behind = fringed_row(sizes, 0, 0, from_prev), fringed_row(sizes, 0, 0, from_next)
    lift0[0], lift0[n0 + 1] = before, behind
    edges0[0], edges0[1] = levels[0].fx[0] * before, levels[0].fx[n0] * behind
    narrow(sizes, place, 0, edges0, edges1, 2)

    widen(sizes, place, 2, coarse, over2, 3)
    for level, first, totals, over, lift, target, upper in (
        (2, 3, total2, over2, lift2, it2, over1),
        (1, 1, total1, over1, lift1, it1, over0),
    ):
        n, kept = sizes.rows[level], levels[level]
        fx, fy, fz, weight, binding = kept.fx, kept.fy, kept.fz, kept.weight, kept.binding
        own, smooth = kept.source, kept.smooth
        fringed = lambda index, message, level=level: fringed_row(sizes, level, index, message)
        if level == 1:
            smooth_at = first + 1
            edge = {2: own[1] + edges1[0], n + 1: own[n] + edges1[1]}
        else:
            smooth_at = first + 2
            edge = {2: own[1] + fringed(first + 1, from_prev)}
            edge[n + 1] = own[n] + fringed(first + 1, from_next)
        edge[1], edge[n + 2] = own[0] + fringed(first, from_prev), own[n + 1] + fringed(first, from_next)
        for row, value in edge.items():
            totals[row - 1] = value
        for row in range(n + 4):
            if row in (0, n + 3):
                value = fringed(smooth_at, from_next if row else from_prev)
                if level == 2:
                    far = fars[1 if row else 0]
                    value = value + jnp.concatenate(get(far, (0, sizes.held[2] // LANES)), axis=1)
            elif row in edge:
                value = weight[row - 1] * totals[row - 1]
            else:
                value = smooth[row - 1]
            lift[row] = value + over[row // 2]
        field = lambda row, lift=lift: lift[row]
        mine = lambda row, own=own, totals=totals, edge=edge: (totals if row in edge else own)[row - 1]
        bound = lambda row, binding=binding: binding[row - 1]
        relax(n + 4, field, (fx, fy, fz, weight, bound), mine, store(target, 1))
        widen(sizes, place, level - 1, target, upper, n + 2)

    held_row = held_rows(sizes, [owns[0], None, None, owns[1]], [borders0])
    fx, fy, fz, weight, v0 = levels[0].fx, levels[0].fy, levels[0].fz, levels[0].weight, levels[0].smooth
    lift0[0] = lift0[0] + over0[0]
    lift0[n0 + 1] = lift0[n0 + 1] + over0[n1 + 1]
    for row in range(1, n0 + 1):
        lift0[row] = v0[row - 1] + over0[(row + 1) // 2]
    field = lambda row: lift0[row]
    bound = lambda row: held_row(0, 1, row - 1)
    relax(n0 + 2, field, (fx, fy, fz, weight, bound), lambda row: held_row(0, 2, row - 1), store(it0, 1))
    step = sizes.depth // CHUNKS
    copies = []
    for chunk in range(CHUNKS):
        part = slice(chunk * step, (chunk + 1) * step)
        result[part] = jnp.swapaxes(it0[:, part, :width], 0, 1)
        copies.append(pltpu.make_async_copy(result.at[part], out.at[part], semaphores.at[chunk]))
        copies[-1].start()
    for copy in copies:
        copy.wait()


def call(body, name, micros, outputs, scratch, place, inputs, copies=0, far_out=False):
    near, far = pl.BlockSpec(memory_space=pltpu.VMEM), pl.BlockSpec(memory_space=pl.ANY)
    scratch = [pltpu.VMEM(shape, f32) for shape in scratch]
    if copies:
        scratch.append(pltpu.SemaphoreType.DMA((copies,)))
    return pl.pallas_call(
        body,
        name=name,
        out_shape=[jax.ShapeDtypeStruct(shape, f32) for shape in outputs],
        in_specs=[pl.BlockSpec(memory_space=pltpu.SMEM)] + [near] * len(inputs),
        out_specs=[far if far_out else near] * len(outputs),
        scratch_shapes=scratch,
        cost_estimate=pl.CostEstimate(flops=int(micros * 1.15e9), bytes_accessed=int(micros * BYTES_A_MICRO), transcendentals=0),
        compiler_params=pltpu.CompilerParams(vmem_limit_bytes=VMEM_LIMIT),
    )(place, *inputs)


def along(value, axis, steps):
    count = lax.axis_size(axis)
    initial, last = max(0, -steps), min(count, count - steps)
    return lax.ppermute(value, axis, [(source, source + steps) for source in range(initial, last)])


def beside(values, sizes):
    if sizes.sides == 1:
        return [[lax.ppermute(value, "width", [(0, 1), (1, 0)]) for value in values]]
    if sizes.sides == 2:
        return [[along(value, "width", steps) for value in values] for steps in (-1, 1)]
    return []


def edge_columns(edges, sizes):
    if sizes.sides == 1:
        return [lax.ppermute(edges[0], "width", [(0, 1), (1, 0)])]
    if sizes.sides == 2:
        return [along(edges[1], "width", -1), along(edges[0], "width", 1)]
    return []


def stages(count):
    stride = 1
    while stride < count:
        radix = 4 if count // stride % 4 == 0 else 2
        yield stride, radix
        stride *= radix


def swap(value, stride, radix, others=None):
    count = lax.axis_size("span")
    others = others or {}
    return [value] + [
        lax.ppermute(others.get(step, value), "span", [(device, device ^ step * stride) for device in range(count)])
        for step in range(1, radix)
    ]


def exchange(pair, stride):
    count = lax.axis_size("span")
    routes = [[], []]
    for low in range(count - stride):
        routes[low // stride % 2] += [(low, low + stride), (low + stride, low)]
    return [None if value is None else lax.ppermute(value, "span", route) for value, route in zip(pair, routes)]


def on_device(right_side, diffusivity, reaction):
    depth, extent_x, extent_y = diffusivity.shape
    sizes = Sizes(depth, extent_x, extent_y, lax.axis_size("span"), lax.axis_size("width"))
    place = jnp.stack([lax.axis_index("span"), lax.axis_index("width")]).astype(jnp.int32)
    n0, n1, n2, n3 = sizes.rows
    s = sizes.sides
    tile = (depth, LANES)
    own = [(depth, count * LANES) for count in sizes.own]
    held = [(depth, count) for count in sizes.held]
    down_message = (sizes.tiles, *tile)
    up_message = (sizes.up_tiles + 1, *tile)
    own0, own1, own2, first, second, *edges = call(
        functools.partial(start_kernel, sizes),
        "start",
        1.1,
        [(2, n0, *own[0]), (2 * n1, *own[1]), (2 * n2, *own[2]), down_message, down_message]
        + [(n0, depth, BORDER)] * 2 * s,
        [(2 * n1, *own[0])],
        place,
        [diffusivity, reaction],
    )
    borders = edge_columns(edges[:s], sizes) + edge_columns(edges[s:], sizes)
    halos = exchange([first, second], 1)
    turned, *edges = call(
        functools.partial(turn_kernel, sizes),
        "turn",
        0.7,
        [(n0, *own[0])] + [(n0, depth, BORDER)] * s,
        [],
        place,
        [right_side],
    )
    borders += edge_columns(edges, sizes)
    plan = list(stages(sizes.span_count))

    part = packing(5)
    far = (sizes.held[2] // LANES, *tile)
    inners = [(sum(inner_rows(sizes, level)), *held[level]) for level in range(3)]
    outers = [(sum(outer_rows(sizes, level)), *held[level]) for level in range(3)]
    inner = call(
        functools.partial(inner_kernel, sizes),
        "inner",
        0.5,
        [(2 * n1, *tile), (2 * n2, *tile), *inners],
        [(2 * n1, *held[0])],
        place,
        [own0, own1, own2, turned, *borders],
    )
    halos, inner = lax.optimization_barrier((halos, inner))
    sides = beside(halos, sizes)
    downs = call(
        functools.partial(down_kernel, sizes),
        "down",
        2.5,
        [*outers, (part, *tile), (part + far[0], *tile), up_message, up_message, far],
        [(5, *tile), (n1 + 2, *held[0])],
        place,
        [own0, own1, own2, turned, *borders, *halos, *sum(sides, []), *inner],
    )
    outer, blocks, with_far, ups, far_second = downs[:3], downs[3], downs[4], list(downs[5:7]), downs[7]
    far_rows = None
    for stride, radix in plan[:-1]:
        count = stride * radix
        if far_rows is None:
            blocks = swap(blocks, stride, radix, {2: with_far})
            far_rows = [blocks[2], exchange([None, far_second], 2)[1]]
        else:
            blocks = swap(blocks, stride, radix)
        (blocks,) = call(
            functools.partial(merge_kernel, sizes, stride, radix),
            "merge",
            0.9,
            [(packing(3 * count + 2), *tile)],
            [(count + 2, *tile), (count, *tile), (count, *tile)],
            place,
            blocks,
        )
    stride, radix = plan[-1]
    blocks = swap(blocks, stride, radix)
    received = lax.optimization_barrier([exchange([ups[0], None], 1)[0], ups[1]])
    received = [received[0], exchange([None, received[1]], 1)[1]] + far_rows
    scratch = [(sizes.span_count + 2, *tile), (max(sizes.span_count // 2, 2), *tile)]
    for index in range(3):
        count = sizes.span_count >> index
        scratch += [(count + 1, *tile)] + [(count, *tile)] * 3 + [(count + 2, *tile)] + [(count, *tile)] * 2
        scratch += [(count + 2, *tile)] * 2
    blocks, received[3] = lax.optimization_barrier((blocks, received[3]))
    (coarse,) = call(
        functools.partial(coarse_kernel, sizes, stride, radix),
        "coarse",
        0.7,
        [(n3 + 2, *tile)],
        scratch,
        place,
        [*blocks, *sum(beside(blocks, sizes), [])],
    )
    scratch = [(n1 + 2, *held[1]), (n2 + 2, *held[2]), diffusivity.shape, (2, *held[0]), (2, *held[1])]
    scratch += [(n3 + 2, *held[2]), (n2 + 2, *held[1]), (n1 + 2, *held[0])]
    scratch += [(n2 + 4, *held[2]), (n1 + 4, *held[1]), (n0 + 2, *held[0])]
    scratch += [(n2 + 2, *held[2]), (n1 + 2, *held[1]), (n0, *held[0])]
    (correction,) = call(
        functools.partial(up_kernel, sizes),
        "up",
        3.0,
        [diffusivity.shape],
        scratch,
        place,
        [coarse, *received, *inner[2:], *outer, own0, turned, *borders],
        copies=CHUNKS,
        far_out=True,
    )
    return correction


def solution(mesh):
    in_specs = (P(None, "span", "width"),) * 3
    return jax.shard_map(
        on_device, mesh=mesh, in_specs=in_specs, out_specs=P(None, "span", "width"), check_vma=False
    )
```

```python
import functools

import jax
import jax.numpy as jnp
from jax import lax
from jax.experimental import pallas as pl
from jax.experimental.pallas import tpu as pltpu
from jax.sharding import PartitionSpec as P

LEVELS = 6
COARSE_SWEEPS = 3
LANES = 128
BORDER = 128
FRINGE = 4
SPREAD = 16
relax_weight = 0.8
f32 = jnp.float32
VMEM_LIMIT = 32 * 1024 * 1024
BYTES_A_MICRO = 3.69e6
CHUNKS = 4


class Sizes:
    def __init__(self, depth, extent_x, extent_y, span_count, width_count):
        self.depth, self.extent_x, self.extent_y = depth, extent_x, extent_y
        self.span_count, self.width_count = span_count, width_count
        self.sides = min(width_count - 1, 2)
        self.own = [(extent_y >> level) // LANES for level in range(3)]
        self.border = [self.sides, min(self.sides, 1), min(self.sides, 1)]
        self.held = [(self.own[level] + self.border[level]) * LANES for level in range(3)] + [LANES] * 3
        self.rows = [extent_x >> level for level in range(4)]
        self.slots = []
        start = 0
        for level in (0, 1, 1, 1, 2, 2, 2):
            self.slots.append((start, self.own[level]))
            start += self.own[level]
        self.tiles = start
        self.up_slots = []
        start = 0
        for level in (0, 1, 1, 2, 2, 2):
            self.up_slots.append((start, self.own[level]))
            start += self.own[level]
        self.up_tiles = start
        self.last = list(stages(span_count))[-1][1]


def put(message, slot, row):
    start, tiles = slot
    for tile in range(tiles):
        message[start + tile] = row[:, tile * LANES : (tile + 1) * LANES]


class Arrived:
    def __init__(self, place, pair, forward, stride=1):
        self.even = place[0] // stride % 2 == 0
        self.first, self.second = (pair[0], pair[1]) if forward else (pair[1], pair[0])

    def __getitem__(self, index):
        return jnp.where(self.even, self.first[index], self.second[index])


def put_pair(place, pair, slot, next_row, prev_row, stride=1):
    even = place[0] // stride % 2 == 0
    put(pair[0], slot, jnp.where(even, next_row, prev_row))
    put(pair[1], slot, jnp.where(even, prev_row, next_row))


def get(message, slot):
    start, tiles = slot
    return [message[start + tile] for tile in range(tiles)]


def lane_at(shape):
    return lax.broadcasted_iota(jnp.int32, shape, len(shape) - 1)


def roll(value, steps, axis):
    return pltpu.roll(value, steps % value.shape[axis], axis=axis)


def reciprocal(value):
    return pltpu.reciprocal(value, approx=True)


def harmonic(first, second, guard):
    total = first + second
    if guard:
        total = jnp.maximum(total, 1e-3)
    return (2.0 * first) * second * reciprocal(total)


def split(value):
    high = value.astype(jnp.bfloat16)
    return high, (value - high.astype(f32)).astype(jnp.bfloat16)


def dot(halves, table):
    high, low = halves
    return jnp.dot(high, table, preferred_element_type=f32) + jnp.dot(low, table, preferred_element_type=f32)


def pair_table(fine, fine_dim, turn, weight):
    shape = (fine, LANES) if fine_dim == 0 else (LANES, fine)
    fine_at = lax.broadcasted_iota(jnp.int32, shape, fine_dim)
    coarse_at = lax.broadcasted_iota(jnp.int32, shape, 1 - fine_dim)
    if turn is not None:
        coarse_at = coarse_at - jnp.where(fine_at >= turn, LANES // 2, 0)
    return jnp.where(fine_at // 2 == coarse_at, weight, 0.0).astype(jnp.bfloat16)


def turns(sizes, place, level):
    if sizes.sides == 0:
        return []
    if level == 0:
        return [jnp.where(place[1] == 0, LANES, 0)] if sizes.sides == 1 else [LANES, 0]
    return [LANES // 2]


def transfer_plan(sizes, place, level, part):
    plan = []
    if level >= 3:
        return [((0, LANES), 0, 3 * LANES // 4)]
    if level == 2:
        return [((0, sizes.held[2]), 0, None)]
    own = sizes.own[level]
    if part != "border":
        plan += [((2 * LANES * tile, 2 * LANES * (tile + 1)), tile, None) for tile in range(own // 2)]
    if part != "own":
        for index, turn in enumerate(turns(sizes, place, level)):
            start = (own + index) * LANES
            plan.append(((start, start + LANES), own // 2, turn))
    return plan


def narrow(sizes, place, level, sums, target, rows, part="all", shift=0):
    depth = sums.shape[1]
    done = {}
    for (start, stop), tile, turn in transfer_plan(sizes, place, level, part):
        start, stop, tile = start - shift, stop - shift, tile - shift // (2 * LANES)
        columns = split(sums[0:rows, :, start:stop].reshape(rows * depth, stop - start))
        result = dot(columns, pair_table(stop - start, 0, turn, 0.25)).reshape(rows, depth, LANES)
        done[tile] = done[tile] + result if tile in done else result
    for tile, result in done.items():
        target[0:rows, :, tile * LANES : (tile + 1) * LANES] = result


def widen(sizes, place, level, coarse, target, rows):
    depth = coarse.shape[1]
    for (start, stop), tile, turn in transfer_plan(sizes, place, level, "all"):
        columns = split(coarse[0:rows, :, tile * LANES : (tile + 1) * LANES].reshape(rows * depth, LANES))
        result = dot(columns, pair_table(stop - start, 1, turn, 4.0))
        target[0:rows, :, start:stop] = result.reshape(rows, depth, stop - start)


class Joined:
    def __init__(self, inner, outer, first):
        self.inner, self.outer, self.first = inner, outer, first

    def find(self, row):
        place, count = row - self.first, 0 if self.inner is None else self.inner.shape[0]
        if 0 <= place < count:
            return self.inner, place
        return self.outer, row if place < 0 else row - count

    def __getitem__(self, row):
        array, place = self.find(row)
        return array[place]

    def __setitem__(self, row, value):
        array, place = self.find(row)
        array[place] = value


class Level:
    def __init__(self, sizes, level, inner, outer):
        self.n, self.halo = sizes.rows[level], 1 if level == 0 else 2
        counts = inner_rows(sizes, level)
        fx, fy, fz, *rest = parts(inner, counts)
        weight, source, smooth = (None, None, None) if level == 2 else (rest[0], None, rest[1])
        if level == 1:
            weight, source, smooth = rest
        others = [None] * 7 if outer is None else parts(outer, outer_rows(sizes, level))
        if level == 0 and outer is not None:
            others = [others[0], None, None, others[1], None, others[2], None]
        h = self.halo
        self.fx = Joined(fx, others[0], h)
        self.fy, self.fz = Joined(fy, others[1], h - 1), Joined(fz, others[2], h - 1)
        self.weight, self.source, self.smooth = (
            Joined(array, other, h) for array, other in zip((weight, source, smooth), others[3:6])
        )
        self.binding = others[6]

    def inner(self):
        first, last = self.halo, self.halo + self.n - 1
        return range(first + 1, last + 1), range(first, last + 1), range(first + 1, last)

    def outer(self):
        count = self.n + 2 * self.halo
        every = (range(1, count), range(1, count - 1), range(1, count - 1))
        return tuple([row for row in rows if row not in mine] for rows, mine in zip(every, self.inner()))


def inner_rows(sizes, level):
    n = sizes.rows[level]
    return [n - 1, n, n] + [[n - 2] * 2, [n - 2] * 3, []][level]


def outer_rows(sizes, level):
    n = sizes.rows[level]
    return [[2, 2, 2], [4, 2, 2, 4, 4, 4, n + 2], [4, 2, 2] + [n + 2] * 4][level]


def coefficients(sizes, place, level, conduct, binding, fx, fy, fz, weight, rows):
    guard = level > 0 or sizes.sides > 1
    for row in rows[0]:
        fx[row - 1] = harmonic(conduct(row - 1), conduct(row), guard)
    for row in rows[1]:
        mine = conduct(row)
        south = harmonic(mine, roll(mine, 1, 1), guard)
        if level == 0 and sizes.sides < 2:
            cut = 0 if sizes.sides == 0 else jnp.where(place[1] == 0, 0, sizes.extent_y)
            south = jnp.where(lane_at(mine.shape) == cut, 0.0, south)
        below = harmonic(mine, roll(mine, 1, 0), guard)
        fy[row - 1] = south
        fz[row - 1] = jnp.where(lax.broadcasted_iota(jnp.int32, mine.shape, 0) == 0, 0.0, below)
    for row in rows[2]:
        south, below = fy[row - 1], fz[row - 1]
        diagonal = fx[row - 1] + fx[row] + binding(row)
        diagonal = diagonal + (south + roll(south, -1, 1)) + (below + roll(below, -1, 0))
        if guard:
            diagonal = jnp.maximum(diagonal, 1e-6)
        weight[row - 1] = relax_weight * reciprocal(diagonal)


def sweep(first, last, field, binding, fx, fy, fz, emit):
    lower = fx[first - 1] * (field(first) - field(first - 1))
    for row in range(first, last + 1):
        mine = field(row)
        upper = fx[row] * (field(row + 1) - mine)
        south = fy[row - 1] * (mine - roll(mine, 1, 1))
        below = fz[row - 1] * (mine - roll(mine, 1, 0))
        across = (south - roll(south, -1, 1)) + (below - roll(below, -1, 0))
        emit(row, binding(row) * mine + (lower - upper) + across)
        lower = upper


def in_pairs(sums, slot_of):
    def add(row, value):
        slot, first = slot_of(row)
        if first:
            sums[slot] = value
        else:
            sums[slot] = sums[slot] + value

    return add


def parts(array, counts):
    views, start = [], 0
    for count in counts:
        views.append(array.at[start : start + count])
        start += count
    return views


def start_kernel(sizes, place, conduct, binding, own0, own1, own2, first, second, top, *refs):
    edges, sums = refs[: 2 * sizes.sides], refs[-1]
    n0, n1, n2 = sizes.rows[:3]
    for at, array in enumerate((conduct, binding)):
        own0[at] = jnp.swapaxes(array[...], 0, 1)
    for at in (0, 1):
        for row in range(n1):
            sums[at * n1 + row] = own0[at, 2 * row] + own0[at, 2 * row + 1]
    narrow(sizes, place, 0, sums, own1, 2 * n1, "own")
    for row in range(2 * n2):
        sums[row, :, : sizes.own[1] * LANES] = own1[2 * row] + own1[2 * row + 1]
    narrow(sizes, place, 1, sums, own2, 2 * n2, "own")
    last = jnp.concatenate([own2[0] + own2[1], own2[n2] + own2[n2 + 1]], axis=0)
    last = dot(split(last), pair_table(LANES, 0, None, 0.25))
    top[0] = last[: sizes.depth] + roll(last[sizes.depth :], LANES // 2, 1)
    ends = []
    for low, at1, at0 in ((n1 - 2, n1 - 1, n0 - 1), (0, 0, 0)):
        edge = n2 - 1 if at0 else 0
        rows = (own0[0, at0], own1[low], own1[low + 1], own1[n1 + at1])
        ends.append(rows + (own2[n2 - 2], own2[n2 - 1], own2[n2 + edge]))
    for slot, next_row, prev_row in zip(sizes.slots, *ends):
        put_pair(place, (first, second), slot, next_row, prev_row)
    for at in (0, 1):
        cut_edges(sizes, place, own0.at[at], edges[at * sizes.sides : (at + 1) * sizes.sides])


def cut_edges(sizes, place, array, edges):
    last = sizes.extent_y - BORDER
    if sizes.sides == 1:
        at = pl.multiple_of(jnp.where(place[1] == 0, last, 0), LANES)
        edges[0][...] = array[:, :, pl.ds(at, BORDER)]
    elif sizes.sides == 2:
        edges[0][...] = array[:, :, last:]
        edges[1][...] = array[:, :, :BORDER]


def turn_kernel(sizes, place, right_side, turned, *edges):
    turned[...] = jnp.swapaxes(right_side[...], 0, 1)
    cut_edges(sizes, place, turned, edges)


def message_row(sizes, place, level, slot, message, beside):
    start, tiles = slot
    row = get(message, slot)
    if sizes.sides == 1:
        left = place[1] != 0
        tile = beside[0][start + jnp.where(left, tiles - 1, 0)]
        if level > 0:
            reach = BORDER >> level
            lane = lane_at(tile.shape)
            first = jnp.where(left, LANES - reach, 0)
            tile = jnp.where((lane >= first) & (lane < first + reach), tile, 0.0)
        row.append(tile)
    elif sizes.sides == 2:
        right, left = beside[0][start], beside[1][start + tiles - 1]
        if level == 0:
            row += [right, left]
        else:
            reach = BORDER >> level
            lane = lane_at(right.shape)
            row.append(jnp.where(lane < reach, right, jnp.where(lane >= LANES - reach, left, 0.0)))
    return jnp.concatenate(row, axis=1)


def fringe_lanes(shape):
    lane = lane_at(shape)
    return (lane < FRINGE) | (lane >= LANES - FRINGE)


def fringes(sizes, rows):
    total = None
    for index, (level, row) in enumerate(rows):
        border = row[:, sizes.own[level] * LANES :]
        tile = border[:, :LANES]
        lane = lane_at(tile.shape)
        if border.shape[1] > LANES:
            tile = jnp.where(lane < FRINGE, tile, border[:, LANES:])
        tile = jnp.where((lane < FRINGE) | (lane >= LANES - FRINGE), tile, 0.0)
        tile = roll(tile, SPREAD * index + SPREAD // 2, 1)
        total = tile if total is None else total + tile
    return total


def fringed_row(sizes, level, index, message):
    row = get(message, sizes.up_slots[index])
    if sizes.border[level]:
        tile = roll(message[sizes.up_tiles], -(SPREAD * index + SPREAD // 2), 1)
        lane = lane_at(tile.shape)
        right, left = jnp.where(lane < FRINGE, tile, 0.0), jnp.where(lane >= LANES - FRINGE, tile, 0.0)
        row += [right, left] if sizes.border[level] == 2 else [right + left]
    return jnp.concatenate(row, axis=1)


def packing(count):
    return -(-count // 2)


def pack_rows(rows, target):
    half = LANES // 2
    lane = lane_at(rows[0].shape)
    for index in range(packing(len(rows))):
        held = jnp.where(lane < half, rows[2 * index], 0.0)
        if 2 * index + 1 < len(rows):
            held = jnp.where(lane < half, held, pltpu.roll(rows[2 * index + 1], half, axis=1))
        target[index] = held


def unpack_rows(sizes, place, tiles, count, others=()):
    half, reach = LANES // 2, BORDER >> 3
    lane = lane_at(tiles.shape[1:])
    rows = []
    for index in range(count):
        held = tiles[index // 2]
        row = jnp.where(lane < half, pltpu.roll(held, half, axis=1) if index % 2 else held, 0.0)
        for side, other in enumerate(others):
            first = LANES - reach if side else half
            if sizes.sides == 1:
                first = jnp.where(place[1] == 0, half, LANES - reach)
            beside = other[index // 2]
            beside = beside if index % 2 else pltpu.roll(beside, half, axis=1)
            row = jnp.where((lane >= first) & (lane < first + reach), beside, row)
        rows.append(row)
    return rows


def merge_into(sizes, place, stride, radix, arrays, source, others=()):
    position = (place[0] // stride) % radix
    source[...] = jnp.zeros(source.shape, f32)
    for step, array in enumerate(arrays):
        at = (position ^ step) * stride
        rows = unpack_rows(sizes, place, array, stride + 2, [other[step] for other in others])
        for index, row in enumerate(rows):
            source[at + index] = source[at + index] + row


def merge_kernel(sizes, stride, radix, final, place, *refs):
    arrays, out, tops, source = refs[:radix], refs[radix], refs[radix + 1], refs[radix + 2]
    merge_into(sizes, place, stride, radix, arrays, source)
    rows = [source[row] for row in range(source.shape[0])]
    pack_rows(rows, out)
    position, start = (place[0] // stride) % radix, packing(stride + 2)
    for step, array in enumerate(arrays):
        for kind in range(tops.shape[0]):
            first = start + kind * stride
            tops[kind, pl.ds((position ^ step) * stride, stride)] = array[first : first + stride]
    if not final:
        start, count = packing(len(rows)), stride * radix
        for kind in range(tops.shape[0]):
            out[start + kind * count : start + (kind + 1) * count] = tops[kind]


def held_rows(sizes, owns, borders):
    def held_row(level, at, row):
        if level > 0:
            row = at * sizes.rows[level] + row
            return jnp.concatenate([owns[level][row], *(array[row] for array in borders[level])], axis=1)
        own = owns[3][row] if at == 2 else owns[0][at, row]
        sides = len(borders[0]) // 3
        return jnp.concatenate([own, *(array[row] for array in borders[0][at * sides : (at + 1) * sides])], axis=1)

    return held_row


def inner_kernel(sizes, place, *refs):
    s = sizes.sides
    owns, borders0, refs = refs[:4], refs[4 : 4 + 3 * s], refs[4 + 3 * s :]
    border1, border2, inner0, inner1, inner2, sums = refs
    n0, n1, n2 = sizes.rows[:3]
    if s:
        for row in range(2 * n1):
            for side in range(s):
                columns = slice(side * LANES, (side + 1) * LANES)
                at, low = row // n1, 2 * (row % n1)
                sums[row, :, columns] = borders0[at * s + side][low] + borders0[at * s + side][low + 1]
        narrow(sizes, place, 0, sums, border1, 2 * n1, "border", sizes.own[0] * LANES)
        for row in range(2 * n2):
            sums[row, :, :LANES] = border1[2 * row] + border1[2 * row + 1]
        narrow(sizes, place, 1, sums, border2, 2 * n2, "border", sizes.own[1] * LANES)
    held_row = held_rows(sizes, owns, [borders0, [border1][:s], [border2][:s]])
    levels = [Level(sizes, level, inner, None) for level, inner in enumerate((inner0, inner1, inner2))]
    for index, level in enumerate(levels):
        conduct = lambda row, index=index, level=level: held_row(index, 0, row - level.halo)
        bound = lambda row, index=index, level=level: held_row(index, 1, row - level.halo)
        coefficients(
            sizes, place, index, conduct, bound, level.fx, level.fy, level.fz, level.weight, level.inner()
        )
        if index == 0:
            right = lambda row: held_row(0, 2, row - 1)
            for row in range(2, n0):
                level.smooth[row - 1] = level.weight[row - 1] * right(row)
            add = in_pairs(sums, lambda row: ((row - 3) // 2, row % 2 == 1))
            field = lambda row, level=level: level.smooth[row - 1]
            emit = lambda row, value: add(row, right(row) - value)
            sweep(3, n0 - 2, field, bound, level.fx, level.fy, level.fz, emit)
        if index == 1:
            narrow(sizes, place, 0, sums, level.source.inner, n1 - 2)
            for row in range(2, n1):
                level.smooth[row] = level.weight[row] * level.source[row]


def down_kernel(sizes, place, *refs):
    s = sizes.sides
    owns, borders0, refs = refs[:4], refs[4 : 4 + 3 * s], refs[4 + 3 * s :]
    pairs_of = [refs[2 * index : 2 * index + 2] for index in range(1 + s)]
    refs = refs[2 * (1 + s) :]
    from_prev, *beside_prev = (Arrived(place, pair, 0) for pair in pairs_of)
    from_next, *beside_next = (Arrived(place, pair, 1) for pair in pairs_of)
    (border1, border2), inners, refs = refs[:2], refs[2:5], refs[5:]
    tops, refs = refs[: sizes.last], refs[sizes.last :]
    outers, contribution, with_far, ups, far, refs = refs[:3], refs[3], refs[4], refs[5:7], refs[7], refs[8:]
    level3, sums = refs
    slots = sizes.slots
    n0, n1, n2 = sizes.rows[:3]
    levels = [Level(sizes, index, inner, outer) for index, (inner, outer) in enumerate(zip(inners, outers))]
    held_row = held_rows(sizes, owns, [borders0, [border1][:s], [border2][:s]])

    def prev_row(level, index):
        return message_row(sizes, place, level, slots[index], from_prev, beside_prev)

    def next_row(level, index):
        return message_row(sizes, place, level, slots[index], from_next, beside_next)

    def conduct0(row):
        if row == 0:
            return prev_row(0, 0)
        if row == n0 + 1:
            return next_row(0, 0)
        return held_row(0, 0, row - 1)

    zero = jnp.zeros((sizes.depth, sizes.held[0]), f32)
    level = levels[0]
    bound0 = lambda row: held_row(0, 1, row - 1)
    right = lambda row: held_row(0, 2, row - 1)
    coefficients(
        sizes, place, 0, conduct0, bound0, level.fx, level.fy, level.fz, level.weight, level.outer()
    )
    for row in (1, n0):
        level.smooth[row - 1] = level.weight[row - 1] * right(row)
    first_slot = lambda row: (row + 1) // 2
    add = in_pairs(
        sums,
        lambda row: (first_slot(row) - (n1 - 2 if row > n0 // 2 else 0), row % 2 == 1 or row == 0),
    )
    field = lambda row, level=level: level.smooth[row - 1] if 0 < row < n0 + 1 else zero
    emit = lambda row, value: add(row, right(row) - value)
    add(0, level.fx[0] * field(1))
    sweep(1, 2, field, bound0, level.fx, level.fy, level.fz, emit)
    sweep(n0 - 1, n0, field, bound0, level.fx, level.fy, level.fz, emit)
    add(n0 + 1, level.fx[n0] * field(n0))
    fine_held = sizes.held[0]
    for index, first in ((1, 1), (2, 4)):
        level, n = levels[index], sizes.rows[index]
        held = sizes.held[index]
        narrow(
            sizes, place, index - 1, sums.at[:, :, :fine_held], level.source.outer, level.source.outer.shape[0]
        )
        binding = level.binding
        binding[0] = prev_row(index, first + 2)
        binding[n + 1] = next_row(index, first + 2)
        for row in range(n):
            binding[row + 1] = held_row(index, 1, row)

        def conduct(row, n=n, index=index, first=first):
            if row < 2:
                return prev_row(index, first + row)
            if row >= n + 2:
                return next_row(index, first + row - n - 2)
            return held_row(index, 0, row - 2)

        bound = lambda row, binding=binding: binding[row - 1]
        coefficients(
            sizes, place, index, conduct, bound, level.fx, level.fy, level.fz, level.weight, level.outer()
        )
        for row in level.outer()[2] if index == 1 else range(1, n + 3):
            level.smooth[row - 1] = level.weight[row - 1] * level.source[row - 1]
        zero = jnp.zeros((sizes.depth, held), f32)
        field = lambda row, level=level, n=n, zero=zero: level.smooth[row - 1] if 0 < row < n + 3 else zero
        add = in_pairs(sums.at[:, :, :held], lambda row: (row // 2, row % 2 == 0))
        emit = lambda row, value, level=level, add=add: add(row, level.source[row - 1] - value)
        add(0, level.fx[0] * field(1))
        sweep(1, n + 2, field, bound, level.fx, level.fy, level.fz, emit)
        add(n + 3, level.fx[n + 2] * field(n + 2))
        fine_held = held
    narrow(sizes, place, 2, sums.at[:, :, : sizes.held[2]], level3, 3)
    tiles = packing(3) + sizes.last
    pack_rows([level3[row] for row in range(3)], contribution)
    for kind, top in enumerate(tops):
        contribution[packing(3) + kind] = top[0]
    with_far[0:tiles] = contribution[...]
    v0, s1, v1 = levels[0].smooth, levels[1].source, levels[1].smooth
    s2, v2 = levels[2].source, levels[2].smooth
    next_rows = (v0[n0 - 1], s1[n1], v1[n1 - 1], s2[n2], s2[n2 + 1], v2[n2 - 1])
    prev_rows = (v0[0], s1[1], v1[2], s2[1], s2[0], v2[2])
    for slot, next_row, prev_row in zip(sizes.up_slots, next_rows, prev_rows):
        put_pair(place, ups, slot, next_row, prev_row)
    if s:
        ends = [fringes(sizes, list(zip((0, 1, 1, 2, 2, 2), rows))) for rows in (next_rows, prev_rows)]
        put_pair(place, ups, (sizes.up_tiles, 1), *ends)
    far_tiles = sizes.held[2] // LANES
    put_pair(place, (with_far.at[tiles : tiles + far_tiles], far), (0, far_tiles), v2[n2 + 1], v2[0], 2)


def relax(count, field, refs_of, source, target):
    fx, fy, fz, weight, binding = refs_of

    def update(row, value):
        target(row, field(row) + weight[row - 1] * (source(row) - value))

    sweep(1, count - 2, field, binding, fx, fy, fz, update)


def store(array, first):
    def put_row(row, value):
        array[row - first] = value

    return put_row


def coarse_kernel(sizes, stride, radix, place, *refs):
    blocks, refs = refs[:radix], refs[radix:]
    others, refs = [refs[side * radix : (side + 1) * radix] for side in range(sizes.sides)], refs[sizes.sides * radix :]
    tops, beside_tops, refs = refs[0], refs[1 : 1 + sizes.sides], refs[1 + sizes.sides :]
    out, merged, sums = refs[:3]
    coarse = [refs[3 + 9 * index : 12 + 9 * index] for index in range(3)]
    total = sizes.span_count
    merge_into(sizes, place, stride, radix, blocks, merged, others)
    position = (place[0] // stride) % radix
    for kind in range(radix):
        for low in range(stride):
            tile, beside_tiles = tops[kind, low], [array[kind, low] for array in beside_tops]
            rows = unpack_rows(sizes, place, tile[None], 2, [other[None] for other in beside_tiles])
            row = (position ^ kind) * stride + low
            coarse[0][4][row + 1], coarse[0][5][row] = rows
    zero = jnp.zeros((sizes.depth, LANES), f32)
    for index in range(3):
        level = 3 + index
        fx, fy, fz, weight, conduct, binding, source, smooth, iterate = coarse[index]
        count = total >> index
        for array in (conduct, smooth, iterate):
            array[0] = zero
            array[count + 1] = zero
        if index == 0:
            source = merged.at[1 : count + 1]
        bound = lambda row, binding=binding: binding[row - 1]
        at_row = lambda row, conduct=conduct: conduct[row]
        every = (range(1, count + 2), range(1, count + 1), range(1, count + 1))
        coefficients(sizes, place, level, at_row, bound, fx, fy, fz, weight, every)
        for row in range(count):
            smooth[row + 1] = weight[row] * source[row]
        if index < 2:
            conduct_next, binding_next, source_next = coarse[index + 1][4:7]
            half = count // 2
            for row in range(half):
                sums[row, :, :LANES] = conduct[2 * row + 1] + conduct[2 * row + 2]
            narrow(sizes, place, level, sums, conduct_next.at[1 : half + 1], half)
            for row in range(half):
                sums[row, :, :LANES] = binding[2 * row] + binding[2 * row + 1]
            narrow(sizes, place, level, sums, binding_next, half)

            def add(row, value, source=source):
                value = source[row - 1] - value
                slot = (row - 1) // 2
                if row % 2 == 1:
                    sums[slot, :, :LANES] = value
                else:
                    sums[slot, :, :LANES] = sums[slot, :, :LANES] + value

            sweep(1, count, lambda row, smooth=smooth: smooth[row], bound, fx, fy, fz, add)
            narrow(sizes, place, level, sums, source_next, half)

    fx, fy, fz, weight, conduct, binding, source, smooth, iterate = coarse[2]
    held, other = smooth, iterate
    for _ in range(COARSE_SWEEPS - 1):
        field = lambda row, held=held: held[row]
        mine = lambda row: source[row - 1]
        bound = lambda row: binding[row - 1]
        relax((total >> 2) + 2, field, (fx, fy, fz, weight, bound), mine, store(other, 0))
        held, other = other, held
    for index in (1, 0):
        fx, fy, fz, weight, conduct, binding, source, smooth, iterate = coarse[index]
        if index == 0:
            source = merged.at[1 : total + 1]
        count = total >> index
        widen(sizes, place, 3 + index, held.at[1 : count // 2 + 1], sums, count // 2)
        for row in range(count):
            smooth[row + 1] = smooth[row + 1] + sums[row // 2, :, :LANES]
        field = lambda row, smooth=smooth: smooth[row]
        mine = lambda row, source=source: source[row - 1]
        bound = lambda row, binding=binding: binding[row - 1]
        relax(count + 2, field, (fx, fy, fz, weight, bound), mine, store(iterate, 0))
        held = iterate

    out[...] = held[pl.ds(place[0], 3)]


def up_kernel(sizes, place, coarse, *refs):
    s = sizes.sides
    pair, far_pair, inners, outers, owns = refs[:2], refs[2:4], refs[4:7], refs[7:10], refs[10:12]
    levels = [Level(sizes, index, inner, outer) for index, (inner, outer) in enumerate(zip(inners, outers))]
    from_prev, from_next = (Arrived(place, pair, forward) for forward in (0, 1))
    tiles = packing(3) + sizes.last
    far_pair = (far_pair[0].at[tiles : tiles + sizes.held[2] // LANES], far_pair[1])
    fars = [Arrived(place, far_pair, forward, 2) for forward in (0, 1)]
    borders0, out, refs = refs[12 : 12 + 3 * s], refs[12 + 3 * s], refs[13 + 3 * s :]
    total1, total2, result, edges0, edges1 = refs[:5]
    over2, over1, over0, lift2, lift1, lift0, it2, it1, it0, semaphores = refs[5:]
    slots = sizes.slots
    n0, n1, n2 = sizes.rows[:3]
    width = sizes.own[0] * LANES

    before, behind = fringed_row(sizes, 0, 0, from_prev), fringed_row(sizes, 0, 0, from_next)
    lift0[0], lift0[n0 + 1] = before, behind
    edges0[0], edges0[1] = levels[0].fx[0] * before, levels[0].fx[n0] * behind
    narrow(sizes, place, 0, edges0, edges1, 2)

    widen(sizes, place, 2, coarse, over2, 3)
    for level, first, totals, over, lift, target, upper in (
        (2, 3, total2, over2, lift2, it2, over1),
        (1, 1, total1, over1, lift1, it1, over0),
    ):
        n, kept = sizes.rows[level], levels[level]
        fx, fy, fz, weight, binding = kept.fx, kept.fy, kept.fz, kept.weight, kept.binding
        own, smooth = kept.source, kept.smooth
        fringed = lambda index, message, level=level: fringed_row(sizes, level, index, message)
        if level == 1:
            smooth_at = first + 1
            edge = {2: own[1] + edges1[0], n + 1: own[n] + edges1[1]}
        else:
            smooth_at = first + 2
            edge = {2: own[1] + fringed(first + 1, from_prev)}
            edge[n + 1] = own[n] + fringed(first + 1, from_next)
        edge[1], edge[n + 2] = own[0] + fringed(first, from_prev), own[n + 1] + fringed(first, from_next)
        for row, value in edge.items():
            totals[row - 1] = value
        for row in range(n + 4):
            if row in (0, n + 3):
                value = fringed(smooth_at, from_next if row else from_prev)
                if level == 2:
                    far = fars[1 if row else 0]
                    value = value + jnp.concatenate(get(far, (0, sizes.held[2] // LANES)), axis=1)
            elif row in edge:
                value = weight[row - 1] * totals[row - 1]
            else:
                value = smooth[row - 1]
            lift[row] = value + over[row // 2]
        field = lambda row, lift=lift: lift[row]
        mine = lambda row, own=own, totals=totals, edge=edge: (totals if row in edge else own)[row - 1]
        bound = lambda row, binding=binding: binding[row - 1]
        relax(n + 4, field, (fx, fy, fz, weight, bound), mine, store(target, 1))
        widen(sizes, place, level - 1, target, upper, n + 2)

    held_row = held_rows(sizes, [owns[0], None, None, owns[1]], [borders0])
    fx, fy, fz, weight, v0 = levels[0].fx, levels[0].fy, levels[0].fz, levels[0].weight, levels[0].smooth
    lift0[0] = lift0[0] + over0[0]
    lift0[n0 + 1] = lift0[n0 + 1] + over0[n1 + 1]
    for row in range(1, n0 + 1):
        lift0[row] = v0[row - 1] + over0[(row + 1) // 2]
    field = lambda row: lift0[row]
    bound = lambda row: held_row(0, 1, row - 1)
    relax(n0 + 2, field, (fx, fy, fz, weight, bound), lambda row: held_row(0, 2, row - 1), store(it0, 1))
    step = sizes.depth // CHUNKS
    copies = []
    for chunk in range(CHUNKS):
        part = slice(chunk * step, (chunk + 1) * step)
        result[part] = jnp.swapaxes(it0[:, part, :width], 0, 1)
        copies.append(pltpu.make_async_copy(result.at[part], out.at[part], semaphores.at[chunk]))
        copies[-1].start()
    for copy in copies:
        copy.wait()


def call(body, name, micros, outputs, scratch, place, inputs, copies=0, far_out=False):
    near, far = pl.BlockSpec(memory_space=pltpu.VMEM), pl.BlockSpec(memory_space=pl.ANY)
    scratch = [pltpu.VMEM(shape, f32) for shape in scratch]
    if copies:
        scratch.append(pltpu.SemaphoreType.DMA((copies,)))
    return pl.pallas_call(
        body,
        name=name,
        out_shape=[jax.ShapeDtypeStruct(shape, f32) for shape in outputs],
        in_specs=[pl.BlockSpec(memory_space=pltpu.SMEM)] + [near] * len(inputs),
        out_specs=[far if far_out else near] * len(outputs),
        scratch_shapes=scratch,
        cost_estimate=pl.CostEstimate(flops=int(micros * 1.15e9), bytes_accessed=int(micros * BYTES_A_MICRO), transcendentals=0),
        compiler_params=pltpu.CompilerParams(vmem_limit_bytes=VMEM_LIMIT),
    )(place, *inputs)


def along(value, axis, steps):
    count = lax.axis_size(axis)
    initial, last = max(0, -steps), min(count, count - steps)
    return lax.ppermute(value, axis, [(source, source + steps) for source in range(initial, last)])


def beside(values, sizes):
    if sizes.sides == 1:
        return [[lax.ppermute(value, "width", [(0, 1), (1, 0)]) for value in values]]
    if sizes.sides == 2:
        return [[along(value, "width", steps) for value in values] for steps in (-1, 1)]
    return []


def edge_columns(edges, sizes):
    if sizes.sides == 1:
        return [lax.ppermute(edges[0], "width", [(0, 1), (1, 0)])]
    if sizes.sides == 2:
        return [along(edges[1], "width", -1), along(edges[0], "width", 1)]
    return []


def stages(count):
    stride = 1
    while stride < count:
        radix = 4 if count // stride % 4 == 0 else 2
        yield stride, radix
        stride *= radix


def swap(value, stride, radix, others=None):
    count = lax.axis_size("span")
    others = others or {}
    return [value] + [
        lax.ppermute(others.get(step, value), "span", [(device, device ^ step * stride) for device in range(count)])
        for step in range(1, radix)
    ]


def exchange(pair, stride):
    count = lax.axis_size("span")
    routes = [[], []]
    for low in range(count - stride):
        routes[low // stride % 2] += [(low, low + stride), (low + stride, low)]
    return [None if value is None else lax.ppermute(value, "span", route) for value, route in zip(pair, routes)]


def on_device(right_side, diffusivity, reaction):
    depth, extent_x, extent_y = diffusivity.shape
    sizes = Sizes(depth, extent_x, extent_y, lax.axis_size("span"), lax.axis_size("width"))
    place = jnp.stack([lax.axis_index("span"), lax.axis_index("width")]).astype(jnp.int32)
    n0, n1, n2, n3 = sizes.rows
    s = sizes.sides
    tile = (depth, LANES)
    own = [(depth, count * LANES) for count in sizes.own]
    held = [(depth, count) for count in sizes.held]
    down_message = (sizes.tiles, *tile)
    up_message = (sizes.up_tiles + 1, *tile)
    own0, own1, own2, first, second, top, *edges = call(
        functools.partial(start_kernel, sizes),
        "start",
        1.1,
        [(2, n0, *own[0]), (2 * n1, *own[1]), (2 * n2, *own[2]), down_message, down_message, (1, *tile)]
        + [(n0, depth, BORDER)] * 2 * s,
        [(2 * n1, *own[0])],
        place,
        [diffusivity, reaction],
    )
    borders = edge_columns(edges[:s], sizes) + edge_columns(edges[s:], sizes)
    halos = exchange([first, second], 1)
    turned, *edges = call(
        functools.partial(turn_kernel, sizes),
        "turn",
        0.7,
        [(n0, *own[0])] + [(n0, depth, BORDER)] * s,
        [],
        place,
        [right_side],
    )
    borders += edge_columns(edges, sizes)
    plan = list(stages(sizes.span_count))

    part = packing(3) + sizes.last
    far = (sizes.held[2] // LANES, *tile)
    inners = [(sum(inner_rows(sizes, level)), *held[level]) for level in range(3)]
    outers = [(sum(outer_rows(sizes, level)), *held[level]) for level in range(3)]
    inner = call(
        functools.partial(inner_kernel, sizes),
        "inner",
        0.5,
        [(2 * n1, *tile), (2 * n2, *tile), *inners],
        [(2 * n1, *held[0])],
        place,
        [own0, own1, own2, turned, *borders],
    )
    inner, top = lax.optimization_barrier((inner, top))
    tops = swap(top, *plan[-1])
    halos, inner, tops = lax.optimization_barrier((halos, inner, tops))
    sides = beside(halos, sizes)
    downs = call(
        functools.partial(down_kernel, sizes),
        "down",
        2.5,
        [*outers, (part, *tile), (part + far[0], *tile), up_message, up_message, far],
        [(3, *tile), (n1 + 2, *held[0])],
        place,
        [own0, own1, own2, turned, *borders, *halos, *sum(sides, []), *inner, *tops],
    )
    outer, blocks, with_far, ups, far_second = downs[:3], downs[3], downs[4], list(downs[5:7]), downs[7]
    far_rows = None
    for stride, radix in plan[:-1]:
        count = stride * radix
        if far_rows is None:
            blocks = swap(blocks, stride, radix, {2: with_far})
            far_rows = [blocks[2]]
            blocks[1], ups[0] = lax.optimization_barrier((blocks[1], ups[0]))
        else:
            blocks = swap(blocks, stride, radix)
        final = (stride, radix) == plan[-2]
        rows = packing(count + 2) + (0 if final else sizes.last * count)
        blocks, top_tiles = call(
            functools.partial(merge_kernel, sizes, stride, radix, final),
            "merge",
            0.7,
            [(rows, *tile), (sizes.last, count, *tile)],
            [(count + 2, *tile)],
            place,
            blocks,
        )
    stride, radix = plan[-1]
    blocks = swap(blocks, stride, radix)
    received = lax.optimization_barrier([exchange([ups[0], None], 1)[0], ups[1]])
    far_rows.append(exchange([None, far_second], 2)[1])
    received = [received[0], exchange([None, received[1]], 1)[1]] + far_rows
    scratch = [(sizes.span_count + 2, *tile), (max(sizes.span_count // 2, 2), *tile)]
    for index in range(3):
        count = sizes.span_count >> index
        scratch += [(count + 1, *tile)] + [(count, *tile)] * 3 + [(count + 2, *tile)] + [(count, *tile)] * 2
        scratch += [(count + 2, *tile)] * 2
    blocks, received[3], top_tiles = lax.optimization_barrier((blocks, received[3], top_tiles))
    (coarse,) = call(
        functools.partial(coarse_kernel, sizes, stride, radix),
        "coarse",
        0.01,
        [(n3 + 2, *tile)],
        scratch,
        place,
        [*blocks, *sum(beside(blocks, sizes), []), top_tiles, *sum(beside([top_tiles], sizes), [])],
    )
    scratch = [(n1 + 2, *held[1]), (n2 + 2, *held[2]), diffusivity.shape, (2, *held[0]), (2, *held[1])]
    scratch += [(n3 + 2, *held[2]), (n2 + 2, *held[1]), (n1 + 2, *held[0])]
    scratch += [(n2 + 4, *held[2]), (n1 + 4, *held[1]), (n0 + 2, *held[0])]
    scratch += [(n2 + 2, *held[2]), (n1 + 2, *held[1]), (n0, *held[0])]
    (correction,) = call(
        functools.partial(up_kernel, sizes),
        "up",
        3.0,
        [diffusivity.shape],
        scratch,
        place,
        [coarse, *received, *inner[2:], *outer, own0, turned, *borders],
        copies=CHUNKS,
        far_out=True,
    )
    return correction


def solution(mesh):
    in_specs = (P(None, "span", "width"),) * 3
    return jax.shard_map(
        on_device, mesh=mesh, in_specs=in_specs, out_specs=P(None, "span", "width"), check_vma=False
    )
```

```python
import functools

import jax
import jax.numpy as jnp
from jax import lax
from jax.experimental import pallas as pl
from jax.experimental.pallas import tpu as pltpu
from jax.sharding import PartitionSpec as P

LEVELS = 6
COARSE_SWEEPS = 3
LANES = 128
BORDER = 128
FRINGE = 4
SPREAD = 16
relax_weight = 0.8
f32 = jnp.float32
VMEM_LIMIT = 32 * 1024 * 1024
BYTES_A_MICRO = 3.69e6
CHUNKS = 4


class Sizes:
    def __init__(self, depth, extent_x, extent_y, span_count, width_count):
        self.depth, self.extent_x, self.extent_y = depth, extent_x, extent_y
        self.span_count, self.width_count = span_count, width_count
        self.sides = min(width_count - 1, 2)
        self.own = [(extent_y >> level) // LANES for level in range(3)]
        self.border = [self.sides, min(self.sides, 1), min(self.sides, 1)]
        self.held = [(self.own[level] + self.border[level]) * LANES for level in range(3)] + [LANES] * 3
        self.rows = [extent_x >> level for level in range(4)]
        self.slots = []
        start = 0
        for level in (0, 1, 1, 1, 2, 2):
            self.slots.append((start, self.own[level]))
            start += self.own[level]
        self.tiles = start
        self.up_slots = []
        start = 0
        for level in (0, 1, 1, 2, 2, 2):
            self.up_slots.append((start, self.own[level]))
            start += self.own[level]
        self.up_tiles = start


def put(message, slot, row):
    start, tiles = slot
    for tile in range(tiles):
        message[start + tile] = row[:, tile * LANES : (tile + 1) * LANES]


class Arrived:
    def __init__(self, place, pair, forward, stride=1):
        self.even = place[0] // stride % 2 == 0
        self.first, self.second = (pair[0], pair[1]) if forward else (pair[1], pair[0])

    def __getitem__(self, index):
        return jnp.where(self.even, self.first[index], self.second[index])


def put_pair(place, pair, slot, next_row, prev_row, stride=1):
    even = place[0] // stride % 2 == 0
    put(pair[0], slot, jnp.where(even, next_row, prev_row))
    put(pair[1], slot, jnp.where(even, prev_row, next_row))


def get(message, slot):
    start, tiles = slot
    return [message[start + tile] for tile in range(tiles)]


def lane_at(shape):
    return lax.broadcasted_iota(jnp.int32, shape, len(shape) - 1)


def roll(value, steps, axis):
    return pltpu.roll(value, steps % value.shape[axis], axis=axis)


def reciprocal(value):
    return pltpu.reciprocal(value, approx=True)


def harmonic(first, second, guard):
    total = first + second
    if guard:
        total = jnp.maximum(total, 1e-3)
    return (2.0 * first) * second * reciprocal(total)


def split(value):
    high = value.astype(jnp.bfloat16)
    return high, (value - high.astype(f32)).astype(jnp.bfloat16)


def dot(halves, table):
    high, low = halves
    return jnp.dot(high, table, preferred_element_type=f32) + jnp.dot(low, table, preferred_element_type=f32)


def pair_table(fine, fine_dim, turn, weight):
    shape = (fine, LANES) if fine_dim == 0 else (LANES, fine)
    fine_at = lax.broadcasted_iota(jnp.int32, shape, fine_dim)
    coarse_at = lax.broadcasted_iota(jnp.int32, shape, 1 - fine_dim)
    if turn is not None:
        coarse_at = coarse_at - jnp.where(fine_at >= turn, LANES // 2, 0)
    return jnp.where(fine_at // 2 == coarse_at, weight, 0.0).astype(jnp.bfloat16)


def turns(sizes, place, level):
    if sizes.sides == 0:
        return []
    if level == 0:
        return [jnp.where(place[1] == 0, LANES, 0)] if sizes.sides == 1 else [LANES, 0]
    return [LANES // 2]


def transfer_plan(sizes, place, level, part):
    plan = []
    if level >= 3:
        return [((0, LANES), 0, 3 * LANES // 4)]
    if level == 2:
        return [((0, sizes.held[2]), 0, None)]
    own = sizes.own[level]
    if part != "border":
        plan += [((2 * LANES * tile, 2 * LANES * (tile + 1)), tile, None) for tile in range(own // 2)]
    if part != "own":
        for index, turn in enumerate(turns(sizes, place, level)):
            start = (own + index) * LANES
            plan.append(((start, start + LANES), own // 2, turn))
    return plan


def narrow(sizes, place, level, sums, target, rows, part="all", shift=0):
    depth = sums.shape[1]
    done = {}
    for (start, stop), tile, turn in transfer_plan(sizes, place, level, part):
        start, stop, tile = start - shift, stop - shift, tile - shift // (2 * LANES)
        columns = split(sums[0:rows, :, start:stop].reshape(rows * depth, stop - start))
        result = dot(columns, pair_table(stop - start, 0, turn, 0.25)).reshape(rows, depth, LANES)
        done[tile] = done[tile] + result if tile in done else result
    for tile, result in done.items():
        target[0:rows, :, tile * LANES : (tile + 1) * LANES] = result


def widen(sizes, place, level, coarse, target, rows):
    depth = coarse.shape[1]
    for (start, stop), tile, turn in transfer_plan(sizes, place, level, "all"):
        columns = split(coarse[0:rows, :, tile * LANES : (tile + 1) * LANES].reshape(rows * depth, LANES))
        result = dot(columns, pair_table(stop - start, 1, turn, 4.0))
        target[0:rows, :, start:stop] = result.reshape(rows, depth, stop - start)


class Joined:
    def __init__(self, inner, outer, first):
        self.inner, self.outer, self.first = inner, outer, first

    def find(self, row):
        place, count = row - self.first, 0 if self.inner is None else self.inner.shape[0]
        if 0 <= place < count:
            return self.inner, place
        return self.outer, row if place < 0 else row - count

    def __getitem__(self, row):
        array, place = self.find(row)
        return array[place]

    def __setitem__(self, row, value):
        array, place = self.find(row)
        array[place] = value


class Level:
    def __init__(self, sizes, level, inner, outer):
        self.n, self.halo = sizes.rows[level], 1 if level == 0 else 2
        counts = inner_rows(sizes, level)
        fx, fy, fz, *rest = parts(inner, counts)
        weight, source, smooth = (None, None, None) if level == 2 else (rest[0], None, rest[1])
        if level == 1:
            weight, source, smooth = rest
        others = [None] * 7 if outer is None else parts(outer, outer_rows(sizes, level))
        if level == 0 and outer is not None:
            others = [others[0], None, None, others[1], None, others[2], None]
        h = self.halo
        self.fx = Joined(fx, others[0], h)
        self.fy, self.fz = Joined(fy, others[1], h - 1), Joined(fz, others[2], h - 1)
        self.weight, self.source, self.smooth = (
            Joined(array, other, h) for array, other in zip((weight, source, smooth), others[3:6])
        )
        self.binding = others[6]

    def inner(self):
        first, last = self.halo, self.halo + self.n - 1
        return range(first + 1, last + 1), range(first, last + 1), range(first + 1, last)

    def outer(self):
        count = self.n + 2 * self.halo
        every = (range(1, count), range(1, count - 1), range(1, count - 1))
        return tuple([row for row in rows if row not in mine] for rows, mine in zip(every, self.inner()))


def inner_rows(sizes, level):
    n = sizes.rows[level]
    return [n - 1, n, n] + [[n - 2] * 2, [n - 2] * 3, []][level]


def outer_rows(sizes, level):
    n = sizes.rows[level]
    return [[2, 2, 2], [4, 2, 2, 4, 4, 4, n + 2], [4, 2, 2] + [n + 2] * 4][level]


def coefficients(sizes, place, level, conduct, binding, fx, fy, fz, weight, rows):
    guard = level > 0 or sizes.sides > 1
    for row in rows[0]:
        fx[row - 1] = harmonic(conduct(row - 1), conduct(row), guard)
    for row in rows[1]:
        mine = conduct(row)
        south = harmonic(mine, roll(mine, 1, 1), guard)
        if level == 0 and sizes.sides < 2:
            cut = 0 if sizes.sides == 0 else jnp.where(place[1] == 0, 0, sizes.extent_y)
            south = jnp.where(lane_at(mine.shape) == cut, 0.0, south)
        below = harmonic(mine, roll(mine, 1, 0), guard)
        fy[row - 1] = south
        fz[row - 1] = jnp.where(lax.broadcasted_iota(jnp.int32, mine.shape, 0) == 0, 0.0, below)
    for row in rows[2]:
        south, below = fy[row - 1], fz[row - 1]
        diagonal = fx[row - 1] + fx[row] + binding(row)
        diagonal = diagonal + (south + roll(south, -1, 1)) + (below + roll(below, -1, 0))
        if guard:
            diagonal = jnp.maximum(diagonal, 1e-6)
        weight[row - 1] = relax_weight * reciprocal(diagonal)


def sweep(first, last, field, binding, fx, fy, fz, emit):
    lower = fx[first - 1] * (field(first) - field(first - 1))
    for row in range(first, last + 1):
        mine = field(row)
        upper = fx[row] * (field(row + 1) - mine)
        south = fy[row - 1] * (mine - roll(mine, 1, 1))
        below = fz[row - 1] * (mine - roll(mine, 1, 0))
        across = (south - roll(south, -1, 1)) + (below - roll(below, -1, 0))
        emit(row, binding(row) * mine + (lower - upper) + across)
        lower = upper


def in_pairs(sums, slot_of):
    def add(row, value):
        slot, first = slot_of(row)
        if first:
            sums[slot] = value
        else:
            sums[slot] = sums[slot] + value

    return add


def parts(array, counts):
    views, start = [], 0
    for count in counts:
        views.append(array.at[start : start + count])
        start += count
    return views


def start_kernel(sizes, place, conduct, binding, own0, own1, own2, first, second, *refs):
    edges, sums = refs[: 2 * sizes.sides], refs[-1]
    n0, n1, n2 = sizes.rows[:3]
    for at, array in enumerate((conduct, binding)):
        own0[at] = jnp.swapaxes(array[...], 0, 1)
    for at in (0, 1):
        for row in range(n1):
            sums[at * n1 + row] = own0[at, 2 * row] + own0[at, 2 * row + 1]
    narrow(sizes, place, 0, sums, own1, 2 * n1, "own")
    for row in range(2 * n2):
        sums[row, :, : sizes.own[1] * LANES] = own1[2 * row] + own1[2 * row + 1]
    narrow(sizes, place, 1, sums, own2, 2 * n2, "own")
    ends = []
    for low, at1, at0 in ((n1 - 2, n1 - 1, n0 - 1), (0, 0, 0)):
        near, far = (n2 - 1, n2 - 2) if at0 else (0, 1)
        rows = (own0[0, at0], own1[low], own1[low + 1], own1[n1 + at1], own2[far], own2[n2 + near])
        ends.append(rows)
    for slot, next_row, prev_row in zip(sizes.slots, *ends):
        put_pair(place, (first, second), slot, next_row, prev_row)
    for at in (0, 1):
        cut_edges(sizes, place, own0.at[at], edges[at * sizes.sides : (at + 1) * sizes.sides])


def cut_edges(sizes, place, array, edges):
    last = sizes.extent_y - BORDER
    if sizes.sides == 1:
        at = pl.multiple_of(jnp.where(place[1] == 0, last, 0), LANES)
        edges[0][...] = array[:, :, pl.ds(at, BORDER)]
    elif sizes.sides == 2:
        edges[0][...] = array[:, :, last:]
        edges[1][...] = array[:, :, :BORDER]


def turn_kernel(sizes, place, right_side, turned, *edges):
    turned[...] = jnp.swapaxes(right_side[...], 0, 1)
    cut_edges(sizes, place, turned, edges)


def message_row(sizes, place, level, slot, message, beside):
    start, tiles = slot
    row = get(message, slot)
    if sizes.sides == 1:
        left = place[1] != 0
        tile = beside[0][start + jnp.where(left, tiles - 1, 0)]
        if level > 0:
            reach = BORDER >> level
            lane = lane_at(tile.shape)
            first = jnp.where(left, LANES - reach, 0)
            tile = jnp.where((lane >= first) & (lane < first + reach), tile, 0.0)
        row.append(tile)
    elif sizes.sides == 2:
        right, left = beside[0][start], beside[1][start + tiles - 1]
        if level == 0:
            row += [right, left]
        else:
            reach = BORDER >> level
            lane = lane_at(right.shape)
            row.append(jnp.where(lane < reach, right, jnp.where(lane >= LANES - reach, left, 0.0)))
    return jnp.concatenate(row, axis=1)


def fringe_lanes(shape):
    lane = lane_at(shape)
    return (lane < FRINGE) | (lane >= LANES - FRINGE)


def fringes(sizes, rows):
    total = None
    for index, (level, row) in enumerate(rows):
        border = row[:, sizes.own[level] * LANES :]
        tile = border[:, :LANES]
        lane = lane_at(tile.shape)
        if border.shape[1] > LANES:
            tile = jnp.where(lane < FRINGE, tile, border[:, LANES:])
        tile = jnp.where((lane < FRINGE) | (lane >= LANES - FRINGE), tile, 0.0)
        tile = roll(tile, SPREAD * index + SPREAD // 2, 1)
        total = tile if total is None else total + tile
    return total


def fringed_row(sizes, level, index, message):
    row = get(message, sizes.up_slots[index])
    if sizes.border[level]:
        tile = roll(message[sizes.up_tiles], -(SPREAD * index + SPREAD // 2), 1)
        lane = lane_at(tile.shape)
        right, left = jnp.where(lane < FRINGE, tile, 0.0), jnp.where(lane >= LANES - FRINGE, tile, 0.0)
        row += [right, left] if sizes.border[level] == 2 else [right + left]
    return jnp.concatenate(row, axis=1)


def packing(count):
    return -(-count // 2)


def pack_rows(rows, target):
    half = LANES // 2
    lane = lane_at(rows[0].shape)
    for index in range(packing(len(rows))):
        held = jnp.where(lane < half, rows[2 * index], 0.0)
        if 2 * index + 1 < len(rows):
            held = jnp.where(lane < half, held, pltpu.roll(rows[2 * index + 1], half, axis=1))
        target[index] = held


def unpack_rows(sizes, place, tiles, count, others=()):
    half, reach = LANES // 2, BORDER >> 3
    lane = lane_at(tiles.shape[1:])
    rows = []
    for index in range(count):
        held = tiles[index // 2]
        row = jnp.where(lane < half, pltpu.roll(held, half, axis=1) if index % 2 else held, 0.0)
        for side, other in enumerate(others):
            first = LANES - reach if side else half
            if sizes.sides == 1:
                first = jnp.where(place[1] == 0, half, LANES - reach)
            beside = other[index // 2]
            beside = beside if index % 2 else pltpu.roll(beside, half, axis=1)
            row = jnp.where((lane >= first) & (lane < first + reach), beside, row)
        rows.append(row)
    return rows


def merge_into(sizes, place, stride, radix, arrays, source, conduct, binding, first, others=()):
    position = (place[0] // stride) % radix
    source[...] = jnp.zeros(source.shape, f32)
    for step, array in enumerate(arrays):
        at = (position ^ step) * stride
        rows = unpack_rows(sizes, place, array, 3 * stride + 2, [other[step] for other in others])
        for index, row in enumerate(rows[: stride + 2]):
            source[at + index] = source[at + index] + row
        for index in range(stride):
            conduct[at + index + first] = rows[stride + 2 + index]
            binding[at + index] = rows[2 * stride + 2 + index]


def merge_kernel(sizes, stride, radix, place, *refs):
    arrays, out, (source, conduct, binding) = refs[:radix], refs[radix], refs[radix + 1 :]
    merge_into(sizes, place, stride, radix, arrays, source, conduct, binding, 0)
    count = stride * radix
    rows = [source[row] for row in range(count + 2)]
    rows += [conduct[row] for row in range(count)] + [binding[row] for row in range(count)]
    pack_rows(rows, out)


def held_rows(sizes, owns, borders):
    def held_row(level, at, row):
        if level > 0:
            row = at * sizes.rows[level] + row
            return jnp.concatenate([owns[level][row], *(array[row] for array in borders[level])], axis=1)
        own = owns[3][row] if at == 2 else owns[0][at, row]
        sides = len(borders[0]) // 3
        return jnp.concatenate([own, *(array[row] for array in borders[0][at * sides : (at + 1) * sides])], axis=1)

    return held_row


def inner_kernel(sizes, place, *refs):
    s = sizes.sides
    owns, borders0, refs = refs[:4], refs[4 : 4 + 3 * s], refs[4 + 3 * s :]
    border1, border2, inner0, inner1, inner2, sums = refs
    n0, n1, n2 = sizes.rows[:3]
    if s:
        for row in range(2 * n1):
            for side in range(s):
                columns = slice(side * LANES, (side + 1) * LANES)
                at, low = row // n1, 2 * (row % n1)
                sums[row, :, columns] = borders0[at * s + side][low] + borders0[at * s + side][low + 1]
        narrow(sizes, place, 0, sums, border1, 2 * n1, "border", sizes.own[0] * LANES)
        for row in range(2 * n2):
            sums[row, :, :LANES] = border1[2 * row] + border1[2 * row + 1]
        narrow(sizes, place, 1, sums, border2, 2 * n2, "border", sizes.own[1] * LANES)
    held_row = held_rows(sizes, owns, [borders0, [border1][:s], [border2][:s]])
    levels = [Level(sizes, level, inner, None) for level, inner in enumerate((inner0, inner1, inner2))]
    for index, level in enumerate(levels):
        conduct = lambda row, index=index, level=level: held_row(index, 0, row - level.halo)
        bound = lambda row, index=index, level=level: held_row(index, 1, row - level.halo)
        coefficients(
            sizes, place, index, conduct, bound, level.fx, level.fy, level.fz, level.weight, level.inner()
        )
        if index == 0:
            right = lambda row: held_row(0, 2, row - 1)
            for row in range(2, n0):
                level.smooth[row - 1] = level.weight[row - 1] * right(row)
            add = in_pairs(sums, lambda row: ((row - 3) // 2, row % 2 == 1))
            field = lambda row, level=level: level.smooth[row - 1]
            emit = lambda row, value: add(row, right(row) - value)
            sweep(3, n0 - 2, field, bound, level.fx, level.fy, level.fz, emit)
        if index == 1:
            narrow(sizes, place, 0, sums, level.source.inner, n1 - 2)
            for row in range(2, n1):
                level.smooth[row] = level.weight[row] * level.source[row]


def down_kernel(sizes, place, *refs):
    s = sizes.sides
    owns, borders0, refs = refs[:4], refs[4 : 4 + 3 * s], refs[4 + 3 * s :]
    pairs_of = [refs[2 * index : 2 * index + 2] for index in range(1 + s)]
    refs = refs[2 * (1 + s) :]
    from_prev, *beside_prev = (Arrived(place, pair, 0) for pair in pairs_of)
    from_next, *beside_next = (Arrived(place, pair, 1) for pair in pairs_of)
    (border1, border2), inners, refs = refs[:2], refs[2:5], refs[5:]
    outers, contribution, with_far, ups, far, refs = refs[:3], refs[3], refs[4], refs[5:7], refs[7], refs[8:]
    level3, near, sums = refs
    slots = sizes.slots
    n0, n1, n2 = sizes.rows[:3]
    levels = [Level(sizes, index, inner, outer) for index, (inner, outer) in enumerate(zip(inners, outers))]
    held_row = held_rows(sizes, owns, [borders0, [border1][:s], [border2][:s]])

    def prev_row(level, index):
        return message_row(sizes, place, level, slots[index], from_prev, beside_prev)

    def next_row(level, index):
        return message_row(sizes, place, level, slots[index], from_next, beside_next)

    def conduct0(row):
        if row == 0:
            return prev_row(0, 0)
        if row == n0 + 1:
            return next_row(0, 0)
        return held_row(0, 0, row - 1)

    for at, row_of in enumerate((prev_row, next_row)):
        sums[at, :, : sizes.held[1]] = row_of(1, 1) + row_of(1, 2)
    narrow(sizes, place, 1, sums.at[:, :, : sizes.held[1]], near, 2)
    zero = jnp.zeros((sizes.depth, sizes.held[0]), f32)
    level = levels[0]
    bound0 = lambda row: held_row(0, 1, row - 1)
    right = lambda row: held_row(0, 2, row - 1)
    coefficients(
        sizes, place, 0, conduct0, bound0, level.fx, level.fy, level.fz, level.weight, level.outer()
    )
    for row in (1, n0):
        level.smooth[row - 1] = level.weight[row - 1] * right(row)
    first_slot = lambda row: (row + 1) // 2
    add = in_pairs(
        sums,
        lambda row: (first_slot(row) - (n1 - 2 if row > n0 // 2 else 0), row % 2 == 1 or row == 0),
    )
    field = lambda row, level=level: level.smooth[row - 1] if 0 < row < n0 + 1 else zero
    emit = lambda row, value: add(row, right(row) - value)
    add(0, level.fx[0] * field(1))
    sweep(1, 2, field, bound0, level.fx, level.fy, level.fz, emit)
    sweep(n0 - 1, n0, field, bound0, level.fx, level.fy, level.fz, emit)
    add(n0 + 1, level.fx[n0] * field(n0))
    fine_held = sizes.held[0]
    for index in (1, 2):
        level, n = levels[index], sizes.rows[index]
        held = sizes.held[index]
        narrow(
            sizes, place, index - 1, sums.at[:, :, :fine_held], level.source.outer, level.source.outer.shape[0]
        )
        binding = level.binding
        binding[0] = prev_row(index, 3 if index == 1 else 5)
        binding[n + 1] = next_row(index, 3 if index == 1 else 5)
        for row in range(n):
            binding[row + 1] = held_row(index, 1, row)

        def conduct(row, n=n, index=index):
            if 2 <= row < n + 2:
                return held_row(index, 0, row - 2)
            if index == 1:
                return prev_row(1, 1 + row) if row < 2 else next_row(1, row - n - 1)
            if row in (1, n + 2):
                return near[0 if row == 1 else 1]
            return (prev_row if row == 0 else next_row)(2, 4)

        bound = lambda row, binding=binding: binding[row - 1]
        coefficients(
            sizes, place, index, conduct, bound, level.fx, level.fy, level.fz, level.weight, level.outer()
        )
        for row in level.outer()[2] if index == 1 else range(1, n + 3):
            level.smooth[row - 1] = level.weight[row - 1] * level.source[row - 1]
        zero = jnp.zeros((sizes.depth, held), f32)
        field = lambda row, level=level, n=n, zero=zero: level.smooth[row - 1] if 0 < row < n + 3 else zero
        add = in_pairs(sums.at[:, :, :held], lambda row: (row // 2, row % 2 == 0))
        emit = lambda row, value, level=level, add=add: add(row, level.source[row - 1] - value)
        add(0, level.fx[0] * field(1))
        sweep(1, n + 2, field, bound, level.fx, level.fy, level.fz, emit)
        add(n + 3, level.fx[n + 2] * field(n + 2))
        fine_held = held
    narrow(sizes, place, 2, sums.at[:, :, : sizes.held[2]], level3, 3)
    for at in (0, 1):
        sums[at, :, : sizes.held[2]] = held_row(2, at, 0) + held_row(2, at, 1)
    narrow(sizes, place, 2, sums.at[:, :, : sizes.held[2]], level3.at[3:5], 2)
    tiles = packing(5)
    pack_rows([level3[row] for row in range(5)], contribution)
    with_far[0:tiles] = contribution[...]
    v0, s1, v1 = levels[0].smooth, levels[1].source, levels[1].smooth
    s2, v2 = levels[2].source, levels[2].smooth
    next_rows = (v0[n0 - 1], s1[n1], v1[n1 - 1], s2[n2], s2[n2 + 1], v2[n2 - 1])
    prev_rows = (v0[0], s1[1], v1[2], s2[1], s2[0], v2[2])
    for slot, next_row, prev_row in zip(sizes.up_slots, next_rows, prev_rows):
        put_pair(place, ups, slot, next_row, prev_row)
    if s:
        ends = [fringes(sizes, list(zip((0, 1, 1, 2, 2, 2), rows))) for rows in (next_rows, prev_rows)]
        put_pair(place, ups, (sizes.up_tiles, 1), *ends)
    far_tiles = sizes.held[2] // LANES
    put_pair(place, (with_far.at[tiles : tiles + far_tiles], far), (0, far_tiles), v2[n2 + 1], v2[0], 2)


def relax(count, field, refs_of, source, target):
    fx, fy, fz, weight, binding = refs_of

    def update(row, value):
        target(row, field(row) + weight[row - 1] * (source(row) - value))

    sweep(1, count - 2, field, binding, fx, fy, fz, update)


def store(array, first):
    def put_row(row, value):
        array[row - first] = value

    return put_row


def coarse_kernel(sizes, stride, radix, place, *refs):
    blocks, refs = refs[:radix], refs[radix:]
    others, refs = [refs[side * radix : (side + 1) * radix] for side in range(sizes.sides)], refs[sizes.sides * radix :]
    out, merged, sums, both, defects = refs[:5]
    coarse = [refs[5 + 9 * index : 14 + 9 * index] for index in range(3)]
    total = sizes.span_count
    merge_into(sizes, place, stride, radix, blocks, merged, coarse[0][4], coarse[0][5], 1, others)
    zero = jnp.zeros((sizes.depth, LANES), f32)
    for index in range(3):
        level = 3 + index
        fx, fy, fz, weight, conduct, binding, source, smooth, iterate = coarse[index]
        count, half = total >> index, total >> index + 1
        for array in (conduct, smooth, iterate):
            array[0] = zero
            array[count + 1] = zero
        if index < 2:
            conduct_next, binding_next = coarse[index + 1][4:6]
            for row in range(half):
                sums[row] = conduct[2 * row + 1] + conduct[2 * row + 2]
                sums[half + row] = binding[2 * row] + binding[2 * row + 1]
            narrow(sizes, place, level, sums, both, 2 * half)
            for row in range(half):
                conduct_next[row + 1], binding_next[row] = both[row], both[half + row]
        bound = lambda row, binding=binding: binding[row - 1]
        at_row = lambda row, conduct=conduct: conduct[row]
        every = (range(1, count + 2), range(1, count + 1), range(1, count + 1))
        coefficients(sizes, place, level, at_row, bound, fx, fy, fz, weight, every)
    for index in range(3):
        level = 3 + index
        fx, fy, fz, weight, conduct, binding, source, smooth, iterate = coarse[index]
        count = total >> index
        bound = lambda row, binding=binding: binding[row - 1]
        if index == 0:
            source = merged.at[1 : count + 1]
        for row in range(count):
            smooth[row + 1] = weight[row] * source[row]
        if index < 2:
            add = in_pairs(defects, lambda row: ((row - 1) // 2, row % 2 == 1))
            emit = lambda row, value, source=source, add=add: add(row, source[row - 1] - value)
            sweep(1, count, lambda row, smooth=smooth: smooth[row], bound, fx, fy, fz, emit)
            narrow(sizes, place, level, defects, coarse[index + 1][6], count // 2)

    fx, fy, fz, weight, conduct, binding, source, smooth, iterate = coarse[2]
    held, other = smooth, iterate
    for _ in range(COARSE_SWEEPS - 1):
        field = lambda row, held=held: held[row]
        mine = lambda row: source[row - 1]
        bound = lambda row: binding[row - 1]
        relax((total >> 2) + 2, field, (fx, fy, fz, weight, bound), mine, store(other, 0))
        held, other = other, held
    for index in (1, 0):
        fx, fy, fz, weight, conduct, binding, source, smooth, iterate = coarse[index]
        if index == 0:
            source = merged.at[1 : total + 1]
        count = total >> index
        widen(sizes, place, 3 + index, held.at[1 : count // 2 + 1], sums, count // 2)
        for row in range(count):
            smooth[row + 1] = smooth[row + 1] + sums[row // 2, :, :LANES]
        field = lambda row, smooth=smooth: smooth[row]
        mine = lambda row, source=source: source[row - 1]
        bound = lambda row, binding=binding: binding[row - 1]
        relax(count + 2, field, (fx, fy, fz, weight, bound), mine, store(iterate, 0))
        held = iterate

    out[...] = held[pl.ds(place[0], 3)]


def up_kernel(sizes, place, coarse, *refs):
    s = sizes.sides
    pair, far_pair, inners, outers, owns = refs[:2], refs[2:4], refs[4:7], refs[7:10], refs[10:12]
    levels = [Level(sizes, index, inner, outer) for index, (inner, outer) in enumerate(zip(inners, outers))]
    from_prev, from_next = (Arrived(place, pair, forward) for forward in (0, 1))
    tiles = packing(5)
    far_pair = (far_pair[0].at[tiles : tiles + sizes.held[2] // LANES], far_pair[1])
    fars = [Arrived(place, far_pair, forward, 2) for forward in (0, 1)]
    borders0, out, refs = refs[12 : 12 + 3 * s], refs[12 + 3 * s], refs[13 + 3 * s :]
    total1, total2, result, edges0, edges1 = refs[:5]
    over2, over1, over0, lift2, lift1, lift0, it2, it1, it0, semaphores = refs[5:]
    slots = sizes.slots
    n0, n1, n2 = sizes.rows[:3]
    width = sizes.own[0] * LANES

    before, behind = fringed_row(sizes, 0, 0, from_prev), fringed_row(sizes, 0, 0, from_next)
    lift0[0], lift0[n0 + 1] = before, behind
    edges0[0], edges0[1] = levels[0].fx[0] * before, levels[0].fx[n0] * behind
    narrow(sizes, place, 0, edges0, edges1, 2)

    widen(sizes, place, 2, coarse, over2, 3)
    for level, first, totals, over, lift, target, upper in (
        (2, 3, total2, over2, lift2, it2, over1),
        (1, 1, total1, over1, lift1, it1, over0),
    ):
        n, kept = sizes.rows[level], levels[level]
        fx, fy, fz, weight, binding = kept.fx, kept.fy, kept.fz, kept.weight, kept.binding
        own, smooth = kept.source, kept.smooth
        fringed = lambda index, message, level=level: fringed_row(sizes, level, index, message)
        if level == 1:
            smooth_at = first + 1
            edge = {2: own[1] + edges1[0], n + 1: own[n] + edges1[1]}
        else:
            smooth_at = first + 2
            edge = {2: own[1] + fringed(first + 1, from_prev)}
            edge[n + 1] = own[n] + fringed(first + 1, from_next)
        edge[1], edge[n + 2] = own[0] + fringed(first, from_prev), own[n + 1] + fringed(first, from_next)
        for row, value in edge.items():
            totals[row - 1] = value
        for row in range(n + 4):
            if row in (0, n + 3):
                value = fringed(smooth_at, from_next if row else from_prev)
                if level == 2:
                    far = fars[1 if row else 0]
                    value = value + jnp.concatenate(get(far, (0, sizes.held[2] // LANES)), axis=1)
            elif row in edge:
                value = weight[row - 1] * totals[row - 1]
            else:
                value = smooth[row - 1]
            lift[row] = value + over[row // 2]
        field = lambda row, lift=lift: lift[row]
        mine = lambda row, own=own, totals=totals, edge=edge: (totals if row in edge else own)[row - 1]
        bound = lambda row, binding=binding: binding[row - 1]
        relax(n + 4, field, (fx, fy, fz, weight, bound), mine, store(target, 1))
        widen(sizes, place, level - 1, target, upper, n + 2)

    held_row = held_rows(sizes, [owns[0], None, None, owns[1]], [borders0])
    fx, fy, fz, weight, v0 = levels[0].fx, levels[0].fy, levels[0].fz, levels[0].weight, levels[0].smooth
    lift0[0] = lift0[0] + over0[0]
    lift0[n0 + 1] = lift0[n0 + 1] + over0[n1 + 1]
    for row in range(1, n0 + 1):
        lift0[row] = v0[row - 1] + over0[(row + 1) // 2]
    field = lambda row: lift0[row]
    bound = lambda row: held_row(0, 1, row - 1)
    relax(n0 + 2, field, (fx, fy, fz, weight, bound), lambda row: held_row(0, 2, row - 1), store(it0, 1))
    step = sizes.depth // CHUNKS
    copies = []
    for chunk in range(CHUNKS):
        part = slice(chunk * step, (chunk + 1) * step)
        result[part] = jnp.swapaxes(it0[:, part, :width], 0, 1)
        copies.append(pltpu.make_async_copy(result.at[part], out.at[part], semaphores.at[chunk]))
        copies[-1].start()
    for copy in copies:
        copy.wait()


def call(body, name, micros, outputs, scratch, place, inputs, copies=0, far_out=False):
    near, far = pl.BlockSpec(memory_space=pltpu.VMEM), pl.BlockSpec(memory_space=pl.ANY)
    scratch = [pltpu.VMEM(shape, f32) for shape in scratch]
    if copies:
        scratch.append(pltpu.SemaphoreType.DMA((copies,)))
    return pl.pallas_call(
        body,
        name=name,
        out_shape=[jax.ShapeDtypeStruct(shape, f32) for shape in outputs],
        in_specs=[pl.BlockSpec(memory_space=pltpu.SMEM)] + [near] * len(inputs),
        out_specs=[far if far_out else near] * len(outputs),
        scratch_shapes=scratch,
        cost_estimate=pl.CostEstimate(flops=int(micros * 1.15e9), bytes_accessed=int(micros * BYTES_A_MICRO), transcendentals=0),
        compiler_params=pltpu.CompilerParams(vmem_limit_bytes=VMEM_LIMIT),
    )(place, *inputs)


def along(value, axis, steps):
    count = lax.axis_size(axis)
    initial, last = max(0, -steps), min(count, count - steps)
    return lax.ppermute(value, axis, [(source, source + steps) for source in range(initial, last)])


def beside(values, sizes):
    if sizes.sides == 1:
        return [[lax.ppermute(value, "width", [(0, 1), (1, 0)]) for value in values]]
    if sizes.sides == 2:
        return [[along(value, "width", steps) for value in values] for steps in (-1, 1)]
    return []


def edge_columns(edges, sizes):
    if sizes.sides == 1:
        return [lax.ppermute(edges[0], "width", [(0, 1), (1, 0)])]
    if sizes.sides == 2:
        return [along(edges[1], "width", -1), along(edges[0], "width", 1)]
    return []


def stages(count):
    stride = 1
    while stride < count:
        radix = 4 if count // stride % 4 == 0 else 2
        yield stride, radix
        stride *= radix


def swap(value, stride, radix, others=None):
    count = lax.axis_size("span")
    others = others or {}
    return [value] + [
        lax.ppermute(others.get(step, value), "span", [(device, device ^ step * stride) for device in range(count)])
        for step in range(1, radix)
    ]


def exchange(pair, stride):
    count = lax.axis_size("span")
    routes = [[], []]
    for low in range(count - stride):
        routes[low // stride % 2] += [(low, low + stride), (low + stride, low)]
    return [None if value is None else lax.ppermute(value, "span", route) for value, route in zip(pair, routes)]


def on_device(right_side, diffusivity, reaction):
    depth, extent_x, extent_y = diffusivity.shape
    sizes = Sizes(depth, extent_x, extent_y, lax.axis_size("span"), lax.axis_size("width"))
    place = jnp.stack([lax.axis_index("span"), lax.axis_index("width")]).astype(jnp.int32)
    n0, n1, n2, n3 = sizes.rows
    s = sizes.sides
    tile = (depth, LANES)
    own = [(depth, count * LANES) for count in sizes.own]
    held = [(depth, count) for count in sizes.held]
    down_message = (sizes.tiles, *tile)
    up_message = (sizes.up_tiles + 1, *tile)
    own0, own1, own2, first, second, *edges = call(
        functools.partial(start_kernel, sizes),
        "start",
        1.1,
        [(2, n0, *own[0]), (2 * n1, *own[1]), (2 * n2, *own[2]), down_message, down_message]
        + [(n0, depth, BORDER)] * 2 * s,
        [(2 * n1, *own[0])],
        place,
        [diffusivity, reaction],
    )
    borders = edge_columns(edges[:s], sizes) + edge_columns(edges[s:], sizes)
    halos = exchange([first, second], 1)
    turned, *edges = call(
        functools.partial(turn_kernel, sizes),
        "turn",
        0.7,
        [(n0, *own[0])] + [(n0, depth, BORDER)] * s,
        [],
        place,
        [right_side],
    )
    borders += edge_columns(edges, sizes)
    plan = list(stages(sizes.span_count))

    part = packing(5)
    far = (sizes.held[2] // LANES, *tile)
    inners = [(sum(inner_rows(sizes, level)), *held[level]) for level in range(3)]
    outers = [(sum(outer_rows(sizes, level)), *held[level]) for level in range(3)]
    inner = call(
        functools.partial(inner_kernel, sizes),
        "inner",
        0.5,
        [(2 * n1, *tile), (2 * n2, *tile), *inners],
        [(2 * n1, *held[0])],
        place,
        [own0, own1, own2, turned, *borders],
    )
    halos, inner = lax.optimization_barrier((halos, inner))
    sides = beside(halos, sizes)
    downs = call(
        functools.partial(down_kernel, sizes),
        "down",
        2.5,
        [*outers, (part, *tile), (part + far[0], *tile), up_message, up_message, far],
        [(5, *tile), (2, *held[2]), (n1 + 2, *held[0])],
        place,
        [own0, own1, own2, turned, *borders, *halos, *sum(sides, []), *inner],
    )
    outer, blocks, with_far, ups, far_second = downs[:3], downs[3], downs[4], list(downs[5:7]), downs[7]
    far_rows = None
    for stride, radix in plan[:-1]:
        count = stride * radix
        if far_rows is None:
            blocks = swap(blocks, stride, radix, {2: with_far})
            far_rows = [blocks[2], exchange([None, far_second], 2)[1]]
        else:
            blocks = swap(blocks, stride, radix)
        (blocks,) = call(
            functools.partial(merge_kernel, sizes, stride, radix),
            "merge",
            0.9,
            [(packing(3 * count + 2), *tile)],
            [(count + 2, *tile), (count, *tile), (count, *tile)],
            place,
            blocks,
        )
    stride, radix = plan[-1]
    blocks = swap(blocks, stride, radix)
    received = lax.optimization_barrier([exchange([ups[0], None], 1)[0], ups[1]])
    received = [received[0], exchange([None, received[1]], 1)[1]] + far_rows
    scratch = [(sizes.span_count + 2, *tile)] + [(sizes.span_count, *tile)] * 3
    for index in range(3):
        count = sizes.span_count >> index
        scratch += [(count + 1, *tile)] + [(count, *tile)] * 3 + [(count + 2, *tile)] + [(count, *tile)] * 2
        scratch += [(count + 2, *tile)] * 2
    blocks, received[3] = lax.optimization_barrier((blocks, received[3]))
    (coarse,) = call(
        functools.partial(coarse_kernel, sizes, stride, radix),
        "coarse",
        0.7,
        [(n3 + 2, *tile)],
        scratch,
        place,
        [*blocks, *sum(beside(blocks, sizes), [])],
    )
    scratch = [(n1 + 2, *held[1]), (n2 + 2, *held[2]), diffusivity.shape, (2, *held[0]), (2, *held[1])]
    scratch += [(n3 + 2, *held[2]), (n2 + 2, *held[1]), (n1 + 2, *held[0])]
    scratch += [(n2 + 4, *held[2]), (n1 + 4, *held[1]), (n0 + 2, *held[0])]
    scratch += [(n2 + 2, *held[2]), (n1 + 2, *held[1]), (n0, *held[0])]
    (correction,) = call(
        functools.partial(up_kernel, sizes),
        "up",
        3.0,
        [diffusivity.shape],
        scratch,
        place,
        [coarse, *received, *inner[2:], *outer, own0, turned, *borders],
        copies=CHUNKS,
        far_out=True,
    )
    return correction


def solution(mesh):
    in_specs = (P(None, "span", "width"),) * 3
    return jax.shard_map(
        on_device, mesh=mesh, in_specs=in_specs, out_specs=P(None, "span", "width"), check_vma=False
    )
```

```python
import functools

import jax
import jax.numpy as jnp
from jax import lax
from jax.experimental import pallas as pl
from jax.experimental.pallas import tpu as pltpu
from jax.sharding import PartitionSpec as P

LEVELS = 6
COARSE_SWEEPS = 3
LANES = 128
BORDER = 128
FRINGE = 4
SPREAD = 16
relax_weight = 0.8
f32 = jnp.float32
VMEM_LIMIT = 32 * 1024 * 1024
BYTES_A_MICRO = 3.69e6
CHUNKS = 4


class Sizes:
    def __init__(self, depth, extent_x, extent_y, span_count, width_count):
        self.depth, self.extent_x, self.extent_y = depth, extent_x, extent_y
        self.span_count, self.width_count = span_count, width_count
        self.sides = min(width_count - 1, 2)
        self.own = [(extent_y >> level) // LANES for level in range(3)]
        self.border = [self.sides, min(self.sides, 1), min(self.sides, 1)]
        self.held = [(self.own[level] + self.border[level]) * LANES for level in range(3)] + [LANES] * 3
        self.rows = [extent_x >> level for level in range(4)]
        self.slots = []
        start = 0
        for level in (0, 1, 1, 1, 2, 2):
            self.slots.append((start, self.own[level]))
            start += self.own[level]
        self.tiles = start
        self.up_slots = []
        start = 0
        for level in (0, 1, 1, 2, 2, 2):
            self.up_slots.append((start, self.own[level]))
            start += self.own[level]
        self.up_tiles = start


def put(message, slot, row):
    start, tiles = slot
    for tile in range(tiles):
        message[start + tile] = row[:, tile * LANES : (tile + 1) * LANES]


class Arrived:
    def __init__(self, place, pair, forward, stride=1):
        self.even = place[0] // stride % 2 == 0
        self.first, self.second = (pair[0], pair[1]) if forward else (pair[1], pair[0])

    def __getitem__(self, index):
        return jnp.where(self.even, self.first[index], self.second[index])


def put_pair(place, pair, slot, next_row, prev_row, stride=1):
    even = place[0] // stride % 2 == 0
    put(pair[0], slot, jnp.where(even, next_row, prev_row))
    put(pair[1], slot, jnp.where(even, prev_row, next_row))


def get(message, slot):
    start, tiles = slot
    return [message[start + tile] for tile in range(tiles)]


def lane_at(shape):
    return lax.broadcasted_iota(jnp.int32, shape, len(shape) - 1)


def roll(value, steps, axis):
    return pltpu.roll(value, steps % value.shape[axis], axis=axis)


def reciprocal(value):
    return pltpu.reciprocal(value, approx=True)


def harmonic(first, second, guard):
    total = first + second
    if guard:
        total = jnp.maximum(total, 1e-3)
    return (2.0 * first) * second * reciprocal(total)


def split(value):
    high = value.astype(jnp.bfloat16)
    return high, (value - high.astype(f32)).astype(jnp.bfloat16)


def dot(halves, table):
    high, low = halves
    return jnp.dot(high, table, preferred_element_type=f32) + jnp.dot(low, table, preferred_element_type=f32)


def pair_table(fine, fine_dim, turn, weight):
    shape = (fine, LANES) if fine_dim == 0 else (LANES, fine)
    fine_at = lax.broadcasted_iota(jnp.int32, shape, fine_dim)
    coarse_at = lax.broadcasted_iota(jnp.int32, shape, 1 - fine_dim)
    if turn is not None:
        coarse_at = coarse_at - jnp.where(fine_at >= turn, LANES // 2, 0)
    return jnp.where(fine_at // 2 == coarse_at, weight, 0.0).astype(jnp.bfloat16)


def turns(sizes, place, level):
    if sizes.sides == 0:
        return []
    if level == 0:
        return [jnp.where(place[1] == 0, LANES, 0)] if sizes.sides == 1 else [LANES, 0]
    return [LANES // 2]


def transfer_plan(sizes, place, level, part):
    plan = []
    if level >= 3:
        return [((0, LANES), 0, 3 * LANES // 4)]
    if level == 2:
        return [((0, sizes.held[2]), 0, None)]
    own = sizes.own[level]
    if part != "border":
        plan += [((2 * LANES * tile, 2 * LANES * (tile + 1)), tile, None) for tile in range(own // 2)]
    if part != "own":
        for index, turn in enumerate(turns(sizes, place, level)):
            start = (own + index) * LANES
            plan.append(((start, start + LANES), own // 2, turn))
    return plan


def narrow(sizes, place, level, sums, target, rows, part="all", shift=0):
    depth = sums.shape[1]
    done = {}
    for (start, stop), tile, turn in transfer_plan(sizes, place, level, part):
        start, stop, tile = start - shift, stop - shift, tile - shift // (2 * LANES)
        columns = split(sums[0:rows, :, start:stop].reshape(rows * depth, stop - start))
        result = dot(columns, pair_table(stop - start, 0, turn, 0.25)).reshape(rows, depth, LANES)
        done[tile] = done[tile] + result if tile in done else result
    for tile, result in done.items():
        target[0:rows, :, tile * LANES : (tile + 1) * LANES] = result


def widen(sizes, place, level, coarse, target, rows):
    depth = coarse.shape[1]
    for (start, stop), tile, turn in transfer_plan(sizes, place, level, "all"):
        columns = split(coarse[0:rows, :, tile * LANES : (tile + 1) * LANES].reshape(rows * depth, LANES))
        result = dot(columns, pair_table(stop - start, 1, turn, 4.0))
        target[0:rows, :, start:stop] = result.reshape(rows, depth, stop - start)


class Joined:
    def __init__(self, inner, outer, first):
        self.inner, self.outer, self.first = inner, outer, first

    def find(self, row):
        place, count = row - self.first, 0 if self.inner is None else self.inner.shape[0]
        if 0 <= place < count:
            return self.inner, place
        return self.outer, row if place < 0 else row - count

    def __getitem__(self, row):
        array, place = self.find(row)
        return array[place]

    def __setitem__(self, row, value):
        array, place = self.find(row)
        array[place] = value


class Level:
    def __init__(self, sizes, level, inner, outer):
        self.n, self.halo = sizes.rows[level], 1 if level == 0 else 2
        counts = inner_rows(sizes, level)
        fx, fy, fz, *rest = parts(inner, counts)
        weight, source, smooth = (None, None, None) if level == 2 else (rest[0], None, rest[1])
        if level == 1:
            weight, source, smooth = rest
        others = [None] * 7 if outer is None else parts(outer, outer_rows(sizes, level))
        if level == 0 and outer is not None:
            others = [others[0], None, None, others[1], None, others[2], None]
        h = self.halo
        self.fx = Joined(fx, others[0], h)
        self.fy, self.fz = Joined(fy, others[1], h - 1), Joined(fz, others[2], h - 1)
        self.weight, self.source, self.smooth = (
            Joined(array, other, h) for array, other in zip((weight, source, smooth), others[3:6])
        )
        self.binding = others[6]

    def inner(self):
        first, last = self.halo, self.halo + self.n - 1
        return range(first + 1, last + 1), range(first, last + 1), range(first + 1, last)

    def outer(self):
        count = self.n + 2 * self.halo
        every = (range(1, count), range(1, count - 1), range(1, count - 1))
        return tuple([row for row in rows if row not in mine] for rows, mine in zip(every, self.inner()))


def inner_rows(sizes, level):
    n = sizes.rows[level]
    return [n - 1, n, n] + [[n - 2] * 2, [n - 2] * 3, []][level]


def outer_rows(sizes, level):
    n = sizes.rows[level]
    return [[2, 2, 2], [4, 2, 2, 4, 4, 4, n + 2], [4, 2, 2] + [n + 2] * 4][level]


def coefficients(sizes, place, level, conduct, binding, fx, fy, fz, weight, rows):
    guard = level > 0 or sizes.sides > 1
    for row in rows[0]:
        fx[row - 1] = harmonic(conduct(row - 1), conduct(row), guard)
    for row in rows[1]:
        mine = conduct(row)
        south = harmonic(mine, roll(mine, 1, 1), guard)
        if level == 0 and sizes.sides < 2:
            cut = 0 if sizes.sides == 0 else jnp.where(place[1] == 0, 0, sizes.extent_y)
            south = jnp.where(lane_at(mine.shape) == cut, 0.0, south)
        below = harmonic(mine, roll(mine, 1, 0), guard)
        fy[row - 1] = south
        fz[row - 1] = jnp.where(lax.broadcasted_iota(jnp.int32, mine.shape, 0) == 0, 0.0, below)
    for row in rows[2]:
        south, below = fy[row - 1], fz[row - 1]
        diagonal = fx[row - 1] + fx[row] + binding(row)
        diagonal = diagonal + (south + roll(south, -1, 1)) + (below + roll(below, -1, 0))
        if guard:
            diagonal = jnp.maximum(diagonal, 1e-6)
        weight[row - 1] = relax_weight * reciprocal(diagonal)


def sweep(first, last, field, binding, fx, fy, fz, emit):
    lower = fx[first - 1] * (field(first) - field(first - 1))
    for row in range(first, last + 1):
        mine = field(row)
        upper = fx[row] * (field(row + 1) - mine)
        south = fy[row - 1] * (mine - roll(mine, 1, 1))
        below = fz[row - 1] * (mine - roll(mine, 1, 0))
        across = (south - roll(south, -1, 1)) + (below - roll(below, -1, 0))
        emit(row, binding(row) * mine + (lower - upper) + across)
        lower = upper


def in_pairs(sums, slot_of):
    def add(row, value):
        slot, first = slot_of(row)
        if first:
            sums[slot] = value
        else:
            sums[slot] = sums[slot] + value

    return add


def parts(array, counts):
    views, start = [], 0
    for count in counts:
        views.append(array.at[start : start + count])
        start += count
    return views


def start_kernel(sizes, place, conduct, binding, own0, own1, own2, first, second, *refs):
    edges, sums = refs[: 2 * sizes.sides], refs[-1]
    n0, n1, n2 = sizes.rows[:3]
    for at, array in enumerate((conduct, binding)):
        own0[at] = jnp.swapaxes(array[...], 0, 1)
    for at in (0, 1):
        for row in range(n1):
            sums[at * n1 + row] = own0[at, 2 * row] + own0[at, 2 * row + 1]
    narrow(sizes, place, 0, sums, own1, 2 * n1, "own")
    for row in range(2 * n2):
        sums[row, :, : sizes.own[1] * LANES] = own1[2 * row] + own1[2 * row + 1]
    narrow(sizes, place, 1, sums, own2, 2 * n2, "own")
    ends = []
    for low, at1, at0 in ((n1 - 2, n1 - 1, n0 - 1), (0, 0, 0)):
        near, far = (n2 - 1, n2 - 2) if at0 else (0, 1)
        rows = (own0[0, at0], own1[low], own1[low + 1], own1[n1 + at1], own2[far], own2[n2 + near])
        ends.append(rows)
    for slot, next_row, prev_row in zip(sizes.slots, *ends):
        put_pair(place, (first, second), slot, next_row, prev_row)
    for at in (0, 1):
        cut_edges(sizes, place, own0.at[at], edges[at * sizes.sides : (at + 1) * sizes.sides])


def cut_edges(sizes, place, array, edges):
    last = sizes.extent_y - BORDER
    if sizes.sides == 1:
        at = pl.multiple_of(jnp.where(place[1] == 0, last, 0), LANES)
        edges[0][...] = array[:, :, pl.ds(at, BORDER)]
    elif sizes.sides == 2:
        edges[0][...] = array[:, :, last:]
        edges[1][...] = array[:, :, :BORDER]


def turn_kernel(sizes, place, right_side, turned, *edges):
    turned[...] = jnp.swapaxes(right_side[...], 0, 1)
    cut_edges(sizes, place, turned, edges)


def message_row(sizes, place, level, slot, message, beside):
    start, tiles = slot
    row = get(message, slot)
    if sizes.sides == 1:
        left = place[1] != 0
        tile = beside[0][start + jnp.where(left, tiles - 1, 0)]
        if level > 0:
            reach = BORDER >> level
            lane = lane_at(tile.shape)
            first = jnp.where(left, LANES - reach, 0)
            tile = jnp.where((lane >= first) & (lane < first + reach), tile, 0.0)
        row.append(tile)
    elif sizes.sides == 2:
        right, left = beside[0][start], beside[1][start + tiles - 1]
        if level == 0:
            row += [right, left]
        else:
            reach = BORDER >> level
            lane = lane_at(right.shape)
            row.append(jnp.where(lane < reach, right, jnp.where(lane >= LANES - reach, left, 0.0)))
    return jnp.concatenate(row, axis=1)


def fringe_lanes(shape):
    lane = lane_at(shape)
    return (lane < FRINGE) | (lane >= LANES - FRINGE)


def fringes(sizes, rows):
    total = None
    for index, (level, row) in enumerate(rows):
        border = row[:, sizes.own[level] * LANES :]
        tile = border[:, :LANES]
        lane = lane_at(tile.shape)
        if border.shape[1] > LANES:
            tile = jnp.where(lane < FRINGE, tile, border[:, LANES:])
        tile = jnp.where((lane < FRINGE) | (lane >= LANES - FRINGE), tile, 0.0)
        tile = roll(tile, SPREAD * index + SPREAD // 2, 1)
        total = tile if total is None else total + tile
    return total


def fringed_row(sizes, level, index, message):
    row = get(message, sizes.up_slots[index])
    if sizes.border[level]:
        tile = roll(message[sizes.up_tiles], -(SPREAD * index + SPREAD // 2), 1)
        lane = lane_at(tile.shape)
        right, left = jnp.where(lane < FRINGE, tile, 0.0), jnp.where(lane >= LANES - FRINGE, tile, 0.0)
        row += [right, left] if sizes.border[level] == 2 else [right + left]
    return jnp.concatenate(row, axis=1)


def packing(count):
    return -(-count // 2)


def pack_rows(rows, target):
    half = LANES // 2
    lane = lane_at(rows[0].shape)
    for index in range(packing(len(rows))):
        held = jnp.where(lane < half, rows[2 * index], 0.0)
        if 2 * index + 1 < len(rows):
            held = jnp.where(lane < half, held, pltpu.roll(rows[2 * index + 1], half, axis=1))
        target[index] = held


def unpack_rows(sizes, place, tiles, count, others=()):
    half, reach = LANES // 2, BORDER >> 3
    lane = lane_at(tiles.shape[1:])
    rows = []
    for index in range(count):
        held = tiles[index // 2]
        row = jnp.where(lane < half, pltpu.roll(held, half, axis=1) if index % 2 else held, 0.0)
        for side, other in enumerate(others):
            first = LANES - reach if side else half
            if sizes.sides == 1:
                first = jnp.where(place[1] == 0, half, LANES - reach)
            beside = other[index // 2]
            beside = beside if index % 2 else pltpu.roll(beside, half, axis=1)
            row = jnp.where((lane >= first) & (lane < first + reach), beside, row)
        rows.append(row)
    return rows


def merge_into(sizes, place, stride, radix, arrays, source, conduct, binding, first, others=()):
    position = (place[0] // stride) % radix
    source[...] = jnp.zeros(source.shape, f32)
    for step, array in enumerate(arrays):
        at = (position ^ step) * stride
        rows = unpack_rows(sizes, place, array, 3 * stride + 2, [other[step] for other in others])
        for index, row in enumerate(rows[: stride + 2]):
            source[at + index] = source[at + index] + row
        for index in range(stride):
            conduct[at + index + first] = rows[stride + 2 + index]
            binding[at + index] = rows[2 * stride + 2 + index]


def merge_kernel(sizes, stride, radix, place, *refs):
    arrays, out, (source, conduct, binding) = refs[:radix][::-1], refs[radix], refs[radix + 1 :]
    merge_into(sizes, place, stride, radix, arrays, source, conduct, binding, 0)
    count = stride * radix
    rows = [source[row] for row in range(count + 2)]
    rows += [conduct[row] for row in range(count)] + [binding[row] for row in range(count)]
    pack_rows(rows, out)


def held_rows(sizes, owns, borders):
    def held_row(level, at, row):
        if level > 0:
            row = at * sizes.rows[level] + row
            return jnp.concatenate([owns[level][row], *(array[row] for array in borders[level])], axis=1)
        own = owns[3][row] if at == 2 else owns[0][at, row]
        sides = len(borders[0]) // 3
        return jnp.concatenate([own, *(array[row] for array in borders[0][at * sides : (at + 1) * sides])], axis=1)

    return held_row


def inner_kernel(sizes, place, *refs):
    s = sizes.sides
    owns, borders0, refs = refs[:4], refs[4 : 4 + 3 * s], refs[4 + 3 * s :]
    border1, border2, inner0, inner1, inner2, sums = refs
    n0, n1, n2 = sizes.rows[:3]
    if s:
        for row in range(2 * n1):
            for side in range(s):
                columns = slice(side * LANES, (side + 1) * LANES)
                at, low = row // n1, 2 * (row % n1)
                sums[row, :, columns] = borders0[at * s + side][low] + borders0[at * s + side][low + 1]
        narrow(sizes, place, 0, sums, border1, 2 * n1, "border", sizes.own[0] * LANES)
        for row in range(2 * n2):
            sums[row, :, :LANES] = border1[2 * row] + border1[2 * row + 1]
        narrow(sizes, place, 1, sums, border2, 2 * n2, "border", sizes.own[1] * LANES)
    held_row = held_rows(sizes, owns, [borders0, [border1][:s], [border2][:s]])
    levels = [Level(sizes, level, inner, None) for level, inner in enumerate((inner0, inner1, inner2))]
    for index, level in enumerate(levels):
        conduct = lambda row, index=index, level=level: held_row(index, 0, row - level.halo)
        bound = lambda row, index=index, level=level: held_row(index, 1, row - level.halo)
        coefficients(
            sizes, place, index, conduct, bound, level.fx, level.fy, level.fz, level.weight, level.inner()
        )
        if index == 0:
            right = lambda row: held_row(0, 2, row - 1)
            for row in range(2, n0):
                level.smooth[row - 1] = level.weight[row - 1] * right(row)
            add = in_pairs(sums, lambda row: ((row - 3) // 2, row % 2 == 1))
            field = lambda row, level=level: level.smooth[row - 1]
            emit = lambda row, value: add(row, right(row) - value)
            sweep(3, n0 - 2, field, bound, level.fx, level.fy, level.fz, emit)
        if index == 1:
            narrow(sizes, place, 0, sums, level.source.inner, n1 - 2)
            for row in range(2, n1):
                level.smooth[row] = level.weight[row] * level.source[row]


def down_kernel(sizes, place, *refs):
    s = sizes.sides
    owns, borders0, refs = refs[:4], refs[4 : 4 + 3 * s], refs[4 + 3 * s :]
    pairs_of = [refs[2 * index : 2 * index + 2] for index in range(1 + s)]
    refs = refs[2 * (1 + s) :]
    from_prev, *beside_prev = (Arrived(place, pair, 0) for pair in pairs_of)
    from_next, *beside_next = (Arrived(place, pair, 1) for pair in pairs_of)
    (border1, border2), inners, refs = refs[:2], refs[2:5], refs[5:]
    outers, contribution, with_far, ups, far, refs = refs[:3], refs[3], refs[4], refs[5:7], refs[7], refs[8:]
    level3, near, sums = refs
    slots = sizes.slots
    n0, n1, n2 = sizes.rows[:3]
    levels = [Level(sizes, index, inner, outer) for index, (inner, outer) in enumerate(zip(inners, outers))]
    held_row = held_rows(sizes, owns, [borders0, [border1][:s], [border2][:s]])

    def prev_row(level, index):
        return message_row(sizes, place, level, slots[index], from_prev, beside_prev)

    def next_row(level, index):
        return message_row(sizes, place, level, slots[index], from_next, beside_next)

    def conduct0(row):
        if row == 0:
            return prev_row(0, 0)
        if row == n0 + 1:
            return next_row(0, 0)
        return held_row(0, 0, row - 1)

    for at, row_of in enumerate((prev_row, next_row)):
        sums[at, :, : sizes.held[1]] = row_of(1, 1) + row_of(1, 2)
    narrow(sizes, place, 1, sums.at[:, :, : sizes.held[1]], near, 2)
    zero = jnp.zeros((sizes.depth, sizes.held[0]), f32)
    level = levels[0]
    bound0 = lambda row: held_row(0, 1, row - 1)
    right = lambda row: held_row(0, 2, row - 1)
    coefficients(
        sizes, place, 0, conduct0, bound0, level.fx, level.fy, level.fz, level.weight, level.outer()
    )
    for row in (1, n0):
        level.smooth[row - 1] = level.weight[row - 1] * right(row)
    first_slot = lambda row: (row + 1) // 2
    add = in_pairs(
        sums,
        lambda row: (first_slot(row) - (n1 - 2 if row > n0 // 2 else 0), row % 2 == 1 or row == 0),
    )
    field = lambda row, level=level: level.smooth[row - 1] if 0 < row < n0 + 1 else zero
    emit = lambda row, value: add(row, right(row) - value)
    add(0, level.fx[0] * field(1))
    sweep(1, 2, field, bound0, level.fx, level.fy, level.fz, emit)
    sweep(n0 - 1, n0, field, bound0, level.fx, level.fy, level.fz, emit)
    add(n0 + 1, level.fx[n0] * field(n0))
    fine_held = sizes.held[0]
    for index in (1, 2):
        level, n = levels[index], sizes.rows[index]
        held = sizes.held[index]
        narrow(
            sizes, place, index - 1, sums.at[:, :, :fine_held], level.source.outer, level.source.outer.shape[0]
        )
        binding = level.binding
        binding[0] = prev_row(index, 3 if index == 1 else 5)
        binding[n + 1] = next_row(index, 3 if index == 1 else 5)
        for row in range(n):
            binding[row + 1] = held_row(index, 1, row)

        def conduct(row, n=n, index=index):
            if 2 <= row < n + 2:
                return held_row(index, 0, row - 2)
            if index == 1:
                return prev_row(1, 1 + row) if row < 2 else next_row(1, row - n - 1)
            if row in (1, n + 2):
                return near[0 if row == 1 else 1]
            return (prev_row if row == 0 else next_row)(2, 4)

        bound = lambda row, binding=binding: binding[row - 1]
        coefficients(
            sizes, place, index, conduct, bound, level.fx, level.fy, level.fz, level.weight, level.outer()
        )
        for row in level.outer()[2] if index == 1 else range(1, n + 3):
            level.smooth[row - 1] = level.weight[row - 1] * level.source[row - 1]
        zero = jnp.zeros((sizes.depth, held), f32)
        field = lambda row, level=level, n=n, zero=zero: level.smooth[row - 1] if 0 < row < n + 3 else zero
        add = in_pairs(sums.at[:, :, :held], lambda row: (row // 2, row % 2 == 0))
        emit = lambda row, value, level=level, add=add: add(row, level.source[row - 1] - value)
        add(0, level.fx[0] * field(1))
        sweep(1, n + 2, field, bound, level.fx, level.fy, level.fz, emit)
        add(n + 3, level.fx[n + 2] * field(n + 2))
        fine_held = held
    narrow(sizes, place, 2, sums.at[:, :, : sizes.held[2]], level3, 3)
    for at in (0, 1):
        sums[at, :, : sizes.held[2]] = held_row(2, at, 0) + held_row(2, at, 1)
    narrow(sizes, place, 2, sums.at[:, :, : sizes.held[2]], level3.at[3:5], 2)
    tiles = packing(5)
    pack_rows([level3[row] for row in range(5)], contribution)
    with_far[0:tiles] = contribution[...]
    v0, s1, v1 = levels[0].smooth, levels[1].source, levels[1].smooth
    s2, v2 = levels[2].source, levels[2].smooth
    next_rows = (v0[n0 - 1], s1[n1], v1[n1 - 1], s2[n2], s2[n2 + 1], v2[n2 - 1])
    prev_rows = (v0[0], s1[1], v1[2], s2[1], s2[0], v2[2])
    for slot, next_row, prev_row in zip(sizes.up_slots, next_rows, prev_rows):
        put_pair(place, ups, slot, next_row, prev_row)
    if s:
        ends = [fringes(sizes, list(zip((0, 1, 1, 2, 2, 2), rows))) for rows in (next_rows, prev_rows)]
        put_pair(place, ups, (sizes.up_tiles, 1), *ends)
    far_tiles = sizes.held[2] // LANES
    put_pair(place, (with_far.at[tiles : tiles + far_tiles], far), (0, far_tiles), v2[n2 + 1], v2[0], 2)


def relax(count, field, refs_of, source, target):
    fx, fy, fz, weight, binding = refs_of

    def update(row, value):
        target(row, field(row) + weight[row - 1] * (source(row) - value))

    sweep(1, count - 2, field, binding, fx, fy, fz, update)


def store(array, first):
    def put_row(row, value):
        array[row - first] = value

    return put_row


def coarse_kernel(sizes, stride, radix, place, *refs):
    blocks, refs = refs[:radix], refs[radix:]
    others, refs = [refs[side * radix : (side + 1) * radix] for side in range(sizes.sides)], refs[sizes.sides * radix :]
    out, merged, sums, both, defects = refs[:5]
    coarse = [refs[5 + 9 * index : 14 + 9 * index] for index in range(3)]
    total = sizes.span_count
    merge_into(sizes, place, stride, radix, blocks, merged, coarse[0][4], coarse[0][5], 1, others)
    zero = jnp.zeros((sizes.depth, LANES), f32)
    for index in range(3):
        level = 3 + index
        fx, fy, fz, weight, conduct, binding, source, smooth, iterate = coarse[index]
        count, half = total >> index, total >> index + 1
        for array in (conduct, smooth, iterate):
            array[0] = zero
            array[count + 1] = zero
        if index < 2:
            conduct_next, binding_next = coarse[index + 1][4:6]
            for row in range(half):
                sums[row] = conduct[2 * row + 1] + conduct[2 * row + 2]
                sums[half + row] = binding[2 * row] + binding[2 * row + 1]
            narrow(sizes, place, level, sums, both, 2 * half)
            for row in range(half):
                conduct_next[row + 1], binding_next[row] = both[row], both[half + row]
        bound = lambda row, binding=binding: binding[row - 1]
        at_row = lambda row, conduct=conduct: conduct[row]
        every = (range(1, count + 2), range(1, count + 1), range(1, count + 1))
        coefficients(sizes, place, level, at_row, bound, fx, fy, fz, weight, every)
    for index in range(3):
        level = 3 + index
        fx, fy, fz, weight, conduct, binding, source, smooth, iterate = coarse[index]
        count = total >> index
        bound = lambda row, binding=binding: binding[row - 1]
        if index == 0:
            source = merged.at[1 : count + 1]
        for row in range(count):
            smooth[row + 1] = weight[row] * source[row]
        if index < 2:
            add = in_pairs(defects, lambda row: ((row - 1) // 2, row % 2 == 1))
            emit = lambda row, value, source=source, add=add: add(row, source[row - 1] - value)
            sweep(1, count, lambda row, smooth=smooth: smooth[row], bound, fx, fy, fz, emit)
            narrow(sizes, place, level, defects, coarse[index + 1][6], count // 2)

    fx, fy, fz, weight, conduct, binding, source, smooth, iterate = coarse[2]
    held, other = smooth, iterate
    for _ in range(COARSE_SWEEPS - 1):
        field = lambda row, held=held: held[row]
        mine = lambda row: source[row - 1]
        bound = lambda row: binding[row - 1]
        relax((total >> 2) + 2, field, (fx, fy, fz, weight, bound), mine, store(other, 0))
        held, other = other, held
    for index in (1, 0):
        fx, fy, fz, weight, conduct, binding, source, smooth, iterate = coarse[index]
        if index == 0:
            source = merged.at[1 : total + 1]
        count = total >> index
        widen(sizes, place, 3 + index, held.at[1 : count // 2 + 1], sums, count // 2)
        for row in range(count):
            smooth[row + 1] = smooth[row + 1] + sums[row // 2, :, :LANES]
        field = lambda row, smooth=smooth: smooth[row]
        mine = lambda row, source=source: source[row - 1]
        bound = lambda row, binding=binding: binding[row - 1]
        relax(count + 2, field, (fx, fy, fz, weight, bound), mine, store(iterate, 0))
        held = iterate

    out[...] = held[pl.ds(place[0], 3)]


def up_kernel(sizes, place, coarse, *refs):
    s = sizes.sides
    pair, far_pair, inners, outers, owns = refs[:2], refs[2:4], refs[4:7], refs[7:10], refs[10:12]
    levels = [Level(sizes, index, inner, outer) for index, (inner, outer) in enumerate(zip(inners, outers))]
    from_prev, from_next = (Arrived(place, pair, forward) for forward in (0, 1))
    tiles = packing(5)
    far_pair = (far_pair[0].at[tiles : tiles + sizes.held[2] // LANES], far_pair[1])
    fars = [Arrived(place, far_pair, forward, 2) for forward in (0, 1)]
    borders0, out, refs = refs[12 : 12 + 3 * s], refs[12 + 3 * s], refs[13 + 3 * s :]
    total1, total2, result, edges0, edges1 = refs[:5]
    over2, over1, over0, lift2, lift1, lift0, it2, it1, it0, semaphores = refs[5:]
    slots = sizes.slots
    n0, n1, n2 = sizes.rows[:3]
    width = sizes.own[0] * LANES

    before, behind = fringed_row(sizes, 0, 0, from_prev), fringed_row(sizes, 0, 0, from_next)
    lift0[0], lift0[n0 + 1] = before, behind
    edges0[0], edges0[1] = levels[0].fx[0] * before, levels[0].fx[n0] * behind
    narrow(sizes, place, 0, edges0, edges1, 2)

    widen(sizes, place, 2, coarse, over2, 3)
    for level, first, totals, over, lift, target, upper in (
        (2, 3, total2, over2, lift2, it2, over1),
        (1, 1, total1, over1, lift1, it1, over0),
    ):
        n, kept = sizes.rows[level], levels[level]
        fx, fy, fz, weight, binding = kept.fx, kept.fy, kept.fz, kept.weight, kept.binding
        own, smooth = kept.source, kept.smooth
        fringed = lambda index, message, level=level: fringed_row(sizes, level, index, message)
        if level == 1:
            smooth_at = first + 1
            edge = {2: own[1] + edges1[0], n + 1: own[n] + edges1[1]}
        else:
            smooth_at = first + 2
            edge = {2: own[1] + fringed(first + 1, from_prev)}
            edge[n + 1] = own[n] + fringed(first + 1, from_next)
        edge[1], edge[n + 2] = own[0] + fringed(first, from_prev), own[n + 1] + fringed(first, from_next)
        for row, value in edge.items():
            totals[row - 1] = value
        for row in range(n + 4):
            if row in (0, n + 3):
                value = fringed(smooth_at, from_next if row else from_prev)
                if level == 2:
                    far = fars[1 if row else 0]
                    value = value + jnp.concatenate(get(far, (0, sizes.held[2] // LANES)), axis=1)
            elif row in edge:
                value = weight[row - 1] * totals[row - 1]
            else:
                value = smooth[row - 1]
            lift[row] = value + over[row // 2]
        field = lambda row, lift=lift: lift[row]
        mine = lambda row, own=own, totals=totals, edge=edge: (totals if row in edge else own)[row - 1]
        bound = lambda row, binding=binding: binding[row - 1]
        relax(n + 4, field, (fx, fy, fz, weight, bound), mine, store(target, 1))
        widen(sizes, place, level - 1, target, upper, n + 2)

    held_row = held_rows(sizes, [owns[0], None, None, owns[1]], [borders0])
    fx, fy, fz, weight, v0 = levels[0].fx, levels[0].fy, levels[0].fz, levels[0].weight, levels[0].smooth
    lift0[0] = lift0[0] + over0[0]
    lift0[n0 + 1] = lift0[n0 + 1] + over0[n1 + 1]
    for row in range(1, n0 + 1):
        lift0[row] = v0[row - 1] + over0[(row + 1) // 2]
    field = lambda row: lift0[row]
    bound = lambda row: held_row(0, 1, row - 1)
    relax(n0 + 2, field, (fx, fy, fz, weight, bound), lambda row: held_row(0, 2, row - 1), store(it0, 1))
    step = sizes.depth // CHUNKS
    copies = []
    for chunk in range(CHUNKS):
        part = slice(chunk * step, (chunk + 1) * step)
        result[part] = jnp.swapaxes(it0[:, part, :width], 0, 1)
        copies.append(pltpu.make_async_copy(result.at[part], out.at[part], semaphores.at[chunk]))
        copies[-1].start()
    for copy in copies:
        copy.wait()


def call(body, name, micros, outputs, scratch, place, inputs, copies=0, far_out=False):
    near, far = pl.BlockSpec(memory_space=pltpu.VMEM), pl.BlockSpec(memory_space=pl.ANY)
    scratch = [pltpu.VMEM(shape, f32) for shape in scratch]
    if copies:
        scratch.append(pltpu.SemaphoreType.DMA((copies,)))
    return pl.pallas_call(
        body,
        name=name,
        out_shape=[jax.ShapeDtypeStruct(shape, f32) for shape in outputs],
        in_specs=[pl.BlockSpec(memory_space=pltpu.SMEM)] + [near] * len(inputs),
        out_specs=[far if far_out else near] * len(outputs),
        scratch_shapes=scratch,
        cost_estimate=pl.CostEstimate(flops=int(micros * 1.15e9), bytes_accessed=int(micros * BYTES_A_MICRO), transcendentals=0),
        compiler_params=pltpu.CompilerParams(vmem_limit_bytes=VMEM_LIMIT),
    )(place, *inputs)


def along(value, axis, steps):
    count = lax.axis_size(axis)
    initial, last = max(0, -steps), min(count, count - steps)
    return lax.ppermute(value, axis, [(source, source + steps) for source in range(initial, last)])


def beside(values, sizes):
    if sizes.sides == 1:
        return [[lax.ppermute(value, "width", [(0, 1), (1, 0)]) for value in values]]
    if sizes.sides == 2:
        return [[along(value, "width", steps) for value in values] for steps in (-1, 1)]
    return []


def edge_columns(edges, sizes):
    if sizes.sides == 1:
        return [lax.ppermute(edges[0], "width", [(0, 1), (1, 0)])]
    if sizes.sides == 2:
        return [along(edges[1], "width", -1), along(edges[0], "width", 1)]
    return []


def stages(count):
    stride = 1
    while stride < count:
        radix = 4 if count // stride % 4 == 0 else 2
        yield stride, radix
        stride *= radix


def swap(value, stride, radix, others=None):
    count = lax.axis_size("span")
    others = others or {}
    return [value] + [
        lax.ppermute(others.get(step, value), "span", [(device, device ^ step * stride) for device in range(count)])
        for step in range(1, radix)
    ]


def exchange(pair, stride):
    count = lax.axis_size("span")
    routes = [[], []]
    for low in range(count - stride):
        routes[low // stride % 2] += [(low, low + stride), (low + stride, low)]
    return [None if value is None else lax.ppermute(value, "span", route) for value, route in zip(pair, routes)]


def on_device(right_side, diffusivity, reaction):
    depth, extent_x, extent_y = diffusivity.shape
    sizes = Sizes(depth, extent_x, extent_y, lax.axis_size("span"), lax.axis_size("width"))
    place = jnp.stack([lax.axis_index("span"), lax.axis_index("width")]).astype(jnp.int32)
    n0, n1, n2, n3 = sizes.rows
    s = sizes.sides
    tile = (depth, LANES)
    own = [(depth, count * LANES) for count in sizes.own]
    held = [(depth, count) for count in sizes.held]
    down_message = (sizes.tiles, *tile)
    up_message = (sizes.up_tiles + 1, *tile)
    own0, own1, own2, first, second, *edges = call(
        functools.partial(start_kernel, sizes),
        "start",
        1.1,
        [(2, n0, *own[0]), (2 * n1, *own[1]), (2 * n2, *own[2]), down_message, down_message]
        + [(n0, depth, BORDER)] * 2 * s,
        [(2 * n1, *own[0])],
        place,
        [diffusivity, reaction],
    )
    borders = edge_columns(edges[:s], sizes) + edge_columns(edges[s:], sizes)
    halos = exchange([first, second], 1)
    turned, *edges = call(
        functools.partial(turn_kernel, sizes),
        "turn",
        0.7,
        [(n0, *own[0])] + [(n0, depth, BORDER)] * s,
        [],
        place,
        [right_side],
    )
    borders += edge_columns(edges, sizes)
    plan = list(stages(sizes.span_count))

    part = packing(5)
    far = (sizes.held[2] // LANES, *tile)
    inners = [(sum(inner_rows(sizes, level)), *held[level]) for level in range(3)]
    outers = [(sum(outer_rows(sizes, level)), *held[level]) for level in range(3)]
    inner = call(
        functools.partial(inner_kernel, sizes),
        "inner",
        0.5,
        [(2 * n1, *tile), (2 * n2, *tile), *inners],
        [(2 * n1, *held[0])],
        place,
        [own0, own1, own2, turned, *borders],
    )
    halos, inner = lax.optimization_barrier((halos, inner))
    sides = beside(halos, sizes)
    downs = call(
        functools.partial(down_kernel, sizes),
        "down",
        2.5,
        [*outers, (part, *tile), (part + far[0], *tile), up_message, up_message, far],
        [(5, *tile), (2, *held[2]), (n1 + 2, *held[0])],
        place,
        [own0, own1, own2, turned, *borders, *halos, *sum(sides, []), *inner],
    )
    outer, blocks, with_far, ups, far_second = downs[:3], downs[3], downs[4], list(downs[5:7]), downs[7]
    far_rows = None
    for stride, radix in plan[:-1]:
        count = stride * radix
        if far_rows is None:
            blocks = swap(blocks, stride, radix, {2: with_far})
            far_rows = [blocks[2], exchange([None, far_second], 2)[1]]
        else:
            blocks = swap(blocks, stride, radix)
        (blocks,) = call(
            functools.partial(merge_kernel, sizes, stride, radix),
            "merge",
            0.9,
            [(packing(3 * count + 2), *tile)],
            [(count + 2, *tile), (count, *tile), (count, *tile)],
            place,
            blocks[::-1],
        )
    stride, radix = plan[-1]
    blocks = swap(blocks, stride, radix)
    received = lax.optimization_barrier([exchange([ups[0], None], 1)[0], ups[1]])
    received = [received[0], exchange([None, received[1]], 1)[1]] + far_rows
    scratch = [(sizes.span_count + 2, *tile)] + [(sizes.span_count, *tile)] * 3
    for index in range(3):
        count = sizes.span_count >> index
        scratch += [(count + 1, *tile)] + [(count, *tile)] * 3 + [(count + 2, *tile)] + [(count, *tile)] * 2
        scratch += [(count + 2, *tile)] * 2
    blocks, received[3] = lax.optimization_barrier((blocks[::-1], received[3]))
    blocks = blocks[::-1]
    (coarse,) = call(
        functools.partial(coarse_kernel, sizes, stride, radix),
        "coarse",
        0.7,
        [(n3 + 2, *tile)],
        scratch,
        place,
        [*blocks, *sum(beside(blocks, sizes), [])],
    )
    scratch = [(n1 + 2, *held[1]), (n2 + 2, *held[2]), diffusivity.shape, (2, *held[0]), (2, *held[1])]
    scratch += [(n3 + 2, *held[2]), (n2 + 2, *held[1]), (n1 + 2, *held[0])]
    scratch += [(n2 + 4, *held[2]), (n1 + 4, *held[1]), (n0 + 2, *held[0])]
    scratch += [(n2 + 2, *held[2]), (n1 + 2, *held[1]), (n0, *held[0])]
    (correction,) = call(
        functools.partial(up_kernel, sizes),
        "up",
        3.0,
        [diffusivity.shape],
        scratch,
        place,
        [coarse, *received, *inner[2:], *outer, own0, turned, *borders],
        copies=CHUNKS,
        far_out=True,
    )
    return correction


def solution(mesh):
    in_specs = (P(None, "span", "width"),) * 3
    return jax.shard_map(
        on_device, mesh=mesh, in_specs=in_specs, out_specs=P(None, "span", "width"), check_vma=False
    )
```

```python
import functools

import jax
import jax.numpy as jnp
from jax import lax
from jax.experimental import pallas as pl
from jax.experimental.pallas import tpu as pltpu
from jax.sharding import PartitionSpec as P

LEVELS = 6
COARSE_SWEEPS = 3
LANES = 128
BORDER = 128
FRINGE = 4
SPREAD = 16
relax_weight = 0.8
f32 = jnp.float32
VMEM_LIMIT = 32 * 1024 * 1024
BYTES_A_MICRO = 3.69e6
CHUNKS = 4


class Sizes:
    def __init__(self, depth, extent_x, extent_y, span_count, width_count):
        self.depth, self.extent_x, self.extent_y = depth, extent_x, extent_y
        self.span_count, self.width_count = span_count, width_count
        self.sides = min(width_count - 1, 2)
        self.own = [(extent_y >> level) // LANES for level in range(3)]
        self.border = [self.sides, min(self.sides, 1), min(self.sides, 1)]
        self.held = [(self.own[level] + self.border[level]) * LANES for level in range(3)] + [LANES] * 3
        self.rows = [extent_x >> level for level in range(4)]
        self.slots = []
        start = 0
        for level in (0, 1, 1, 1, 2, 2):
            self.slots.append((start, self.own[level]))
            start += self.own[level]
        self.tiles = start
        self.up_slots = []
        start = 0
        for level in (0, 1, 1, 2, 2, 2):
            self.up_slots.append((start, self.own[level]))
            start += self.own[level]
        self.up_tiles = start


def put(message, slot, row):
    start, tiles = slot
    for tile in range(tiles):
        message[start + tile] = row[:, tile * LANES : (tile + 1) * LANES]


class Arrived:
    def __init__(self, place, pair, forward, stride=1):
        self.even = place[0] // stride % 2 == 0
        self.first, self.second = (pair[0], pair[1]) if forward else (pair[1], pair[0])

    def __getitem__(self, index):
        return jnp.where(self.even, self.first[index], self.second[index])


def put_pair(place, pair, slot, next_row, prev_row, stride=1):
    even = place[0] // stride % 2 == 0
    put(pair[0], slot, jnp.where(even, next_row, prev_row))
    put(pair[1], slot, jnp.where(even, prev_row, next_row))


def get(message, slot):
    start, tiles = slot
    return [message[start + tile] for tile in range(tiles)]


def lane_at(shape):
    return lax.broadcasted_iota(jnp.int32, shape, len(shape) - 1)


def roll(value, steps, axis):
    return pltpu.roll(value, steps % value.shape[axis], axis=axis)


def reciprocal(value):
    return pltpu.reciprocal(value, approx=True)


def harmonic(first, second, guard):
    total = first + second
    if guard:
        total = jnp.maximum(total, 1e-3)
    return (2.0 * first) * second * reciprocal(total)


def split(value):
    high = value.astype(jnp.bfloat16)
    return high, (value - high.astype(f32)).astype(jnp.bfloat16)


def dot(halves, table):
    high, low = halves
    return jnp.dot(high, table, preferred_element_type=f32) + jnp.dot(low, table, preferred_element_type=f32)


def pair_table(fine, fine_dim, turn, weight):
    shape = (fine, LANES) if fine_dim == 0 else (LANES, fine)
    fine_at = lax.broadcasted_iota(jnp.int32, shape, fine_dim)
    coarse_at = lax.broadcasted_iota(jnp.int32, shape, 1 - fine_dim)
    if turn is not None:
        coarse_at = coarse_at - jnp.where(fine_at >= turn, LANES // 2, 0)
    return jnp.where(fine_at // 2 == coarse_at, weight, 0.0).astype(jnp.bfloat16)


def turns(sizes, place, level):
    if sizes.sides == 0:
        return []
    if level == 0:
        return [jnp.where(place[1] == 0, LANES, 0)] if sizes.sides == 1 else [LANES, 0]
    return [LANES // 2]


def transfer_plan(sizes, place, level, part):
    plan = []
    if level >= 3:
        return [((0, LANES), 0, 3 * LANES // 4)]
    if level == 2:
        return [((0, sizes.held[2]), 0, None)]
    own = sizes.own[level]
    if part != "border":
        plan += [((2 * LANES * tile, 2 * LANES * (tile + 1)), tile, None) for tile in range(own // 2)]
    if part != "own":
        for index, turn in enumerate(turns(sizes, place, level)):
            start = (own + index) * LANES
            plan.append(((start, start + LANES), own // 2, turn))
    return plan


def narrow(sizes, place, level, sums, target, rows, part="all", shift=0):
    depth = sums.shape[1]
    done = {}
    for (start, stop), tile, turn in transfer_plan(sizes, place, level, part):
        start, stop, tile = start - shift, stop - shift, tile - shift // (2 * LANES)
        columns = split(sums[0:rows, :, start:stop].reshape(rows * depth, stop - start))
        result = dot(columns, pair_table(stop - start, 0, turn, 0.25)).reshape(rows, depth, LANES)
        done[tile] = done[tile] + result if tile in done else result
    for tile, result in done.items():
        target[0:rows, :, tile * LANES : (tile + 1) * LANES] = result


def widen(sizes, place, level, coarse, target, rows):
    depth = coarse.shape[1]
    for (start, stop), tile, turn in transfer_plan(sizes, place, level, "all"):
        columns = split(coarse[0:rows, :, tile * LANES : (tile + 1) * LANES].reshape(rows * depth, LANES))
        result = dot(columns, pair_table(stop - start, 1, turn, 4.0))
        target[0:rows, :, start:stop] = result.reshape(rows, depth, stop - start)


class Joined:
    def __init__(self, inner, outer, first):
        self.inner, self.outer, self.first = inner, outer, first

    def find(self, row):
        place, count = row - self.first, 0 if self.inner is None else self.inner.shape[0]
        if 0 <= place < count:
            return self.inner, place
        return self.outer, row if place < 0 else row - count

    def __getitem__(self, row):
        array, place = self.find(row)
        return array[place]

    def __setitem__(self, row, value):
        array, place = self.find(row)
        array[place] = value


class Level:
    def __init__(self, sizes, level, inner, outer):
        self.n, self.halo = sizes.rows[level], 1 if level == 0 else 2
        counts = inner_rows(sizes, level)
        fx, fy, fz, *rest = parts(inner, counts)
        weight, source, smooth = (None, None, None) if level == 2 else (rest[0], None, rest[1])
        if level == 1:
            weight, source, smooth = rest
        others = [None] * 7 if outer is None else parts(outer, outer_rows(sizes, level))
        if level == 0 and outer is not None:
            others = [others[0], None, None, others[1], None, others[2], None]
        h = self.halo
        self.fx = Joined(fx, others[0], h)
        self.fy, self.fz = Joined(fy, others[1], h - 1), Joined(fz, others[2], h - 1)
        self.weight, self.source, self.smooth = (
            Joined(array, other, h) for array, other in zip((weight, source, smooth), others[3:6])
        )
        self.binding = others[6]

    def inner(self):
        first, last = self.halo, self.halo + self.n - 1
        return range(first + 1, last + 1), range(first, last + 1), range(first + 1, last)

    def outer(self):
        count = self.n + 2 * self.halo
        every = (range(1, count), range(1, count - 1), range(1, count - 1))
        return tuple([row for row in rows if row not in mine] for rows, mine in zip(every, self.inner()))


def inner_rows(sizes, level):
    n = sizes.rows[level]
    return [n - 1, n, n] + [[n - 2] * 2, [n - 2] * 3, []][level]


def outer_rows(sizes, level):
    n = sizes.rows[level]
    return [[2, 2, 2], [4, 2, 2, 4, 4, 4, n + 2], [4, 2, 2] + [n + 2] * 4][level]


def coefficients(sizes, place, level, conduct, binding, fx, fy, fz, weight, rows):
    guard = level > 0 or sizes.sides > 1
    for row in rows[0]:
        fx[row - 1] = harmonic(conduct(row - 1), conduct(row), guard)
    for row in rows[1]:
        mine = conduct(row)
        south = harmonic(mine, roll(mine, 1, 1), guard)
        if level == 0 and sizes.sides < 2:
            cut = 0 if sizes.sides == 0 else jnp.where(place[1] == 0, 0, sizes.extent_y)
            south = jnp.where(lane_at(mine.shape) == cut, 0.0, south)
        below = harmonic(mine, roll(mine, 1, 0), guard)
        fy[row - 1] = south
        fz[row - 1] = jnp.where(lax.broadcasted_iota(jnp.int32, mine.shape, 0) == 0, 0.0, below)
    for row in rows[2]:
        south, below = fy[row - 1], fz[row - 1]
        diagonal = fx[row - 1] + fx[row] + binding(row)
        diagonal = diagonal + (south + roll(south, -1, 1)) + (below + roll(below, -1, 0))
        if guard:
            diagonal = jnp.maximum(diagonal, 1e-6)
        weight[row - 1] = relax_weight * reciprocal(diagonal)


def sweep(first, last, field, binding, fx, fy, fz, emit, width=None):
    cut = lambda value: value if width is None else value[:, :width]
    lower = cut(fx[first - 1]) * (cut(field(first)) - cut(field(first - 1)))
    for row in range(first, last + 1):
        mine = field(row)
        south = fy[row - 1] * (mine - roll(mine, 1, 1))
        across = cut(south - roll(south, -1, 1))
        mine = cut(mine)
        upper = cut(fx[row]) * (cut(field(row + 1)) - mine)
        below = cut(fz[row - 1]) * (mine - roll(mine, 1, 0))
        across = across + (below - roll(below, -1, 0))
        emit(row, binding(row) * mine + (lower - upper) + across)
        lower = upper


def in_pairs(sums, slot_of):
    def add(row, value):
        slot, first = slot_of(row)
        if first:
            sums[slot] = value
        else:
            sums[slot] = sums[slot] + value

    return add


def parts(array, counts):
    views, start = [], 0
    for count in counts:
        views.append(array.at[start : start + count])
        start += count
    return views


def start_kernel(sizes, place, conduct, binding, own0, own1, own2, first, second, *refs):
    edges, sums = refs[: 2 * sizes.sides], refs[-1]
    n0, n1, n2 = sizes.rows[:3]
    for at, array in enumerate((conduct, binding)):
        own0[at] = jnp.swapaxes(array[...], 0, 1)
    for at in (0, 1):
        for row in range(n1):
            sums[at * n1 + row] = own0[at, 2 * row] + own0[at, 2 * row + 1]
    narrow(sizes, place, 0, sums, own1, 2 * n1, "own")
    for row in range(2 * n2):
        sums[row, :, : sizes.own[1] * LANES] = own1[2 * row] + own1[2 * row + 1]
    narrow(sizes, place, 1, sums, own2, 2 * n2, "own")
    ends = []
    for low, at1, at0 in ((n1 - 2, n1 - 1, n0 - 1), (0, 0, 0)):
        near, far = (n2 - 1, n2 - 2) if at0 else (0, 1)
        rows = (own0[0, at0], own1[low], own1[low + 1], own1[n1 + at1], own2[far], own2[n2 + near])
        ends.append(rows)
    for slot, next_row, prev_row in zip(sizes.slots, *ends):
        put_pair(place, (first, second), slot, next_row, prev_row)
    for at in (0, 1):
        cut_edges(sizes, place, own0.at[at], edges[at * sizes.sides : (at + 1) * sizes.sides])


def cut_edges(sizes, place, array, edges):
    last = sizes.extent_y - BORDER
    if sizes.sides == 1:
        at = pl.multiple_of(jnp.where(place[1] == 0, last, 0), LANES)
        edges[0][...] = array[:, :, pl.ds(at, BORDER)]
    elif sizes.sides == 2:
        edges[0][...] = array[:, :, last:]
        edges[1][...] = array[:, :, :BORDER]


def turn_kernel(sizes, place, right_side, turned, *edges):
    turned[...] = jnp.swapaxes(right_side[...], 0, 1)
    cut_edges(sizes, place, turned, edges)


def message_row(sizes, place, level, slot, message, beside):
    start, tiles = slot
    row = get(message, slot)
    if sizes.sides == 1:
        left = place[1] != 0
        tile = beside[0][start + jnp.where(left, tiles - 1, 0)]
        if level > 0:
            reach = BORDER >> level
            lane = lane_at(tile.shape)
            first = jnp.where(left, LANES - reach, 0)
            tile = jnp.where((lane >= first) & (lane < first + reach), tile, 0.0)
        row.append(tile)
    elif sizes.sides == 2:
        right, left = beside[0][start], beside[1][start + tiles - 1]
        if level == 0:
            row += [right, left]
        else:
            reach = BORDER >> level
            lane = lane_at(right.shape)
            row.append(jnp.where(lane < reach, right, jnp.where(lane >= LANES - reach, left, 0.0)))
    return jnp.concatenate(row, axis=1)


def fringe_lanes(shape):
    lane = lane_at(shape)
    return (lane < FRINGE) | (lane >= LANES - FRINGE)


def fringes(sizes, rows):
    total = None
    for index, (level, row) in enumerate(rows):
        border = row[:, sizes.own[level] * LANES :]
        tile = border[:, :LANES]
        lane = lane_at(tile.shape)
        if border.shape[1] > LANES:
            tile = jnp.where(lane < FRINGE, tile, border[:, LANES:])
        tile = jnp.where((lane < FRINGE) | (lane >= LANES - FRINGE), tile, 0.0)
        tile = roll(tile, SPREAD * index + SPREAD // 2, 1)
        total = tile if total is None else total + tile
    return total


def fringed_row(sizes, level, index, message):
    row = get(message, sizes.up_slots[index])
    if sizes.border[level]:
        tile = roll(message[sizes.up_tiles], -(SPREAD * index + SPREAD // 2), 1)
        lane = lane_at(tile.shape)
        right, left = jnp.where(lane < FRINGE, tile, 0.0), jnp.where(lane >= LANES - FRINGE, tile, 0.0)
        row += [right, left] if sizes.border[level] == 2 else [right + left]
    return jnp.concatenate(row, axis=1)


def packing(count):
    return -(-count // 2)


def pack_rows(rows, target):
    half = LANES // 2
    lane = lane_at(rows[0].shape)
    for index in range(packing(len(rows))):
        held = jnp.where(lane < half, rows[2 * index], 0.0)
        if 2 * index + 1 < len(rows):
            held = jnp.where(lane < half, held, pltpu.roll(rows[2 * index + 1], half, axis=1))
        target[index] = held


def unpack_rows(sizes, place, tiles, count, others=()):
    half, reach = LANES // 2, BORDER >> 3
    lane = lane_at(tiles.shape[1:])
    rows = []
    for index in range(count):
        held = tiles[index // 2]
        row = jnp.where(lane < half, pltpu.roll(held, half, axis=1) if index % 2 else held, 0.0)
        for side, other in enumerate(others):
            first = LANES - reach if side else half
            if sizes.sides == 1:
                first = jnp.where(place[1] == 0, half, LANES - reach)
            beside = other[index // 2]
            beside = beside if index % 2 else pltpu.roll(beside, half, axis=1)
            row = jnp.where((lane >= first) & (lane < first + reach), beside, row)
        rows.append(row)
    return rows


def merge_into(sizes, place, stride, radix, arrays, source, conduct, binding, first, others=()):
    position = (place[0] // stride) % radix
    source[...] = jnp.zeros(source.shape, f32)
    for step, array in enumerate(arrays):
        at = (position ^ step) * stride
        rows = unpack_rows(sizes, place, array, 3 * stride + 2, [other[step] for other in others])
        for index, row in enumerate(rows[: stride + 2]):
            source[at + index] = source[at + index] + row
        for index in range(stride):
            conduct[at + index + first] = rows[stride + 2 + index]
            binding[at + index] = rows[2 * stride + 2 + index]


def merge_kernel(sizes, stride, radix, place, *refs):
    arrays, out, (source, conduct, binding) = refs[:radix], refs[radix], refs[radix + 1 :]
    merge_into(sizes, place, stride, radix, arrays, source, conduct, binding, 0)
    count = stride * radix
    rows = [source[row] for row in range(count + 2)]
    rows += [conduct[row] for row in range(count)] + [binding[row] for row in range(count)]
    pack_rows(rows, out)


def held_rows(sizes, owns, borders):
    def held_row(level, at, row):
        if level > 0:
            row = at * sizes.rows[level] + row
            return jnp.concatenate([owns[level][row], *(array[row] for array in borders[level])], axis=1)
        own = owns[3][row] if at == 2 else owns[0][at, row]
        sides = len(borders[0]) // 3
        return jnp.concatenate([own, *(array[row] for array in borders[0][at * sides : (at + 1) * sides])], axis=1)

    return held_row


def inner_kernel(sizes, place, *refs):
    s = sizes.sides
    owns, borders0, refs = refs[:4], refs[4 : 4 + 3 * s], refs[4 + 3 * s :]
    border1, border2, inner0, inner1, inner2, sums = refs
    n0, n1, n2 = sizes.rows[:3]
    if s:
        for row in range(2 * n1):
            for side in range(s):
                columns = slice(side * LANES, (side + 1) * LANES)
                at, low = row // n1, 2 * (row % n1)
                sums[row, :, columns] = borders0[at * s + side][low] + borders0[at * s + side][low + 1]
        narrow(sizes, place, 0, sums, border1, 2 * n1, "border", sizes.own[0] * LANES)
        for row in range(2 * n2):
            sums[row, :, :LANES] = border1[2 * row] + border1[2 * row + 1]
        narrow(sizes, place, 1, sums, border2, 2 * n2, "border", sizes.own[1] * LANES)
    held_row = held_rows(sizes, owns, [borders0, [border1][:s], [border2][:s]])
    levels = [Level(sizes, level, inner, None) for level, inner in enumerate((inner0, inner1, inner2))]
    for index, level in enumerate(levels):
        conduct = lambda row, index=index, level=level: held_row(index, 0, row - level.halo)
        bound = lambda row, index=index, level=level: held_row(index, 1, row - level.halo)
        coefficients(
            sizes, place, index, conduct, bound, level.fx, level.fy, level.fz, level.weight, level.inner()
        )
        if index == 0:
            right = lambda row: held_row(0, 2, row - 1)
            for row in range(2, n0):
                level.smooth[row - 1] = level.weight[row - 1] * right(row)
            add = in_pairs(sums, lambda row: ((row - 3) // 2, row % 2 == 1))
            field = lambda row, level=level: level.smooth[row - 1]
            emit = lambda row, value: add(row, right(row) - value)
            sweep(3, n0 - 2, field, bound, level.fx, level.fy, level.fz, emit)
        if index == 1:
            narrow(sizes, place, 0, sums, level.source.inner, n1 - 2)
            for row in range(2, n1):
                level.smooth[row] = level.weight[row] * level.source[row]


def down_kernel(sizes, place, *refs):
    s = sizes.sides
    owns, borders0, refs = refs[:4], refs[4 : 4 + 3 * s], refs[4 + 3 * s :]
    pairs_of = [refs[2 * index : 2 * index + 2] for index in range(1 + s)]
    refs = refs[2 * (1 + s) :]
    from_prev, *beside_prev = (Arrived(place, pair, 0) for pair in pairs_of)
    from_next, *beside_next = (Arrived(place, pair, 1) for pair in pairs_of)
    (border1, border2), inners, refs = refs[:2], refs[2:5], refs[5:]
    outers, contribution, with_far, ups, far, refs = refs[:3], refs[3], refs[4], refs[5:7], refs[7], refs[8:]
    level3, near, sums = refs
    slots = sizes.slots
    n0, n1, n2 = sizes.rows[:3]
    levels = [Level(sizes, index, inner, outer) for index, (inner, outer) in enumerate(zip(inners, outers))]
    held_row = held_rows(sizes, owns, [borders0, [border1][:s], [border2][:s]])

    def prev_row(level, index):
        return message_row(sizes, place, level, slots[index], from_prev, beside_prev)

    def next_row(level, index):
        return message_row(sizes, place, level, slots[index], from_next, beside_next)

    def conduct0(row):
        if row == 0:
            return prev_row(0, 0)
        if row == n0 + 1:
            return next_row(0, 0)
        return held_row(0, 0, row - 1)

    for at, row_of in enumerate((prev_row, next_row)):
        sums[at, :, : sizes.held[1]] = row_of(1, 1) + row_of(1, 2)
    narrow(sizes, place, 1, sums.at[:, :, : sizes.held[1]], near, 2)
    zero = jnp.zeros((sizes.depth, sizes.held[0]), f32)
    level = levels[0]
    bound0 = lambda row: held_row(0, 1, row - 1)
    right = lambda row: held_row(0, 2, row - 1)
    coefficients(
        sizes, place, 0, conduct0, bound0, level.fx, level.fy, level.fz, level.weight, level.outer()
    )
    for row in (1, n0):
        level.smooth[row - 1] = level.weight[row - 1] * right(row)
    first_slot = lambda row: (row + 1) // 2
    add = in_pairs(
        sums,
        lambda row: (first_slot(row) - (n1 - 2 if row > n0 // 2 else 0), row % 2 == 1 or row == 0),
    )
    field = lambda row, level=level: level.smooth[row - 1] if 0 < row < n0 + 1 else zero
    emit = lambda row, value: add(row, right(row) - value)
    add(0, level.fx[0] * field(1))
    sweep(1, 2, field, bound0, level.fx, level.fy, level.fz, emit)
    sweep(n0 - 1, n0, field, bound0, level.fx, level.fy, level.fz, emit)
    add(n0 + 1, level.fx[n0] * field(n0))
    fine_held = sizes.held[0]
    for index in (1, 2):
        level, n = levels[index], sizes.rows[index]
        held = sizes.held[index]
        narrow(
            sizes, place, index - 1, sums.at[:, :, :fine_held], level.source.outer, level.source.outer.shape[0]
        )
        binding = level.binding
        binding[0] = prev_row(index, 3 if index == 1 else 5)
        binding[n + 1] = next_row(index, 3 if index == 1 else 5)
        for row in range(n):
            binding[row + 1] = held_row(index, 1, row)

        def conduct(row, n=n, index=index):
            if 2 <= row < n + 2:
                return held_row(index, 0, row - 2)
            if index == 1:
                return prev_row(1, 1 + row) if row < 2 else next_row(1, row - n - 1)
            if row in (1, n + 2):
                return near[0 if row == 1 else 1]
            return (prev_row if row == 0 else next_row)(2, 4)

        bound = lambda row, binding=binding: binding[row - 1]
        coefficients(
            sizes, place, index, conduct, bound, level.fx, level.fy, level.fz, level.weight, level.outer()
        )
        for row in level.outer()[2] if index == 1 else range(1, n + 3):
            level.smooth[row - 1] = level.weight[row - 1] * level.source[row - 1]
        zero = jnp.zeros((sizes.depth, held), f32)
        field = lambda row, level=level, n=n, zero=zero: level.smooth[row - 1] if 0 < row < n + 3 else zero
        add = in_pairs(sums.at[:, :, :held], lambda row: (row // 2, row % 2 == 0))
        emit = lambda row, value, level=level, add=add: add(row, level.source[row - 1] - value)
        add(0, level.fx[0] * field(1))
        sweep(1, n + 2, field, bound, level.fx, level.fy, level.fz, emit)
        add(n + 3, level.fx[n + 2] * field(n + 2))
        fine_held = held
    narrow(sizes, place, 2, sums.at[:, :, : sizes.held[2]], level3, 3)
    for at in (0, 1):
        sums[at, :, : sizes.held[2]] = held_row(2, at, 0) + held_row(2, at, 1)
    narrow(sizes, place, 2, sums.at[:, :, : sizes.held[2]], level3.at[3:5], 2)
    tiles = packing(5)
    pack_rows([level3[row] for row in range(5)], contribution)
    with_far[0:tiles] = contribution[...]
    v0, s1, v1 = levels[0].smooth, levels[1].source, levels[1].smooth
    s2, v2 = levels[2].source, levels[2].smooth
    next_rows = (v0[n0 - 1], s1[n1], v1[n1 - 1], s2[n2], s2[n2 + 1], v2[n2 - 1])
    prev_rows = (v0[0], s1[1], v1[2], s2[1], s2[0], v2[2])
    for slot, next_row, prev_row in zip(sizes.up_slots, next_rows, prev_rows):
        put_pair(place, ups, slot, next_row, prev_row)
    if s:
        ends = [fringes(sizes, list(zip((0, 1, 1, 2, 2, 2), rows))) for rows in (next_rows, prev_rows)]
        put_pair(place, ups, (sizes.up_tiles, 1), *ends)
    far_tiles = sizes.held[2] // LANES
    put_pair(place, (with_far.at[tiles : tiles + far_tiles], far), (0, far_tiles), v2[n2 + 1], v2[0], 2)


def relax(count, field, refs_of, source, target):
    fx, fy, fz, weight, binding = refs_of

    def update(row, value):
        target(row, field(row) + weight[row - 1] * (source(row) - value))

    sweep(1, count - 2, field, binding, fx, fy, fz, update)


def store(array, first):
    def put_row(row, value):
        array[row - first] = value

    return put_row


def coarse_kernel(sizes, stride, radix, place, *refs):
    blocks, refs = refs[:radix], refs[radix:]
    others, refs = [refs[side * radix : (side + 1) * radix] for side in range(sizes.sides)], refs[sizes.sides * radix :]
    out, merged, sums, both, defects = refs[:5]
    coarse = [refs[5 + 9 * index : 14 + 9 * index] for index in range(3)]
    total = sizes.span_count
    merge_into(sizes, place, stride, radix, blocks, merged, coarse[0][4], coarse[0][5], 1, others)
    zero = jnp.zeros((sizes.depth, LANES), f32)
    for index in range(3):
        level = 3 + index
        fx, fy, fz, weight, conduct, binding, source, smooth, iterate = coarse[index]
        count, half = total >> index, total >> index + 1
        for array in (conduct, smooth, iterate):
            array[0] = zero
            array[count + 1] = zero
        if index < 2:
            conduct_next, binding_next = coarse[index + 1][4:6]
            for row in range(half):
                sums[row] = conduct[2 * row + 1] + conduct[2 * row + 2]
                sums[half + row] = binding[2 * row] + binding[2 * row + 1]
            narrow(sizes, place, level, sums, both, 2 * half)
            for row in range(half):
                conduct_next[row + 1], binding_next[row] = both[row], both[half + row]
        bound = lambda row, binding=binding: binding[row - 1]
        at_row = lambda row, conduct=conduct: conduct[row]
        every = (range(1, count + 2), range(1, count + 1), range(1, count + 1))
        coefficients(sizes, place, level, at_row, bound, fx, fy, fz, weight, every)
    for index in range(3):
        level = 3 + index
        fx, fy, fz, weight, conduct, binding, source, smooth, iterate = coarse[index]
        count = total >> index
        bound = lambda row, binding=binding: binding[row - 1]
        if index == 0:
            source = merged.at[1 : count + 1]
        for row in range(count):
            smooth[row + 1] = weight[row] * source[row]
        if index < 2:
            add = in_pairs(defects, lambda row: ((row - 1) // 2, row % 2 == 1))
            emit = lambda row, value, source=source, add=add: add(row, source[row - 1] - value)
            sweep(1, count, lambda row, smooth=smooth: smooth[row], bound, fx, fy, fz, emit)
            narrow(sizes, place, level, defects, coarse[index + 1][6], count // 2)

    fx, fy, fz, weight, conduct, binding, source, smooth, iterate = coarse[2]
    held, other = smooth, iterate
    for _ in range(COARSE_SWEEPS - 1):
        field = lambda row, held=held: held[row]
        mine = lambda row: source[row - 1]
        bound = lambda row: binding[row - 1]
        relax((total >> 2) + 2, field, (fx, fy, fz, weight, bound), mine, store(other, 0))
        held, other = other, held
    for index in (1, 0):
        fx, fy, fz, weight, conduct, binding, source, smooth, iterate = coarse[index]
        if index == 0:
            source = merged.at[1 : total + 1]
        count = total >> index
        widen(sizes, place, 3 + index, held.at[1 : count // 2 + 1], sums, count // 2)
        for row in range(count):
            smooth[row + 1] = smooth[row + 1] + sums[row // 2, :, :LANES]
        if index == 0:
            break
        field = lambda row, smooth=smooth: smooth[row]
        mine = lambda row, source=source: source[row - 1]
        bound = lambda row, binding=binding: binding[row - 1]
        relax(count + 2, field, (fx, fy, fz, weight, bound), mine, store(iterate, 0))
        held = iterate

    for at in range(3):
        row = jnp.clip(place[0] + at, 1, total)
        mine = smooth[row]
        lower, upper = fx[row - 1] * (mine - smooth[row - 1]), fx[row] * (smooth[row + 1] - mine)
        south = fy[row - 1] * (mine - roll(mine, 1, 1))
        below = fz[row - 1] * (mine - roll(mine, 1, 0))
        across = (south - roll(south, -1, 1)) + (below - roll(below, -1, 0))
        value = binding[row - 1] * mine + (lower - upper) + across
        value = mine + weight[row - 1] * (source[row - 1] - value)
        out[at] = jnp.where(row == place[0] + at, value, 0.0)


def up_kernel(sizes, place, coarse, *refs):
    s = sizes.sides
    pair, far_pair, inners, outers, owns = refs[:2], refs[2:4], refs[4:7], refs[7:10], refs[10:12]
    levels = [Level(sizes, index, inner, outer) for index, (inner, outer) in enumerate(zip(inners, outers))]
    from_prev, from_next = (Arrived(place, pair, forward) for forward in (0, 1))
    tiles = packing(5)
    far_pair = (far_pair[0].at[tiles : tiles + sizes.held[2] // LANES], far_pair[1])
    fars = [Arrived(place, far_pair, forward, 2) for forward in (0, 1)]
    borders0, out, refs = refs[12 : 12 + 3 * s], refs[12 + 3 * s], refs[13 + 3 * s :]
    total1, total2, result, edges0, edges1 = refs[:5]
    over2, over1, over0, lift2, lift1, lift0, it2, it1, it0, semaphores = refs[5:]
    slots = sizes.slots
    n0, n1, n2 = sizes.rows[:3]
    width = sizes.own[0] * LANES

    before, behind = fringed_row(sizes, 0, 0, from_prev), fringed_row(sizes, 0, 0, from_next)
    lift0[0], lift0[n0 + 1] = before, behind
    edges0[0], edges0[1] = levels[0].fx[0] * before, levels[0].fx[n0] * behind
    narrow(sizes, place, 0, edges0, edges1, 2)

    widen(sizes, place, 2, coarse, over2, 3)
    for level, first, totals, over, lift, target, upper in (
        (2, 3, total2, over2, lift2, it2, over1),
        (1, 1, total1, over1, lift1, it1, over0),
    ):
        n, kept = sizes.rows[level], levels[level]
        fx, fy, fz, weight, binding = kept.fx, kept.fy, kept.fz, kept.weight, kept.binding
        own, smooth = kept.source, kept.smooth
        fringed = lambda index, message, level=level: fringed_row(sizes, level, index, message)
        if level == 1:
            smooth_at = first + 1
            edge = {2: own[1] + edges1[0], n + 1: own[n] + edges1[1]}
        else:
            smooth_at = first + 2
            edge = {2: own[1] + fringed(first + 1, from_prev)}
            edge[n + 1] = own[n] + fringed(first + 1, from_next)
        edge[1], edge[n + 2] = own[0] + fringed(first, from_prev), own[n + 1] + fringed(first, from_next)
        for row, value in edge.items():
            totals[row - 1] = value
        for row in range(n + 4):
            if row in (0, n + 3):
                value = fringed(smooth_at, from_next if row else from_prev)
                if level == 2:
                    far = fars[1 if row else 0]
                    value = value + jnp.concatenate(get(far, (0, sizes.held[2] // LANES)), axis=1)
            elif row in edge:
                value = weight[row - 1] * totals[row - 1]
            else:
                value = smooth[row - 1]
            lift[row] = value + over[row // 2]
        field = lambda row, lift=lift: lift[row]
        mine = lambda row, own=own, totals=totals, edge=edge: (totals if row in edge else own)[row - 1]
        bound = lambda row, binding=binding: binding[row - 1]
        relax(n + 4, field, (fx, fy, fz, weight, bound), mine, store(target, 1))
        widen(sizes, place, level - 1, target, upper, n + 2)

    fx, fy, fz, weight, v0 = levels[0].fx, levels[0].fy, levels[0].fz, levels[0].weight, levels[0].smooth
    lift0[0] = lift0[0] + over0[0]
    lift0[n0 + 1] = lift0[n0 + 1] + over0[n1 + 1]
    for row in range(1, n0 + 1):
        lift0[row] = v0[row - 1] + over0[(row + 1) // 2]
    field = lambda row: lift0[row]

    def relax_own(row, value):
        it0[row - 1] = lift0[row, :, :width] + weight[row - 1][:, :width] * (owns[1][row - 1] - value)

    sweep(1, n0, field, lambda row: owns[0][1, row - 1], fx, fy, fz, relax_own, width)
    step = sizes.depth // CHUNKS
    copies = []
    for chunk in range(CHUNKS):
        part = slice(chunk * step, (chunk + 1) * step)
        result[part] = jnp.swapaxes(it0[:, part, :width], 0, 1)
        copies.append(pltpu.make_async_copy(result.at[part], out.at[part], semaphores.at[chunk]))
        copies[-1].start()
    for copy in copies:
        copy.wait()


def call(body, name, micros, outputs, scratch, place, inputs, copies=0, far_out=False):
    near, far = pl.BlockSpec(memory_space=pltpu.VMEM), pl.BlockSpec(memory_space=pl.ANY)
    scratch = [pltpu.VMEM(shape, f32) for shape in scratch]
    if copies:
        scratch.append(pltpu.SemaphoreType.DMA((copies,)))
    return pl.pallas_call(
        body,
        name=name,
        out_shape=[jax.ShapeDtypeStruct(shape, f32) for shape in outputs],
        in_specs=[pl.BlockSpec(memory_space=pltpu.SMEM)] + [near] * len(inputs),
        out_specs=[far if far_out else near] * len(outputs),
        scratch_shapes=scratch,
        cost_estimate=pl.CostEstimate(flops=int(micros * 1.15e9), bytes_accessed=int(micros * BYTES_A_MICRO), transcendentals=0),
        compiler_params=pltpu.CompilerParams(vmem_limit_bytes=VMEM_LIMIT),
    )(place, *inputs)


def along(value, axis, steps):
    count = lax.axis_size(axis)
    initial, last = max(0, -steps), min(count, count - steps)
    return lax.ppermute(value, axis, [(source, source + steps) for source in range(initial, last)])


def beside(values, sizes):
    if sizes.sides == 1:
        return [[lax.ppermute(value, "width", [(0, 1), (1, 0)]) for value in values]]
    if sizes.sides == 2:
        return [[along(value, "width", steps) for value in values] for steps in (-1, 1)]
    return []


def edge_columns(edges, sizes):
    if sizes.sides == 1:
        return [lax.ppermute(edges[0], "width", [(0, 1), (1, 0)])]
    if sizes.sides == 2:
        return [along(edges[1], "width", -1), along(edges[0], "width", 1)]
    return []


def stages(count):
    stride = 1
    while stride < count:
        radix = 4 if count // stride % 4 == 0 else 2
        yield stride, radix
        stride *= radix


def swap(value, stride, radix, others=None):
    count = lax.axis_size("span")
    others = others or {}
    return [value] + [
        lax.ppermute(others.get(step, value), "span", [(device, device ^ step * stride) for device in range(count)])
        for step in range(1, radix)
    ]


def exchange(pair, stride):
    count = lax.axis_size("span")
    routes = [[], []]
    for low in range(count - stride):
        routes[low // stride % 2] += [(low, low + stride), (low + stride, low)]
    return [None if value is None else lax.ppermute(value, "span", route) for value, route in zip(pair, routes)]


def on_device(right_side, diffusivity, reaction):
    depth, extent_x, extent_y = diffusivity.shape
    sizes = Sizes(depth, extent_x, extent_y, lax.axis_size("span"), lax.axis_size("width"))
    place = jnp.stack([lax.axis_index("span"), lax.axis_index("width")]).astype(jnp.int32)
    n0, n1, n2, n3 = sizes.rows
    s = sizes.sides
    tile = (depth, LANES)
    own = [(depth, count * LANES) for count in sizes.own]
    held = [(depth, count) for count in sizes.held]
    down_message = (sizes.tiles, *tile)
    up_message = (sizes.up_tiles + 1, *tile)
    own0, own1, own2, first, second, *edges = call(
        functools.partial(start_kernel, sizes),
        "start",
        1.1,
        [(2, n0, *own[0]), (2 * n1, *own[1]), (2 * n2, *own[2]), down_message, down_message]
        + [(n0, depth, BORDER)] * 2 * s,
        [(2 * n1, *own[0])],
        place,
        [diffusivity, reaction],
    )
    borders = edge_columns(edges[:s], sizes) + edge_columns(edges[s:], sizes)
    halos = exchange([first, second], 1)
    turned, *edges = call(
        functools.partial(turn_kernel, sizes),
        "turn",
        0.7,
        [(n0, *own[0])] + [(n0, depth, BORDER)] * s,
        [],
        place,
        [right_side],
    )
    borders += edge_columns(edges, sizes)
    plan = list(stages(sizes.span_count))

    part = packing(5)
    far = (sizes.held[2] // LANES, *tile)
    inners = [(sum(inner_rows(sizes, level)), *held[level]) for level in range(3)]
    outers = [(sum(outer_rows(sizes, level)), *held[level]) for level in range(3)]
    inner = call(
        functools.partial(inner_kernel, sizes),
        "inner",
        0.5,
        [(2 * n1, *tile), (2 * n2, *tile), *inners],
        [(2 * n1, *held[0])],
        place,
        [own0, own1, own2, turned, *borders],
    )
    halos, inner = lax.optimization_barrier((halos, inner))
    sides = beside(halos, sizes)
    downs = call(
        functools.partial(down_kernel, sizes),
        "down",
        2.5,
        [*outers, (part, *tile), (part + far[0], *tile), up_message, up_message, far],
        [(5, *tile), (2, *held[2]), (n1 + 2, *held[0])],
        place,
        [own0, own1, own2, turned, *borders, *halos, *sum(sides, []), *inner],
    )
    outer, blocks, with_far, ups, far_second = downs[:3], downs[3], downs[4], list(downs[5:7]), downs[7]
    far_rows = None
    for stride, radix in plan[:-1]:
        count = stride * radix
        if far_rows is None:
            blocks = swap(blocks, stride, radix, {2: with_far})
            far_rows = [blocks[2], exchange([None, far_second], 2)[1]]
        else:
            blocks = swap(blocks, stride, radix)
        (blocks,) = call(
            functools.partial(merge_kernel, sizes, stride, radix),
            "merge",
            0.9,
            [(packing(3 * count + 2), *tile)],
            [(count + 2, *tile), (count, *tile), (count, *tile)],
            place,
            blocks,
        )
    stride, radix = plan[-1]
    blocks = swap(blocks, stride, radix)
    received = lax.optimization_barrier([exchange([ups[0], None], 1)[0], ups[1]])
    received = [received[0], exchange([None, received[1]], 1)[1]] + far_rows
    scratch = [(sizes.span_count + 2, *tile)] + [(sizes.span_count, *tile)] * 3
    for index in range(3):
        count = sizes.span_count >> index
        scratch += [(count + 1, *tile)] + [(count, *tile)] * 3 + [(count + 2, *tile)] + [(count, *tile)] * 2
        scratch += [(count + 2, *tile)] * 2
    blocks, received[3] = lax.optimization_barrier((blocks, received[3]))
    (coarse,) = call(
        functools.partial(coarse_kernel, sizes, stride, radix),
        "coarse",
        0.7,
        [(n3 + 2, *tile)],
        scratch,
        place,
        [*blocks, *sum(beside(blocks, sizes), [])],
    )
    scratch = [(n1 + 2, *held[1]), (n2 + 2, *held[2]), diffusivity.shape, (2, *held[0]), (2, *held[1])]
    scratch += [(n3 + 2, *held[2]), (n2 + 2, *held[1]), (n1 + 2, *held[0])]
    scratch += [(n2 + 4, *held[2]), (n1 + 4, *held[1]), (n0 + 2, *held[0])]
    scratch += [(n2 + 2, *held[2]), (n1 + 2, *held[1]), (n0, *own[0])]
    (correction,) = call(
        functools.partial(up_kernel, sizes),
        "up",
        3.0,
        [diffusivity.shape],
        scratch,
        place,
        [coarse, *received, *inner[2:], *outer, own0, turned, *borders],
        copies=CHUNKS,
        far_out=True,
    )
    return correction


def solution(mesh):
    in_specs = (P(None, "span", "width"),) * 3
    return jax.shard_map(
        on_device, mesh=mesh, in_specs=in_specs, out_specs=P(None, "span", "width"), check_vma=False
    )
```

```python
import functools

import jax
import jax.numpy as jnp
from jax import lax
from jax.experimental import pallas as pl
from jax.experimental.pallas import tpu as pltpu
from jax.sharding import PartitionSpec as P

LEVELS = 6
COARSE_SWEEPS = 3
LANES = 128
BORDER = 128
FRINGE = 4
SPREAD = 16
relax_weight = 0.8
f32 = jnp.float32
VMEM_LIMIT = 32 * 1024 * 1024
BYTES_A_MICRO = 3.69e6
CHUNKS = 4
PIECES = 4


class Sizes:
    def __init__(self, depth, extent_x, extent_y, span_count, width_count):
        self.depth, self.extent_x, self.extent_y = depth, extent_x, extent_y
        self.span_count, self.width_count = span_count, width_count
        self.sides = min(width_count - 1, 2)
        self.own = [(extent_y >> level) // LANES for level in range(3)]
        self.border = [self.sides, min(self.sides, 1), min(self.sides, 1)]
        self.held = [(self.own[level] + self.border[level]) * LANES for level in range(3)] + [LANES] * 3
        self.rows = [extent_x >> level for level in range(4)]
        self.slots = []
        start = 0
        for level in (0, 1, 1, 1, 2, 2):
            self.slots.append((start, self.own[level]))
            start += self.own[level]
        self.tiles = start
        self.up_slots = []
        start = 0
        for level in (0, 1, 1, 2, 2, 2):
            self.up_slots.append((start, self.own[level]))
            start += self.own[level]
        self.up_tiles = start


def put(message, slot, row):
    start, tiles = slot
    for tile in range(tiles):
        message[start + tile] = row[:, tile * LANES : (tile + 1) * LANES]


class Arrived:
    def __init__(self, place, pair, forward, stride=1):
        self.even = place[0] // stride % 2 == 0
        self.first, self.second = (pair[0], pair[1]) if forward else (pair[1], pair[0])

    def __getitem__(self, index):
        return jnp.where(self.even, self.first[index], self.second[index])


def put_pair(place, pair, slot, next_row, prev_row, stride=1):
    even = place[0] // stride % 2 == 0
    put(pair[0], slot, jnp.where(even, next_row, prev_row))
    put(pair[1], slot, jnp.where(even, prev_row, next_row))


def get(message, slot):
    start, tiles = slot
    return [message[start + tile] for tile in range(tiles)]


def lane_at(shape):
    return lax.broadcasted_iota(jnp.int32, shape, len(shape) - 1)


def roll(value, steps, axis):
    return pltpu.roll(value, steps % value.shape[axis], axis=axis)


def reciprocal(value):
    return pltpu.reciprocal(value, approx=True)


def harmonic(first, second, guard):
    total = first + second
    if guard:
        total = jnp.maximum(total, 1e-3)
    return (2.0 * first) * second * reciprocal(total)


def split(value):
    high = value.astype(jnp.bfloat16)
    return high, (value - high.astype(f32)).astype(jnp.bfloat16)


def dot(halves, table):
    high, low = halves
    return jnp.dot(high, table, preferred_element_type=f32) + jnp.dot(low, table, preferred_element_type=f32)


def pair_table(fine, fine_dim, turn, weight):
    shape = (fine, LANES) if fine_dim == 0 else (LANES, fine)
    fine_at = lax.broadcasted_iota(jnp.int32, shape, fine_dim)
    coarse_at = lax.broadcasted_iota(jnp.int32, shape, 1 - fine_dim)
    if turn is not None:
        coarse_at = coarse_at - jnp.where(fine_at >= turn, LANES // 2, 0)
    return jnp.where(fine_at // 2 == coarse_at, weight, 0.0).astype(jnp.bfloat16)


def turns(sizes, place, level):
    if sizes.sides == 0:
        return []
    if level == 0:
        return [jnp.where(place[1] == 0, LANES, 0)] if sizes.sides == 1 else [LANES, 0]
    return [LANES // 2]


def transfer_plan(sizes, place, level, part):
    plan = []
    if level >= 3:
        return [((0, LANES), 0, 3 * LANES // 4)]
    if level == 2:
        return [((0, sizes.held[2]), 0, None)]
    own = sizes.own[level]
    if part != "border":
        plan += [((2 * LANES * tile, 2 * LANES * (tile + 1)), tile, None) for tile in range(own // 2)]
    if part != "own":
        for index, turn in enumerate(turns(sizes, place, level)):
            start = (own + index) * LANES
            plan.append(((start, start + LANES), own // 2, turn))
    return plan


def narrow(sizes, place, level, sums, target, rows, part="all", shift=0):
    depth = sums.shape[1]
    done = {}
    for (start, stop), tile, turn in transfer_plan(sizes, place, level, part):
        start, stop, tile = start - shift, stop - shift, tile - shift // (2 * LANES)
        columns = split(sums[0:rows, :, start:stop].reshape(rows * depth, stop - start))
        result = dot(columns, pair_table(stop - start, 0, turn, 0.25)).reshape(rows, depth, LANES)
        done[tile] = done[tile] + result if tile in done else result
    for tile, result in done.items():
        target[0:rows, :, tile * LANES : (tile + 1) * LANES] = result


def widen(sizes, place, level, coarse, target, rows):
    depth = coarse.shape[1]
    for (start, stop), tile, turn in transfer_plan(sizes, place, level, "all"):
        columns = split(coarse[0:rows, :, tile * LANES : (tile + 1) * LANES].reshape(rows * depth, LANES))
        result = dot(columns, pair_table(stop - start, 1, turn, 4.0))
        target[0:rows, :, start:stop] = result.reshape(rows, depth, stop - start)


class Joined:
    def __init__(self, inner, outer, first):
        self.inner, self.outer, self.first = inner, outer, first

    def find(self, row):
        place, count = row - self.first, 0 if self.inner is None else self.inner.shape[0]
        if 0 <= place < count:
            return self.inner, place
        return self.outer, row if place < 0 else row - count

    def __getitem__(self, row):
        array, place = self.find(row)
        return array[place]

    def __setitem__(self, row, value):
        array, place = self.find(row)
        array[place] = value


class Level:
    def __init__(self, sizes, level, inner, outer):
        self.n, self.halo = sizes.rows[level], 1 if level == 0 else 2
        counts = inner_rows(sizes, level)
        fx, fy, fz, *rest = parts(inner, counts)
        weight, source, smooth = (None, None, None) if level == 2 else (rest[0], None, rest[1])
        if level == 1:
            weight, source, smooth = rest
        others = [None] * 7 if outer is None else parts(outer, outer_rows(sizes, level))
        if level == 0 and outer is not None:
            others = [others[0], None, None, others[1], None, others[2], None]
        h = self.halo
        self.fx = Joined(fx, others[0], h)
        self.fy, self.fz = Joined(fy, others[1], h - 1), Joined(fz, others[2], h - 1)
        self.weight, self.source, self.smooth = (
            Joined(array, other, h) for array, other in zip((weight, source, smooth), others[3:6])
        )
        self.binding = others[6]

    def inner(self):
        first, last = self.halo, self.halo + self.n - 1
        return range(first + 1, last + 1), range(first, last + 1), range(first + 1, last)

    def outer(self):
        count = self.n + 2 * self.halo
        every = (range(1, count), range(1, count - 1), range(1, count - 1))
        return tuple([row for row in rows if row not in mine] for rows, mine in zip(every, self.inner()))


def inner_rows(sizes, level):
    n = sizes.rows[level]
    return [n - 1, n, n] + [[n - 2] * 2, [n - 2] * 3, []][level]


def outer_rows(sizes, level):
    n = sizes.rows[level]
    return [[2, 2, 2], [4, 2, 2, 4, 4, 4, n + 2], [4, 2, 2] + [n + 2] * 4][level]


def coefficients(sizes, place, level, conduct, binding, fx, fy, fz, weight, rows):
    guard = level > 0 or sizes.sides > 1
    for row in rows[0]:
        fx[row - 1] = harmonic(conduct(row - 1), conduct(row), guard)
    for row in rows[1]:
        mine = conduct(row)
        south = harmonic(mine, roll(mine, 1, 1), guard)
        if level == 0 and sizes.sides < 2:
            cut = 0 if sizes.sides == 0 else jnp.where(place[1] == 0, 0, sizes.extent_y)
            south = jnp.where(lane_at(mine.shape) == cut, 0.0, south)
        below = harmonic(mine, roll(mine, 1, 0), guard)
        fy[row - 1] = south
        fz[row - 1] = jnp.where(lax.broadcasted_iota(jnp.int32, mine.shape, 0) == 0, 0.0, below)
    for row in rows[2]:
        south, below = fy[row - 1], fz[row - 1]
        diagonal = fx[row - 1] + fx[row] + binding(row)
        diagonal = diagonal + (south + roll(south, -1, 1)) + (below + roll(below, -1, 0))
        if guard:
            diagonal = jnp.maximum(diagonal, 1e-6)
        weight[row - 1] = relax_weight * reciprocal(diagonal)


def sweep(first, last, field, binding, fx, fy, fz, emit, width=None):
    cut = lambda value: value if width is None else value[:, :width]
    lower = cut(fx[first - 1]) * (cut(field(first)) - cut(field(first - 1)))
    for row in range(first, last + 1):
        mine = field(row)
        south = fy[row - 1] * (mine - roll(mine, 1, 1))
        across = cut(south - roll(south, -1, 1))
        mine = cut(mine)
        upper = cut(fx[row]) * (cut(field(row + 1)) - mine)
        below = cut(fz[row - 1]) * (mine - roll(mine, 1, 0))
        across = across + (below - roll(below, -1, 0))
        emit(row, binding(row) * mine + (lower - upper) + across)
        lower = upper


def in_pairs(sums, slot_of):
    def add(row, value):
        slot, first = slot_of(row)
        if first:
            sums[slot] = value
        else:
            sums[slot] = sums[slot] + value

    return add


def parts(array, counts):
    views, start = [], 0
    for count in counts:
        views.append(array.at[start : start + count])
        start += count
    return views


def start_kernel(sizes, place, conduct, binding, own0, own1, own2, first, second, *refs):
    edges, sums = refs[: 2 * sizes.sides], refs[-1]
    n0, n1, n2 = sizes.rows[:3]
    for at, array in enumerate((conduct, binding)):
        own0[at] = jnp.swapaxes(array[...], 0, 1)
    for at in (0, 1):
        for row in range(n1):
            sums[at * n1 + row] = own0[at, 2 * row] + own0[at, 2 * row + 1]
    narrow(sizes, place, 0, sums, own1, 2 * n1, "own")
    for row in range(2 * n2):
        sums[row, :, : sizes.own[1] * LANES] = own1[2 * row] + own1[2 * row + 1]
    narrow(sizes, place, 1, sums, own2, 2 * n2, "own")
    ends = []
    for low, at1, at0 in ((n1 - 2, n1 - 1, n0 - 1), (0, 0, 0)):
        near, far = (n2 - 1, n2 - 2) if at0 else (0, 1)
        rows = (own0[0, at0], own1[low], own1[low + 1], own1[n1 + at1], own2[far], own2[n2 + near])
        ends.append(rows)
    for slot, next_row, prev_row in zip(sizes.slots, *ends):
        put_pair(place, (first, second), slot, next_row, prev_row)
    for at in (0, 1):
        cut_edges(sizes, place, own0.at[at], edges[at * sizes.sides : (at + 1) * sizes.sides])


def cut_edges(sizes, place, array, edges):
    last = sizes.extent_y - BORDER
    if sizes.sides == 1:
        at = pl.multiple_of(jnp.where(place[1] == 0, last, 0), LANES)
        edges[0][...] = array[:, :, pl.ds(at, BORDER)]
    elif sizes.sides == 2:
        edges[0][...] = array[:, :, last:]
        edges[1][...] = array[:, :, :BORDER]


def turn_kernel(sizes, place, right_side, turned, *edges):
    turned[...] = jnp.swapaxes(right_side[...], 0, 1)
    cut_edges(sizes, place, turned, edges)


def message_row(sizes, place, level, slot, message, beside):
    start, tiles = slot
    row = get(message, slot)
    if sizes.sides == 1:
        left = place[1] != 0
        tile = beside[0][start + jnp.where(left, tiles - 1, 0)]
        if level > 0:
            reach = BORDER >> level
            lane = lane_at(tile.shape)
            first = jnp.where(left, LANES - reach, 0)
            tile = jnp.where((lane >= first) & (lane < first + reach), tile, 0.0)
        row.append(tile)
    elif sizes.sides == 2:
        right, left = beside[0][start], beside[1][start + tiles - 1]
        if level == 0:
            row += [right, left]
        else:
            reach = BORDER >> level
            lane = lane_at(right.shape)
            row.append(jnp.where(lane < reach, right, jnp.where(lane >= LANES - reach, left, 0.0)))
    return jnp.concatenate(row, axis=1)


def fringe_lanes(shape):
    lane = lane_at(shape)
    return (lane < FRINGE) | (lane >= LANES - FRINGE)


def fringes(sizes, rows):
    total = None
    for index, (level, row) in enumerate(rows):
        border = row[:, sizes.own[level] * LANES :]
        tile = border[:, :LANES]
        lane = lane_at(tile.shape)
        if border.shape[1] > LANES:
            tile = jnp.where(lane < FRINGE, tile, border[:, LANES:])
        tile = jnp.where((lane < FRINGE) | (lane >= LANES - FRINGE), tile, 0.0)
        tile = roll(tile, SPREAD * index + SPREAD // 2, 1)
        total = tile if total is None else total + tile
    return total


def fringed_row(sizes, level, index, message):
    row = get(message, sizes.up_slots[index])
    if sizes.border[level]:
        tile = roll(message[sizes.up_tiles], -(SPREAD * index + SPREAD // 2), 1)
        lane = lane_at(tile.shape)
        right, left = jnp.where(lane < FRINGE, tile, 0.0), jnp.where(lane >= LANES - FRINGE, tile, 0.0)
        row += [right, left] if sizes.border[level] == 2 else [right + left]
    return jnp.concatenate(row, axis=1)


def packing(count):
    return -(-count // 2)


def pack_rows(rows, target):
    half = LANES // 2
    lane = lane_at(rows[0].shape)
    for index in range(packing(len(rows))):
        held = jnp.where(lane < half, rows[2 * index], 0.0)
        if 2 * index + 1 < len(rows):
            held = jnp.where(lane < half, held, pltpu.roll(rows[2 * index + 1], half, axis=1))
        target[index] = held


def unpack_rows(sizes, place, tiles, count, others=()):
    half, reach = LANES // 2, BORDER >> 3
    lane = lane_at(tiles.shape[1:])
    rows = []
    for index in range(count):
        held = tiles[index // 2]
        row = jnp.where(lane < half, pltpu.roll(held, half, axis=1) if index % 2 else held, 0.0)
        for side, other in enumerate(others):
            first = LANES - reach if side else half
            if sizes.sides == 1:
                first = jnp.where(place[1] == 0, half, LANES - reach)
            beside = other[index // 2]
            beside = beside if index % 2 else pltpu.roll(beside, half, axis=1)
            row = jnp.where((lane >= first) & (lane < first + reach), beside, row)
        rows.append(row)
    return rows


def merge_into(sizes, place, stride, radix, arrays, source, conduct, binding, first, others=()):
    position = (place[0] // stride) % radix
    source[...] = jnp.zeros(source.shape, f32)
    for step, array in enumerate(arrays):
        at = (position ^ step) * stride
        rows = unpack_rows(sizes, place, array, 3 * stride + 2, [other[step] for other in others])
        for index, row in enumerate(rows[: stride + 2]):
            source[at + index] = source[at + index] + row
        for index in range(stride):
            conduct[at + index + first] = rows[stride + 2 + index]
            binding[at + index] = rows[2 * stride + 2 + index]


def merge_kernel(sizes, stride, radix, place, *refs):
    arrays, out, (source, conduct, binding) = refs[:radix], refs[radix], refs[radix + 1 :]
    merge_into(sizes, place, stride, radix, arrays, source, conduct, binding, 0)
    count = stride * radix
    rows = [source[row] for row in range(count + 2)]
    rows += [conduct[row] for row in range(count)] + [binding[row] for row in range(count)]
    pack_rows(rows, out)


def held_rows(sizes, owns, borders):
    def held_row(level, at, row):
        if level > 0:
            row = at * sizes.rows[level] + row
            return jnp.concatenate([owns[level][row], *(array[row] for array in borders[level])], axis=1)
        own = owns[3][row] if at == 2 else owns[0][at, row]
        sides = len(borders[0]) // 3
        return jnp.concatenate([own, *(array[row] for array in borders[0][at * sides : (at + 1) * sides])], axis=1)

    return held_row


def inner_kernel(sizes, place, *refs):
    s = sizes.sides
    owns, borders0, refs = refs[:4], refs[4 : 4 + 3 * s], refs[4 + 3 * s :]
    border1, border2, inner0, inner1, inner2, sums = refs
    n0, n1, n2 = sizes.rows[:3]
    if s:
        for row in range(2 * n1):
            for side in range(s):
                columns = slice(side * LANES, (side + 1) * LANES)
                at, low = row // n1, 2 * (row % n1)
                sums[row, :, columns] = borders0[at * s + side][low] + borders0[at * s + side][low + 1]
        narrow(sizes, place, 0, sums, border1, 2 * n1, "border", sizes.own[0] * LANES)
        for row in range(2 * n2):
            sums[row, :, :LANES] = border1[2 * row] + border1[2 * row + 1]
        narrow(sizes, place, 1, sums, border2, 2 * n2, "border", sizes.own[1] * LANES)
    held_row = held_rows(sizes, owns, [borders0, [border1][:s], [border2][:s]])
    levels = [Level(sizes, level, inner, None) for level, inner in enumerate((inner0, inner1, inner2))]
    for index, level in enumerate(levels):
        conduct = lambda row, index=index, level=level: held_row(index, 0, row - level.halo)
        bound = lambda row, index=index, level=level: held_row(index, 1, row - level.halo)
        coefficients(
            sizes, place, index, conduct, bound, level.fx, level.fy, level.fz, level.weight, level.inner()
        )
        if index == 0:
            right = lambda row: held_row(0, 2, row - 1)
            for row in range(2, n0):
                level.smooth[row - 1] = level.weight[row - 1] * right(row)
            add = in_pairs(sums, lambda row: ((row - 3) // 2, row % 2 == 1))
            field = lambda row, level=level: level.smooth[row - 1]
            emit = lambda row, value: add(row, right(row) - value)
            sweep(3, n0 - 2, field, bound, level.fx, level.fy, level.fz, emit)
        if index == 1:
            narrow(sizes, place, 0, sums, level.source.inner, n1 - 2)
            for row in range(2, n1):
                level.smooth[row] = level.weight[row] * level.source[row]


def down_kernel(sizes, place, *refs):
    s = sizes.sides
    owns, borders0, refs = refs[:4], refs[4 : 4 + 3 * s], refs[4 + 3 * s :]
    pairs_of = [refs[2 * index : 2 * index + 2] for index in range(1 + s)]
    refs = refs[2 * (1 + s) :]
    from_prev, *beside_prev = (Arrived(place, pair, 0) for pair in pairs_of)
    from_next, *beside_next = (Arrived(place, pair, 1) for pair in pairs_of)
    (border1, border2), inners, refs = refs[:2], refs[2:5], refs[5:]
    outers, contribution, with_far, ups, far, refs = refs[:3], refs[3], refs[4], refs[5:7], refs[7], refs[8:]
    level3, near, sums = refs
    slots = sizes.slots
    n0, n1, n2 = sizes.rows[:3]
    levels = [Level(sizes, index, inner, outer) for index, (inner, outer) in enumerate(zip(inners, outers))]
    held_row = held_rows(sizes, owns, [borders0, [border1][:s], [border2][:s]])

    def prev_row(level, index):
        return message_row(sizes, place, level, slots[index], from_prev, beside_prev)

    def next_row(level, index):
        return message_row(sizes, place, level, slots[index], from_next, beside_next)

    def conduct0(row):
        if row == 0:
            return prev_row(0, 0)
        if row == n0 + 1:
            return next_row(0, 0)
        return held_row(0, 0, row - 1)

    for at, row_of in enumerate((prev_row, next_row)):
        sums[at, :, : sizes.held[1]] = row_of(1, 1) + row_of(1, 2)
    narrow(sizes, place, 1, sums.at[:, :, : sizes.held[1]], near, 2)
    zero = jnp.zeros((sizes.depth, sizes.held[0]), f32)
    level = levels[0]
    bound0 = lambda row: held_row(0, 1, row - 1)
    right = lambda row: held_row(0, 2, row - 1)
    coefficients(
        sizes, place, 0, conduct0, bound0, level.fx, level.fy, level.fz, level.weight, level.outer()
    )
    for row in (1, n0):
        level.smooth[row - 1] = level.weight[row - 1] * right(row)
    first_slot = lambda row: (row + 1) // 2
    add = in_pairs(
        sums,
        lambda row: (first_slot(row) - (n1 - 2 if row > n0 // 2 else 0), row % 2 == 1 or row == 0),
    )
    field = lambda row, level=level: level.smooth[row - 1] if 0 < row < n0 + 1 else zero
    emit = lambda row, value: add(row, right(row) - value)
    add(0, level.fx[0] * field(1))
    sweep(1, 2, field, bound0, level.fx, level.fy, level.fz, emit)
    sweep(n0 - 1, n0, field, bound0, level.fx, level.fy, level.fz, emit)
    add(n0 + 1, level.fx[n0] * field(n0))
    fine_held = sizes.held[0]
    for index in (1, 2):
        level, n = levels[index], sizes.rows[index]
        held = sizes.held[index]
        narrow(
            sizes, place, index - 1, sums.at[:, :, :fine_held], level.source.outer, level.source.outer.shape[0]
        )
        binding = level.binding
        binding[0] = prev_row(index, 3 if index == 1 else 5)
        binding[n + 1] = next_row(index, 3 if index == 1 else 5)
        for row in range(n):
            binding[row + 1] = held_row(index, 1, row)

        def conduct(row, n=n, index=index):
            if 2 <= row < n + 2:
                return held_row(index, 0, row - 2)
            if index == 1:
                return prev_row(1, 1 + row) if row < 2 else next_row(1, row - n - 1)
            if row in (1, n + 2):
                return near[0 if row == 1 else 1]
            return (prev_row if row == 0 else next_row)(2, 4)

        bound = lambda row, binding=binding: binding[row - 1]
        coefficients(
            sizes, place, index, conduct, bound, level.fx, level.fy, level.fz, level.weight, level.outer()
        )
        for row in level.outer()[2] if index == 1 else range(1, n + 3):
            level.smooth[row - 1] = level.weight[row - 1] * level.source[row - 1]
        zero = jnp.zeros((sizes.depth, held), f32)
        field = lambda row, level=level, n=n, zero=zero: level.smooth[row - 1] if 0 < row < n + 3 else zero
        add = in_pairs(sums.at[:, :, :held], lambda row: (row // 2, row % 2 == 0))
        emit = lambda row, value, level=level, add=add: add(row, level.source[row - 1] - value)
        add(0, level.fx[0] * field(1))
        sweep(1, n + 2, field, bound, level.fx, level.fy, level.fz, emit)
        add(n + 3, level.fx[n + 2] * field(n + 2))
        fine_held = held
    narrow(sizes, place, 2, sums.at[:, :, : sizes.held[2]], level3, 3)
    for at in (0, 1):
        sums[at, :, : sizes.held[2]] = held_row(2, at, 0) + held_row(2, at, 1)
    narrow(sizes, place, 2, sums.at[:, :, : sizes.held[2]], level3.at[3:5], 2)
    tiles = packing(5)
    pack_rows([level3[row] for row in range(5)], contribution)
    with_far[0:tiles] = contribution[...]
    v0, s1, v1 = levels[0].smooth, levels[1].source, levels[1].smooth
    s2, v2 = levels[2].source, levels[2].smooth
    next_rows = (v0[n0 - 1], s1[n1], v1[n1 - 1], s2[n2], s2[n2 + 1], v2[n2 - 1])
    prev_rows = (v0[0], s1[1], v1[2], s2[1], s2[0], v2[2])
    for slot, next_row, prev_row in zip(sizes.up_slots, next_rows, prev_rows):
        put_pair(place, ups, slot, next_row, prev_row)
    if s:
        ends = [fringes(sizes, list(zip((0, 1, 1, 2, 2, 2), rows))) for rows in (next_rows, prev_rows)]
        put_pair(place, ups, (sizes.up_tiles, 1), *ends)
    far_tiles = sizes.held[2] // LANES
    put_pair(place, (with_far.at[tiles : tiles + far_tiles], far), (0, far_tiles), v2[n2 + 1], v2[0], 2)


def relax(count, field, refs_of, source, target):
    fx, fy, fz, weight, binding = refs_of

    def update(row, value):
        target(row, field(row) + weight[row - 1] * (source(row) - value))

    sweep(1, count - 2, field, binding, fx, fy, fz, update)


def store(array, first):
    def put_row(row, value):
        array[row - first] = value

    return put_row


def coarse_kernel(sizes, stride, radix, place, *refs):
    blocks, refs = refs[:radix], refs[radix:]
    others, refs = [refs[side * radix : (side + 1) * radix] for side in range(sizes.sides)], refs[sizes.sides * radix :]
    out, merged, sums, both, defects = refs[:5]
    coarse = [refs[5 + 9 * index : 14 + 9 * index] for index in range(3)]
    total = sizes.span_count
    merge_into(sizes, place, stride, radix, blocks, merged, coarse[0][4], coarse[0][5], 1, others)
    zero = jnp.zeros((sizes.depth, LANES), f32)
    for index in range(3):
        level = 3 + index
        fx, fy, fz, weight, conduct, binding, source, smooth, iterate = coarse[index]
        count, half = total >> index, total >> index + 1
        for array in (conduct, smooth, iterate):
            array[0] = zero
            array[count + 1] = zero
        if index < 2:
            conduct_next, binding_next = coarse[index + 1][4:6]
            for row in range(half):
                sums[row] = conduct[2 * row + 1] + conduct[2 * row + 2]
                sums[half + row] = binding[2 * row] + binding[2 * row + 1]
            narrow(sizes, place, level, sums, both, 2 * half)
            for row in range(half):
                conduct_next[row + 1], binding_next[row] = both[row], both[half + row]
        bound = lambda row, binding=binding: binding[row - 1]
        at_row = lambda row, conduct=conduct: conduct[row]
        every = (range(1, count + 2), range(1, count + 1), range(1, count + 1))
        coefficients(sizes, place, level, at_row, bound, fx, fy, fz, weight, every)
    for index in range(3):
        level = 3 + index
        fx, fy, fz, weight, conduct, binding, source, smooth, iterate = coarse[index]
        count = total >> index
        bound = lambda row, binding=binding: binding[row - 1]
        if index == 0:
            source = merged.at[1 : count + 1]
        for row in range(count):
            smooth[row + 1] = weight[row] * source[row]
        if index < 2:
            add = in_pairs(defects, lambda row: ((row - 1) // 2, row % 2 == 1))
            emit = lambda row, value, source=source, add=add: add(row, source[row - 1] - value)
            sweep(1, count, lambda row, smooth=smooth: smooth[row], bound, fx, fy, fz, emit)
            narrow(sizes, place, level, defects, coarse[index + 1][6], count // 2)

    fx, fy, fz, weight, conduct, binding, source, smooth, iterate = coarse[2]
    held, other = smooth, iterate
    for _ in range(COARSE_SWEEPS - 1):
        field = lambda row, held=held: held[row]
        mine = lambda row: source[row - 1]
        bound = lambda row: binding[row - 1]
        relax((total >> 2) + 2, field, (fx, fy, fz, weight, bound), mine, store(other, 0))
        held, other = other, held
    for index in (1, 0):
        fx, fy, fz, weight, conduct, binding, source, smooth, iterate = coarse[index]
        if index == 0:
            source = merged.at[1 : total + 1]
        count = total >> index
        widen(sizes, place, 3 + index, held.at[1 : count // 2 + 1], sums, count // 2)
        for row in range(count):
            smooth[row + 1] = smooth[row + 1] + sums[row // 2, :, :LANES]
        if index == 0:
            break
        field = lambda row, smooth=smooth: smooth[row]
        mine = lambda row, source=source: source[row - 1]
        bound = lambda row, binding=binding: binding[row - 1]
        relax(count + 2, field, (fx, fy, fz, weight, bound), mine, store(iterate, 0))
        held = iterate

    for at in range(3):
        row = jnp.clip(place[0] + at, 1, total)
        mine = smooth[row]
        lower, upper = fx[row - 1] * (mine - smooth[row - 1]), fx[row] * (smooth[row + 1] - mine)
        south = fy[row - 1] * (mine - roll(mine, 1, 1))
        below = fz[row - 1] * (mine - roll(mine, 1, 0))
        across = (south - roll(south, -1, 1)) + (below - roll(below, -1, 0))
        value = binding[row - 1] * mine + (lower - upper) + across
        value = mine + weight[row - 1] * (source[row - 1] - value)
        out[at] = jnp.where(row == place[0] + at, value, 0.0)


def up_kernel(sizes, place, coarse, *refs):
    s = sizes.sides
    pair, far_pair, inners, outers, owns = refs[:2], refs[2:4], refs[4:7], refs[7:10], refs[10:12]
    levels = [Level(sizes, index, inner, outer) for index, (inner, outer) in enumerate(zip(inners, outers))]
    from_prev, from_next = (Arrived(place, pair, forward) for forward in (0, 1))
    tiles = packing(5)
    far_pair = (far_pair[0].at[tiles : tiles + sizes.held[2] // LANES], far_pair[1])
    fars = [Arrived(place, far_pair, forward, 2) for forward in (0, 1)]
    borders0, out, refs = refs[12 : 12 + 3 * s], refs[12 + 3 * s], refs[13 + 3 * s :]
    total1, total2, result, edges0, edges1 = refs[:5]
    over2, over1, over0, lift2, lift1, lift0, it2, it1, it0, semaphores = refs[5:]
    slots = sizes.slots
    n0, n1, n2 = sizes.rows[:3]
    width = sizes.own[0] * LANES

    before, behind = fringed_row(sizes, 0, 0, from_prev), fringed_row(sizes, 0, 0, from_next)
    lift0[0], lift0[n0 + 1] = before, behind
    edges0[0], edges0[1] = levels[0].fx[0] * before, levels[0].fx[n0] * behind
    narrow(sizes, place, 0, edges0, edges1, 2)

    widen(sizes, place, 2, coarse, over2, 3)
    for level, first, totals, over, lift, target, upper in (
        (2, 3, total2, over2, lift2, it2, over1),
        (1, 1, total1, over1, lift1, it1, over0),
    ):
        n, kept = sizes.rows[level], levels[level]
        fx, fy, fz, weight, binding = kept.fx, kept.fy, kept.fz, kept.weight, kept.binding
        own, smooth = kept.source, kept.smooth
        fringed = lambda index, message, level=level: fringed_row(sizes, level, index, message)
        if level == 1:
            smooth_at = first + 1
            edge = {2: own[1] + edges1[0], n + 1: own[n] + edges1[1]}
        else:
            smooth_at = first + 2
            edge = {2: own[1] + fringed(first + 1, from_prev)}
            edge[n + 1] = own[n] + fringed(first + 1, from_next)
        edge[1], edge[n + 2] = own[0] + fringed(first, from_prev), own[n + 1] + fringed(first, from_next)
        for row, value in edge.items():
            totals[row - 1] = value
        for row in range(n + 4):
            if row in (0, n + 3):
                value = fringed(smooth_at, from_next if row else from_prev)
                if level == 2:
                    far = fars[1 if row else 0]
                    value = value + jnp.concatenate(get(far, (0, sizes.held[2] // LANES)), axis=1)
            elif row in edge:
                value = weight[row - 1] * totals[row - 1]
            else:
                value = smooth[row - 1]
            lift[row] = value + over[row // 2]
        field = lambda row, lift=lift: lift[row]
        mine = lambda row, own=own, totals=totals, edge=edge: (totals if row in edge else own)[row - 1]
        bound = lambda row, binding=binding: binding[row - 1]
        relax(n + 4, field, (fx, fy, fz, weight, bound), mine, store(target, 1))
        widen(sizes, place, level - 1, target, upper, n + 2)

    fx, fy, fz, weight, v0 = levels[0].fx, levels[0].fy, levels[0].fz, levels[0].weight, levels[0].smooth
    lift0[0] = lift0[0] + over0[0]
    lift0[n0 + 1] = lift0[n0 + 1] + over0[n1 + 1]
    for row in range(1, n0 + 1):
        lift0[row] = v0[row - 1] + over0[(row + 1) // 2]
    field = lambda row: lift0[row]

    def relax_own(row, value):
        it0[row - 1] = lift0[row, :, :width] + weight[row - 1][:, :width] * (owns[1][row - 1] - value)

    sweep(1, n0, field, lambda row: owns[0][1, row - 1], fx, fy, fz, relax_own, width)
    step = sizes.depth // CHUNKS
    copies = []
    for chunk in range(CHUNKS):
        part = slice(chunk * step, (chunk + 1) * step)
        result[part] = jnp.swapaxes(it0[:, part], 0, 1)
        for piece in range(PIECES):
            start = chunk * step + piece * (step // PIECES)
            part = slice(start, start + step // PIECES)
            copies.append(pltpu.make_async_copy(result.at[part], out.at[part], semaphores.at[len(copies)]))
            copies[-1].start()
    for copy in copies:
        copy.wait()


def call(body, name, micros, outputs, scratch, place, inputs, copies=0, far_out=False):
    near, far = pl.BlockSpec(memory_space=pltpu.VMEM), pl.BlockSpec(memory_space=pl.ANY)
    scratch = [pltpu.VMEM(shape, f32) for shape in scratch]
    if copies:
        scratch.append(pltpu.SemaphoreType.DMA((copies,)))
    return pl.pallas_call(
        body,
        name=name,
        out_shape=[jax.ShapeDtypeStruct(shape, f32) for shape in outputs],
        in_specs=[pl.BlockSpec(memory_space=pltpu.SMEM)] + [near] * len(inputs),
        out_specs=[far if far_out else near] * len(outputs),
        scratch_shapes=scratch,
        cost_estimate=pl.CostEstimate(flops=int(micros * 1.15e9), bytes_accessed=int(micros * BYTES_A_MICRO), transcendentals=0),
        compiler_params=pltpu.CompilerParams(vmem_limit_bytes=VMEM_LIMIT),
    )(place, *inputs)


def along(value, axis, steps):
    count = lax.axis_size(axis)
    initial, last = max(0, -steps), min(count, count - steps)
    return lax.ppermute(value, axis, [(source, source + steps) for source in range(initial, last)])


def beside(values, sizes):
    if sizes.sides == 1:
        return [[lax.ppermute(value, "width", [(0, 1), (1, 0)]) for value in values]]
    if sizes.sides == 2:
        return [[along(value, "width", steps) for value in values] for steps in (-1, 1)]
    return []


def edge_columns(edges, sizes):
    if sizes.sides == 1:
        return [lax.ppermute(edges[0], "width", [(0, 1), (1, 0)])]
    if sizes.sides == 2:
        return [along(edges[1], "width", -1), along(edges[0], "width", 1)]
    return []


def stages(count):
    stride = 1
    while stride < count:
        radix = 4 if count // stride % 4 == 0 else 2
        yield stride, radix
        stride *= radix


def swap(value, stride, radix, others=None):
    count = lax.axis_size("span")
    others = others or {}
    return [value] + [
        lax.ppermute(others.get(step, value), "span", [(device, device ^ step * stride) for device in range(count)])
        for step in range(1, radix)
    ]


def exchange(pair, stride):
    count = lax.axis_size("span")
    routes = [[], []]
    for low in range(count - stride):
        routes[low // stride % 2] += [(low, low + stride), (low + stride, low)]
    return [None if value is None else lax.ppermute(value, "span", route) for value, route in zip(pair, routes)]


def on_device(right_side, diffusivity, reaction):
    depth, extent_x, extent_y = diffusivity.shape
    sizes = Sizes(depth, extent_x, extent_y, lax.axis_size("span"), lax.axis_size("width"))
    place = jnp.stack([lax.axis_index("span"), lax.axis_index("width")]).astype(jnp.int32)
    n0, n1, n2, n3 = sizes.rows
    s = sizes.sides
    tile = (depth, LANES)
    own = [(depth, count * LANES) for count in sizes.own]
    held = [(depth, count) for count in sizes.held]
    down_message = (sizes.tiles, *tile)
    up_message = (sizes.up_tiles + 1, *tile)
    own0, own1, own2, first, second, *edges = call(
        functools.partial(start_kernel, sizes),
        "start",
        1.1,
        [(2, n0, *own[0]), (2 * n1, *own[1]), (2 * n2, *own[2]), down_message, down_message]
        + [(n0, depth, BORDER)] * 2 * s,
        [(2 * n1, *own[0])],
        place,
        [diffusivity, reaction],
    )
    borders = edge_columns(edges[:s], sizes) + edge_columns(edges[s:], sizes)
    halos = exchange([first, second], 1)
    turned, *edges = call(
        functools.partial(turn_kernel, sizes),
        "turn",
        0.7,
        [(n0, *own[0])] + [(n0, depth, BORDER)] * s,
        [],
        place,
        [right_side],
    )
    borders += edge_columns(edges, sizes)
    plan = list(stages(sizes.span_count))

    part = packing(5)
    far = (sizes.held[2] // LANES, *tile)
    inners = [(sum(inner_rows(sizes, level)), *held[level]) for level in range(3)]
    outers = [(sum(outer_rows(sizes, level)), *held[level]) for level in range(3)]
    inner = call(
        functools.partial(inner_kernel, sizes),
        "inner",
        0.5,
        [(2 * n1, *tile), (2 * n2, *tile), *inners],
        [(2 * n1, *held[0])],
        place,
        [own0, own1, own2, turned, *borders],
    )
    halos, inner = lax.optimization_barrier((halos, inner))
    sides = beside(halos, sizes)
    downs = call(
        functools.partial(down_kernel, sizes),
        "down",
        2.5,
        [*outers, (part, *tile), (part + far[0], *tile), up_message, up_message, far],
        [(5, *tile), (2, *held[2]), (n1 + 2, *held[0])],
        place,
        [own0, own1, own2, turned, *borders, *halos, *sum(sides, []), *inner],
    )
    outer, blocks, with_far, ups, far_second = downs[:3], downs[3], downs[4], list(downs[5:7]), downs[7]
    far_rows = None
    for stride, radix in plan[:-1]:
        count = stride * radix
        if far_rows is None:
            blocks = swap(blocks, stride, radix, {2: with_far})
            far_rows = [blocks[2], exchange([None, far_second], 2)[1]]
        else:
            blocks = swap(blocks, stride, radix)
        (blocks,) = call(
            functools.partial(merge_kernel, sizes, stride, radix),
            "merge",
            0.9,
            [(packing(3 * count + 2), *tile)],
            [(count + 2, *tile), (count, *tile), (count, *tile)],
            place,
            blocks,
        )
    stride, radix = plan[-1]
    blocks = swap(blocks, stride, radix)
    received = lax.optimization_barrier([exchange([ups[0], None], 1)[0], ups[1]])
    received = [received[0], exchange([None, received[1]], 1)[1]] + far_rows
    scratch = [(sizes.span_count + 2, *tile)] + [(sizes.span_count, *tile)] * 3
    for index in range(3):
        count = sizes.span_count >> index
        scratch += [(count + 1, *tile)] + [(count, *tile)] * 3 + [(count + 2, *tile)] + [(count, *tile)] * 2
        scratch += [(count + 2, *tile)] * 2
    blocks, received[3] = lax.optimization_barrier((blocks, received[3]))
    (coarse,) = call(
        functools.partial(coarse_kernel, sizes, stride, radix),
        "coarse",
        0.7,
        [(n3 + 2, *tile)],
        scratch,
        place,
        [*blocks, *sum(beside(blocks, sizes), [])],
    )
    scratch = [(n1 + 2, *held[1]), (n2 + 2, *held[2]), diffusivity.shape, (2, *held[0]), (2, *held[1])]
    scratch += [(n3 + 2, *held[2]), (n2 + 2, *held[1]), (n1 + 2, *held[0])]
    scratch += [(n2 + 4, *held[2]), (n1 + 4, *held[1]), (n0 + 2, *held[0])]
    scratch += [(n2 + 2, *held[2]), (n1 + 2, *held[1]), (n0, *own[0])]
    (correction,) = call(
        functools.partial(up_kernel, sizes),
        "up",
        3.0,
        [diffusivity.shape],
        scratch,
        place,
        [coarse, *received, *inner[2:], *outer, own0, turned, *borders],
        copies=CHUNKS * PIECES,
        far_out=True,
    )
    return correction


def solution(mesh):
    in_specs = (P(None, "span", "width"),) * 3
    return jax.shard_map(
        on_device, mesh=mesh, in_specs=in_specs, out_specs=P(None, "span", "width"), check_vma=False
    )
```

```python
import functools

import jax
import jax.numpy as jnp
from jax import lax
from jax.experimental import pallas as pl
from jax.experimental.pallas import tpu as pltpu
from jax.sharding import PartitionSpec as P

LEVELS = 6
COARSE_SWEEPS = 3
LANES = 128
BORDER = 128
FRINGE = 4
SPREAD = 16
relax_weight = 0.8
f32 = jnp.float32
VMEM_LIMIT = 32 * 1024 * 1024
BYTES_A_MICRO = 3.69e6
CHUNKS = 4


class Sizes:
    def __init__(self, depth, extent_x, extent_y, span_count, width_count):
        self.depth, self.extent_x, self.extent_y = depth, extent_x, extent_y
        self.span_count, self.width_count = span_count, width_count
        self.sides = min(width_count - 1, 2)
        self.own = [(extent_y >> level) // LANES for level in range(3)]
        self.border = [self.sides, min(self.sides, 1), min(self.sides, 1)]
        self.held = [(self.own[level] + self.border[level]) * LANES for level in range(3)] + [LANES] * 3
        self.rows = [extent_x >> level for level in range(4)]
        self.slots = []
        start = 0
        for level in (0, 1, 1, 1, 2, 2):
            self.slots.append((start, self.own[level]))
            start += self.own[level]
        self.tiles = start
        self.up_slots = []
        start = 0
        for level in (0, 1, 1, 2, 2, 2):
            self.up_slots.append((start, self.own[level]))
            start += self.own[level]
        self.up_tiles = start


def put(message, slot, row):
    start, tiles = slot
    for tile in range(tiles):
        message[start + tile] = row[:, tile * LANES : (tile + 1) * LANES]


class Arrived:
    def __init__(self, place, pair, forward, stride=1):
        self.even = place[0] // stride % 2 == 0
        self.first, self.second = (pair[0], pair[1]) if forward else (pair[1], pair[0])

    def __getitem__(self, index):
        return jnp.where(self.even, self.first[index], self.second[index])


def put_pair(place, pair, slot, next_row, prev_row, stride=1):
    even = place[0] // stride % 2 == 0
    put(pair[0], slot, jnp.where(even, next_row, prev_row))
    put(pair[1], slot, jnp.where(even, prev_row, next_row))


def get(message, slot):
    start, tiles = slot
    return [message[start + tile] for tile in range(tiles)]


def lane_at(shape):
    return lax.broadcasted_iota(jnp.int32, shape, len(shape) - 1)


def roll(value, steps, axis):
    return pltpu.roll(value, steps % value.shape[axis], axis=axis)


def reciprocal(value):
    return pltpu.reciprocal(value, approx=True)


def harmonic(first, second, guard):
    total = first + second
    if guard:
        total = jnp.maximum(total, 1e-3)
    return (2.0 * first) * second * reciprocal(total)


def split(value):
    high = value.astype(jnp.bfloat16)
    return high, (value - high.astype(f32)).astype(jnp.bfloat16)


def dot(halves, table):
    high, low = halves
    return jnp.dot(high, table, preferred_element_type=f32) + jnp.dot(low, table, preferred_element_type=f32)


def pair_table(fine, fine_dim, turn, weight):
    shape = (fine, LANES) if fine_dim == 0 else (LANES, fine)
    fine_at = lax.broadcasted_iota(jnp.int32, shape, fine_dim)
    coarse_at = lax.broadcasted_iota(jnp.int32, shape, 1 - fine_dim)
    if turn is not None:
        coarse_at = coarse_at - jnp.where(fine_at >= turn, LANES // 2, 0)
    return jnp.where(fine_at // 2 == coarse_at, weight, 0.0).astype(jnp.bfloat16)


def turns(sizes, place, level):
    if sizes.sides == 0:
        return []
    if level == 0:
        return [jnp.where(place[1] == 0, LANES, 0)] if sizes.sides == 1 else [LANES, 0]
    return [LANES // 2]


def transfer_plan(sizes, place, level, part):
    plan = []
    if level >= 3:
        return [((0, LANES), 0, 3 * LANES // 4)]
    if level == 2:
        return [((0, sizes.held[2]), 0, None)]
    own = sizes.own[level]
    if part != "border":
        plan += [((2 * LANES * tile, 2 * LANES * (tile + 1)), tile, None) for tile in range(own // 2)]
    if part != "own":
        for index, turn in enumerate(turns(sizes, place, level)):
            start = (own + index) * LANES
            plan.append(((start, start + LANES), own // 2, turn))
    return plan


def narrow(sizes, place, level, sums, target, rows, part="all", shift=0):
    depth = sums.shape[1]
    done = {}
    for (start, stop), tile, turn in transfer_plan(sizes, place, level, part):
        start, stop, tile = start - shift, stop - shift, tile - shift // (2 * LANES)
        columns = split(sums[0:rows, :, start:stop].reshape(rows * depth, stop - start))
        result = dot(columns, pair_table(stop - start, 0, turn, 0.25)).reshape(rows, depth, LANES)
        done[tile] = done[tile] + result if tile in done else result
    for tile, result in done.items():
        target[0:rows, :, tile * LANES : (tile + 1) * LANES] = result


def widen(sizes, place, level, coarse, target, rows):
    depth = coarse.shape[1]
    for (start, stop), tile, turn in transfer_plan(sizes, place, level, "all"):
        columns = split(coarse[0:rows, :, tile * LANES : (tile + 1) * LANES].reshape(rows * depth, LANES))
        result = dot(columns, pair_table(stop - start, 1, turn, 4.0))
        target[0:rows, :, start:stop] = result.reshape(rows, depth, stop - start)


class Joined:
    def __init__(self, inner, outer, first):
        self.inner, self.outer, self.first = inner, outer, first

    def find(self, row):
        place, count = row - self.first, 0 if self.inner is None else self.inner.shape[0]
        if 0 <= place < count:
            return self.inner, place
        return self.outer, row if place < 0 else row - count

    def __getitem__(self, row):
        array, place = self.find(row)
        return array[place]

    def __setitem__(self, row, value):
        array, place = self.find(row)
        array[place] = value


class Level:
    def __init__(self, sizes, level, inner, outer):
        self.n, self.halo = sizes.rows[level], 1 if level == 0 else 2
        counts = inner_rows(sizes, level)
        fx, fy, fz, *rest = parts(inner, counts)
        weight, source, smooth = (None, None, None) if level == 2 else (rest[0], None, rest[1])
        if level == 1:
            weight, source, smooth = rest
        others = [None] * 7 if outer is None else parts(outer, outer_rows(sizes, level))
        if level == 0 and outer is not None:
            others = [others[0], None, None, others[1], None, others[2], None]
        h = self.halo
        self.fx = Joined(fx, others[0], h)
        self.fy, self.fz = Joined(fy, others[1], h - 1), Joined(fz, others[2], h - 1)
        self.weight, self.source, self.smooth = (
            Joined(array, other, h) for array, other in zip((weight, source, smooth), others[3:6])
        )
        self.binding = others[6]

    def inner(self):
        first, last = self.halo, self.halo + self.n - 1
        return range(first + 1, last + 1), range(first, last + 1), range(first + 1, last)

    def outer(self):
        count = self.n + 2 * self.halo
        every = (range(1, count), range(1, count - 1), range(1, count - 1))
        return tuple([row for row in rows if row not in mine] for rows, mine in zip(every, self.inner()))


def inner_rows(sizes, level):
    n = sizes.rows[level]
    return [n - 1, n, n] + [[n - 2] * 2, [n - 2] * 3, []][level]


def outer_rows(sizes, level):
    n = sizes.rows[level]
    return [[2, 2, 2], [4, 2, 2, 4, 4, 4, n + 2], [4, 2, 2] + [n + 2] * 4][level]


def coefficients(sizes, place, level, conduct, binding, fx, fy, fz, weight, rows):
    guard = level > 0 or sizes.sides > 1
    for row in rows[0]:
        fx[row - 1] = harmonic(conduct(row - 1), conduct(row), guard)
    for row in rows[1]:
        mine = conduct(row)
        south = harmonic(mine, roll(mine, 1, 1), guard)
        if level == 0 and sizes.sides < 2:
            cut = 0 if sizes.sides == 0 else jnp.where(place[1] == 0, 0, sizes.extent_y)
            south = jnp.where(lane_at(mine.shape) == cut, 0.0, south)
        below = harmonic(mine, roll(mine, 1, 0), guard)
        fy[row - 1] = south
        fz[row - 1] = jnp.where(lax.broadcasted_iota(jnp.int32, mine.shape, 0) == 0, 0.0, below)
    for row in rows[2]:
        south, below = fy[row - 1], fz[row - 1]
        diagonal = fx[row - 1] + fx[row] + binding(row)
        diagonal = diagonal + (south + roll(south, -1, 1)) + (below + roll(below, -1, 0))
        if guard:
            diagonal = jnp.maximum(diagonal, 1e-6)
        weight[row - 1] = relax_weight * reciprocal(diagonal)


def sweep(first, last, field, binding, fx, fy, fz, emit, width=None):
    cut = lambda value: value if width is None else value[:, :width]
    lower = cut(fx[first - 1]) * (cut(field(first)) - cut(field(first - 1)))
    for row in range(first, last + 1):
        mine = field(row)
        south = fy[row - 1] * (mine - roll(mine, 1, 1))
        across = cut(south - roll(south, -1, 1))
        mine = cut(mine)
        upper = cut(fx[row]) * (cut(field(row + 1)) - mine)
        below = cut(fz[row - 1]) * (mine - roll(mine, 1, 0))
        across = across + (below - roll(below, -1, 0))
        emit(row, binding(row) * mine + (lower - upper) + across)
        lower = upper


def in_pairs(sums, slot_of):
    def add(row, value):
        slot, first = slot_of(row)
        if first:
            sums[slot] = value
        else:
            sums[slot] = sums[slot] + value

    return add


def parts(array, counts):
    views, start = [], 0
    for count in counts:
        views.append(array.at[start : start + count])
        start += count
    return views


def start_kernel(sizes, place, conduct, binding, own0, own1, own2, first, second, *refs):
    edges, sums = refs[: 2 * sizes.sides], refs[-1]
    n0, n1, n2 = sizes.rows[:3]
    for at, array in enumerate((conduct, binding)):
        own0[at] = jnp.swapaxes(array[...], 0, 1)
    for at in (0, 1):
        for row in range(n1):
            sums[at * n1 + row] = own0[at, 2 * row] + own0[at, 2 * row + 1]
    narrow(sizes, place, 0, sums, own1, 2 * n1, "own")
    for row in range(2 * n2):
        sums[row, :, : sizes.own[1] * LANES] = own1[2 * row] + own1[2 * row + 1]
    narrow(sizes, place, 1, sums, own2, 2 * n2, "own")
    ends = []
    for low, at1, at0 in ((n1 - 2, n1 - 1, n0 - 1), (0, 0, 0)):
        near, far = (n2 - 1, n2 - 2) if at0 else (0, 1)
        rows = (own0[0, at0], own1[low], own1[low + 1], own1[n1 + at1], own2[far], own2[n2 + near])
        ends.append(rows)
    for slot, next_row, prev_row in zip(sizes.slots, *ends):
        put_pair(place, (first, second), slot, next_row, prev_row)
    for at in (0, 1):
        cut_edges(sizes, place, own0.at[at], edges[at * sizes.sides : (at + 1) * sizes.sides])


def cut_edges(sizes, place, array, edges):
    last = sizes.extent_y - BORDER
    if sizes.sides == 1:
        at = pl.multiple_of(jnp.where(place[1] == 0, last, 0), LANES)
        edges[0][...] = array[:, :, pl.ds(at, BORDER)]
    elif sizes.sides == 2:
        edges[0][...] = array[:, :, last:]
        edges[1][...] = array[:, :, :BORDER]


def turn_kernel(sizes, place, right_side, turned, *edges):
    turned[...] = jnp.swapaxes(right_side[...], 0, 1)
    cut_edges(sizes, place, turned, edges)


def message_row(sizes, place, level, slot, message, beside):
    start, tiles = slot
    row = get(message, slot)
    if sizes.sides == 1:
        left = place[1] != 0
        tile = beside[0][start + jnp.where(left, tiles - 1, 0)]
        if level > 0:
            reach = BORDER >> level
            lane = lane_at(tile.shape)
            first = jnp.where(left, LANES - reach, 0)
            tile = jnp.where((lane >= first) & (lane < first + reach), tile, 0.0)
        row.append(tile)
    elif sizes.sides == 2:
        right, left = beside[0][start], beside[1][start + tiles - 1]
        if level == 0:
            row += [right, left]
        else:
            reach = BORDER >> level
            lane = lane_at(right.shape)
            row.append(jnp.where(lane < reach, right, jnp.where(lane >= LANES - reach, left, 0.0)))
    return jnp.concatenate(row, axis=1)


def fringe_lanes(shape):
    lane = lane_at(shape)
    return (lane < FRINGE) | (lane >= LANES - FRINGE)


def fringes(sizes, rows):
    total = None
    for index, (level, row) in enumerate(rows):
        border = row[:, sizes.own[level] * LANES :]
        tile = border[:, :LANES]
        lane = lane_at(tile.shape)
        if border.shape[1] > LANES:
            tile = jnp.where(lane < FRINGE, tile, border[:, LANES:])
        tile = jnp.where((lane < FRINGE) | (lane >= LANES - FRINGE), tile, 0.0)
        tile = roll(tile, SPREAD * index + SPREAD // 2, 1)
        total = tile if total is None else total + tile
    return total


def fringed_row(sizes, level, index, message):
    row = get(message, sizes.up_slots[index])
    if sizes.border[level]:
        tile = roll(message[sizes.up_tiles], -(SPREAD * index + SPREAD // 2), 1)
        lane = lane_at(tile.shape)
        right, left = jnp.where(lane < FRINGE, tile, 0.0), jnp.where(lane >= LANES - FRINGE, tile, 0.0)
        row += [right, left] if sizes.border[level] == 2 else [right + left]
    return jnp.concatenate(row, axis=1)


def packing(count):
    return -(-count // 2)


def pack_rows(rows, target):
    half = LANES // 2
    lane = lane_at(rows[0].shape)
    for index in range(packing(len(rows))):
        held = jnp.where(lane < half, rows[2 * index], 0.0)
        if 2 * index + 1 < len(rows):
            held = jnp.where(lane < half, held, pltpu.roll(rows[2 * index + 1], half, axis=1))
        target[index] = held


def unpack_rows(sizes, place, tiles, count, others=()):
    half, reach = LANES // 2, BORDER >> 3
    lane = lane_at(tiles.shape[1:])
    rows = []
    for index in range(count):
        held = tiles[index // 2]
        row = jnp.where(lane < half, pltpu.roll(held, half, axis=1) if index % 2 else held, 0.0)
        for side, other in enumerate(others):
            first = LANES - reach if side else half
            if sizes.sides == 1:
                first = jnp.where(place[1] == 0, half, LANES - reach)
            beside = other[index // 2]
            beside = beside if index % 2 else pltpu.roll(beside, half, axis=1)
            row = jnp.where((lane >= first) & (lane < first + reach), beside, row)
        rows.append(row)
    return rows


def merge_into(sizes, place, stride, radix, arrays, source, conduct, binding, first, others=()):
    position = (place[0] // stride) % radix
    source[...] = jnp.zeros(source.shape, f32)
    for step, array in enumerate(arrays):
        at = (position ^ step) * stride
        rows = unpack_rows(sizes, place, array, 3 * stride + 2, [other[step] for other in others])
        for index, row in enumerate(rows[: stride + 2]):
            source[at + index] = source[at + index] + row
        for index in range(stride):
            conduct[at + index + first] = rows[stride + 2 + index]
            binding[at + index] = rows[2 * stride + 2 + index]


def merge_kernel(sizes, stride, radix, place, *refs):
    arrays, out, (source, conduct, binding) = refs[:radix], refs[radix], refs[radix + 1 :]
    merge_into(sizes, place, stride, radix, arrays, source, conduct, binding, 0)
    count = stride * radix
    rows = [source[row] for row in range(count + 2)]
    rows += [conduct[row] for row in range(count)] + [binding[row] for row in range(count)]
    pack_rows(rows, out)


def held_rows(sizes, owns, borders):
    def held_row(level, at, row):
        if level > 0:
            row = at * sizes.rows[level] + row
            return jnp.concatenate([owns[level][row], *(array[row] for array in borders[level])], axis=1)
        own = owns[3][row] if at == 2 else owns[0][at, row]
        sides = len(borders[0]) // 3
        return jnp.concatenate([own, *(array[row] for array in borders[0][at * sides : (at + 1) * sides])], axis=1)

    return held_row


def inner_kernel(sizes, place, *refs):
    s = sizes.sides
    owns, borders0, refs = refs[:4], refs[4 : 4 + 3 * s], refs[4 + 3 * s :]
    border1, border2, inner0, inner1, inner2, sums = refs
    n0, n1, n2 = sizes.rows[:3]
    if s:
        for row in range(2 * n1):
            for side in range(s):
                columns = slice(side * LANES, (side + 1) * LANES)
                at, low = row // n1, 2 * (row % n1)
                sums[row, :, columns] = borders0[at * s + side][low] + borders0[at * s + side][low + 1]
        narrow(sizes, place, 0, sums, border1, 2 * n1, "border", sizes.own[0] * LANES)
        for row in range(2 * n2):
            sums[row, :, :LANES] = border1[2 * row] + border1[2 * row + 1]
        narrow(sizes, place, 1, sums, border2, 2 * n2, "border", sizes.own[1] * LANES)
    held_row = held_rows(sizes, owns, [borders0, [border1][:s], [border2][:s]])
    levels = [Level(sizes, level, inner, None) for level, inner in enumerate((inner0, inner1, inner2))]
    for index, level in enumerate(levels):
        conduct = lambda row, index=index, level=level: held_row(index, 0, row - level.halo)
        bound = lambda row, index=index, level=level: held_row(index, 1, row - level.halo)
        coefficients(
            sizes, place, index, conduct, bound, level.fx, level.fy, level.fz, level.weight, level.inner()
        )
        if index == 0:
            right = lambda row: held_row(0, 2, row - 1)
            for row in range(2, n0):
                level.smooth[row - 1] = level.weight[row - 1] * right(row)
            add = in_pairs(sums, lambda row: ((row - 3) // 2, row % 2 == 1))
            field = lambda row, level=level: level.smooth[row - 1]
            emit = lambda row, value: add(row, right(row) - value)
            sweep(3, n0 - 2, field, bound, level.fx, level.fy, level.fz, emit)
        if index == 1:
            narrow(sizes, place, 0, sums, level.source.inner, n1 - 2)
            for row in range(2, n1):
                level.smooth[row] = level.weight[row] * level.source[row]


def down_kernel(sizes, place, *refs):
    s = sizes.sides
    owns, borders0, refs = refs[:4], refs[4 : 4 + 3 * s], refs[4 + 3 * s :]
    pairs_of = [refs[2 * index : 2 * index + 2] for index in range(1 + s)]
    refs = refs[2 * (1 + s) :]
    from_prev, *beside_prev = (Arrived(place, pair, 0) for pair in pairs_of)
    from_next, *beside_next = (Arrived(place, pair, 1) for pair in pairs_of)
    (border1, border2), inners, refs = refs[:2], refs[2:5], refs[5:]
    outers, contribution, with_far, ups, far, refs = refs[:3], refs[3], refs[4], refs[5:7], refs[7], refs[8:]
    level3, near, sums = refs
    slots = sizes.slots
    n0, n1, n2 = sizes.rows[:3]
    levels = [Level(sizes, index, inner, outer) for index, (inner, outer) in enumerate(zip(inners, outers))]
    held_row = held_rows(sizes, owns, [borders0, [border1][:s], [border2][:s]])

    def prev_row(level, index):
        return message_row(sizes, place, level, slots[index], from_prev, beside_prev)

    def next_row(level, index):
        return message_row(sizes, place, level, slots[index], from_next, beside_next)

    def conduct0(row):
        if row == 0:
            return prev_row(0, 0)
        if row == n0 + 1:
            return next_row(0, 0)
        return held_row(0, 0, row - 1)

    for at, row_of in enumerate((prev_row, next_row)):
        sums[at, :, : sizes.held[1]] = row_of(1, 1) + row_of(1, 2)
    narrow(sizes, place, 1, sums.at[:, :, : sizes.held[1]], near, 2)
    zero = jnp.zeros((sizes.depth, sizes.held[0]), f32)
    level = levels[0]
    bound0 = lambda row: held_row(0, 1, row - 1)
    right = lambda row: held_row(0, 2, row - 1)
    coefficients(
        sizes, place, 0, conduct0, bound0, level.fx, level.fy, level.fz, level.weight, level.outer()
    )
    for row in (1, n0):
        level.smooth[row - 1] = level.weight[row - 1] * right(row)
    first_slot = lambda row: (row + 1) // 2
    add = in_pairs(
        sums,
        lambda row: (first_slot(row) - (n1 - 2 if row > n0 // 2 else 0), row % 2 == 1 or row == 0),
    )
    field = lambda row, level=level: level.smooth[row - 1] if 0 < row < n0 + 1 else zero
    emit = lambda row, value: add(row, right(row) - value)
    add(0, level.fx[0] * field(1))
    sweep(1, 2, field, bound0, level.fx, level.fy, level.fz, emit)
    sweep(n0 - 1, n0, field, bound0, level.fx, level.fy, level.fz, emit)
    add(n0 + 1, level.fx[n0] * field(n0))
    fine_held = sizes.held[0]
    for index in (1, 2):
        level, n = levels[index], sizes.rows[index]
        held = sizes.held[index]
        narrow(
            sizes, place, index - 1, sums.at[:, :, :fine_held], level.source.outer, level.source.outer.shape[0]
        )
        binding = level.binding
        binding[0] = prev_row(index, 3 if index == 1 else 5)
        binding[n + 1] = next_row(index, 3 if index == 1 else 5)
        for row in range(n):
            binding[row + 1] = held_row(index, 1, row)

        def conduct(row, n=n, index=index):
            if 2 <= row < n + 2:
                return held_row(index, 0, row - 2)
            if index == 1:
                return prev_row(1, 1 + row) if row < 2 else next_row(1, row - n - 1)
            if row in (1, n + 2):
                return near[0 if row == 1 else 1]
            return (prev_row if row == 0 else next_row)(2, 4)

        bound = lambda row, binding=binding: binding[row - 1]
        coefficients(
            sizes, place, index, conduct, bound, level.fx, level.fy, level.fz, level.weight, level.outer()
        )
        for row in level.outer()[2] if index == 1 else range(1, n + 3):
            level.smooth[row - 1] = level.weight[row - 1] * level.source[row - 1]
        zero = jnp.zeros((sizes.depth, held), f32)
        field = lambda row, level=level, n=n, zero=zero: level.smooth[row - 1] if 0 < row < n + 3 else zero
        add = in_pairs(sums.at[:, :, :held], lambda row: (row // 2, row % 2 == 0))
        emit = lambda row, value, level=level, add=add: add(row, level.source[row - 1] - value)
        add(0, level.fx[0] * field(1))
        sweep(1, n + 2, field, bound, level.fx, level.fy, level.fz, emit)
        add(n + 3, level.fx[n + 2] * field(n + 2))
        fine_held = held
    narrow(sizes, place, 2, sums.at[:, :, : sizes.held[2]], level3, 3)
    for at in (0, 1):
        sums[at, :, : sizes.held[2]] = held_row(2, at, 0) + held_row(2, at, 1)
    narrow(sizes, place, 2, sums.at[:, :, : sizes.held[2]], level3.at[3:5], 2)
    tiles = packing(5)
    pack_rows([level3[row] for row in range(5)], contribution)
    with_far[0:tiles] = contribution[...]
    v0, s1, v1 = levels[0].smooth, levels[1].source, levels[1].smooth
    s2, v2 = levels[2].source, levels[2].smooth
    next_rows = (v0[n0 - 1], s1[n1], v1[n1 - 1], s2[n2], s2[n2 + 1], v2[n2 - 1])
    prev_rows = (v0[0], s1[1], v1[2], s2[1], s2[0], v2[2])
    for slot, next_row, prev_row in zip(sizes.up_slots, next_rows, prev_rows):
        put_pair(place, ups, slot, next_row, prev_row)
    if s:
        ends = [fringes(sizes, list(zip((0, 1, 1, 2, 2, 2), rows))) for rows in (next_rows, prev_rows)]
        put_pair(place, ups, (sizes.up_tiles, 1), *ends)
    far_tiles = sizes.held[2] // LANES
    put_pair(place, (with_far.at[tiles : tiles + far_tiles], far), (0, far_tiles), v2[n2 + 1], v2[0], 2)


def relax(count, field, refs_of, source, target):
    fx, fy, fz, weight, binding = refs_of

    def update(row, value):
        target(row, field(row) + weight[row - 1] * (source(row) - value))

    sweep(1, count - 2, field, binding, fx, fy, fz, update)


def store(array, first):
    def put_row(row, value):
        array[row - first] = value

    return put_row


def coarse_kernel(sizes, stride, radix, place, *refs):
    blocks, refs = refs[:radix], refs[radix:]
    others, refs = [refs[side * radix : (side + 1) * radix] for side in range(sizes.sides)], refs[sizes.sides * radix :]
    out, merged, sums, both, defects = refs[:5]
    coarse = [refs[5 + 9 * index : 14 + 9 * index] for index in range(3)]
    total = sizes.span_count
    merge_into(sizes, place, stride, radix, blocks, merged, coarse[0][4], coarse[0][5], 1, others)
    zero = jnp.zeros((sizes.depth, LANES), f32)
    for index in range(3):
        level = 3 + index
        fx, fy, fz, weight, conduct, binding, source, smooth, iterate = coarse[index]
        count, half = total >> index, total >> index + 1
        for array in (conduct, smooth, iterate):
            array[0] = zero
            array[count + 1] = zero
        if index < 2:
            conduct_next, binding_next = coarse[index + 1][4:6]
            for row in range(half):
                sums[row] = conduct[2 * row + 1] + conduct[2 * row + 2]
                sums[half + row] = binding[2 * row] + binding[2 * row + 1]
            narrow(sizes, place, level, sums, both, 2 * half)
            for row in range(half):
                conduct_next[row + 1], binding_next[row] = both[row], both[half + row]
        bound = lambda row, binding=binding: binding[row - 1]
        at_row = lambda row, conduct=conduct: conduct[row]
        every = (range(1, count + 2), range(1, count + 1), range(1, count + 1))
        coefficients(sizes, place, level, at_row, bound, fx, fy, fz, weight, every)
    for index in range(3):
        level = 3 + index
        fx, fy, fz, weight, conduct, binding, source, smooth, iterate = coarse[index]
        count = total >> index
        bound = lambda row, binding=binding: binding[row - 1]
        if index == 0:
            source = merged.at[1 : count + 1]
        for row in range(count):
            smooth[row + 1] = weight[row] * source[row]
        if index < 2:
            add = in_pairs(defects, lambda row: ((row - 1) // 2, row % 2 == 1))
            emit = lambda row, value, source=source, add=add: add(row, source[row - 1] - value)
            sweep(1, count, lambda row, smooth=smooth: smooth[row], bound, fx, fy, fz, emit)
            narrow(sizes, place, level, defects, coarse[index + 1][6], count // 2)

    fx, fy, fz, weight, conduct, binding, source, smooth, iterate = coarse[2]
    held, other = smooth, iterate
    for _ in range(COARSE_SWEEPS - 1):
        field = lambda row, held=held: held[row]
        mine = lambda row: source[row - 1]
        bound = lambda row: binding[row - 1]
        relax((total >> 2) + 2, field, (fx, fy, fz, weight, bound), mine, store(other, 0))
        held, other = other, held
    for index in (1, 0):
        fx, fy, fz, weight, conduct, binding, source, smooth, iterate = coarse[index]
        if index == 0:
            source = merged.at[1 : total + 1]
        count = total >> index
        widen(sizes, place, 3 + index, held.at[1 : count // 2 + 1], sums, count // 2)
        for row in range(count):
            smooth[row + 1] = smooth[row + 1] + sums[row // 2, :, :LANES]
        if index == 0:
            break
        field = lambda row, smooth=smooth: smooth[row]
        mine = lambda row, source=source: source[row - 1]
        bound = lambda row, binding=binding: binding[row - 1]
        relax(count + 2, field, (fx, fy, fz, weight, bound), mine, store(iterate, 0))
        held = iterate

    for at in range(3):
        row = jnp.clip(place[0] + at, 1, total)
        mine = smooth[row]
        lower, upper = fx[row - 1] * (mine - smooth[row - 1]), fx[row] * (smooth[row + 1] - mine)
        south = fy[row - 1] * (mine - roll(mine, 1, 1))
        below = fz[row - 1] * (mine - roll(mine, 1, 0))
        across = (south - roll(south, -1, 1)) + (below - roll(below, -1, 0))
        value = binding[row - 1] * mine + (lower - upper) + across
        value = mine + weight[row - 1] * (source[row - 1] - value)
        out[at] = jnp.where(row == place[0] + at, value, 0.0)


def up_kernel(sizes, place, coarse, *refs):
    s = sizes.sides
    pair, far_pair, inners, outers, owns = refs[:2], refs[2:4], refs[4:7], refs[7:10], refs[10:12]
    levels = [Level(sizes, index, inner, outer) for index, (inner, outer) in enumerate(zip(inners, outers))]
    from_prev, from_next = (Arrived(place, pair, forward) for forward in (0, 1))
    tiles = packing(5)
    far_pair = (far_pair[0].at[tiles : tiles + sizes.held[2] // LANES], far_pair[1])
    fars = [Arrived(place, far_pair, forward, 2) for forward in (0, 1)]
    borders0, out, refs = refs[12 : 12 + 3 * s], refs[12 + 3 * s], refs[13 + 3 * s :]
    total1, total2, result, edges0, edges1 = refs[:5]
    over2, over1, over0, lift2, lift1, lift0, it2, it1, it0, semaphores = refs[5:]
    slots = sizes.slots
    n0, n1, n2 = sizes.rows[:3]
    width = sizes.own[0] * LANES

    before, behind = fringed_row(sizes, 0, 0, from_prev), fringed_row(sizes, 0, 0, from_next)
    lift0[0], lift0[n0 + 1] = before, behind
    edges0[0], edges0[1] = levels[0].fx[0] * before, levels[0].fx[n0] * behind
    narrow(sizes, place, 0, edges0, edges1, 2)

    widen(sizes, place, 2, coarse, over2, 3)
    for level, first, totals, over, lift, target, upper in (
        (2, 3, total2, over2, lift2, it2, over1),
        (1, 1, total1, over1, lift1, it1, over0),
    ):
        n, kept = sizes.rows[level], levels[level]
        fx, fy, fz, weight, binding = kept.fx, kept.fy, kept.fz, kept.weight, kept.binding
        own, smooth = kept.source, kept.smooth
        fringed = lambda index, message, level=level: fringed_row(sizes, level, index, message)
        if level == 1:
            smooth_at = first + 1
            edge = {2: own[1] + edges1[0], n + 1: own[n] + edges1[1]}
        else:
            smooth_at = first + 2
            edge = {2: own[1] + fringed(first + 1, from_prev)}
            edge[n + 1] = own[n] + fringed(first + 1, from_next)
        edge[1], edge[n + 2] = own[0] + fringed(first, from_prev), own[n + 1] + fringed(first, from_next)
        for row, value in edge.items():
            totals[row - 1] = value
        for row in range(n + 4):
            if row in (0, n + 3):
                value = fringed(smooth_at, from_next if row else from_prev)
                if level == 2:
                    far = fars[1 if row else 0]
                    value = value + jnp.concatenate(get(far, (0, sizes.held[2] // LANES)), axis=1)
            elif row in edge:
                value = weight[row - 1] * totals[row - 1]
            else:
                value = smooth[row - 1]
            lift[row] = value + over[row // 2]
        field = lambda row, lift=lift: lift[row]
        mine = lambda row, own=own, totals=totals, edge=edge: (totals if row in edge else own)[row - 1]
        bound = lambda row, binding=binding: binding[row - 1]
        relax(n + 4, field, (fx, fy, fz, weight, bound), mine, store(target, 1))
        widen(sizes, place, level - 1, target, upper, n + 2)

    fx, fy, fz, weight, v0 = levels[0].fx, levels[0].fy, levels[0].fz, levels[0].weight, levels[0].smooth
    lift0[0] = lift0[0] + over0[0]
    lift0[n0 + 1] = lift0[n0 + 1] + over0[n1 + 1]
    for row in range(1, n0 + 1):
        lift0[row] = v0[row - 1] + over0[(row + 1) // 2]
    field = lambda row: lift0[row]

    def relax_own(row, value):
        it0[row - 1] = lift0[row, :, :width] + weight[row - 1][:, :width] * (owns[1][row - 1] - value)

    sweep(1, n0, field, lambda row: owns[0][1, row - 1], fx, fy, fz, relax_own, width)
    step = sizes.depth // CHUNKS
    copies = []
    for chunk in range(CHUNKS):
        part = slice(chunk * step, (chunk + 1) * step)
        result[part] = jnp.swapaxes(it0[:, part, :width], 0, 1)
        copies.append(pltpu.make_async_copy(result.at[part], out.at[part], semaphores.at[chunk]))
        copies[-1].start()
    for copy in copies:
        copy.wait()


def call(body, name, micros, outputs, scratch, place, inputs, copies=0, far_out=False):
    near, far = pl.BlockSpec(memory_space=pltpu.VMEM), pl.BlockSpec(memory_space=pl.ANY)
    scratch = [pltpu.VMEM(shape, f32) for shape in scratch]
    if copies:
        scratch.append(pltpu.SemaphoreType.DMA((copies,)))
    return pl.pallas_call(
        body,
        name=name,
        out_shape=[jax.ShapeDtypeStruct(shape, f32) for shape in outputs],
        in_specs=[pl.BlockSpec(memory_space=pltpu.SMEM)] + [near] * len(inputs),
        out_specs=[far if far_out else near] * len(outputs),
        scratch_shapes=scratch,
        cost_estimate=pl.CostEstimate(flops=int(micros * 1.15e9), bytes_accessed=int(micros * BYTES_A_MICRO), transcendentals=0),
        compiler_params=pltpu.CompilerParams(vmem_limit_bytes=VMEM_LIMIT),
    )(place, *inputs)


def along(value, axis, steps):
    count = lax.axis_size(axis)
    initial, last = max(0, -steps), min(count, count - steps)
    return lax.ppermute(value, axis, [(source, source + steps) for source in range(initial, last)])


def beside(values, sizes):
    if sizes.sides == 1:
        return [[lax.ppermute(value, "width", [(0, 1), (1, 0)]) for value in values]]
    if sizes.sides == 2:
        return [[along(value, "width", steps) for value in values] for steps in (-1, 1)]
    return []


def edge_columns(edges, sizes):
    if sizes.sides == 1:
        return [lax.ppermute(edges[0], "width", [(0, 1), (1, 0)])]
    if sizes.sides == 2:
        return [along(edges[1], "width", -1), along(edges[0], "width", 1)]
    return []


def stages(count):
    stride = 1
    while stride < count:
        radix = 4 if count // stride % 4 == 0 else 2
        yield stride, radix
        stride *= radix


def swap(value, stride, radix, others=None):
    count = lax.axis_size("span")
    others = others or {}
    return [value] + [
        lax.ppermute(others.get(step, value), "span", [(device, device ^ step * stride) for device in range(count)])
        for step in range(1, radix)
    ]


def exchange(pair, stride):
    count = lax.axis_size("span")
    routes = [[], []]
    for low in range(count - stride):
        routes[low // stride % 2] += [(low, low + stride), (low + stride, low)]
    return [None if value is None else lax.ppermute(value, "span", route) for value, route in zip(pair, routes)]


def on_device(right_side, diffusivity, reaction):
    depth, extent_x, extent_y = diffusivity.shape
    sizes = Sizes(depth, extent_x, extent_y, lax.axis_size("span"), lax.axis_size("width"))
    place = jnp.stack([lax.axis_index("span"), lax.axis_index("width")]).astype(jnp.int32)
    n0, n1, n2, n3 = sizes.rows
    s = sizes.sides
    tile = (depth, LANES)
    own = [(depth, count * LANES) for count in sizes.own]
    held = [(depth, count) for count in sizes.held]
    down_message = (sizes.tiles, *tile)
    up_message = (sizes.up_tiles + 1, *tile)
    own0, own1, own2, first, second, *edges = call(
        functools.partial(start_kernel, sizes),
        "start",
        1.1,
        [(2, n0, *own[0]), (2 * n1, *own[1]), (2 * n2, *own[2]), down_message, down_message]
        + [(n0, depth, BORDER)] * 2 * s,
        [(2 * n1, *own[0])],
        place,
        [diffusivity, reaction],
    )
    borders = edge_columns(edges[:s], sizes) + edge_columns(edges[s:], sizes)
    halos = exchange([first, second], 1)
    turned, *edges = call(
        functools.partial(turn_kernel, sizes),
        "turn",
        0.7,
        [(n0, *own[0])] + [(n0, depth, BORDER)] * s,
        [],
        place,
        [right_side],
    )
    borders += edge_columns(edges, sizes)
    plan = list(stages(sizes.span_count))

    part = packing(5)
    far = (sizes.held[2] // LANES, *tile)
    inners = [(sum(inner_rows(sizes, level)), *held[level]) for level in range(3)]
    outers = [(sum(outer_rows(sizes, level)), *held[level]) for level in range(3)]
    inner = call(
        functools.partial(inner_kernel, sizes),
        "inner",
        0.5,
        [(2 * n1, *tile), (2 * n2, *tile), *inners],
        [(2 * n1, *held[0])],
        place,
        [own0, own1, own2, turned, *borders],
    )
    halos, inner = lax.optimization_barrier((halos, inner))
    sides = beside(halos, sizes)
    downs = call(
        functools.partial(down_kernel, sizes),
        "down",
        2.5,
        [*outers, (part, *tile), (part + far[0], *tile), up_message, up_message, far],
        [(5, *tile), (2, *held[2]), (n1 + 2, *held[0])],
        place,
        [own0, own1, own2, turned, *borders, *halos, *sum(sides, []), *inner],
    )
    outer, blocks, with_far, ups, far_second = downs[:3], downs[3], downs[4], list(downs[5:7]), downs[7]
    far_rows = None
    for stride, radix in plan[:-1]:
        count = stride * radix
        if far_rows is None:
            blocks = swap(blocks, stride, radix, {2: with_far})
            far_rows = [blocks[2], exchange([None, far_second], 2)[1]]
        else:
            blocks = swap(blocks, stride, radix)
        (blocks,) = call(
            functools.partial(merge_kernel, sizes, stride, radix),
            "merge",
            0.9,
            [(packing(3 * count + 2), *tile)],
            [(count + 2, *tile), (count, *tile), (count, *tile)],
            place,
            blocks,
        )
    stride, radix = plan[-1]
    blocks = swap(blocks, stride, radix)
    received = lax.optimization_barrier([exchange([ups[0], None], 1)[0], ups[1]])
    received = [received[0], exchange([None, received[1]], 1)[1]] + far_rows
    scratch = [(sizes.span_count + 2, *tile)] + [(sizes.span_count, *tile)] * 3
    for index in range(3):
        count = sizes.span_count >> index
        scratch += [(count + 1, *tile)] + [(count, *tile)] * 3 + [(count + 2, *tile)] + [(count, *tile)] * 2
        scratch += [(count + 2, *tile)] * 2
    own_part = beside(blocks[:1], sizes)
    blocks, received[3], own_part = lax.optimization_barrier((blocks, received[3], own_part))
    swapped = [first + rest for first, rest in zip(own_part, beside(blocks[1:], sizes))]
    (coarse,) = call(
        functools.partial(coarse_kernel, sizes, stride, radix),
        "coarse",
        0.7,
        [(n3 + 2, *tile)],
        scratch,
        place,
        [*blocks, *sum(swapped, [])],
    )
    scratch = [(n1 + 2, *held[1]), (n2 + 2, *held[2]), diffusivity.shape, (2, *held[0]), (2, *held[1])]
    scratch += [(n3 + 2, *held[2]), (n2 + 2, *held[1]), (n1 + 2, *held[0])]
    scratch += [(n2 + 4, *held[2]), (n1 + 4, *held[1]), (n0 + 2, *held[0])]
    scratch += [(n2 + 2, *held[2]), (n1 + 2, *held[1]), (n0, *own[0])]
    (correction,) = call(
        functools.partial(up_kernel, sizes),
        "up",
        3.0,
        [diffusivity.shape],
        scratch,
        place,
        [coarse, *received, *inner[2:], *outer, own0, turned, *borders],
        copies=CHUNKS,
        far_out=True,
    )
    return correction


def solution(mesh):
    in_specs = (P(None, "span", "width"),) * 3
    return jax.shard_map(
        on_device, mesh=mesh, in_specs=in_specs, out_specs=P(None, "span", "width"), check_vma=False
    )
```

```python
import functools

import jax
import jax.numpy as jnp
from jax import lax
from jax.experimental import pallas as pl
from jax.experimental.pallas import tpu as pltpu
from jax.sharding import PartitionSpec as P

LEVELS = 6
COARSE_SWEEPS = 3
LANES = 128
BORDER = 128
FRINGE = 4
SPREAD = 16
relax_weight = 0.8
f32 = jnp.float32
VMEM_LIMIT = 32 * 1024 * 1024
BYTES_A_MICRO = 3.69e6
CHUNKS = 4


class Sizes:
    def __init__(self, depth, extent_x, extent_y, span_count, width_count):
        self.depth, self.extent_x, self.extent_y = depth, extent_x, extent_y
        self.span_count, self.width_count = span_count, width_count
        self.sides = min(width_count - 1, 2)
        self.own = [(extent_y >> level) // LANES for level in range(3)]
        self.border = [self.sides, min(self.sides, 1), min(self.sides, 1)]
        self.held = [(self.own[level] + self.border[level]) * LANES for level in range(3)] + [LANES] * 3
        self.rows = [extent_x >> level for level in range(4)]
        self.slots = []
        start = 0
        for level in (0, 1, 1, 1, 2, 2):
            self.slots.append((start, self.own[level]))
            start += self.own[level]
        self.tiles = start
        self.up_slots = []
        start = 0
        for level in (0, 1, 1, 2, 2, 2):
            self.up_slots.append((start, self.own[level]))
            start += self.own[level]
        self.up_tiles = start


def put(message, slot, row):
    start, tiles = slot
    for tile in range(tiles):
        message[start + tile] = row[:, tile * LANES : (tile + 1) * LANES]


class Arrived:
    def __init__(self, place, pair, forward, stride=1):
        self.even = place[0] // stride % 2 == 0
        self.first, self.second = (pair[0], pair[1]) if forward else (pair[1], pair[0])

    def __getitem__(self, index):
        return jnp.where(self.even, self.first[index], self.second[index])


def put_pair(place, pair, slot, next_row, prev_row, stride=1):
    even = place[0] // stride % 2 == 0
    put(pair[0], slot, jnp.where(even, next_row, prev_row))
    put(pair[1], slot, jnp.where(even, prev_row, next_row))


def get(message, slot):
    start, tiles = slot
    return [message[start + tile] for tile in range(tiles)]


def lane_at(shape):
    return lax.broadcasted_iota(jnp.int32, shape, len(shape) - 1)


def roll(value, steps, axis):
    return pltpu.roll(value, steps % value.shape[axis], axis=axis)


def reciprocal(value):
    return pltpu.reciprocal(value, approx=True)


def harmonic(first, second, guard):
    total = first + second
    if guard:
        total = jnp.maximum(total, 1e-3)
    return (2.0 * first) * second * reciprocal(total)


def split(value):
    high = value.astype(jnp.bfloat16)
    return high, (value - high.astype(f32)).astype(jnp.bfloat16)


def dot(halves, table):
    high, low = halves
    return jnp.dot(high, table, preferred_element_type=f32) + jnp.dot(low, table, preferred_element_type=f32)


def pair_table(fine, fine_dim, turn, weight):
    shape = (fine, LANES) if fine_dim == 0 else (LANES, fine)
    fine_at = lax.broadcasted_iota(jnp.int32, shape, fine_dim)
    coarse_at = lax.broadcasted_iota(jnp.int32, shape, 1 - fine_dim)
    if turn is not None:
        coarse_at = coarse_at - jnp.where(fine_at >= turn, LANES // 2, 0)
    return jnp.where(fine_at // 2 == coarse_at, weight, 0.0).astype(jnp.bfloat16)


def turns(sizes, place, level):
    if sizes.sides == 0:
        return []
    if level == 0:
        return [jnp.where(place[1] == 0, LANES, 0)] if sizes.sides == 1 else [LANES, 0]
    return [LANES // 2]


def transfer_plan(sizes, place, level, part):
    plan = []
    if level >= 3:
        return [((0, LANES), 0, 3 * LANES // 4)]
    if level == 2:
        return [((0, sizes.held[2]), 0, None)]
    own = sizes.own[level]
    if part != "border":
        plan += [((2 * LANES * tile, 2 * LANES * (tile + 1)), tile, None) for tile in range(own // 2)]
    if part != "own":
        for index, turn in enumerate(turns(sizes, place, level)):
            start = (own + index) * LANES
            plan.append(((start, start + LANES), own // 2, turn))
    return plan


def narrow(sizes, place, level, sums, target, rows, part="all", shift=0):
    depth = sums.shape[1]
    done = {}
    for (start, stop), tile, turn in transfer_plan(sizes, place, level, part):
        start, stop, tile = start - shift, stop - shift, tile - shift // (2 * LANES)
        columns = split(sums[0:rows, :, start:stop].reshape(rows * depth, stop - start))
        result = dot(columns, pair_table(stop - start, 0, turn, 0.25)).reshape(rows, depth, LANES)
        done[tile] = done[tile] + result if tile in done else result
    for tile, result in done.items():
        target[0:rows, :, tile * LANES : (tile + 1) * LANES] = result


def widen(sizes, place, level, coarse, target, rows):
    depth = coarse.shape[1]
    for (start, stop), tile, turn in transfer_plan(sizes, place, level, "all"):
        columns = split(coarse[0:rows, :, tile * LANES : (tile + 1) * LANES].reshape(rows * depth, LANES))
        result = dot(columns, pair_table(stop - start, 1, turn, 4.0))
        target[0:rows, :, start:stop] = result.reshape(rows, depth, stop - start)


class Joined:
    def __init__(self, inner, outer, first):
        self.inner, self.outer, self.first = inner, outer, first

    def find(self, row):
        place, count = row - self.first, 0 if self.inner is None else self.inner.shape[0]
        if 0 <= place < count:
            return self.inner, place
        return self.outer, row if place < 0 else row - count

    def __getitem__(self, row):
        array, place = self.find(row)
        return array[place]

    def __setitem__(self, row, value):
        array, place = self.find(row)
        array[place] = value


class Level:
    def __init__(self, sizes, level, inner, outer):
        self.n, self.halo = sizes.rows[level], 1 if level == 0 else 2
        counts = inner_rows(sizes, level)
        fx, fy, fz, *rest = parts(inner, counts)
        weight, source, smooth = (None, None, None) if level == 2 else (rest[0], None, rest[1])
        if level == 1:
            weight, source, smooth = rest
        others = [None] * 7 if outer is None else parts(outer, outer_rows(sizes, level))
        if level == 0 and outer is not None:
            others = [others[0], None, None, others[1], None, others[2], None]
        h = self.halo
        self.fx = Joined(fx, others[0], h)
        self.fy, self.fz = Joined(fy, others[1], h - 1), Joined(fz, others[2], h - 1)
        self.weight, self.source, self.smooth = (
            Joined(array, other, h) for array, other in zip((weight, source, smooth), others[3:6])
        )
        self.binding = others[6]

    def inner(self):
        first, last = self.halo, self.halo + self.n - 1
        return range(first + 1, last + 1), range(first, last + 1), range(first + 1, last)

    def outer(self):
        count = self.n + 2 * self.halo
        every = (range(1, count), range(1, count - 1), range(1, count - 1))
        return tuple([row for row in rows if row not in mine] for rows, mine in zip(every, self.inner()))


def inner_rows(sizes, level):
    n = sizes.rows[level]
    return [n - 1, n, n] + [[n - 2] * 2, [n - 2] * 3, []][level]


def outer_rows(sizes, level):
    n = sizes.rows[level]
    return [[2, 2, 2], [4, 2, 2, 4, 4, 4, n + 2], [4, 2, 2] + [n + 2] * 4][level]


def coefficients(sizes, place, level, conduct, binding, fx, fy, fz, weight, rows):
    guard = level > 0 or sizes.sides > 1
    for row in rows[0]:
        fx[row - 1] = harmonic(conduct(row - 1), conduct(row), guard)
    for row in rows[1]:
        mine = conduct(row)
        south = harmonic(mine, roll(mine, 1, 1), guard)
        if level == 0 and sizes.sides < 2:
            cut = 0 if sizes.sides == 0 else jnp.where(place[1] == 0, 0, sizes.extent_y)
            south = jnp.where(lane_at(mine.shape) == cut, 0.0, south)
        below = harmonic(mine, roll(mine, 1, 0), guard)
        fy[row - 1] = south
        fz[row - 1] = jnp.where(lax.broadcasted_iota(jnp.int32, mine.shape, 0) == 0, 0.0, below)
    for row in rows[2]:
        south, below = fy[row - 1], fz[row - 1]
        diagonal = fx[row - 1] + fx[row] + binding(row)
        diagonal = diagonal + (south + roll(south, -1, 1)) + (below + roll(below, -1, 0))
        if guard:
            diagonal = jnp.maximum(diagonal, 1e-6)
        weight[row - 1] = relax_weight * reciprocal(diagonal)


def sweep(first, last, field, binding, fx, fy, fz, emit, width=None):
    cut = lambda value: value if width is None else value[:, :width]
    lower = cut(fx[first - 1]) * (cut(field(first)) - cut(field(first - 1)))
    for row in range(first, last + 1):
        mine = field(row)
        south = fy[row - 1] * (mine - roll(mine, 1, 1))
        across = cut(south - roll(south, -1, 1))
        mine = cut(mine)
        upper = cut(fx[row]) * (cut(field(row + 1)) - mine)
        below = cut(fz[row - 1]) * (mine - roll(mine, 1, 0))
        across = across + (below - roll(below, -1, 0))
        emit(row, binding(row) * mine + (lower - upper) + across)
        lower = upper


def in_pairs(sums, slot_of):
    def add(row, value):
        slot, first = slot_of(row)
        if first:
            sums[slot] = value
        else:
            sums[slot] = sums[slot] + value

    return add


def parts(array, counts):
    views, start = [], 0
    for count in counts:
        views.append(array.at[start : start + count])
        start += count
    return views


def start_kernel(sizes, place, conduct, binding, own0, own1, own2, first, second, *refs):
    edges, sums = refs[: 2 * sizes.sides], refs[-1]
    n0, n1, n2 = sizes.rows[:3]
    for at, array in enumerate((conduct, binding)):
        own0[at] = jnp.swapaxes(array[...], 0, 1)
    for at in (0, 1):
        for row in range(n1):
            sums[at * n1 + row] = own0[at, 2 * row] + own0[at, 2 * row + 1]
    narrow(sizes, place, 0, sums, own1, 2 * n1, "own")
    for row in range(2 * n2):
        sums[row, :, : sizes.own[1] * LANES] = own1[2 * row] + own1[2 * row + 1]
    narrow(sizes, place, 1, sums, own2, 2 * n2, "own")
    ends = []
    for low, at1, at0 in ((n1 - 2, n1 - 1, n0 - 1), (0, 0, 0)):
        near, far = (n2 - 1, n2 - 2) if at0 else (0, 1)
        rows = (own0[0, at0], own1[low], own1[low + 1], own1[n1 + at1], own2[far], own2[n2 + near])
        ends.append(rows)
    for slot, next_row, prev_row in zip(sizes.slots, *ends):
        put_pair(place, (first, second), slot, next_row, prev_row)
    for at in (0, 1):
        cut_edges(sizes, place, own0.at[at], edges[at * sizes.sides : (at + 1) * sizes.sides])


def cut_edges(sizes, place, array, edges):
    last = sizes.extent_y - BORDER
    if sizes.sides == 1:
        at = pl.multiple_of(jnp.where(place[1] == 0, last, 0), LANES)
        edges[0][...] = array[:, :, pl.ds(at, BORDER)]
    elif sizes.sides == 2:
        edges[0][...] = array[:, :, last:]
        edges[1][...] = array[:, :, :BORDER]


def turn_kernel(sizes, place, right_side, turned, *edges):
    turned[...] = jnp.swapaxes(right_side[...], 0, 1)
    cut_edges(sizes, place, turned, edges)


def message_row(sizes, place, level, slot, message, beside):
    start, tiles = slot
    row = get(message, slot)
    if sizes.sides == 1:
        left = place[1] != 0
        tile = beside[0][start + jnp.where(left, tiles - 1, 0)]
        if level > 0:
            reach = BORDER >> level
            lane = lane_at(tile.shape)
            first = jnp.where(left, LANES - reach, 0)
            tile = jnp.where((lane >= first) & (lane < first + reach), tile, 0.0)
        row.append(tile)
    elif sizes.sides == 2:
        right, left = beside[0][start], beside[1][start + tiles - 1]
        if level == 0:
            row += [right, left]
        else:
            reach = BORDER >> level
            lane = lane_at(right.shape)
            row.append(jnp.where(lane < reach, right, jnp.where(lane >= LANES - reach, left, 0.0)))
    return jnp.concatenate(row, axis=1)


def fringe_lanes(shape):
    lane = lane_at(shape)
    return (lane < FRINGE) | (lane >= LANES - FRINGE)


def fringes(sizes, rows):
    total = None
    for index, (level, row) in enumerate(rows):
        border = row[:, sizes.own[level] * LANES :]
        tile = border[:, :LANES]
        lane = lane_at(tile.shape)
        if border.shape[1] > LANES:
            tile = jnp.where(lane < FRINGE, tile, border[:, LANES:])
        tile = jnp.where((lane < FRINGE) | (lane >= LANES - FRINGE), tile, 0.0)
        tile = roll(tile, SPREAD * index + SPREAD // 2, 1)
        total = tile if total is None else total + tile
    return total


def fringed_row(sizes, level, index, message):
    row = get(message, sizes.up_slots[index])
    if sizes.border[level]:
        tile = roll(message[sizes.up_tiles], -(SPREAD * index + SPREAD // 2), 1)
        lane = lane_at(tile.shape)
        right, left = jnp.where(lane < FRINGE, tile, 0.0), jnp.where(lane >= LANES - FRINGE, tile, 0.0)
        row += [right, left] if sizes.border[level] == 2 else [right + left]
    return jnp.concatenate(row, axis=1)


def packing(count):
    return -(-count // 2)


def pack_rows(rows, target):
    half = LANES // 2
    lane = lane_at(rows[0].shape)
    for index in range(packing(len(rows))):
        held = jnp.where(lane < half, rows[2 * index], 0.0)
        if 2 * index + 1 < len(rows):
            held = jnp.where(lane < half, held, pltpu.roll(rows[2 * index + 1], half, axis=1))
        target[index] = held


def unpack_rows(sizes, place, tiles, count, others=()):
    half, reach = LANES // 2, BORDER >> 3
    lane = lane_at(tiles.shape[1:])
    rows = []
    for index in range(count):
        held = tiles[index // 2]
        row = jnp.where(lane < half, pltpu.roll(held, half, axis=1) if index % 2 else held, 0.0)
        for side, other in enumerate(others):
            first = LANES - reach if side else half
            if sizes.sides == 1:
                first = jnp.where(place[1] == 0, half, LANES - reach)
            beside = other[index // 2]
            beside = beside if index % 2 else pltpu.roll(beside, half, axis=1)
            row = jnp.where((lane >= first) & (lane < first + reach), beside, row)
        rows.append(row)
    return rows


def merge_into(sizes, place, stride, radix, arrays, source, conduct, binding, first, others=()):
    position = (place[0] // stride) % radix
    source[...] = jnp.zeros(source.shape, f32)
    for step, array in enumerate(arrays):
        at = (position ^ step) * stride
        rows = unpack_rows(sizes, place, array, 3 * stride + 2, [other[step] for other in others])
        for index, row in enumerate(rows[: stride + 2]):
            source[at + index] = source[at + index] + row
        for index in range(stride):
            conduct[at + index + first] = rows[stride + 2 + index]
            binding[at + index] = rows[2 * stride + 2 + index]


def merge_kernel(sizes, stride, radix, place, *refs):
    arrays, out, (source, conduct, binding) = refs[:radix], refs[radix], refs[radix + 1 :]
    merge_into(sizes, place, stride, radix, arrays, source, conduct, binding, 0)
    count = stride * radix
    rows = [source[row] for row in range(count + 2)]
    rows += [conduct[row] for row in range(count)] + [binding[row] for row in range(count)]
    pack_rows(rows, out)


def held_rows(sizes, owns, borders):
    def held_row(level, at, row):
        if level > 0:
            row = at * sizes.rows[level] + row
            return jnp.concatenate([owns[level][row], *(array[row] for array in borders[level])], axis=1)
        own = owns[3][row] if at == 2 else owns[0][at, row]
        sides = len(borders[0]) // 3
        return jnp.concatenate([own, *(array[row] for array in borders[0][at * sides : (at + 1) * sides])], axis=1)

    return held_row


def inner_kernel(sizes, place, *refs):
    s = sizes.sides
    owns, borders0, refs = refs[:4], refs[4 : 4 + 3 * s], refs[4 + 3 * s :]
    border1, border2, inner0, inner1, inner2, sums = refs
    n0, n1, n2 = sizes.rows[:3]
    if s:
        for row in range(2 * n1):
            for side in range(s):
                columns = slice(side * LANES, (side + 1) * LANES)
                at, low = row // n1, 2 * (row % n1)
                sums[row, :, columns] = borders0[at * s + side][low] + borders0[at * s + side][low + 1]
        narrow(sizes, place, 0, sums, border1, 2 * n1, "border", sizes.own[0] * LANES)
        for row in range(2 * n2):
            sums[row, :, :LANES] = border1[2 * row] + border1[2 * row + 1]
        narrow(sizes, place, 1, sums, border2, 2 * n2, "border", sizes.own[1] * LANES)
    held_row = held_rows(sizes, owns, [borders0, [border1][:s], [border2][:s]])
    levels = [Level(sizes, level, inner, None) for level, inner in enumerate((inner0, inner1, inner2))]
    for index, level in enumerate(levels):
        conduct = lambda row, index=index, level=level: held_row(index, 0, row - level.halo)
        bound = lambda row, index=index, level=level: held_row(index, 1, row - level.halo)
        coefficients(
            sizes, place, index, conduct, bound, level.fx, level.fy, level.fz, level.weight, level.inner()
        )
        if index == 0:
            right = lambda row: held_row(0, 2, row - 1)
            for row in range(2, n0):
                level.smooth[row - 1] = level.weight[row - 1] * right(row)
            add = in_pairs(sums, lambda row: ((row - 3) // 2, row % 2 == 1))
            field = lambda row, level=level: level.smooth[row - 1]
            emit = lambda row, value: add(row, right(row) - value)
            sweep(3, n0 - 2, field, bound, level.fx, level.fy, level.fz, emit)
        if index == 1:
            narrow(sizes, place, 0, sums, level.source.inner, n1 - 2)
            for row in range(2, n1):
                level.smooth[row] = level.weight[row] * level.source[row]


def down_kernel(sizes, place, *refs):
    s = sizes.sides
    owns, borders0, refs = refs[:4], refs[4 : 4 + 3 * s], refs[4 + 3 * s :]
    pairs_of = [refs[2 * index : 2 * index + 2] for index in range(1 + s)]
    refs = refs[2 * (1 + s) :]
    from_prev, *beside_prev = (Arrived(place, pair, 0) for pair in pairs_of)
    from_next, *beside_next = (Arrived(place, pair, 1) for pair in pairs_of)
    (border1, border2), inners, refs = refs[:2], refs[2:5], refs[5:]
    outers, contribution, with_far, ups, far, refs = refs[:3], refs[3], refs[4], refs[5:7], refs[7], refs[8:]
    level3, near, sums = refs
    slots = sizes.slots
    n0, n1, n2 = sizes.rows[:3]
    levels = [Level(sizes, index, inner, outer) for index, (inner, outer) in enumerate(zip(inners, outers))]
    held_row = held_rows(sizes, owns, [borders0, [border1][:s], [border2][:s]])

    def prev_row(level, index):
        return message_row(sizes, place, level, slots[index], from_prev, beside_prev)

    def next_row(level, index):
        return message_row(sizes, place, level, slots[index], from_next, beside_next)

    def conduct0(row):
        if row == 0:
            return prev_row(0, 0)
        if row == n0 + 1:
            return next_row(0, 0)
        return held_row(0, 0, row - 1)

    for at, row_of in enumerate((prev_row, next_row)):
        sums[at, :, : sizes.held[1]] = row_of(1, 1) + row_of(1, 2)
    narrow(sizes, place, 1, sums.at[:, :, : sizes.held[1]], near, 2)
    zero = jnp.zeros((sizes.depth, sizes.held[0]), f32)
    level = levels[0]
    bound0 = lambda row: held_row(0, 1, row - 1)
    right = lambda row: held_row(0, 2, row - 1)
    coefficients(
        sizes, place, 0, conduct0, bound0, level.fx, level.fy, level.fz, level.weight, level.outer()
    )
    for row in (1, n0):
        level.smooth[row - 1] = level.weight[row - 1] * right(row)
    first_slot = lambda row: (row + 1) // 2
    add = in_pairs(
        sums,
        lambda row: (first_slot(row) - (n1 - 2 if row > n0 // 2 else 0), row % 2 == 1 or row == 0),
    )
    field = lambda row, level=level: level.smooth[row - 1] if 0 < row < n0 + 1 else zero
    emit = lambda row, value: add(row, right(row) - value)
    add(0, level.fx[0] * field(1))
    sweep(1, 2, field, bound0, level.fx, level.fy, level.fz, emit)
    sweep(n0 - 1, n0, field, bound0, level.fx, level.fy, level.fz, emit)
    add(n0 + 1, level.fx[n0] * field(n0))
    fine_held = sizes.held[0]
    for index in (1, 2):
        level, n = levels[index], sizes.rows[index]
        held = sizes.held[index]
        narrow(
            sizes, place, index - 1, sums.at[:, :, :fine_held], level.source.outer, level.source.outer.shape[0]
        )
        binding = level.binding
        binding[0] = prev_row(index, 3 if index == 1 else 5)
        binding[n + 1] = next_row(index, 3 if index == 1 else 5)
        for row in range(n):
            binding[row + 1] = held_row(index, 1, row)

        def conduct(row, n=n, index=index):
            if 2 <= row < n + 2:
                return held_row(index, 0, row - 2)
            if index == 1:
                return prev_row(1, 1 + row) if row < 2 else next_row(1, row - n - 1)
            if row in (1, n + 2):
                return near[0 if row == 1 else 1]
            return (prev_row if row == 0 else next_row)(2, 4)

        bound = lambda row, binding=binding: binding[row - 1]
        coefficients(
            sizes, place, index, conduct, bound, level.fx, level.fy, level.fz, level.weight, level.outer()
        )
        for row in level.outer()[2] if index == 1 else range(1, n + 3):
            level.smooth[row - 1] = level.weight[row - 1] * level.source[row - 1]
        zero = jnp.zeros((sizes.depth, held), f32)
        field = lambda row, level=level, n=n, zero=zero: level.smooth[row - 1] if 0 < row < n + 3 else zero
        add = in_pairs(sums.at[:, :, :held], lambda row: (row // 2, row % 2 == 0))
        emit = lambda row, value, level=level, add=add: add(row, level.source[row - 1] - value)
        add(0, level.fx[0] * field(1))
        sweep(1, n + 2, field, bound, level.fx, level.fy, level.fz, emit)
        add(n + 3, level.fx[n + 2] * field(n + 2))
        fine_held = held
    narrow(sizes, place, 2, sums.at[:, :, : sizes.held[2]], level3, 3)
    for at in (0, 1):
        sums[at, :, : sizes.held[2]] = held_row(2, at, 0) + held_row(2, at, 1)
    narrow(sizes, place, 2, sums.at[:, :, : sizes.held[2]], level3.at[3:5], 2)
    tiles = packing(5)
    pack_rows([level3[row] for row in range(5)], contribution)
    with_far[0:tiles] = contribution[...]
    v0, s1, v1 = levels[0].smooth, levels[1].source, levels[1].smooth
    s2, v2 = levels[2].source, levels[2].smooth
    next_rows = (v0[n0 - 1], s1[n1], v1[n1 - 1], s2[n2], s2[n2 + 1], v2[n2 - 1])
    prev_rows = (v0[0], s1[1], v1[2], s2[1], s2[0], v2[2])
    for slot, next_row, prev_row in zip(sizes.up_slots, next_rows, prev_rows):
        put_pair(place, ups, slot, next_row, prev_row)
    if s:
        ends = [fringes(sizes, list(zip((0, 1, 1, 2, 2, 2), rows))) for rows in (next_rows, prev_rows)]
        put_pair(place, ups, (sizes.up_tiles, 1), *ends)
    far_tiles = sizes.held[2] // LANES
    put_pair(place, (with_far.at[tiles : tiles + far_tiles], far), (0, far_tiles), v2[n2 + 1], v2[0], 2)


def relax(count, field, refs_of, source, target):
    fx, fy, fz, weight, binding = refs_of

    def update(row, value):
        target(row, field(row) + weight[row - 1] * (source(row) - value))

    sweep(1, count - 2, field, binding, fx, fy, fz, update)


def store(array, first):
    def put_row(row, value):
        array[row - first] = value

    return put_row


def coarse_kernel(sizes, stride, radix, place, *refs):
    blocks, refs = refs[:radix], refs[radix:]
    others, refs = [refs[side * radix : (side + 1) * radix] for side in range(sizes.sides)], refs[sizes.sides * radix :]
    out, merged, sums, both, defects = refs[:5]
    coarse = [refs[5 + 9 * index : 14 + 9 * index] for index in range(3)]
    total = sizes.span_count
    merge_into(sizes, place, stride, radix, blocks, merged, coarse[0][4], coarse[0][5], 1, others)
    zero = jnp.zeros((sizes.depth, LANES), f32)
    for index in range(3):
        level = 3 + index
        fx, fy, fz, weight, conduct, binding, source, smooth, iterate = coarse[index]
        count, half = total >> index, total >> index + 1
        for array in (conduct, smooth, iterate):
            array[0] = zero
            array[count + 1] = zero
        if index < 2:
            conduct_next, binding_next = coarse[index + 1][4:6]
            for row in range(half):
                sums[row] = conduct[2 * row + 1] + conduct[2 * row + 2]
                sums[half + row] = binding[2 * row] + binding[2 * row + 1]
            narrow(sizes, place, level, sums, both, 2 * half)
            for row in range(half):
                conduct_next[row + 1], binding_next[row] = both[row], both[half + row]
        bound = lambda row, binding=binding: binding[row - 1]
        at_row = lambda row, conduct=conduct: conduct[row]
        every = (range(1, count + 2), range(1, count + 1), range(1, count + 1))
        coefficients(sizes, place, level, at_row, bound, fx, fy, fz, weight, every)
    for index in range(3):
        level = 3 + index
        fx, fy, fz, weight, conduct, binding, source, smooth, iterate = coarse[index]
        count = total >> index
        bound = lambda row, binding=binding: binding[row - 1]
        if index == 0:
            source = merged.at[1 : count + 1]
        for row in range(count):
            smooth[row + 1] = weight[row] * source[row]
        if index < 2:
            add = in_pairs(defects, lambda row: ((row - 1) // 2, row % 2 == 1))
            emit = lambda row, value, source=source, add=add: add(row, source[row - 1] - value)
            sweep(1, count, lambda row, smooth=smooth: smooth[row], bound, fx, fy, fz, emit)
            narrow(sizes, place, level, defects, coarse[index + 1][6], count // 2)

    fx, fy, fz, weight, conduct, binding, source, smooth, iterate = coarse[2]
    held, other = smooth, iterate
    for _ in range(COARSE_SWEEPS - 1):
        field = lambda row, held=held: held[row]
        mine = lambda row: source[row - 1]
        bound = lambda row: binding[row - 1]
        relax((total >> 2) + 2, field, (fx, fy, fz, weight, bound), mine, store(other, 0))
        held, other = other, held
    for index in (1, 0):
        fx, fy, fz, weight, conduct, binding, source, smooth, iterate = coarse[index]
        if index == 0:
            source = merged.at[1 : total + 1]
        count = total >> index
        widen(sizes, place, 3 + index, held.at[1 : count // 2 + 1], sums, count // 2)
        for row in range(count):
            smooth[row + 1] = smooth[row + 1] + sums[row // 2, :, :LANES]
        if index == 0:
            break
        field = lambda row, smooth=smooth: smooth[row]
        mine = lambda row, source=source: source[row - 1]
        bound = lambda row, binding=binding: binding[row - 1]
        relax(count + 2, field, (fx, fy, fz, weight, bound), mine, store(iterate, 0))
        held = iterate

    for at in range(3):
        row = jnp.clip(place[0] + at, 1, total)
        mine = smooth[row]
        lower, upper = fx[row - 1] * (mine - smooth[row - 1]), fx[row] * (smooth[row + 1] - mine)
        south = fy[row - 1] * (mine - roll(mine, 1, 1))
        below = fz[row - 1] * (mine - roll(mine, 1, 0))
        across = (south - roll(south, -1, 1)) + (below - roll(below, -1, 0))
        value = binding[row - 1] * mine + (lower - upper) + across
        value = mine + weight[row - 1] * (source[row - 1] - value)
        out[at] = jnp.where(row == place[0] + at, value, 0.0)


def up_kernel(sizes, place, coarse, *refs):
    s = sizes.sides
    pair, far_pair, inners, outers, owns = refs[:2], refs[2:4], refs[4:7], refs[7:10], refs[10:12]
    levels = [Level(sizes, index, inner, outer) for index, (inner, outer) in enumerate(zip(inners, outers))]
    from_prev, from_next = (Arrived(place, pair, forward) for forward in (0, 1))
    tiles = packing(5)
    far_pair = (far_pair[0].at[tiles : tiles + sizes.held[2] // LANES], far_pair[1])
    fars = [Arrived(place, far_pair, forward, 2) for forward in (0, 1)]
    borders0, out, refs = refs[12 : 12 + 3 * s], refs[12 + 3 * s], refs[13 + 3 * s :]
    total1, total2, result, edges0, edges1 = refs[:5]
    over2, over1, over0, lift2, lift1, lift0, it2, it1, it0, semaphores = refs[5:]
    slots = sizes.slots
    n0, n1, n2 = sizes.rows[:3]
    width = sizes.own[0] * LANES

    before, behind = fringed_row(sizes, 0, 0, from_prev), fringed_row(sizes, 0, 0, from_next)
    lift0[0], lift0[n0 + 1] = before, behind
    edges0[0], edges0[1] = levels[0].fx[0] * before, levels[0].fx[n0] * behind
    narrow(sizes, place, 0, edges0, edges1, 2)

    widen(sizes, place, 2, coarse, over2, 3)
    for level, first, totals, over, lift, target, upper in (
        (2, 3, total2, over2, lift2, it2, over1),
        (1, 1, total1, over1, lift1, it1, over0),
    ):
        n, kept = sizes.rows[level], levels[level]
        fx, fy, fz, weight, binding = kept.fx, kept.fy, kept.fz, kept.weight, kept.binding
        own, smooth = kept.source, kept.smooth
        fringed = lambda index, message, level=level: fringed_row(sizes, level, index, message)
        if level == 1:
            smooth_at = first + 1
            edge = {2: own[1] + edges1[0], n + 1: own[n] + edges1[1]}
        else:
            smooth_at = first + 2
            edge = {2: own[1] + fringed(first + 1, from_prev)}
            edge[n + 1] = own[n] + fringed(first + 1, from_next)
        edge[1], edge[n + 2] = own[0] + fringed(first, from_prev), own[n + 1] + fringed(first, from_next)
        for row, value in edge.items():
            totals[row - 1] = value
        for row in range(n + 4):
            if row in (0, n + 3):
                value = fringed(smooth_at, from_next if row else from_prev)
                if level == 2:
                    far = fars[1 if row else 0]
                    value = value + jnp.concatenate(get(far, (0, sizes.held[2] // LANES)), axis=1)
            elif row in edge:
                value = weight[row - 1] * totals[row - 1]
            else:
                value = smooth[row - 1]
            lift[row] = value + over[row // 2]
        field = lambda row, lift=lift: lift[row]
        mine = lambda row, own=own, totals=totals, edge=edge: (totals if row in edge else own)[row - 1]
        bound = lambda row, binding=binding: binding[row - 1]
        relax(n + 4, field, (fx, fy, fz, weight, bound), mine, store(target, 1))
        widen(sizes, place, level - 1, target, upper, n + 2)

    fx, fy, fz, weight, v0 = levels[0].fx, levels[0].fy, levels[0].fz, levels[0].weight, levels[0].smooth
    lift0[0] = lift0[0] + over0[0]
    lift0[n0 + 1] = lift0[n0 + 1] + over0[n1 + 1]
    for row in range(1, n0 + 1):
        lift0[row] = v0[row - 1] + over0[(row + 1) // 2]
    field = lambda row: lift0[row]

    def relax_own(row, value):
        it0[row - 1] = lift0[row, :, :width] + weight[row - 1][:, :width] * (owns[1][row - 1] - value)

    sweep(1, n0, field, lambda row: owns[0][1, row - 1], fx, fy, fz, relax_own, width)
    step = sizes.depth // CHUNKS
    copies = []
    for chunk in range(CHUNKS):
        part = slice(chunk * step, (chunk + 1) * step)
        result[part] = jnp.swapaxes(it0[:, part, :width], 0, 1)
        copies.append(pltpu.make_async_copy(result.at[part], out.at[part], semaphores.at[chunk]))
        copies[-1].start()
    for copy in copies:
        copy.wait()


def call(body, name, micros, outputs, scratch, place, inputs, copies=0, far_out=False):
    near, far = pl.BlockSpec(memory_space=pltpu.VMEM), pl.BlockSpec(memory_space=pl.ANY)
    scratch = [pltpu.VMEM(shape, f32) for shape in scratch]
    if copies:
        scratch.append(pltpu.SemaphoreType.DMA((copies,)))
    return pl.pallas_call(
        body,
        name=name,
        out_shape=[jax.ShapeDtypeStruct(shape, f32) for shape in outputs],
        in_specs=[pl.BlockSpec(memory_space=pltpu.SMEM)] + [near] * len(inputs),
        out_specs=[far if far_out else near] * len(outputs),
        scratch_shapes=scratch,
        cost_estimate=pl.CostEstimate(flops=int(micros * 1.15e9), bytes_accessed=int(micros * BYTES_A_MICRO), transcendentals=0),
        compiler_params=pltpu.CompilerParams(vmem_limit_bytes=VMEM_LIMIT),
    )(place, *inputs)


def along(value, axis, steps):
    count = lax.axis_size(axis)
    initial, last = max(0, -steps), min(count, count - steps)
    return lax.ppermute(value, axis, [(source, source + steps) for source in range(initial, last)])


def beside(values, sizes):
    if sizes.sides == 1:
        return [[lax.ppermute(value, "width", [(0, 1), (1, 0)]) for value in values]]
    if sizes.sides == 2:
        return [[along(value, "width", steps) for value in values] for steps in (-1, 1)]
    return []


def edge_columns(edges, sizes):
    if sizes.sides == 1:
        return [lax.ppermute(edges[0], "width", [(0, 1), (1, 0)])]
    if sizes.sides == 2:
        return [along(edges[1], "width", -1), along(edges[0], "width", 1)]
    return []


def stages(count):
    stride = 1
    while stride < count:
        radix = 4 if count // stride % 4 == 0 else 2
        yield stride, radix
        stride *= radix


def swap(value, stride, radix, others=None):
    count = lax.axis_size("span")
    others = others or {}
    return [value] + [
        lax.ppermute(others.get(step, value), "span", [(device, device ^ step * stride) for device in range(count)])
        for step in range(1, radix)
    ]


def exchange(pair, stride):
    count = lax.axis_size("span")
    routes = [[], []]
    for low in range(count - stride):
        routes[low // stride % 2] += [(low, low + stride), (low + stride, low)]
    return [None if value is None else lax.ppermute(value, "span", route) for value, route in zip(pair, routes)]


def on_device(right_side, diffusivity, reaction):
    depth, extent_x, extent_y = diffusivity.shape
    sizes = Sizes(depth, extent_x, extent_y, lax.axis_size("span"), lax.axis_size("width"))
    place = jnp.stack([lax.axis_index("span"), lax.axis_index("width")]).astype(jnp.int32)
    n0, n1, n2, n3 = sizes.rows
    s = sizes.sides
    tile = (depth, LANES)
    own = [(depth, count * LANES) for count in sizes.own]
    held = [(depth, count) for count in sizes.held]
    down_message = (sizes.tiles, *tile)
    up_message = (sizes.up_tiles + 1, *tile)
    own0, own1, own2, first, second, *edges = call(
        functools.partial(start_kernel, sizes),
        "start",
        1.1,
        [(2, n0, *own[0]), (2 * n1, *own[1]), (2 * n2, *own[2]), down_message, down_message]
        + [(n0, depth, BORDER)] * 2 * s,
        [(2 * n1, *own[0])],
        place,
        [diffusivity, reaction],
    )
    borders = edge_columns(edges[:s], sizes) + edge_columns(edges[s:], sizes)
    halos = exchange([first, second], 1)
    turned, *edges = call(
        functools.partial(turn_kernel, sizes),
        "turn",
        0.7,
        [(n0, *own[0])] + [(n0, depth, BORDER)] * s,
        [],
        place,
        [right_side],
    )
    borders += edge_columns(edges, sizes)
    plan = list(stages(sizes.span_count))

    part = packing(5)
    far = (sizes.held[2] // LANES, *tile)
    inners = [(sum(inner_rows(sizes, level)), *held[level]) for level in range(3)]
    outers = [(sum(outer_rows(sizes, level)), *held[level]) for level in range(3)]
    inner = call(
        functools.partial(inner_kernel, sizes),
        "inner",
        0.5,
        [(2 * n1, *tile), (2 * n2, *tile), *inners],
        [(2 * n1, *held[0])],
        place,
        [own0, own1, own2, turned, *borders],
    )
    early, inner = lax.optimization_barrier((halos[0], inner))
    first_sides = beside([early], sizes)
    second, first_sides = lax.optimization_barrier((halos[1], first_sides))
    halos = [early, second]
    sides = [one + two for one, two in zip(first_sides, beside([second], sizes))]
    downs = call(
        functools.partial(down_kernel, sizes),
        "down",
        2.5,
        [*outers, (part, *tile), (part + far[0], *tile), up_message, up_message, far],
        [(5, *tile), (2, *held[2]), (n1 + 2, *held[0])],
        place,
        [own0, own1, own2, turned, *borders, *halos, *sum(sides, []), *inner],
    )
    outer, blocks, with_far, ups, far_second = downs[:3], downs[3], downs[4], list(downs[5:7]), downs[7]
    far_rows = None
    for stride, radix in plan[:-1]:
        count = stride * radix
        if far_rows is None:
            blocks = swap(blocks, stride, radix, {2: with_far})
            far_rows = [blocks[2], exchange([None, far_second], 2)[1]]
        else:
            blocks = swap(blocks, stride, radix)
        (blocks,) = call(
            functools.partial(merge_kernel, sizes, stride, radix),
            "merge",
            0.9,
            [(packing(3 * count + 2), *tile)],
            [(count + 2, *tile), (count, *tile), (count, *tile)],
            place,
            blocks,
        )
    stride, radix = plan[-1]
    blocks = swap(blocks, stride, radix)
    received = lax.optimization_barrier([exchange([ups[0], None], 1)[0], ups[1]])
    received = [received[0], exchange([None, received[1]], 1)[1]] + far_rows
    scratch = [(sizes.span_count + 2, *tile)] + [(sizes.span_count, *tile)] * 3
    for index in range(3):
        count = sizes.span_count >> index
        scratch += [(count + 1, *tile)] + [(count, *tile)] * 3 + [(count + 2, *tile)] + [(count, *tile)] * 2
        scratch += [(count + 2, *tile)] * 2
    blocks, received[3] = lax.optimization_barrier((blocks, received[3]))
    (coarse,) = call(
        functools.partial(coarse_kernel, sizes, stride, radix),
        "coarse",
        0.7,
        [(n3 + 2, *tile)],
        scratch,
        place,
        [*blocks, *sum(beside(blocks, sizes), [])],
    )
    scratch = [(n1 + 2, *held[1]), (n2 + 2, *held[2]), diffusivity.shape, (2, *held[0]), (2, *held[1])]
    scratch += [(n3 + 2, *held[2]), (n2 + 2, *held[1]), (n1 + 2, *held[0])]
    scratch += [(n2 + 4, *held[2]), (n1 + 4, *held[1]), (n0 + 2, *held[0])]
    scratch += [(n2 + 2, *held[2]), (n1 + 2, *held[1]), (n0, *own[0])]
    (correction,) = call(
        functools.partial(up_kernel, sizes),
        "up",
        3.0,
        [diffusivity.shape],
        scratch,
        place,
        [coarse, *received, *inner[2:], *outer, own0, turned, *borders],
        copies=CHUNKS,
        far_out=True,
    )
    return correction


def solution(mesh):
    in_specs = (P(None, "span", "width"),) * 3
    return jax.shard_map(
        on_device, mesh=mesh, in_specs=in_specs, out_specs=P(None, "span", "width"), check_vma=False
    )
```

```python
import functools

import jax
import jax.numpy as jnp
from jax import lax
from jax.experimental import pallas as pl
from jax.experimental.pallas import tpu as pltpu
from jax.sharding import PartitionSpec as P

LEVELS = 6
COARSE_SWEEPS = 3
LANES = 128
BORDER = 128
FRINGE = 4
SPREAD = 16
relax_weight = 0.8
f32 = jnp.float32
VMEM_LIMIT = 32 * 1024 * 1024
BYTES_A_MICRO = 3.69e6
CHUNKS = 4


class Sizes:
    def __init__(self, depth, extent_x, extent_y, span_count, width_count):
        self.depth, self.extent_x, self.extent_y = depth, extent_x, extent_y
        self.span_count, self.width_count = span_count, width_count
        self.sides = min(width_count - 1, 2)
        self.own = [(extent_y >> level) // LANES for level in range(3)]
        self.border = [self.sides, min(self.sides, 1), min(self.sides, 1)]
        self.held = [(self.own[level] + self.border[level]) * LANES for level in range(3)] + [LANES] * 3
        self.rows = [extent_x >> level for level in range(4)]
        self.slots = []
        start = 0
        for level in (0, 1, 1, 1, 2, 2):
            self.slots.append((start, self.own[level]))
            start += self.own[level]
        self.tiles = start
        self.up_slots = []
        start = 0
        for level in (0, 1, 1, 2, 2, 2):
            self.up_slots.append((start, self.own[level]))
            start += self.own[level]
        self.up_tiles = start


def put(message, slot, row):
    start, tiles = slot
    for tile in range(tiles):
        message[start + tile] = row[:, tile * LANES : (tile + 1) * LANES]


class Arrived:
    def __init__(self, place, pair, forward, stride=1):
        self.even = place[0] // stride % 2 == 0
        self.first, self.second = (pair[0], pair[1]) if forward else (pair[1], pair[0])

    def __getitem__(self, index):
        return jnp.where(self.even, self.first[index], self.second[index])


def put_pair(place, pair, slot, next_row, prev_row, stride=1):
    even = place[0] // stride % 2 == 0
    put(pair[0], slot, jnp.where(even, next_row, prev_row))
    put(pair[1], slot, jnp.where(even, prev_row, next_row))


def get(message, slot):
    start, tiles = slot
    return [message[start + tile] for tile in range(tiles)]


def lane_at(shape):
    return lax.broadcasted_iota(jnp.int32, shape, len(shape) - 1)


def roll(value, steps, axis):
    return pltpu.roll(value, steps % value.shape[axis], axis=axis)


def reciprocal(value):
    return pltpu.reciprocal(value, approx=True)


def harmonic(first, second, guard):
    total = first + second
    if guard:
        total = jnp.maximum(total, 1e-3)
    return (2.0 * first) * second * reciprocal(total)


def split(value):
    high = value.astype(jnp.bfloat16)
    return high, (value - high.astype(f32)).astype(jnp.bfloat16)


def dot(halves, table):
    high, low = halves
    return jnp.dot(high, table, preferred_element_type=f32) + jnp.dot(low, table, preferred_element_type=f32)


def pair_table(fine, fine_dim, turn, weight):
    shape = (fine, LANES) if fine_dim == 0 else (LANES, fine)
    fine_at = lax.broadcasted_iota(jnp.int32, shape, fine_dim)
    coarse_at = lax.broadcasted_iota(jnp.int32, shape, 1 - fine_dim)
    if turn is not None:
        coarse_at = coarse_at - jnp.where(fine_at >= turn, LANES // 2, 0)
    return jnp.where(fine_at // 2 == coarse_at, weight, 0.0).astype(jnp.bfloat16)


def turns(sizes, place, level):
    if sizes.sides == 0:
        return []
    if level == 0:
        return [jnp.where(place[1] == 0, LANES, 0)] if sizes.sides == 1 else [LANES, 0]
    return [LANES // 2]


def transfer_plan(sizes, place, level, part):
    plan = []
    if level >= 3:
        return [((0, LANES), 0, 3 * LANES // 4)]
    if level == 2:
        return [((0, sizes.held[2]), 0, None)]
    own = sizes.own[level]
    if part != "border":
        plan += [((2 * LANES * tile, 2 * LANES * (tile + 1)), tile, None) for tile in range(own // 2)]
    if part != "own":
        for index, turn in enumerate(turns(sizes, place, level)):
            start = (own + index) * LANES
            plan.append(((start, start + LANES), own // 2, turn))
    return plan


def narrow(sizes, place, level, sums, target, rows, part="all", shift=0):
    depth = sums.shape[1]
    done = {}
    for (start, stop), tile, turn in transfer_plan(sizes, place, level, part):
        start, stop, tile = start - shift, stop - shift, tile - shift // (2 * LANES)
        columns = split(sums[0:rows, :, start:stop].reshape(rows * depth, stop - start))
        result = dot(columns, pair_table(stop - start, 0, turn, 0.25)).reshape(rows, depth, LANES)
        done[tile] = done[tile] + result if tile in done else result
    for tile, result in done.items():
        target[0:rows, :, tile * LANES : (tile + 1) * LANES] = result


def widen(sizes, place, level, coarse, target, rows):
    depth = coarse.shape[1]
    for (start, stop), tile, turn in transfer_plan(sizes, place, level, "all"):
        columns = split(coarse[0:rows, :, tile * LANES : (tile + 1) * LANES].reshape(rows * depth, LANES))
        result = dot(columns, pair_table(stop - start, 1, turn, 4.0))
        target[0:rows, :, start:stop] = result.reshape(rows, depth, stop - start)


class Joined:
    def __init__(self, inner, outer, first):
        self.inner, self.outer, self.first = inner, outer, first

    def find(self, row):
        place, count = row - self.first, 0 if self.inner is None else self.inner.shape[0]
        if 0 <= place < count:
            return self.inner, place
        return self.outer, row if place < 0 else row - count

    def __getitem__(self, row):
        array, place = self.find(row)
        return array[place]

    def __setitem__(self, row, value):
        array, place = self.find(row)
        array[place] = value


class Level:
    def __init__(self, sizes, level, inner, outer):
        self.n, self.halo = sizes.rows[level], 1 if level == 0 else 2
        counts = inner_rows(sizes, level)
        fx, fy, fz, *rest = parts(inner, counts)
        weight, source, smooth = (None, None, None) if level == 2 else (rest[0], None, rest[1])
        if level == 1:
            weight, source, smooth = rest
        others = [None] * 7 if outer is None else parts(outer, outer_rows(sizes, level))
        if level == 0 and outer is not None:
            others = [others[0], None, None, others[1], None, others[2], None]
        h = self.halo
        self.fx = Joined(fx, others[0], h)
        self.fy, self.fz = Joined(fy, others[1], h - 1), Joined(fz, others[2], h - 1)
        self.weight, self.source, self.smooth = (
            Joined(array, other, h) for array, other in zip((weight, source, smooth), others[3:6])
        )
        self.binding = others[6]

    def inner(self):
        first, last = self.halo, self.halo + self.n - 1
        return range(first + 1, last + 1), range(first, last + 1), range(first + 1, last)

    def outer(self):
        count = self.n + 2 * self.halo
        every = (range(1, count), range(1, count - 1), range(1, count - 1))
        return tuple([row for row in rows if row not in mine] for rows, mine in zip(every, self.inner()))


def inner_rows(sizes, level):
    n = sizes.rows[level]
    return [n - 1, n, n] + [[n - 2] * 2, [n - 2] * 3, []][level]


def outer_rows(sizes, level):
    n = sizes.rows[level]
    return [[2, 2, 2], [4, 2, 2, 4, 4, 4, n + 2], [4, 2, 2] + [n + 2] * 4][level]


def coefficients(sizes, place, level, conduct, binding, fx, fy, fz, weight, rows):
    guard = level > 0 or sizes.sides > 1
    for row in rows[0]:
        fx[row - 1] = harmonic(conduct(row - 1), conduct(row), guard)
    for row in rows[1]:
        mine = conduct(row)
        south = harmonic(mine, roll(mine, 1, 1), guard)
        if level == 0 and sizes.sides < 2:
            cut = 0 if sizes.sides == 0 else jnp.where(place[1] == 0, 0, sizes.extent_y)
            south = jnp.where(lane_at(mine.shape) == cut, 0.0, south)
        below = harmonic(mine, roll(mine, 1, 0), guard)
        fy[row - 1] = south
        fz[row - 1] = jnp.where(lax.broadcasted_iota(jnp.int32, mine.shape, 0) == 0, 0.0, below)
    for row in rows[2]:
        south, below = fy[row - 1], fz[row - 1]
        diagonal = fx[row - 1] + fx[row] + binding(row)
        diagonal = diagonal + (south + roll(south, -1, 1)) + (below + roll(below, -1, 0))
        if guard:
            diagonal = jnp.maximum(diagonal, 1e-6)
        weight[row - 1] = relax_weight * reciprocal(diagonal)


def sweep(first, last, field, binding, fx, fy, fz, emit, width=None):
    cut = lambda value: value if width is None else value[:, :width]
    lower = cut(fx[first - 1]) * (cut(field(first)) - cut(field(first - 1)))
    for row in range(first, last + 1):
        mine = field(row)
        south = fy[row - 1] * (mine - roll(mine, 1, 1))
        across = cut(south - roll(south, -1, 1))
        mine = cut(mine)
        upper = cut(fx[row]) * (cut(field(row + 1)) - mine)
        below = cut(fz[row - 1]) * (mine - roll(mine, 1, 0))
        across = across + (below - roll(below, -1, 0))
        emit(row, binding(row) * mine + (lower - upper) + across)
        lower = upper


def in_pairs(sums, slot_of):
    def add(row, value):
        slot, first = slot_of(row)
        if first:
            sums[slot] = value
        else:
            sums[slot] = sums[slot] + value

    return add


def parts(array, counts):
    views, start = [], 0
    for count in counts:
        views.append(array.at[start : start + count])
        start += count
    return views


def start_kernel(sizes, place, conduct, binding, own0, own1, own2, first, second, *refs):
    edges, sums = refs[: 2 * sizes.sides], refs[-1]
    n0, n1, n2 = sizes.rows[:3]
    for at, array in enumerate((conduct, binding)):
        own0[at] = jnp.swapaxes(array[...], 0, 1)
    for at in (0, 1):
        for row in range(n1):
            sums[at * n1 + row] = own0[at, 2 * row] + own0[at, 2 * row + 1]
    narrow(sizes, place, 0, sums, own1, 2 * n1, "own")
    for row in range(2 * n2):
        sums[row, :, : sizes.own[1] * LANES] = own1[2 * row] + own1[2 * row + 1]
    narrow(sizes, place, 1, sums, own2, 2 * n2, "own")
    ends = []
    for low, at1, at0 in ((n1 - 2, n1 - 1, n0 - 1), (0, 0, 0)):
        near, far = (n2 - 1, n2 - 2) if at0 else (0, 1)
        rows = (own0[0, at0], own1[low], own1[low + 1], own1[n1 + at1], own2[far], own2[n2 + near])
        ends.append(rows)
    for slot, next_row, prev_row in zip(sizes.slots, *ends):
        put_pair(place, (first, second), slot, next_row, prev_row)
    for at in (0, 1):
        cut_edges(sizes, place, own0.at[at], edges[at * sizes.sides : (at + 1) * sizes.sides])


def cut_edges(sizes, place, array, edges):
    last = sizes.extent_y - BORDER
    if sizes.sides == 1:
        at = pl.multiple_of(jnp.where(place[1] == 0, last, 0), LANES)
        edges[0][...] = array[:, :, pl.ds(at, BORDER)]
    elif sizes.sides == 2:
        edges[0][...] = array[:, :, last:]
        edges[1][...] = array[:, :, :BORDER]


def turn_kernel(sizes, place, right_side, turned, *edges):
    turned[...] = jnp.swapaxes(right_side[...], 0, 1)
    cut_edges(sizes, place, turned, edges)


def message_row(sizes, place, level, slot, message, beside):
    start, tiles = slot
    row = get(message, slot)
    if sizes.sides == 1:
        left = place[1] != 0
        tile = beside[0][start + jnp.where(left, tiles - 1, 0)]
        if level > 0:
            reach = BORDER >> level
            lane = lane_at(tile.shape)
            first = jnp.where(left, LANES - reach, 0)
            tile = jnp.where((lane >= first) & (lane < first + reach), tile, 0.0)
        row.append(tile)
    elif sizes.sides == 2:
        right, left = beside[0][start], beside[1][start + tiles - 1]
        if level == 0:
            row += [right, left]
        else:
            reach = BORDER >> level
            lane = lane_at(right.shape)
            row.append(jnp.where(lane < reach, right, jnp.where(lane >= LANES - reach, left, 0.0)))
    return jnp.concatenate(row, axis=1)


def fringe_lanes(shape):
    lane = lane_at(shape)
    return (lane < FRINGE) | (lane >= LANES - FRINGE)


def fringes(sizes, rows):
    total = None
    for index, (level, row) in enumerate(rows):
        border = row[:, sizes.own[level] * LANES :]
        tile = border[:, :LANES]
        lane = lane_at(tile.shape)
        if border.shape[1] > LANES:
            tile = jnp.where(lane < FRINGE, tile, border[:, LANES:])
        tile = jnp.where((lane < FRINGE) | (lane >= LANES - FRINGE), tile, 0.0)
        tile = roll(tile, SPREAD * index + SPREAD // 2, 1)
        total = tile if total is None else total + tile
    return total


def fringed_row(sizes, level, index, message):
    row = get(message, sizes.up_slots[index])
    if sizes.border[level]:
        tile = roll(message[sizes.up_tiles], -(SPREAD * index + SPREAD // 2), 1)
        lane = lane_at(tile.shape)
        right, left = jnp.where(lane < FRINGE, tile, 0.0), jnp.where(lane >= LANES - FRINGE, tile, 0.0)
        row += [right, left] if sizes.border[level] == 2 else [right + left]
    return jnp.concatenate(row, axis=1)


def packing(count):
    return -(-count // 2)


def pack_rows(rows, target):
    half = LANES // 2
    lane = lane_at(rows[0].shape)
    for index in range(packing(len(rows))):
        held = jnp.where(lane < half, rows[2 * index], 0.0)
        if 2 * index + 1 < len(rows):
            held = jnp.where(lane < half, held, pltpu.roll(rows[2 * index + 1], half, axis=1))
        target[index] = held


def unpack_rows(sizes, place, tiles, count, others=()):
    half, reach = LANES // 2, BORDER >> 3
    lane = lane_at(tiles.shape[1:])
    rows = []
    for index in range(count):
        held = tiles[index // 2]
        row = jnp.where(lane < half, pltpu.roll(held, half, axis=1) if index % 2 else held, 0.0)
        for side, other in enumerate(others):
            first = LANES - reach if side else half
            if sizes.sides == 1:
                first = jnp.where(place[1] == 0, half, LANES - reach)
            beside = other[index // 2]
            beside = beside if index % 2 else pltpu.roll(beside, half, axis=1)
            row = jnp.where((lane >= first) & (lane < first + reach), beside, row)
        rows.append(row)
    return rows


def merge_into(sizes, place, stride, radix, arrays, source, conduct, binding, first, others=()):
    position = (place[0] // stride) % radix
    source[...] = jnp.zeros(source.shape, f32)
    for step, array in enumerate(arrays):
        at = (position ^ step) * stride
        rows = unpack_rows(sizes, place, array, 3 * stride + 2, [other[step] for other in others])
        for index, row in enumerate(rows[: stride + 2]):
            source[at + index] = source[at + index] + row
        for index in range(stride):
            conduct[at + index + first] = rows[stride + 2 + index]
            binding[at + index] = rows[2 * stride + 2 + index]


def merge_kernel(sizes, stride, radix, place, *refs):
    arrays, out, (source, conduct, binding) = refs[:radix][::-1], refs[radix], refs[radix + 1 :]
    merge_into(sizes, place, stride, radix, arrays, source, conduct, binding, 0)
    count = stride * radix
    rows = [source[row] for row in range(count + 2)]
    rows += [conduct[row] for row in range(count)] + [binding[row] for row in range(count)]
    pack_rows(rows, out)


def held_rows(sizes, owns, borders):
    def held_row(level, at, row):
        if level > 0:
            row = at * sizes.rows[level] + row
            return jnp.concatenate([owns[level][row], *(array[row] for array in borders[level])], axis=1)
        own = owns[3][row] if at == 2 else owns[0][at, row]
        sides = len(borders[0]) // 3
        return jnp.concatenate([own, *(array[row] for array in borders[0][at * sides : (at + 1) * sides])], axis=1)

    return held_row


def inner_kernel(sizes, place, *refs):
    s = sizes.sides
    owns, borders0, refs = refs[:4], refs[4 : 4 + 3 * s], refs[4 + 3 * s :]
    border1, border2, inner0, inner1, inner2, sums = refs
    n0, n1, n2 = sizes.rows[:3]
    if s:
        for row in range(2 * n1):
            for side in range(s):
                columns = slice(side * LANES, (side + 1) * LANES)
                at, low = row // n1, 2 * (row % n1)
                sums[row, :, columns] = borders0[at * s + side][low] + borders0[at * s + side][low + 1]
        narrow(sizes, place, 0, sums, border1, 2 * n1, "border", sizes.own[0] * LANES)
        for row in range(2 * n2):
            sums[row, :, :LANES] = border1[2 * row] + border1[2 * row + 1]
        narrow(sizes, place, 1, sums, border2, 2 * n2, "border", sizes.own[1] * LANES)
    held_row = held_rows(sizes, owns, [borders0, [border1][:s], [border2][:s]])
    levels = [Level(sizes, level, inner, None) for level, inner in enumerate((inner0, inner1, inner2))]
    for index, level in enumerate(levels):
        conduct = lambda row, index=index, level=level: held_row(index, 0, row - level.halo)
        bound = lambda row, index=index, level=level: held_row(index, 1, row - level.halo)
        coefficients(
            sizes, place, index, conduct, bound, level.fx, level.fy, level.fz, level.weight, level.inner()
        )
        if index == 0:
            right = lambda row: held_row(0, 2, row - 1)
            for row in range(2, n0):
                level.smooth[row - 1] = level.weight[row - 1] * right(row)
            add = in_pairs(sums, lambda row: ((row - 3) // 2, row % 2 == 1))
            field = lambda row, level=level: level.smooth[row - 1]
            emit = lambda row, value: add(row, right(row) - value)
            sweep(3, n0 - 2, field, bound, level.fx, level.fy, level.fz, emit)
        if index == 1:
            narrow(sizes, place, 0, sums, level.source.inner, n1 - 2)
            for row in range(2, n1):
                level.smooth[row] = level.weight[row] * level.source[row]


def down_kernel(sizes, place, *refs):
    s = sizes.sides
    owns, borders0, refs = refs[:4], refs[4 : 4 + 3 * s], refs[4 + 3 * s :]
    pairs_of = [refs[2 * index : 2 * index + 2] for index in range(1 + s)]
    refs = refs[2 * (1 + s) :]
    from_prev, *beside_prev = (Arrived(place, pair, 0) for pair in pairs_of)
    from_next, *beside_next = (Arrived(place, pair, 1) for pair in pairs_of)
    (border1, border2), inners, refs = refs[:2], refs[2:5], refs[5:]
    outers, contribution, with_far, ups, far, refs = refs[:3], refs[3], refs[4], refs[5:7], refs[7], refs[8:]
    level3, near, sums = refs
    slots = sizes.slots
    n0, n1, n2 = sizes.rows[:3]
    levels = [Level(sizes, index, inner, outer) for index, (inner, outer) in enumerate(zip(inners, outers))]
    held_row = held_rows(sizes, owns, [borders0, [border1][:s], [border2][:s]])

    def prev_row(level, index):
        return message_row(sizes, place, level, slots[index], from_prev, beside_prev)

    def next_row(level, index):
        return message_row(sizes, place, level, slots[index], from_next, beside_next)

    def conduct0(row):
        if row == 0:
            return prev_row(0, 0)
        if row == n0 + 1:
            return next_row(0, 0)
        return held_row(0, 0, row - 1)

    for at, row_of in enumerate((prev_row, next_row)):
        sums[at, :, : sizes.held[1]] = row_of(1, 1) + row_of(1, 2)
    narrow(sizes, place, 1, sums.at[:, :, : sizes.held[1]], near, 2)
    zero = jnp.zeros((sizes.depth, sizes.held[0]), f32)
    level = levels[0]
    bound0 = lambda row: held_row(0, 1, row - 1)
    right = lambda row: held_row(0, 2, row - 1)
    coefficients(
        sizes, place, 0, conduct0, bound0, level.fx, level.fy, level.fz, level.weight, level.outer()
    )
    for row in (1, n0):
        level.smooth[row - 1] = level.weight[row - 1] * right(row)
    first_slot = lambda row: (row + 1) // 2
    add = in_pairs(
        sums,
        lambda row: (first_slot(row) - (n1 - 2 if row > n0 // 2 else 0), row % 2 == 1 or row == 0),
    )
    field = lambda row, level=level: level.smooth[row - 1] if 0 < row < n0 + 1 else zero
    emit = lambda row, value: add(row, right(row) - value)
    add(0, level.fx[0] * field(1))
    sweep(1, 2, field, bound0, level.fx, level.fy, level.fz, emit)
    sweep(n0 - 1, n0, field, bound0, level.fx, level.fy, level.fz, emit)
    add(n0 + 1, level.fx[n0] * field(n0))
    fine_held = sizes.held[0]
    for index in (1, 2):
        level, n = levels[index], sizes.rows[index]
        held = sizes.held[index]
        narrow(
            sizes, place, index - 1, sums.at[:, :, :fine_held], level.source.outer, level.source.outer.shape[0]
        )
        binding = level.binding
        binding[0] = prev_row(index, 3 if index == 1 else 5)
        binding[n + 1] = next_row(index, 3 if index == 1 else 5)
        for row in range(n):
            binding[row + 1] = held_row(index, 1, row)

        def conduct(row, n=n, index=index):
            if 2 <= row < n + 2:
                return held_row(index, 0, row - 2)
            if index == 1:
                return prev_row(1, 1 + row) if row < 2 else next_row(1, row - n - 1)
            if row in (1, n + 2):
                return near[0 if row == 1 else 1]
            return (prev_row if row == 0 else next_row)(2, 4)

        bound = lambda row, binding=binding: binding[row - 1]
        coefficients(
            sizes, place, index, conduct, bound, level.fx, level.fy, level.fz, level.weight, level.outer()
        )
        for row in level.outer()[2] if index == 1 else range(1, n + 3):
            level.smooth[row - 1] = level.weight[row - 1] * level.source[row - 1]
        zero = jnp.zeros((sizes.depth, held), f32)
        field = lambda row, level=level, n=n, zero=zero: level.smooth[row - 1] if 0 < row < n + 3 else zero
        add = in_pairs(sums.at[:, :, :held], lambda row: (row // 2, row % 2 == 0))
        emit = lambda row, value, level=level, add=add: add(row, level.source[row - 1] - value)
        add(0, level.fx[0] * field(1))
        sweep(1, n + 2, field, bound, level.fx, level.fy, level.fz, emit)
        add(n + 3, level.fx[n + 2] * field(n + 2))
        fine_held = held
    narrow(sizes, place, 2, sums.at[:, :, : sizes.held[2]], level3, 3)
    for at in (0, 1):
        sums[at, :, : sizes.held[2]] = held_row(2, at, 0) + held_row(2, at, 1)
    narrow(sizes, place, 2, sums.at[:, :, : sizes.held[2]], level3.at[3:5], 2)
    tiles = packing(5)
    pack_rows([level3[row] for row in range(5)], contribution)
    with_far[0:tiles] = contribution[...]
    v0, s1, v1 = levels[0].smooth, levels[1].source, levels[1].smooth
    s2, v2 = levels[2].source, levels[2].smooth
    next_rows = (v0[n0 - 1], s1[n1], v1[n1 - 1], s2[n2], s2[n2 + 1], v2[n2 - 1])
    prev_rows = (v0[0], s1[1], v1[2], s2[1], s2[0], v2[2])
    for slot, next_row, prev_row in zip(sizes.up_slots, next_rows, prev_rows):
        put_pair(place, ups, slot, next_row, prev_row)
    if s:
        ends = [fringes(sizes, list(zip((0, 1, 1, 2, 2, 2), rows))) for rows in (next_rows, prev_rows)]
        put_pair(place, ups, (sizes.up_tiles, 1), *ends)
    far_tiles = sizes.held[2] // LANES
    put_pair(place, (with_far.at[tiles : tiles + far_tiles], far), (0, far_tiles), v2[n2 + 1], v2[0], 2)


def relax(count, field, refs_of, source, target):
    fx, fy, fz, weight, binding = refs_of

    def update(row, value):
        target(row, field(row) + weight[row - 1] * (source(row) - value))

    sweep(1, count - 2, field, binding, fx, fy, fz, update)


def store(array, first):
    def put_row(row, value):
        array[row - first] = value

    return put_row


def coarse_kernel(sizes, stride, radix, place, *refs):
    blocks, refs = refs[:radix], refs[radix:]
    others, refs = [refs[side * radix : (side + 1) * radix] for side in range(sizes.sides)], refs[sizes.sides * radix :]
    out, merged, sums, both, defects = refs[:5]
    coarse = [refs[5 + 9 * index : 14 + 9 * index] for index in range(3)]
    total = sizes.span_count
    merge_into(sizes, place, stride, radix, blocks, merged, coarse[0][4], coarse[0][5], 1, others)
    zero = jnp.zeros((sizes.depth, LANES), f32)
    for index in range(3):
        level = 3 + index
        fx, fy, fz, weight, conduct, binding, source, smooth, iterate = coarse[index]
        count, half = total >> index, total >> index + 1
        for array in (conduct, smooth, iterate):
            array[0] = zero
            array[count + 1] = zero
        if index < 2:
            conduct_next, binding_next = coarse[index + 1][4:6]
            for row in range(half):
                sums[row] = conduct[2 * row + 1] + conduct[2 * row + 2]
                sums[half + row] = binding[2 * row] + binding[2 * row + 1]
            narrow(sizes, place, level, sums, both, 2 * half)
            for row in range(half):
                conduct_next[row + 1], binding_next[row] = both[row], both[half + row]
        bound = lambda row, binding=binding: binding[row - 1]
        at_row = lambda row, conduct=conduct: conduct[row]
        every = (range(1, count + 2), range(1, count + 1), range(1, count + 1))
        coefficients(sizes, place, level, at_row, bound, fx, fy, fz, weight, every)
    for index in range(3):
        level = 3 + index
        fx, fy, fz, weight, conduct, binding, source, smooth, iterate = coarse[index]
        count = total >> index
        bound = lambda row, binding=binding: binding[row - 1]
        if index == 0:
            source = merged.at[1 : count + 1]
        for row in range(count):
            smooth[row + 1] = weight[row] * source[row]
        if index < 2:
            add = in_pairs(defects, lambda row: ((row - 1) // 2, row % 2 == 1))
            emit = lambda row, value, source=source, add=add: add(row, source[row - 1] - value)
            sweep(1, count, lambda row, smooth=smooth: smooth[row], bound, fx, fy, fz, emit)
            narrow(sizes, place, level, defects, coarse[index + 1][6], count // 2)

    fx, fy, fz, weight, conduct, binding, source, smooth, iterate = coarse[2]
    held, other = smooth, iterate
    for _ in range(COARSE_SWEEPS - 1):
        field = lambda row, held=held: held[row]
        mine = lambda row: source[row - 1]
        bound = lambda row: binding[row - 1]
        relax((total >> 2) + 2, field, (fx, fy, fz, weight, bound), mine, store(other, 0))
        held, other = other, held
    for index in (1, 0):
        fx, fy, fz, weight, conduct, binding, source, smooth, iterate = coarse[index]
        if index == 0:
            source = merged.at[1 : total + 1]
        count = total >> index
        widen(sizes, place, 3 + index, held.at[1 : count // 2 + 1], sums, count // 2)
        for row in range(count):
            smooth[row + 1] = smooth[row + 1] + sums[row // 2, :, :LANES]
        if index == 0:
            break
        field = lambda row, smooth=smooth: smooth[row]
        mine = lambda row, source=source: source[row - 1]
        bound = lambda row, binding=binding: binding[row - 1]
        relax(count + 2, field, (fx, fy, fz, weight, bound), mine, store(iterate, 0))
        held = iterate

    for at in range(3):
        row = jnp.clip(place[0] + at, 1, total)
        mine = smooth[row]
        lower, upper = fx[row - 1] * (mine - smooth[row - 1]), fx[row] * (smooth[row + 1] - mine)
        south = fy[row - 1] * (mine - roll(mine, 1, 1))
        below = fz[row - 1] * (mine - roll(mine, 1, 0))
        across = (south - roll(south, -1, 1)) + (below - roll(below, -1, 0))
        value = binding[row - 1] * mine + (lower - upper) + across
        value = mine + weight[row - 1] * (source[row - 1] - value)
        out[at] = jnp.where(row == place[0] + at, value, 0.0)


def up_kernel(sizes, place, coarse, *refs):
    s = sizes.sides
    pair, far_pair, inners, outers, owns = refs[:2], refs[2:4], refs[4:7], refs[7:10], refs[10:12]
    levels = [Level(sizes, index, inner, outer) for index, (inner, outer) in enumerate(zip(inners, outers))]
    from_prev, from_next = (Arrived(place, pair, forward) for forward in (0, 1))
    tiles = packing(5)
    far_pair = (far_pair[0].at[tiles : tiles + sizes.held[2] // LANES], far_pair[1])
    fars = [Arrived(place, far_pair, forward, 2) for forward in (0, 1)]
    borders0, out, refs = refs[12 : 12 + 3 * s], refs[12 + 3 * s], refs[13 + 3 * s :]
    total1, total2, result, edges0, edges1 = refs[:5]
    over2, over1, over0, lift2, lift1, lift0, it2, it1, it0, semaphores = refs[5:]
    slots = sizes.slots
    n0, n1, n2 = sizes.rows[:3]
    width = sizes.own[0] * LANES

    before, behind = fringed_row(sizes, 0, 0, from_prev), fringed_row(sizes, 0, 0, from_next)
    lift0[0], lift0[n0 + 1] = before, behind
    edges0[0], edges0[1] = levels[0].fx[0] * before, levels[0].fx[n0] * behind
    narrow(sizes, place, 0, edges0, edges1, 2)

    widen(sizes, place, 2, coarse, over2, 3)
    for level, first, totals, over, lift, target, upper in (
        (2, 3, total2, over2, lift2, it2, over1),
        (1, 1, total1, over1, lift1, it1, over0),
    ):
        n, kept = sizes.rows[level], levels[level]
        fx, fy, fz, weight, binding = kept.fx, kept.fy, kept.fz, kept.weight, kept.binding
        own, smooth = kept.source, kept.smooth
        fringed = lambda index, message, level=level: fringed_row(sizes, level, index, message)
        if level == 1:
            smooth_at = first + 1
            edge = {2: own[1] + edges1[0], n + 1: own[n] + edges1[1]}
        else:
            smooth_at = first + 2
            edge = {2: own[1] + fringed(first + 1, from_prev)}
            edge[n + 1] = own[n] + fringed(first + 1, from_next)
        edge[1], edge[n + 2] = own[0] + fringed(first, from_prev), own[n + 1] + fringed(first, from_next)
        for row, value in edge.items():
            totals[row - 1] = value
        for row in range(n + 4):
            if row in (0, n + 3):
                value = fringed(smooth_at, from_next if row else from_prev)
                if level == 2:
                    far = fars[1 if row else 0]
                    value = value + jnp.concatenate(get(far, (0, sizes.held[2] // LANES)), axis=1)
            elif row in edge:
                value = weight[row - 1] * totals[row - 1]
            else:
                value = smooth[row - 1]
            lift[row] = value + over[row // 2]
        field = lambda row, lift=lift: lift[row]
        mine = lambda row, own=own, totals=totals, edge=edge: (totals if row in edge else own)[row - 1]
        bound = lambda row, binding=binding: binding[row - 1]
        relax(n + 4, field, (fx, fy, fz, weight, bound), mine, store(target, 1))
        widen(sizes, place, level - 1, target, upper, n + 2)

    fx, fy, fz, weight, v0 = levels[0].fx, levels[0].fy, levels[0].fz, levels[0].weight, levels[0].smooth
    lift0[0] = lift0[0] + over0[0]
    lift0[n0 + 1] = lift0[n0 + 1] + over0[n1 + 1]
    for row in range(1, n0 + 1):
        lift0[row] = v0[row - 1] + over0[(row + 1) // 2]
    field = lambda row: lift0[row]

    def relax_own(row, value):
        it0[row - 1] = lift0[row, :, :width] + weight[row - 1][:, :width] * (owns[1][row - 1] - value)

    sweep(1, n0, field, lambda row: owns[0][1, row - 1], fx, fy, fz, relax_own, width)
    step = sizes.depth // CHUNKS
    copies = []
    for chunk in range(CHUNKS):
        part = slice(chunk * step, (chunk + 1) * step)
        result[part] = jnp.swapaxes(it0[:, part, :width], 0, 1)
        copies.append(pltpu.make_async_copy(result.at[part], out.at[part], semaphores.at[chunk]))
        copies[-1].start()
    for copy in copies:
        copy.wait()


def call(body, name, micros, outputs, scratch, place, inputs, copies=0, far_out=False):
    near, far = pl.BlockSpec(memory_space=pltpu.VMEM), pl.BlockSpec(memory_space=pl.ANY)
    scratch = [pltpu.VMEM(shape, f32) for shape in scratch]
    if copies:
        scratch.append(pltpu.SemaphoreType.DMA((copies,)))
    return pl.pallas_call(
        body,
        name=name,
        out_shape=[jax.ShapeDtypeStruct(shape, f32) for shape in outputs],
        in_specs=[pl.BlockSpec(memory_space=pltpu.SMEM)] + [near] * len(inputs),
        out_specs=[far if far_out else near] * len(outputs),
        scratch_shapes=scratch,
        cost_estimate=pl.CostEstimate(flops=int(micros * 1.15e9), bytes_accessed=int(micros * BYTES_A_MICRO), transcendentals=0),
        compiler_params=pltpu.CompilerParams(vmem_limit_bytes=VMEM_LIMIT),
    )(place, *inputs)


def along(value, axis, steps):
    count = lax.axis_size(axis)
    initial, last = max(0, -steps), min(count, count - steps)
    return lax.ppermute(value, axis, [(source, source + steps) for source in range(initial, last)])


def beside(values, sizes):
    if sizes.sides == 1:
        return [[lax.ppermute(value, "width", [(0, 1), (1, 0)]) for value in values]]
    if sizes.sides == 2:
        return [[along(value, "width", steps) for value in values] for steps in (-1, 1)]
    return []


def edge_columns(edges, sizes):
    if sizes.sides == 1:
        return [lax.ppermute(edges[0], "width", [(0, 1), (1, 0)])]
    if sizes.sides == 2:
        return [along(edges[1], "width", -1), along(edges[0], "width", 1)]
    return []


def stages(count):
    stride = 1
    while stride < count:
        radix = 4 if count // stride % 4 == 0 else 2
        yield stride, radix
        stride *= radix


def swap(value, stride, radix, others=None):
    count = lax.axis_size("span")
    others = others or {}
    return [value] + [
        lax.ppermute(others.get(step, value), "span", [(device, device ^ step * stride) for device in range(count)])
        for step in range(1, radix)
    ]


def exchange(pair, stride):
    count = lax.axis_size("span")
    routes = [[], []]
    for low in range(count - stride):
        routes[low // stride % 2] += [(low, low + stride), (low + stride, low)]
    return [None if value is None else lax.ppermute(value, "span", route) for value, route in zip(pair, routes)]


def on_device(right_side, diffusivity, reaction):
    depth, extent_x, extent_y = diffusivity.shape
    sizes = Sizes(depth, extent_x, extent_y, lax.axis_size("span"), lax.axis_size("width"))
    place = jnp.stack([lax.axis_index("span"), lax.axis_index("width")]).astype(jnp.int32)
    n0, n1, n2, n3 = sizes.rows
    s = sizes.sides
    tile = (depth, LANES)
    own = [(depth, count * LANES) for count in sizes.own]
    held = [(depth, count) for count in sizes.held]
    down_message = (sizes.tiles, *tile)
    up_message = (sizes.up_tiles + 1, *tile)
    own0, own1, own2, first, second, *edges = call(
        functools.partial(start_kernel, sizes),
        "start",
        1.1,
        [(2, n0, *own[0]), (2 * n1, *own[1]), (2 * n2, *own[2]), down_message, down_message]
        + [(n0, depth, BORDER)] * 2 * s,
        [(2 * n1, *own[0])],
        place,
        [diffusivity, reaction],
    )
    borders = edge_columns(edges[:s], sizes) + edge_columns(edges[s:], sizes)
    halos = exchange([first, second], 1)
    turned, *edges = call(
        functools.partial(turn_kernel, sizes),
        "turn",
        0.7,
        [(n0, *own[0])] + [(n0, depth, BORDER)] * s,
        [],
        place,
        [right_side],
    )
    borders += edge_columns(edges, sizes)
    plan = list(stages(sizes.span_count))

    part = packing(5)
    far = (sizes.held[2] // LANES, *tile)
    inners = [(sum(inner_rows(sizes, level)), *held[level]) for level in range(3)]
    outers = [(sum(outer_rows(sizes, level)), *held[level]) for level in range(3)]
    inner = call(
        functools.partial(inner_kernel, sizes),
        "inner",
        0.5,
        [(2 * n1, *tile), (2 * n2, *tile), *inners],
        [(2 * n1, *held[0])],
        place,
        [own0, own1, own2, turned, *borders],
    )
    halos, inner = lax.optimization_barrier((halos, inner))
    sides = beside(halos, sizes)
    downs = call(
        functools.partial(down_kernel, sizes),
        "down",
        2.5,
        [*outers, (part, *tile), (part + far[0], *tile), up_message, up_message, far],
        [(5, *tile), (2, *held[2]), (n1 + 2, *held[0])],
        place,
        [own0, own1, own2, turned, *borders, *halos, *sum(sides, []), *inner],
    )
    outer, blocks, with_far, ups, far_second = downs[:3], downs[3], downs[4], list(downs[5:7]), downs[7]
    far_rows = None
    for stride, radix in plan[:-1]:
        count = stride * radix
        if far_rows is None:
            blocks = swap(blocks, stride, radix, {2: with_far})
            far_rows = [blocks[2], exchange([None, far_second], 2)[1]]
        else:
            blocks = swap(blocks, stride, radix)
        (blocks,) = call(
            functools.partial(merge_kernel, sizes, stride, radix),
            "merge",
            0.9,
            [(packing(3 * count + 2), *tile)],
            [(count + 2, *tile), (count, *tile), (count, *tile)],
            place,
            blocks[::-1],
        )
    stride, radix = plan[-1]
    blocks = swap(blocks, stride, radix)
    received = lax.optimization_barrier([exchange([ups[0], None], 1)[0], ups[1]])
    received = [received[0], exchange([None, received[1]], 1)[1]] + far_rows
    scratch = [(sizes.span_count + 2, *tile)] + [(sizes.span_count, *tile)] * 3
    for index in range(3):
        count = sizes.span_count >> index
        scratch += [(count + 1, *tile)] + [(count, *tile)] * 3 + [(count + 2, *tile)] + [(count, *tile)] * 2
        scratch += [(count + 2, *tile)] * 2
    blocks, received[3] = lax.optimization_barrier((blocks, received[3]))
    (coarse,) = call(
        functools.partial(coarse_kernel, sizes, stride, radix),
        "coarse",
        0.7,
        [(n3 + 2, *tile)],
        scratch,
        place,
        [*blocks, *sum(beside(blocks, sizes), [])],
    )
    scratch = [(n1 + 2, *held[1]), (n2 + 2, *held[2]), diffusivity.shape, (2, *held[0]), (2, *held[1])]
    scratch += [(n3 + 2, *held[2]), (n2 + 2, *held[1]), (n1 + 2, *held[0])]
    scratch += [(n2 + 4, *held[2]), (n1 + 4, *held[1]), (n0 + 2, *held[0])]
    scratch += [(n2 + 2, *held[2]), (n1 + 2, *held[1]), (n0, *own[0])]
    (correction,) = call(
        functools.partial(up_kernel, sizes),
        "up",
        3.0,
        [diffusivity.shape],
        scratch,
        place,
        [coarse, *received, *inner[2:], *outer, own0, turned, *borders],
        copies=CHUNKS,
        far_out=True,
    )
    return correction


def solution(mesh):
    in_specs = (P(None, "span", "width"),) * 3
    return jax.shard_map(
        on_device, mesh=mesh, in_specs=in_specs, out_specs=P(None, "span", "width"), check_vma=False
    )
```
